32 devices in a mesh: dp: 8 (over z, y), fsdp: 4 (over x, core).
Axes of the slice: x: 2, y: 2, z: 4, core: 2. Of those that a mesh axis runs over, the one named last changes fastest.
Arguments:
- tokens: bfloat16 [12288, 512], P(('dp', 'fsdp')), may hold values from -6 to 6
- cotangent: bfloat16 [12288, 512], P(('dp', 'fsdp')), may hold values from -6 to 6
- doc_triples: int32 [8, 16], P('dp'), may hold values from 1 to 448, 512 in all within a row
- w_qkv: float32 [2, 512, 1536], P(None, 'dp', 'fsdp'), may hold values from -0.25 to 0.25
- w_out: float32 [2, 512, 512], P(None, 'dp', 'fsdp'), may hold values from -0.75 to 0.75
- w_in: float32 [2, 512, 2048], P(None, 'dp', 'fsdp'), may hold values from -0.25 to 0.25
- w_down: float32 [2, 512, 2048], P(None, 'dp', 'fsdp'), may hold values from -0.125 to 0.125
- w_pool: float32 [512, 1536], P('dp', 'fsdp'), may hold values from -0.15625 to 0.15625
- w_up: float32 [512, 1536], P('dp', 'fsdp'), may hold values from -0.25 to 0.25
- gains: float32 [512, 4], P('dp'), may hold values from 0.5 to 1.5
- m_qkv: float32 [2, 512, 1536], P(None, 'dp', 'fsdp'), may hold values from -1662.7688 to 1662.7688
- m_out: float32 [2, 512, 512], P(None, 'dp', 'fsdp'), may hold values from -2494.153 to 2494.153
- m_in: float32 [2, 512, 2048], P(None, 'dp', 'fsdp'), may hold values from -3325.5376 to 3325.5376
- m_down: float32 [2, 512, 2048], P(None, 'dp', 'fsdp'), may hold values from -5819.691 to 5819.691
- m_pool: float32 [512, 1536], P('dp', 'fsdp'), may hold values from -9600 to 9600
- m_up: float32 [512, 1536], P('dp', 'fsdp'), may hold values from -7200 to 7200
- m_gains: float32 [512, 4], P('dp'), may hold values from -320 to 320
Outputs:
- out_act: bfloat16 [12288, 512], P(('dp', 'fsdp'))
- grad_in: float32 [12288, 512], P(('dp', 'fsdp'))
- m_qkv_new: float32 [2, 512, 1536], P(None, 'dp', 'fsdp')
- m_out_new: float32 [2, 512, 512], P(None, 'dp', 'fsdp')
- m_in_new: float32 [2, 512, 2048], P(None, 'dp', 'fsdp')
- m_down_new: float32 [2, 512, 2048], P(None, 'dp', 'fsdp')
- m_pool_new: float32 [512, 1536], P('dp', 'fsdp')
- m_up_new: float32 [512, 1536], P('dp', 'fsdp')
- w_qkv_new: float32 [2, 512, 1536], P(None, 'dp', 'fsdp')
- w_out_new: float32 [2, 512, 512], P(None, 'dp', 'fsdp')
- w_in_new: float32 [2, 512, 2048], P(None, 'dp', 'fsdp')
- w_down_new: float32 [2, 512, 2048], P(None, 'dp', 'fsdp')
- w_pool_new: float32 [512, 1536], P('dp', 'fsdp')
- w_up_new: float32 [512, 1536], P('dp', 'fsdp')
- gain_moments: float32 [512, 4], P('dp')
- gains_new: float32 [512, 4], P('dp')
- moment_rms: float32 [10], replicated
The draws below stay inside these ranges and needn't reach their ends.
Inputs may be any that keep to these rules, and one draw needn't show every extreme that they name: `doc_triples`: each row lists one bin's document lengths in order; they sum to 512, and one of them is exactly 448.
All inputs are finite; a program needn't handle non-finite values.
Results may differ from the reference program's by a relative error of at most 0.025.
Values may be sent and summed in bfloat16 or wider, within the bound.
A program may use at most 192 MiB of HBM per device.

```python
import math
import jax
import jax.numpy as jnp
import numpy as np
from jax import lax

D = 512
HEAD = 64
FF = 2048
TOK_DEV = 384
DOCS = 16
NS_STEPS = 5
BIN = 1536
TOKENS = 12288
N_DP = 8
N_FSDP = 4


def rising(key, shape, scale, top):
    base = jax.random.truncated_normal(key, -6.0, 6.0, shape, jnp.float32)
    rows = shape[-2]
    cols = shape[-1]
    row_factor = 1.0 + (top - 1.0) * jnp.arange(rows, dtype=jnp.float32) / (rows - 1)
    col_factor = 1.0 + (top - 1.0) * jnp.arange(cols, dtype=jnp.float32) / (cols - 1)
    return base * scale * row_factor[:, None] * col_factor[None, :]


def draw_m_qkv(key, part):
    key = jax.random.fold_in(key, 11)
    return rising(key, (2, D, 3 * D), 0.1 * TOKENS ** 0.5, 3.0)


def draw_m_out(key, part):
    key = jax.random.fold_in(key, 12)
    return rising(key, (2, D, D), 0.15 * TOKENS ** 0.5, 3.0)


def draw_m_in(key, part):
    key = jax.random.fold_in(key, 13)
    return rising(key, (2, D, FF), 0.2 * TOKENS ** 0.5, 3.0)


def draw_m_down(key, part):
    key = jax.random.fold_in(key, 14)
    return rising(key, (2, D, FF), 0.35 * TOKENS ** 0.5, 3.0)


def draw_m_pool(key, part):
    key = jax.random.fold_in(key, 15)
    return rising(key, (D, 3 * D), (TOKENS // 3) ** 0.5, 3.0)


def draw_m_up(key, part):
    key = jax.random.fold_in(key, 16)
    return rising(key, (D, 3 * D), 0.75 * (TOKENS // 3) ** 0.5, 3.0)


def level_of(stream_key, dims, split, smallest, largest):
    def one(position, shards_of):
        heights = jax.random.uniform(jax.random.fold_in(jax.random.fold_in(stream_key, 6), position), (shards_of,), jnp.float32, smallest / len(split), largest / len(split))
        return jnp.repeat(jnp.exp(heights), dims[position] // shards_of).reshape((-1,) + (1,) * (len(dims) - position - 1))

    loudness = one(*split[0])
    for cut in split[1:]:
        loudness = loudness * one(*cut)
    return loudness


def profile(amount, total, limit, skew):
    weights = [(1 << 20) // math.isqrt(rank ** skew) + 1 for rank in range(2, amount + 1)]
    spare, counts = total - limit - (amount - 1), [1] * (amount - 1)
    while spare > 0:
        candidates = [i for i in range(amount - 1) if counts[i] < limit]
        mass, left = sum([weights[i] for i in candidates]), spare
        for i in candidates:
            addition = min(limit - counts[i], max(1, left * weights[i] // mass), spare)
            counts[i] = counts[i] + addition
            spare = spare - addition
    return np.array([limit] + counts)


def ragged(stream_key, number_of, total, most, slope):
    if number_of == 2:
        one = jax.random.randint(stream_key, (), max(1, total - most), min(most, total - 1) + 1)
        return jnp.stack([one, total - one])
    sizes = jnp.asarray(profile(number_of, total, most, slope), jnp.int32)
    couples = (number_of - 1) // 2
    donor, receiver = sizes[1:1 + 2 * couples:2], sizes[2:2 + 2 * couples:2]
    slack = jnp.minimum(donor - 1, most - receiver)
    moved = jax.random.randint(jax.random.fold_in(stream_key, 1), (couples,), 0, 1 << 20) % (slack + 1)
    sizes = sizes.at[1:1 + 2 * couples:2].set(donor - moved).at[2:2 + 2 * couples:2].set(receiver + moved)
    return sizes[jax.random.permutation(jax.random.fold_in(stream_key, 2), number_of)]


def bell_draw(rng, dims, scale, bound, split=(), kind=jnp.bfloat16):
    factor_of = level_of(rng, dims, split, -0.22, 0.18) if split else 1.0
    drawn = jax.random.normal(rng, dims, jnp.float32) * scale * factor_of
    return jnp.minimum(jnp.maximum(drawn, -bound), bound).astype(kind)


def setup_inputs(seed: int = 0) -> dict:
    streams_of = jax.random.split(jax.random.key(seed), 18)
    tokens = bell_draw(streams_of[0], (TOKENS, D), 1.0, 6.0, ((0, 32),))
    cotangent = bell_draw(streams_of[1], (TOKENS, D), 1.0, 6.0, ((0, 32),))
    doc_triples = jax.vmap(lambda own: ragged(own, DOCS, TOK_DEV * N_FSDP // 3, TOK_DEV * N_FSDP // 3 - TOK_DEV // 6, 2))(jax.random.split(streams_of[2], N_DP)).reshape((N_DP, DOCS)).astype(jnp.int32)
    w_qkv = bell_draw(streams_of[3], (2, D, 3 * D), D ** -0.5, 0.25, ((1, 8), (2, 4)), jnp.float32)
    w_out = bell_draw(streams_of[4], (2, D, D), (D // 8) ** -0.5, 0.75, ((1, 8), (2, 4)), jnp.float32)
    w_in = bell_draw(streams_of[5], (2, D, FF), D ** -0.5, 0.25, ((1, 8), (2, 4)), jnp.float32)
    w_down = bell_draw(streams_of[6], (2, D, FF), FF ** -0.5, 0.125, ((1, 8), (2, 4)), jnp.float32)
    w_pool = bell_draw(streams_of[7], (D, 3 * D), (3 * D) ** -0.5, 0.15625, ((0, 8), (1, 4)), jnp.float32)
    w_up = bell_draw(streams_of[8], (D, 3 * D), D ** -0.5, 0.25, ((0, 8), (1, 4)), jnp.float32)
    gains = jnp.clip(1.0 + 0.1 * jax.random.normal(streams_of[9], (D, 4), jnp.float32), 0.5, 1.5)
    m_qkv = draw_m_qkv(jax.random.fold_in(streams_of[17], 71), 0)
    m_out = draw_m_out(jax.random.fold_in(streams_of[17], 71), 0)
    m_in = draw_m_in(jax.random.fold_in(streams_of[17], 71), 0)
    m_down = draw_m_down(jax.random.fold_in(streams_of[17], 71), 0)
    m_pool = draw_m_pool(jax.random.fold_in(streams_of[17], 71), 0)
    m_up = draw_m_up(jax.random.fold_in(streams_of[17], 71), 0)
    m_gains = bell_draw(streams_of[16], (D, 4), (0.5 * TOKENS ** 0.5), 320.0, ((0, 8),), jnp.float32)
    return dict(tokens=tokens, cotangent=cotangent, doc_triples=doc_triples, w_qkv=w_qkv, w_out=w_out, w_in=w_in, w_down=w_down, w_pool=w_pool, w_up=w_up, gains=gains, m_qkv=m_qkv, m_out=m_out, m_in=m_in, m_down=m_down, m_pool=m_pool, m_up=m_up, m_gains=m_gains)


@jax.custom_vjp
def low(v):
    return lax.optimization_barrier(v.astype(jnp.bfloat16)).astype(jnp.float32)

@jax.custom_vjp
def low_back(v):
    return v

def low_keep(v):
    return (low(v), None)

def low_pass(kept, grad):
    return (grad,)

def back_keep(v):
    return (v, None)

def back_low(kept, grad):
    return (low(grad),)
low.defvjp(low_keep, low_pass)
low_back.defvjp(back_keep, back_low)
NS_COEFS = (3.4445, -4.775, 2.0315)
STEP_SCALES = (0.8660254, 1.4142136, 1.0, 0.5, 0.5, 0.8660254)
MOMENT_DECAY = 0.95
GAIN_DECAY = 0.9
GAIN_RATE = 0.001
LN_EPS = 1e-05
NORM_EPS = 1e-07
MASKED = -1e+30

def matmul_hi(left, right):
    return jnp.dot(left, right, precision=lax.Precision.HIGHEST, preferred_element_type=jnp.float32)

def layer_norm(values, gain_vec):
    row_mean = lax.optimization_barrier(jnp.mean(values, axis=-1, keepdims=True))
    centred = values - row_mean
    spread = lax.optimization_barrier(jnp.mean(centred * centred, axis=-1, keepdims=True))
    return centred * lax.rsqrt(spread + LN_EPS) * gain_vec

def gelu_tanh(values):
    return 0.5 * values * (1.0 + jnp.tanh(0.7978845608028654 * (values + 0.044715 * values * values * values)))

def rotate(values, positions):
    tok_rows = values.shape[0]
    half_size = HEAD // 2
    grouped = values.reshape(tok_rows, -1, HEAD)
    frequency = 10000.0 ** (-jnp.arange(half_size, dtype=jnp.float32) / half_size)
    angles = positions.astype(jnp.float32)[:, None] * frequency[None, :]
    cosine = jnp.cos(angles)[:, None, :]
    sine_part = jnp.sin(angles)[:, None, :]
    first_half = grouped[..., :half_size]
    second_half = grouped[..., half_size:]
    turned = jnp.concatenate([first_half * cosine - second_half * sine_part, first_half * sine_part + second_half * cosine], axis=-1)
    return turned.reshape(tok_rows, -1)

def doc_layout(triples, positions):
    doc_ends = jnp.cumsum(triples * 3).astype(jnp.int32)
    reached = positions[:, None] >= doc_ends[None, :]
    segment = lax.optimization_barrier(jnp.sum(reached.astype(jnp.int32), axis=1)).astype(jnp.int32)
    doc_start = lax.optimization_barrier(jnp.max(jnp.where(reached, doc_ends[None, :], 0), axis=1)).astype(jnp.int32)
    return (segment, doc_start)

def block(residual, positions, segment, gain_pair, matrices):
    w_qkv, w_out, w_in, w_down = matrices
    tok_rows, model_width = residual.shape
    head_count = model_width // HEAD
    normed = low(layer_norm(residual, gain_pair[:, 0]))
    qkv_rows = low_back(matmul_hi(normed, w_qkv))
    query = low(rotate(qkv_rows[:, :model_width], positions)).reshape(tok_rows, head_count, HEAD)
    key_rot = low(rotate(qkv_rows[:, model_width:2 * model_width], positions)).reshape(tok_rows, head_count, HEAD)
    value_rows = low(qkv_rows[:, 2 * model_width:]).reshape(tok_rows, head_count, HEAD)
    raw_scores = low_back(jnp.einsum('qhd,khd->hqk', query, key_rot, precision=lax.Precision.HIGHEST))
    allowed = (positions[None, :] <= positions[:, None]) & (segment[None, :] == segment[:, None])
    scores = jnp.where(allowed[None], raw_scores * 0.125, MASKED)
    row_max = lax.optimization_barrier(jnp.max(scores, axis=2, keepdims=True))
    exp_scores = jnp.exp(scores - row_max)
    prob_values = low(exp_scores / lax.optimization_barrier(jnp.sum(exp_scores, axis=2, keepdims=True)))
    attended = jnp.einsum('hqk,khd->qhd', prob_values, value_rows, precision=lax.Precision.HIGHEST).reshape(tok_rows, model_width)
    attended = low_back(low(attended))
    middle = residual + low_back(matmul_hi(attended, w_out))
    normed_two = low(layer_norm(middle, gain_pair[:, 1]))
    pre_act = low_back(matmul_hi(normed_two, w_in))
    hidden = low(gelu_tanh(pre_act))
    return middle + low_back(matmul_hi(hidden, w_down.T))

def hourglass(residual, triples, lowered):
    w_qkv, w_out, w_in, w_down, w_pool, w_up, gains_low = lowered
    bin_rows, model_width = residual.shape
    short_rows = bin_rows // 3
    positions = jnp.arange(bin_rows, dtype=jnp.int32)
    segment, doc_start = doc_layout(triples, positions)
    after_one = block(residual, positions, segment, gains_low[:, 0:2], (w_qkv[0], w_out[0], w_in[0], w_down[0]))
    shifted = jnp.concatenate([jnp.zeros((2, model_width), jnp.float32), after_one[:bin_rows - 2]], axis=0).reshape(short_rows, 3, model_width)
    group_gate = jnp.where(positions[::3] == doc_start[::3], 0.0, 1.0).astype(jnp.float32)
    keep_mask = jnp.stack([group_gate, group_gate, jnp.ones_like(group_gate)], axis=1)[:, :, None]
    pool_input = low((shifted * keep_mask).reshape(short_rows, 3 * model_width))
    pooled = low_back(matmul_hi(pool_input, w_pool.T))
    short_pos = jnp.arange(short_rows, dtype=jnp.int32)
    after_two = block(pooled, short_pos, segment[::3], gains_low[:, 2:4], (w_qkv[1], w_out[1], w_in[1], w_down[1]))
    lifted = low_back(matmul_hi(low(after_two), w_up)).reshape(bin_rows, model_width)
    return after_one + lifted

def orthogonalize(moment, norm_val):
    coef_a, coef_b, coef_c = NS_COEFS
    ns_block = (moment / (norm_val + NORM_EPS)).astype(jnp.bfloat16)
    for ns_step in range(NS_STEPS):
        gram_matrix = jnp.dot(ns_block, ns_block.T, preferred_element_type=jnp.float32).astype(jnp.bfloat16)
        poly_term = (coef_b * gram_matrix.astype(jnp.float32) + coef_c * jnp.dot(gram_matrix, gram_matrix, preferred_element_type=jnp.float32)).astype(jnp.bfloat16)
        ns_block = (coef_a * ns_block.astype(jnp.float32) + jnp.dot(poly_term, ns_block, preferred_element_type=jnp.float32)).astype(jnp.bfloat16)
    return ns_block.astype(jnp.float32)

def reference(tokens, cotangent, doc_triples, w_qkv, w_out, w_in, w_down, w_pool, w_up, gains, m_qkv, m_out, m_in, m_down, m_pool, m_up, m_gains):
    weights_all = (w_qkv, w_out, w_in, w_down, w_pool, w_up, gains)
    residual = tokens.astype(jnp.float32).reshape(N_DP, BIN, D)

    def forward(residual_all, weights_in):
        lowered = tuple((low(weight) for weight in weights_in))

        def one_bin(carry_value, bin_items):
            return (carry_value, jax.checkpoint(hourglass)(bin_items[0], bin_items[1], lowered))
        return lax.scan(one_bin, jnp.zeros((), jnp.float32), (residual_all, doc_triples))[1]
    layer_out, pull_back = jax.vjp(forward, residual, weights_all)
    grad_resid, grads = pull_back(cotangent.astype(jnp.float32).reshape(N_DP, BIN, D))
    old_moments = (m_qkv, m_out, m_in, m_down, m_pool, m_up)
    moments = tuple((MOMENT_DECAY * old_moments[kind_id] + grads[kind_id] for kind_id in range(6)))
    pieces = []
    for kind_id in range(4):
        pieces.append(moments[kind_id][0])
        pieces.append(moments[kind_id][1])
    pieces.append(moments[4])
    pieces.append(moments[5])
    norm_list = [jnp.sqrt(jnp.sum(piece * piece)) for piece in pieces]
    moment_rms = jnp.stack([norm_list[idx] / jnp.sqrt(jnp.float32(pieces[idx].size) * TOKENS) for idx in range(10)]).astype(jnp.float32)
    ortho = [orthogonalize(pieces[idx], norm_list[idx]) for idx in range(10)]
    new_weights = []
    for kind_id in range(4):
        new_weights.append(jnp.stack([weights_all[kind_id][blk_id] - STEP_SCALES[kind_id] * ortho[2 * kind_id + blk_id] for blk_id in range(2)]))
    new_weights.append(w_pool - STEP_SCALES[4] * ortho[8])
    new_weights.append(w_up - STEP_SCALES[5] * ortho[9])
    gain_moments = GAIN_DECAY * m_gains + grads[6]
    gains_new = gains - GAIN_RATE * gain_moments
    return (layer_out.reshape(TOKENS, D).astype(jnp.bfloat16), grad_resid.reshape(TOKENS, D), moments[0], moments[1], moments[2], moments[3], moments[4], moments[5], new_weights[0], new_weights[1], new_weights[2], new_weights[3], new_weights[4], new_weights[5], gain_moments, gains_new, moment_rms)
```

```python
import functools

import jax
import jax.numpy as jnp
import numpy as np
from jax import lax
from jax.experimental import pallas as pl
from jax.experimental.pallas import tpu as pltpu
from jax.sharding import PartitionSpec as P

HEAD = 64
NS_STEPS = 5
NS_COEFS = (3.4445, -4.775, 2.0315)
STEP_SCALES = (0.8660254, 1.4142136, 1.0, 0.5, 0.5, 0.8660254)
MOMENT_DECAY = 0.95
GAIN_DECAY = 0.9
GAIN_RATE = 0.001
LN_EPS = 1e-05
NORM_EPS = 1e-07
MASKED = -1e30
HALO = 16
QB = 256
LANES = 128
VMEM_BYTES = 56 << 20
BF = jnp.bfloat16
F32 = jnp.float32
MESH = pl.DeviceIdType.MESH


def dot_nn(left, right):
    return lax.dot_general(left, right, (((1,), (0,)), ((), ())), preferred_element_type=F32)


def dot_nt(left, right):
    return lax.dot_general(left, right, (((1,), (1,)), ((), ())), preferred_element_type=F32)


def dot_tn(left, right):
    return lax.dot_general(left, right, (((0,), (0,)), ((), ())), preferred_element_type=F32)


def layer_norm(values, gain):
    mean = jnp.mean(values, axis=-1, keepdims=True)
    centred = values - mean
    spread = jnp.mean(centred * centred, axis=-1, keepdims=True)
    return centred * lax.rsqrt(spread + LN_EPS) * gain


def layer_norm_back(values, gain, grad):
    mean = jnp.mean(values, axis=-1, keepdims=True)
    centred = values - mean
    spread = jnp.mean(centred * centred, axis=-1, keepdims=True)
    scale = lax.rsqrt(spread + LN_EPS)
    unit = centred * scale
    scaled = grad * gain
    part = jnp.mean(scaled, axis=-1, keepdims=True)
    along = jnp.mean(scaled * unit, axis=-1, keepdims=True)
    return scale * (scaled - part - unit * along), grad * unit


def gelu(values):
    return 0.5 * values * (1.0 + jnp.tanh(0.7978845608028654 * (values + 0.044715 * values * values * values)))


def gelu_both(values):
    square = values * values
    turn = jnp.tanh(0.7978845608028654 * (values + 0.044715 * values * square))
    slope = 0.7978845608028654 * (1.0 + 3.0 * 0.044715 * square)
    half = 0.5 * (1.0 + turn)
    return values * half, half + 0.5 * values * (1.0 - turn * turn) * slope


def partner(values):
    width = values.shape[1]
    if width == LANES:
        lane = lax.broadcasted_iota(jnp.int32, values.shape, 1)
        ahead = pltpu.roll(values, LANES - HEAD // 2, 1)
        behind = pltpu.roll(values, HEAD // 2, 1)
        return jnp.where(lane % HEAD < HEAD // 2, ahead, behind)
    parts = []
    for at in range(0, width, HEAD):
        parts += [values[:, at + HEAD // 2 : at + HEAD], values[:, at : at + HEAD // 2]]
    return jnp.concatenate(parts, axis=1)


def widen(values):
    rows, width = values.shape
    if width >= LANES:
        return values
    return jnp.concatenate([values, jnp.zeros((rows, LANES - width), values.dtype)], axis=1)


def params():
    return pltpu.CompilerParams(vmem_limit_bytes=VMEM_BYTES)


def smem():
    return pl.BlockSpec(memory_space=pltpu.SMEM)


def vmem():
    return pl.BlockSpec(memory_space=pltpu.VMEM)


def cost(flops, moved):
    return pl.CostEstimate(flops=int(flops), bytes_accessed=int(moved), transcendentals=0)


def local_kernel(body, name, outs, scratch, me, *arrays, flops=0):
    moved = sum(a.size * a.dtype.itemsize for a in arrays)
    moved += sum(int(np.prod(s)) * jnp.dtype(t).itemsize for s, t in outs)
    return pl.pallas_call(
        body,
        out_shape=[jax.ShapeDtypeStruct(s, t) for s, t in outs],
        in_specs=[smem()] + [vmem()] * len(arrays),
        out_specs=[vmem()] * len(outs),
        scratch_shapes=[pltpu.VMEM(s, t) for s, t in scratch],
        compiler_params=params(),
        cost_estimate=cost(flops, moved),
        name=name,
    )(me, *arrays)


def at_rows(me, step, rows):
    return pl.multiple_of((me ^ step) * rows, 16)


def head_inputs(qs, ks, rows, q, k, fq, fk, heads):
    lane = lax.broadcasted_iota(jnp.int32, (q.shape[0], LANES), 1)
    q, k = widen(q), widen(k)
    for h in range(heads):
        mine = lane // HEAD == h
        qs[h, rows, :] = jnp.where(mine, q * 0.125, fq).astype(BF)
        ks[h, rows, :] = jnp.where(mine, k, fk).astype(BF)


def scores_t(ks, qs, h, start, stop):
    top = dot_nt(ks[h, 0:stop, :], qs[h, start:stop, :])
    key = lax.broadcasted_iota(jnp.int32, (stop - start, stop - start), 0)
    query = lax.broadcasted_iota(jnp.int32, (stop - start, stop - start), 1)
    last = jnp.where(key <= query, top[start:, :], MASKED)
    if start == 0:
        return last
    return jnp.concatenate([top[:start, :], last], axis=0)


def attn_forward(me, pieces, gain, w_qkv, fq, fk, cos, sin):
    count = len(pieces)
    rows, width = pieces[0].shape
    total = rows * count
    hd = w_qkv.shape[1] // 3
    heads = hd // HEAD
    blk = min(QB, total)

    def body(me_ref, *refs):
        piece_refs = refs[:count]
        gain_ref, w_ref, fq_ref, fk_ref, cos_ref, sin_ref, n1, qkv, out, qs, ks, vt = refs[count:]
        me_now = me_ref[0]
        for step in range(count):
            base = at_rows(me_now, step, rows)
            for r in range(0, rows, LANES):
                block = piece_refs[step][r : r + LANES, :].astype(F32)
                n1[pl.ds(base + r, LANES), :] = layer_norm(block, gain_ref[...]).astype(BF)
        for r in range(0, total, blk):
            here = slice(r, r + blk)
            got = dot_nn(n1[here, :], w_ref[...])
            q, k, v = got[:, :hd], got[:, hd : 2 * hd], got[:, 2 * hd :]
            q = (q * cos_ref[here, :] + partner(q) * sin_ref[here, :]).astype(BF)
            k = (k * cos_ref[here, :] + partner(k) * sin_ref[here, :]).astype(BF)
            qkv[here, 0:hd] = q
            qkv[here, hd : 2 * hd] = k
            qkv[here, 2 * hd : 3 * hd] = v.astype(BF)
            head_inputs(
                qs, ks, here, q.astype(F32), k.astype(F32), fq_ref[here, :].astype(F32), fk_ref[here, :].astype(F32), heads
            )
            vt[:, here] = v.T.astype(BF)
        for r in range(0, total, blk):
            stop = r + blk
            found = []
            for h in range(heads):
                s = scores_t(ks, qs, h, r, stop)
                e = jnp.exp(s - jnp.max(s, axis=0, keepdims=True))
                p = (e * (1.0 / jnp.sum(e, axis=0, keepdims=True))).astype(BF)
                found.append(dot_nn(vt[h * HEAD : (h + 1) * HEAD, 0:stop], p))
            out[r:stop, :] = jnp.concatenate(found, axis=0).T.astype(BF)

    return local_kernel(
        body,
        "attn_forward",
        [((total, width), BF), ((total, 3 * hd), BF), ((total, hd), BF)],
        [((heads, total, LANES), BF), ((heads, total, LANES), BF), ((hd, total), BF)],
        me,
        *pieces,
        gain,
        w_qkv,
        fq,
        fk,
        cos,
        sin,
        flops=8e9,
    )


def attn_backward(me, pieces, qkv, wo_own, w_qkv, fq, fk, cos, sin):
    count = len(pieces)
    rows, width = pieces[0].shape
    total = rows * count
    hd = w_qkv.shape[1] // 3
    heads = hd // HEAD
    blk = min(QB, total)

    def body(me_ref, *refs):
        piece_refs = refs[:count]
        qkv_ref, wo_ref, w_ref, fq_ref, fk_ref, cos_ref, sin_ref = refs[count : count + 7]
        whole, dqkv, keep, send, qs, ks, qz, doz, kt, dk, dv = refs[count + 7 :]
        me_now = me_ref[0]
        for step in range(count):
            base = at_rows(me_now, step, rows)
            whole[pl.ds(base, rows), :] = piece_refs[step][...]
        lane = lax.broadcasted_iota(jnp.int32, (blk, LANES), 1)
        for r in range(0, total, blk):
            here = slice(r, r + blk)
            q = qkv_ref[here, 0:hd].astype(F32)
            k = qkv_ref[here, hd : 2 * hd].astype(F32)
            head_inputs(qs, ks, here, q, k, fq_ref[here, :].astype(F32), fk_ref[here, :].astype(F32), heads)
            kt[:, here] = k.T.astype(BF)
            do = widen(dot_nt(whole[here, :], wo_ref[...]))
            q = widen(q)
            for h in range(heads):
                mine = lane // HEAD == h
                qz[h, here, :] = jnp.where(mine, q, 0.0).astype(BF)
                doz[h, here, :] = jnp.where(mine, do, 0.0).astype(BF)
            dk[here, :] = jnp.zeros((blk, LANES), F32)
            dv[here, :] = jnp.zeros((blk, LANES), F32)
        for r in range(0, total, blk):
            stop = r + blk
            here = slice(r, stop)
            found = []
            add_k = None
            for h in range(heads):
                s = scores_t(ks, qs, h, r, stop)
                e = jnp.exp(s - jnp.max(s, axis=0, keepdims=True))
                p = e * (1.0 / jnp.sum(e, axis=0, keepdims=True))
                v = widen(qkv_ref[0:stop, 2 * hd : 3 * hd])
                dp = dot_nt(v, doz[h, here, :])
                mid = jnp.sum(p * dp, axis=0, keepdims=True)
                dr = (p * (dp - mid) * 0.125).astype(BF)
                part_v = dot_nn(p.astype(BF), doz[h, here, :])
                part_k = dot_nn(dr, qz[h, here, :])
                add_v = part_v if add_k is None else add_v + part_v
                add_k = part_k if add_k is None else add_k + part_k
                found.append(dot_nn(kt[h * HEAD : (h + 1) * HEAD, 0:stop], dr))
            dk[0:stop, :] += add_k
            dv[0:stop, :] += add_v
            dq = jnp.concatenate(found, axis=0).T
            dqkv[here, 0:hd] = (dq * cos_ref[here, :] - partner(dq) * sin_ref[here, :]).astype(BF)
        for r in range(0, total, blk):
            here = slice(r, r + blk)
            grad = dk[here, 0:hd]
            dqkv[here, hd : 2 * hd] = (grad * cos_ref[here, :] - partner(grad) * sin_ref[here, :]).astype(BF)
            dqkv[here, 2 * hd : 3 * hd] = dv[here, 0:hd].astype(BF)
        for step in range(count):
            base = at_rows(me_now, step, rows)
            part = dot_nt(dqkv[pl.ds(base, rows), :], w_ref[...])
            if step % 2:
                send[step // 2] = part.astype(BF)
            else:
                keep[step // 2] = part

    return local_kernel(
        body,
        "attn_backward",
        [
            ((total, width), BF),
            ((total, 3 * hd), BF),
            ((count // 2, rows, width), F32),
            ((count // 2, rows, width), BF),
        ],
        [((heads, total, LANES), BF)] * 4 + [((hd, total), BF), ((total, LANES), F32), ((total, LANES), F32)],
        me,
        *pieces,
        qkv,
        wo_own,
        w_qkv,
        fq,
        fk,
        cos,
        sin,
        flops=16e9,
    )


def mix_forward(me, pieces, att, wo, wi, wd, gain, halo):
    count = len(pieces)
    rows, width = pieces[0].shape
    total = rows * count
    hd = att[0].shape[1]
    fj = wi.shape[1]
    long_rows = rows + halo

    def body(me_ref, *refs):
        piece_refs, refs = refs[:count], refs[count:]
        att_refs, refs = refs[:count], refs[count:]
        wo_refs, refs = refs[:count], refs[count:]
        wi_ref, wd_ref, gain_ref, n2, att_rel, wo_own, mid, keep, send, blocks, full, turned, m_all, part_all = refs
        me_now = me_ref[0]
        for step in range(count):
            blocks[me_now ^ step] = wo_refs[step][...]
            att_rel[:, step * hd : (step + 1) * hd] = att_refs[step][...]
        for at in range(count):
            full[:, at * hd : (at + 1) * hd] = blocks[at]
        for step in range(count):
            base = at_rows(me_now, step, hd)
            turned[step * hd : (step + 1) * hd, :] = full[pl.ds(base, hd), :]
        wo_own[...] = turned[0:hd, :]
        for step in range(count):
            base = at_rows(me_now, step, rows)
            for r in range(0, rows, LANES):
                at = pl.ds(base + r, LANES)
                m = piece_refs[step][r : r + LANES, :].astype(F32) + dot_nn(att_rel[at, :], turned[...])
                m_all[at, :] = m
                low = layer_norm(m, gain_ref[...]).astype(BF)
                n2[step * rows + r : step * rows + r + LANES, :] = low
                hid = gelu(dot_nn(low, wi_ref[...])).astype(BF)
                part_all[at, :] = dot_nt(hid, wd_ref[...])
        for step in range(count):
            base = at_rows(me_now, step, rows)
            out = (send if step % 2 else keep).at[step // 2]
            out[halo:long_rows, :] = part_all[pl.ds(base, rows), :].astype(out.dtype)
            if halo:
                before = pl.multiple_of(lax.rem(base + total - halo, total), 16)
                out[0:halo, :] = part_all[pl.ds(before, halo), :].astype(out.dtype)
                if step == 0:
                    mid[0:halo, :] = m_all[pl.ds(before, halo), :]
            if step == 0:
                mid[halo:long_rows, :] = m_all[pl.ds(base, rows), :]

    return local_kernel(
        body,
        "mix_forward",
        [
            ((total, width), BF),
            ((total, width), BF),
            ((hd, width), BF),
            ((long_rows, width), F32),
            ((count // 2, long_rows, width), F32),
            ((count // 2, long_rows, width), BF),
        ],
        [
            ((count, width, hd), BF),
            ((width, width), BF),
            ((width, width), BF),
            ((total, width), F32),
            ((total, width), F32),
        ],
        me,
        *pieces,
        *att,
        *wo,
        wi,
        wd,
        gain,
        flops=2 * total * width * (width + 2 * fj),
    )


def mix_backward(me, grads, n2, wi, wd):
    count = len(grads)
    rows, width = grads[0].shape
    total = rows * count
    fj = wi.shape[1]

    def body(me_ref, *refs):
        grad_refs = refs[:count]
        n2_ref, wi_ref, wd_ref, whole, hid, dpre, keep, send = refs[count:]
        for step in range(count):
            out = (send if step % 2 else keep).at[step // 2]
            for r in range(0, rows, LANES):
                at = slice(step * rows + r, step * rows + r + LANES)
                grad = grad_refs[step][r : r + LANES, :]
                whole[at, :] = grad
                value, slope = gelu_both(dot_nn(n2_ref[at, :], wi_ref[...]))
                hid[at, :] = value.astype(BF)
                low = (dot_nn(grad, wd_ref[...]) * slope).astype(BF)
                dpre[at, :] = low
                out[r : r + LANES, :] = dot_nt(low, wi_ref[...]).astype(out.dtype)

    return local_kernel(
        body,
        "mix_backward",
        [
            ((total, width), BF),
            ((total, fj), BF),
            ((total, fj), BF),
            ((count // 2, rows, width), F32),
            ((count // 2, rows, width), BF),
        ],
        [],
        me,
        *grads,
        n2,
        wi,
        wd,
        flops=6 * total * width * fj,
    )


def norm_backward(me, values, gain, total_in, got, above):
    rows, width = values.shape

    def body(me_ref, v_ref, gain_ref, t_ref, got_ref, above_ref, full, low, dgain):
        acc = jnp.zeros((1, width), F32)
        for r in range(0, rows, LANES):
            at = slice(r, r + LANES)
            grad = t_ref[at, :] + got_ref[at, :].astype(F32)
            dx, dg = layer_norm_back(v_ref[at, :].astype(F32), gain_ref[...], grad)
            dx = dx + above_ref[at, :]
            full[at, :] = dx
            low[at, :] = dx.astype(BF)
            acc = acc + jnp.sum(dg, axis=0, keepdims=True)
        dgain[...] = jnp.broadcast_to(acc, (8, width))

    return local_kernel(
        body,
        "norm_backward",
        [((rows, width), F32), ((rows, width), BF), ((8, width), F32)],
        [],
        me,
        values,
        gain,
        total_in,
        got,
        above,
    )


def spread_write(hold, values):
    for c in range(hold.shape[0]):
        hold[c] = values[:, c * LANES : (c + 1) * LANES]


def spread_read(hold):
    return jnp.concatenate([hold[c] for c in range(hold.shape[0])], axis=1)


def strided_read(hold, start, amount):
    return jnp.concatenate([hold[c, pl.ds(start, amount, stride=3), :] for c in range(hold.shape[0])], axis=1)


def strided_write(hold, start, amount, values):
    for c in range(hold.shape[0]):
        hold[c, pl.ds(start, amount, stride=3), :] = values[:, c * LANES : (c + 1) * LANES]


def pool_forward(me, mid, total_in, got, gate, wp):
    count = len(wp)
    long_rows, width = mid.shape
    rows = long_rows - HALO
    short = rows // 3
    cols = wp[0].shape[1]

    def body(me_ref, mid_ref, t_ref, got_ref, gate_ref, *refs):
        wp_refs = refs[:count]
        after, blocks, s0, hold = refs[count:]
        me_now = me_ref[0]
        a = mid_ref[...] + t_ref[...] + got_ref[...].astype(F32)
        spread_write(hold, a)
        after[...] = a[HALO:, :]
        parts = []
        for k in range(3):
            part = strided_read(hold, HALO - 2 + k, short)
            if k < 2:
                part = jnp.where(gate_ref[0:short, :] > 0.0, part, 0.0)
            parts.append(part)
        z = jnp.concatenate(parts, axis=1).astype(BF)
        for at in range(count):
            blocks[at] = z[:, at * cols : (at + 1) * cols]
        acc = jnp.zeros((short, width), F32)
        for step in range(count):
            acc = acc + dot_nt(blocks[me_now ^ step], wp_refs[step][...])
        s0[...] = acc

    return local_kernel(
        body,
        "pool_forward",
        [((rows, width), F32), ((count, short, cols), BF), ((short, width), F32)],
        [((width // LANES, long_rows, LANES), F32)],
        me,
        mid,
        total_in,
        got,
        gate,
        *wp,
        flops=2 * short * width * 3 * width,
    )


def up_backward(me, cot, wu):
    count = len(wu)
    rows, width = cot.shape
    short = rows // 3
    cols = wu[0].shape[1]

    def body(me_ref, cot_ref, *refs):
        wu_refs = refs[:count]
        blocks, full, low, hold = refs[count:]
        me_now = me_ref[0]
        spread_write(hold, cot_ref[...].astype(F32))
        lifted = jnp.concatenate([strided_read(hold, k, short) for k in range(3)], axis=1).astype(BF)
        for at in range(count):
            blocks[at] = lifted[:, at * cols : (at + 1) * cols]
        acc = jnp.zeros((short, width), F32)
        for step in range(count):
            acc = acc + dot_nt(blocks[me_now ^ step], wu_refs[step][...])
        full[...] = acc
        low[...] = acc.astype(BF)

    return local_kernel(
        body,
        "up_backward",
        [((count, short, cols), BF), ((short, width), F32), ((short, width), BF)],
        [((width // LANES, rows, LANES), F32)],
        me,
        cot,
        *wu,
        flops=2 * short * width * 3 * width,
    )


def up_forward(me, mid, total_in, got, after, wu):
    count = len(wu)
    short, width = mid.shape
    rows = short * 3
    cols = wu[0].shape[1]

    def body(me_ref, mid_ref, t_ref, got_ref, after_ref, *refs):
        wu_refs = refs[:count]
        low, out, blocks, hold = refs[count:]
        me_now = me_ref[0]
        s1 = (mid_ref[...] + t_ref[...] + got_ref[...].astype(F32)).astype(BF)
        low[...] = s1
        for step in range(count):
            blocks[me_now ^ step] = dot_nn(s1, wu_refs[step][...])
        lift = jnp.concatenate([blocks[at] for at in range(count)], axis=1)
        for k in range(3):
            strided_write(hold, k, short, lift[:, k * width : (k + 1) * width])
        out[...] = (after_ref[...] + spread_read(hold)).astype(BF)

    return local_kernel(
        body,
        "up_forward",
        [((short, width), BF), ((rows, width), BF)],
        [((count, short, cols), F32), ((width // LANES, rows, LANES), F32)],
        me,
        mid,
        total_in,
        got,
        after,
        *wu,
        flops=2 * short * width * 3 * width,
    )


def pool_backward(me, ds0, ds0_next, gate, wp, cot):
    count = len(wp)
    short, width = ds0.shape
    rows = short * 3
    cols = wp[0].shape[1]

    def body(me_ref, ds0_ref, next_ref, gate_ref, cot_ref, *refs):
        wp_refs = refs[:count]
        full, low, blocks, hold, spread = refs[count:]
        me_now = me_ref[0]
        grad = jnp.concatenate([ds0_ref[...], next_ref[...]], axis=0)
        for step in range(count):
            blocks[me_now ^ step] = dot_nn(grad, wp_refs[step][...])
        for at in range(count):
            hold[:, at * cols : (at + 1) * cols] = blocks[at]
        strided_write(spread, 0, short, hold[0:short, 2 * width : 3 * width])
        open_gate = gate_ref[1 : short + 1, :] > 0.0
        for k in range(2):
            part = hold[1 : short + 1, k * width : (k + 1) * width]
            strided_write(spread, k + 1, short, jnp.where(open_gate, part, 0.0))
        da = cot_ref[...].astype(F32) + spread_read(spread)
        full[...] = da
        low[...] = da.astype(BF)

    return local_kernel(
        body,
        "pool_backward",
        [((rows, width), F32), ((rows, width), BF)],
        [((count, short + HALO, cols), F32), ((short + HALO, 3 * width), F32), ((width // LANES, rows, LANES), F32)],
        me,
        ds0,
        ds0_next,
        gate,
        cot,
        *wp,
        flops=2 * short * width * 3 * width,
    )


def swap(value, axis, bit):
    return lax.ppermute(value, axis, [(i, i ^ bit) for i in range(lax.axis_size(axis))])


def gather_pieces(value):
    count = lax.axis_size("fsdp")
    pieces = {0: value}
    bit = count // 2
    while bit:
        for step in list(pieces):
            pieces[step ^ bit] = swap(pieces[step], "fsdp", bit)
        bit //= 2
    return [pieces[step] for step in range(count)]


def finish_scatter(keep, send):
    total = keep + swap(send, "fsdp", 1).astype(F32)
    bit = 2
    while total.shape[0] > 2:
        total = total[0::2] + swap(total[1::2].astype(BF), "fsdp", bit).astype(F32)
        bit *= 2
    return total[0], swap(total[1].astype(BF), "fsdp", bit)


def exchange_blocks(blocks, me):
    count = lax.axis_size("fsdp")
    out = []
    for step in range(count):
        block = lax.dynamic_index_in_dim(blocks, me ^ step, 0, keepdims=False)
        out.append(swap(block, "fsdp", step) if step else block)
    return out


def gather_rows(value, y_count):
    count = lax.axis_size("dp")
    pieces = {0: value}
    for step in range(y_count, count, y_count):
        pieces[step] = swap(value, "dp", step)
    for base in range(0, count, y_count):
        for step in range(1, y_count):
            pieces[base ^ step] = swap(pieces[base], "dp", step)
    return [pieces[step] for step in range(count)]


def assemble_rows(dp_index, pieces, widths):
    count = len(pieces)
    rows = pieces[0].shape[0]

    def body(me_ref, *refs):
        piece_refs, outs = refs[:count], refs[count:]
        me_now = me_ref[0]
        for step in range(count):
            base = pl.multiple_of((me_now ^ step) * rows, 16)
            at = 0
            for out, width in zip(outs, widths):
                out[pl.ds(base, rows), :] = piece_refs[step][:, at : at + width]
                at += width

    return local_kernel(body, "assemble_rows", [((rows * count, w), BF) for w in widths], [], dp_index, *pieces)


def scatter_rows(grad, dp_index, y_count):
    count = lax.axis_size("dp")
    rows = grad.shape[0] // count
    z_count = count // y_count
    z, y = dp_index // y_count, dp_index % y_count
    grid = grad.reshape(z_count, y_count, rows, grad.shape[1])
    total = lax.dynamic_index_in_dim(grid, y, 1, keepdims=False).astype(F32)
    for step in range(1, y_count):
        out = lax.dynamic_index_in_dim(grid, y ^ step, 1, keepdims=False)
        total = total + swap(out, "dp", step).astype(F32)
    low = total.astype(BF)
    own = lax.dynamic_index_in_dim(total, z, 0, keepdims=False)
    for step in range(1, z_count):
        out = lax.dynamic_index_in_dim(low, z ^ step, 0, keepdims=False)
        own = own + swap(out, "dp", step * y_count).astype(F32)
    return own


def head_order(block, inverse=False):
    count = lax.axis_size("fsdp")
    me = lax.axis_index("fsdp")
    hd = block.shape[-1] // 3
    if not inverse:
        got = [
            lax.ppermute(block[..., t * hd : (t + 1) * hd], "fsdp", [(j, (3 * j + t) % count) for j in range(count)])
            for t in range(3)
        ]
        kinds = []
        for t in range(3):
            table = np.zeros(count, np.int32)
            for j in range(count):
                table[(3 * j + t) % count] = (3 * j + t) // count
            kinds.append(jnp.asarray(table)[me])
        return jnp.concatenate(
            [sum(jnp.where(kinds[t] == kind, got[t], 0) for t in range(3)) for kind in range(3)], axis=-1
        )
    mine = [block[..., t * hd : (t + 1) * hd] for t in range(3)]
    out = []
    for t in range(3):
        table = np.zeros(count, np.int32)
        for j in range(count):
            table[(3 * j + t) % count] = (3 * j + t) // count
        kind = jnp.asarray(table)[me]
        chosen = sum(jnp.where(kind == other, mine[other], 0) for other in range(3))
        out.append(lax.ppermute(chosen, "fsdp", [((3 * j + t) % count, j) for j in range(count)]))
    return jnp.concatenate(out, axis=-1)


def owners_of(amount, dp_count, fs_count):
    found = []
    half = dp_count // 2
    for k in range(amount):
        found.append((dp_count // 4 + k % half, (2 * (k // half)) % fs_count + (2 * (k // half)) // fs_count))
    return found


def round_up(width):
    return -(-width // LANES) * LANES


def push_pieces(pieces, dp_count, fs_count):
    amount = len(pieces)
    widths = [p.shape[1] for p in pieces]
    rows = pieces[0].shape[0]
    wide = max(widths)
    devices = dp_count * fs_count
    owners = owners_of(amount, dp_count, fs_count)

    def body(*refs):
        srcs, out, send_sem, recv_sem = refs[:amount], refs[amount], refs[amount + 1], refs[amount + 2]
        dp, fs = lax.axis_index("dp"), lax.axis_index("fsdp")
        slot = fs * dp_count + dp
        out[...] = jnp.zeros(out.shape, BF)
        barrier = pltpu.get_barrier_semaphore()
        owned = 0
        for k in range(amount):
            mine = (dp == owners[k][0]) & (fs == owners[k][1])
            owned = owned + mine.astype(jnp.int32)

            @pl.when(mine)
            def _():
                def greet(t, carry):
                    @pl.when(t != slot)
                    def _():
                        pl.semaphore_signal(
                            barrier, inc=1, device_id=(lax.rem(t, dp_count), t // dp_count), device_id_type=MESH
                        )

                    return carry

                lax.fori_loop(0, devices, greet, 0)

        pl.semaphore_wait(barrier, amount - owned)
        for k in range(amount):
            mine = (dp == owners[k][0]) & (fs == owners[k][1])
            copy = pltpu.make_async_remote_copy(
                src_ref=srcs[k],
                dst_ref=out.at[slot, :, 0 : widths[k]],
                send_sem=send_sem.at[k],
                recv_sem=recv_sem,
                device_id=owners[k],
                device_id_type=MESH,
            )

            @pl.when(jnp.logical_not(mine))
            def _():
                copy.start()

            @pl.when(mine)
            def _():
                out[slot, :, 0 : widths[k]] = srcs[k][...]

        for k in range(amount):
            mine = (dp == owners[k][0]) & (fs == owners[k][1])

            @pl.when(mine)
            def _():
                landed = out.at[0 : devices - 1, :, 0 : widths[k]]
                pltpu.make_async_copy(landed, landed, recv_sem).wait()

            @pl.when(jnp.logical_not(mine))
            def _():
                pltpu.make_async_copy(srcs[k], srcs[k], send_sem.at[k]).wait()

    return pl.pallas_call(
        body,
        out_shape=jax.ShapeDtypeStruct((devices, rows, wide), BF),
        in_specs=[vmem()] * amount,
        out_specs=vmem(),
        scratch_shapes=[pltpu.SemaphoreType.DMA((amount,)), pltpu.SemaphoreType.DMA],
        compiler_params=pltpu.CompilerParams(collective_id=1, has_side_effects=True, vmem_limit_bytes=VMEM_BYTES),
        name="push_pieces",
    )(*pieces)


def orthogonalize(own, stacked):
    count, rows, wide = stacked.shape
    coef_a, coef_b, coef_c = NS_COEFS

    def body(own_ref, in_ref, out, norm, x):
        @pl.when(own_ref[0] > 0)
        def _():
            for at in range(count):
                x[:, at * wide : (at + 1) * wide] = in_ref[at]
            square = jnp.zeros((1, 1), F32)
            for r in range(0, rows, 64):
                block = x[r : r + 64, :].astype(F32)
                square = square + jnp.sum(jnp.sum(block * block, axis=0, keepdims=True), axis=1, keepdims=True)
            length = jnp.sqrt(square)
            norm[...] = jnp.broadcast_to(length, norm.shape)
            scale = 1.0 / (length + NORM_EPS)
            for turn in range(NS_STEPS):
                gram = dot_nt(x[...], x[...])
                if turn == 0:
                    gram = gram * (scale * scale)
                gram = gram.astype(BF)
                poly = (coef_b * gram.astype(F32) + coef_c * dot_nn(gram, gram)).astype(BF)
                for at in range(0, count * wide, 512):
                    here = slice(at, at + 512)
                    block = x[:, here]
                    new = coef_a * block.astype(F32) + dot_nn(poly, block)
                    if turn == 0:
                        new = new * scale
                    x[:, here] = new.astype(BF)
            for at in range(count):
                out[at] = x[:, at * wide : (at + 1) * wide]

    return pl.pallas_call(
        body,
        out_shape=[jax.ShapeDtypeStruct(stacked.shape, BF), jax.ShapeDtypeStruct((8, LANES), F32)],
        in_specs=[smem(), vmem()],
        out_specs=[vmem(), vmem()],
        scratch_shapes=[pltpu.VMEM((rows, count * wide), BF)],
        compiler_params=params(),
        name="orthogonalize",
    )(own, stacked)


def return_pieces(ortho, norm, widths, dp_count, fs_count):
    amount = len(widths)
    devices, rows, wide = ortho.shape
    owners = owners_of(amount, dp_count, fs_count)

    def body(src, norm_ref, out, norms, send_sem, recv_sem, norm_send, norm_recv):
        dp, fs = lax.axis_index("dp"), lax.axis_index("fsdp")
        slot = fs * dp_count + dp
        barrier = pltpu.get_barrier_semaphore()
        owned = 0
        for k in range(amount):
            mine = (dp == owners[k][0]) & (fs == owners[k][1])
            owned = owned + mine.astype(jnp.int32)

            @pl.when(jnp.logical_not(mine))
            def _():
                pl.semaphore_signal(barrier, inc=1, device_id=owners[k], device_id_type=MESH)

        @pl.when(owned > 0)
        def _():
            pl.semaphore_wait(barrier, devices - 1)

        for k in range(amount):
            mine = (dp == owners[k][0]) & (fs == owners[k][1])
            width = widths[k]

            @pl.when(mine)
            def _():
                def give(t, carry):
                    @pl.when(t != slot)
                    def _():
                        there = (lax.rem(t, dp_count), t // dp_count)
                        pltpu.make_async_remote_copy(
                            src_ref=src.at[t, :, 0:width],
                            dst_ref=out.at[k, :, 0:width],
                            send_sem=send_sem,
                            recv_sem=recv_sem.at[k],
                            device_id=there,
                            device_id_type=MESH,
                        ).start()
                        pltpu.make_async_remote_copy(
                            src_ref=norm_ref,
                            dst_ref=norms.at[k],
                            send_sem=norm_send,
                            recv_sem=norm_recv.at[k],
                            device_id=there,
                            device_id_type=MESH,
                        ).start()

                    return carry

                lax.fori_loop(0, devices, give, 0)
                out[k, :, 0:width] = src[slot, :, 0:width]
                norms[k] = norm_ref[...]

        for k in range(amount):
            mine = (dp == owners[k][0]) & (fs == owners[k][1])
            width = widths[k]

            @pl.when(jnp.logical_not(mine))
            def _():
                landed = out.at[k, :, 0:width]
                pltpu.make_async_copy(landed, landed, recv_sem.at[k]).wait()
                pltpu.make_async_copy(norms.at[k], norms.at[k], norm_recv.at[k]).wait()

            @pl.when(mine)
            def _():
                left = src.at[0 : devices - 1, :, 0:width]
                pltpu.make_async_copy(left, left, send_sem).wait()
                def drain(t, carry):
                    pltpu.make_async_copy(norm_ref, norm_ref, norm_send).wait()
                    return carry

                lax.fori_loop(0, devices - 1, drain, 0)

    return pl.pallas_call(
        body,
        out_shape=[jax.ShapeDtypeStruct((amount, rows, wide), BF), jax.ShapeDtypeStruct((amount, 8, LANES), F32)],
        in_specs=[vmem(), vmem()],
        out_specs=[vmem(), vmem()],
        scratch_shapes=[
            pltpu.SemaphoreType.DMA,
            pltpu.SemaphoreType.DMA((amount,)),
            pltpu.SemaphoreType.DMA,
            pltpu.SemaphoreType.DMA((amount,)),
        ],
        compiler_params=pltpu.CompilerParams(collective_id=2, has_side_effects=True, vmem_limit_bytes=VMEM_BYTES),
        name="return_pieces",
    )(ortho, norm)


def rope_tables(total, hd):
    half = HEAD // 2
    frequency = (np.float32(10000.0) ** (-np.arange(half, dtype=np.float32) / np.float32(half))).astype(np.float32)
    angle = (np.arange(total, dtype=np.float32)[:, None] * frequency[None, :]).astype(np.float32)
    cos, sin = np.cos(angle), np.sin(angle)
    cos = np.tile(np.concatenate([cos, cos], axis=1), (1, hd // HEAD))
    sin = np.tile(np.concatenate([-sin, sin], axis=1), (1, hd // HEAD))
    return jnp.asarray(cos, F32), jnp.asarray(sin, F32)


def mask_features(segment, docs):
    same = segment[:, None] == jnp.arange(HEAD, dtype=jnp.int32)[None, :]
    used = jnp.arange(HEAD)[None, :] < docs
    fq = jnp.where(used & ~same, MASKED, 0.0).astype(BF)
    fk = same.astype(BF)
    return jnp.concatenate([fq, fq], axis=1), jnp.concatenate([fk, fk], axis=1)


def on_device(
    y_count,
    tokens,
    cotangent,
    doc_triples,
    w_qkv,
    w_out,
    w_in,
    w_down,
    w_pool,
    w_up,
    gains,
    m_qkv,
    m_out,
    m_in,
    m_down,
    m_pool,
    m_up,
    m_gains,
):
    rows, width = tokens.shape
    short = rows // 3
    fs_count, dp_count = lax.axis_size("fsdp"), lax.axis_size("dp")
    me, dp_me = lax.axis_index("fsdp"), lax.axis_index("dp")
    me_arr, dp_arr = me.astype(jnp.int32).reshape(1), dp_me.astype(jnp.int32).reshape(1)
    total, short_total = rows * fs_count, short * fs_count
    hd = width // fs_count
    fj = w_in.shape[2]
    pool_cols = w_pool.shape[1]

    order = head_order(w_qkv.astype(BF))
    gain_pad = jnp.pad(gains.astype(BF), ((0, 0), (0, LANES - 4)))
    first = jnp.concatenate([order[0], gain_pad], axis=1)
    second = jnp.concatenate([w_in[0], w_down[0], w_out[0]], axis=1).astype(BF)
    third = jnp.concatenate([w_pool, w_up, w_in[1], w_down[1], w_out[1]], axis=1).astype(BF)
    third = jnp.concatenate([order[1], third], axis=1)
    tok_pieces = gather_pieces(tokens)
    wqkv0, gain_all = assemble_rows(dp_arr, gather_rows(first, y_count), [3 * hd, LANES])
    wi0, wd0, wo0 = assemble_rows(dp_arr, gather_rows(second, y_count), [fj, fj, hd])
    wqkv1, wp, wu, wi1, wd1, wo1 = assemble_rows(
        dp_arr, gather_rows(third, y_count), [3 * hd, pool_cols, pool_cols, fj, fj, hd]
    )
    gain_rows = gain_all[:, 0:4].astype(F32).T
    gain = [gain_rows[k : k + 1] for k in range(4)]
    wo0_p, wo1_p = gather_pieces(wo0), gather_pieces(wo1)
    wp_p, wu_p = gather_pieces(wp), gather_pieces(wu)

    ends = jnp.cumsum(doc_triples[0]).astype(jnp.int32)
    short_all = jnp.arange(short_total, dtype=jnp.int32)
    reached = short_all[:, None] >= ends[None, :]
    short_segment = jnp.sum(reached.astype(jnp.int32), axis=1)
    segment = jnp.repeat(short_segment, 3)
    begins = jnp.any(short_all[:, None] == ends[None, :], axis=1) | (short_all == 0)
    gate = jnp.pad(jnp.where(begins, 0.0, 1.0).astype(F32), (0, HALO))
    gate = lax.dynamic_slice(gate, (me * short,), (short + HALO,))[:, None]
    docs = doc_triples.shape[1]
    fq0, fk0 = mask_features(segment, docs)
    fq1, fk1 = mask_features(short_segment, docs)
    cos0, sin0 = rope_tables(total, hd)
    cos1, sin1 = cos0[:short_total], sin0[:short_total]

    n1, qkv, att = attn_forward(me_arr, tok_pieces, gain[0], wqkv0, fq0, fk0, cos0, sin0)
    n2, att_rel, wo_own, mid, keep, send = mix_forward(
        me_arr, tok_pieces, gather_pieces(att), wo0_p, wi0, wd0, gain[1], HALO
    )
    total_in, got = finish_scatter(keep, send)
    after, z_blocks, s0 = pool_forward(me_arr, mid, total_in, got, gate, wp_p)
    s0_p = gather_pieces(s0)
    z_p = exchange_blocks(z_blocks, me)
    c_blocks, ds1, ds1_low = up_backward(me_arr, cotangent, wu_p)
    c_p = exchange_blocks(c_blocks, me)
    ds1_p = gather_pieces(ds1_low)
    n1b, qkvb, attb = attn_forward(me_arr, s0_p, gain[2], wqkv1, fq1, fk1, cos1, sin1)
    n2b, attb_rel, wob_own, midb, keep, send = mix_forward(
        me_arr, s0_p, gather_pieces(attb), wo1_p, wi1, wd1, gain[3], 0
    )
    total_in, got = finish_scatter(keep, send)
    s1, layer_out = up_forward(me_arr, midb, total_in, got, after, wu_p)
    s1_p = gather_pieces(s1)
    g_up = dot_tn(jnp.concatenate(s1_p), jnp.concatenate(c_p))

    def block_back(d_pieces, above, n1, n2, att_rel, wo_own, wqkv, wi, wd, qkv, mid, own_in, gain_one, gain_two, tables):
        whole, hid, dpre, keep, send = mix_backward(me_arr, d_pieces, n2, wi, wd)
        g_down = dot_tn(whole, hid)
        g_in = dot_tn(n2, dpre)
        total_in, got = finish_scatter(keep, send)
        dm, dm_low, dgain_two = norm_backward(me_arr, mid, gain_two, total_in, got, above)
        da_all, dqkv, keep, send = attn_backward(me_arr, gather_pieces(dm_low), qkv, wo_own, wqkv, *tables)
        g_qkv = dot_tn(n1, dqkv)
        own = lax.dynamic_slice(da_all, (0, me * hd), (da_all.shape[0], hd))
        g_out = dot_tn(att_rel, own).reshape(fs_count, hd, hd)
        g_out = jnp.concatenate(
            [lax.dynamic_index_in_dim(g_out, me ^ k, 0, keepdims=False) for k in range(fs_count)], axis=0
        )
        total_in, got = finish_scatter(keep, send)
        dr, dr_low, dgain_one = norm_backward(me_arr, own_in, gain_one, total_in, got, dm)
        return dr, dr_low, (g_qkv, g_out, g_in, g_down), (dgain_one, dgain_two)

    _, ds0, grads_b, dgain_b = block_back(
        ds1_p,
        ds1,
        n1b,
        n2b,
        attb_rel,
        wob_own,
        wqkv1,
        wi1,
        wd1,
        qkvb,
        midb,
        s0,
        gain[2],
        gain[3],
        (fq1, fk1, cos1, sin1),
    )
    ds0_next = lax.ppermute(ds0[:HALO], "fsdp", [(i + 1, i) for i in range(fs_count - 1)])
    da, da_low = pool_backward(me_arr, ds0, ds0_next, gate, wp_p, cotangent)
    ds0_p = gather_pieces(ds0)
    g_pool = dot_tn(jnp.concatenate(ds0_p), jnp.concatenate(z_p))
    group_b = jnp.concatenate([grads_b[0], g_pool, g_up, grads_b[2], grads_b[3], grads_b[1]], axis=1).astype(BF)
    sum_b = scatter_rows(group_b, dp_me, y_count)

    grad_in, _, grads_a, dgain_a = block_back(
        gather_pieces(da_low),
        da,
        n1,
        n2,
        att_rel,
        wo_own,
        wqkv0,
        wi0,
        wd0,
        qkv,
        mid[HALO:],
        tokens,
        gain[0],
        gain[1],
        (fq0, fk0, cos0, sin0),
    )
    sum_ff = scatter_rows(jnp.concatenate([grads_a[2], grads_a[3]], axis=1).astype(BF), dp_me, y_count)
    sum_at = scatter_rows(jnp.concatenate([grads_a[0], grads_a[1]], axis=1).astype(BF), dp_me, y_count)

    dgain = jnp.concatenate([dgain_a[0][:1], dgain_a[1][:1], dgain_b[0][:1], dgain_b[1][:1]], axis=0)
    bit = 1
    while bit < fs_count:
        dgain = dgain + swap(dgain, "fsdp", bit)
        bit *= 2
    own_rows = width // dp_count
    dgain_t = jnp.pad(dgain.T.astype(BF), ((0, 0), (0, LANES - 4)))
    gain_total = scatter_rows(dgain_t, dp_me, y_count)[:, 0:4]
    gain_moments = GAIN_DECAY * m_gains + gain_total
    new_gains = gains - GAIN_RATE * gain_moments

    at = 3 * hd
    qkv_b = sum_b[:, 0:at]
    pool_g, up_g = sum_b[:, at : at + pool_cols], sum_b[:, at + pool_cols : at + 2 * pool_cols]
    at += 2 * pool_cols
    in_b, down_b, out_b = sum_b[:, at : at + fj], sum_b[:, at + fj : at + 2 * fj], sum_b[:, at + 2 * fj :]
    qkv_g = head_order(jnp.stack([sum_at[:, : 3 * hd], qkv_b]), inverse=True)
    out_g = jnp.stack([sum_at[:, 3 * hd :], out_b])
    in_g = jnp.stack([sum_ff[:, :fj], in_b])
    down_g = jnp.stack([sum_ff[:, fj:], down_b])
    old = (m_qkv, m_out, m_in, m_down, m_pool, m_up)
    moments = [MOMENT_DECAY * m + g for m, g in zip(old, (qkv_g, out_g, in_g, down_g, pool_g, up_g))]

    listed = [(2, 0), (2, 1), (3, 0), (3, 1), (0, 0), (0, 1), (4, None), (5, None), (1, 0), (1, 1)]

    def piece_of(arrays, kind, blk):
        return arrays[kind] if blk is None else arrays[kind][blk]

    pieces, widths = [], []
    for kind, blk in listed:
        piece = piece_of(moments, kind, blk).astype(BF)
        wide = round_up(piece.shape[1])
        widths.append(wide)
        pieces.append(jnp.pad(piece, ((0, 0), (0, wide - piece.shape[1]))))
    pushed = push_pieces(pieces, dp_count, fs_count)
    owned = jnp.zeros((), jnp.bool_)
    for o_dp, o_fs in owners_of(len(listed), dp_count, fs_count):
        owned = owned | ((dp_me == o_dp) & (me == o_fs))
    stacked = pushed.reshape(fs_count, width, pushed.shape[2])
    ortho, norm = orthogonalize(owned.astype(jnp.int32).reshape(1), stacked)
    results, norms = return_pieces(ortho.reshape(pushed.shape), norm, widths, dp_count, fs_count)

    weights = (w_qkv, w_out, w_in, w_down, w_pool, w_up)
    all_tokens = float(total * dp_count)
    new_parts, rms = {}, {}
    for k, (kind, blk) in enumerate(listed):
        old_part = piece_of(weights, kind, blk)
        new_parts[kind, blk] = old_part - STEP_SCALES[kind] * results[k, :, : old_part.shape[1]].astype(F32)
        entries = float(old_part.size * fs_count * dp_count) * all_tokens
        rms[kind, blk] = norms[k, 0, 0] / np.float32(entries**0.5)
    new_weights = [jnp.stack([new_parts[kind, 0], new_parts[kind, 1]]) for kind in range(4)]
    new_weights += [new_parts[4, None], new_parts[5, None]]
    moment_rms = jnp.stack(
        [rms[kind, blk] for kind in range(4) for blk in range(2)] + [rms[4, None], rms[5, None]]
    )
    return (layer_out, grad_in, *moments, *new_weights, gain_moments, new_gains, moment_rms)


def solution(mesh):
    by_row, by_dp = P(("dp", "fsdp"), None), P("dp", None)
    stacked, flat = P(None, "dp", "fsdp"), P("dp", "fsdp")
    matrices = (stacked,) * 4 + (flat,) * 2
    y_count = max(1, mesh.shape["fsdp"] // 2)
    return jax.shard_map(
        functools.partial(on_device, y_count),
        mesh=mesh,
        in_specs=(by_row, by_row, by_dp, *matrices, by_dp, *matrices, by_dp),
        out_specs=(by_row, by_row, *matrices, *matrices, by_dp, by_dp, P()),
        check_vma=False,
    )
```

```python
import functools

import jax
import jax.numpy as jnp
import numpy as np
from jax import lax
from jax.experimental import pallas as pl
from jax.experimental.pallas import tpu as pltpu
from jax.sharding import PartitionSpec as P

HEAD = 64
NS_STEPS = 5
NS_COEFS = (3.4445, -4.775, 2.0315)
STEP_SCALES = (0.8660254, 1.4142136, 1.0, 0.5, 0.5, 0.8660254)
MOMENT_DECAY = 0.95
GAIN_DECAY = 0.9
GAIN_RATE = 0.001
LN_EPS = 1e-05
NORM_EPS = 1e-07
MASKED = -1e30
HALO = 16
QB = 256
LANES = 128
VMEM_BYTES = 56 << 20
BF = jnp.bfloat16
F32 = jnp.float32
MESH = pl.DeviceIdType.MESH


def dot_nn(left, right):
    return lax.dot_general(left, right, (((1,), (0,)), ((), ())), preferred_element_type=F32)


def dot_nt(left, right):
    return lax.dot_general(left, right, (((1,), (1,)), ((), ())), preferred_element_type=F32)


def dot_tn(left, right):
    return lax.dot_general(left, right, (((0,), (0,)), ((), ())), preferred_element_type=F32)


def layer_norm(values, gain):
    mean = jnp.mean(values, axis=-1, keepdims=True)
    centred = values - mean
    spread = jnp.mean(centred * centred, axis=-1, keepdims=True)
    return centred * lax.rsqrt(spread + LN_EPS) * gain


def layer_norm_back(values, gain, grad):
    mean = jnp.mean(values, axis=-1, keepdims=True)
    centred = values - mean
    spread = jnp.mean(centred * centred, axis=-1, keepdims=True)
    scale = lax.rsqrt(spread + LN_EPS)
    unit = centred * scale
    scaled = grad * gain
    part = jnp.mean(scaled, axis=-1, keepdims=True)
    along = jnp.mean(scaled * unit, axis=-1, keepdims=True)
    return scale * (scaled - part - unit * along), grad * unit


def gelu(values):
    return 0.5 * values * (1.0 + jnp.tanh(0.7978845608028654 * (values + 0.044715 * values * values * values)))


def gelu_both(values):
    square = values * values
    turn = jnp.tanh(0.7978845608028654 * (values + 0.044715 * values * square))
    slope = 0.7978845608028654 * (1.0 + 3.0 * 0.044715 * square)
    half = 0.5 * (1.0 + turn)
    return values * half, half + 0.5 * values * (1.0 - turn * turn) * slope


def partner(values):
    width = values.shape[1]
    if width == LANES:
        lane = lax.broadcasted_iota(jnp.int32, values.shape, 1)
        ahead = pltpu.roll(values, LANES - HEAD // 2, 1)
        behind = pltpu.roll(values, HEAD // 2, 1)
        return jnp.where(lane % HEAD < HEAD // 2, ahead, behind)
    parts = []
    for at in range(0, width, HEAD):
        parts += [values[:, at + HEAD // 2 : at + HEAD], values[:, at : at + HEAD // 2]]
    return jnp.concatenate(parts, axis=1)


def widen(values):
    rows, width = values.shape
    if width >= LANES:
        return values
    return jnp.concatenate([values, jnp.zeros((rows, LANES - width), values.dtype)], axis=1)


def params():
    return pltpu.CompilerParams(vmem_limit_bytes=VMEM_BYTES)


def smem():
    return pl.BlockSpec(memory_space=pltpu.SMEM)


def vmem():
    return pl.BlockSpec(memory_space=pltpu.VMEM)


def cost(flops, moved):
    return pl.CostEstimate(flops=int(flops), bytes_accessed=int(moved), transcendentals=0)


def local_kernel(body, name, outs, scratch, me, *arrays, flops=0):
    moved = sum(a.size * a.dtype.itemsize for a in arrays)
    moved += sum(int(np.prod(s)) * jnp.dtype(t).itemsize for s, t in outs)
    return pl.pallas_call(
        body,
        out_shape=[jax.ShapeDtypeStruct(s, t) for s, t in outs],
        in_specs=[smem()] + [vmem()] * len(arrays),
        out_specs=[vmem()] * len(outs),
        scratch_shapes=[pltpu.VMEM(s, t) for s, t in scratch],
        compiler_params=params(),
        cost_estimate=cost(flops, moved),
        name=name,
    )(me, *arrays)


def at_rows(me, step, rows):
    return pl.multiple_of((me ^ step) * rows, 16)


def head_inputs(qs, ks, rows, q, k, fq, fk, heads):
    lane = lax.broadcasted_iota(jnp.int32, (q.shape[0], LANES), 1)
    q, k = widen(q), widen(k)
    for h in range(heads):
        mine = lane // HEAD == h
        qs[h, rows, :] = jnp.where(mine, q * 0.125, fq).astype(BF)
        ks[h, rows, :] = jnp.where(mine, k, fk).astype(BF)


def scores_t(ks, qs, h, start, stop):
    top = dot_nt(ks[h, 0:stop, :], qs[h, start:stop, :])
    key = lax.broadcasted_iota(jnp.int32, (stop - start, stop - start), 0)
    query = lax.broadcasted_iota(jnp.int32, (stop - start, stop - start), 1)
    last = jnp.where(key <= query, top[start:, :], MASKED)
    if start == 0:
        return last
    return jnp.concatenate([top[:start, :], last], axis=0)


def attn_forward(me, pieces, gain, w_qkv, fq, fk, cos, sin):
    count = len(pieces)
    rows, width = pieces[0].shape
    total = rows * count
    hd = w_qkv.shape[1] // 3
    heads = hd // HEAD
    blk = min(QB, total)

    def body(me_ref, *refs):
        piece_refs = refs[:count]
        gain_ref, w_ref, fq_ref, fk_ref, cos_ref, sin_ref, n1, qkv, out, qs, ks, vt = refs[count:]
        me_now = me_ref[0]
        for step in range(count):
            base = at_rows(me_now, step, rows)
            for r in range(0, rows, LANES):
                block = piece_refs[step][r : r + LANES, :].astype(F32)
                n1[pl.ds(base + r, LANES), :] = layer_norm(block, gain_ref[...]).astype(BF)
        for r in range(0, total, blk):
            here = slice(r, r + blk)
            got = dot_nn(n1[here, :], w_ref[...])
            q, k, v = got[:, :hd], got[:, hd : 2 * hd], got[:, 2 * hd :]
            q = (q * cos_ref[here, :] + partner(q) * sin_ref[here, :]).astype(BF)
            k = (k * cos_ref[here, :] + partner(k) * sin_ref[here, :]).astype(BF)
            qkv[here, 0:hd] = q
            qkv[here, hd : 2 * hd] = k
            qkv[here, 2 * hd : 3 * hd] = v.astype(BF)
            head_inputs(
                qs, ks, here, q.astype(F32), k.astype(F32), fq_ref[here, :].astype(F32), fk_ref[here, :].astype(F32), heads
            )
            vt[:, here] = v.T.astype(BF)
        for r in range(0, total, blk):
            stop = r + blk
            found = []
            for h in range(heads):
                s = scores_t(ks, qs, h, r, stop)
                e = jnp.exp(s - jnp.max(s, axis=0, keepdims=True))
                p = (e * (1.0 / jnp.sum(e, axis=0, keepdims=True))).astype(BF)
                found.append(dot_nn(vt[h * HEAD : (h + 1) * HEAD, 0:stop], p))
            out[r:stop, :] = jnp.concatenate(found, axis=0).T.astype(BF)

    return local_kernel(
        body,
        "attn_forward",
        [((total, width), BF), ((total, 3 * hd), BF), ((total, hd), BF)],
        [((heads, total, LANES), BF), ((heads, total, LANES), BF), ((hd, total), BF)],
        me,
        *pieces,
        gain,
        w_qkv,
        fq,
        fk,
        cos,
        sin,
        flops=8e9,
    )


def attn_backward(me, pieces, qkv, wo_own, w_qkv, fq, fk, cos, sin):
    count = len(pieces)
    rows, width = pieces[0].shape
    total = rows * count
    hd = w_qkv.shape[1] // 3
    heads = hd // HEAD
    blk = min(QB, total)

    def body(me_ref, *refs):
        piece_refs = refs[:count]
        qkv_ref, wo_ref, w_ref, fq_ref, fk_ref, cos_ref, sin_ref = refs[count : count + 7]
        whole, dqkv, keep, send, qs, ks, qz, doz, kt, dk, dv = refs[count + 7 :]
        me_now = me_ref[0]
        for step in range(count):
            base = at_rows(me_now, step, rows)
            whole[pl.ds(base, rows), :] = piece_refs[step][...]
        lane = lax.broadcasted_iota(jnp.int32, (blk, LANES), 1)
        for r in range(0, total, blk):
            here = slice(r, r + blk)
            q = qkv_ref[here, 0:hd].astype(F32)
            k = qkv_ref[here, hd : 2 * hd].astype(F32)
            head_inputs(qs, ks, here, q, k, fq_ref[here, :].astype(F32), fk_ref[here, :].astype(F32), heads)
            kt[:, here] = k.T.astype(BF)
            do = widen(dot_nt(whole[here, :], wo_ref[...]))
            q = widen(q)
            for h in range(heads):
                mine = lane // HEAD == h
                qz[h, here, :] = jnp.where(mine, q, 0.0).astype(BF)
                doz[h, here, :] = jnp.where(mine, do, 0.0).astype(BF)
            dk[here, :] = jnp.zeros((blk, LANES), F32)
            dv[here, :] = jnp.zeros((blk, LANES), F32)
        for r in range(0, total, blk):
            stop = r + blk
            here = slice(r, stop)
            found = []
            add_k = None
            for h in range(heads):
                s = scores_t(ks, qs, h, r, stop)
                e = jnp.exp(s - jnp.max(s, axis=0, keepdims=True))
                p = e * (1.0 / jnp.sum(e, axis=0, keepdims=True))
                v = widen(qkv_ref[0:stop, 2 * hd : 3 * hd])
                dp = dot_nt(v, doz[h, here, :])
                mid = jnp.sum(p * dp, axis=0, keepdims=True)
                dr = (p * (dp - mid) * 0.125).astype(BF)
                part_v = dot_nn(p.astype(BF), doz[h, here, :])
                part_k = dot_nn(dr, qz[h, here, :])
                add_v = part_v if add_k is None else add_v + part_v
                add_k = part_k if add_k is None else add_k + part_k
                found.append(dot_nn(kt[h * HEAD : (h + 1) * HEAD, 0:stop], dr))
            dk[0:stop, :] += add_k
            dv[0:stop, :] += add_v
            dq = jnp.concatenate(found, axis=0).T
            dqkv[here, 0:hd] = (dq * cos_ref[here, :] - partner(dq) * sin_ref[here, :]).astype(BF)
        for r in range(0, total, blk):
            here = slice(r, r + blk)
            grad = dk[here, 0:hd]
            dqkv[here, hd : 2 * hd] = (grad * cos_ref[here, :] - partner(grad) * sin_ref[here, :]).astype(BF)
            dqkv[here, 2 * hd : 3 * hd] = dv[here, 0:hd].astype(BF)
        for step in range(count):
            base = at_rows(me_now, step, rows)
            part = dot_nt(dqkv[pl.ds(base, rows), :], w_ref[...])
            if step % 2:
                send[step // 2] = part.astype(BF)
            else:
                keep[step // 2] = part

    return local_kernel(
        body,
        "attn_backward",
        [
            ((total, width), BF),
            ((total, 3 * hd), BF),
            ((count // 2, rows, width), F32),
            ((count // 2, rows, width), BF),
        ],
        [((heads, total, LANES), BF)] * 4 + [((hd, total), BF), ((total, LANES), F32), ((total, LANES), F32)],
        me,
        *pieces,
        qkv,
        wo_own,
        w_qkv,
        fq,
        fk,
        cos,
        sin,
        flops=16e9,
    )


def mix_forward(me, pieces, att, wo, wi, wd, gain, halo):
    count = len(pieces)
    rows, width = pieces[0].shape
    total = rows * count
    hd = att[0].shape[1]
    fj = wi.shape[1]
    long_rows = rows + halo

    def body(me_ref, *refs):
        piece_refs, refs = refs[:count], refs[count:]
        att_refs, refs = refs[:count], refs[count:]
        wo_refs, refs = refs[:count], refs[count:]
        wi_ref, wd_ref, gain_ref, n2, att_rel, wo_own, mid, keep, send, blocks, full, turned, m_all, part_all = refs
        me_now = me_ref[0]
        for step in range(count):
            blocks[me_now ^ step] = wo_refs[step][...]
            att_rel[:, step * hd : (step + 1) * hd] = att_refs[step][...]
        for at in range(count):
            full[:, at * hd : (at + 1) * hd] = blocks[at]
        for step in range(count):
            base = at_rows(me_now, step, hd)
            turned[step * hd : (step + 1) * hd, :] = full[pl.ds(base, hd), :]
        wo_own[...] = turned[0:hd, :]
        for step in range(count):
            base = at_rows(me_now, step, rows)
            for r in range(0, rows, LANES):
                at = pl.ds(base + r, LANES)
                m = piece_refs[step][r : r + LANES, :].astype(F32) + dot_nn(att_rel[at, :], turned[...])
                m_all[at, :] = m
                low = layer_norm(m, gain_ref[...]).astype(BF)
                n2[step * rows + r : step * rows + r + LANES, :] = low
                hid = gelu(dot_nn(low, wi_ref[...])).astype(BF)
                part_all[at, :] = dot_nt(hid, wd_ref[...])
        for step in range(count):
            base = at_rows(me_now, step, rows)
            out = (send if step % 2 else keep).at[step // 2]
            out[halo:long_rows, :] = part_all[pl.ds(base, rows), :].astype(out.dtype)
            if halo:
                before = pl.multiple_of(lax.rem(base + total - halo, total), 16)
                out[0:halo, :] = part_all[pl.ds(before, halo), :].astype(out.dtype)
                if step == 0:
                    mid[0:halo, :] = m_all[pl.ds(before, halo), :]
            if step == 0:
                mid[halo:long_rows, :] = m_all[pl.ds(base, rows), :]

    return local_kernel(
        body,
        "mix_forward",
        [
            ((total, width), BF),
            ((total, width), BF),
            ((hd, width), BF),
            ((long_rows, width), F32),
            ((count // 2, long_rows, width), F32),
            ((count // 2, long_rows, width), BF),
        ],
        [
            ((count, width, hd), BF),
            ((width, width), BF),
            ((width, width), BF),
            ((total, width), F32),
            ((total, width), F32),
        ],
        me,
        *pieces,
        *att,
        *wo,
        wi,
        wd,
        gain,
        flops=2 * total * width * (width + 2 * fj),
    )


def mix_backward(me, grads, n2, wi, wd):
    count = len(grads)
    rows, width = grads[0].shape
    total = rows * count
    fj = wi.shape[1]

    def body(me_ref, *refs):
        grad_refs = refs[:count]
        n2_ref, wi_ref, wd_ref, whole, hid, dpre, keep, send = refs[count:]
        for step in range(count):
            out = (send if step % 2 else keep).at[step // 2]
            for r in range(0, rows, LANES):
                at = slice(step * rows + r, step * rows + r + LANES)
                grad = grad_refs[step][r : r + LANES, :]
                whole[at, :] = grad
                value, slope = gelu_both(dot_nn(n2_ref[at, :], wi_ref[...]))
                hid[at, :] = value.astype(BF)
                low = (dot_nn(grad, wd_ref[...]) * slope).astype(BF)
                dpre[at, :] = low
                out[r : r + LANES, :] = dot_nt(low, wi_ref[...]).astype(out.dtype)

    return local_kernel(
        body,
        "mix_backward",
        [
            ((total, width), BF),
            ((total, fj), BF),
            ((total, fj), BF),
            ((count // 2, rows, width), F32),
            ((count // 2, rows, width), BF),
        ],
        [],
        me,
        *grads,
        n2,
        wi,
        wd,
        flops=6 * total * width * fj,
    )


def norm_backward(me, values, gain, total_in, got, above):
    rows, width = values.shape

    def body(me_ref, v_ref, gain_ref, t_ref, got_ref, above_ref, full, low, dgain):
        acc = jnp.zeros((1, width), F32)
        for r in range(0, rows, LANES):
            at = slice(r, r + LANES)
            grad = t_ref[at, :] + got_ref[at, :].astype(F32)
            dx, dg = layer_norm_back(v_ref[at, :].astype(F32), gain_ref[...], grad)
            dx = dx + above_ref[at, :]
            full[at, :] = dx
            low[at, :] = dx.astype(BF)
            acc = acc + jnp.sum(dg, axis=0, keepdims=True)
        dgain[...] = jnp.broadcast_to(acc, (8, width))

    return local_kernel(
        body,
        "norm_backward",
        [((rows, width), F32), ((rows, width), BF), ((8, width), F32)],
        [],
        me,
        values,
        gain,
        total_in,
        got,
        above,
    )


def spread_write(hold, values):
    for c in range(hold.shape[0]):
        hold[c] = values[:, c * LANES : (c + 1) * LANES]


def spread_read(hold):
    return jnp.concatenate([hold[c] for c in range(hold.shape[0])], axis=1)


def strided_read(hold, start, amount):
    return jnp.concatenate([hold[c, pl.ds(start, amount, stride=3), :] for c in range(hold.shape[0])], axis=1)


def strided_write(hold, start, amount, values):
    for c in range(hold.shape[0]):
        hold[c, pl.ds(start, amount, stride=3), :] = values[:, c * LANES : (c + 1) * LANES]


def pool_forward(me, mid, total_in, got, gate, wp):
    count = len(wp)
    long_rows, width = mid.shape
    rows = long_rows - HALO
    short = rows // 3
    cols = wp[0].shape[1]

    def body(me_ref, mid_ref, t_ref, got_ref, gate_ref, *refs):
        wp_refs = refs[:count]
        after, blocks, s0, hold = refs[count:]
        me_now = me_ref[0]
        a = mid_ref[...] + t_ref[...] + got_ref[...].astype(F32)
        spread_write(hold, a)
        after[...] = a[HALO:, :]
        parts = []
        for k in range(3):
            part = strided_read(hold, HALO - 2 + k, short)
            if k < 2:
                part = jnp.where(gate_ref[0:short, :] > 0.0, part, 0.0)
            parts.append(part)
        z = jnp.concatenate(parts, axis=1).astype(BF)
        for at in range(count):
            blocks[at] = z[:, at * cols : (at + 1) * cols]
        acc = jnp.zeros((short, width), F32)
        for step in range(count):
            acc = acc + dot_nt(blocks[me_now ^ step], wp_refs[step][...])
        s0[...] = acc

    return local_kernel(
        body,
        "pool_forward",
        [((rows, width), F32), ((count, short, cols), BF), ((short, width), F32)],
        [((width // LANES, long_rows, LANES), F32)],
        me,
        mid,
        total_in,
        got,
        gate,
        *wp,
        flops=2 * short * width * 3 * width,
    )


def up_backward(me, cot, wu):
    count = len(wu)
    rows, width = cot.shape
    short = rows // 3
    cols = wu[0].shape[1]

    def body(me_ref, cot_ref, *refs):
        wu_refs = refs[:count]
        blocks, full, low, hold = refs[count:]
        me_now = me_ref[0]
        spread_write(hold, cot_ref[...].astype(F32))
        lifted = jnp.concatenate([strided_read(hold, k, short) for k in range(3)], axis=1).astype(BF)
        for at in range(count):
            blocks[at] = lifted[:, at * cols : (at + 1) * cols]
        acc = jnp.zeros((short, width), F32)
        for step in range(count):
            acc = acc + dot_nt(blocks[me_now ^ step], wu_refs[step][...])
        full[...] = acc
        low[...] = acc.astype(BF)

    return local_kernel(
        body,
        "up_backward",
        [((count, short, cols), BF), ((short, width), F32), ((short, width), BF)],
        [((width // LANES, rows, LANES), F32)],
        me,
        cot,
        *wu,
        flops=2 * short * width * 3 * width,
    )


def up_forward(me, mid, total_in, got, after, wu):
    count = len(wu)
    short, width = mid.shape
    rows = short * 3
    cols = wu[0].shape[1]

    def body(me_ref, mid_ref, t_ref, got_ref, after_ref, *refs):
        wu_refs = refs[:count]
        low, out, blocks, hold = refs[count:]
        me_now = me_ref[0]
        s1 = (mid_ref[...] + t_ref[...] + got_ref[...].astype(F32)).astype(BF)
        low[...] = s1
        for step in range(count):
            blocks[me_now ^ step] = dot_nn(s1, wu_refs[step][...])
        lift = jnp.concatenate([blocks[at] for at in range(count)], axis=1)
        for k in range(3):
            strided_write(hold, k, short, lift[:, k * width : (k + 1) * width])
        out[...] = (after_ref[...] + spread_read(hold)).astype(BF)

    return local_kernel(
        body,
        "up_forward",
        [((short, width), BF), ((rows, width), BF)],
        [((count, short, cols), F32), ((width // LANES, rows, LANES), F32)],
        me,
        mid,
        total_in,
        got,
        after,
        *wu,
        flops=2 * short * width * 3 * width,
    )


def pool_backward(me, ds0, ds0_next, gate, wp, cot):
    count = len(wp)
    short, width = ds0.shape
    rows = short * 3
    cols = wp[0].shape[1]

    def body(me_ref, ds0_ref, next_ref, gate_ref, cot_ref, *refs):
        wp_refs = refs[:count]
        full, low, blocks, hold, spread = refs[count:]
        me_now = me_ref[0]
        grad = jnp.concatenate([ds0_ref[...], next_ref[...]], axis=0)
        for step in range(count):
            blocks[me_now ^ step] = dot_nn(grad, wp_refs[step][...])
        for at in range(count):
            hold[:, at * cols : (at + 1) * cols] = blocks[at]
        strided_write(spread, 0, short, hold[0:short, 2 * width : 3 * width])
        open_gate = gate_ref[1 : short + 1, :] > 0.0
        for k in range(2):
            part = hold[1 : short + 1, k * width : (k + 1) * width]
            strided_write(spread, k + 1, short, jnp.where(open_gate, part, 0.0))
        da = cot_ref[...].astype(F32) + spread_read(spread)
        full[...] = da
        low[...] = da.astype(BF)

    return local_kernel(
        body,
        "pool_backward",
        [((rows, width), F32), ((rows, width), BF)],
        [((count, short + HALO, cols), F32), ((short + HALO, 3 * width), F32), ((width // LANES, rows, LANES), F32)],
        me,
        ds0,
        ds0_next,
        gate,
        cot,
        *wp,
        flops=2 * short * width * 3 * width,
    )


def flip(value, step):
    bit = 1
    while bit <= step:
        if step & bit:
            value = value + bit - 2 * bit * lax.rem(lax.div(value, bit), 2)
        bit *= 2
    return value


class Net:
    def __init__(self, send, recv):
        self.send, self.recv, self.used, self.open = send, recv, 0, []

    def make(self, src, dst, device):
        at = self.used
        self.used += 1
        return pltpu.make_async_remote_copy(
            src_ref=src,
            dst_ref=dst,
            send_sem=self.send.at[at],
            recv_sem=self.recv.at[at],
            device_id=device,
            device_id_type=MESH,
        )

    def start(self, src, dst, device):
        copy = self.make(src, dst, device)
        copy.start()
        self.open.append(copy)
        return copy

    def finish(self):
        for copy in self.open:
            copy.wait_send()


class Flight:
    def __init__(self, net, dp, fs, fs_count, pieces, src):
        self.net, self.dp, self.fs, self.pieces = net, dp, fs, pieces
        self.top, self.copies, self.waited = fs_count // 2, {}, set()
        bit = self.top
        while bit:
            self.copies[bit] = net.start(src, pieces.at[bit], (dp, flip(fs, bit)))
            bit //= 2

    def ready(self, step):
        if step and step not in self.waited:
            self.waited.add(step)
            self.copies[step].wait_recv()

    def relay(self):
        known, bit = [self.top], self.top // 2
        while bit:
            fresh = []
            for step in known:
                self.ready(step)
                there = (self.dp, flip(self.fs, bit))
                self.copies[step + bit] = self.net.start(self.pieces.at[step], self.pieces.at[step + bit], there)
                fresh.append(step + bit)
            known = known + [bit] + fresh
            bit //= 2

    def all_ready(self):
        for step in sorted(self.copies):
            self.ready(step)


def doc_bounds(triples, docs):
    lane = lax.broadcasted_iota(jnp.int32, (1, LANES), 1)
    lane = jnp.where(lane >= HEAD, lane - HEAD, lane)
    first = jnp.full((1, LANES), -1, jnp.int32)
    end = jnp.full((1, LANES), -1, jnp.int32)
    at = jnp.int32(0)
    for j in range(docs):
        here = lane == j
        first = jnp.where(here, at, first)
        at = at + triples[0, j]
        end = jnp.where(here, at, end)
    return first, end, lane


def softmax_block(ks, qs, h, r, stop):
    s = scores_t(ks, qs, h, r, stop)
    e = jnp.exp(s - jnp.max(s, axis=0, keepdims=True))
    return e, 1.0 / jnp.sum(e, axis=0, keepdims=True)


def forward_one(y_count, dp_count, fs_count, tokens, triples, weights, gains, cos, sin):
    rows, width = tokens.shape
    total, short = rows * fs_count, rows // 3
    long_rows = rows + HALO
    wqkv, wout, win, wdown, wpool, wup = weights
    rw = wqkv.shape[1]
    hd, fj, pc = wout.shape[2], win.shape[2], wpool.shape[1]
    heads = hd // HEAD
    docs = triples.shape[1]
    z_count = dp_count // y_count
    cw = pc + hd + 2 * fj
    blk = QB
    sems = 64 + 14 * dp_count

    def body(
        tok, triples_ref, q_in, o_in, i_in, d_in, p_in, u_in, g_in, cos_ref, sin_ref,
        n1, qkv, att_rel, wo_own, n2, mid, after, z_out, s0_out, wq_out, wb, wp, wq1_out, wc, gain_out,
        toks, st_q, wq0, wq1, gall, wo, wo_at, att, qs, ks, vt, turned, hold, work, low, part, m_tail, part_tail,
        sbuf, rbuf, xsend, xrecv, acc, thin, send_sem, recv_sem,
    ):
        dp, fs = lax.axis_index("dp"), lax.axis_index("fsdp")
        net = Net(send_sem, recv_sem)

        def own(buf):
            return buf.at[pl.ds(pl.multiple_of(dp * rw, 16), rw), :]

        def of(buf, step):
            return buf.at[pl.ds(pl.multiple_of(flip(dp, step) * rw, 16), rw), :]

        for b in range(2):
            for t in range(3):
                st_q[b, t] = q_in[b, :, t * hd : (t + 1) * hd].astype(BF)
        here = pl.ds(pl.multiple_of(dp * rw, 16), rw)
        gall[here, :] = jnp.concatenate([g_in[...], jnp.zeros((rw, LANES - 4), F32)], axis=1).astype(BF)
        wo[0, here, :] = o_in[0].astype(BF)
        wb[here, 0:fj] = i_in[0].astype(BF)
        wb[here, fj : 2 * fj] = d_in[0].astype(BF)
        wp[0, here, :] = p_in[...].astype(BF)
        wc[here, 0:pc] = u_in[...].astype(BF)
        wc[here, pc : pc + hd] = o_in[1].astype(BF)
        wc[here, pc + hd : pc + hd + fj] = i_in[1].astype(BF)
        wc[here, pc + hd + fj : cw] = d_in[1].astype(BF)

        barrier = pltpu.get_barrier_semaphore()
        for m in range(z_count):
            for e in range(fs_count):
                if m or e:
                    there = (flip(dp, m * y_count), flip(fs, e))
                    pl.semaphore_signal(barrier, inc=1, device_id=there, device_id_type=MESH)
        for j in range(1, y_count):
            pl.semaphore_signal(barrier, inc=1, device_id=(flip(dp, j), fs), device_id_type=MESH)
        pl.semaphore_wait(barrier, z_count * fs_count - 1 + y_count - 1)

        def along_z(bufs):
            found = [[] for _ in range(z_count)]
            for m in range(1, z_count):
                for buf in bufs:
                    found[m].append(net.start(own(buf), own(buf), (flip(dp, m * y_count), fs)))
            return found

        def along_y(bufs, m):
            return [
                net.start(of(buf, m * y_count), of(buf, m * y_count), (flip(dp, j), fs))
                for j in range(1, y_count)
                for buf in bufs
            ]

        def wait_all(copies):
            for copy in copies:
                copy.wait_recv()

        def heads_along_z(b, wq):
            found = []
            for m in range(z_count):
                line = []
                for t in range(3):
                    place = 3 * fs + t
                    kind, to = lax.div(place, fs_count), lax.rem(place, fs_count)
                    copy = net.make(st_q.at[b, t], wq.at[kind, here, :], (flip(dp, m * y_count), to))
                    if m == 0:

                        @pl.when(to != fs)
                        def _():
                            copy.start()

                        @pl.when(to == fs)
                        def _():
                            wq[kind, here, :] = st_q[b, t]

                        line.append((copy, to != fs))
                    else:
                        copy.start()
                        net.open.append(copy)
                        line.append((copy, None))
                found.append(line)
            return found

        def heads_along_y(wq, line, m):
            for copy, when in line:
                if when is None:
                    copy.wait_recv()
                else:

                    @pl.when(when)
                    def _():
                        copy.wait_recv()
                        copy.wait_send()

            at = pl.ds(pl.multiple_of(flip(dp, m * y_count) * rw, 16), rw)
            return [
                net.start(wq.at[:, at, :], wq.at[:, at, :], (flip(dp, j), fs)) for j in range(1, y_count)
            ]


        def spread(pieces, src):
            return Flight(net, dp, fs, fs_count, pieces, src)

        heads0 = heads_along_z(0, wq0)
        gz = along_z([gall])
        y0 = along_y([gall], 0)
        tk = spread(toks, tok)
        toks[0] = tok[...]
        oz = along_z([wo.at[0]])
        y1 = along_y([wo.at[0]], 0)
        lane_first, lane_end, lane = doc_bounds(triples_ref, docs)
        for m in range(z_count):
            y0 += heads_along_y(wq0, heads0[m], m)
            if m:
                wait_all(gz[m])
                y0 += along_y([gall], m)
        bz = along_z([wb])
        y2 = along_y([wb], 0)
        for m in range(1, z_count):
            wait_all(oz[m])
            y1 += along_y([wo.at[0]], m)
        tk.relay()
        wait_all(y0)
        gain_rows = gall[...].astype(F32).T[0:8, :]
        gain_out[...] = gain_rows
        for t in range(3):
            wq_out[:, t * hd : (t + 1) * hd] = wq0[t]
        for e in range(fs_count):
            tk.ready(e)
            base = pl.multiple_of(flip(fs, e) * rows, 16)
            for r in range(0, rows, LANES):
                block = toks[e, r : r + LANES, :].astype(F32)
                n1[pl.ds(base + r, LANES), :] = layer_norm(block, gain_rows[0:1]).astype(BF)

        lane_head = lax.broadcasted_iota(jnp.int32, (blk, LANES), 1)
        for r in range(0, total, blk):
            at = slice(r, r + blk)
            got = dot_nn(n1[at, :], wq_out[...])
            q, k, v = got[:, :hd], got[:, hd : 2 * hd], got[:, 2 * hd :]
            q = (q * cos_ref[at, :] + partner(q) * sin_ref[at, :]).astype(BF)
            k = (k * cos_ref[at, :] + partner(k) * sin_ref[at, :]).astype(BF)
            qkv[at, 0:hd] = q
            qkv[at, hd : 2 * hd] = k
            qkv[at, 2 * hd : 3 * hd] = v.astype(BF)
            row = lax.broadcasted_iota(jnp.int32, (blk, LANES), 0) + r
            inside = (row >= 3 * lane_first) & (row < 3 * lane_end)
            fk = jnp.where(inside, 1.0, 0.0)
            fq = jnp.where(inside | (lane >= docs), 0.0, MASKED)
            head_inputs(qs, ks, at, q.astype(F32), k.astype(F32), fq, fk, heads)
            vt[:, at] = v.T.astype(BF)

        flights = []
        for n, r in enumerate(range(0, total, blk)):
            stop = r + blk
            found = []
            for h in range(heads):
                e, inv = softmax_block(ks, qs, h, r, stop)
                found.append(dot_nn(vt[h * HEAD : (h + 1) * HEAD, 0:stop], e.astype(BF)) * inv)
            att[0, r:stop, :] = jnp.concatenate(found, axis=0).T.astype(BF)
            flights.append(spread(att.at[:, r:stop, :], att.at[0, r:stop, :]))
            if n == 0:
                wait_all(y1)
                wo_f = spread(wo, wo.at[0])
            if n == 2:
                for m in range(1, z_count):
                    wait_all(bz[m])
                    y2 += along_y([wb], m)
                wz = along_z([wp.at[0]])
                y3 = along_y([wp.at[0]], 0)
                heads1 = heads_along_z(1, wq1)
                cz = along_z([wc])
                y4 = along_y([wc], 0)
            if n == 3:
                wo_f.relay()
            if n >= 2:
                flights[n - 2].relay()
        for flight in flights[-2:]:
            flight.relay()
        wo_f.all_ready()
        for e in range(fs_count):
            wo_at[flip(fs, e)] = wo[e]
        for e in range(fs_count):
            hold[:, e * hd : (e + 1) * hd] = wo_at[e]
        for e in range(fs_count):
            base = pl.multiple_of(flip(fs, e) * hd, 16)
            turned[e * hd : (e + 1) * hd, :] = hold[pl.ds(base, hd), :]
        wo_own[...] = turned[0:hd, :]
        for flight in flights:
            flight.all_ready()
        for m in range(1, z_count):
            wait_all(wz[m])
            y3 += along_y([wp.at[0]], m)
        wait_all(y2)

        def mix(x_block, o_block, amount, keep_mid, keep_n2, out):
            work[0:amount, 0:width] = x_block.astype(F32) + dot_nn(o_block, turned[...])
            for r in range(0, amount, HEAD):
                m = work[r : r + HEAD, 0:width]
                if keep_mid is not None:
                    keep_mid[r : r + HEAD, :] = m
                value = layer_norm(m, gain_rows[1:2]).astype(BF)
                low[r : r + HEAD, 0:width] = value
                if keep_n2 is not None:
                    keep_n2[r : r + HEAD, :] = value
            work[0:amount, 0:fj] = dot_nn(low[0:amount, 0:width], wb[:, 0:fj])
            for r in range(0, amount, HEAD):
                low[r : r + HEAD, 0:fj] = gelu(work[r : r + HEAD, 0:fj]).astype(BF)
            out[0:amount, :] = dot_nt(low[0:amount, 0:fj], wb[:, fj : 2 * fj])

        for e in range(fs_count):
            at = pl.ds(pl.multiple_of(flip(fs, e) * rows + rows - HALO, 16), HALO)
            for k in range(fs_count):
                att_rel[e * HALO : (e + 1) * HALO, k * hd : (k + 1) * hd] = att[k, at, :]
        tails = jnp.concatenate([toks[e, rows - HALO : rows, :] for e in range(fs_count)], axis=0)
        mix(tails, att_rel[0 : fs_count * HALO, :], fs_count * HALO, m_tail, None, part_tail)

        for e in range(fs_count):
            base = pl.multiple_of(flip(fs, e) * rows, 16)
            for k in range(fs_count):
                att_rel[pl.ds(base, rows), k * hd : (k + 1) * hd] = att[k, pl.ds(base, rows), :]

        def before(e):
            place = flip(fs, e) + fs_count - 1
            place = lax.rem(place, fs_count)
            apart = jnp.int32(0)
            bit = 1
            while bit < fs_count:
                one = lax.rem(lax.div(place, bit), 2)
                two = lax.rem(lax.div(fs, bit), 2)
                apart = apart + bit * lax.rem(one + two, 2)
                bit *= 2
            return pl.multiple_of(apart * HALO, 16)

        def partial_for(e, out):
            base = pl.multiple_of(flip(fs, e) * rows, 16)
            mix(
                toks[e],
                att_rel[pl.ds(base, rows), :],
                rows,
                mid if e == 0 else None,
                n2.at[e * rows : (e + 1) * rows, :],
                part,
            )
            out[0:HALO, :] = part_tail[pl.ds(before(e), HALO), :].astype(out.dtype)
            out[HALO:long_rows, :] = part[0:rows, :].astype(out.dtype)

        half = fs_count // 2
        first_hops = {}
        for j in reversed(range(half)):
            partial_for(2 * j + 1, sbuf.at[j])
            first_hops[j] = net.start(sbuf.at[j], rbuf.at[j], (dp, flip(fs, 1)))
            if j == half - 1:
                for m in range(z_count):
                    y4 += heads_along_y(wq1, heads1[m], m)
                wait_all(y3)
                wp_f = spread(wp, wp.at[0])
            if j:
                partial_for(2 * j, acc.at[j])
                first_hops[j].wait_recv()
                acc[j] = acc[j] + rbuf[j].astype(F32)
                if half == 2:
                    xsend[0] = acc[1].astype(BF)
                    last_hop = net.start(xsend.at[0], xrecv.at[0], (dp, flip(fs, 2)))
            if j == half - 1:
                for m in range(1, z_count):
                    wait_all(cz[m])
                    y4 += along_y([wc], m)
        partial_for(0, acc.at[0])
        first_hops[0].wait_recv()
        acc[0] = acc[0] + rbuf[0].astype(F32)
        wp_f.relay()
        if half > 2:
            bit, active = 2, list(range(half))
            slot = 0
            while bit < fs_count:
                stay = [j for j in active if not (2 * j) & bit]
                hops = {}
                for j in stay:
                    give = j + bit // 2
                    xsend[slot] = acc[give].astype(BF)
                    hops[j] = (net.start(xsend.at[slot], xrecv.at[slot], (dp, flip(fs, bit))), slot)
                    slot += 1
                for j in stay:
                    hops[j][0].wait_recv()
                    acc[j] = acc[j] + xrecv[hops[j][1]].astype(F32)
                active, bit = stay, bit * 2
        elif half == 2:
            last_hop.wait_recv()
            acc[0] = acc[0] + xrecv[0].astype(F32)
        a_tail = acc[0, 0:HALO, :] + m_tail[pl.ds(before(0), HALO), :]
        a_own = acc[0, HALO:long_rows, :] + mid[...]
        after[...] = a_own
        for c in range(width // LANES):
            thin[c, 0:HALO, :] = a_tail[:, c * LANES : (c + 1) * LANES]
            thin[c, HALO:long_rows, :] = a_own[:, c * LANES : (c + 1) * LANES]

        row = lax.broadcasted_iota(jnp.int32, (short, LANES), 0) + fs * short
        begins = jnp.max(jnp.where(row == lane_first, 1.0, 0.0), axis=1, keepdims=True)
        parts = []
        for k in range(3):
            value = strided_read(thin, HALO - 2 + k, short)
            parts.append(jnp.where(begins > 0.0, 0.0, value) if k < 2 else value)
        z = jnp.concatenate(parts, axis=1).astype(BF)
        for e in range(fs_count):
            z_out[e] = z[:, e * pc : (e + 1) * pc]
        pooled = jnp.zeros((short, width), F32)
        for e in range(fs_count):
            wp_f.ready(e)
            pooled = pooled + dot_nt(z_out[flip(fs, e)], wp[e])
        s0_out[...] = pooled
        wait_all(y4)
        for t in range(3):
            wq1_out[:, t * hd : (t + 1) * hd] = wq1[t]
        net.finish()

    half = fs_count // 2
    outs = [
        ((total, width), BF),
        ((total, 3 * hd), BF),
        ((total, width), BF),
        ((hd, width), BF),
        ((total, width), BF),
        ((rows, width), F32),
        ((rows, width), F32),
        ((fs_count, short, pc), BF),
        ((short, width), F32),
        ((width, 3 * hd), BF),
        ((width, 2 * fj), BF),
        ((fs_count, width, pc), BF),
        ((width, 3 * hd), BF),
        ((width, cw), BF),
        ((8, width), F32),
    ]
    wide = max(width, fj)
    scratch = [
        ((fs_count, rows, width), BF),
        ((2, 3, rw, hd), BF),
        ((3, width, hd), BF),
        ((3, width, hd), BF),
        ((width, LANES), BF),
        ((fs_count, width, hd), BF),
        ((fs_count, width, hd), BF),
        ((fs_count, total, hd), BF),
        ((heads, total, LANES), BF),
        ((heads, total, LANES), BF),
        ((hd, total), BF),
        ((width, width), BF),
        ((width, width), BF),
        ((rows, wide), F32),
        ((rows, wide), BF),
        ((rows, width), F32),
        ((fs_count * HALO, width), F32),
        ((fs_count * HALO, width), F32),
        ((half, long_rows, width), BF),
        ((half, long_rows, width), BF),
        ((half - 1, long_rows, width), BF),
        ((half - 1, long_rows, width), BF),
        ((half, long_rows, width), F32),
        ((width // LANES, long_rows, LANES), F32),
    ]
    return pl.pallas_call(
        body,
        out_shape=[jax.ShapeDtypeStruct(s, t) for s, t in outs],
        in_specs=[vmem(), smem()] + [vmem()] * 9,
        out_specs=[vmem()] * len(outs),
        scratch_shapes=[pltpu.VMEM(s, t) for s, t in scratch] + [pltpu.SemaphoreType.DMA((sems,))] * 2,
        compiler_params=pltpu.CompilerParams(collective_id=3, has_side_effects=True, vmem_limit_bytes=VMEM_BYTES),
        cost_estimate=cost(2e10, 3e7),
        name="forward_one",
    )(tokens, triples, *weights, gains, cos, sin)


def swap(value, axis, bit):
    return lax.ppermute(value, axis, [(i, i ^ bit) for i in range(lax.axis_size(axis))])


def gather_pieces(value):
    count = lax.axis_size("fsdp")
    pieces = {0: value}
    bit = count // 2
    while bit:
        for step in list(pieces):
            pieces[step ^ bit] = swap(pieces[step], "fsdp", bit)
        bit //= 2
    return [pieces[step] for step in range(count)]


def finish_scatter(keep, send):
    total = keep + swap(send, "fsdp", 1).astype(F32)
    bit = 2
    while total.shape[0] > 2:
        total = total[0::2] + swap(total[1::2].astype(BF), "fsdp", bit).astype(F32)
        bit *= 2
    return total[0], swap(total[1].astype(BF), "fsdp", bit)


def exchange_blocks(blocks, me):
    count = lax.axis_size("fsdp")
    out = []
    for step in range(count):
        block = lax.dynamic_index_in_dim(blocks, me ^ step, 0, keepdims=False)
        out.append(swap(block, "fsdp", step) if step else block)
    return out


def gather_rows(value, y_count):
    count = lax.axis_size("dp")
    pieces = {0: value}
    for step in range(y_count, count, y_count):
        pieces[step] = swap(value, "dp", step)
    for base in range(0, count, y_count):
        for step in range(1, y_count):
            pieces[base ^ step] = swap(pieces[base], "dp", step)
    return [pieces[step] for step in range(count)]


def assemble_rows(dp_index, pieces, widths):
    count = len(pieces)
    rows = pieces[0].shape[0]

    def body(me_ref, *refs):
        piece_refs, outs = refs[:count], refs[count:]
        me_now = me_ref[0]
        for step in range(count):
            base = pl.multiple_of((me_now ^ step) * rows, 16)
            at = 0
            for out, width in zip(outs, widths):
                out[pl.ds(base, rows), :] = piece_refs[step][:, at : at + width]
                at += width

    return local_kernel(body, "assemble_rows", [((rows * count, w), BF) for w in widths], [], dp_index, *pieces)


def scatter_rows(grad, dp_index, y_count):
    count = lax.axis_size("dp")
    rows = grad.shape[0] // count
    z_count = count // y_count
    z, y = dp_index // y_count, dp_index % y_count
    grid = grad.reshape(z_count, y_count, rows, grad.shape[1])
    total = lax.dynamic_index_in_dim(grid, y, 1, keepdims=False).astype(F32)
    for step in range(1, y_count):
        out = lax.dynamic_index_in_dim(grid, y ^ step, 1, keepdims=False)
        total = total + swap(out, "dp", step).astype(F32)
    low = total.astype(BF)
    own = lax.dynamic_index_in_dim(total, z, 0, keepdims=False)
    for step in range(1, z_count):
        out = lax.dynamic_index_in_dim(low, z ^ step, 0, keepdims=False)
        own = own + swap(out, "dp", step * y_count).astype(F32)
    return own


def head_order(block, inverse=False):
    count = lax.axis_size("fsdp")
    me = lax.axis_index("fsdp")
    hd = block.shape[-1] // 3
    if not inverse:
        got = [
            lax.ppermute(block[..., t * hd : (t + 1) * hd], "fsdp", [(j, (3 * j + t) % count) for j in range(count)])
            for t in range(3)
        ]
        kinds = []
        for t in range(3):
            table = np.zeros(count, np.int32)
            for j in range(count):
                table[(3 * j + t) % count] = (3 * j + t) // count
            kinds.append(jnp.asarray(table)[me])
        return jnp.concatenate(
            [sum(jnp.where(kinds[t] == kind, got[t], 0) for t in range(3)) for kind in range(3)], axis=-1
        )
    mine = [block[..., t * hd : (t + 1) * hd] for t in range(3)]
    out = []
    for t in range(3):
        table = np.zeros(count, np.int32)
        for j in range(count):
            table[(3 * j + t) % count] = (3 * j + t) // count
        kind = jnp.asarray(table)[me]
        chosen = sum(jnp.where(kind == other, mine[other], 0) for other in range(3))
        out.append(lax.ppermute(chosen, "fsdp", [((3 * j + t) % count, j) for j in range(count)]))
    return jnp.concatenate(out, axis=-1)


def owners_of(amount, dp_count, fs_count):
    found = []
    half = dp_count // 2
    for k in range(amount):
        found.append((dp_count // 4 + k % half, (2 * (k // half)) % fs_count + (2 * (k // half)) // fs_count))
    return found


def round_up(width):
    return -(-width // LANES) * LANES


def push_pieces(pieces, dp_count, fs_count):
    amount = len(pieces)
    widths = [p.shape[1] for p in pieces]
    rows = pieces[0].shape[0]
    wide = max(widths)
    devices = dp_count * fs_count
    owners = owners_of(amount, dp_count, fs_count)

    def body(*refs):
        srcs, out, send_sem, recv_sem = refs[:amount], refs[amount], refs[amount + 1], refs[amount + 2]
        dp, fs = lax.axis_index("dp"), lax.axis_index("fsdp")
        slot = fs * dp_count + dp
        out[...] = jnp.zeros(out.shape, BF)
        barrier = pltpu.get_barrier_semaphore()
        owned = 0
        for k in range(amount):
            mine = (dp == owners[k][0]) & (fs == owners[k][1])
            owned = owned + mine.astype(jnp.int32)

            @pl.when(mine)
            def _():
                def greet(t, carry):
                    @pl.when(t != slot)
                    def _():
                        pl.semaphore_signal(
                            barrier, inc=1, device_id=(lax.rem(t, dp_count), t // dp_count), device_id_type=MESH
                        )

                    return carry

                lax.fori_loop(0, devices, greet, 0)

        pl.semaphore_wait(barrier, amount - owned)
        for k in range(amount):
            mine = (dp == owners[k][0]) & (fs == owners[k][1])
            copy = pltpu.make_async_remote_copy(
                src_ref=srcs[k],
                dst_ref=out.at[slot, :, 0 : widths[k]],
                send_sem=send_sem.at[k],
                recv_sem=recv_sem,
                device_id=owners[k],
                device_id_type=MESH,
            )

            @pl.when(jnp.logical_not(mine))
            def _():
                copy.start()

            @pl.when(mine)
            def _():
                out[slot, :, 0 : widths[k]] = srcs[k][...]

        for k in range(amount):
            mine = (dp == owners[k][0]) & (fs == owners[k][1])

            @pl.when(mine)
            def _():
                landed = out.at[0 : devices - 1, :, 0 : widths[k]]
                pltpu.make_async_copy(landed, landed, recv_sem).wait()

            @pl.when(jnp.logical_not(mine))
            def _():
                pltpu.make_async_copy(srcs[k], srcs[k], send_sem.at[k]).wait()

    return pl.pallas_call(
        body,
        out_shape=jax.ShapeDtypeStruct((devices, rows, wide), BF),
        in_specs=[vmem()] * amount,
        out_specs=vmem(),
        scratch_shapes=[pltpu.SemaphoreType.DMA((amount,)), pltpu.SemaphoreType.DMA],
        compiler_params=pltpu.CompilerParams(collective_id=1, has_side_effects=True, vmem_limit_bytes=VMEM_BYTES),
        name="push_pieces",
    )(*pieces)


def orthogonalize(own, stacked):
    count, rows, wide = stacked.shape
    coef_a, coef_b, coef_c = NS_COEFS

    def body(own_ref, in_ref, out, norm, x):
        @pl.when(own_ref[0] > 0)
        def _():
            for at in range(count):
                x[:, at * wide : (at + 1) * wide] = in_ref[at]
            square = jnp.zeros((1, 1), F32)
            for r in range(0, rows, 64):
                block = x[r : r + 64, :].astype(F32)
                square = square + jnp.sum(jnp.sum(block * block, axis=0, keepdims=True), axis=1, keepdims=True)
            length = jnp.sqrt(square)
            norm[...] = jnp.broadcast_to(length, norm.shape)
            scale = 1.0 / (length + NORM_EPS)
            for turn in range(NS_STEPS):
                gram = dot_nt(x[...], x[...])
                if turn == 0:
                    gram = gram * (scale * scale)
                gram = gram.astype(BF)
                poly = (coef_b * gram.astype(F32) + coef_c * dot_nn(gram, gram)).astype(BF)
                for at in range(0, count * wide, 512):
                    here = slice(at, at + 512)
                    block = x[:, here]
                    new = coef_a * block.astype(F32) + dot_nn(poly, block)
                    if turn == 0:
                        new = new * scale
                    x[:, here] = new.astype(BF)
            for at in range(count):
                out[at] = x[:, at * wide : (at + 1) * wide]

    return pl.pallas_call(
        body,
        out_shape=[jax.ShapeDtypeStruct(stacked.shape, BF), jax.ShapeDtypeStruct((8, LANES), F32)],
        in_specs=[smem(), vmem()],
        out_specs=[vmem(), vmem()],
        scratch_shapes=[pltpu.VMEM((rows, count * wide), BF)],
        compiler_params=params(),
        name="orthogonalize",
    )(own, stacked)


def return_pieces(ortho, norm, widths, dp_count, fs_count):
    amount = len(widths)
    devices, rows, wide = ortho.shape
    owners = owners_of(amount, dp_count, fs_count)

    def body(src, norm_ref, out, norms, send_sem, recv_sem, norm_send, norm_recv):
        dp, fs = lax.axis_index("dp"), lax.axis_index("fsdp")
        slot = fs * dp_count + dp
        barrier = pltpu.get_barrier_semaphore()
        owned = 0
        for k in range(amount):
            mine = (dp == owners[k][0]) & (fs == owners[k][1])
            owned = owned + mine.astype(jnp.int32)

            @pl.when(jnp.logical_not(mine))
            def _():
                pl.semaphore_signal(barrier, inc=1, device_id=owners[k], device_id_type=MESH)

        @pl.when(owned > 0)
        def _():
            pl.semaphore_wait(barrier, devices - 1)

        for k in range(amount):
            mine = (dp == owners[k][0]) & (fs == owners[k][1])
            width = widths[k]

            @pl.when(mine)
            def _():
                def give(t, carry):
                    @pl.when(t != slot)
                    def _():
                        there = (lax.rem(t, dp_count), t // dp_count)
                        pltpu.make_async_remote_copy(
                            src_ref=src.at[t, :, 0:width],
                            dst_ref=out.at[k, :, 0:width],
                            send_sem=send_sem,
                            recv_sem=recv_sem.at[k],
                            device_id=there,
                            device_id_type=MESH,
                        ).start()
                        pltpu.make_async_remote_copy(
                            src_ref=norm_ref,
                            dst_ref=norms.at[k],
                            send_sem=norm_send,
                            recv_sem=norm_recv.at[k],
                            device_id=there,
                            device_id_type=MESH,
                        ).start()

                    return carry

                lax.fori_loop(0, devices, give, 0)
                out[k, :, 0:width] = src[slot, :, 0:width]
                norms[k] = norm_ref[...]

        for k in range(amount):
            mine = (dp == owners[k][0]) & (fs == owners[k][1])
            width = widths[k]

            @pl.when(jnp.logical_not(mine))
            def _():
                landed = out.at[k, :, 0:width]
                pltpu.make_async_copy(landed, landed, recv_sem.at[k]).wait()
                pltpu.make_async_copy(norms.at[k], norms.at[k], norm_recv.at[k]).wait()

            @pl.when(mine)
            def _():
                left = src.at[0 : devices - 1, :, 0:width]
                pltpu.make_async_copy(left, left, send_sem).wait()
                def drain(t, carry):
                    pltpu.make_async_copy(norm_ref, norm_ref, norm_send).wait()
                    return carry

                lax.fori_loop(0, devices - 1, drain, 0)

    return pl.pallas_call(
        body,
        out_shape=[jax.ShapeDtypeStruct((amount, rows, wide), BF), jax.ShapeDtypeStruct((amount, 8, LANES), F32)],
        in_specs=[vmem(), vmem()],
        out_specs=[vmem(), vmem()],
        scratch_shapes=[
            pltpu.SemaphoreType.DMA,
            pltpu.SemaphoreType.DMA((amount,)),
            pltpu.SemaphoreType.DMA,
            pltpu.SemaphoreType.DMA((amount,)),
        ],
        compiler_params=pltpu.CompilerParams(collective_id=2, has_side_effects=True, vmem_limit_bytes=VMEM_BYTES),
        name="return_pieces",
    )(ortho, norm)


def rope_tables(total, hd):
    half = HEAD // 2
    frequency = (np.float32(10000.0) ** (-np.arange(half, dtype=np.float32) / np.float32(half))).astype(np.float32)
    angle = (np.arange(total, dtype=np.float32)[:, None] * frequency[None, :]).astype(np.float32)
    cos, sin = np.cos(angle), np.sin(angle)
    cos = np.tile(np.concatenate([cos, cos], axis=1), (1, hd // HEAD))
    sin = np.tile(np.concatenate([-sin, sin], axis=1), (1, hd // HEAD))
    return jnp.asarray(cos, F32), jnp.asarray(sin, F32)


def mask_features(segment, docs):
    same = segment[:, None] == jnp.arange(HEAD, dtype=jnp.int32)[None, :]
    used = jnp.arange(HEAD)[None, :] < docs
    fq = jnp.where(used & ~same, MASKED, 0.0).astype(BF)
    fk = same.astype(BF)
    return jnp.concatenate([fq, fq], axis=1), jnp.concatenate([fk, fk], axis=1)


def on_device(
    y_count,
    tokens,
    cotangent,
    doc_triples,
    w_qkv,
    w_out,
    w_in,
    w_down,
    w_pool,
    w_up,
    gains,
    m_qkv,
    m_out,
    m_in,
    m_down,
    m_pool,
    m_up,
    m_gains,
):
    rows, width = tokens.shape
    short = rows // 3
    fs_count, dp_count = lax.axis_size("fsdp"), lax.axis_size("dp")
    me, dp_me = lax.axis_index("fsdp"), lax.axis_index("dp")
    me_arr, dp_arr = me.astype(jnp.int32).reshape(1), dp_me.astype(jnp.int32).reshape(1)
    total, short_total = rows * fs_count, short * fs_count
    hd = width // fs_count
    fj = w_in.shape[2]
    pool_cols = w_pool.shape[1]

    ends = jnp.cumsum(doc_triples[0]).astype(jnp.int32)
    short_all = jnp.arange(short_total, dtype=jnp.int32)
    reached = short_all[:, None] >= ends[None, :]
    short_segment = jnp.sum(reached.astype(jnp.int32), axis=1)
    segment = jnp.repeat(short_segment, 3)
    begins = jnp.any(short_all[:, None] == ends[None, :], axis=1) | (short_all == 0)
    gate = jnp.pad(jnp.where(begins, 0.0, 1.0).astype(F32), (0, HALO))
    gate = lax.dynamic_slice(gate, (me * short,), (short + HALO,))[:, None]
    docs = doc_triples.shape[1]
    fq0, fk0 = mask_features(segment, docs)
    fq1, fk1 = mask_features(short_segment, docs)
    cos0, sin0 = rope_tables(total, hd)
    cos1, sin1 = cos0[:short_total], sin0[:short_total]

    old_weights = (w_qkv, w_out, w_in, w_down, w_pool, w_up)
    n1, qkv, att_rel, wo_own, n2, mid, after, z_blocks, s0, wqkv0, ff0, wp_all, wqkv1, rest, gain_rows = forward_one(
        y_count, dp_count, fs_count, tokens, doc_triples, old_weights, gains, cos0, sin0
    )
    gain = [gain_rows[k : k + 1] for k in range(4)]
    wi0, wd0 = ff0[:, :fj], ff0[:, fj:]
    wu, wo1 = rest[:, :pool_cols], rest[:, pool_cols : pool_cols + hd]
    wi1, wd1 = rest[:, pool_cols + hd : pool_cols + hd + fj], rest[:, pool_cols + hd + fj :]
    wp_p = [wp_all[e] for e in range(fs_count)]
    wo1_p, wu_p = gather_pieces(wo1), gather_pieces(wu)
    s0_p = gather_pieces(s0)
    z_p = exchange_blocks(z_blocks, me)
    c_blocks, ds1, ds1_low = up_backward(me_arr, cotangent, wu_p)
    c_p = exchange_blocks(c_blocks, me)
    ds1_p = gather_pieces(ds1_low)
    n1b, qkvb, attb = attn_forward(me_arr, s0_p, gain[2], wqkv1, fq1, fk1, cos1, sin1)
    n2b, attb_rel, wob_own, midb, keep, send = mix_forward(
        me_arr, s0_p, gather_pieces(attb), wo1_p, wi1, wd1, gain[3], 0
    )
    total_in, got = finish_scatter(keep, send)
    s1, layer_out = up_forward(me_arr, midb, total_in, got, after, wu_p)
    s1_p = gather_pieces(s1)
    g_up = dot_tn(jnp.concatenate(s1_p), jnp.concatenate(c_p))

    def block_back(d_pieces, above, n1, n2, att_rel, wo_own, wqkv, wi, wd, qkv, mid, own_in, gain_one, gain_two, tables):
        whole, hid, dpre, keep, send = mix_backward(me_arr, d_pieces, n2, wi, wd)
        g_down = dot_tn(whole, hid)
        g_in = dot_tn(n2, dpre)
        total_in, got = finish_scatter(keep, send)
        dm, dm_low, dgain_two = norm_backward(me_arr, mid, gain_two, total_in, got, above)
        da_all, dqkv, keep, send = attn_backward(me_arr, gather_pieces(dm_low), qkv, wo_own, wqkv, *tables)
        g_qkv = dot_tn(n1, dqkv)
        own = lax.dynamic_slice(da_all, (0, me * hd), (da_all.shape[0], hd))
        g_out = dot_tn(att_rel, own).reshape(fs_count, hd, hd)
        g_out = jnp.concatenate(
            [lax.dynamic_index_in_dim(g_out, me ^ k, 0, keepdims=False) for k in range(fs_count)], axis=0
        )
        total_in, got = finish_scatter(keep, send)
        dr, dr_low, dgain_one = norm_backward(me_arr, own_in, gain_one, total_in, got, dm)
        return dr, dr_low, (g_qkv, g_out, g_in, g_down), (dgain_one, dgain_two)

    _, ds0, grads_b, dgain_b = block_back(
        ds1_p,
        ds1,
        n1b,
        n2b,
        attb_rel,
        wob_own,
        wqkv1,
        wi1,
        wd1,
        qkvb,
        midb,
        s0,
        gain[2],
        gain[3],
        (fq1, fk1, cos1, sin1),
    )
    ds0_next = lax.ppermute(ds0[:HALO], "fsdp", [(i + 1, i) for i in range(fs_count - 1)])
    da, da_low = pool_backward(me_arr, ds0, ds0_next, gate, wp_p, cotangent)
    ds0_p = gather_pieces(ds0)
    g_pool = dot_tn(jnp.concatenate(ds0_p), jnp.concatenate(z_p))
    group_b = jnp.concatenate([grads_b[0], g_pool, g_up, grads_b[2], grads_b[3], grads_b[1]], axis=1).astype(BF)
    sum_b = scatter_rows(group_b, dp_me, y_count)

    grad_in, _, grads_a, dgain_a = block_back(
        gather_pieces(da_low),
        da,
        n1,
        n2,
        att_rel,
        wo_own,
        wqkv0,
        wi0,
        wd0,
        qkv,
        mid,
        tokens,
        gain[0],
        gain[1],
        (fq0, fk0, cos0, sin0),
    )
    sum_ff = scatter_rows(jnp.concatenate([grads_a[2], grads_a[3]], axis=1).astype(BF), dp_me, y_count)
    sum_at = scatter_rows(jnp.concatenate([grads_a[0], grads_a[1]], axis=1).astype(BF), dp_me, y_count)

    dgain = jnp.concatenate([dgain_a[0][:1], dgain_a[1][:1], dgain_b[0][:1], dgain_b[1][:1]], axis=0)
    bit = 1
    while bit < fs_count:
        dgain = dgain + swap(dgain, "fsdp", bit)
        bit *= 2
    own_rows = width // dp_count
    dgain_t = jnp.pad(dgain.T.astype(BF), ((0, 0), (0, LANES - 4)))
    gain_total = scatter_rows(dgain_t, dp_me, y_count)[:, 0:4]
    gain_moments = GAIN_DECAY * m_gains + gain_total
    new_gains = gains - GAIN_RATE * gain_moments

    at = 3 * hd
    qkv_b = sum_b[:, 0:at]
    pool_g, up_g = sum_b[:, at : at + pool_cols], sum_b[:, at + pool_cols : at + 2 * pool_cols]
    at += 2 * pool_cols
    in_b, down_b, out_b = sum_b[:, at : at + fj], sum_b[:, at + fj : at + 2 * fj], sum_b[:, at + 2 * fj :]
    qkv_g = head_order(jnp.stack([sum_at[:, : 3 * hd], qkv_b]), inverse=True)
    out_g = jnp.stack([sum_at[:, 3 * hd :], out_b])
    in_g = jnp.stack([sum_ff[:, :fj], in_b])
    down_g = jnp.stack([sum_ff[:, fj:], down_b])
    old = (m_qkv, m_out, m_in, m_down, m_pool, m_up)
    moments = [MOMENT_DECAY * m + g for m, g in zip(old, (qkv_g, out_g, in_g, down_g, pool_g, up_g))]

    listed = [(2, 0), (2, 1), (3, 0), (3, 1), (0, 0), (0, 1), (4, None), (5, None), (1, 0), (1, 1)]

    def piece_of(arrays, kind, blk):
        return arrays[kind] if blk is None else arrays[kind][blk]

    pieces, widths = [], []
    for kind, blk in listed:
        piece = piece_of(moments, kind, blk).astype(BF)
        wide = round_up(piece.shape[1])
        widths.append(wide)
        pieces.append(jnp.pad(piece, ((0, 0), (0, wide - piece.shape[1]))))
    pushed = push_pieces(pieces, dp_count, fs_count)
    owned = jnp.zeros((), jnp.bool_)
    for o_dp, o_fs in owners_of(len(listed), dp_count, fs_count):
        owned = owned | ((dp_me == o_dp) & (me == o_fs))
    stacked = pushed.reshape(fs_count, width, pushed.shape[2])
    ortho, norm = orthogonalize(owned.astype(jnp.int32).reshape(1), stacked)
    results, norms = return_pieces(ortho.reshape(pushed.shape), norm, widths, dp_count, fs_count)

    weights = (w_qkv, w_out, w_in, w_down, w_pool, w_up)
    all_tokens = float(total * dp_count)
    new_parts, rms = {}, {}
    for k, (kind, blk) in enumerate(listed):
        old_part = piece_of(weights, kind, blk)
        new_parts[kind, blk] = old_part - STEP_SCALES[kind] * results[k, :, : old_part.shape[1]].astype(F32)
        entries = float(old_part.size * fs_count * dp_count) * all_tokens
        rms[kind, blk] = norms[k, 0, 0] / np.float32(entries**0.5)
    new_weights = [jnp.stack([new_parts[kind, 0], new_parts[kind, 1]]) for kind in range(4)]
    new_weights += [new_parts[4, None], new_parts[5, None]]
    moment_rms = jnp.stack(
        [rms[kind, blk] for kind in range(4) for blk in range(2)] + [rms[4, None], rms[5, None]]
    )
    return (layer_out, grad_in, *moments, *new_weights, gain_moments, new_gains, moment_rms)


def solution(mesh):
    by_row, by_dp = P(("dp", "fsdp"), None), P("dp", None)
    stacked, flat = P(None, "dp", "fsdp"), P("dp", "fsdp")
    matrices = (stacked,) * 4 + (flat,) * 2
    y_count = max(1, mesh.shape["fsdp"] // 2)
    return jax.shard_map(
        functools.partial(on_device, y_count),
        mesh=mesh,
        in_specs=(by_row, by_row, by_dp, *matrices, by_dp, *matrices, by_dp),
        out_specs=(by_row, by_row, *matrices, *matrices, by_dp, by_dp, P()),
        check_vma=False,
    )
```

```python
import functools

import jax
import jax.numpy as jnp
import numpy as np
from jax import lax
from jax.experimental import pallas as pl
from jax.experimental.pallas import tpu as pltpu
from jax.sharding import PartitionSpec as P

HEAD = 64
NS_STEPS = 5
NS_COEFS = (3.4445, -4.775, 2.0315)
STEP_SCALES = (0.8660254, 1.4142136, 1.0, 0.5, 0.5, 0.8660254)
MOMENT_DECAY = 0.95
GAIN_DECAY = 0.9
GAIN_RATE = 0.001
LN_EPS = 1e-05
NORM_EPS = 1e-07
MASKED = -1e30
HALO = 16
QB = 256
LANES = 128
VMEM_BYTES = 60 << 20
BF = jnp.bfloat16
F32 = jnp.float32
MESH = pl.DeviceIdType.MESH


def dot_nn(left, right):
    return lax.dot_general(left, right, (((1,), (0,)), ((), ())), preferred_element_type=F32)


def dot_nt(left, right):
    return lax.dot_general(left, right, (((1,), (1,)), ((), ())), preferred_element_type=F32)


def dot_tn(left, right):
    return lax.dot_general(left, right, (((0,), (0,)), ((), ())), preferred_element_type=F32)


def layer_norm(values, gain):
    mean = jnp.mean(values, axis=-1, keepdims=True)
    centred = values - mean
    spread = jnp.mean(centred * centred, axis=-1, keepdims=True)
    return centred * lax.rsqrt(spread + LN_EPS) * gain


def layer_norm_back(values, gain, grad):
    mean = jnp.mean(values, axis=-1, keepdims=True)
    centred = values - mean
    spread = jnp.mean(centred * centred, axis=-1, keepdims=True)
    scale = lax.rsqrt(spread + LN_EPS)
    unit = centred * scale
    scaled = grad * gain
    part = jnp.mean(scaled, axis=-1, keepdims=True)
    along = jnp.mean(scaled * unit, axis=-1, keepdims=True)
    return scale * (scaled - part - unit * along), grad * unit


def gelu(values):
    return 0.5 * values * (1.0 + jnp.tanh(0.7978845608028654 * (values + 0.044715 * values * values * values)))


def gelu_both(values):
    square = values * values
    turn = jnp.tanh(0.7978845608028654 * (values + 0.044715 * values * square))
    slope = 0.7978845608028654 * (1.0 + 3.0 * 0.044715 * square)
    half = 0.5 * (1.0 + turn)
    return values * half, half + 0.5 * values * (1.0 - turn * turn) * slope


def partner(values):
    width = values.shape[1]
    if width == LANES:
        lane = lax.broadcasted_iota(jnp.int32, values.shape, 1)
        ahead = pltpu.roll(values, LANES - HEAD // 2, 1)
        behind = pltpu.roll(values, HEAD // 2, 1)
        return jnp.where(lane % HEAD < HEAD // 2, ahead, behind)
    parts = []
    for at in range(0, width, HEAD):
        parts += [values[:, at + HEAD // 2 : at + HEAD], values[:, at : at + HEAD // 2]]
    return jnp.concatenate(parts, axis=1)


def widen(values):
    rows, width = values.shape
    if width >= LANES:
        return values
    return jnp.concatenate([values, jnp.zeros((rows, LANES - width), values.dtype)], axis=1)


def params():
    return pltpu.CompilerParams(vmem_limit_bytes=VMEM_BYTES)


def smem():
    return pl.BlockSpec(memory_space=pltpu.SMEM)


def vmem():
    return pl.BlockSpec(memory_space=pltpu.VMEM)


def cost(flops, moved):
    return pl.CostEstimate(flops=int(flops), bytes_accessed=int(moved), transcendentals=0)


def local_kernel(body, name, outs, scratch, me, *arrays, flops=0):
    moved = sum(a.size * a.dtype.itemsize for a in arrays)
    moved += sum(int(np.prod(s)) * jnp.dtype(t).itemsize for s, t in outs)
    return pl.pallas_call(
        body,
        out_shape=[jax.ShapeDtypeStruct(s, t) for s, t in outs],
        in_specs=[smem()] + [vmem()] * len(arrays),
        out_specs=[vmem()] * len(outs),
        scratch_shapes=[pltpu.VMEM(s, t) for s, t in scratch],
        compiler_params=params(),
        cost_estimate=cost(flops, moved),
        name=name,
    )(me, *arrays)


def at_rows(me, step, rows):
    return pl.multiple_of((me ^ step) * rows, 16)


def head_inputs(qs, ks, rows, q, k, fq, fk, heads):
    lane = lax.broadcasted_iota(jnp.int32, (q.shape[0], LANES), 1)
    q, k = widen(q), widen(k)
    for h in range(heads):
        mine = lane // HEAD == h
        qs[h, rows, :] = jnp.where(mine, q * 0.125, fq).astype(BF)
        ks[h, rows, :] = jnp.where(mine, k, fk).astype(BF)


def scores_t(ks, qs, h, start, stop):
    top = dot_nt(ks[h, 0:stop, :], qs[h, start:stop, :])
    key = lax.broadcasted_iota(jnp.int32, (stop - start, stop - start), 0)
    query = lax.broadcasted_iota(jnp.int32, (stop - start, stop - start), 1)
    last = jnp.where(key <= query, top[start:, :], MASKED)
    if start == 0:
        return last
    return jnp.concatenate([top[:start, :], last], axis=0)


def attn_forward(me, pieces, gain, w_qkv, fq, fk, cos, sin):
    count = len(pieces)
    rows, width = pieces[0].shape
    total = rows * count
    hd = w_qkv.shape[1] // 3
    heads = hd // HEAD
    blk = min(QB, total)

    def body(me_ref, *refs):
        piece_refs = refs[:count]
        gain_ref, w_ref, fq_ref, fk_ref, cos_ref, sin_ref, n1, qkv, out, qs, ks, vt = refs[count:]
        me_now = me_ref[0]
        for step in range(count):
            base = at_rows(me_now, step, rows)
            for r in range(0, rows, LANES):
                block = piece_refs[step][r : r + LANES, :].astype(F32)
                n1[pl.ds(base + r, LANES), :] = layer_norm(block, gain_ref[...]).astype(BF)
        for r in range(0, total, blk):
            here = slice(r, r + blk)
            got = dot_nn(n1[here, :], w_ref[...])
            q, k, v = got[:, :hd], got[:, hd : 2 * hd], got[:, 2 * hd :]
            q = (q * cos_ref[here, :] + partner(q) * sin_ref[here, :]).astype(BF)
            k = (k * cos_ref[here, :] + partner(k) * sin_ref[here, :]).astype(BF)
            qkv[here, 0:hd] = q
            qkv[here, hd : 2 * hd] = k
            qkv[here, 2 * hd : 3 * hd] = v.astype(BF)
            head_inputs(
                qs, ks, here, q.astype(F32), k.astype(F32), fq_ref[here, :].astype(F32), fk_ref[here, :].astype(F32), heads
            )
            vt[:, here] = v.T.astype(BF)
        for r in range(0, total, blk):
            stop = r + blk
            found = []
            for h in range(heads):
                s = scores_t(ks, qs, h, r, stop)
                e = jnp.exp(s - jnp.max(s, axis=0, keepdims=True))
                p = (e * (1.0 / jnp.sum(e, axis=0, keepdims=True))).astype(BF)
                found.append(dot_nn(vt[h * HEAD : (h + 1) * HEAD, 0:stop], p))
            out[r:stop, :] = jnp.concatenate(found, axis=0).T.astype(BF)

    return local_kernel(
        body,
        "attn_forward",
        [((total, width), BF), ((total, 3 * hd), BF), ((total, hd), BF)],
        [((heads, total, LANES), BF), ((heads, total, LANES), BF), ((hd, total), BF)],
        me,
        *pieces,
        gain,
        w_qkv,
        fq,
        fk,
        cos,
        sin,
        flops=8e9,
    )


def attn_backward(me, pieces, qkv, wo_own, w_qkv, fq, fk, cos, sin):
    count = len(pieces)
    rows, width = pieces[0].shape
    total = rows * count
    hd = w_qkv.shape[1] // 3
    heads = hd // HEAD
    blk = min(QB, total)

    def body(me_ref, *refs):
        piece_refs = refs[:count]
        qkv_ref, wo_ref, w_ref, fq_ref, fk_ref, cos_ref, sin_ref = refs[count : count + 7]
        whole, dqkv, keep, send, qs, ks, qz, doz, kt, dk, dv = refs[count + 7 :]
        me_now = me_ref[0]
        for step in range(count):
            base = at_rows(me_now, step, rows)
            whole[pl.ds(base, rows), :] = piece_refs[step][...]
        lane = lax.broadcasted_iota(jnp.int32, (blk, LANES), 1)
        for r in range(0, total, blk):
            here = slice(r, r + blk)
            q = qkv_ref[here, 0:hd].astype(F32)
            k = qkv_ref[here, hd : 2 * hd].astype(F32)
            head_inputs(qs, ks, here, q, k, fq_ref[here, :].astype(F32), fk_ref[here, :].astype(F32), heads)
            kt[:, here] = k.T.astype(BF)
            do = widen(dot_nt(whole[here, :], wo_ref[...]))
            q = widen(q)
            for h in range(heads):
                mine = lane // HEAD == h
                qz[h, here, :] = jnp.where(mine, q, 0.0).astype(BF)
                doz[h, here, :] = jnp.where(mine, do, 0.0).astype(BF)
            dk[here, :] = jnp.zeros((blk, LANES), F32)
            dv[here, :] = jnp.zeros((blk, LANES), F32)
        for r in range(0, total, blk):
            stop = r + blk
            here = slice(r, stop)
            found = []
            add_k = None
            for h in range(heads):
                s = scores_t(ks, qs, h, r, stop)
                e = jnp.exp(s - jnp.max(s, axis=0, keepdims=True))
                p = e * (1.0 / jnp.sum(e, axis=0, keepdims=True))
                v = widen(qkv_ref[0:stop, 2 * hd : 3 * hd])
                dp = dot_nt(v, doz[h, here, :])
                mid = jnp.sum(p * dp, axis=0, keepdims=True)
                dr = (p * (dp - mid) * 0.125).astype(BF)
                part_v = dot_nn(p.astype(BF), doz[h, here, :])
                part_k = dot_nn(dr, qz[h, here, :])
                add_v = part_v if add_k is None else add_v + part_v
                add_k = part_k if add_k is None else add_k + part_k
                found.append(dot_nn(kt[h * HEAD : (h + 1) * HEAD, 0:stop], dr))
            dk[0:stop, :] += add_k
            dv[0:stop, :] += add_v
            dq = jnp.concatenate(found, axis=0).T
            dqkv[here, 0:hd] = (dq * cos_ref[here, :] - partner(dq) * sin_ref[here, :]).astype(BF)
        for r in range(0, total, blk):
            here = slice(r, r + blk)
            grad = dk[here, 0:hd]
            dqkv[here, hd : 2 * hd] = (grad * cos_ref[here, :] - partner(grad) * sin_ref[here, :]).astype(BF)
            dqkv[here, 2 * hd : 3 * hd] = dv[here, 0:hd].astype(BF)
        for step in range(count):
            base = at_rows(me_now, step, rows)
            part = dot_nt(dqkv[pl.ds(base, rows), :], w_ref[...])
            if step % 2:
                send[step // 2] = part.astype(BF)
            else:
                keep[step // 2] = part

    return local_kernel(
        body,
        "attn_backward",
        [
            ((total, width), BF),
            ((total, 3 * hd), BF),
            ((count // 2, rows, width), F32),
            ((count // 2, rows, width), BF),
        ],
        [((heads, total, LANES), BF)] * 4 + [((hd, total), BF), ((total, LANES), F32), ((total, LANES), F32)],
        me,
        *pieces,
        qkv,
        wo_own,
        w_qkv,
        fq,
        fk,
        cos,
        sin,
        flops=16e9,
    )


def mix_forward(me, pieces, att, wo, wi, wd, gain, halo):
    count = len(pieces)
    rows, width = pieces[0].shape
    total = rows * count
    hd = att[0].shape[1]
    fj = wi.shape[1]
    long_rows = rows + halo

    def body(me_ref, *refs):
        piece_refs, refs = refs[:count], refs[count:]
        att_refs, refs = refs[:count], refs[count:]
        wo_refs, refs = refs[:count], refs[count:]
        wi_ref, wd_ref, gain_ref, n2, att_rel, wo_own, mid, keep, send, blocks, full, turned, m_all, part_all = refs
        me_now = me_ref[0]
        for step in range(count):
            blocks[me_now ^ step] = wo_refs[step][...]
            att_rel[:, step * hd : (step + 1) * hd] = att_refs[step][...]
        for at in range(count):
            full[:, at * hd : (at + 1) * hd] = blocks[at]
        for step in range(count):
            base = at_rows(me_now, step, hd)
            turned[step * hd : (step + 1) * hd, :] = full[pl.ds(base, hd), :]
        wo_own[...] = turned[0:hd, :]
        for step in range(count):
            base = at_rows(me_now, step, rows)
            for r in range(0, rows, LANES):
                at = pl.ds(base + r, LANES)
                m = piece_refs[step][r : r + LANES, :].astype(F32) + dot_nn(att_rel[at, :], turned[...])
                m_all[at, :] = m
                low = layer_norm(m, gain_ref[...]).astype(BF)
                n2[step * rows + r : step * rows + r + LANES, :] = low
                hid = gelu(dot_nn(low, wi_ref[...])).astype(BF)
                part_all[at, :] = dot_nt(hid, wd_ref[...])
        for step in range(count):
            base = at_rows(me_now, step, rows)
            out = (send if step % 2 else keep).at[step // 2]
            out[halo:long_rows, :] = part_all[pl.ds(base, rows), :].astype(out.dtype)
            if halo:
                before = pl.multiple_of(lax.rem(base + total - halo, total), 16)
                out[0:halo, :] = part_all[pl.ds(before, halo), :].astype(out.dtype)
                if step == 0:
                    mid[0:halo, :] = m_all[pl.ds(before, halo), :]
            if step == 0:
                mid[halo:long_rows, :] = m_all[pl.ds(base, rows), :]

    return local_kernel(
        body,
        "mix_forward",
        [
            ((total, width), BF),
            ((total, width), BF),
            ((hd, width), BF),
            ((long_rows, width), F32),
            ((count // 2, long_rows, width), F32),
            ((count // 2, long_rows, width), BF),
        ],
        [
            ((count, width, hd), BF),
            ((width, width), BF),
            ((width, width), BF),
            ((total, width), F32),
            ((total, width), F32),
        ],
        me,
        *pieces,
        *att,
        *wo,
        wi,
        wd,
        gain,
        flops=2 * total * width * (width + 2 * fj),
    )


def mix_backward(me, grads, n2, wi, wd):
    count = len(grads)
    rows, width = grads[0].shape
    total = rows * count
    fj = wi.shape[1]

    def body(me_ref, *refs):
        grad_refs = refs[:count]
        n2_ref, wi_ref, wd_ref, whole, hid, dpre, keep, send = refs[count:]
        for step in range(count):
            out = (send if step % 2 else keep).at[step // 2]
            for r in range(0, rows, LANES):
                at = slice(step * rows + r, step * rows + r + LANES)
                grad = grad_refs[step][r : r + LANES, :]
                whole[at, :] = grad
                value, slope = gelu_both(dot_nn(n2_ref[at, :], wi_ref[...]))
                hid[at, :] = value.astype(BF)
                low = (dot_nn(grad, wd_ref[...]) * slope).astype(BF)
                dpre[at, :] = low
                out[r : r + LANES, :] = dot_nt(low, wi_ref[...]).astype(out.dtype)

    return local_kernel(
        body,
        "mix_backward",
        [
            ((total, width), BF),
            ((total, fj), BF),
            ((total, fj), BF),
            ((count // 2, rows, width), F32),
            ((count // 2, rows, width), BF),
        ],
        [],
        me,
        *grads,
        n2,
        wi,
        wd,
        flops=6 * total * width * fj,
    )


def norm_backward(me, values, gain, total_in, got, above):
    rows, width = values.shape

    def body(me_ref, v_ref, gain_ref, t_ref, got_ref, above_ref, full, low, dgain):
        acc = jnp.zeros((1, width), F32)
        for r in range(0, rows, LANES):
            at = slice(r, r + LANES)
            grad = t_ref[at, :] + got_ref[at, :].astype(F32)
            dx, dg = layer_norm_back(v_ref[at, :].astype(F32), gain_ref[...], grad)
            dx = dx + above_ref[at, :]
            full[at, :] = dx
            low[at, :] = dx.astype(BF)
            acc = acc + jnp.sum(dg, axis=0, keepdims=True)
        dgain[...] = jnp.broadcast_to(acc, (8, width))

    return local_kernel(
        body,
        "norm_backward",
        [((rows, width), F32), ((rows, width), BF), ((8, width), F32)],
        [],
        me,
        values,
        gain,
        total_in,
        got,
        above,
    )


def spread_write(hold, values):
    for c in range(hold.shape[0]):
        hold[c] = values[:, c * LANES : (c + 1) * LANES]


def spread_read(hold):
    return jnp.concatenate([hold[c] for c in range(hold.shape[0])], axis=1)


def strided_read(hold, start, amount):
    return jnp.concatenate([hold[c, pl.ds(start, amount, stride=3), :] for c in range(hold.shape[0])], axis=1)


def strided_write(hold, start, amount, values):
    for c in range(hold.shape[0]):
        hold[c, pl.ds(start, amount, stride=3), :] = values[:, c * LANES : (c + 1) * LANES]


def pool_forward(me, mid, total_in, got, gate, wp):
    count = len(wp)
    long_rows, width = mid.shape
    rows = long_rows - HALO
    short = rows // 3
    cols = wp[0].shape[1]

    def body(me_ref, mid_ref, t_ref, got_ref, gate_ref, *refs):
        wp_refs = refs[:count]
        after, blocks, s0, hold = refs[count:]
        me_now = me_ref[0]
        a = mid_ref[...] + t_ref[...] + got_ref[...].astype(F32)
        spread_write(hold, a)
        after[...] = a[HALO:, :]
        parts = []
        for k in range(3):
            part = strided_read(hold, HALO - 2 + k, short)
            if k < 2:
                part = jnp.where(gate_ref[0:short, :] > 0.0, part, 0.0)
            parts.append(part)
        z = jnp.concatenate(parts, axis=1).astype(BF)
        for at in range(count):
            blocks[at] = z[:, at * cols : (at + 1) * cols]
        acc = jnp.zeros((short, width), F32)
        for step in range(count):
            acc = acc + dot_nt(blocks[me_now ^ step], wp_refs[step][...])
        s0[...] = acc

    return local_kernel(
        body,
        "pool_forward",
        [((rows, width), F32), ((count, short, cols), BF), ((short, width), F32)],
        [((width // LANES, long_rows, LANES), F32)],
        me,
        mid,
        total_in,
        got,
        gate,
        *wp,
        flops=2 * short * width * 3 * width,
    )


def up_backward(me, cot, wu):
    count = len(wu)
    rows, width = cot.shape
    short = rows // 3
    cols = wu[0].shape[1]

    def body(me_ref, cot_ref, *refs):
        wu_refs = refs[:count]
        blocks, full, low, hold = refs[count:]
        me_now = me_ref[0]
        spread_write(hold, cot_ref[...].astype(F32))
        lifted = jnp.concatenate([strided_read(hold, k, short) for k in range(3)], axis=1).astype(BF)
        for at in range(count):
            blocks[at] = lifted[:, at * cols : (at + 1) * cols]
        acc = jnp.zeros((short, width), F32)
        for step in range(count):
            acc = acc + dot_nt(blocks[me_now ^ step], wu_refs[step][...])
        full[...] = acc
        low[...] = acc.astype(BF)

    return local_kernel(
        body,
        "up_backward",
        [((count, short, cols), BF), ((short, width), F32), ((short, width), BF)],
        [((width // LANES, rows, LANES), F32)],
        me,
        cot,
        *wu,
        flops=2 * short * width * 3 * width,
    )


def up_forward(me, mid, total_in, got, after, wu):
    count = len(wu)
    short, width = mid.shape
    rows = short * 3
    cols = wu[0].shape[1]

    def body(me_ref, mid_ref, t_ref, got_ref, after_ref, *refs):
        wu_refs = refs[:count]
        low, out, blocks, hold = refs[count:]
        me_now = me_ref[0]
        s1 = (mid_ref[...] + t_ref[...] + got_ref[...].astype(F32)).astype(BF)
        low[...] = s1
        for step in range(count):
            blocks[me_now ^ step] = dot_nn(s1, wu_refs[step][...])
        lift = jnp.concatenate([blocks[at] for at in range(count)], axis=1)
        for k in range(3):
            strided_write(hold, k, short, lift[:, k * width : (k + 1) * width])
        out[...] = (after_ref[...] + spread_read(hold)).astype(BF)

    return local_kernel(
        body,
        "up_forward",
        [((short, width), BF), ((rows, width), BF)],
        [((count, short, cols), F32), ((width // LANES, rows, LANES), F32)],
        me,
        mid,
        total_in,
        got,
        after,
        *wu,
        flops=2 * short * width * 3 * width,
    )


def pool_backward(me, ds0, ds0_next, gate, wp, cot):
    count = len(wp)
    short, width = ds0.shape
    rows = short * 3
    cols = wp[0].shape[1]

    def body(me_ref, ds0_ref, next_ref, gate_ref, cot_ref, *refs):
        wp_refs = refs[:count]
        full, low, blocks, hold, spread = refs[count:]
        me_now = me_ref[0]
        grad = jnp.concatenate([ds0_ref[...], next_ref[...]], axis=0)
        for step in range(count):
            blocks[me_now ^ step] = dot_nn(grad, wp_refs[step][...])
        for at in range(count):
            hold[:, at * cols : (at + 1) * cols] = blocks[at]
        strided_write(spread, 0, short, hold[0:short, 2 * width : 3 * width])
        open_gate = gate_ref[1 : short + 1, :] > 0.0
        for k in range(2):
            part = hold[1 : short + 1, k * width : (k + 1) * width]
            strided_write(spread, k + 1, short, jnp.where(open_gate, part, 0.0))
        da = cot_ref[...].astype(F32) + spread_read(spread)
        full[...] = da
        low[...] = da.astype(BF)

    return local_kernel(
        body,
        "pool_backward",
        [((rows, width), F32), ((rows, width), BF)],
        [((count, short + HALO, cols), F32), ((short + HALO, 3 * width), F32), ((width // LANES, rows, LANES), F32)],
        me,
        ds0,
        ds0_next,
        gate,
        cot,
        *wp,
        flops=2 * short * width * 3 * width,
    )


def flip(value, step):
    bit = 1
    while bit <= step:
        if step & bit:
            value = value + bit - 2 * bit * lax.rem(lax.div(value, bit), 2)
        bit *= 2
    return value


class Net:
    def __init__(self, send, recv):
        self.send, self.recv, self.used, self.open = send, recv, 0, []

    def make(self, src, dst, device):
        at = self.used
        self.used += 1
        return pltpu.make_async_remote_copy(
            src_ref=src,
            dst_ref=dst,
            send_sem=self.send.at[at],
            recv_sem=self.recv.at[at],
            device_id=device,
            device_id_type=MESH,
        )

    def start(self, src, dst, device):
        copy = self.make(src, dst, device)
        copy.start()
        self.open.append(copy)
        return copy

    def finish(self):
        for copy in self.open:
            copy.wait_send()


class Flight:
    def __init__(self, net, dp, fs, fs_count, pieces, src):
        self.net, self.dp, self.fs, self.pieces = net, dp, fs, pieces
        self.top, self.copies, self.waited = fs_count // 2, {}, set()
        bit = self.top
        while bit:
            self.copies[bit] = net.start(src, pieces.at[bit], (dp, flip(fs, bit)))
            bit //= 2

    def ready(self, step):
        if step and step not in self.waited:
            self.waited.add(step)
            self.copies[step].wait_recv()

    def relay(self):
        known, bit = [self.top], self.top // 2
        while bit:
            fresh = []
            for step in known:
                self.ready(step)
                there = (self.dp, flip(self.fs, bit))
                self.copies[step + bit] = self.net.start(self.pieces.at[step], self.pieces.at[step + bit], there)
                fresh.append(step + bit)
            known = known + [bit] + fresh
            bit //= 2

    def all_ready(self):
        for step in sorted(self.copies):
            self.ready(step)


def doc_bounds(triples, docs):
    lane = lax.broadcasted_iota(jnp.int32, (1, LANES), 1)
    lane = jnp.where(lane >= HEAD, lane - HEAD, lane)
    first = jnp.full((1, LANES), -1, jnp.int32)
    end = jnp.full((1, LANES), -1, jnp.int32)
    at = jnp.int32(0)
    for j in range(docs):
        here = lane == j
        first = jnp.where(here, at, first)
        at = at + triples[0, j]
        end = jnp.where(here, at, end)
    return first, end, lane


def softmax_block(ks, qs, h, r, stop):
    s = scores_t(ks, qs, h, r, stop)
    e = jnp.exp(s - jnp.max(s, axis=0, keepdims=True))
    return e, 1.0 / jnp.sum(e, axis=0, keepdims=True)


def forward_one(y_count, dp_count, fs_count, tokens, triples, weights, gains, cos, sin):
    rows, width = tokens.shape
    total, short = rows * fs_count, rows // 3
    long_rows = rows + HALO
    wqkv, wout, win, wdown, wpool, wup = weights
    rw = wqkv.shape[1]
    hd, fj, pc = wout.shape[2], win.shape[2], wpool.shape[1]
    heads = hd // HEAD
    docs = triples.shape[1]
    z_count = dp_count // y_count
    cw = pc + hd + 2 * fj
    blk = QB
    sems = 64 + 14 * dp_count

    def body(
        tok, triples_ref, q_in, o_in, i_in, d_in, p_in, u_in, g_in, cos_ref, sin_ref,
        n1, qkv, att_rel, wo_own, n2, mid, after, z_out, s0_out, wq_out, wb, wp, wq1_out, wc, gain_out,
        toks, st_q, wq0, wq1, gall, wo, wo_at, att, qs, ks, vt, turned, hold, work, low, part, m_tail, part_tail,
        sbuf, rbuf, xsend, xrecv, acc, thin, send_sem, recv_sem,
    ):
        dp, fs = lax.axis_index("dp"), lax.axis_index("fsdp")
        net = Net(send_sem, recv_sem)

        def own(buf):
            return buf.at[pl.ds(pl.multiple_of(dp * rw, 16), rw), :]

        def of(buf, step):
            return buf.at[pl.ds(pl.multiple_of(flip(dp, step) * rw, 16), rw), :]

        for b in range(2):
            for t in range(3):
                st_q[b, t] = q_in[b, :, t * hd : (t + 1) * hd].astype(BF)
        here = pl.ds(pl.multiple_of(dp * rw, 16), rw)
        gall[here, :] = jnp.concatenate([g_in[...], jnp.zeros((rw, LANES - 4), F32)], axis=1).astype(BF)
        wo[0, here, :] = o_in[0].astype(BF)
        wb[here, 0:fj] = i_in[0].astype(BF)
        wb[here, fj : 2 * fj] = d_in[0].astype(BF)
        wp[0, here, :] = p_in[...].astype(BF)
        wc[here, 0:pc] = u_in[...].astype(BF)
        wc[here, pc : pc + hd] = o_in[1].astype(BF)
        wc[here, pc + hd : pc + hd + fj] = i_in[1].astype(BF)
        wc[here, pc + hd + fj : cw] = d_in[1].astype(BF)

        barrier = pltpu.get_barrier_semaphore()
        for m in range(z_count):
            for e in range(fs_count):
                if m or e:
                    there = (flip(dp, m * y_count), flip(fs, e))
                    pl.semaphore_signal(barrier, inc=1, device_id=there, device_id_type=MESH)
        for j in range(1, y_count):
            pl.semaphore_signal(barrier, inc=1, device_id=(flip(dp, j), fs), device_id_type=MESH)
        pl.semaphore_wait(barrier, z_count * fs_count - 1 + y_count - 1)

        def along_z(bufs):
            found = [[] for _ in range(z_count)]
            for m in range(1, z_count):
                for buf in bufs:
                    found[m].append(net.start(own(buf), own(buf), (flip(dp, m * y_count), fs)))
            return found

        def along_y(bufs, m):
            return [
                net.start(of(buf, m * y_count), of(buf, m * y_count), (flip(dp, j), fs))
                for j in range(1, y_count)
                for buf in bufs
            ]

        def wait_all(copies):
            for copy in copies:
                copy.wait_recv()

        def heads_along_z(b, wq):
            found = []
            for m in range(z_count):
                line = []
                for t in range(3):
                    place = 3 * fs + t
                    kind, to = lax.div(place, fs_count), lax.rem(place, fs_count)
                    copy = net.make(st_q.at[b, t], wq.at[kind, here, :], (flip(dp, m * y_count), to))
                    if m == 0:

                        @pl.when(to != fs)
                        def _():
                            copy.start()

                        @pl.when(to == fs)
                        def _():
                            wq[kind, here, :] = st_q[b, t]

                        line.append((copy, to != fs))
                    else:
                        copy.start()
                        net.open.append(copy)
                        line.append((copy, None))
                found.append(line)
            return found

        def heads_along_y(wq, line, m):
            for copy, when in line:
                if when is None:
                    copy.wait_recv()
                else:

                    @pl.when(when)
                    def _():
                        copy.wait_recv()
                        copy.wait_send()

            at = pl.ds(pl.multiple_of(flip(dp, m * y_count) * rw, 16), rw)
            return [
                net.start(wq.at[:, at, :], wq.at[:, at, :], (flip(dp, j), fs)) for j in range(1, y_count)
            ]


        def spread(pieces, src):
            return Flight(net, dp, fs, fs_count, pieces, src)

        heads0 = heads_along_z(0, wq0)
        gz = along_z([gall])
        y0 = along_y([gall], 0)
        tk = spread(toks, tok)
        toks[0] = tok[...]
        oz = along_z([wo.at[0]])
        y1 = along_y([wo.at[0]], 0)
        lane_first, lane_end, lane = doc_bounds(triples_ref, docs)
        for m in range(z_count):
            y0 += heads_along_y(wq0, heads0[m], m)
            if m:
                wait_all(gz[m])
                y0 += along_y([gall], m)
        bz = along_z([wb])
        y2 = along_y([wb], 0)
        for m in range(1, z_count):
            wait_all(oz[m])
            y1 += along_y([wo.at[0]], m)
        tk.relay()
        wait_all(y0)
        gain_rows = gall[...].astype(F32).T[0:8, :]
        gain_out[...] = gain_rows
        for t in range(3):
            wq_out[:, t * hd : (t + 1) * hd] = wq0[t]
        for e in range(fs_count):
            tk.ready(e)
            base = pl.multiple_of(flip(fs, e) * rows, 16)
            for r in range(0, rows, LANES):
                block = toks[e, r : r + LANES, :].astype(F32)
                n1[pl.ds(base + r, LANES), :] = layer_norm(block, gain_rows[0:1]).astype(BF)

        lane_head = lax.broadcasted_iota(jnp.int32, (blk, LANES), 1)
        for r in range(0, total, blk):
            at = slice(r, r + blk)
            got = dot_nn(n1[at, :], wq_out[...])
            q, k, v = got[:, :hd], got[:, hd : 2 * hd], got[:, 2 * hd :]
            q = (q * cos_ref[at, :] + partner(q) * sin_ref[at, :]).astype(BF)
            k = (k * cos_ref[at, :] + partner(k) * sin_ref[at, :]).astype(BF)
            qkv[at, 0:hd] = q
            qkv[at, hd : 2 * hd] = k
            qkv[at, 2 * hd : 3 * hd] = v.astype(BF)
            row = lax.broadcasted_iota(jnp.int32, (blk, LANES), 0) + r
            inside = (row >= 3 * lane_first) & (row < 3 * lane_end)
            fk = jnp.where(inside, 1.0, 0.0)
            fq = jnp.where(inside | (lane >= docs), 0.0, MASKED)
            head_inputs(qs, ks, at, q.astype(F32), k.astype(F32), fq, fk, heads)
            vt[:, at] = v.T.astype(BF)

        flights = []
        for n, r in enumerate(range(0, total, blk)):
            stop = r + blk
            found = []
            for h in range(heads):
                e, inv = softmax_block(ks, qs, h, r, stop)
                found.append(dot_nn(vt[h * HEAD : (h + 1) * HEAD, 0:stop], e.astype(BF)) * inv)
            att[0, r:stop, :] = jnp.concatenate(found, axis=0).T.astype(BF)
            flights.append(spread(att.at[:, r:stop, :], att.at[0, r:stop, :]))
            if n == 0:
                wait_all(y1)
                wo_f = spread(wo, wo.at[0])
            if n == 2:
                for m in range(1, z_count):
                    wait_all(bz[m])
                    y2 += along_y([wb], m)
                wz = along_z([wp.at[0]])
                y3 = along_y([wp.at[0]], 0)
                heads1 = heads_along_z(1, wq1)
                cz = along_z([wc])
                y4 = along_y([wc], 0)
            if n == 3:
                wo_f.relay()
            if n >= 2:
                flights[n - 2].relay()
        for flight in flights[-2:]:
            flight.relay()
        wo_f.all_ready()
        for e in range(fs_count):
            wo_at[flip(fs, e)] = wo[e]
        for e in range(fs_count):
            hold[:, e * hd : (e + 1) * hd] = wo_at[e]
        for e in range(fs_count):
            base = pl.multiple_of(flip(fs, e) * hd, 16)
            turned[e * hd : (e + 1) * hd, :] = hold[pl.ds(base, hd), :]
        wo_own[...] = turned[0:hd, :]
        for flight in flights:
            flight.all_ready()
        for m in range(1, z_count):
            wait_all(wz[m])
            y3 += along_y([wp.at[0]], m)
        wait_all(y2)

        def mix(x_block, o_block, amount, keep_mid, keep_n2, out):
            work[0:amount, 0:width] = x_block.astype(F32) + dot_nn(o_block, turned[...])
            for r in range(0, amount, HEAD):
                m = work[r : r + HEAD, 0:width]
                if keep_mid is not None:
                    keep_mid[r : r + HEAD, :] = m
                value = layer_norm(m, gain_rows[1:2]).astype(BF)
                low[r : r + HEAD, 0:width] = value
                if keep_n2 is not None:
                    keep_n2[r : r + HEAD, :] = value
            work[0:amount, 0:fj] = dot_nn(low[0:amount, 0:width], wb[:, 0:fj])
            for r in range(0, amount, HEAD):
                low[r : r + HEAD, 0:fj] = gelu(work[r : r + HEAD, 0:fj]).astype(BF)
            out[0:amount, :] = dot_nt(low[0:amount, 0:fj], wb[:, fj : 2 * fj])

        for e in range(fs_count):
            at = pl.ds(pl.multiple_of(flip(fs, e) * rows + rows - HALO, 16), HALO)
            for k in range(fs_count):
                att_rel[e * HALO : (e + 1) * HALO, k * hd : (k + 1) * hd] = att[k, at, :]
        tails = jnp.concatenate([toks[e, rows - HALO : rows, :] for e in range(fs_count)], axis=0)
        mix(tails, att_rel[0 : fs_count * HALO, :], fs_count * HALO, m_tail, None, part_tail)

        for e in range(fs_count):
            base = pl.multiple_of(flip(fs, e) * rows, 16)
            for k in range(fs_count):
                att_rel[pl.ds(base, rows), k * hd : (k + 1) * hd] = att[k, pl.ds(base, rows), :]

        def before(e):
            place = flip(fs, e) + fs_count - 1
            place = lax.rem(place, fs_count)
            apart = jnp.int32(0)
            bit = 1
            while bit < fs_count:
                one = lax.rem(lax.div(place, bit), 2)
                two = lax.rem(lax.div(fs, bit), 2)
                apart = apart + bit * lax.rem(one + two, 2)
                bit *= 2
            return pl.multiple_of(apart * HALO, 16)

        def partial_for(e, out):
            base = pl.multiple_of(flip(fs, e) * rows, 16)
            mix(
                toks[e],
                att_rel[pl.ds(base, rows), :],
                rows,
                mid if e == 0 else None,
                n2.at[e * rows : (e + 1) * rows, :],
                part,
            )
            out[0:HALO, :] = part_tail[pl.ds(before(e), HALO), :].astype(out.dtype)
            out[HALO:long_rows, :] = part[0:rows, :].astype(out.dtype)

        half = fs_count // 2
        first_hops = {}
        for j in reversed(range(half)):
            partial_for(2 * j + 1, sbuf.at[j])
            first_hops[j] = net.start(sbuf.at[j], rbuf.at[j], (dp, flip(fs, 1)))
            if j == half - 1:
                for m in range(z_count):
                    y4 += heads_along_y(wq1, heads1[m], m)
                wait_all(y3)
                wp_f = spread(wp, wp.at[0])
            if j:
                partial_for(2 * j, acc.at[j])
                first_hops[j].wait_recv()
                acc[j] = acc[j] + rbuf[j].astype(F32)
                if half == 2:
                    xsend[0] = acc[1].astype(BF)
                    last_hop = net.start(xsend.at[0], xrecv.at[0], (dp, flip(fs, 2)))
            if j == half - 1:
                for m in range(1, z_count):
                    wait_all(cz[m])
                    y4 += along_y([wc], m)
        partial_for(0, acc.at[0])
        first_hops[0].wait_recv()
        acc[0] = acc[0] + rbuf[0].astype(F32)
        wp_f.relay()
        if half > 2:
            bit, active = 2, list(range(half))
            slot = 0
            while bit < fs_count:
                stay = [j for j in active if not (2 * j) & bit]
                hops = {}
                for j in stay:
                    give = j + bit // 2
                    xsend[slot] = acc[give].astype(BF)
                    hops[j] = (net.start(xsend.at[slot], xrecv.at[slot], (dp, flip(fs, bit))), slot)
                    slot += 1
                for j in stay:
                    hops[j][0].wait_recv()
                    acc[j] = acc[j] + xrecv[hops[j][1]].astype(F32)
                active, bit = stay, bit * 2
        elif half == 2:
            last_hop.wait_recv()
            acc[0] = acc[0] + xrecv[0].astype(F32)
        a_tail = acc[0, 0:HALO, :] + m_tail[pl.ds(before(0), HALO), :]
        a_own = acc[0, HALO:long_rows, :] + mid[...]
        after[...] = a_own
        for c in range(width // LANES):
            thin[c, 0:HALO, :] = a_tail[:, c * LANES : (c + 1) * LANES]
            thin[c, HALO:long_rows, :] = a_own[:, c * LANES : (c + 1) * LANES]

        row = lax.broadcasted_iota(jnp.int32, (short, LANES), 0) + fs * short
        begins = jnp.max(jnp.where(row == lane_first, 1.0, 0.0), axis=1, keepdims=True)
        parts = []
        for k in range(3):
            value = strided_read(thin, HALO - 2 + k, short)
            parts.append(jnp.where(begins > 0.0, 0.0, value) if k < 2 else value)
        z = jnp.concatenate(parts, axis=1).astype(BF)
        for e in range(fs_count):
            z_out[e] = z[:, e * pc : (e + 1) * pc]
        pooled = jnp.zeros((short, width), F32)
        for e in range(fs_count):
            wp_f.ready(e)
            pooled = pooled + dot_nt(z_out[flip(fs, e)], wp[e])
        s0_out[...] = pooled
        wait_all(y4)
        for t in range(3):
            wq1_out[:, t * hd : (t + 1) * hd] = wq1[t]
        net.finish()

    half = fs_count // 2
    outs = [
        ((total, width), BF),
        ((total, 3 * hd), BF),
        ((total, width), BF),
        ((hd, width), BF),
        ((total, width), BF),
        ((rows, width), F32),
        ((rows, width), F32),
        ((fs_count, short, pc), BF),
        ((short, width), F32),
        ((width, 3 * hd), BF),
        ((width, 2 * fj), BF),
        ((fs_count, width, pc), BF),
        ((width, 3 * hd), BF),
        ((width, cw), BF),
        ((8, width), F32),
    ]
    wide = max(width, fj)
    scratch = [
        ((fs_count, rows, width), BF),
        ((2, 3, rw, hd), BF),
        ((3, width, hd), BF),
        ((3, width, hd), BF),
        ((width, LANES), BF),
        ((fs_count, width, hd), BF),
        ((fs_count, width, hd), BF),
        ((fs_count, total, hd), BF),
        ((heads, total, LANES), BF),
        ((heads, total, LANES), BF),
        ((hd, total), BF),
        ((width, width), BF),
        ((width, width), BF),
        ((rows, wide), F32),
        ((rows, wide), BF),
        ((rows, width), F32),
        ((fs_count * HALO, width), F32),
        ((fs_count * HALO, width), F32),
        ((half, long_rows, width), BF),
        ((half, long_rows, width), BF),
        ((half - 1, long_rows, width), BF),
        ((half - 1, long_rows, width), BF),
        ((half, long_rows, width), F32),
        ((width // LANES, long_rows, LANES), F32),
    ]
    return pl.pallas_call(
        body,
        out_shape=[jax.ShapeDtypeStruct(s, t) for s, t in outs],
        in_specs=[vmem(), smem()] + [vmem()] * 9,
        out_specs=[vmem()] * len(outs),
        scratch_shapes=[pltpu.VMEM(s, t) for s, t in scratch] + [pltpu.SemaphoreType.DMA((sems,))] * 2,
        compiler_params=pltpu.CompilerParams(collective_id=3, has_side_effects=True, vmem_limit_bytes=VMEM_BYTES),
        cost_estimate=cost(2e10, 3e7),
        name="forward_one",
    )(tokens, triples, *weights, gains, cos, sin)


class RowSum:
    def __init__(self, net, place, grad, ybuf, zsend, zrecv, total, q_send=None, q_recv=None, q_total=None):
        self.net, self.grad, self.ybuf = net, grad, ybuf
        self.zsend, self.zrecv, self.total = zsend, zrecv, total
        self.q_send, self.q_recv, self.q_total = q_send, q_recv, q_total
        self.dp, self.fs, self.y_count, self.z_count, self.fs_count, self.rw = place
        self.ys, self.zs, self.qs = {}, {}, []

    def rows_of(self, step):
        return pl.ds(pl.multiple_of(flip(self.dp, step) * self.rw, 16), self.rw)

    def start(self):
        for m in list(range(1, self.z_count)) + [0]:
            self.ys[m] = [
                self.net.start(
                    self.grad.at[self.rows_of(m * self.y_count + j), :],
                    self.ybuf.at[j - 1, m],
                    (flip(self.dp, j), self.fs),
                )
                for j in range(1, self.y_count)
            ]
        if self.q_send is not None:
            self.q_base = self.net.used
            self.net.used += 3 * self.z_count

    def owner(self, kind):
        place = kind * self.fs_count + self.fs
        return lax.div(place, 3), lax.rem(place, 3)

    def service(self, m):
        for copy in self.ys[m]:
            copy.wait_recv()
        got = self.grad[self.rows_of(m * self.y_count), :].astype(F32)
        for j in range(1, self.y_count):
            got = got + self.ybuf[j - 1, m].astype(F32)
        there = flip(self.dp, m * self.y_count)
        lo = 0
        if self.q_send is not None:
            hd = self.q_send.shape[3]
            lo = 3 * hd
            for kind in range(3):
                to, slot = self.owner(kind)
                self.q_send[m, kind] = got[:, kind * hd : (kind + 1) * hd].astype(BF)
                copy = pltpu.make_async_remote_copy(
                    src_ref=self.q_send.at[m, kind],
                    dst_ref=self.q_recv.at[m, slot],
                    send_sem=self.net.send.at[self.q_base + 3 * m + kind],
                    recv_sem=self.net.recv.at[self.q_base + 3 * m + slot],
                    device_id=(there, to),
                    device_id_type=MESH,
                )
                if m:
                    copy.start()
                    self.qs.append((copy, None))
                else:

                    @pl.when(to != self.fs)
                    def _():
                        copy.start()

                    @pl.when(to == self.fs)
                    def _():
                        self.q_recv[0, slot] = self.q_send[0, kind]

                    self.qs.append((copy, to != self.fs))
        width = self.total.shape[1]
        rest = got[:, lo : lo + width]
        if m:
            self.zsend[m - 1] = rest.astype(BF)
            self.zs[m] = self.net.start(self.zsend.at[m - 1], self.zrecv.at[m - 1], (there, self.fs))
        else:
            self.total[...] = rest

    def finish(self):
        rest = self.total[...]
        for m in range(1, self.z_count):
            self.zs[m].wait_recv()
            rest = rest + self.zrecv[m - 1].astype(F32)
        self.total[...] = rest
        if self.q_send is None:
            return
        for t in range(3):
            giver = lax.rem(3 * self.fs + t, self.fs_count)
            for m in range(self.z_count):
                landed = self.q_recv.at[m, t]
                wait = pltpu.make_async_copy(landed, landed, self.net.recv.at[self.q_base + 3 * m + t])
                if m:
                    wait.wait()
                else:

                    @pl.when(giver != self.fs)
                    def _():
                        wait.wait()

        for t in range(3):
            block = self.q_recv[0, t].astype(F32)
            for m in range(1, self.z_count):
                block = block + self.q_recv[m, t].astype(F32)
            self.q_total[t] = block
        for copy, when in self.qs:
            if when is None:
                copy.wait_send()
            else:

                @pl.when(when)
                def _():
                    copy.wait_send()


class Scatter:
    def __init__(self, net, dp, fs, fs_count, sbuf, rbuf, xsend, xrecv, acc):
        self.net, self.dp, self.fs, self.half = net, dp, fs, fs_count // 2
        self.sbuf, self.rbuf, self.xsend, self.xrecv, self.acc = sbuf, rbuf, xsend, xrecv, acc
        self.first, self.hops, self.slot = {}, {}, 0

    def send_odd(self, j):
        self.first[j] = self.net.start(self.sbuf.at[j], self.rbuf.at[j], (self.dp, flip(self.fs, 1)))

    def join(self, j):
        self.first[j].wait_recv()
        self.acc[j] = self.acc[j] + self.rbuf[j].astype(F32)

    def give(self, j):
        bit = (2 * j) & -(2 * j)
        slot = self.slot
        self.slot += 1
        self.xsend[slot] = self.acc[j].astype(BF)
        self.hops[j] = (self.net.start(self.xsend.at[slot], self.xrecv.at[slot], (self.dp, flip(self.fs, bit))), slot)

    def take(self, j):
        low = j & -j
        copy, slot = self.hops[j]
        copy.wait_recv()
        self.acc[j - low] = self.acc[j - low] + self.xrecv[slot].astype(F32)

    def sent(self):
        for copy in list(self.first.values()) + [copy for copy, _ in self.hops.values()]:
            copy.wait_send()
            self.net.open = [other for other in self.net.open if other is not copy]

    def upper(self):
        if self.half == 2:
            self.give(1)

    def finish(self):
        if self.half == 2:
            self.take(1)
            return
        bit = 1
        while bit < self.half:
            gives = [j for j in range(self.half) if j & bit and not j & (bit - 1)]
            for j in gives:
                self.give(j)
            for j in gives:
                self.take(j)
            bit *= 2


def query_rows(total):
    return QB if total <= 2048 else QB // 2


def backward_one(
    y_count, dp_count, fs_count, da, n2, ff, mid, gain_rows, qkv, wo_own, wq, cos, sin, triples, n1, att_rel, tokens, group_b
):
    rows, width = tokens.shape
    total = rows * fs_count
    fj, hd = ff.shape[1] // 2, wq.shape[1] // 3
    heads, docs = hd // HEAD, triples.shape[1]
    z_count, rw = dp_count // y_count, width // dp_count
    cb = group_b.shape[1]
    blk, half = query_rows(total), fs_count // 2
    blocks = total // blk
    sems = 96 + 12 * dp_count

    def body(
        da_ref, n2_ref, ff_ref, mid_ref, gain_ref, qkv_ref, wo_ref, wq_ref, cos_ref, sin_ref, triples_ref, n1_ref, att_ref, tok, gb,
        grad_in, dgain, sum_b, sum_ff, sum_o, sum_q,
        dfs, das, hid, slope, dpre, work, qs, ks, kt, dk, dv, dqkv, dm, cols, g_ff, g_at,
        sbuf, rbuf, xsend, xrecv, acc, yb, zsb, zrb, qsb, qrb, yf, zsf, zrf, ya, zsa, zra, qsa, qra, send_sem, recv_sem,
        *ps,
    ):
        dp, fs = lax.axis_index("dp"), lax.axis_index("fsdp")
        net = Net(send_sem, recv_sem)
        place = (dp, fs, y_count, z_count, fs_count, rw)
        dfs[0] = da_ref[...].astype(BF)
        barrier = pltpu.get_barrier_semaphore()
        for m in range(z_count):
            for e in range(fs_count):
                if m or e:
                    there = (flip(dp, m * y_count), flip(fs, e))
                    pl.semaphore_signal(barrier, inc=1, device_id=there, device_id_type=MESH)
        for j in range(1, y_count):
            pl.semaphore_signal(barrier, inc=1, device_id=(flip(dp, j), fs), device_id_type=MESH)
        pl.semaphore_wait(barrier, z_count * fs_count - 1 + y_count - 1)

        def spread(pieces):
            return Flight(net, dp, fs, fs_count, pieces, pieces.at[0])

        df_f = spread(dfs)
        sum_of_b = RowSum(net, place, gb, yb, zsb, zrb, sum_b, qsb, qrb, sum_q.at[1])
        sum_of_b.start()

        def activate(e):
            at = slice(e * rows, (e + 1) * rows)
            work[:, 0:fj] = dot_nn(n2_ref[at, :], ff_ref[:, 0:fj])
            for r in range(0, rows, HEAD):
                value, rate = gelu_both(work[r : r + HEAD, 0:fj])
                hid[e * rows + r : e * rows + r + HEAD, :] = value.astype(BF)
                slope[e * rows + r : e * rows + r + HEAD, :] = rate.astype(BF)

        def pull(e, out):
            work[:, 0:fj] = dot_nn(dfs[e], ff_ref[:, fj : 2 * fj])
            for r in range(0, rows, HEAD):
                at = slice(e * rows + r, e * rows + r + HEAD)
                dpre[at, :] = (work[r : r + HEAD, 0:fj] * slope[at, :].astype(F32)).astype(BF)
            out[...] = dot_nt(dpre[e * rows : (e + 1) * rows, :], ff_ref[:, 0:fj]).astype(out.dtype)

        def part_into(scatter, e, fill):
            if e % 2:
                fill(e, scatter.sbuf.at[e // 2])
                scatter.send_odd(e // 2)
            else:
                fill(e, scatter.acc.at[e // 2])

        ff_sum = Scatter(net, dp, fs, fs_count, sbuf, rbuf, xsend, xrecv, acc)
        for e in range(fs_count):
            activate(e)
            if e < 2:
                df_f.ready(e)
                part_into(ff_sum, e, pull)
        df_f.relay()
        sum_of_b.service(1)
        for e in range(2, fs_count):
            df_f.ready(e)
            part_into(ff_sum, e, pull)
        for j in range(1, half):
            ff_sum.join(j)
        ff_sum.upper()
        for m in range(2, z_count):
            sum_of_b.service(m)
        ff_sum.join(0)
        g_ff[:, 0:fj] = dot_tn(n2_ref[...], dpre[...]).astype(BF)
        g_ff[:, fj : 2 * fj] = dot_tn(dfs[...].reshape(total, width), hid[...]).astype(BF)
        sum_of_b.service(0)
        sum_of_ff = RowSum(net, place, g_ff, yf, zsf, zrf, sum_ff)
        sum_of_ff.start()

        lane_first, lane_end, lane = doc_bounds(triples_ref, docs)
        for r in range(0, total, blk):
            at = slice(r, r + blk)
            q = qkv_ref[at, 0:hd].astype(F32)
            k = qkv_ref[at, hd : 2 * hd].astype(F32)
            row = lax.broadcasted_iota(jnp.int32, (blk, LANES), 0) + r
            inside = (row >= 3 * lane_first) & (row < 3 * lane_end)
            fk = jnp.where(inside, 1.0, 0.0)
            fq = jnp.where(inside | (lane >= docs), 0.0, MASKED)
            head_inputs(qs, ks, at, q, k, fq, fk, heads)
            kt[:, at] = k.T.astype(BF)
            dk[at, :] = jnp.zeros((blk, LANES), F32)
            dv[at, :] = jnp.zeros((blk, LANES), F32)

        def recompute(n):
            r = n * blk
            for h in range(heads):
                e, inv = softmax_block(ks, qs, h, r, r + blk)
                ps[n][h] = (e * inv).astype(BF)

        for n in range(blocks // 2):
            recompute(n)

        ff_sum.finish()
        for r in range(0, rows, LANES):
            at = slice(r, r + LANES)
            dx, dg = layer_norm_back(mid_ref[at, :], gain_ref[1:2, :], acc[0, at, :])
            dx = dx + da_ref[at, :]
            dm[at, :] = dx
            das[0, at, :] = dx.astype(BF)
            dg = jnp.sum(dg, axis=0, keepdims=True)
            gain_two = dg if r == 0 else gain_two + dg
        da_f = spread(das)
        for n in range(blocks // 2, blocks):
            recompute(n)
        for m in range(1, z_count):
            sum_of_ff.service(m)
        sum_of_ff.service(0)
        da_f.relay()

        place_of = lax.broadcasted_iota(jnp.int32, (blk, LANES), 1) // HEAD
        for r in range(0, total, blk):
            at = slice(r, r + blk)
            q = widen(qkv_ref[at, 0:hd].astype(F32))
            for h in range(heads):
                qs[h, at, :] = jnp.where(place_of == h, q, 0.0).astype(BF)
        lane_head = lax.broadcasted_iota(jnp.int32, (rows, LANES), 1) // HEAD
        for e in range(fs_count):
            da_f.ready(e)
            base = pl.multiple_of(flip(fs, e) * rows, 16)
            do = widen(dot_nt(das[e], wo_ref[...]))
            for h in range(heads):
                ks[h, pl.ds(base, rows), :] = jnp.where(lane_head == h, do, 0.0).astype(BF)
            for k in range(fs_count):

                @pl.when(fs == k)
                def _():
                    cols[pl.ds(base, rows), :] = das[e, :, k * hd : (k + 1) * hd]

        g_out = dot_tn(att_ref[...], cols[...]).astype(BF)
        for e in range(fs_count):
            base = pl.multiple_of(flip(fs, e) * hd, 16)
            g_at[pl.ds(base, hd), 3 * hd : 4 * hd] = g_out[e * hd : (e + 1) * hd, :]
        sum_of_b.finish()

        for n in range(blocks):
            r, stop = n * blk, (n + 1) * blk
            at = slice(r, stop)
            found = []
            add_k = add_v = None
            for h in range(heads):
                p = ps[n][h]
                v = widen(qkv_ref[0:stop, 2 * hd : 3 * hd])
                grad = dot_nt(v, ks[h, at, :])
                wide = p.astype(F32)
                middle = jnp.sum(wide * grad, axis=0, keepdims=True)
                dr = (wide * (grad - middle) * 0.125).astype(BF)
                part_v = dot_nn(p, ks[h, at, :])
                part_k = dot_nn(dr, qs[h, at, :])
                add_v = part_v if add_v is None else add_v + part_v
                add_k = part_k if add_k is None else add_k + part_k
                found.append(dot_nn(kt[h * HEAD : (h + 1) * HEAD, 0:stop], dr))
            dk[0:stop, :] += add_k
            dv[0:stop, :] += add_v
            dq = jnp.concatenate(found, axis=0).T
            dqkv[at, 0:hd] = (dq * cos_ref[at, :] - partner(dq) * sin_ref[at, :]).astype(BF)
        for r in range(0, total, blk):
            at = slice(r, r + blk)
            grad = dk[at, 0:hd]
            dqkv[at, hd : 2 * hd] = (grad * cos_ref[at, :] - partner(grad) * sin_ref[at, :]).astype(BF)
            dqkv[at, 2 * hd : 3 * hd] = dv[at, 0:hd].astype(BF)
        g_at[:, 0 : 3 * hd] = dot_tn(n1_ref[...], dqkv[...]).astype(BF)
        sum_of_at = RowSum(net, place, g_at, ya, zsa, zra, sum_o, qsa, qra, sum_q.at[0])
        sum_of_at.start()

        ff_sum.sent()
        at_sum = Scatter(net, dp, fs, fs_count, sbuf, rbuf, xsend, xrecv, acc)

        def push_out(e, out):
            base = pl.multiple_of(flip(fs, e) * rows, 16)
            out[...] = dot_nt(dqkv[pl.ds(base, rows), :], wq_ref[...]).astype(out.dtype)

        for e in reversed(range(2, fs_count)):
            part_into(at_sum, e, push_out)
        part_into(at_sum, 1, push_out)
        for j in range(1, half):
            at_sum.join(j)
        at_sum.upper()
        for m in range(1, z_count):
            sum_of_at.service(m)
        sum_of_at.service(0)
        part_into(at_sum, 0, push_out)
        at_sum.join(0)
        sum_of_ff.finish()
        at_sum.finish()
        for r in range(0, rows, LANES):
            at = slice(r, r + LANES)
            dx, dg = layer_norm_back(tok[at, :].astype(F32), gain_ref[0:1, :], acc[0, at, :])
            grad_in[at, :] = dx + dm[at, :]
            dg = jnp.sum(dg, axis=0, keepdims=True)
            gain_one = dg if r == 0 else gain_one + dg
        which = lax.broadcasted_iota(jnp.int32, (8, width), 0)
        dgain[...] = jnp.where(which == 0, gain_one, jnp.where(which == 1, gain_two, 0.0))
        sum_of_at.finish()
        net.finish()

    outs = [
        ((rows, width), F32),
        ((8, width), F32),
        ((rw, cb - 3 * hd), F32),
        ((rw, 2 * fj), F32),
        ((rw, hd), F32),
        ((2, 3, rw, hd), F32),
    ]
    wide = max(width, fj)
    zy = (y_count - 1, z_count, rw)
    scratch = [
        ((fs_count, rows, width), BF),
        ((fs_count, rows, width), BF),
        ((total, fj), BF),
        ((total, fj), BF),
        ((total, fj), BF),
        ((rows, wide), F32),
        ((heads, total, LANES), BF),
        ((heads, total, LANES), BF),
        ((hd, total), BF),
        ((total, LANES), F32),
        ((total, LANES), F32),
        ((total, 3 * hd), BF),
        ((rows, width), F32),
        ((total, hd), BF),
        ((width, 2 * fj), BF),
        ((width, 4 * hd), BF),
        ((half, rows, width), BF),
        ((half, rows, width), BF),
        ((half - 1, rows, width), BF),
        ((half - 1, rows, width), BF),
        ((half, rows, width), F32),
        (zy + (cb,), BF),
        ((z_count - 1, rw, cb - 3 * hd), BF),
        ((z_count - 1, rw, cb - 3 * hd), BF),
        ((z_count, 3, rw, hd), BF),
        ((z_count, 3, rw, hd), BF),
        (zy + (2 * fj,), BF),
        ((z_count - 1, rw, 2 * fj), BF),
        ((z_count - 1, rw, 2 * fj), BF),
        (zy + (4 * hd,), BF),
        ((z_count - 1, rw, hd), BF),
        ((z_count - 1, rw, hd), BF),
        ((z_count, 3, rw, hd), BF),
        ((z_count, 3, rw, hd), BF),
    ]
    tail = [pltpu.VMEM((heads, (n + 1) * blk, blk), BF) for n in range(blocks)]
    arrays = (da, n2, ff, mid, gain_rows, qkv, wo_own, wq, cos, sin, triples, n1, att_rel, tokens, group_b)
    return pl.pallas_call(
        body,
        out_shape=[jax.ShapeDtypeStruct(s, t) for s, t in outs],
        in_specs=[vmem()] * 10 + [smem()] + [vmem()] * 4,
        out_specs=[vmem()] * len(outs),
        scratch_shapes=[pltpu.VMEM(s, t) for s, t in scratch] + [pltpu.SemaphoreType.DMA((sems,))] * 2 + tail,
        compiler_params=pltpu.CompilerParams(collective_id=4, has_side_effects=True, vmem_limit_bytes=VMEM_BYTES),
        cost_estimate=cost(4e10, 3e7),
        name="backward_one",
    )(*arrays)


def swap(value, axis, bit):
    return lax.ppermute(value, axis, [(i, i ^ bit) for i in range(lax.axis_size(axis))])


def gather_pieces(value):
    count = lax.axis_size("fsdp")
    pieces = {0: value}
    bit = count // 2
    while bit:
        for step in list(pieces):
            pieces[step ^ bit] = swap(pieces[step], "fsdp", bit)
        bit //= 2
    return [pieces[step] for step in range(count)]


def finish_scatter(keep, send):
    total = keep + swap(send, "fsdp", 1).astype(F32)
    bit = 2
    while total.shape[0] > 2:
        total = total[0::2] + swap(total[1::2].astype(BF), "fsdp", bit).astype(F32)
        bit *= 2
    return total[0], swap(total[1].astype(BF), "fsdp", bit)


def exchange_blocks(blocks, me):
    count = lax.axis_size("fsdp")
    out = []
    for step in range(count):
        block = lax.dynamic_index_in_dim(blocks, me ^ step, 0, keepdims=False)
        out.append(swap(block, "fsdp", step) if step else block)
    return out


def gather_rows(value, y_count):
    count = lax.axis_size("dp")
    pieces = {0: value}
    for step in range(y_count, count, y_count):
        pieces[step] = swap(value, "dp", step)
    for base in range(0, count, y_count):
        for step in range(1, y_count):
            pieces[base ^ step] = swap(pieces[base], "dp", step)
    return [pieces[step] for step in range(count)]


def assemble_rows(dp_index, pieces, widths):
    count = len(pieces)
    rows = pieces[0].shape[0]

    def body(me_ref, *refs):
        piece_refs, outs = refs[:count], refs[count:]
        me_now = me_ref[0]
        for step in range(count):
            base = pl.multiple_of((me_now ^ step) * rows, 16)
            at = 0
            for out, width in zip(outs, widths):
                out[pl.ds(base, rows), :] = piece_refs[step][:, at : at + width]
                at += width

    return local_kernel(body, "assemble_rows", [((rows * count, w), BF) for w in widths], [], dp_index, *pieces)


def scatter_rows(grad, dp_index, y_count):
    count = lax.axis_size("dp")
    rows = grad.shape[0] // count
    z_count = count // y_count
    z, y = dp_index // y_count, dp_index % y_count
    grid = grad.reshape(z_count, y_count, rows, grad.shape[1])
    total = lax.dynamic_index_in_dim(grid, y, 1, keepdims=False).astype(F32)
    for step in range(1, y_count):
        out = lax.dynamic_index_in_dim(grid, y ^ step, 1, keepdims=False)
        total = total + swap(out, "dp", step).astype(F32)
    low = total.astype(BF)
    own = lax.dynamic_index_in_dim(total, z, 0, keepdims=False)
    for step in range(1, z_count):
        out = lax.dynamic_index_in_dim(low, z ^ step, 0, keepdims=False)
        own = own + swap(out, "dp", step * y_count).astype(F32)
    return own


def head_order(block, inverse=False):
    count = lax.axis_size("fsdp")
    me = lax.axis_index("fsdp")
    hd = block.shape[-1] // 3
    if not inverse:
        got = [
            lax.ppermute(block[..., t * hd : (t + 1) * hd], "fsdp", [(j, (3 * j + t) % count) for j in range(count)])
            for t in range(3)
        ]
        kinds = []
        for t in range(3):
            table = np.zeros(count, np.int32)
            for j in range(count):
                table[(3 * j + t) % count] = (3 * j + t) // count
            kinds.append(jnp.asarray(table)[me])
        return jnp.concatenate(
            [sum(jnp.where(kinds[t] == kind, got[t], 0) for t in range(3)) for kind in range(3)], axis=-1
        )
    mine = [block[..., t * hd : (t + 1) * hd] for t in range(3)]
    out = []
    for t in range(3):
        table = np.zeros(count, np.int32)
        for j in range(count):
            table[(3 * j + t) % count] = (3 * j + t) // count
        kind = jnp.asarray(table)[me]
        chosen = sum(jnp.where(kind == other, mine[other], 0) for other in range(3))
        out.append(lax.ppermute(chosen, "fsdp", [((3 * j + t) % count, j) for j in range(count)]))
    return jnp.concatenate(out, axis=-1)


def owners_of(amount, dp_count, fs_count):
    found = []
    half = dp_count // 2
    for k in range(amount):
        found.append((dp_count // 4 + k % half, (2 * (k // half)) % fs_count + (2 * (k // half)) // fs_count))
    return found


def round_up(width):
    return -(-width // LANES) * LANES


def newton_schulz(box, x, norm, count, width, dp_count, rw, done):
    coef_a, coef_b, coef_c = NS_COEFS
    rows = dp_count * rw
    square = jnp.zeros((1, 1), F32)
    for at in range(count):
        block = box[at * dp_count : (at + 1) * dp_count, :, 0:width].reshape(rows, width)
        x[:, at * width : (at + 1) * width] = block
        wide = block.astype(F32)
        square = square + jnp.sum(jnp.sum(wide * wide, axis=0, keepdims=True), axis=1, keepdims=True)
    length = jnp.sqrt(square)
    norm[...] = jnp.broadcast_to(length, norm.shape)
    scale = 1.0 / (length + NORM_EPS)
    span = count * width
    for turn in range(NS_STEPS):
        gram = dot_nt(x[:, 0:span], x[:, 0:span])
        if turn == 0:
            gram = gram * (scale * scale)
        gram = gram.astype(BF)
        poly = (coef_b * gram.astype(F32) + coef_c * dot_nn(gram, gram)).astype(BF)
        for at in range(count):
            here = slice(at * width, (at + 1) * width)
            block = x[:, here]
            new = coef_a * block.astype(F32) + dot_nn(poly, block)
            if turn == 0:
                new = new * scale
            if turn < NS_STEPS - 1:
                x[:, here] = new.astype(BF)
            else:
                box[at * dp_count : (at + 1) * dp_count, :, 0:width] = new.astype(BF).reshape(dp_count, rw, width)
                done(at)


def muon(y_count, dp_count, fs_count, sums, moments, dgains):
    sum_q, sum_o, sum_ff, sum_rest = sums
    rw, hd = sum_o.shape
    fj = sum_ff.shape[1] // 2
    pc = moments[4].shape[1]
    width = rw * dp_count
    z_count = dp_count // y_count
    devices = dp_count * fs_count
    widths = [fj, fj, fj, fj, 3 * hd, 3 * hd, pc, pc, hd, hd]
    widths = [round_up(w) for w in widths]
    amount, wide = len(widths), max(widths)
    owners = owners_of(amount, dp_count, fs_count)
    classes = sorted(set(widths))
    sems = 64 + amount

    def body(
        q_ref, o_ref, ff_ref, rest_ref, mq, mo, mi, md, mp, mu, ga, gb_one, gb_two,
        out, norms, dgain, box, x, norm, tiles, tsend, *rest_refs,
    ):
        pieces = rest_refs[:amount]
        send_sem, recv_sem, push_send, push_recv, give_send, give_recv, norm_send, norm_recv = rest_refs[amount:]
        dp, fs = lax.axis_index("dp"), lax.axis_index("fsdp")
        slot = fs * dp_count + dp
        net = Net(send_sem, recv_sem)

        def put(k, value):
            have = value.shape[1]
            if have < widths[k]:
                value = jnp.concatenate([value, jnp.zeros((rw, widths[k] - have), F32)], axis=1)
            pieces[k][...] = value.astype(BF)

        at = 2 * pc
        put(0, MOMENT_DECAY * mi[0] + ff_ref[:, 0:fj])
        put(1, MOMENT_DECAY * mi[1] + rest_ref[:, at : at + fj])
        put(2, MOMENT_DECAY * md[0] + ff_ref[:, fj : 2 * fj])
        put(3, MOMENT_DECAY * md[1] + rest_ref[:, at + fj : at + 2 * fj])
        for b in range(2):
            put(4 + b, MOMENT_DECAY * mq[b] + jnp.concatenate([q_ref[b, t] for t in range(3)], axis=1))
        put(6, MOMENT_DECAY * mp[...] + rest_ref[:, 0:pc])
        put(7, MOMENT_DECAY * mu[...] + rest_ref[:, pc : 2 * pc])
        put(8, MOMENT_DECAY * mo[0] + o_ref[...])
        put(9, MOMENT_DECAY * mo[1] + rest_ref[:, at + 2 * fj :])
        which = lax.broadcasted_iota(jnp.int32, (8, width), 0)
        tiles[0] = jnp.where(
            which < 2, ga[...], jnp.where(which == 2, gb_one[0:1, :], jnp.where(which == 3, gb_two[0:1, :], 0.0))
        )
        if any(w != wide for w in widths):
            box[...] = jnp.zeros(box.shape, BF)

        barrier = pltpu.get_barrier_semaphore()

        def greet(t, carry):
            @pl.when(t != slot)
            def _():
                there = (lax.rem(t, dp_count), lax.div(t, dp_count))
                pl.semaphore_signal(barrier, inc=1, device_id=there, device_id_type=MESH)

            return carry

        lax.fori_loop(0, devices, greet, 0)
        pl.semaphore_wait(barrier, devices - 1)

        mine = [(dp == owners[k][0]) & (fs == owners[k][1]) for k in range(amount)]
        for k in range(amount):
            copy = pltpu.make_async_remote_copy(
                src_ref=pieces[k],
                dst_ref=box.at[slot, :, 0 : widths[k]],
                send_sem=push_send.at[k],
                recv_sem=push_recv,
                device_id=owners[k],
                device_id_type=MESH,
            )

            @pl.when(jnp.logical_not(mine[k]))
            def _():
                copy.start()

            @pl.when(mine[k])
            def _():
                box[slot, :, 0 : widths[k]] = pieces[k][...]

        hop = net.start(tiles.at[0], tiles.at[1], (dp, flip(fs, 1)))

        for k in range(amount):

            @pl.when(mine[k])
            def _():
                landed = box.at[0 : devices - 1, :, 0 : widths[k]]
                pltpu.make_async_copy(landed, landed, push_recv).wait()

        which_k = jnp.int32(0)
        for k in range(1, amount):
            which_k = which_k + k * mine[k].astype(jnp.int32)
        for w in classes:
            chosen = None
            for k in range(amount):
                if widths[k] == w:
                    chosen = mine[k] if chosen is None else chosen | mine[k]

            @pl.when(chosen)
            def _():
                def done(block):
                    def give(i, carry):
                        t = block * dp_count + i

                        @pl.when(t != slot)
                        def _():
                            pltpu.make_async_remote_copy(
                                src_ref=box.at[t, :, 0:w],
                                dst_ref=out.at[which_k, :, 0:w],
                                send_sem=give_send,
                                recv_sem=give_recv.at[which_k],
                                device_id=(i, block),
                                device_id_type=MESH,
                            ).start()
                            pltpu.make_async_remote_copy(
                                src_ref=norm,
                                dst_ref=norms.at[which_k],
                                send_sem=norm_send,
                                recv_sem=norm_recv.at[which_k],
                                device_id=(i, block),
                                device_id_type=MESH,
                            ).start()

                        return carry

                    lax.fori_loop(0, dp_count, give, 0)

                newton_schulz(box, x, norm, fs_count, w, dp_count, rw, done)
                out[which_k, :, 0:w] = box[slot, :, 0:w]
                norms[which_k] = norm[...]

        total = tiles[0]
        hop.wait_recv()
        total = total + tiles[1]
        at = 2
        bit = 2
        hops = [((dp, flip(fs, 1 << n)), None) for n in range(1, fs_count.bit_length() - 1)]
        hops += [((flip(dp, 1 << n), fs), None) for n in range(dp_count.bit_length() - 1)]
        for n, (there, _) in enumerate(hops):
            tsend[n] = total
            hop = net.start(tsend.at[n], tiles.at[2 + n], there)
            hop.wait_recv()
            total = total + tiles[2 + n]
        dgain[...] = total

        for k in range(amount):
            w = widths[k]

            @pl.when(jnp.logical_not(mine[k]))
            def _():
                landed = out.at[k, :, 0:w]
                pltpu.make_async_copy(landed, landed, give_recv.at[k]).wait()
                pltpu.make_async_copy(norms.at[k], norms.at[k], norm_recv.at[k]).wait()
                pltpu.make_async_copy(pieces[k], pieces[k], push_send.at[k]).wait()

            @pl.when(mine[k])
            def _():
                left = box.at[0 : devices - 1, :, 0:w]
                pltpu.make_async_copy(left, left, give_send).wait()

                def drain(t, carry):
                    pltpu.make_async_copy(norm, norm, norm_send).wait()
                    return carry

                lax.fori_loop(0, devices - 1, drain, 0)

        net.finish()

    hops = (fs_count.bit_length() - 1) + (dp_count.bit_length() - 1)
    outs = [((amount, rw, wide), BF), ((amount, 8, LANES), F32), ((8, width), F32)]
    scratch = [
        ((devices, rw, wide), BF),
        ((width, fs_count * wide), BF),
        ((8, LANES), F32),
        ((hops + 1, 8, width), F32),
        ((hops, 8, width), F32),
    ] + [((rw, w), BF) for w in widths]
    dma = pltpu.SemaphoreType.DMA
    return pl.pallas_call(
        body,
        out_shape=[jax.ShapeDtypeStruct(s, t) for s, t in outs],
        in_specs=[vmem()] * 13,
        out_specs=[vmem()] * len(outs),
        scratch_shapes=[pltpu.VMEM(s, t) for s, t in scratch]
        + [dma((sems,)), dma((sems,)), dma((amount,)), dma, dma, dma((amount,)), dma, dma((amount,))],
        compiler_params=pltpu.CompilerParams(collective_id=1, has_side_effects=True, vmem_limit_bytes=VMEM_BYTES),
        name="muon",
    )(sum_q, sum_o, sum_ff, sum_rest, *moments, *dgains)


def update(dp_arr, sums, results, dgain, moments, weights, m_gains, gains):
    sum_q, sum_o, sum_ff, sum_rest = sums
    rw, hd = sum_o.shape
    fj = sum_ff.shape[1] // 2
    pc = moments[4].shape[1]
    width = dgain.shape[1]

    def body(me_ref, q_ref, o_ref, ff_ref, rest_ref, res, dg, *refs):
        m_in, w_in, (mg, g), refs = refs[:6], refs[6:12], refs[12:14], refs[14:]
        m_out, w_out, (mg_out, g_out), turned = refs[:6], refs[6:12], refs[12:14], refs[14]
        at = 2 * pc
        grads = [
            [jnp.concatenate([q_ref[b, t] for t in range(3)], axis=1) for b in range(2)],
            [o_ref[...], rest_ref[:, at + 2 * fj :]],
            [ff_ref[:, 0:fj], rest_ref[:, at : at + fj]],
            [ff_ref[:, fj : 2 * fj], rest_ref[:, at + fj : at + 2 * fj]],
            [rest_ref[:, 0:pc]],
            [rest_ref[:, pc : 2 * pc]],
        ]
        places = [(4, 5), (8, 9), (0, 1), (2, 3), (6,), (7,)]
        for kind in range(6):
            for b in range(len(grads[kind])):
                here = (b,) if kind < 4 else (slice(None),)
                have = m_in[kind].shape[-1]
                m_out[kind][here] = MOMENT_DECAY * m_in[kind][here] + grads[kind][b]
                turn = res[places[kind][b], :, 0:have].astype(F32)
                w_out[kind][here] = w_in[kind][here] - STEP_SCALES[kind] * turn
        turned[...] = jnp.concatenate([dg[...], jnp.zeros((LANES - 8, width), F32)], axis=0).T
        grad = turned[pl.ds(pl.multiple_of(me_ref[0] * rw, 16), rw), 0:4]
        fresh = GAIN_DECAY * mg[...] + grad
        mg_out[...] = fresh
        g_out[...] = g[...] - GAIN_RATE * fresh

    outs = [(a.shape, F32) for a in (*moments, *weights, m_gains, gains)]
    return local_kernel(
        body,
        "update",
        outs,
        [((width, LANES), F32)],
        dp_arr,
        sum_q,
        sum_o,
        sum_ff,
        sum_rest,
        results,
        dgain,
        *moments,
        *weights,
        m_gains,
        gains,
    )


def rope_tables(total, hd):
    half = HEAD // 2
    frequency = (np.float32(10000.0) ** (-np.arange(half, dtype=np.float32) / np.float32(half))).astype(np.float32)
    angle = (np.arange(total, dtype=np.float32)[:, None] * frequency[None, :]).astype(np.float32)
    cos, sin = np.cos(angle), np.sin(angle)
    cos = np.tile(np.concatenate([cos, cos], axis=1), (1, hd // HEAD))
    sin = np.tile(np.concatenate([-sin, sin], axis=1), (1, hd // HEAD))
    return jnp.asarray(cos, F32), jnp.asarray(sin, F32)


def mask_features(segment, docs):
    same = segment[:, None] == jnp.arange(HEAD, dtype=jnp.int32)[None, :]
    used = jnp.arange(HEAD)[None, :] < docs
    fq = jnp.where(used & ~same, MASKED, 0.0).astype(BF)
    fk = same.astype(BF)
    return jnp.concatenate([fq, fq], axis=1), jnp.concatenate([fk, fk], axis=1)


def on_device(
    y_count,
    tokens,
    cotangent,
    doc_triples,
    w_qkv,
    w_out,
    w_in,
    w_down,
    w_pool,
    w_up,
    gains,
    m_qkv,
    m_out,
    m_in,
    m_down,
    m_pool,
    m_up,
    m_gains,
):
    rows, width = tokens.shape
    short = rows // 3
    fs_count, dp_count = lax.axis_size("fsdp"), lax.axis_size("dp")
    me, dp_me = lax.axis_index("fsdp"), lax.axis_index("dp")
    me_arr, dp_arr = me.astype(jnp.int32).reshape(1), dp_me.astype(jnp.int32).reshape(1)
    total, short_total = rows * fs_count, short * fs_count
    hd = width // fs_count
    fj = w_in.shape[2]
    pool_cols = w_pool.shape[1]

    ends = jnp.cumsum(doc_triples[0]).astype(jnp.int32)
    short_all = jnp.arange(short_total, dtype=jnp.int32)
    reached = short_all[:, None] >= ends[None, :]
    short_segment = jnp.sum(reached.astype(jnp.int32), axis=1)
    segment = jnp.repeat(short_segment, 3)
    begins = jnp.any(short_all[:, None] == ends[None, :], axis=1) | (short_all == 0)
    gate = jnp.pad(jnp.where(begins, 0.0, 1.0).astype(F32), (0, HALO))
    gate = lax.dynamic_slice(gate, (me * short,), (short + HALO,))[:, None]
    docs = doc_triples.shape[1]
    fq0, fk0 = mask_features(segment, docs)
    fq1, fk1 = mask_features(short_segment, docs)
    cos0, sin0 = rope_tables(total, hd)
    cos1, sin1 = cos0[:short_total], sin0[:short_total]

    old_weights = (w_qkv, w_out, w_in, w_down, w_pool, w_up)
    n1, qkv, att_rel, wo_own, n2, mid, after, z_blocks, s0, wqkv0, ff0, wp_all, wqkv1, rest, gain_rows = forward_one(
        y_count, dp_count, fs_count, tokens, doc_triples, old_weights, gains, cos0, sin0
    )
    gain = [gain_rows[k : k + 1] for k in range(4)]
    wi0, wd0 = ff0[:, :fj], ff0[:, fj:]
    wu, wo1 = rest[:, :pool_cols], rest[:, pool_cols : pool_cols + hd]
    wi1, wd1 = rest[:, pool_cols + hd : pool_cols + hd + fj], rest[:, pool_cols + hd + fj :]
    wp_p = [wp_all[e] for e in range(fs_count)]
    wo1_p, wu_p = gather_pieces(wo1), gather_pieces(wu)
    s0_p = gather_pieces(s0)
    z_p = exchange_blocks(z_blocks, me)
    c_blocks, ds1, ds1_low = up_backward(me_arr, cotangent, wu_p)
    c_p = exchange_blocks(c_blocks, me)
    ds1_p = gather_pieces(ds1_low)
    n1b, qkvb, attb = attn_forward(me_arr, s0_p, gain[2], wqkv1, fq1, fk1, cos1, sin1)
    n2b, attb_rel, wob_own, midb, keep, send = mix_forward(
        me_arr, s0_p, gather_pieces(attb), wo1_p, wi1, wd1, gain[3], 0
    )
    total_in, got = finish_scatter(keep, send)
    s1, layer_out = up_forward(me_arr, midb, total_in, got, after, wu_p)
    s1_p = gather_pieces(s1)
    g_up = dot_tn(jnp.concatenate(s1_p), jnp.concatenate(c_p))

    def block_back(d_pieces, above, n1, n2, att_rel, wo_own, wqkv, wi, wd, qkv, mid, own_in, gain_one, gain_two, tables):
        whole, hid, dpre, keep, send = mix_backward(me_arr, d_pieces, n2, wi, wd)
        g_down = dot_tn(whole, hid)
        g_in = dot_tn(n2, dpre)
        total_in, got = finish_scatter(keep, send)
        dm, dm_low, dgain_two = norm_backward(me_arr, mid, gain_two, total_in, got, above)
        da_all, dqkv, keep, send = attn_backward(me_arr, gather_pieces(dm_low), qkv, wo_own, wqkv, *tables)
        g_qkv = dot_tn(n1, dqkv)
        own = lax.dynamic_slice(da_all, (0, me * hd), (da_all.shape[0], hd))
        g_out = dot_tn(att_rel, own).reshape(fs_count, hd, hd)
        g_out = jnp.concatenate(
            [lax.dynamic_index_in_dim(g_out, me ^ k, 0, keepdims=False) for k in range(fs_count)], axis=0
        )
        total_in, got = finish_scatter(keep, send)
        dr, dr_low, dgain_one = norm_backward(me_arr, own_in, gain_one, total_in, got, dm)
        return dr, dr_low, (g_qkv, g_out, g_in, g_down), (dgain_one, dgain_two)

    _, ds0, grads_b, dgain_b = block_back(
        ds1_p,
        ds1,
        n1b,
        n2b,
        attb_rel,
        wob_own,
        wqkv1,
        wi1,
        wd1,
        qkvb,
        midb,
        s0,
        gain[2],
        gain[3],
        (fq1, fk1, cos1, sin1),
    )
    ds0_next = lax.ppermute(ds0[:HALO], "fsdp", [(i + 1, i) for i in range(fs_count - 1)])
    da, da_low = pool_backward(me_arr, ds0, ds0_next, gate, wp_p, cotangent)
    ds0_p = gather_pieces(ds0)
    g_pool = dot_tn(jnp.concatenate(ds0_p), jnp.concatenate(z_p))
    group_b = jnp.concatenate([grads_b[0], g_pool, g_up, grads_b[2], grads_b[3], grads_b[1]], axis=1).astype(BF)
    grad_in, dgain_a, sum_rest, sum_ff, sum_o, sum_q = backward_one(
        y_count,
        dp_count,
        fs_count,
        da,
        n2,
        ff0,
        mid,
        gain_rows,
        qkv,
        wo_own,
        wqkv0,
        cos0,
        sin0,
        doc_triples,
        n1,
        att_rel,
        tokens,
        group_b,
    )

    sums = (sum_q, sum_o, sum_ff, sum_rest)
    moments = (m_qkv, m_out, m_in, m_down, m_pool, m_up)
    results, norms, dgain = muon(y_count, dp_count, fs_count, sums, moments, (dgain_a, dgain_b[0], dgain_b[1]))
    fresh = update(dp_arr, sums, results, dgain, moments, old_weights, m_gains, gains)
    all_tokens = float(total * dp_count)
    entries = [m.size // (2 if m.ndim == 3 else 1) for m in moments for _ in range(2 if m.ndim == 3 else 1)]
    roots = np.array([float(n * fs_count * dp_count) * all_tokens for n in entries], np.float64) ** 0.5
    lengths = norms[:, 0, 0]
    lengths = jnp.concatenate([lengths[4:6], lengths[8:10], lengths[0:4], lengths[6:8]])
    moment_rms = lengths / jnp.asarray(roots, F32)
    return (layer_out, grad_in, *fresh, moment_rms)


def solution(mesh):
    by_row, by_dp = P(("dp", "fsdp"), None), P("dp", None)
    stacked, flat = P(None, "dp", "fsdp"), P("dp", "fsdp")
    matrices = (stacked,) * 4 + (flat,) * 2
    y_count = max(1, mesh.shape["fsdp"] // 2)
    return jax.shard_map(
        functools.partial(on_device, y_count),
        mesh=mesh,
        in_specs=(by_row, by_row, by_dp, *matrices, by_dp, *matrices, by_dp),
        out_specs=(by_row, by_row, *matrices, *matrices, by_dp, by_dp, P()),
        check_vma=False,
    )
```

```python
import functools

import jax
import jax.numpy as jnp
import numpy as np
from jax import lax
from jax.experimental import pallas as pl
from jax.experimental.pallas import tpu as pltpu
from jax.sharding import PartitionSpec as P

HEAD = 64
NS_STEPS = 5
NS_COEFS = (3.4445, -4.775, 2.0315)
STEP_SCALES = (0.8660254, 1.4142136, 1.0, 0.5, 0.5, 0.8660254)
MOMENT_DECAY = 0.95
GAIN_DECAY = 0.9
GAIN_RATE = 0.001
LN_EPS = 1e-05
NORM_EPS = 1e-07
MASKED = -1e30
HALO = 16
QB = 256
LANES = 128
VMEM_BYTES = 60 << 20
BF = jnp.bfloat16
F32 = jnp.float32
MESH = pl.DeviceIdType.MESH


def dot_nn(left, right):
    return lax.dot_general(left, right, (((1,), (0,)), ((), ())), preferred_element_type=F32)


def dot_nt(left, right):
    return lax.dot_general(left, right, (((1,), (1,)), ((), ())), preferred_element_type=F32)


def dot_tn(left, right):
    return lax.dot_general(left, right, (((0,), (0,)), ((), ())), preferred_element_type=F32)


def layer_norm(values, gain):
    mean = jnp.mean(values, axis=-1, keepdims=True)
    centred = values - mean
    spread = jnp.mean(centred * centred, axis=-1, keepdims=True)
    return centred * lax.rsqrt(spread + LN_EPS) * gain


def layer_norm_back(values, gain, grad):
    mean = jnp.mean(values, axis=-1, keepdims=True)
    centred = values - mean
    spread = jnp.mean(centred * centred, axis=-1, keepdims=True)
    scale = lax.rsqrt(spread + LN_EPS)
    unit = centred * scale
    scaled = grad * gain
    part = jnp.mean(scaled, axis=-1, keepdims=True)
    along = jnp.mean(scaled * unit, axis=-1, keepdims=True)
    return scale * (scaled - part - unit * along), grad * unit


def gelu(values):
    return 0.5 * values * (1.0 + jnp.tanh(0.7978845608028654 * (values + 0.044715 * values * values * values)))


def gelu_both(values):
    square = values * values
    turn = jnp.tanh(0.7978845608028654 * (values + 0.044715 * values * square))
    slope = 0.7978845608028654 * (1.0 + 3.0 * 0.044715 * square)
    half = 0.5 * (1.0 + turn)
    return values * half, half + 0.5 * values * (1.0 - turn * turn) * slope


def partner(values):
    width = values.shape[1]
    if width == LANES:
        lane = lax.broadcasted_iota(jnp.int32, values.shape, 1)
        ahead = pltpu.roll(values, LANES - HEAD // 2, 1)
        behind = pltpu.roll(values, HEAD // 2, 1)
        return jnp.where(lane % HEAD < HEAD // 2, ahead, behind)
    parts = []
    for at in range(0, width, HEAD):
        parts += [values[:, at + HEAD // 2 : at + HEAD], values[:, at : at + HEAD // 2]]
    return jnp.concatenate(parts, axis=1)


def widen(values):
    rows, width = values.shape
    if width >= LANES:
        return values
    return jnp.concatenate([values, jnp.zeros((rows, LANES - width), values.dtype)], axis=1)


def params():
    return pltpu.CompilerParams(vmem_limit_bytes=VMEM_BYTES)


def smem():
    return pl.BlockSpec(memory_space=pltpu.SMEM)


def vmem():
    return pl.BlockSpec(memory_space=pltpu.VMEM)


def cost(flops, moved):
    return pl.CostEstimate(flops=int(flops), bytes_accessed=int(moved), transcendentals=0)


def local_kernel(body, name, outs, scratch, me, *arrays, flops=0):
    moved = sum(a.size * a.dtype.itemsize for a in arrays)
    moved += sum(int(np.prod(s)) * jnp.dtype(t).itemsize for s, t in outs)
    return pl.pallas_call(
        body,
        out_shape=[jax.ShapeDtypeStruct(s, t) for s, t in outs],
        in_specs=[smem()] + [vmem()] * len(arrays),
        out_specs=[vmem()] * len(outs),
        scratch_shapes=[pltpu.VMEM(s, t) for s, t in scratch],
        compiler_params=params(),
        cost_estimate=cost(flops, moved),
        name=name,
    )(me, *arrays)


def at_rows(me, step, rows):
    return pl.multiple_of((me ^ step) * rows, 16)


def head_inputs(qs, ks, rows, q, k, fq, fk, heads):
    lane = lax.broadcasted_iota(jnp.int32, (q.shape[0], LANES), 1)
    q, k = widen(q), widen(k)
    for h in range(heads):
        mine = lane // HEAD == h
        qs[h, rows, :] = jnp.where(mine, q * 0.125, fq).astype(BF)
        ks[h, rows, :] = jnp.where(mine, k, fk).astype(BF)


def scores_t(ks, qs, h, start, stop):
    top = dot_nt(ks[h, 0:stop, :], qs[h, start:stop, :])
    key = lax.broadcasted_iota(jnp.int32, (stop - start, stop - start), 0)
    query = lax.broadcasted_iota(jnp.int32, (stop - start, stop - start), 1)
    last = jnp.where(key <= query, top[start:, :], MASKED)
    if start == 0:
        return last
    return jnp.concatenate([top[:start, :], last], axis=0)


def spread_write(hold, values):
    for c in range(hold.shape[0]):
        hold[c] = values[:, c * LANES : (c + 1) * LANES]


def spread_read(hold):
    return jnp.concatenate([hold[c] for c in range(hold.shape[0])], axis=1)


def strided_read(hold, start, amount):
    return jnp.concatenate([hold[c, pl.ds(start, amount, stride=3), :] for c in range(hold.shape[0])], axis=1)


def strided_write(hold, start, amount, values):
    for c in range(hold.shape[0]):
        hold[c, pl.ds(start, amount, stride=3), :] = values[:, c * LANES : (c + 1) * LANES]


def flip(value, step):
    bit = 1
    while bit <= step:
        if step & bit:
            value = value + bit - 2 * bit * lax.rem(lax.div(value, bit), 2)
        bit *= 2
    return value


class Net:
    def __init__(self, send, recv):
        self.send, self.recv, self.used, self.open = send, recv, 0, []

    def make(self, src, dst, device):
        at = self.used
        self.used += 1
        return pltpu.make_async_remote_copy(
            src_ref=src,
            dst_ref=dst,
            send_sem=self.send.at[at],
            recv_sem=self.recv.at[at],
            device_id=device,
            device_id_type=MESH,
        )

    def start(self, src, dst, device):
        copy = self.make(src, dst, device)
        copy.start()
        self.open.append(copy)
        return copy

    def finish(self):
        for copy in self.open:
            copy.wait_send()


class Flight:
    def __init__(self, net, dp, fs, fs_count, pieces, src):
        self.net, self.dp, self.fs, self.pieces = net, dp, fs, pieces
        self.top, self.copies, self.waited = fs_count // 2, {}, set()
        bit = self.top
        while bit:
            self.copies[bit] = net.start(src, pieces.at[bit], (dp, flip(fs, bit)))
            bit //= 2

    def ready(self, step):
        if step and step not in self.waited:
            self.waited.add(step)
            self.copies[step].wait_recv()

    def relay(self):
        known, bit = [self.top], self.top // 2
        while bit:
            fresh = []
            for step in known:
                self.ready(step)
                there = (self.dp, flip(self.fs, bit))
                self.copies[step + bit] = self.net.start(self.pieces.at[step], self.pieces.at[step + bit], there)
                fresh.append(step + bit)
            known = known + [bit] + fresh
            bit //= 2

    def all_ready(self):
        for step in sorted(self.copies):
            self.ready(step)


def doc_bounds(triples, docs):
    lane = lax.broadcasted_iota(jnp.int32, (1, LANES), 1)
    lane = jnp.where(lane >= HEAD, lane - HEAD, lane)
    first = jnp.full((1, LANES), -1, jnp.int32)
    end = jnp.full((1, LANES), -1, jnp.int32)
    at = jnp.int32(0)
    for j in range(docs):
        here = lane == j
        first = jnp.where(here, at, first)
        at = at + triples[0, j]
        end = jnp.where(here, at, end)
    return first, end, lane


def softmax_block(ks, qs, h, r, stop):
    s = scores_t(ks, qs, h, r, stop)
    e = jnp.exp(s - jnp.max(s, axis=0, keepdims=True))
    return e, 1.0 / jnp.sum(e, axis=0, keepdims=True)


def forward_one(y_count, dp_count, fs_count, tokens, triples, weights, gains, cos, sin):
    rows, width = tokens.shape
    total, short = rows * fs_count, rows // 3
    long_rows = rows + HALO
    wqkv, wout, win, wdown, wpool, wup = weights
    rw = wqkv.shape[1]
    hd, fj, pc = wout.shape[2], win.shape[2], wpool.shape[1]
    heads = hd // HEAD
    docs = triples.shape[1]
    z_count = dp_count // y_count
    cw = pc + hd + 2 * fj
    blk = QB
    sems = 64 + 14 * dp_count

    def body(
        tok, triples_ref, q_in, o_in, i_in, d_in, p_in, u_in, g_in, cos_ref, sin_ref,
        n1, qkv, att_rel, wo_own, n2, mid, after, z_out, s0_out, wq_out, wb, wp, wq1_out, wc, gain_out,
        toks, st_q, wq0, wq1, gall, wo, wo_at, att, qs, ks, vt, turned, hold, work, low, part, m_tail, part_tail,
        sbuf, rbuf, xsend, xrecv, acc, thin, send_sem, recv_sem,
    ):
        dp, fs = lax.axis_index("dp"), lax.axis_index("fsdp")
        net = Net(send_sem, recv_sem)

        def own(buf):
            return buf.at[pl.ds(pl.multiple_of(dp * rw, 16), rw), :]

        def of(buf, step):
            return buf.at[pl.ds(pl.multiple_of(flip(dp, step) * rw, 16), rw), :]

        for b in range(2):
            for t in range(3):
                st_q[b, t] = q_in[b, :, t * hd : (t + 1) * hd].astype(BF)
        here = pl.ds(pl.multiple_of(dp * rw, 16), rw)
        gall[here, :] = jnp.concatenate([g_in[...], jnp.zeros((rw, LANES - 4), F32)], axis=1).astype(BF)
        wo[0, here, :] = o_in[0].astype(BF)
        wb[here, 0:fj] = i_in[0].astype(BF)
        wb[here, fj : 2 * fj] = d_in[0].astype(BF)
        wp[0, here, :] = p_in[...].astype(BF)
        wc[here, 0:pc] = u_in[...].astype(BF)
        wc[here, pc : pc + hd] = o_in[1].astype(BF)
        wc[here, pc + hd : pc + hd + fj] = i_in[1].astype(BF)
        wc[here, pc + hd + fj : cw] = d_in[1].astype(BF)

        barrier = pltpu.get_barrier_semaphore()
        for m in range(z_count):
            for e in range(fs_count):
                if m or e:
                    there = (flip(dp, m * y_count), flip(fs, e))
                    pl.semaphore_signal(barrier, inc=1, device_id=there, device_id_type=MESH)
        for j in range(1, y_count):
            pl.semaphore_signal(barrier, inc=1, device_id=(flip(dp, j), fs), device_id_type=MESH)
        pl.semaphore_wait(barrier, z_count * fs_count - 1 + y_count - 1)

        def along_z(bufs):
            found = [[] for _ in range(z_count)]
            for m in range(1, z_count):
                for buf in bufs:
                    found[m].append(net.start(own(buf), own(buf), (flip(dp, m * y_count), fs)))
            return found

        def along_y(bufs, m):
            return [
                net.start(of(buf, m * y_count), of(buf, m * y_count), (flip(dp, j), fs))
                for j in range(1, y_count)
                for buf in bufs
            ]

        def wait_all(copies):
            for copy in copies:
                copy.wait_recv()

        def heads_along_z(b, wq):
            found = []
            for m in range(z_count):
                line = []
                for t in range(3):
                    place = 3 * fs + t
                    kind, to = lax.div(place, fs_count), lax.rem(place, fs_count)
                    copy = net.make(st_q.at[b, t], wq.at[kind, here, :], (flip(dp, m * y_count), to))
                    if m == 0:

                        @pl.when(to != fs)
                        def _():
                            copy.start()

                        @pl.when(to == fs)
                        def _():
                            wq[kind, here, :] = st_q[b, t]

                        line.append((copy, to != fs))
                    else:
                        copy.start()
                        net.open.append(copy)
                        line.append((copy, None))
                found.append(line)
            return found

        def heads_along_y(wq, line, m):
            for copy, when in line:
                if when is None:
                    copy.wait_recv()
                else:

                    @pl.when(when)
                    def _():
                        copy.wait_recv()
                        copy.wait_send()

            at = pl.ds(pl.multiple_of(flip(dp, m * y_count) * rw, 16), rw)
            return [
                net.start(wq.at[:, at, :], wq.at[:, at, :], (flip(dp, j), fs)) for j in range(1, y_count)
            ]


        def spread(pieces, src):
            return Flight(net, dp, fs, fs_count, pieces, src)

        heads0 = heads_along_z(0, wq0)
        gz = along_z([gall])
        y0 = along_y([gall], 0)
        tk = spread(toks, tok)
        toks[0] = tok[...]
        oz = along_z([wo.at[0]])
        y1 = along_y([wo.at[0]], 0)
        lane_first, lane_end, lane = doc_bounds(triples_ref, docs)
        for m in range(z_count):
            y0 += heads_along_y(wq0, heads0[m], m)
            if m:
                wait_all(gz[m])
                y0 += along_y([gall], m)
        bz = along_z([wb])
        y2 = along_y([wb], 0)
        for m in range(1, z_count):
            wait_all(oz[m])
            y1 += along_y([wo.at[0]], m)
        tk.relay()
        wait_all(y0)
        gain_rows = gall[...].astype(F32).T[0:8, :]
        gain_out[...] = gain_rows
        for t in range(3):
            wq_out[:, t * hd : (t + 1) * hd] = wq0[t]
        for e in range(fs_count):
            tk.ready(e)
            base = pl.multiple_of(flip(fs, e) * rows, 16)
            for r in range(0, rows, LANES):
                block = toks[e, r : r + LANES, :].astype(F32)
                n1[pl.ds(base + r, LANES), :] = layer_norm(block, gain_rows[0:1]).astype(BF)

        lane_head = lax.broadcasted_iota(jnp.int32, (blk, LANES), 1)
        for r in range(0, total, blk):
            at = slice(r, r + blk)
            got = dot_nn(n1[at, :], wq_out[...])
            q, k, v = got[:, :hd], got[:, hd : 2 * hd], got[:, 2 * hd :]
            q = (q * cos_ref[at, :] + partner(q) * sin_ref[at, :]).astype(BF)
            k = (k * cos_ref[at, :] + partner(k) * sin_ref[at, :]).astype(BF)
            qkv[at, 0:hd] = q
            qkv[at, hd : 2 * hd] = k
            qkv[at, 2 * hd : 3 * hd] = v.astype(BF)
            row = lax.broadcasted_iota(jnp.int32, (blk, LANES), 0) + r
            inside = (row >= 3 * lane_first) & (row < 3 * lane_end)
            fk = jnp.where(inside, 1.0, 0.0)
            fq = jnp.where(inside | (lane >= docs), 0.0, MASKED)
            head_inputs(qs, ks, at, q.astype(F32), k.astype(F32), fq, fk, heads)
            vt[:, at] = v.T.astype(BF)

        flights = []
        for n, r in enumerate(range(0, total, blk)):
            stop = r + blk
            found = []
            for h in range(heads):
                e, inv = softmax_block(ks, qs, h, r, stop)
                found.append(dot_nn(vt[h * HEAD : (h + 1) * HEAD, 0:stop], e.astype(BF)) * inv)
            att[0, r:stop, :] = jnp.concatenate(found, axis=0).T.astype(BF)
            flights.append(spread(att.at[:, r:stop, :], att.at[0, r:stop, :]))
            if n == 0:
                wait_all(y1)
                wo_f = spread(wo, wo.at[0])
            if n == 2:
                for m in range(1, z_count):
                    wait_all(bz[m])
                    y2 += along_y([wb], m)
                wz = along_z([wp.at[0]])
                y3 = along_y([wp.at[0]], 0)
                heads1 = heads_along_z(1, wq1)
                cz = along_z([wc])
                y4 = along_y([wc], 0)
            if n == 3:
                wo_f.relay()
            if n >= 2:
                flights[n - 2].relay()
        for flight in flights[-2:]:
            flight.relay()
        wo_f.all_ready()
        for e in range(fs_count):
            wo_at[flip(fs, e)] = wo[e]
        for e in range(fs_count):
            hold[:, e * hd : (e + 1) * hd] = wo_at[e]
        for e in range(fs_count):
            base = pl.multiple_of(flip(fs, e) * hd, 16)
            turned[e * hd : (e + 1) * hd, :] = hold[pl.ds(base, hd), :]
        wo_own[...] = turned[0:hd, :]
        for flight in flights:
            flight.all_ready()
        for m in range(1, z_count):
            wait_all(wz[m])
            y3 += along_y([wp.at[0]], m)
        wait_all(y2)

        def mix(x_block, o_block, amount, keep_mid, keep_n2, out):
            work[0:amount, 0:width] = x_block.astype(F32) + dot_nn(o_block, turned[...])
            for r in range(0, amount, HEAD):
                m = work[r : r + HEAD, 0:width]
                if keep_mid is not None:
                    keep_mid[r : r + HEAD, :] = m
                value = layer_norm(m, gain_rows[1:2]).astype(BF)
                low[r : r + HEAD, 0:width] = value
                if keep_n2 is not None:
                    keep_n2[r : r + HEAD, :] = value
            work[0:amount, 0:fj] = dot_nn(low[0:amount, 0:width], wb[:, 0:fj])
            for r in range(0, amount, HEAD):
                low[r : r + HEAD, 0:fj] = gelu(work[r : r + HEAD, 0:fj]).astype(BF)
            out[0:amount, :] = dot_nt(low[0:amount, 0:fj], wb[:, fj : 2 * fj])

        for e in range(fs_count):
            at = pl.ds(pl.multiple_of(flip(fs, e) * rows + rows - HALO, 16), HALO)
            for k in range(fs_count):
                att_rel[e * HALO : (e + 1) * HALO, k * hd : (k + 1) * hd] = att[k, at, :]
        tails = jnp.concatenate([toks[e, rows - HALO : rows, :] for e in range(fs_count)], axis=0)
        mix(tails, att_rel[0 : fs_count * HALO, :], fs_count * HALO, m_tail, None, part_tail)

        for e in range(fs_count):
            base = pl.multiple_of(flip(fs, e) * rows, 16)
            for k in range(fs_count):
                att_rel[pl.ds(base, rows), k * hd : (k + 1) * hd] = att[k, pl.ds(base, rows), :]

        def before(e):
            place = flip(fs, e) + fs_count - 1
            place = lax.rem(place, fs_count)
            apart = jnp.int32(0)
            bit = 1
            while bit < fs_count:
                one = lax.rem(lax.div(place, bit), 2)
                two = lax.rem(lax.div(fs, bit), 2)
                apart = apart + bit * lax.rem(one + two, 2)
                bit *= 2
            return pl.multiple_of(apart * HALO, 16)

        def partial_for(e, out):
            base = pl.multiple_of(flip(fs, e) * rows, 16)
            mix(
                toks[e],
                att_rel[pl.ds(base, rows), :],
                rows,
                mid if e == 0 else None,
                n2.at[e * rows : (e + 1) * rows, :],
                part,
            )
            out[0:HALO, :] = part_tail[pl.ds(before(e), HALO), :].astype(out.dtype)
            out[HALO:long_rows, :] = part[0:rows, :].astype(out.dtype)

        half = fs_count // 2
        first_hops = {}
        for j in reversed(range(half)):
            partial_for(2 * j + 1, sbuf.at[j])
            first_hops[j] = net.start(sbuf.at[j], rbuf.at[j], (dp, flip(fs, 1)))
            if j == half - 1:
                for m in range(z_count):
                    y4 += heads_along_y(wq1, heads1[m], m)
                wait_all(y3)
                wp_f = spread(wp, wp.at[0])
            if j:
                partial_for(2 * j, acc.at[j])
                first_hops[j].wait_recv()
                acc[j] = acc[j] + rbuf[j].astype(F32)
                if half == 2:
                    xsend[0] = acc[1].astype(BF)
                    last_hop = net.start(xsend.at[0], xrecv.at[0], (dp, flip(fs, 2)))
            if j == half - 1:
                for m in range(1, z_count):
                    wait_all(cz[m])
                    y4 += along_y([wc], m)
        partial_for(0, acc.at[0])
        first_hops[0].wait_recv()
        acc[0] = acc[0] + rbuf[0].astype(F32)
        wp_f.relay()
        if half > 2:
            bit, active = 2, list(range(half))
            slot = 0
            while bit < fs_count:
                stay = [j for j in active if not (2 * j) & bit]
                hops = {}
                for j in stay:
                    give = j + bit // 2
                    xsend[slot] = acc[give].astype(BF)
                    hops[j] = (net.start(xsend.at[slot], xrecv.at[slot], (dp, flip(fs, bit))), slot)
                    slot += 1
                for j in stay:
                    hops[j][0].wait_recv()
                    acc[j] = acc[j] + xrecv[hops[j][1]].astype(F32)
                active, bit = stay, bit * 2
        elif half == 2:
            last_hop.wait_recv()
            acc[0] = acc[0] + xrecv[0].astype(F32)
        a_tail = acc[0, 0:HALO, :] + m_tail[pl.ds(before(0), HALO), :]
        a_own = acc[0, HALO:long_rows, :] + mid[...]
        after[...] = a_own
        for c in range(width // LANES):
            thin[c, 0:HALO, :] = a_tail[:, c * LANES : (c + 1) * LANES]
            thin[c, HALO:long_rows, :] = a_own[:, c * LANES : (c + 1) * LANES]

        row = lax.broadcasted_iota(jnp.int32, (short, LANES), 0) + fs * short
        begins = jnp.max(jnp.where(row == lane_first, 1.0, 0.0), axis=1, keepdims=True)
        parts = []
        for k in range(3):
            value = strided_read(thin, HALO - 2 + k, short)
            parts.append(jnp.where(begins > 0.0, 0.0, value) if k < 2 else value)
        z = jnp.concatenate(parts, axis=1).astype(BF)
        for e in range(fs_count):
            z_out[e] = z[:, e * pc : (e + 1) * pc]
        pooled = jnp.zeros((short, width), F32)
        for e in range(fs_count):
            wp_f.ready(e)
            pooled = pooled + dot_nt(z_out[flip(fs, e)], wp[e])
        s0_out[...] = pooled
        wait_all(y4)
        for t in range(3):
            wq1_out[:, t * hd : (t + 1) * hd] = wq1[t]
        net.finish()

    half = fs_count // 2
    outs = [
        ((total, width), BF),
        ((total, 3 * hd), BF),
        ((total, width), BF),
        ((hd, width), BF),
        ((total, width), BF),
        ((rows, width), F32),
        ((rows, width), F32),
        ((fs_count, short, pc), BF),
        ((short, width), F32),
        ((width, 3 * hd), BF),
        ((width, 2 * fj), BF),
        ((fs_count, width, pc), BF),
        ((width, 3 * hd), BF),
        ((width, cw), BF),
        ((8, width), F32),
    ]
    wide = max(width, fj)
    scratch = [
        ((fs_count, rows, width), BF),
        ((2, 3, rw, hd), BF),
        ((3, width, hd), BF),
        ((3, width, hd), BF),
        ((width, LANES), BF),
        ((fs_count, width, hd), BF),
        ((fs_count, width, hd), BF),
        ((fs_count, total, hd), BF),
        ((heads, total, LANES), BF),
        ((heads, total, LANES), BF),
        ((hd, total), BF),
        ((width, width), BF),
        ((width, width), BF),
        ((rows, wide), F32),
        ((rows, wide), BF),
        ((rows, width), F32),
        ((fs_count * HALO, width), F32),
        ((fs_count * HALO, width), F32),
        ((half, long_rows, width), BF),
        ((half, long_rows, width), BF),
        ((half - 1, long_rows, width), BF),
        ((half - 1, long_rows, width), BF),
        ((half, long_rows, width), F32),
        ((width // LANES, long_rows, LANES), F32),
    ]
    return pl.pallas_call(
        body,
        out_shape=[jax.ShapeDtypeStruct(s, t) for s, t in outs],
        in_specs=[vmem(), smem()] + [vmem()] * 9,
        out_specs=[vmem()] * len(outs),
        scratch_shapes=[pltpu.VMEM(s, t) for s, t in scratch] + [pltpu.SemaphoreType.DMA((sems,))] * 2,
        compiler_params=pltpu.CompilerParams(collective_id=3, has_side_effects=True, vmem_limit_bytes=VMEM_BYTES),
        cost_estimate=cost(2e10, 3e7),
        name="forward_one",
    )(tokens, triples, *weights, gains, cos, sin)


class RowSum:
    def __init__(self, net, place, grad, ybuf, zsend, zrecv, total, q_send=None, q_recv=None, q_total=None):
        self.net, self.grad, self.ybuf = net, grad, ybuf
        self.zsend, self.zrecv, self.total = zsend, zrecv, total
        self.q_send, self.q_recv, self.q_total = q_send, q_recv, q_total
        self.dp, self.fs, self.y_count, self.z_count, self.fs_count, self.rw = place
        self.ys, self.zs, self.qs = {}, {}, []

    def rows_of(self, step):
        return pl.ds(pl.multiple_of(flip(self.dp, step) * self.rw, 16), self.rw)

    def start(self):
        for m in list(range(1, self.z_count)) + [0]:
            self.ys[m] = [
                self.net.start(
                    self.grad.at[self.rows_of(m * self.y_count + j), :],
                    self.ybuf.at[j - 1, m],
                    (flip(self.dp, j), self.fs),
                )
                for j in range(1, self.y_count)
            ]
        if self.q_send is not None:
            self.q_base = self.net.used
            self.net.used += 3 * self.z_count

    def owner(self, kind):
        place = kind * self.fs_count + self.fs
        return lax.div(place, 3), lax.rem(place, 3)

    def service(self, m):
        for copy in self.ys[m]:
            copy.wait_recv()
        got = self.grad[self.rows_of(m * self.y_count), :].astype(F32)
        for j in range(1, self.y_count):
            got = got + self.ybuf[j - 1, m].astype(F32)
        there = flip(self.dp, m * self.y_count)
        lo = 0
        if self.q_send is not None:
            hd = self.q_send.shape[3]
            lo = 3 * hd
            for kind in range(3):
                to, slot = self.owner(kind)
                self.q_send[m, kind] = got[:, kind * hd : (kind + 1) * hd].astype(BF)
                copy = pltpu.make_async_remote_copy(
                    src_ref=self.q_send.at[m, kind],
                    dst_ref=self.q_recv.at[m, slot],
                    send_sem=self.net.send.at[self.q_base + 3 * m + kind],
                    recv_sem=self.net.recv.at[self.q_base + 3 * m + slot],
                    device_id=(there, to),
                    device_id_type=MESH,
                )
                if m:
                    copy.start()
                    self.qs.append((copy, None))
                else:

                    @pl.when(to != self.fs)
                    def _():
                        copy.start()

                    @pl.when(to == self.fs)
                    def _():
                        self.q_recv[0, slot] = self.q_send[0, kind]

                    self.qs.append((copy, to != self.fs))
        width = self.total.shape[1]
        rest = got[:, lo : lo + width]
        if m:
            self.zsend[m - 1] = rest.astype(BF)
            self.zs[m] = self.net.start(self.zsend.at[m - 1], self.zrecv.at[m - 1], (there, self.fs))
        else:
            self.total[...] = rest

    def finish(self):
        rest = self.total[...]
        for m in range(1, self.z_count):
            self.zs[m].wait_recv()
            rest = rest + self.zrecv[m - 1].astype(F32)
        self.total[...] = rest
        if self.q_send is None:
            return
        for t in range(3):
            giver = lax.rem(3 * self.fs + t, self.fs_count)
            for m in range(self.z_count):
                landed = self.q_recv.at[m, t]
                wait = pltpu.make_async_copy(landed, landed, self.net.recv.at[self.q_base + 3 * m + t])
                if m:
                    wait.wait()
                else:

                    @pl.when(giver != self.fs)
                    def _():
                        wait.wait()

        for t in range(3):
            block = self.q_recv[0, t].astype(F32)
            for m in range(1, self.z_count):
                block = block + self.q_recv[m, t].astype(F32)
            self.q_total[t] = block
        for copy, when in self.qs:
            if when is None:
                copy.wait_send()
            else:

                @pl.when(when)
                def _():
                    copy.wait_send()


class Scatter:
    def __init__(self, net, dp, fs, fs_count, sbuf, rbuf, xsend, xrecv, acc):
        self.net, self.dp, self.fs, self.half = net, dp, fs, fs_count // 2
        self.sbuf, self.rbuf, self.xsend, self.xrecv, self.acc = sbuf, rbuf, xsend, xrecv, acc
        self.first, self.hops, self.slot = {}, {}, 0

    def send_odd(self, j):
        self.first[j] = self.net.start(self.sbuf.at[j], self.rbuf.at[j], (self.dp, flip(self.fs, 1)))

    def join(self, j):
        self.first[j].wait_recv()
        self.acc[j] = self.acc[j] + self.rbuf[j].astype(F32)

    def give(self, j):
        bit = (2 * j) & -(2 * j)
        slot = self.slot
        self.slot += 1
        self.xsend[slot] = self.acc[j].astype(BF)
        self.hops[j] = (self.net.start(self.xsend.at[slot], self.xrecv.at[slot], (self.dp, flip(self.fs, bit))), slot)

    def take(self, j):
        low = j & -j
        copy, slot = self.hops[j]
        copy.wait_recv()
        self.acc[j - low] = self.acc[j - low] + self.xrecv[slot].astype(F32)

    def sent(self):
        for copy in list(self.first.values()) + [copy for copy, _ in self.hops.values()]:
            copy.wait_send()
            self.net.open = [other for other in self.net.open if other is not copy]

    def upper(self):
        if self.half == 2:
            self.give(1)

    def finish(self):
        if self.half == 2:
            self.take(1)
            return
        bit = 1
        while bit < self.half:
            gives = [j for j in range(self.half) if j & bit and not j & (bit - 1)]
            for j in gives:
                self.give(j)
            for j in gives:
                self.take(j)
            bit *= 2


def query_rows(total):
    return QB if total <= 2048 else QB // 2


def backward_one(
    y_count, dp_count, fs_count, da, n2, ff, mid, gain_rows, qkv, wo_own, wq, cos, sin, triples, n1, att_rel, tokens, group_b
):
    rows, width = tokens.shape
    total = rows * fs_count
    fj, hd = ff.shape[1] // 2, wq.shape[1] // 3
    heads, docs = hd // HEAD, triples.shape[1]
    z_count, rw = dp_count // y_count, width // dp_count
    cb = group_b.shape[1]
    blk, half = query_rows(total), fs_count // 2
    blocks = total // blk
    sems = 96 + 12 * dp_count

    def body(
        da_ref, n2_ref, ff_ref, mid_ref, gain_ref, qkv_ref, wo_ref, wq_ref, cos_ref, sin_ref, triples_ref, n1_ref, att_ref, tok, gb,
        grad_in, dgain, sum_b, sum_ff, sum_o, sum_q,
        dfs, das, hid, slope, dpre, work, qs, ks, kt, dk, dv, dqkv, dm, cols, g_ff, g_at,
        sbuf, rbuf, xsend, xrecv, acc, yb, zsb, zrb, qsb, qrb, yf, zsf, zrf, ya, zsa, zra, qsa, qra, send_sem, recv_sem,
        *ps,
    ):
        dp, fs = lax.axis_index("dp"), lax.axis_index("fsdp")
        net = Net(send_sem, recv_sem)
        place = (dp, fs, y_count, z_count, fs_count, rw)
        dfs[0] = da_ref[...].astype(BF)
        barrier = pltpu.get_barrier_semaphore()
        for m in range(z_count):
            for e in range(fs_count):
                if m or e:
                    there = (flip(dp, m * y_count), flip(fs, e))
                    pl.semaphore_signal(barrier, inc=1, device_id=there, device_id_type=MESH)
        for j in range(1, y_count):
            pl.semaphore_signal(barrier, inc=1, device_id=(flip(dp, j), fs), device_id_type=MESH)
        pl.semaphore_wait(barrier, z_count * fs_count - 1 + y_count - 1)

        def spread(pieces):
            return Flight(net, dp, fs, fs_count, pieces, pieces.at[0])

        df_f = spread(dfs)
        sum_of_b = RowSum(net, place, gb, yb, zsb, zrb, sum_b, qsb, qrb, sum_q.at[1])
        sum_of_b.start()

        def activate(e):
            at = slice(e * rows, (e + 1) * rows)
            work[:, 0:fj] = dot_nn(n2_ref[at, :], ff_ref[:, 0:fj])
            for r in range(0, rows, HEAD):
                value, rate = gelu_both(work[r : r + HEAD, 0:fj])
                hid[e * rows + r : e * rows + r + HEAD, :] = value.astype(BF)
                slope[e * rows + r : e * rows + r + HEAD, :] = rate.astype(BF)

        def pull(e, out):
            work[:, 0:fj] = dot_nn(dfs[e], ff_ref[:, fj : 2 * fj])
            for r in range(0, rows, HEAD):
                at = slice(e * rows + r, e * rows + r + HEAD)
                dpre[at, :] = (work[r : r + HEAD, 0:fj] * slope[at, :].astype(F32)).astype(BF)
            out[...] = dot_nt(dpre[e * rows : (e + 1) * rows, :], ff_ref[:, 0:fj]).astype(out.dtype)

        def part_into(scatter, e, fill):
            if e % 2:
                fill(e, scatter.sbuf.at[e // 2])
                scatter.send_odd(e // 2)
            else:
                fill(e, scatter.acc.at[e // 2])

        ff_sum = Scatter(net, dp, fs, fs_count, sbuf, rbuf, xsend, xrecv, acc)
        for e in range(fs_count):
            activate(e)
            if e < 2:
                df_f.ready(e)
                part_into(ff_sum, e, pull)
        df_f.relay()
        sum_of_b.service(1)
        for e in range(2, fs_count):
            df_f.ready(e)
            part_into(ff_sum, e, pull)
        for j in range(1, half):
            ff_sum.join(j)
        ff_sum.upper()
        for m in range(2, z_count):
            sum_of_b.service(m)
        ff_sum.join(0)
        g_ff[:, 0:fj] = dot_tn(n2_ref[...], dpre[...]).astype(BF)
        g_ff[:, fj : 2 * fj] = dot_tn(dfs[...].reshape(total, width), hid[...]).astype(BF)
        sum_of_b.service(0)
        sum_of_ff = RowSum(net, place, g_ff, yf, zsf, zrf, sum_ff)
        sum_of_ff.start()

        lane_first, lane_end, lane = doc_bounds(triples_ref, docs)
        for r in range(0, total, blk):
            at = slice(r, r + blk)
            q = qkv_ref[at, 0:hd].astype(F32)
            k = qkv_ref[at, hd : 2 * hd].astype(F32)
            row = lax.broadcasted_iota(jnp.int32, (blk, LANES), 0) + r
            inside = (row >= 3 * lane_first) & (row < 3 * lane_end)
            fk = jnp.where(inside, 1.0, 0.0)
            fq = jnp.where(inside | (lane >= docs), 0.0, MASKED)
            head_inputs(qs, ks, at, q, k, fq, fk, heads)
            kt[:, at] = k.T.astype(BF)
            dk[at, :] = jnp.zeros((blk, LANES), F32)
            dv[at, :] = jnp.zeros((blk, LANES), F32)

        def recompute(n):
            r = n * blk
            for h in range(heads):
                e, inv = softmax_block(ks, qs, h, r, r + blk)
                ps[n][h] = (e * inv).astype(BF)

        for n in range(blocks // 2):
            recompute(n)

        ff_sum.finish()
        for r in range(0, rows, LANES):
            at = slice(r, r + LANES)
            dx, dg = layer_norm_back(mid_ref[at, :], gain_ref[1:2, :], acc[0, at, :])
            dx = dx + da_ref[at, :]
            dm[at, :] = dx
            das[0, at, :] = dx.astype(BF)
            dg = jnp.sum(dg, axis=0, keepdims=True)
            gain_two = dg if r == 0 else gain_two + dg
        da_f = spread(das)
        for n in range(blocks // 2, blocks):
            recompute(n)
        for m in range(1, z_count):
            sum_of_ff.service(m)
        sum_of_ff.service(0)
        da_f.relay()

        place_of = lax.broadcasted_iota(jnp.int32, (blk, LANES), 1) // HEAD
        for r in range(0, total, blk):
            at = slice(r, r + blk)
            q = widen(qkv_ref[at, 0:hd].astype(F32))
            for h in range(heads):
                qs[h, at, :] = jnp.where(place_of == h, q, 0.0).astype(BF)
        lane_head = lax.broadcasted_iota(jnp.int32, (rows, LANES), 1) // HEAD
        for e in range(fs_count):
            da_f.ready(e)
            base = pl.multiple_of(flip(fs, e) * rows, 16)
            do = widen(dot_nt(das[e], wo_ref[...]))
            for h in range(heads):
                ks[h, pl.ds(base, rows), :] = jnp.where(lane_head == h, do, 0.0).astype(BF)
            for k in range(fs_count):

                @pl.when(fs == k)
                def _():
                    cols[pl.ds(base, rows), :] = das[e, :, k * hd : (k + 1) * hd]

        g_out = dot_tn(att_ref[...], cols[...]).astype(BF)
        for e in range(fs_count):
            base = pl.multiple_of(flip(fs, e) * hd, 16)
            g_at[pl.ds(base, hd), 3 * hd : 4 * hd] = g_out[e * hd : (e + 1) * hd, :]
        sum_of_b.finish()

        for n in range(blocks):
            r, stop = n * blk, (n + 1) * blk
            at = slice(r, stop)
            found = []
            add_k = add_v = None
            for h in range(heads):
                p = ps[n][h]
                v = widen(qkv_ref[0:stop, 2 * hd : 3 * hd])
                grad = dot_nt(v, ks[h, at, :])
                wide = p.astype(F32)
                middle = jnp.sum(wide * grad, axis=0, keepdims=True)
                dr = (wide * (grad - middle) * 0.125).astype(BF)
                part_v = dot_nn(p, ks[h, at, :])
                part_k = dot_nn(dr, qs[h, at, :])
                add_v = part_v if add_v is None else add_v + part_v
                add_k = part_k if add_k is None else add_k + part_k
                found.append(dot_nn(kt[h * HEAD : (h + 1) * HEAD, 0:stop], dr))
            dk[0:stop, :] += add_k
            dv[0:stop, :] += add_v
            dq = jnp.concatenate(found, axis=0).T
            dqkv[at, 0:hd] = (dq * cos_ref[at, :] - partner(dq) * sin_ref[at, :]).astype(BF)
        for r in range(0, total, blk):
            at = slice(r, r + blk)
            grad = dk[at, 0:hd]
            dqkv[at, hd : 2 * hd] = (grad * cos_ref[at, :] - partner(grad) * sin_ref[at, :]).astype(BF)
            dqkv[at, 2 * hd : 3 * hd] = dv[at, 0:hd].astype(BF)
        g_at[:, 0 : 3 * hd] = dot_tn(n1_ref[...], dqkv[...]).astype(BF)
        sum_of_at = RowSum(net, place, g_at, ya, zsa, zra, sum_o, qsa, qra, sum_q.at[0])
        sum_of_at.start()

        ff_sum.sent()
        at_sum = Scatter(net, dp, fs, fs_count, sbuf, rbuf, xsend, xrecv, acc)

        def push_out(e, out):
            base = pl.multiple_of(flip(fs, e) * rows, 16)
            out[...] = dot_nt(dqkv[pl.ds(base, rows), :], wq_ref[...]).astype(out.dtype)

        for e in reversed(range(2, fs_count)):
            part_into(at_sum, e, push_out)
        part_into(at_sum, 1, push_out)
        for j in range(1, half):
            at_sum.join(j)
        at_sum.upper()
        for m in range(1, z_count):
            sum_of_at.service(m)
        sum_of_at.service(0)
        part_into(at_sum, 0, push_out)
        at_sum.join(0)
        sum_of_ff.finish()
        at_sum.finish()
        for r in range(0, rows, LANES):
            at = slice(r, r + LANES)
            dx, dg = layer_norm_back(tok[at, :].astype(F32), gain_ref[0:1, :], acc[0, at, :])
            grad_in[at, :] = dx + dm[at, :]
            dg = jnp.sum(dg, axis=0, keepdims=True)
            gain_one = dg if r == 0 else gain_one + dg
        which = lax.broadcasted_iota(jnp.int32, (8, width), 0)
        dgain[...] = jnp.where(which == 0, gain_one, jnp.where(which == 1, gain_two, 0.0))
        sum_of_at.finish()
        net.finish()

    outs = [
        ((rows, width), F32),
        ((8, width), F32),
        ((rw, cb - 3 * hd), F32),
        ((rw, 2 * fj), F32),
        ((rw, hd), F32),
        ((2, 3, rw, hd), F32),
    ]
    wide = max(width, fj)
    zy = (y_count - 1, z_count, rw)
    scratch = [
        ((fs_count, rows, width), BF),
        ((fs_count, rows, width), BF),
        ((total, fj), BF),
        ((total, fj), BF),
        ((total, fj), BF),
        ((rows, wide), F32),
        ((heads, total, LANES), BF),
        ((heads, total, LANES), BF),
        ((hd, total), BF),
        ((total, LANES), F32),
        ((total, LANES), F32),
        ((total, 3 * hd), BF),
        ((rows, width), F32),
        ((total, hd), BF),
        ((width, 2 * fj), BF),
        ((width, 4 * hd), BF),
        ((half, rows, width), BF),
        ((half, rows, width), BF),
        ((half - 1, rows, width), BF),
        ((half - 1, rows, width), BF),
        ((half, rows, width), F32),
        (zy + (cb,), BF),
        ((z_count - 1, rw, cb - 3 * hd), BF),
        ((z_count - 1, rw, cb - 3 * hd), BF),
        ((z_count, 3, rw, hd), BF),
        ((z_count, 3, rw, hd), BF),
        (zy + (2 * fj,), BF),
        ((z_count - 1, rw, 2 * fj), BF),
        ((z_count - 1, rw, 2 * fj), BF),
        (zy + (4 * hd,), BF),
        ((z_count - 1, rw, hd), BF),
        ((z_count - 1, rw, hd), BF),
        ((z_count, 3, rw, hd), BF),
        ((z_count, 3, rw, hd), BF),
    ]
    tail = [pltpu.VMEM((heads, (n + 1) * blk, blk), BF) for n in range(blocks)]
    arrays = (da, n2, ff, mid, gain_rows, qkv, wo_own, wq, cos, sin, triples, n1, att_rel, tokens, group_b)
    return pl.pallas_call(
        body,
        out_shape=[jax.ShapeDtypeStruct(s, t) for s, t in outs],
        in_specs=[vmem()] * 10 + [smem()] + [vmem()] * 4,
        out_specs=[vmem()] * len(outs),
        scratch_shapes=[pltpu.VMEM(s, t) for s, t in scratch] + [pltpu.SemaphoreType.DMA((sems,))] * 2 + tail,
        compiler_params=pltpu.CompilerParams(collective_id=4, has_side_effects=True, vmem_limit_bytes=VMEM_BYTES),
        cost_estimate=cost(4e10, 3e7),
        name="backward_one",
    )(*arrays)


def middle(dp_count, fs_count, s0, after, z_blocks, cot, wq, rest, wp, gain_rows, cos, sin, triples):
    short, width = s0.shape
    rows, total = short * 3, short * fs_count
    hd = wq.shape[1] // 3
    pc = wp.shape[2]
    fj = (rest.shape[1] - pc - hd) // 2
    heads, docs = hd // HEAD, triples.shape[1]
    blk = min(QB, total)
    blocks, half = total // blk, fs_count // 2
    io = pc + hd
    cb = 4 * hd + 2 * pc + 2 * fj
    sems = 64 + 16 * fs_count

    def body(
        s0_ref, after_ref, z_ref, cot_ref, wq_ref, rest_ref, wp_ref, gain_ref, cos_ref, sin_ref, triples_ref,
        out, da, group, dgain,
        s0s, x_all, wos, wo_at, hold, turned, wus, wu_own, wo_src, c_own, c_rel, z_rel, dfs, df_all, das, cols, s1s, ds0s, nxt,
        n1, n2, qkv, att, att_rel, qs, ks, vt, kt, dk, dv, dqkv, work, hid, slope, dpre, m_all, dm,
        sf, rf, xf, yf, af, sb, rb, xb, yb, ab, sa, ra, xa, ya, aa, thin, spread_rows, lift, send_sem, recv_sem, *ps,
    ):
        dp, fs = lax.axis_index("dp"), lax.axis_index("fsdp")
        net = Net(send_sem, recv_sem)

        def base_of(e, amount):
            return pl.multiple_of(flip(fs, e) * amount, 16)

        def spread(pieces, src=None):
            return Flight(net, dp, fs, fs_count, pieces, pieces.at[0] if src is None else src)

        wu_own[...] = rest_ref[:, 0:pc]
        wo_src[...] = rest_ref[:, pc:io]
        nxt[...] = jnp.zeros(nxt.shape, BF)
        barrier = pltpu.get_barrier_semaphore()
        for e in range(1, fs_count):
            pl.semaphore_signal(barrier, inc=1, device_id=(dp, flip(fs, e)), device_id_type=MESH)
        pl.semaphore_wait(barrier, fs_count - 1)

        s0_f = spread(s0s, s0_ref)
        s0s[0] = s0_ref[...]
        wo_f = spread(wos, wo_src)
        wos[0] = wo_src[...]
        spread_write(thin, cot_ref[...].astype(F32))
        lifted = jnp.concatenate([strided_read(thin, k, short) for k in range(3)], axis=1).astype(BF)
        for e in range(fs_count):
            c_own[e] = lifted[:, e * pc : (e + 1) * pc]

        def exchange(blocks_of, landed):
            found = []
            for e in range(1, fs_count):
                found.append(net.start(blocks_of.at[flip(fs, e)], landed.at[e], (dp, flip(fs, e))))
            landed[0] = blocks_of[fs]
            return found

        wu_f = spread(wus, wu_own)
        wus[0] = wu_own[...]
        c_f = exchange(c_own, c_rel)

        lane_first, lane_end, lane = doc_bounds(triples_ref, docs)
        s0_f.relay()
        for e in range(fs_count):
            s0_f.ready(e)
            at = pl.ds(base_of(e, short), short)
            value = s0s[e]
            x_all[at, :] = value
            n1[at, :] = layer_norm(value, gain_ref[2:3, :]).astype(BF)
        for r in range(0, total, blk):
            at = slice(r, r + blk)
            got = dot_nn(n1[at, :], wq_ref[...])
            q, k, v = got[:, :hd], got[:, hd : 2 * hd], got[:, 2 * hd :]
            q = (q * cos_ref[at, :] + partner(q) * sin_ref[at, :]).astype(BF)
            k = (k * cos_ref[at, :] + partner(k) * sin_ref[at, :]).astype(BF)
            qkv[at, 0:hd] = q
            qkv[at, hd : 2 * hd] = k
            qkv[at, 2 * hd : 3 * hd] = v.astype(BF)
            row = lax.broadcasted_iota(jnp.int32, (blk, LANES), 0) + r
            inside = (row >= lane_first) & (row < lane_end)
            fk = jnp.where(inside, 1.0, 0.0)
            fq = jnp.where(inside | (lane >= docs), 0.0, MASKED)
            head_inputs(qs, ks, at, q.astype(F32), k.astype(F32), fq, fk, heads)
            vt[:, at] = v.T.astype(BF)
            kt[:, at] = k.astype(F32).T.astype(BF)
            dk[at, :] = jnp.zeros((blk, LANES), F32)
            dv[at, :] = jnp.zeros((blk, LANES), F32)
        flights = []
        for n in range(blocks):
            r, stop = n * blk, (n + 1) * blk
            found = []
            for h in range(heads):
                e, inv = softmax_block(ks, qs, h, r, stop)
                ps[n][h] = (e * inv).astype(BF)
                found.append(dot_nn(vt[h * HEAD : (h + 1) * HEAD, 0:stop], ps[n][h]))
            att[0, r:stop, :] = jnp.concatenate(found, axis=0).T.astype(BF)
            flights.append(spread(att.at[:, r:stop, :], att.at[0, r:stop, :]))
            if n == 0:
                wo_f.relay()
        place_of = lax.broadcasted_iota(jnp.int32, (blk, LANES), 1) // HEAD
        for r in range(0, total, blk):
            at = slice(r, r + blk)
            q = widen(qkv[at, 0:hd].astype(F32))
            for h in range(heads):
                qs[h, at, :] = jnp.where(place_of == h, q, 0.0).astype(BF)

        wu_f.relay()
        acc = jnp.zeros((short, width), F32)
        for e in range(fs_count):
            wu_f.ready(e)
            acc = acc + dot_nt(c_own[flip(fs, e)], wus[e])
        ds1 = acc
        dfs[0] = ds1.astype(BF)
        df_f = spread(dfs)
        z_f = exchange(z_ref, z_rel)

        for flight in flights:
            flight.relay()
        wo_f.all_ready()
        for e in range(fs_count):
            wo_at[flip(fs, e)] = wos[e]
        for e in range(fs_count):
            hold[:, e * hd : (e + 1) * hd] = wo_at[e]
        for e in range(fs_count):
            turned[e * hd : (e + 1) * hd, :] = hold[pl.ds(base_of(e, hd), hd), :]
        for flight in flights:
            flight.all_ready()
        for e in range(fs_count):
            att_rel[:, e * hd : (e + 1) * hd] = att[e]

        work[:, 0:width] = x_all[...] + dot_nn(att_rel[...], turned[...])
        for r in range(0, total, HEAD):
            m = work[r : r + HEAD, 0:width]
            m_all[r : r + HEAD, :] = m
            n2[r : r + HEAD, :] = layer_norm(m, gain_ref[3:4, :]).astype(BF)
        work[:, 0:fj] = dot_nn(n2[...], rest_ref[:, io : io + fj])
        for r in range(0, total, HEAD):
            value, rate = gelu_both(work[r : r + HEAD, 0:fj])
            hid[r : r + HEAD, :] = value.astype(BF)
            slope[r : r + HEAD, :] = rate
        work[:, 0:width] = dot_nt(hid[...], rest_ref[:, io + fj :])

        def give_out(scatter, source):
            for e in reversed(range(fs_count)):
                value = source[pl.ds(base_of(e, short), short), 0:width]
                if e % 2:
                    scatter.sbuf[e // 2] = value.astype(BF)
                    scatter.send_odd(e // 2)
                else:
                    scatter.acc[e // 2] = value

        fwd = Scatter(net, dp, fs, fs_count, sf, rf, xf, yf, af)
        give_out(fwd, work)
        df_f.relay()
        for e in range(fs_count):
            df_f.ready(e)
            df_all[pl.ds(base_of(e, short), short), :] = dfs[e]
        work[:, 0:fj] = dot_nn(df_all[...], rest_ref[:, io + fj :])
        for r in range(0, total, HEAD):
            at = slice(r, r + HEAD)
            dpre[at, :] = (work[at, 0:fj] * slope[at, :]).astype(BF)
        work[:, 0:width] = dot_nt(dpre[...], rest_ref[:, io : io + fj])
        bwd = Scatter(net, dp, fs, fs_count, sb, rb, xb, yb, ab)
        give_out(bwd, work)
        for j in range(1, half):
            bwd.join(j)
        bwd.upper()
        for j in range(1, half):
            fwd.join(j)
        fwd.upper()
        at = 3 * hd + 2 * pc
        group[:, at : at + fj] = dot_tn(n2[...], dpre[...]).astype(BF)
        group[:, at + fj : at + 2 * fj] = dot_tn(df_all[...], hid[...]).astype(BF)
        bwd.join(0)
        bwd.finish()
        m_own = m_all[pl.ds(base_of(0, short), short), :]
        dx, dg = layer_norm_back(m_own, gain_ref[3:4, :], ab[0])
        dx = dx + ds1
        dm[...] = dx
        das[0] = dx.astype(BF)
        da_f = spread(das)
        gain_two = jnp.sum(dg, axis=0, keepdims=True)

        fwd.join(0)
        fwd.finish()
        s1s[0] = (m_own + af[0]).astype(BF)
        s1_f = spread(s1s)
        for e in range(fs_count):
            lift[flip(fs, e)] = dot_nn(s1s[0], wus[e])
        lifted = jnp.concatenate([lift[e] for e in range(fs_count)], axis=1)
        for k in range(3):
            strided_write(thin, k, short, lifted[:, k * width : (k + 1) * width])
        out[...] = (after_ref[...] + spread_read(thin)).astype(BF)

        da_f.relay()
        s1_f.relay()
        for e in range(fs_count):
            da_f.ready(e)
            at = pl.ds(base_of(e, short), short)
            do = widen(dot_nt(das[e], turned[0:hd, :]))
            lane_head = lax.broadcasted_iota(jnp.int32, (short, LANES), 1) // HEAD
            for h in range(heads):
                ks[h, at, :] = jnp.where(lane_head == h, do, 0.0).astype(BF)
            for k in range(fs_count):

                @pl.when(fs == k)
                def _():
                    cols[at, :] = das[e, :, k * hd : (k + 1) * hd]

        g_out = dot_tn(att_rel[...], cols[...]).astype(BF)
        for e in range(fs_count):
            group[pl.ds(base_of(e, hd), hd), cb - hd : cb] = g_out[e * hd : (e + 1) * hd, :]
        for n in range(blocks):
            r, stop = n * blk, (n + 1) * blk
            at = slice(r, stop)
            found = []
            add_k = add_v = None
            for h in range(heads):
                p = ps[n][h]
                grad = dot_nt(widen(qkv[0:stop, 2 * hd : 3 * hd]), ks[h, at, :])
                wide = p.astype(F32)
                inner = jnp.sum(wide * grad, axis=0, keepdims=True)
                dr = (wide * (grad - inner) * 0.125).astype(BF)
                part_v = dot_nn(p, ks[h, at, :])
                part_k = dot_nn(dr, qs[h, at, :])
                add_v = part_v if add_v is None else add_v + part_v
                add_k = part_k if add_k is None else add_k + part_k
                found.append(dot_nn(kt[h * HEAD : (h + 1) * HEAD, 0:stop], dr))
            dk[0:stop, :] += add_k
            dv[0:stop, :] += add_v
            dq = jnp.concatenate(found, axis=0).T
            dqkv[at, 0:hd] = (dq * cos_ref[at, :] - partner(dq) * sin_ref[at, :]).astype(BF)
        for r in range(0, total, blk):
            at = slice(r, r + blk)
            grad = dk[at, 0:hd]
            dqkv[at, hd : 2 * hd] = (grad * cos_ref[at, :] - partner(grad) * sin_ref[at, :]).astype(BF)
            dqkv[at, 2 * hd : 3 * hd] = dv[at, 0:hd].astype(BF)
        work[:, 0:width] = dot_nt(dqkv[...], wq_ref[...])
        first = Scatter(net, dp, fs, fs_count, sa, ra, xa, ya, aa)
        give_out(first, work)
        for j in range(1, half):
            first.join(j)
        first.upper()
        group[:, 0 : 3 * hd] = dot_tn(n1[...], dqkv[...]).astype(BF)
        s1_f.all_ready()
        for copy in c_f:
            copy.wait_recv()
        g_up = jnp.zeros((width, pc), F32)
        for e in range(fs_count):
            g_up = g_up + dot_tn(s1s[e], c_rel[e])
        group[:, 3 * hd + pc : 3 * hd + 2 * pc] = g_up.astype(BF)
        first.join(0)
        first.finish()
        dx, dg = layer_norm_back(s0_ref[...], gain_ref[2:3, :], aa[0])
        ds0s[0] = (dx + dm[...]).astype(BF)
        gain_one = jnp.sum(dg, axis=0, keepdims=True)
        which = lax.broadcasted_iota(jnp.int32, (8, width), 0)
        dgain[...] = jnp.where(which == 0, gain_one, jnp.where(which == 1, gain_two, 0.0))

        hop = net.make(ds0s.at[0, 0:HALO, :], nxt, (dp, lax.rem(fs + fs_count - 1, fs_count)))

        @pl.when(fs > 0)
        def _():
            hop.start()

        ds0_f = spread(ds0s)
        row = lax.broadcasted_iota(jnp.int32, (short, LANES), 0) + fs * short + 1
        shut = jnp.max(jnp.where((row == lane_first) | (row >= total), 1.0, 0.0), axis=1, keepdims=True) > 0.0

        @pl.when(fs < fs_count - 1)
        def _():
            hop.wait_recv()

        grad = jnp.concatenate([ds0s[0], nxt[...]], axis=0)
        for e in range(fs_count):
            lift_at = dot_nn(grad, wp_ref[e])
            spread_rows[flip(fs, e)] = lift_at
        dz = jnp.concatenate([spread_rows[e] for e in range(fs_count)], axis=1)
        strided_write(thin, 0, short, dz[0:short, 2 * width : 3 * width])
        for k in range(2):
            part = dz[1 : short + 1, k * width : (k + 1) * width]
            strided_write(thin, k + 1, short, jnp.where(shut, 0.0, part))
        da[...] = cot_ref[...].astype(F32) + spread_read(thin)
        ds0_f.relay()
        for copy in z_f:
            copy.wait_recv()
        g_pool = jnp.zeros((width, pc), F32)
        for e in range(fs_count):
            ds0_f.ready(e)
            g_pool = g_pool + dot_tn(ds0s[e], z_rel[e])
        group[:, 3 * hd : 3 * hd + pc] = g_pool.astype(BF)

        @pl.when(fs > 0)
        def _():
            hop.wait_send()

        net.finish()

    wide = max(width, fj)
    pieces = (fs_count, short, width)
    scatter = [((half, short, width), BF)] * 2 + [((half - 1, short, width), BF)] * 2 + [((half, short, width), F32)]
    outs = [((rows, width), BF), ((rows, width), F32), ((width, cb), BF), ((8, width), F32)]
    scratch = [
        (pieces, F32),
        ((total, width), F32),
        ((fs_count, width, hd), BF),
        ((fs_count, width, hd), BF),
        ((width, width), BF),
        ((width, width), BF),
        ((fs_count, width, pc), BF),
        ((width, pc), BF),
        ((width, hd), BF),
        ((fs_count, short, pc), BF),
        ((fs_count, short, pc), BF),
        ((fs_count, short, pc), BF),
        (pieces, BF),
        ((total, width), BF),
        (pieces, BF),
        ((total, hd), BF),
        (pieces, BF),
        (pieces, BF),
        ((HALO, width), BF),
        ((total, width), BF),
        ((total, width), BF),
        ((total, 3 * hd), BF),
        ((fs_count, total, hd), BF),
        ((total, width), BF),
        ((heads, total, LANES), BF),
        ((heads, total, LANES), BF),
        ((hd, total), BF),
        ((hd, total), BF),
        ((total, LANES), F32),
        ((total, LANES), F32),
        ((total, 3 * hd), BF),
        ((total, wide), F32),
        ((total, fj), BF),
        ((total, fj), F32),
        ((total, fj), BF),
        ((total, width), F32),
        ((short, width), F32),
        *scatter,
        *scatter,
        *scatter,
        ((width // LANES, rows, LANES), F32),
        ((fs_count, short + HALO, pc), F32),
        ((fs_count, short, pc), F32),
    ]
    tail = [pltpu.VMEM((heads, (n + 1) * blk, blk), BF) for n in range(blocks)]
    arrays = (s0, after, z_blocks, cot, wq, rest, wp, gain_rows, cos, sin, triples)
    return pl.pallas_call(
        body,
        out_shape=[jax.ShapeDtypeStruct(s, t) for s, t in outs],
        in_specs=[vmem()] * 10 + [smem()],
        out_specs=[vmem()] * len(outs),
        scratch_shapes=[pltpu.VMEM(s, t) for s, t in scratch] + [pltpu.SemaphoreType.DMA((sems,))] * 2 + tail,
        compiler_params=pltpu.CompilerParams(collective_id=2, has_side_effects=True, vmem_limit_bytes=VMEM_BYTES),
        cost_estimate=cost(2e10, 2e7),
        name="middle",
    )(*arrays)


def owners_of(amount, dp_count, fs_count):
    found = []
    half = dp_count // 2
    for k in range(amount):
        found.append((dp_count // 4 + k % half, (2 * (k // half)) % fs_count + (2 * (k // half)) // fs_count))
    return found


def round_up(width):
    return -(-width // LANES) * LANES


def newton_schulz(box, x, norm, count, width, dp_count, rw, done):
    coef_a, coef_b, coef_c = NS_COEFS
    rows = dp_count * rw
    square = jnp.zeros((1, 1), F32)
    for at in range(count):
        block = box[at * dp_count : (at + 1) * dp_count, :, 0:width].reshape(rows, width)
        x[:, at * width : (at + 1) * width] = block
        wide = block.astype(F32)
        square = square + jnp.sum(jnp.sum(wide * wide, axis=0, keepdims=True), axis=1, keepdims=True)
    length = jnp.sqrt(square)
    norm[...] = jnp.broadcast_to(length, norm.shape)
    scale = 1.0 / (length + NORM_EPS)
    span = count * width
    for turn in range(NS_STEPS):
        gram = dot_nt(x[:, 0:span], x[:, 0:span])
        if turn == 0:
            gram = gram * (scale * scale)
        gram = gram.astype(BF)
        poly = (coef_b * gram.astype(F32) + coef_c * dot_nn(gram, gram)).astype(BF)
        for at in range(count):
            here = slice(at * width, (at + 1) * width)
            block = x[:, here]
            new = coef_a * block.astype(F32) + dot_nn(poly, block)
            if turn == 0:
                new = new * scale
            if turn < NS_STEPS - 1:
                x[:, here] = new.astype(BF)
            else:
                box[at * dp_count : (at + 1) * dp_count, :, 0:width] = new.astype(BF).reshape(dp_count, rw, width)
                done(at)


def muon(y_count, dp_count, fs_count, sums, moments, dgains):
    sum_q, sum_o, sum_ff, sum_rest = sums
    rw, hd = sum_o.shape
    fj = sum_ff.shape[1] // 2
    pc = moments[4].shape[1]
    width = rw * dp_count
    z_count = dp_count // y_count
    devices = dp_count * fs_count
    widths = [fj, fj, fj, fj, 3 * hd, 3 * hd, pc, pc, hd, hd]
    widths = [round_up(w) for w in widths]
    amount, wide = len(widths), max(widths)
    owners = owners_of(amount, dp_count, fs_count)
    classes = sorted(set(widths))
    sems = 64 + amount

    def body(
        q_ref, o_ref, ff_ref, rest_ref, mq, mo, mi, md, mp, mu, ga, gb,
        out, norms, dgain, box, x, norm, tiles, tsend, *rest_refs,
    ):
        pieces = rest_refs[:amount]
        send_sem, recv_sem, push_send, push_recv, give_send, give_recv, norm_send, norm_recv = rest_refs[amount:]
        dp, fs = lax.axis_index("dp"), lax.axis_index("fsdp")
        slot = fs * dp_count + dp
        net = Net(send_sem, recv_sem)

        def put(k, value):
            have = value.shape[1]
            if have < widths[k]:
                value = jnp.concatenate([value, jnp.zeros((rw, widths[k] - have), F32)], axis=1)
            pieces[k][...] = value.astype(BF)

        at = 2 * pc
        put(0, MOMENT_DECAY * mi[0] + ff_ref[:, 0:fj])
        put(1, MOMENT_DECAY * mi[1] + rest_ref[:, at : at + fj])
        put(2, MOMENT_DECAY * md[0] + ff_ref[:, fj : 2 * fj])
        put(3, MOMENT_DECAY * md[1] + rest_ref[:, at + fj : at + 2 * fj])
        for b in range(2):
            put(4 + b, MOMENT_DECAY * mq[b] + jnp.concatenate([q_ref[b, t] for t in range(3)], axis=1))
        put(6, MOMENT_DECAY * mp[...] + rest_ref[:, 0:pc])
        put(7, MOMENT_DECAY * mu[...] + rest_ref[:, pc : 2 * pc])
        put(8, MOMENT_DECAY * mo[0] + o_ref[...])
        put(9, MOMENT_DECAY * mo[1] + rest_ref[:, at + 2 * fj :])
        which = lax.broadcasted_iota(jnp.int32, (8, width), 0)
        tiles[0] = jnp.where(
            which < 2, ga[...], jnp.where(which == 2, gb[0:1, :], jnp.where(which == 3, gb[1:2, :], 0.0))
        )
        if any(w != wide for w in widths):
            box[...] = jnp.zeros(box.shape, BF)

        barrier = pltpu.get_barrier_semaphore()

        def greet(t, carry):
            @pl.when(t != slot)
            def _():
                there = (lax.rem(t, dp_count), lax.div(t, dp_count))
                pl.semaphore_signal(barrier, inc=1, device_id=there, device_id_type=MESH)

            return carry

        lax.fori_loop(0, devices, greet, 0)
        pl.semaphore_wait(barrier, devices - 1)

        mine = [(dp == owners[k][0]) & (fs == owners[k][1]) for k in range(amount)]
        for k in range(amount):
            copy = pltpu.make_async_remote_copy(
                src_ref=pieces[k],
                dst_ref=box.at[slot, :, 0 : widths[k]],
                send_sem=push_send.at[k],
                recv_sem=push_recv,
                device_id=owners[k],
                device_id_type=MESH,
            )

            @pl.when(jnp.logical_not(mine[k]))
            def _():
                copy.start()

            @pl.when(mine[k])
            def _():
                box[slot, :, 0 : widths[k]] = pieces[k][...]

        hop = net.start(tiles.at[0], tiles.at[1], (dp, flip(fs, 1)))

        for k in range(amount):

            @pl.when(mine[k])
            def _():
                landed = box.at[0 : devices - 1, :, 0 : widths[k]]
                pltpu.make_async_copy(landed, landed, push_recv).wait()

        which_k = jnp.int32(0)
        for k in range(1, amount):
            which_k = which_k + k * mine[k].astype(jnp.int32)
        for w in classes:
            chosen = None
            for k in range(amount):
                if widths[k] == w:
                    chosen = mine[k] if chosen is None else chosen | mine[k]

            @pl.when(chosen)
            def _():
                def done(block):
                    def give(i, carry):
                        t = block * dp_count + i

                        @pl.when(t != slot)
                        def _():
                            pltpu.make_async_remote_copy(
                                src_ref=box.at[t, :, 0:w],
                                dst_ref=out.at[which_k, :, 0:w],
                                send_sem=give_send,
                                recv_sem=give_recv.at[which_k],
                                device_id=(i, block),
                                device_id_type=MESH,
                            ).start()
                            pltpu.make_async_remote_copy(
                                src_ref=norm,
                                dst_ref=norms.at[which_k],
                                send_sem=norm_send,
                                recv_sem=norm_recv.at[which_k],
                                device_id=(i, block),
                                device_id_type=MESH,
                            ).start()

                        return carry

                    lax.fori_loop(0, dp_count, give, 0)

                newton_schulz(box, x, norm, fs_count, w, dp_count, rw, done)
                out[which_k, :, 0:w] = box[slot, :, 0:w]
                norms[which_k] = norm[...]

        total = tiles[0]
        hop.wait_recv()
        total = total + tiles[1]
        at = 2
        bit = 2
        hops = [((dp, flip(fs, 1 << n)), None) for n in range(1, fs_count.bit_length() - 1)]
        hops += [((flip(dp, 1 << n), fs), None) for n in range(dp_count.bit_length() - 1)]
        for n, (there, _) in enumerate(hops):
            tsend[n] = total
            hop = net.start(tsend.at[n], tiles.at[2 + n], there)
            hop.wait_recv()
            total = total + tiles[2 + n]
        dgain[...] = total

        for k in range(amount):
            w = widths[k]

            @pl.when(jnp.logical_not(mine[k]))
            def _():
                landed = out.at[k, :, 0:w]
                pltpu.make_async_copy(landed, landed, give_recv.at[k]).wait()
                pltpu.make_async_copy(norms.at[k], norms.at[k], norm_recv.at[k]).wait()
                pltpu.make_async_copy(pieces[k], pieces[k], push_send.at[k]).wait()

            @pl.when(mine[k])
            def _():
                left = box.at[0 : devices - 1, :, 0:w]
                pltpu.make_async_copy(left, left, give_send).wait()

                def drain(t, carry):
                    pltpu.make_async_copy(norm, norm, norm_send).wait()
                    return carry

                lax.fori_loop(0, devices - 1, drain, 0)

        net.finish()

    hops = (fs_count.bit_length() - 1) + (dp_count.bit_length() - 1)
    outs = [((amount, rw, wide), BF), ((amount, 8, LANES), F32), ((8, width), F32)]
    scratch = [
        ((devices, rw, wide), BF),
        ((width, fs_count * wide), BF),
        ((8, LANES), F32),
        ((hops + 1, 8, width), F32),
        ((hops, 8, width), F32),
    ] + [((rw, w), BF) for w in widths]
    dma = pltpu.SemaphoreType.DMA
    return pl.pallas_call(
        body,
        out_shape=[jax.ShapeDtypeStruct(s, t) for s, t in outs],
        in_specs=[vmem()] * 12,
        out_specs=[vmem()] * len(outs),
        scratch_shapes=[pltpu.VMEM(s, t) for s, t in scratch]
        + [dma((sems,)), dma((sems,)), dma((amount,)), dma, dma, dma((amount,)), dma, dma((amount,))],
        compiler_params=pltpu.CompilerParams(collective_id=1, has_side_effects=True, vmem_limit_bytes=VMEM_BYTES),
        name="muon",
    )(sum_q, sum_o, sum_ff, sum_rest, *moments, *dgains)


def update(dp_arr, sums, results, dgain, moments, weights, m_gains, gains):
    sum_q, sum_o, sum_ff, sum_rest = sums
    rw, hd = sum_o.shape
    fj = sum_ff.shape[1] // 2
    pc = moments[4].shape[1]
    width = dgain.shape[1]

    def body(me_ref, q_ref, o_ref, ff_ref, rest_ref, res, dg, *refs):
        m_in, w_in, (mg, g), refs = refs[:6], refs[6:12], refs[12:14], refs[14:]
        m_out, w_out, (mg_out, g_out), turned = refs[:6], refs[6:12], refs[12:14], refs[14]
        at = 2 * pc
        grads = [
            [jnp.concatenate([q_ref[b, t] for t in range(3)], axis=1) for b in range(2)],
            [o_ref[...], rest_ref[:, at + 2 * fj :]],
            [ff_ref[:, 0:fj], rest_ref[:, at : at + fj]],
            [ff_ref[:, fj : 2 * fj], rest_ref[:, at + fj : at + 2 * fj]],
            [rest_ref[:, 0:pc]],
            [rest_ref[:, pc : 2 * pc]],
        ]
        places = [(4, 5), (8, 9), (0, 1), (2, 3), (6,), (7,)]
        for kind in range(6):
            for b in range(len(grads[kind])):
                here = (b,) if kind < 4 else (slice(None),)
                have = m_in[kind].shape[-1]
                m_out[kind][here] = MOMENT_DECAY * m_in[kind][here] + grads[kind][b]
                turn = res[places[kind][b], :, 0:have].astype(F32)
                w_out[kind][here] = w_in[kind][here] - STEP_SCALES[kind] * turn
        turned[...] = jnp.concatenate([dg[...], jnp.zeros((LANES - 8, width), F32)], axis=0).T
        grad = turned[pl.ds(pl.multiple_of(me_ref[0] * rw, 16), rw), 0:4]
        fresh = GAIN_DECAY * mg[...] + grad
        mg_out[...] = fresh
        g_out[...] = g[...] - GAIN_RATE * fresh

    outs = [(a.shape, F32) for a in (*moments, *weights, m_gains, gains)]
    return local_kernel(
        body,
        "update",
        outs,
        [((width, LANES), F32)],
        dp_arr,
        sum_q,
        sum_o,
        sum_ff,
        sum_rest,
        results,
        dgain,
        *moments,
        *weights,
        m_gains,
        gains,
    )


def rope_tables(total, hd):
    half = HEAD // 2
    frequency = (np.float32(10000.0) ** (-np.arange(half, dtype=np.float32) / np.float32(half))).astype(np.float32)
    angle = (np.arange(total, dtype=np.float32)[:, None] * frequency[None, :]).astype(np.float32)
    cos, sin = np.cos(angle), np.sin(angle)
    cos = np.tile(np.concatenate([cos, cos], axis=1), (1, hd // HEAD))
    sin = np.tile(np.concatenate([-sin, sin], axis=1), (1, hd // HEAD))
    return jnp.asarray(cos, F32), jnp.asarray(sin, F32)


def on_device(
    y_count,
    tokens,
    cotangent,
    doc_triples,
    w_qkv,
    w_out,
    w_in,
    w_down,
    w_pool,
    w_up,
    gains,
    m_qkv,
    m_out,
    m_in,
    m_down,
    m_pool,
    m_up,
    m_gains,
):
    rows, width = tokens.shape
    short = rows // 3
    fs_count, dp_count = lax.axis_size("fsdp"), lax.axis_size("dp")
    me, dp_me = lax.axis_index("fsdp"), lax.axis_index("dp")
    me_arr, dp_arr = me.astype(jnp.int32).reshape(1), dp_me.astype(jnp.int32).reshape(1)
    total, short_total = rows * fs_count, short * fs_count
    hd = width // fs_count
    fj = w_in.shape[2]
    pool_cols = w_pool.shape[1]

    cos0, sin0 = rope_tables(total, hd)
    cos1, sin1 = cos0[:short_total], sin0[:short_total]

    old_weights = (w_qkv, w_out, w_in, w_down, w_pool, w_up)
    n1, qkv, att_rel, wo_own, n2, mid, after, z_blocks, s0, wqkv0, ff0, wp_all, wqkv1, rest, gain_rows = forward_one(
        y_count, dp_count, fs_count, tokens, doc_triples, old_weights, gains, cos0, sin0
    )
    layer_out, da, group_b, dgain_b = middle(
        dp_count, fs_count, s0, after, z_blocks, cotangent, wqkv1, rest, wp_all, gain_rows, cos1, sin1, doc_triples
    )
    grad_in, dgain_a, sum_rest, sum_ff, sum_o, sum_q = backward_one(
        y_count,
        dp_count,
        fs_count,
        da,
        n2,
        ff0,
        mid,
        gain_rows,
        qkv,
        wo_own,
        wqkv0,
        cos0,
        sin0,
        doc_triples,
        n1,
        att_rel,
        tokens,
        group_b,
    )

    sums = (sum_q, sum_o, sum_ff, sum_rest)
    moments = (m_qkv, m_out, m_in, m_down, m_pool, m_up)
    results, norms, dgain = muon(y_count, dp_count, fs_count, sums, moments, (dgain_a, dgain_b))
    fresh = update(dp_arr, sums, results, dgain, moments, old_weights, m_gains, gains)
    all_tokens = float(total * dp_count)
    entries = [m.size // (2 if m.ndim == 3 else 1) for m in moments for _ in range(2 if m.ndim == 3 else 1)]
    roots = np.array([float(n * fs_count * dp_count) * all_tokens for n in entries], np.float64) ** 0.5
    lengths = norms[:, 0, 0]
    lengths = jnp.concatenate([lengths[4:6], lengths[8:10], lengths[0:4], lengths[6:8]])
    moment_rms = lengths / jnp.asarray(roots, F32)
    return (layer_out, grad_in, *fresh, moment_rms)


def solution(mesh):
    by_row, by_dp = P(("dp", "fsdp"), None), P("dp", None)
    stacked, flat = P(None, "dp", "fsdp"), P("dp", "fsdp")
    matrices = (stacked,) * 4 + (flat,) * 2
    y_count = max(1, mesh.shape["fsdp"] // 2)
    return jax.shard_map(
        functools.partial(on_device, y_count),
        mesh=mesh,
        in_specs=(by_row, by_row, by_dp, *matrices, by_dp, *matrices, by_dp),
        out_specs=(by_row, by_row, *matrices, *matrices, by_dp, by_dp, P()),
        check_vma=False,
    )
```

```python
import functools

import jax
import jax.numpy as jnp
import numpy as np
from jax import lax
from jax.experimental import pallas as pl
from jax.experimental.pallas import tpu as pltpu
from jax.sharding import PartitionSpec as P

HEAD = 64
NS_STEPS = 5
NS_COEFS = (3.4445, -4.775, 2.0315)
STEP_SCALES = (0.8660254, 1.4142136, 1.0, 0.5, 0.5, 0.8660254)
MOMENT_DECAY = 0.95
GAIN_DECAY = 0.9
GAIN_RATE = 0.001
LN_EPS = 1e-05
NORM_EPS = 1e-07
MASKED = -1e30
HALO = 16
QB = 256
LANES = 128
VMEM_BYTES = 60 << 20
BF = jnp.bfloat16
F32 = jnp.float32
MESH = pl.DeviceIdType.MESH


def dot_nn(left, right):
    return lax.dot_general(left, right, (((1,), (0,)), ((), ())), preferred_element_type=F32)


def dot_nt(left, right):
    return lax.dot_general(left, right, (((1,), (1,)), ((), ())), preferred_element_type=F32)


def dot_tn(left, right):
    return lax.dot_general(left, right, (((0,), (0,)), ((), ())), preferred_element_type=F32)


def layer_norm(values, gain):
    mean = jnp.mean(values, axis=-1, keepdims=True)
    centred = values - mean
    spread = jnp.mean(centred * centred, axis=-1, keepdims=True)
    return centred * lax.rsqrt(spread + LN_EPS) * gain


def layer_norm_back(values, gain, grad):
    mean = jnp.mean(values, axis=-1, keepdims=True)
    centred = values - mean
    spread = jnp.mean(centred * centred, axis=-1, keepdims=True)
    scale = lax.rsqrt(spread + LN_EPS)
    unit = centred * scale
    scaled = grad * gain
    part = jnp.mean(scaled, axis=-1, keepdims=True)
    along = jnp.mean(scaled * unit, axis=-1, keepdims=True)
    return scale * (scaled - part - unit * along), grad * unit


def gelu(values):
    return 0.5 * values * (1.0 + jnp.tanh(0.7978845608028654 * (values + 0.044715 * values * values * values)))


def gelu_both(values):
    square = values * values
    turn = jnp.tanh(0.7978845608028654 * (values + 0.044715 * values * square))
    slope = 0.7978845608028654 * (1.0 + 3.0 * 0.044715 * square)
    half = 0.5 * (1.0 + turn)
    return values * half, half + 0.5 * values * (1.0 - turn * turn) * slope


def partner(values):
    width = values.shape[1]
    if width == LANES:
        lane = lax.broadcasted_iota(jnp.int32, values.shape, 1)
        ahead = pltpu.roll(values, LANES - HEAD // 2, 1)
        behind = pltpu.roll(values, HEAD // 2, 1)
        return jnp.where(lane % HEAD < HEAD // 2, ahead, behind)
    parts = []
    for at in range(0, width, HEAD):
        parts += [values[:, at + HEAD // 2 : at + HEAD], values[:, at : at + HEAD // 2]]
    return jnp.concatenate(parts, axis=1)


def widen(values):
    rows, width = values.shape
    if width >= LANES:
        return values
    return jnp.concatenate([values, jnp.zeros((rows, LANES - width), values.dtype)], axis=1)


def params():
    return pltpu.CompilerParams(vmem_limit_bytes=VMEM_BYTES)


def smem():
    return pl.BlockSpec(memory_space=pltpu.SMEM)


def vmem():
    return pl.BlockSpec(memory_space=pltpu.VMEM)


def hbm():
    return pl.BlockSpec(memory_space=pl.ANY)


def cost(flops, moved):
    return pl.CostEstimate(flops=int(flops), bytes_accessed=int(moved), transcendentals=0)


def local_kernel(body, name, outs, scratch, me, *arrays, flops=0):
    moved = sum(a.size * a.dtype.itemsize for a in arrays)
    moved += sum(int(np.prod(s)) * jnp.dtype(t).itemsize for s, t in outs)
    return pl.pallas_call(
        body,
        out_shape=[jax.ShapeDtypeStruct(s, t) for s, t in outs],
        in_specs=[smem()] + [vmem()] * len(arrays),
        out_specs=[vmem()] * len(outs),
        scratch_shapes=[pltpu.VMEM(s, t) for s, t in scratch],
        compiler_params=params(),
        cost_estimate=cost(flops, moved),
        name=name,
    )(me, *arrays)


def at_rows(me, step, rows):
    return pl.multiple_of((me ^ step) * rows, 16)


def head_inputs(qs, ks, rows, q, k, fq, fk, heads):
    lane = lax.broadcasted_iota(jnp.int32, (q.shape[0], LANES), 1)
    q, k = widen(q), widen(k)
    for h in range(heads):
        mine = lane // HEAD == h
        qs[h, rows, :] = jnp.where(mine, q * 0.125, fq).astype(BF)
        ks[h, rows, :] = jnp.where(mine, k, fk).astype(BF)


def scores_t(ks, qs, h, start, stop):
    top = dot_nt(ks[h, 0:stop, :], qs[h, start:stop, :])
    key = lax.broadcasted_iota(jnp.int32, (stop - start, stop - start), 0)
    query = lax.broadcasted_iota(jnp.int32, (stop - start, stop - start), 1)
    last = jnp.where(key <= query, top[start:, :], MASKED)
    if start == 0:
        return last
    return jnp.concatenate([top[:start, :], last], axis=0)


def spread_write(hold, values):
    for c in range(hold.shape[0]):
        hold[c] = values[:, c * LANES : (c + 1) * LANES]


def spread_read(hold):
    return jnp.concatenate([hold[c] for c in range(hold.shape[0])], axis=1)


def strided_read(hold, start, amount):
    return jnp.concatenate([hold[c, pl.ds(start, amount, stride=3), :] for c in range(hold.shape[0])], axis=1)


def strided_write(hold, start, amount, values):
    for c in range(hold.shape[0]):
        hold[c, pl.ds(start, amount, stride=3), :] = values[:, c * LANES : (c + 1) * LANES]


def flip(value, step):
    bit = 1
    while bit <= step:
        if step & bit:
            value = value + bit - 2 * bit * lax.rem(lax.div(value, bit), 2)
        bit *= 2
    return value


class Net:
    def __init__(self, send, recv):
        self.send, self.recv, self.used, self.open = send, recv, 0, []

    def make(self, src, dst, device):
        at = self.used
        self.used += 1
        return pltpu.make_async_remote_copy(
            src_ref=src,
            dst_ref=dst,
            send_sem=self.send.at[at],
            recv_sem=self.recv.at[at],
            device_id=device,
            device_id_type=MESH,
        )

    def start(self, src, dst, device):
        copy = self.make(src, dst, device)
        copy.start()
        self.open.append(copy)
        return copy

    def local(self, src, dst):
        at = self.used
        self.used += 1
        copy = pltpu.make_async_copy(src, dst, self.send.at[at])
        copy.start()
        return copy

    def finish(self):
        for copy in self.open:
            copy.wait_send()


class Flight:
    def __init__(self, net, dp, fs, fs_count, pieces, src):
        self.net, self.dp, self.fs, self.pieces = net, dp, fs, pieces
        self.top, self.copies, self.waited = fs_count // 2, {}, set()
        bit = self.top
        while bit:
            self.copies[bit] = net.start(src, pieces.at[bit], (dp, flip(fs, bit)))
            bit //= 2

    def ready(self, step):
        if step and step not in self.waited:
            self.waited.add(step)
            self.copies[step].wait_recv()

    def relay(self):
        known, bit = [self.top], self.top // 2
        while bit:
            fresh = []
            for step in known:
                self.ready(step)
                there = (self.dp, flip(self.fs, bit))
                self.copies[step + bit] = self.net.start(self.pieces.at[step], self.pieces.at[step + bit], there)
                fresh.append(step + bit)
            known = known + [bit] + fresh
            bit //= 2

    def all_ready(self):
        for step in sorted(self.copies):
            self.ready(step)


def doc_bounds(triples, docs):
    lane = lax.broadcasted_iota(jnp.int32, (1, LANES), 1)
    lane = jnp.where(lane >= HEAD, lane - HEAD, lane)
    first = jnp.full((1, LANES), -1, jnp.int32)
    end = jnp.full((1, LANES), -1, jnp.int32)
    at = jnp.int32(0)
    for j in range(docs):
        here = lane == j
        first = jnp.where(here, at, first)
        at = at + triples[0, j]
        end = jnp.where(here, at, end)
    return first, end, lane


def softmax_block(ks, qs, h, r, stop):
    s = scores_t(ks, qs, h, r, stop)
    e = jnp.exp(s - jnp.max(s, axis=0, keepdims=True))
    return e, 1.0 / jnp.sum(e, axis=0, keepdims=True)


def forward_one(y_count, dp_count, fs_count, tokens, cot, triples, weights, gains_t, cos, sin):
    rows, width = tokens.shape
    total, short = rows * fs_count, rows // 3
    long_rows = rows + HALO
    wqkv, wout, win, wdown, wpool, wup = weights
    rw = wqkv.shape[1]
    hd, fj, pc = wout.shape[2], win.shape[2], wpool.shape[1]
    heads = hd // HEAD
    docs = triples.shape[1]
    z_count = dp_count // y_count
    blk = QB
    sems = 96 + 16 * dp_count

    def body(
        tok, cot_ref, triples_ref, q_in, o_in, i_in, d_in, p_in, u_in, g_in, cos_ref, sin_ref,
        n1_hbm, qkv_hbm, att_hbm, wo_own, n2_hbm, mid, after, z_out, s0_out, wq_out, wi, wd, wp, wq1_out, wu, c_rel, gain_out,
        n1, qkv, att_rel, n2, toks, c_own, st_q, wq0, wq1, gall, wo, wo_at, att, qs, ks, vt, turned, hold, work, low, part, m_tail, part_tail,
        sbuf, rbuf, xsend, xrecv, acc, thin, send_sem, recv_sem,
    ):
        dp, fs = lax.axis_index("dp"), lax.axis_index("fsdp")
        net = Net(send_sem, recv_sem)

        def own(buf):
            return buf.at[pl.ds(pl.multiple_of(dp * rw, 16), rw), :]

        def of(buf, step):
            return buf.at[pl.ds(pl.multiple_of(flip(dp, step) * rw, 16), rw), :]

        for b in range(2):
            for t in range(3):
                st_q[b, t] = q_in[b, :, t * hd : (t + 1) * hd].astype(BF)
        here = pl.ds(pl.multiple_of(dp * rw, 16), rw)
        wide_gain = jnp.concatenate([g_in[...], jnp.zeros((LANES - 4, rw), F32)], axis=0).T
        gall[here, :] = wide_gain.astype(BF)
        wo[0, here, :] = o_in[0].astype(BF)
        wi[here, :] = i_in[0].astype(BF)
        wd[here, :] = d_in[0].astype(BF)
        wp[0, here, :] = p_in[...].astype(BF)
        wu[here, :] = u_in[...].astype(BF)

        barrier = pltpu.get_barrier_semaphore()
        for m in range(z_count):
            for e in range(fs_count):
                if m or e:
                    there = (flip(dp, m * y_count), flip(fs, e))
                    pl.semaphore_signal(barrier, inc=1, device_id=there, device_id_type=MESH)
        for j in range(1, y_count):
            pl.semaphore_signal(barrier, inc=1, device_id=(flip(dp, j), fs), device_id_type=MESH)
        pl.semaphore_wait(barrier, z_count * fs_count - 1 + y_count - 1)

        def along_z(bufs):
            found = [[] for _ in range(z_count)]
            for m in range(1, z_count):
                for buf in bufs:
                    found[m].append(net.start(own(buf), own(buf), (flip(dp, m * y_count), fs)))
            return found

        def along_y(bufs, m):
            return [
                net.start(of(buf, m * y_count), of(buf, m * y_count), (flip(dp, j), fs))
                for j in range(1, y_count)
                for buf in bufs
            ]

        def wait_all(copies):
            for copy in copies:
                copy.wait_recv()

        def heads_along_z(b, wq):
            found = []
            for m in range(z_count):
                line = []
                for t in range(3):
                    place = 3 * fs + t
                    kind, to = lax.div(place, fs_count), lax.rem(place, fs_count)
                    copy = net.make(st_q.at[b, t], wq.at[kind, here, :], (flip(dp, m * y_count), to))
                    if m == 0:

                        @pl.when(to != fs)
                        def _():
                            copy.start()

                        @pl.when(to == fs)
                        def _():
                            wq[kind, here, :] = st_q[b, t]

                        line.append((copy, to != fs))
                    else:
                        copy.start()
                        net.open.append(copy)
                        line.append((copy, None))
                found.append(line)
            return found

        def heads_along_y(wq, line, m):
            for copy, when in line:
                if when is None:
                    copy.wait_recv()
                else:

                    @pl.when(when)
                    def _():
                        copy.wait_recv()
                        copy.wait_send()

            at = pl.ds(pl.multiple_of(flip(dp, m * y_count) * rw, 16), rw)
            return [
                net.start(wq.at[:, at, :], wq.at[:, at, :], (flip(dp, j), fs)) for j in range(1, y_count)
            ]


        def spread(pieces, src):
            return Flight(net, dp, fs, fs_count, pieces, src)

        heads0 = heads_along_z(0, wq0)
        gz = along_z([gall])
        y0 = along_y([gall], 0)
        tk = spread(toks, tok)
        toks[0] = tok[...]
        zs = {}
        zs["wo"] = along_z([wo.at[0]])
        zs["wi"] = along_z([wi])
        ys = {"wo": along_y([wo.at[0]], 0), "wi": along_y([wi], 0)}
        spread_write(thin.at[:, 0:rows, :], cot_ref[...].astype(F32))
        lifted = jnp.concatenate([strided_read(thin, n, short) for n in range(3)], axis=1).astype(BF)
        for e in range(fs_count):
            c_own[e] = lifted[:, e * pc : (e + 1) * pc]
        c_rel[0] = c_own[fs]
        c_f = [
            net.start(c_own.at[flip(fs, e)], c_rel.at[e], (dp, flip(fs, e))) for e in range(1, fs_count)
        ]
        lane_first, lane_end, lane = doc_bounds(triples_ref, docs)
        for m in range(z_count):
            y0 += heads_along_y(wq0, heads0[m], m)
            if m:
                wait_all(gz[m])
                y0 += along_y([gall], m)
        zs["wp"] = along_z([wp.at[0]])
        zs["wd"] = along_z([wd])
        ys["wp"] = along_y([wp.at[0]], 0)
        ys["wd"] = along_y([wd], 0)

        def pass_on(name, bufs):
            for m in range(1, z_count):
                wait_all(zs[name][m])
                ys[name] += along_y(bufs, m)

        pass_on("wo", [wo.at[0]])
        tk.relay()
        heads1 = heads_along_z(1, wq1)
        zs["wu"] = along_z([wu])
        wait_all(y0)
        gain_rows = gall[...].astype(F32).T[0:8, :]
        gain_out[...] = gain_rows
        for t in range(3):
            wq_out[:, t * hd : (t + 1) * hd] = wq0[t]
        for e in range(fs_count):
            tk.ready(e)
            base = pl.multiple_of(flip(fs, e) * rows, 16)
            for r in range(0, rows, LANES):
                block = toks[e, r : r + LANES, :].astype(F32)
                n1[pl.ds(base + r, LANES), :] = layer_norm(block, gain_rows[0:1]).astype(BF)
            at = pl.ds(base, rows)
            got = dot_nn(n1[at, :], wq_out[...])
            q, k, v = got[:, :hd], got[:, hd : 2 * hd], got[:, 2 * hd :]
            q = (q * cos_ref[at, :] + partner(q) * sin_ref[at, :]).astype(BF)
            k = (k * cos_ref[at, :] + partner(k) * sin_ref[at, :]).astype(BF)
            qkv[at, 0:hd] = q
            qkv[at, hd : 2 * hd] = k
            qkv[at, 2 * hd : 3 * hd] = v.astype(BF)
            row = lax.broadcasted_iota(jnp.int32, (rows, LANES), 0) + base
            inside = (row >= 3 * lane_first) & (row < 3 * lane_end)
            fk = jnp.where(inside, 1.0, 0.0)
            fq = jnp.where(inside | (lane >= docs), 0.0, MASKED)
            head_inputs(qs, ks, at, q.astype(F32), k.astype(F32), fq, fk, heads)
        for r in range(0, total, blk):
            at = slice(r, r + blk)
            vt[:, at] = qkv[at, 2 * hd : 3 * hd].astype(F32).T.astype(BF)
        stores = [net.local(n1, n1_hbm)]
        stores.append(net.local(qkv, qkv_hbm))

        flights = []
        for n, r in enumerate(range(0, total, blk)):
            stop = r + blk
            found = []
            for h in range(heads):
                e, inv = softmax_block(ks, qs, h, r, stop)
                found.append(dot_nn(vt[h * HEAD : (h + 1) * HEAD, 0:stop], e.astype(BF)) * inv)
            att[0, r:stop, :] = jnp.concatenate(found, axis=0).T.astype(BF)
            flights.append(spread(att.at[:, r:stop, :], att.at[0, r:stop, :]))
            if n == 0:
                wait_all(ys["wo"])
                wo_f = spread(wo, wo.at[0])
            if n == 1:
                pass_on("wi", [wi])
            if n == 3:
                pass_on("wp", [wp.at[0]])
                wo_f.relay()
            if n == 5:
                pass_on("wd", [wd])
                ys["wu"] = along_y([wu], 0)
            if n >= 2:
                flights[n - 2].relay()
        for flight in flights[-2:]:
            flight.relay()
        wait_all(ys["wp"])
        wp_f = spread(wp, wp.at[0])
        ys["heads1"] = []
        for m in range(z_count):
            ys["heads1"] += heads_along_y(wq1, heads1[m], m)
        wo_f.all_ready()
        for e in range(fs_count):
            wo_at[flip(fs, e)] = wo[e]
        for e in range(fs_count):
            hold[:, e * hd : (e + 1) * hd] = wo_at[e]
        for e in range(fs_count):
            base = pl.multiple_of(flip(fs, e) * hd, 16)
            turned[e * hd : (e + 1) * hd, :] = hold[pl.ds(base, hd), :]
        wo_own[...] = turned[0:hd, :]
        for flight in flights:
            flight.all_ready()
        wait_all(ys["wi"])
        wait_all(ys["wd"])

        def mix(x_block, o_block, amount, keep_mid, keep_n2, out):
            work[0:amount, 0:width] = x_block.astype(F32) + dot_nn(o_block, turned[...])
            for r in range(0, amount, HEAD):
                m = work[r : r + HEAD, 0:width]
                if keep_mid is not None:
                    keep_mid[r : r + HEAD, :] = m
                value = layer_norm(m, gain_rows[1:2]).astype(BF)
                low[r : r + HEAD, 0:width] = value
                if keep_n2 is not None:
                    keep_n2[r : r + HEAD, :] = value
            work[0:amount, 0:fj] = dot_nn(low[0:amount, 0:width], wi[...])
            for r in range(0, amount, HEAD):
                low[r : r + HEAD, 0:fj] = gelu(work[r : r + HEAD, 0:fj]).astype(BF)
            out[0:amount, :] = dot_nt(low[0:amount, 0:fj], wd[...])

        for e in range(fs_count):
            at = pl.ds(pl.multiple_of(flip(fs, e) * rows + rows - HALO, 16), HALO)
            for k in range(fs_count):
                att_rel[e * HALO : (e + 1) * HALO, k * hd : (k + 1) * hd] = att[k, at, :]
        tails = jnp.concatenate([toks[e, rows - HALO : rows, :] for e in range(fs_count)], axis=0)
        mix(tails, att_rel[0 : fs_count * HALO, :], fs_count * HALO, m_tail, None, part_tail)

        for e in range(fs_count):
            base = pl.multiple_of(flip(fs, e) * rows, 16)
            for k in range(fs_count):
                att_rel[pl.ds(base, rows), k * hd : (k + 1) * hd] = att[k, pl.ds(base, rows), :]

        def before(e):
            place = flip(fs, e) + fs_count - 1
            place = lax.rem(place, fs_count)
            apart = jnp.int32(0)
            bit = 1
            while bit < fs_count:
                one = lax.rem(lax.div(place, bit), 2)
                two = lax.rem(lax.div(fs, bit), 2)
                apart = apart + bit * lax.rem(one + two, 2)
                bit *= 2
            return pl.multiple_of(apart * HALO, 16)

        def partial_for(e, out):
            base = pl.multiple_of(flip(fs, e) * rows, 16)
            mix(
                toks[e],
                att_rel[pl.ds(base, rows), :],
                rows,
                mid if e == 0 else None,
                n2.at[e * rows : (e + 1) * rows, :],
                part,
            )
            out[0:HALO, :] = part_tail[pl.ds(before(e), HALO), :].astype(out.dtype)
            out[HALO:long_rows, :] = part[0:rows, :].astype(out.dtype)

        stores.append(net.local(att_rel, att_hbm))
        half = fs_count // 2
        first_hops = {}
        for j in reversed(range(half)):
            partial_for(2 * j + 1, sbuf.at[j])
            first_hops[j] = net.start(sbuf.at[j], rbuf.at[j], (dp, flip(fs, 1)))
            if j == half - 1:
                pass_on("wu", [wu])
            if j:
                partial_for(2 * j, acc.at[j])
                first_hops[j].wait_recv()
                acc[j] = acc[j] + rbuf[j].astype(F32)
                if half == 2:
                    xsend[0] = acc[1].astype(BF)
                    last_hop = net.start(xsend.at[0], xrecv.at[0], (dp, flip(fs, 2)))
            if j == half - 1:
                wp_f.relay()
        partial_for(0, acc.at[0])
        first_hops[0].wait_recv()
        acc[0] = acc[0] + rbuf[0].astype(F32)
        if half > 2:
            bit, active = 2, list(range(half))
            slot = 0
            while bit < fs_count:
                stay = [j for j in active if not (2 * j) & bit]
                hops = {}
                for j in stay:
                    give = j + bit // 2
                    xsend[slot] = acc[give].astype(BF)
                    hops[j] = (net.start(xsend.at[slot], xrecv.at[slot], (dp, flip(fs, bit))), slot)
                    slot += 1
                for j in stay:
                    hops[j][0].wait_recv()
                    acc[j] = acc[j] + xrecv[hops[j][1]].astype(F32)
                active, bit = stay, bit * 2
        elif half == 2:
            last_hop.wait_recv()
            acc[0] = acc[0] + xrecv[0].astype(F32)
        a_tail = acc[0, 0:HALO, :] + m_tail[pl.ds(before(0), HALO), :]
        a_own = acc[0, HALO:long_rows, :] + mid[...]
        after[...] = a_own
        for c in range(width // LANES):
            thin[c, 0:HALO, :] = a_tail[:, c * LANES : (c + 1) * LANES]
            thin[c, HALO:long_rows, :] = a_own[:, c * LANES : (c + 1) * LANES]

        stores.append(net.local(n2, n2_hbm))

        row = lax.broadcasted_iota(jnp.int32, (short, LANES), 0) + fs * short
        begins = jnp.max(jnp.where(row == lane_first, 1.0, 0.0), axis=1, keepdims=True)
        parts = []
        for k in range(3):
            value = strided_read(thin, HALO - 2 + k, short)
            parts.append(jnp.where(begins > 0.0, 0.0, value) if k < 2 else value)
        z = jnp.concatenate(parts, axis=1).astype(BF)
        for e in range(fs_count):
            z_out[e] = z[:, e * pc : (e + 1) * pc]
        pooled = jnp.zeros((short, width), F32)
        for e in range(fs_count):
            wp_f.ready(e)
            pooled = pooled + dot_nt(z_out[flip(fs, e)], wp[e])
        s0_out[...] = pooled
        for name in ("heads1", "wu"):
            wait_all(ys[name])
        wait_all(c_f)
        for t in range(3):
            wq1_out[:, t * hd : (t + 1) * hd] = wq1[t]
        for copy in stores:
            copy.wait()
        net.finish()

    half = fs_count // 2
    outs = [
        ((total, width), BF),
        ((total, 3 * hd), BF),
        ((total, width), BF),
        ((hd, width), BF),
        ((total, width), BF),
        ((rows, width), F32),
        ((rows, width), F32),
        ((fs_count, short, pc), BF),
        ((short, width), F32),
        ((width, 3 * hd), BF),
        ((width, fj), BF),
        ((width, fj), BF),
        ((fs_count, width, pc), BF),
        ((width, 3 * hd), BF),
        ((width, pc), BF),
        ((fs_count, short, pc), BF),
        ((8, width), F32),
    ]
    wide = max(width, fj)
    scratch = [
        ((total, width), BF),
        ((total, 3 * hd), BF),
        ((total, width), BF),
        ((total, width), BF),
        ((fs_count, rows, width), BF),
        ((fs_count, short, pc), BF),
        ((2, 3, rw, hd), BF),
        ((3, width, hd), BF),
        ((3, width, hd), BF),
        ((width, LANES), BF),
        ((fs_count, width, hd), BF),
        ((fs_count, width, hd), BF),
        ((fs_count, total, hd), BF),
        ((heads, total, LANES), BF),
        ((heads, total, LANES), BF),
        ((hd, total), BF),
        ((width, width), BF),
        ((width, width), BF),
        ((rows, wide), F32),
        ((rows, wide), BF),
        ((rows, width), F32),
        ((fs_count * HALO, width), F32),
        ((fs_count * HALO, width), F32),
        ((half, long_rows, width), BF),
        ((half, long_rows, width), BF),
        ((half - 1, long_rows, width), BF),
        ((half - 1, long_rows, width), BF),
        ((half, long_rows, width), F32),
        ((width // LANES, long_rows, LANES), F32),
    ]
    return pl.pallas_call(
        body,
        out_shape=[jax.ShapeDtypeStruct(s, t) for s, t in outs],
        in_specs=[vmem(), vmem(), smem()] + [vmem()] * 9,
        out_specs=[hbm() if n in (0, 1, 2, 4) else vmem() for n in range(len(outs))],
        scratch_shapes=[pltpu.VMEM(s, t) for s, t in scratch] + [pltpu.SemaphoreType.DMA((sems,))] * 2,
        compiler_params=pltpu.CompilerParams(collective_id=3, has_side_effects=True, vmem_limit_bytes=VMEM_BYTES),
        cost_estimate=cost(2e10, 3e7),
        name="forward_one",
    )(tokens, cot, triples, *weights, gains_t, cos, sin)


def forward_all(y_count, dp_count, fs_count, tokens, cot, triples, weights, gains_t, cos, sin):
    rows, width = tokens.shape
    total, short = rows * fs_count, rows // 3
    long_rows = rows + HALO
    wqkv, wout, win, wdown, wpool, wup = weights
    rw = wqkv.shape[1]
    hd, fj, pc = wout.shape[2], win.shape[2], wpool.shape[1]
    heads = hd // HEAD
    docs = triples.shape[1]
    z_count = dp_count // y_count
    blk = query_rows(total)
    total_b = short * fs_count
    blk_b = min(QB, total_b)
    blocks_b, half = total_b // blk_b, fs_count // 2
    cb = 4 * hd + 2 * pc
    sems = 192 + 22 * dp_count + 16 * fs_count

    def body(
        tok, cot_ref, triples_ref, q_in, o_in, i_in, d_in, p_in, u_in, g_in, cos_ref, sin_ref,
        n1_hbm, qkv_hbm, att_hbm, n2_hbm, wo_own, mid, wq_out, wi, wd, gain_out, out, da, dfs_out, group, sum_ff, dgain,
        after, z_out, s0_out, wp, wq1_out, wu, c_rel,
        n1, qkv, att_rel, n2, toks, c_own, st_q, wq0, wq1, gall, wo, wo_at, att, qs, ks, vt, turned, hold, work, low, part, m_tail, part_tail, sbuf, rbuf, xsend, xrecv, acc, thin,
        b_wos, b_wi_ref, b_wd_ref, b_g_ff, b_yg, b_zsg, b_zrg, b_sd, b_rd, b_xd, b_yd, b_ad, b_lift_send, b_lift_rel, b_s0s, b_x_all, b_wo_at, b_hold, b_turned, b_z_rel, b_dfs, b_df_all, b_das, b_cols, b_s1s, b_ds0s, b_nxt, b_n1, b_n2, b_qkv, b_att, b_att_rel, b_qs, b_ks, b_vt, b_kt, b_dk, b_dv, b_dqkv, b_work, b_hid, b_slope, b_dpre, b_m_all, b_dm, b_sf, b_rf, b_xf, b_yf, b_af, b_sb, b_rb, b_xb, b_yb, b_ab, b_sa, b_ra, b_xa, b_ya, b_aa, b_thin, b_spread_rows, b_lift,
        send_sem, recv_sem, *ps,
    ):
        dp, fs = lax.axis_index("dp"), lax.axis_index("fsdp")
        net = Net(send_sem, recv_sem)

        def own(buf):
            return buf.at[pl.ds(pl.multiple_of(dp * rw, 16), rw), :]

        def of(buf, step):
            return buf.at[pl.ds(pl.multiple_of(flip(dp, step) * rw, 16), rw), :]

        for b in range(2):
            for t in range(3):
                st_q[b, t] = q_in[b, :, t * hd : (t + 1) * hd].astype(BF)
        here = pl.ds(pl.multiple_of(dp * rw, 16), rw)
        wide_gain = jnp.concatenate([g_in[...], jnp.zeros((LANES - 4, rw), F32)], axis=0).T
        gall[here, :] = wide_gain.astype(BF)
        wo[0, here, :] = o_in[0].astype(BF)
        wi[here, :] = i_in[0].astype(BF)
        wd[here, :] = d_in[0].astype(BF)
        wp[0, here, :] = p_in[...].astype(BF)
        wu[here, :] = u_in[...].astype(BF)
        b_wos[0, here, :] = o_in[1].astype(BF)
        b_wi_ref[here, :] = i_in[1].astype(BF)
        b_wd_ref[here, :] = d_in[1].astype(BF)

        barrier = pltpu.get_barrier_semaphore()
        for m in range(z_count):
            for e in range(fs_count):
                if m or e:
                    there = (flip(dp, m * y_count), flip(fs, e))
                    pl.semaphore_signal(barrier, inc=1, device_id=there, device_id_type=MESH)
        for j in range(1, y_count):
            pl.semaphore_signal(barrier, inc=1, device_id=(flip(dp, j), fs), device_id_type=MESH)
        pl.semaphore_wait(barrier, z_count * fs_count - 1 + y_count - 1)

        def along_z(bufs):
            found = [[] for _ in range(z_count)]
            for m in range(1, z_count):
                for buf in bufs:
                    found[m].append(net.start(own(buf), own(buf), (flip(dp, m * y_count), fs)))
            return found

        def along_y(bufs, m):
            return [
                net.start(of(buf, m * y_count), of(buf, m * y_count), (flip(dp, j), fs))
                for j in range(1, y_count)
                for buf in bufs
            ]

        def wait_all(copies):
            for copy in copies:
                copy.wait_recv()

        def heads_along_z(b, wq):
            found = []
            for m in range(z_count):
                line = []
                for t in range(3):
                    place = 3 * fs + t
                    kind, to = lax.div(place, fs_count), lax.rem(place, fs_count)
                    copy = net.make(st_q.at[b, t], wq.at[kind, here, :], (flip(dp, m * y_count), to))
                    if m == 0:

                        @pl.when(to != fs)
                        def _():
                            copy.start()

                        @pl.when(to == fs)
                        def _():
                            wq[kind, here, :] = st_q[b, t]

                        line.append((copy, to != fs))
                    else:
                        copy.start()
                        net.open.append(copy)
                        line.append((copy, None))
                found.append(line)
            return found

        def heads_along_y(wq, line, m):
            for copy, when in line:
                if when is None:
                    copy.wait_recv()
                else:

                    @pl.when(when)
                    def _():
                        copy.wait_recv()
                        copy.wait_send()

            at = pl.ds(pl.multiple_of(flip(dp, m * y_count) * rw, 16), rw)
            return [
                net.start(wq.at[:, at, :], wq.at[:, at, :], (flip(dp, j), fs)) for j in range(1, y_count)
            ]


        def spread(pieces, src):
            return Flight(net, dp, fs, fs_count, pieces, src)

        heads0 = heads_along_z(0, wq0)
        gz = along_z([gall])
        y0 = along_y([gall], 0)
        tk = spread(toks, tok)
        toks[0] = tok[...]
        zs = {}
        zs["wo"] = along_z([wo.at[0]])
        zs["wi"] = along_z([wi])
        ys = {"wo": along_y([wo.at[0]], 0), "wi": along_y([wi], 0)}
        spread_write(thin.at[:, 0:rows, :], cot_ref[...].astype(F32))
        lifted = jnp.concatenate([strided_read(thin, n, short) for n in range(3)], axis=1).astype(BF)
        for e in range(fs_count):
            c_own[e] = lifted[:, e * pc : (e + 1) * pc]
        c_rel[0] = c_own[fs]
        c_f = [
            net.start(c_own.at[flip(fs, e)], c_rel.at[e], (dp, flip(fs, e))) for e in range(1, fs_count)
        ]
        lane_first, lane_end, lane = doc_bounds(triples_ref, docs)
        for m in range(z_count):
            y0 += heads_along_y(wq0, heads0[m], m)
            if m:
                wait_all(gz[m])
                y0 += along_y([gall], m)
        zs["wp"] = along_z([wp.at[0]])
        zs["wd"] = along_z([wd])
        ys["wp"] = along_y([wp.at[0]], 0)
        ys["wd"] = along_y([wd], 0)

        def pass_on(name, bufs):
            for m in range(1, z_count):
                wait_all(zs[name][m])
                ys[name] += along_y(bufs, m)

        pass_on("wo", [wo.at[0]])
        tk.relay()
        heads1 = heads_along_z(1, wq1)
        zs["wu"] = along_z([wu])
        later = (b_wos.at[0], b_wi_ref, b_wd_ref)
        came = [[line[0] for line in along_z([buf])[1:]] for buf in later]
        wait_all(y0)
        gain_rows = gall[...].astype(F32).T[0:8, :]
        gain_out[...] = gain_rows
        for t in range(3):
            wq_out[:, t * hd : (t + 1) * hd] = wq0[t]
        for e in range(fs_count):
            tk.ready(e)
            base = pl.multiple_of(flip(fs, e) * rows, 16)
            for r in range(0, rows, LANES):
                block = toks[e, r : r + LANES, :].astype(F32)
                n1[pl.ds(base + r, LANES), :] = layer_norm(block, gain_rows[0:1]).astype(BF)
            at = pl.ds(base, rows)
            got = dot_nn(n1[at, :], wq_out[...])
            q, k, v = got[:, :hd], got[:, hd : 2 * hd], got[:, 2 * hd :]
            q = (q * cos_ref[at, :] + partner(q) * sin_ref[at, :]).astype(BF)
            k = (k * cos_ref[at, :] + partner(k) * sin_ref[at, :]).astype(BF)
            qkv[at, 0:hd] = q
            qkv[at, hd : 2 * hd] = k
            qkv[at, 2 * hd : 3 * hd] = v.astype(BF)
            row = lax.broadcasted_iota(jnp.int32, (rows, LANES), 0) + base
            inside = (row >= 3 * lane_first) & (row < 3 * lane_end)
            fk = jnp.where(inside, 1.0, 0.0)
            fq = jnp.where(inside | (lane >= docs), 0.0, MASKED)
            head_inputs(qs, ks, at, q.astype(F32), k.astype(F32), fq, fk, heads)
        for r in range(0, total, blk):
            at = slice(r, r + blk)
            vt[:, at] = qkv[at, 2 * hd : 3 * hd].astype(F32).T.astype(BF)
        stores = [net.local(n1, n1_hbm)]
        stores.append(net.local(qkv, qkv_hbm))

        flights = []
        for n, r in enumerate(range(0, total, blk)):
            stop = r + blk
            found = []
            for h in range(heads):
                e, inv = softmax_block(ks, qs, h, r, stop)
                found.append(dot_nn(vt[h * HEAD : (h + 1) * HEAD, 0:stop], e.astype(BF)) * inv)
            att[0, r:stop, :] = jnp.concatenate(found, axis=0).T.astype(BF)
            flights.append(spread(att.at[:, r:stop, :], att.at[0, r:stop, :]))
            if n == 0:
                wait_all(ys["wo"])
                wo_f = spread(wo, wo.at[0])
            if n == 1:
                pass_on("wi", [wi])
            if n == 3:
                pass_on("wp", [wp.at[0]])
                wo_f.relay()
            if n == 5:
                pass_on("wd", [wd])
                ys["wu"] = along_y([wu], 0)
                passed = [along_y([buf], 0) for buf in later]
            if n >= 2:
                flights[n - 2].relay()
        for flight in flights[-2:]:
            flight.relay()
        wait_all(ys["wp"])
        wp_f = spread(wp, wp.at[0])
        ys["heads1"] = []
        for m in range(z_count):
            ys["heads1"] += heads_along_y(wq1, heads1[m], m)
        wo_f.all_ready()
        for e in range(fs_count):
            wo_at[flip(fs, e)] = wo[e]
        for e in range(fs_count):
            hold[:, e * hd : (e + 1) * hd] = wo_at[e]
        for e in range(fs_count):
            base = pl.multiple_of(flip(fs, e) * hd, 16)
            turned[e * hd : (e + 1) * hd, :] = hold[pl.ds(base, hd), :]
        wo_own[...] = turned[0:hd, :]
        for flight in flights:
            flight.all_ready()
        wait_all(ys["wi"])
        wait_all(ys["wd"])

        def mix(x_block, o_block, amount, keep_mid, keep_n2, out):
            work[0:amount, 0:width] = x_block.astype(F32) + dot_nn(o_block, turned[...])
            for r in range(0, amount, HEAD):
                m = work[r : r + HEAD, 0:width]
                if keep_mid is not None:
                    keep_mid[r : r + HEAD, :] = m
                value = layer_norm(m, gain_rows[1:2]).astype(BF)
                low[r : r + HEAD, 0:width] = value
                if keep_n2 is not None:
                    keep_n2[r : r + HEAD, :] = value
            work[0:amount, 0:fj] = dot_nn(low[0:amount, 0:width], wi[...])
            for r in range(0, amount, HEAD):
                low[r : r + HEAD, 0:fj] = gelu(work[r : r + HEAD, 0:fj]).astype(BF)
            out[0:amount, :] = dot_nt(low[0:amount, 0:fj], wd[...])

        for e in range(fs_count):
            at = pl.ds(pl.multiple_of(flip(fs, e) * rows + rows - HALO, 16), HALO)
            for k in range(fs_count):
                att_rel[e * HALO : (e + 1) * HALO, k * hd : (k + 1) * hd] = att[k, at, :]
        tails = jnp.concatenate([toks[e, rows - HALO : rows, :] for e in range(fs_count)], axis=0)
        mix(tails, att_rel[0 : fs_count * HALO, :], fs_count * HALO, m_tail, None, part_tail)

        for e in range(fs_count):
            base = pl.multiple_of(flip(fs, e) * rows, 16)
            for k in range(fs_count):
                att_rel[pl.ds(base, rows), k * hd : (k + 1) * hd] = att[k, pl.ds(base, rows), :]

        def before(e):
            place = flip(fs, e) + fs_count - 1
            place = lax.rem(place, fs_count)
            apart = jnp.int32(0)
            bit = 1
            while bit < fs_count:
                one = lax.rem(lax.div(place, bit), 2)
                two = lax.rem(lax.div(fs, bit), 2)
                apart = apart + bit * lax.rem(one + two, 2)
                bit *= 2
            return pl.multiple_of(apart * HALO, 16)

        def partial_for(e, out):
            base = pl.multiple_of(flip(fs, e) * rows, 16)
            mix(
                toks[e],
                att_rel[pl.ds(base, rows), :],
                rows,
                mid if e == 0 else None,
                n2.at[e * rows : (e + 1) * rows, :],
                part,
            )
            out[0:HALO, :] = part_tail[pl.ds(before(e), HALO), :].astype(out.dtype)
            out[HALO:long_rows, :] = part[0:rows, :].astype(out.dtype)

        stores.append(net.local(att_rel, att_hbm))
        first_hops = {}
        for j in reversed(range(half)):
            partial_for(2 * j + 1, sbuf.at[j])
            first_hops[j] = net.start(sbuf.at[j], rbuf.at[j], (dp, flip(fs, 1)))
            if j == half - 1:
                pass_on("wu", [wu])
            if j:
                partial_for(2 * j, acc.at[j])
                first_hops[j].wait_recv()
                acc[j] = acc[j] + rbuf[j].astype(F32)
                if half == 2:
                    xsend[0] = acc[1].astype(BF)
                    last_hop = net.start(xsend.at[0], xrecv.at[0], (dp, flip(fs, 2)))
            if j == half - 1:
                wp_f.relay()
        partial_for(0, acc.at[0])
        first_hops[0].wait_recv()
        acc[0] = acc[0] + rbuf[0].astype(F32)
        if half > 2:
            bit, active = 2, list(range(half))
            slot = 0
            while bit < fs_count:
                stay = [j for j in active if not (2 * j) & bit]
                hops = {}
                for j in stay:
                    give = j + bit // 2
                    xsend[slot] = acc[give].astype(BF)
                    hops[j] = (net.start(xsend.at[slot], xrecv.at[slot], (dp, flip(fs, bit))), slot)
                    slot += 1
                for j in stay:
                    hops[j][0].wait_recv()
                    acc[j] = acc[j] + xrecv[hops[j][1]].astype(F32)
                active, bit = stay, bit * 2
        elif half == 2:
            last_hop.wait_recv()
            acc[0] = acc[0] + xrecv[0].astype(F32)
        a_tail = acc[0, 0:HALO, :] + m_tail[pl.ds(before(0), HALO), :]
        a_own = acc[0, HALO:long_rows, :] + mid[...]
        after[...] = a_own
        for c in range(width // LANES):
            thin[c, 0:HALO, :] = a_tail[:, c * LANES : (c + 1) * LANES]
            thin[c, HALO:long_rows, :] = a_own[:, c * LANES : (c + 1) * LANES]

        stores.append(net.local(n2, n2_hbm))

        row = lax.broadcasted_iota(jnp.int32, (short, LANES), 0) + fs * short
        begins = jnp.max(jnp.where(row == lane_first, 1.0, 0.0), axis=1, keepdims=True)
        parts = []
        for k in range(3):
            value = strided_read(thin, HALO - 2 + k, short)
            parts.append(jnp.where(begins > 0.0, 0.0, value) if k < 2 else value)
        z = jnp.concatenate(parts, axis=1).astype(BF)
        for e in range(fs_count):
            z_out[e] = z[:, e * pc : (e + 1) * pc]
        pooled = jnp.zeros((short, width), F32)
        for e in range(fs_count):
            wp_f.ready(e)
            pooled = pooled + dot_nt(z_out[flip(fs, e)], wp[e])
        s0_out[...] = pooled
        for name in ("heads1", "wu"):
            wait_all(ys[name])
        wait_all(c_f)
        for t in range(3):
            wq1_out[:, t * hd : (t + 1) * hd] = wq1[t]
        (wos, wi_ref, wd_ref, g_ff, yg, zsg, zrg, sd, rd, xd, yd, ad, lift_send, lift_rel, s0s, x_all, wo_at, hold, turned, z_rel, dfs, df_all, das, cols, s1s, ds0s, nxt, n1, n2, qkv, att, att_rel, qs, ks, vt, kt, dk, dv, dqkv, work, hid, slope, dpre, m_all, dm, sf, rf, xf, yf, af, sb, rb, xb, yb, ab, sa, ra, xa, ya, aa, thin, spread_rows, lift) = (
            b_wos, b_wi_ref, b_wd_ref, b_g_ff, b_yg, b_zsg, b_zrg, b_sd, b_rd, b_xd, b_yd, b_ad, b_lift_send, b_lift_rel, b_s0s, b_x_all, b_wo_at, b_hold, b_turned, b_z_rel, b_dfs, b_df_all, b_das, b_cols, b_s1s, b_ds0s, b_nxt, b_n1, b_n2, b_qkv, b_att, b_att_rel, b_qs, b_ks, b_vt, b_kt, b_dk, b_dv, b_dqkv, b_work, b_hid, b_slope, b_dpre, b_m_all, b_dm, b_sf, b_rf, b_xf, b_yf, b_af, b_sb, b_rb, b_xb, b_yb, b_ab, b_sa, b_ra, b_xa, b_ya, b_aa, b_thin, b_spread_rows, b_lift
        )
        def base_of(e, amount):
            return pl.multiple_of(flip(fs, e) * amount, 16)

        def spread(pieces, src=None):
            return Flight(net, dp, fs, fs_count, pieces, pieces.at[0] if src is None else src)

        s0s[0] = s0_out[...].astype(BF)
        nxt[...] = jnp.zeros(nxt.shape, BF)
        here = pl.ds(pl.multiple_of(dp * rw, 16), rw)
        def of(buf, step):
            return buf.at[pl.ds(pl.multiple_of(flip(dp, step) * rw, 16), rw), :]

        def along_z(buf):
            return [
                net.start(of(buf, 0), of(buf, 0), (flip(dp, m * y_count), fs)) for m in range(1, z_count)
            ]

        def along_y(buf, m):
            return [
                net.start(of(buf, m * y_count), of(buf, m * y_count), (flip(dp, n), fs)) for n in range(1, y_count)
            ]

        def pass_on(buf, came, passed):
            for m in range(1, z_count):
                came[m - 1].wait_recv()
                passed += along_y(buf, m)

        def wait_all(copies):
            for copy in copies:
                copy.wait_recv()

        s0_f = spread(s0s)

        dsum = Scatter(net, dp, fs, fs_count, sd, rd, xd, yd, ad)
        for e in reversed(range(fs_count)):
            part = dot_nt(c_rel[e], wu[...])
            if e % 2:
                sd[e // 2] = part.astype(BF)
                dsum.send_odd(e // 2)
            else:
                ad[e // 2] = part

        def exchange(blocks_of, landed):
            found = []
            for e in range(1, fs_count):
                found.append(net.start(blocks_of.at[flip(fs, e)], landed.at[e], (dp, flip(fs, e))))
            landed[0] = blocks_of[fs]
            return found

        lane_first, lane_end, lane = doc_bounds(triples_ref, docs)
        for n in range(1, half):
            dsum.join(n)
        dsum.upper()
        s0_f.relay()
        pass_on(wos.at[0], came[0], passed[0])
        for e in range(fs_count):
            s0_f.ready(e)
            at = pl.ds(base_of(e, short), short)
            value = s0_out[...] if e == 0 else s0s[e].astype(F32)
            x_all[at, :] = value
            n1[at, :] = layer_norm(value, gain_out[2:3, :]).astype(BF)
        for r in range(0, total_b, blk_b):
            at = slice(r, r + blk_b)
            got = dot_nn(n1[at, :], wq1_out[...])
            q, k, v = got[:, :hd], got[:, hd : 2 * hd], got[:, 2 * hd :]
            q = (q * cos_ref[at, :] + partner(q) * sin_ref[at, :]).astype(BF)
            k = (k * cos_ref[at, :] + partner(k) * sin_ref[at, :]).astype(BF)
            qkv[at, 0:hd] = q
            qkv[at, hd : 2 * hd] = k
            qkv[at, 2 * hd : 3 * hd] = v.astype(BF)
            row = lax.broadcasted_iota(jnp.int32, (blk_b, LANES), 0) + r
            inside = (row >= lane_first) & (row < lane_end)
            fk = jnp.where(inside, 1.0, 0.0)
            fq = jnp.where(inside | (lane >= docs), 0.0, MASKED)
            head_inputs(qs, ks, at, q.astype(F32), k.astype(F32), fq, fk, heads)
            vt[:, at] = v.T.astype(BF)
            kt[:, at] = k.astype(F32).T.astype(BF)
            dk[at, :] = jnp.zeros((blk_b, LANES), F32)
            dv[at, :] = jnp.zeros((blk_b, LANES), F32)
        dsum.join(0)
        dsum.finish()
        dm[...] = ad[0]
        dfs[0] = ad[0].astype(BF)
        df_f = spread(dfs)
        wait_all(passed[0])
        wo_f = spread(wos, wos.at[0])
        flights = []
        for n in range(blocks_b):
            r, stop = n * blk_b, (n + 1) * blk_b
            found = []
            for h in range(heads):
                e, inv = softmax_block(ks, qs, h, r, stop)
                ps[n][h] = (e * inv).astype(BF)
                found.append(dot_nn(vt[h * HEAD : (h + 1) * HEAD, 0:stop], ps[n][h]))
            att[0, r:stop, :] = jnp.concatenate(found, axis=0).T.astype(BF)
            flights.append(spread(att.at[:, r:stop, :], att.at[0, r:stop, :]))
            if n == 0:
                pass_on(wi_ref, came[1], passed[1])
                df_f.relay()
                wo_f.relay()
        place_of = lax.broadcasted_iota(jnp.int32, (blk_b, LANES), 1) // HEAD
        for r in range(0, total_b, blk_b):
            at = slice(r, r + blk_b)
            q = widen(qkv[at, 0:hd].astype(F32))
            for h in range(heads):
                qs[h, at, :] = jnp.where(place_of == h, q, 0.0).astype(BF)

        pass_on(wd_ref, came[2], passed[2])
        wo_f.all_ready()
        for e in range(fs_count):
            wo_at[flip(fs, e)] = wos[e]
        for e in range(fs_count):
            hold[:, e * hd : (e + 1) * hd] = wo_at[e]
        for e in range(fs_count):
            turned[e * hd : (e + 1) * hd, :] = hold[pl.ds(base_of(e, hd), hd), :]
        for flight in flights:
            flight.relay()
        for flight in flights:
            flight.all_ready()
        for e in range(fs_count):
            att_rel[:, e * hd : (e + 1) * hd] = att[e]

        work[:, 0:width] = x_all[...] + dot_nn(att_rel[...], turned[...])
        for r in range(0, total_b, HEAD):
            m = work[r : r + HEAD, 0:width]
            m_all[r : r + HEAD, :] = m
            n2[r : r + HEAD, :] = layer_norm(m, gain_out[3:4, :]).astype(BF)
        wait_all(passed[1])
        work[:, 0:fj] = dot_nn(n2[...], wi_ref[...])
        for r in range(0, total_b, HEAD):
            value, rate = gelu_both(work[r : r + HEAD, 0:fj])
            hid[r : r + HEAD, :] = value.astype(BF)
            slope[r : r + HEAD, :] = rate
        wait_all(passed[2])
        work[:, 0:width] = dot_nt(hid[...], wd_ref[...])

        def give_out(scatter, source):
            for e in reversed(range(fs_count)):
                value = source[pl.ds(base_of(e, short), short), 0:width]
                if e % 2:
                    scatter.sbuf[e // 2] = value.astype(BF)
                    scatter.send_odd(e // 2)
                else:
                    scatter.acc[e // 2] = value

        fwd = Scatter(net, dp, fs, fs_count, sf, rf, xf, yf, af)
        give_out(fwd, work)
        for e in range(fs_count):
            df_f.ready(e)
            df_all[pl.ds(base_of(e, short), short), :] = dfs[e]
        work[:, 0:fj] = dot_nn(df_all[...], wd_ref[...])
        for r in range(0, total_b, HEAD):
            at = slice(r, r + HEAD)
            dpre[at, :] = (work[at, 0:fj] * slope[at, :]).astype(BF)
        work[:, 0:width] = dot_nt(dpre[...], wi_ref[...])
        bwd = Scatter(net, dp, fs, fs_count, sb, rb, xb, yb, ab)
        give_out(bwd, work)
        for j in range(1, half):
            bwd.join(j)
        bwd.upper()
        for j in range(1, half):
            fwd.join(j)
        fwd.upper()
        g_ff[:, 0:fj] = dot_tn(n2[...], dpre[...]).astype(BF)
        g_ff[:, fj : 2 * fj] = dot_tn(df_all[...], hid[...]).astype(BF)
        ff_rows = RowSum(net, (dp, fs, y_count, z_count, fs_count, rw), g_ff, yg, zsg, zrg, sum_ff)
        ff_rows.start()
        bwd.join(0)
        bwd.finish()
        m_own = m_all[pl.ds(base_of(0, short), short), :]
        dx, dg = layer_norm_back(m_own, gain_out[3:4, :], ab[0])
        dx = dx + dm[...]
        dm[...] = dx
        das[0] = dx.astype(BF)
        da_f = spread(das)
        gain_two = jnp.sum(dg, axis=0, keepdims=True)

        fwd.join(0)
        fwd.finish()
        s1s[0] = (m_own + af[0]).astype(BF)
        s1_f = spread(s1s)
        z_f = exchange(z_out, z_rel)
        da_f.relay()
        s1_f.relay()
        for e in range(fs_count):
            da_f.ready(e)
            at = pl.ds(base_of(e, short), short)
            do = widen(dot_nt(das[e], turned[0:hd, :]))
            lane_head = lax.broadcasted_iota(jnp.int32, (short, LANES), 1) // HEAD
            for h in range(heads):
                ks[h, at, :] = jnp.where(lane_head == h, do, 0.0).astype(BF)
            for k in range(fs_count):

                @pl.when(fs == k)
                def _():
                    cols[at, :] = das[e, :, k * hd : (k + 1) * hd]

        g_out = dot_tn(att_rel[...], cols[...]).astype(BF)
        for e in range(fs_count):
            group[pl.ds(base_of(e, hd), hd), cb - hd : cb] = g_out[e * hd : (e + 1) * hd, :]
        for n in range(blocks_b):
            r, stop = n * blk_b, (n + 1) * blk_b
            at = slice(r, stop)
            found = []
            add_k = add_v = None
            for h in range(heads):
                p = ps[n][h]
                grad = dot_nt(widen(qkv[0:stop, 2 * hd : 3 * hd]), ks[h, at, :])
                wide = p.astype(F32)
                inner = jnp.sum(wide * grad, axis=0, keepdims=True)
                dr = (wide * (grad - inner) * 0.125).astype(BF)
                part_v = dot_nn(p, ks[h, at, :])
                part_k = dot_nn(dr, qs[h, at, :])
                add_v = part_v if add_v is None else add_v + part_v
                add_k = part_k if add_k is None else add_k + part_k
                found.append(dot_nn(kt[h * HEAD : (h + 1) * HEAD, 0:stop], dr))
            dk[0:stop, :] += add_k
            dv[0:stop, :] += add_v
            dq = jnp.concatenate(found, axis=0).T
            dqkv[at, 0:hd] = (dq * cos_ref[at, :] - partner(dq) * sin_ref[at, :]).astype(BF)
        for r in range(0, total_b, blk_b):
            at = slice(r, r + blk_b)
            grad = dk[at, 0:hd]
            dqkv[at, hd : 2 * hd] = (grad * cos_ref[at, :] - partner(grad) * sin_ref[at, :]).astype(BF)
            dqkv[at, 2 * hd : 3 * hd] = dv[at, 0:hd].astype(BF)
        work[:, 0:width] = dot_nt(dqkv[...], wq1_out[...])
        first = Scatter(net, dp, fs, fs_count, sa, ra, xa, ya, aa)
        give_out(first, work)
        for j in range(1, half):
            first.join(j)
        first.upper()
        group[:, 0 : 3 * hd] = dot_tn(n1[...], dqkv[...]).astype(BF)
        s1_f.all_ready()
        lift_f = []
        for e in range(fs_count):
            part = dot_nn(s1s[e], wu[...]).astype(BF)
            if e:
                lift_send[e] = part
                lift_f.append(net.start(lift_send.at[e], lift_rel.at[e], (dp, flip(fs, e))))
            else:
                lift_rel[0] = part
        g_up = jnp.zeros((width, pc), F32)
        for e in range(fs_count):
            g_up = g_up + dot_tn(s1s[e], c_rel[e])
        group[:, 3 * hd + pc : 3 * hd + 2 * pc] = g_up.astype(BF)
        for m in range(1, z_count):
            ff_rows.service(m)
        first.join(0)
        first.finish()
        dx, dg = layer_norm_back(s0_out[...], gain_out[2:3, :], aa[0])
        ds0s[0] = (dx + dm[...]).astype(BF)
        gain_one = jnp.sum(dg, axis=0, keepdims=True)
        which = lax.broadcasted_iota(jnp.int32, (8, width), 0)
        dgain[...] = jnp.where(which == 0, gain_one, jnp.where(which == 1, gain_two, 0.0))

        hop = net.make(ds0s.at[0, 0:HALO, :], nxt, (dp, lax.rem(fs + fs_count - 1, fs_count)))

        @pl.when(fs > 0)
        def _():
            hop.start()

        ds0_f = spread(ds0s)
        row = lax.broadcasted_iota(jnp.int32, (short, LANES), 0) + fs * short + 1
        shut = jnp.max(jnp.where((row == lane_first) | (row >= total_b), 1.0, 0.0), axis=1, keepdims=True) > 0.0

        @pl.when(fs < fs_count - 1)
        def _():
            hop.wait_recv()

        grad = jnp.concatenate([ds0s[0], nxt[...]], axis=0)
        for e in range(fs_count):
            lift_at = dot_nn(grad, wp[e])
            spread_rows[flip(fs, e)] = lift_at
        dz = jnp.concatenate([spread_rows[e] for e in range(fs_count)], axis=1)
        strided_write(thin, 0, short, dz[0:short, 2 * width : 3 * width])
        for k in range(2):
            part = dz[1 : short + 1, k * width : (k + 1) * width]
            strided_write(thin, k + 1, short, jnp.where(shut, 0.0, part))
        value = cot_ref[...].astype(F32) + spread_read(thin)
        da[...] = value
        dfs_out[0] = value.astype(BF)
        out_f = spread(dfs_out)
        ff_rows.service(0)
        ds0_f.relay()
        for copy in z_f:
            copy.wait_recv()
        g_pool = jnp.zeros((width, pc), F32)
        for e in range(fs_count):
            ds0_f.ready(e)
            g_pool = g_pool + dot_tn(ds0s[e], z_rel[e])
        group[:, 3 * hd : 3 * hd + pc] = g_pool.astype(BF)

        wait_all(lift_f)
        for e in range(fs_count):
            lift[flip(fs, e)] = lift_rel[e].astype(F32)
        lifted = jnp.concatenate([lift[e] for e in range(fs_count)], axis=1)
        for n in range(3):
            strided_write(thin, n, short, lifted[:, n * width : (n + 1) * width])
        out[...] = (after[...] + spread_read(thin)).astype(BF)
        ff_rows.finish()
        out_f.relay()
        out_f.all_ready()

        @pl.when(fs > 0)
        def _():
            hop.wait_send()

        for copy in stores:
            copy.wait()
        net.finish()

    outs = [
        ((total, width), BF),
        ((total, 3 * hd), BF),
        ((total, width), BF),
        ((total, width), BF),
        ((hd, width), BF),
        ((rows, width), F32),
        ((width, 3 * hd), BF),
        ((width, fj), BF),
        ((width, fj), BF),
        ((8, width), F32),
        ((rows, width), BF),
        ((rows, width), F32),
        ((fs_count, rows, width), BF),
        ((width, cb), BF),
        ((rw, 2 * fj), F32),
        ((8, width), F32),
    ]
    wide = max(width, fj)
    pieces = (fs_count, short, width)
    scatter = [((half, short, width), BF)] * 2 + [((half - 1, short, width), BF)] * 2 + [((half, short, width), F32)]
    scratch = [
        ((rows, width), F32),
        ((fs_count, short, pc), BF),
        ((short, width), F32),
        ((fs_count, width, pc), BF),
        ((width, 3 * hd), BF),
        ((width, pc), BF),
        ((fs_count, short, pc), BF),
        ((total, width), BF),
        ((total, 3 * hd), BF),
        ((total, width), BF),
        ((total, width), BF),
        ((fs_count, rows, width), BF),
        ((fs_count, short, pc), BF),
        ((2, 3, rw, hd), BF),
        ((3, width, hd), BF),
        ((3, width, hd), BF),
        ((width, LANES), BF),
        ((fs_count, width, hd), BF),
        ((fs_count, width, hd), BF),
        ((fs_count, total, hd), BF),
        ((heads, total, LANES), BF),
        ((heads, total, LANES), BF),
        ((hd, total), BF),
        ((width, width), BF),
        ((width, width), BF),
        ((rows, wide), F32),
        ((rows, wide), BF),
        ((rows, width), F32),
        ((fs_count * HALO, width), F32),
        ((fs_count * HALO, width), F32),
        ((half, long_rows, width), BF),
        ((half, long_rows, width), BF),
        ((half - 1, long_rows, width), BF),
        ((half - 1, long_rows, width), BF),
        ((half, long_rows, width), F32),
        ((width // LANES, long_rows, LANES), F32),
        ((fs_count, width, hd), BF),
        ((width, fj), BF),
        ((width, fj), BF),
        ((width, 2 * fj), BF),
        ((y_count - 1, z_count, rw, 2 * fj), BF),
        ((z_count - 1, rw, 2 * fj), BF),
        ((z_count - 1, rw, 2 * fj), BF),
        *scatter,
        ((fs_count, short, pc), BF),
        ((fs_count, short, pc), BF),
        (pieces, BF),
        ((total_b, width), F32),
        ((fs_count, width, hd), BF),
        ((width, width), BF),
        ((width, width), BF),
        ((fs_count, short, pc), BF),
        (pieces, BF),
        ((total_b, width), BF),
        (pieces, BF),
        ((total_b, hd), BF),
        (pieces, BF),
        (pieces, BF),
        ((HALO, width), BF),
        ((total_b, width), BF),
        ((total_b, width), BF),
        ((total_b, 3 * hd), BF),
        ((fs_count, total_b, hd), BF),
        ((total_b, width), BF),
        ((heads, total_b, LANES), BF),
        ((heads, total_b, LANES), BF),
        ((hd, total_b), BF),
        ((hd, total_b), BF),
        ((total_b, LANES), F32),
        ((total_b, LANES), F32),
        ((total_b, 3 * hd), BF),
        ((total_b, wide), F32),
        ((total_b, fj), BF),
        ((total_b, fj), F32),
        ((total_b, fj), BF),
        ((total_b, width), F32),
        ((short, width), F32),
        *scatter,
        *scatter,
        *scatter,
        ((width // LANES, rows, LANES), F32),
        ((fs_count, short + HALO, pc), F32),
        ((fs_count, short, pc), F32),
    ]
    tail = [pltpu.VMEM((heads, (n + 1) * blk_b, blk_b), BF) for n in range(blocks_b)]
    return pl.pallas_call(
        body,
        out_shape=[jax.ShapeDtypeStruct(s, t) for s, t in outs],
        in_specs=[vmem(), vmem(), smem()] + [vmem()] * 9,
        out_specs=[hbm()] * 4 + [vmem()] * (len(outs) - 4),
        scratch_shapes=[pltpu.VMEM(s, t) for s, t in scratch] + [pltpu.SemaphoreType.DMA((sems,))] * 2 + tail,
        compiler_params=pltpu.CompilerParams(collective_id=3, has_side_effects=True, vmem_limit_bytes=VMEM_BYTES),
        cost_estimate=cost(4e10, 5e7),
        name="forward_all",
    )(tokens, cot, triples, *weights, gains_t, cos, sin)


class RowSum:
    def __init__(self, net, place, grad, ybuf, zsend, zrecv, total, q_send=None, q_recv=None, q_total=None):
        self.net, self.grad, self.ybuf = net, grad, ybuf
        self.zsend, self.zrecv, self.total = zsend, zrecv, total
        self.q_send, self.q_recv, self.q_total = q_send, q_recv, q_total
        self.dp, self.fs, self.y_count, self.z_count, self.fs_count, self.rw = place
        self.ys, self.zs, self.qs = {}, {}, []

    def rows_of(self, step):
        return pl.ds(pl.multiple_of(flip(self.dp, step) * self.rw, 16), self.rw)

    def start(self):
        for m in list(range(1, self.z_count)) + [0]:
            self.ys[m] = [
                self.net.start(
                    self.grad.at[self.rows_of(m * self.y_count + j), :],
                    self.ybuf.at[j - 1, m],
                    (flip(self.dp, j), self.fs),
                )
                for j in range(1, self.y_count)
            ]
        if self.q_send is not None:
            self.q_base = self.net.used
            self.net.used += 3 * self.z_count

    def owner(self, kind):
        place = kind * self.fs_count + self.fs
        return lax.div(place, 3), lax.rem(place, 3)

    def service(self, m):
        for copy in self.ys[m]:
            copy.wait_recv()
        got = self.grad[self.rows_of(m * self.y_count), :].astype(F32)
        for j in range(1, self.y_count):
            got = got + self.ybuf[j - 1, m].astype(F32)
        there = flip(self.dp, m * self.y_count)
        lo = 0
        if self.q_send is not None:
            hd = self.q_send.shape[3]
            lo = 3 * hd
            for kind in range(3):
                to, slot = self.owner(kind)
                self.q_send[m, kind] = got[:, kind * hd : (kind + 1) * hd].astype(BF)
                copy = pltpu.make_async_remote_copy(
                    src_ref=self.q_send.at[m, kind],
                    dst_ref=self.q_recv.at[m, slot],
                    send_sem=self.net.send.at[self.q_base + 3 * m + kind],
                    recv_sem=self.net.recv.at[self.q_base + 3 * m + slot],
                    device_id=(there, to),
                    device_id_type=MESH,
                )
                if m:
                    copy.start()
                    self.qs.append((copy, None))
                else:

                    @pl.when(to != self.fs)
                    def _():
                        copy.start()

                    @pl.when(to == self.fs)
                    def _():
                        self.q_recv[0, slot] = self.q_send[0, kind]

                    self.qs.append((copy, to != self.fs))
        width = self.total.shape[1]
        rest = got[:, lo : lo + width]
        if m:
            self.zsend[m - 1] = rest.astype(BF)
            self.zs[m] = self.net.start(self.zsend.at[m - 1], self.zrecv.at[m - 1], (there, self.fs))
        else:
            self.total[...] = rest

    def finish(self):
        rest = self.total[...]
        for m in range(1, self.z_count):
            self.zs[m].wait_recv()
            rest = rest + self.zrecv[m - 1].astype(F32)
        self.total[...] = rest
        if self.q_send is None:
            return
        for t in range(3):
            giver = lax.rem(3 * self.fs + t, self.fs_count)
            for m in range(self.z_count):
                landed = self.q_recv.at[m, t]
                wait = pltpu.make_async_copy(landed, landed, self.net.recv.at[self.q_base + 3 * m + t])
                if m:
                    wait.wait()
                else:

                    @pl.when(giver != self.fs)
                    def _():
                        wait.wait()

        for t in range(3):
            block = self.q_recv[0, t].astype(F32)
            for m in range(1, self.z_count):
                block = block + self.q_recv[m, t].astype(F32)
            self.q_total[t] = block
        for copy, when in self.qs:
            if when is None:
                copy.wait_send()
            else:

                @pl.when(when)
                def _():
                    copy.wait_send()


class Scatter:
    def __init__(self, net, dp, fs, fs_count, sbuf, rbuf, xsend, xrecv, acc):
        self.net, self.dp, self.fs, self.half = net, dp, fs, fs_count // 2
        self.sbuf, self.rbuf, self.xsend, self.xrecv, self.acc = sbuf, rbuf, xsend, xrecv, acc
        self.first, self.hops, self.slot = {}, {}, 0

    def send_odd(self, j):
        self.first[j] = self.net.start(self.sbuf.at[j], self.rbuf.at[j], (self.dp, flip(self.fs, 1)))

    def join(self, j):
        self.first[j].wait_recv()
        self.acc[j] = self.acc[j] + self.rbuf[j].astype(F32)

    def give(self, j):
        bit = (2 * j) & -(2 * j)
        slot = self.slot
        self.slot += 1
        self.xsend[slot] = self.acc[j].astype(BF)
        self.hops[j] = (self.net.start(self.xsend.at[slot], self.xrecv.at[slot], (self.dp, flip(self.fs, bit))), slot)

    def take(self, j):
        low = j & -j
        copy, slot = self.hops[j]
        copy.wait_recv()
        self.acc[j - low] = self.acc[j - low] + self.xrecv[slot].astype(F32)

    def sent(self):
        for copy in list(self.first.values()) + [copy for copy, _ in self.hops.values()]:
            copy.wait_send()
            self.net.open = [other for other in self.net.open if other is not copy]

    def upper(self):
        if self.half == 2:
            self.give(1)

    def finish(self):
        if self.half == 2:
            self.take(1)
            return
        bit = 1
        while bit < self.half:
            gives = [j for j in range(self.half) if j & bit and not j & (bit - 1)]
            for j in gives:
                self.give(j)
            for j in gives:
                self.take(j)
            bit *= 2


def query_rows(total):
    return QB if total <= 2048 else QB // 2


def backward_one(
    y_count, dp_count, fs_count, da, dfs, n2, wi, wd, mid, gain_rows, qkv, wo_own, wq, cos, sin, triples, n1, att_rel, tokens, group_b, dgain_b
):
    rows, width = tokens.shape
    total = rows * fs_count
    fj, hd = wi.shape[1], wq.shape[1] // 3
    heads, docs = hd // HEAD, triples.shape[1]
    z_count, rw = dp_count // y_count, width // dp_count
    cb = group_b.shape[1]
    blk, half = query_rows(total), fs_count // 2
    blocks = total // blk
    sems = 96 + 12 * dp_count

    def body(
        da_ref, dfs, n2_ref, wi_ref, wd_ref, mid_ref, gain_ref, qkv_hbm, wo_ref, wq_ref, cos_hbm, sin_hbm, triples_ref, n1_hbm, att_hbm, tok, gb, dgain_two,
        grad_in, dgain, sum_b, sum_ff, sum_o, sum_q,
        qkv_ref, cos_ref, sin_ref, n1_ref, att_ref, das, hid, slope, dpre, work, qs, ks, kt, dk, dv, dqkv, dm, cols, g_ff, g_at,
        sbuf, rbuf, xsend, xrecv, acc, yb, zsb, zrb, qsb, qrb, yf, zsf, zrf, ya, zsa, zra, qsa, qra, tiles, send_sem, recv_sem,
        *ps,
    ):
        dp, fs = lax.axis_index("dp"), lax.axis_index("fsdp")
        net = Net(send_sem, recv_sem)
        place = (dp, fs, y_count, z_count, fs_count, rw)
        loads = {}
        for name, src, dst in (
            ("qkv", qkv_hbm, qkv_ref),
            ("att", att_hbm, att_ref),
            ("cos", cos_hbm, cos_ref),
            ("sin", sin_hbm, sin_ref),
            ("n1", n1_hbm, n1_ref),
        ):
            loads[name] = net.local(src, dst)
        barrier = pltpu.get_barrier_semaphore()
        for m in range(z_count):
            for e in range(fs_count):
                if m or e:
                    there = (flip(dp, m * y_count), flip(fs, e))
                    pl.semaphore_signal(barrier, inc=1, device_id=there, device_id_type=MESH)
        for j in range(1, y_count):
            pl.semaphore_signal(barrier, inc=1, device_id=(flip(dp, j), fs), device_id_type=MESH)
        pl.semaphore_wait(barrier, z_count * fs_count - 1 + y_count - 1)

        def spread(pieces):
            return Flight(net, dp, fs, fs_count, pieces, pieces.at[0])

        sum_of_b = RowSum(net, place, gb, yb, zsb, zrb, sum_b, qsb, qrb, sum_q.at[1])
        sum_of_b.start()

        def activate(e):
            at = slice(e * rows, (e + 1) * rows)
            work[:, 0:fj] = dot_nn(n2_ref[at, :], wi_ref[...])
            for r in range(0, rows, HEAD):
                value, rate = gelu_both(work[r : r + HEAD, 0:fj])
                hid[e * rows + r : e * rows + r + HEAD, :] = value.astype(BF)
                slope[e * rows + r : e * rows + r + HEAD, :] = rate.astype(BF)

        def pull(e, out):
            work[:, 0:fj] = dot_nn(dfs[e], wd_ref[...])
            for r in range(0, rows, HEAD):
                at = slice(e * rows + r, e * rows + r + HEAD)
                dpre[at, :] = (work[r : r + HEAD, 0:fj] * slope[at, :].astype(F32)).astype(BF)
            out[...] = dot_nt(dpre[e * rows : (e + 1) * rows, :], wi_ref[...]).astype(out.dtype)

        def part_into(scatter, e, fill):
            if e % 2:
                fill(e, scatter.sbuf.at[e // 2])
                scatter.send_odd(e // 2)
            else:
                fill(e, scatter.acc.at[e // 2])

        ff_sum = Scatter(net, dp, fs, fs_count, sbuf, rbuf, xsend, xrecv, acc)
        def both_steps(e):
            activate(e)
            part_into(ff_sum, e, pull)

        for j in reversed(range(1, half)):
            both_steps(2 * j + 1)
            both_steps(2 * j)
        for j in range(1, half):
            ff_sum.join(j)
        ff_sum.upper()
        both_steps(1)
        both_steps(0)
        sum_of_b.service(1)
        for m in range(2, z_count):
            sum_of_b.service(m)
        ff_sum.join(0)
        g_ff[:, 0:fj] = dot_tn(n2_ref[...], dpre[...]).astype(BF)
        g_ff[:, fj : 2 * fj] = dot_tn(dfs[...].reshape(total, width), hid[...]).astype(BF)
        sum_of_b.service(0)
        sum_of_ff = RowSum(net, place, g_ff, yf, zsf, zrf, sum_ff)
        sum_of_ff.start()

        loads["qkv"].wait()
        lane_first, lane_end, lane = doc_bounds(triples_ref, docs)
        for r in range(0, total, blk):
            at = slice(r, r + blk)
            q = qkv_ref[at, 0:hd].astype(F32)
            k = qkv_ref[at, hd : 2 * hd].astype(F32)
            row = lax.broadcasted_iota(jnp.int32, (blk, LANES), 0) + r
            inside = (row >= 3 * lane_first) & (row < 3 * lane_end)
            fk = jnp.where(inside, 1.0, 0.0)
            fq = jnp.where(inside | (lane >= docs), 0.0, MASKED)
            head_inputs(qs, ks, at, q, k, fq, fk, heads)
            kt[:, at] = k.T.astype(BF)
            dk[at, :] = jnp.zeros((blk, LANES), F32)
            dv[at, :] = jnp.zeros((blk, LANES), F32)

        def recompute(n):
            r = n * blk
            for h in range(heads):
                e, inv = softmax_block(ks, qs, h, r, r + blk)
                ps[n][h] = (e * inv).astype(BF)

        for n in range(blocks // 2):
            recompute(n)

        ff_sum.finish()
        for r in range(0, rows, LANES):
            at = slice(r, r + LANES)
            dx, dg = layer_norm_back(mid_ref[at, :], gain_ref[1:2, :], acc[0, at, :])
            dx = dx + da_ref[at, :]
            dm[at, :] = dx
            das[0, at, :] = dx.astype(BF)
            dg = jnp.sum(dg, axis=0, keepdims=True)
            gain_two = dg if r == 0 else gain_two + dg
        da_f = spread(das)
        for n in range(blocks // 2, blocks):
            recompute(n)
        for m in range(1, z_count):
            sum_of_ff.service(m)
        sum_of_ff.service(0)
        da_f.relay()

        place_of = lax.broadcasted_iota(jnp.int32, (blk, LANES), 1) // HEAD
        for r in range(0, total, blk):
            at = slice(r, r + blk)
            q = widen(qkv_ref[at, 0:hd].astype(F32))
            for h in range(heads):
                qs[h, at, :] = jnp.where(place_of == h, q, 0.0).astype(BF)
        lane_head = lax.broadcasted_iota(jnp.int32, (rows, LANES), 1) // HEAD
        for e in range(fs_count):
            da_f.ready(e)
            base = pl.multiple_of(flip(fs, e) * rows, 16)
            do = widen(dot_nt(das[e], wo_ref[...]))
            for h in range(heads):
                ks[h, pl.ds(base, rows), :] = jnp.where(lane_head == h, do, 0.0).astype(BF)
            for k in range(fs_count):

                @pl.when(fs == k)
                def _():
                    cols[pl.ds(base, rows), :] = das[e, :, k * hd : (k + 1) * hd]

        loads["att"].wait()
        g_out = dot_tn(att_ref[...], cols[...]).astype(BF)
        for e in range(fs_count):
            base = pl.multiple_of(flip(fs, e) * hd, 16)
            g_at[pl.ds(base, hd), 3 * hd : 4 * hd] = g_out[e * hd : (e + 1) * hd, :]
        sum_of_b.finish()

        loads["cos"].wait()
        loads["sin"].wait()
        for n in range(blocks):
            r, stop = n * blk, (n + 1) * blk
            at = slice(r, stop)
            found = []
            add_k = add_v = None
            for h in range(heads):
                p = ps[n][h]
                v = widen(qkv_ref[0:stop, 2 * hd : 3 * hd])
                grad = dot_nt(v, ks[h, at, :])
                wide = p.astype(F32)
                middle = jnp.sum(wide * grad, axis=0, keepdims=True)
                dr = (wide * (grad - middle) * 0.125).astype(BF)
                part_v = dot_nn(p, ks[h, at, :])
                part_k = dot_nn(dr, qs[h, at, :])
                add_v = part_v if add_v is None else add_v + part_v
                add_k = part_k if add_k is None else add_k + part_k
                found.append(dot_nn(kt[h * HEAD : (h + 1) * HEAD, 0:stop], dr))
            dk[0:stop, :] += add_k
            dv[0:stop, :] += add_v
            dq = jnp.concatenate(found, axis=0).T
            dqkv[at, 0:hd] = (dq * cos_ref[at, :] - partner(dq) * sin_ref[at, :]).astype(BF)
        for r in range(0, total, blk):
            at = slice(r, r + blk)
            grad = dk[at, 0:hd]
            dqkv[at, hd : 2 * hd] = (grad * cos_ref[at, :] - partner(grad) * sin_ref[at, :]).astype(BF)
            dqkv[at, 2 * hd : 3 * hd] = dv[at, 0:hd].astype(BF)
        loads["n1"].wait()
        g_at[:, 0 : 3 * hd] = dot_tn(n1_ref[...], dqkv[...]).astype(BF)
        sum_of_at = RowSum(net, place, g_at, ya, zsa, zra, sum_o, qsa, qra, sum_q.at[0])
        sum_of_at.start()

        ff_sum.sent()
        at_sum = Scatter(net, dp, fs, fs_count, sbuf, rbuf, xsend, xrecv, acc)
        tiles[0] = jnp.zeros((8, width), F32)

        def push_out(e, out):
            base = pl.multiple_of(flip(fs, e) * rows, 16)
            part = dot_nt(dqkv[pl.ds(base, rows), :], wq_ref[...])
            out[...] = part.astype(out.dtype)
            work[:, 0:width] = part
            total_of = jnp.zeros((8, width), F32)
            for r in range(0, rows, HEAD):
                grown = work[r : r + HEAD, 0:width] * n1_ref[pl.ds(base + r, HEAD), :].astype(F32)
                total_of = total_of + jnp.sum(grown.reshape(HEAD // 8, 8, width), axis=0)
            tiles[0] = tiles[0] + total_of

        for e in reversed(range(2, fs_count)):
            part_into(at_sum, e, push_out)
        part_into(at_sum, 1, push_out)
        for j in range(1, half):
            at_sum.join(j)
        at_sum.upper()
        part_into(at_sum, 0, push_out)
        gain_one = jnp.sum(tiles[0], axis=0, keepdims=True) / gain_ref[0:1, :]
        which = lax.broadcasted_iota(jnp.int32, (8, width), 0)
        both = jnp.where(which == 0, gain_one, jnp.where(which == 1, gain_two, 0.0))
        both = jnp.where(which == 2, dgain_two[0:1, :], jnp.where(which == 3, dgain_two[1:2, :], both))
        hops = [(dp, flip(fs, 1 << n)) for n in range(fs_count.bit_length() - 1)]
        hops += [(flip(dp, 1 << n), fs) for n in range(y_count.bit_length() - 1)]

        def hop_out(n, value):
            tiles[1 + n] = value
            return net.start(tiles.at[1 + n], tiles.at[1 + len(hops) + n], hops[n])

        hop = hop_out(0, both)
        sum_of_at.service(1)
        for n in range(1, len(hops) - 1):
            hop.wait_recv()
            both = both + tiles[len(hops) + n]
            hop = hop_out(n, both)
        for m in range(2, z_count):
            sum_of_at.service(m)
        sum_of_at.service(0)
        at_sum.join(0)
        sum_of_ff.finish()
        at_sum.finish()
        last = len(hops) - 1
        hop.wait_recv()
        both = both + tiles[len(hops) + last]
        hop = hop_out(last, both)
        for r in range(0, rows, LANES):
            at = slice(r, r + LANES)
            dx, _ = layer_norm_back(tok[at, :].astype(F32), gain_ref[0:1, :], acc[0, at, :])
            grad_in[at, :] = dx + dm[at, :]
        hop.wait_recv()
        dgain[...] = both + tiles[1 + len(hops) + last]
        sum_of_at.finish()
        net.finish()

    outs = [
        ((rows, width), F32),
        ((8, width), F32),
        ((rw, cb - 3 * hd), F32),
        ((rw, 2 * fj), F32),
        ((rw, hd), F32),
        ((2, 3, rw, hd), F32),
    ]
    wide = max(width, fj)
    zy = (y_count - 1, z_count, rw)
    scratch = [
        ((total, 3 * hd), BF),
        ((total, hd), F32),
        ((total, hd), F32),
        ((total, width), BF),
        ((total, width), BF),
        ((fs_count, rows, width), BF),
        ((total, fj), BF),
        ((total, fj), BF),
        ((total, fj), BF),
        ((rows, wide), F32),
        ((heads, total, LANES), BF),
        ((heads, total, LANES), BF),
        ((hd, total), BF),
        ((total, LANES), F32),
        ((total, LANES), F32),
        ((total, 3 * hd), BF),
        ((rows, width), F32),
        ((total, hd), BF),
        ((width, 2 * fj), BF),
        ((width, 4 * hd), BF),
        ((half, rows, width), BF),
        ((half, rows, width), BF),
        ((half - 1, rows, width), BF),
        ((half - 1, rows, width), BF),
        ((half, rows, width), F32),
        (zy + (cb,), BF),
        ((z_count - 1, rw, cb - 3 * hd), BF),
        ((z_count - 1, rw, cb - 3 * hd), BF),
        ((z_count, 3, rw, hd), BF),
        ((z_count, 3, rw, hd), BF),
        (zy + (2 * fj,), BF),
        ((z_count - 1, rw, 2 * fj), BF),
        ((z_count - 1, rw, 2 * fj), BF),
        (zy + (4 * hd,), BF),
        ((z_count - 1, rw, hd), BF),
        ((z_count - 1, rw, hd), BF),
        ((z_count, 3, rw, hd), BF),
        ((z_count, 3, rw, hd), BF),
        ((2 * (fs_count.bit_length() + y_count.bit_length() - 2) + 1, 8, width), F32),
    ]
    tail = [pltpu.VMEM((heads, (n + 1) * blk, blk), BF) for n in range(blocks)]
    arrays = (da, dfs, n2, wi, wd, mid, gain_rows, qkv, wo_own, wq, cos, sin, triples, n1, att_rel, tokens, group_b, dgain_b)
    return pl.pallas_call(
        body,
        out_shape=[jax.ShapeDtypeStruct(s, t) for s, t in outs],
        in_specs=[hbm() if n in (7, 10, 11, 13, 14) else smem() if n == 12 else vmem() for n in range(18)],
        out_specs=[vmem()] * len(outs),
        scratch_shapes=[pltpu.VMEM(s, t) for s, t in scratch] + [pltpu.SemaphoreType.DMA((sems,))] * 2 + tail,
        compiler_params=pltpu.CompilerParams(collective_id=4, has_side_effects=True, vmem_limit_bytes=VMEM_BYTES),
        cost_estimate=cost(4e10, 3e7),
        name="backward_one",
    )(*arrays)


def middle(y_count, dp_count, fs_count, s0, after, z_blocks, cot, c_rel, wq, wu, weights, wp, gain_rows, cos, sin, triples):
    short, width = s0.shape
    rows, total = short * 3, short * fs_count
    hd = wq.shape[1] // 3
    pc = wp.shape[2]
    wout, win, wdown = weights
    fj, rw = win.shape[2], win.shape[1]
    z_count = dp_count // y_count
    heads, docs = hd // HEAD, triples.shape[1]
    blk = min(QB, total)
    blocks, half = total // blk, fs_count // 2
    cb = 4 * hd + 2 * pc
    sems = 96 + 16 * fs_count + 6 * dp_count

    def body(
        s0_ref, after_ref, z_ref, cot_ref, c_ref, wq_ref, wu_ref, o_in, i_in, d_in, wp_ref, gain_ref, cos_ref, sin_ref, triples_ref,
        out, da, dfs_out, group, sum_ff, dgain,
        wos, wi_ref, wd_ref, g_ff, yg, zsg, zrg, sd, rd, xd, yd, ad, lift_send, lift_rel,
        s0s, x_all, wo_at, hold, turned, z_rel, dfs, df_all, das, cols, s1s, ds0s, nxt,
        n1, n2, qkv, att, att_rel, qs, ks, vt, kt, dk, dv, dqkv, work, hid, slope, dpre, m_all, dm,
        sf, rf, xf, yf, af, sb, rb, xb, yb, ab, sa, ra, xa, ya, aa, thin, spread_rows, lift, send_sem, recv_sem, *ps,
    ):
        dp, fs = lax.axis_index("dp"), lax.axis_index("fsdp")
        net = Net(send_sem, recv_sem)

        def base_of(e, amount):
            return pl.multiple_of(flip(fs, e) * amount, 16)

        def spread(pieces, src=None):
            return Flight(net, dp, fs, fs_count, pieces, pieces.at[0] if src is None else src)

        s0s[0] = s0_ref[...].astype(BF)
        nxt[...] = jnp.zeros(nxt.shape, BF)
        here = pl.ds(pl.multiple_of(dp * rw, 16), rw)
        wos[0, here, :] = o_in[1].astype(BF)
        wi_ref[here, :] = i_in[1].astype(BF)
        wd_ref[here, :] = d_in[1].astype(BF)
        barrier = pltpu.get_barrier_semaphore()
        for e in range(1, fs_count):
            pl.semaphore_signal(barrier, inc=1, device_id=(dp, flip(fs, e)), device_id_type=MESH)
        others = [m * y_count for m in range(1, z_count)] + list(range(1, y_count))
        for step in others:
            pl.semaphore_signal(barrier, inc=1, device_id=(flip(dp, step), fs), device_id_type=MESH)
        pl.semaphore_wait(barrier, fs_count - 1 + len(others))

        def of(buf, step):
            return buf.at[pl.ds(pl.multiple_of(flip(dp, step) * rw, 16), rw), :]

        def along_z(buf):
            return [
                net.start(of(buf, 0), of(buf, 0), (flip(dp, m * y_count), fs)) for m in range(1, z_count)
            ]

        def along_y(buf, m):
            return [
                net.start(of(buf, m * y_count), of(buf, m * y_count), (flip(dp, n), fs)) for n in range(1, y_count)
            ]

        def pass_on(buf, came, passed):
            for m in range(1, z_count):
                came[m - 1].wait_recv()
                passed += along_y(buf, m)

        def wait_all(copies):
            for copy in copies:
                copy.wait_recv()

        s0_f = spread(s0s)
        came = [along_z(buf) for buf in (wos.at[0], wi_ref, wd_ref)]
        passed = [along_y(buf, 0) for buf in (wos.at[0], wi_ref, wd_ref)]

        dsum = Scatter(net, dp, fs, fs_count, sd, rd, xd, yd, ad)
        for e in reversed(range(fs_count)):
            part = dot_nt(c_ref[e], wu_ref[...])
            if e % 2:
                sd[e // 2] = part.astype(BF)
                dsum.send_odd(e // 2)
            else:
                ad[e // 2] = part

        def exchange(blocks_of, landed):
            found = []
            for e in range(1, fs_count):
                found.append(net.start(blocks_of.at[flip(fs, e)], landed.at[e], (dp, flip(fs, e))))
            landed[0] = blocks_of[fs]
            return found

        lane_first, lane_end, lane = doc_bounds(triples_ref, docs)
        for n in range(1, half):
            dsum.join(n)
        dsum.upper()
        s0_f.relay()
        pass_on(wos.at[0], came[0], passed[0])
        for e in range(fs_count):
            s0_f.ready(e)
            at = pl.ds(base_of(e, short), short)
            value = s0_ref[...] if e == 0 else s0s[e].astype(F32)
            x_all[at, :] = value
            n1[at, :] = layer_norm(value, gain_ref[2:3, :]).astype(BF)
        for r in range(0, total, blk):
            at = slice(r, r + blk)
            got = dot_nn(n1[at, :], wq_ref[...])
            q, k, v = got[:, :hd], got[:, hd : 2 * hd], got[:, 2 * hd :]
            q = (q * cos_ref[at, :] + partner(q) * sin_ref[at, :]).astype(BF)
            k = (k * cos_ref[at, :] + partner(k) * sin_ref[at, :]).astype(BF)
            qkv[at, 0:hd] = q
            qkv[at, hd : 2 * hd] = k
            qkv[at, 2 * hd : 3 * hd] = v.astype(BF)
            row = lax.broadcasted_iota(jnp.int32, (blk, LANES), 0) + r
            inside = (row >= lane_first) & (row < lane_end)
            fk = jnp.where(inside, 1.0, 0.0)
            fq = jnp.where(inside | (lane >= docs), 0.0, MASKED)
            head_inputs(qs, ks, at, q.astype(F32), k.astype(F32), fq, fk, heads)
            vt[:, at] = v.T.astype(BF)
            kt[:, at] = k.astype(F32).T.astype(BF)
            dk[at, :] = jnp.zeros((blk, LANES), F32)
            dv[at, :] = jnp.zeros((blk, LANES), F32)
        dsum.join(0)
        dsum.finish()
        dm[...] = ad[0]
        dfs[0] = ad[0].astype(BF)
        df_f = spread(dfs)
        wait_all(passed[0])
        wo_f = spread(wos, wos.at[0])
        flights = []
        for n in range(blocks):
            r, stop = n * blk, (n + 1) * blk
            found = []
            for h in range(heads):
                e, inv = softmax_block(ks, qs, h, r, stop)
                ps[n][h] = (e * inv).astype(BF)
                found.append(dot_nn(vt[h * HEAD : (h + 1) * HEAD, 0:stop], ps[n][h]))
            att[0, r:stop, :] = jnp.concatenate(found, axis=0).T.astype(BF)
            flights.append(spread(att.at[:, r:stop, :], att.at[0, r:stop, :]))
            if n == 0:
                pass_on(wi_ref, came[1], passed[1])
                df_f.relay()
                wo_f.relay()
        place_of = lax.broadcasted_iota(jnp.int32, (blk, LANES), 1) // HEAD
        for r in range(0, total, blk):
            at = slice(r, r + blk)
            q = widen(qkv[at, 0:hd].astype(F32))
            for h in range(heads):
                qs[h, at, :] = jnp.where(place_of == h, q, 0.0).astype(BF)

        pass_on(wd_ref, came[2], passed[2])
        wo_f.all_ready()
        for e in range(fs_count):
            wo_at[flip(fs, e)] = wos[e]
        for e in range(fs_count):
            hold[:, e * hd : (e + 1) * hd] = wo_at[e]
        for e in range(fs_count):
            turned[e * hd : (e + 1) * hd, :] = hold[pl.ds(base_of(e, hd), hd), :]
        for flight in flights:
            flight.relay()
        for flight in flights:
            flight.all_ready()
        for e in range(fs_count):
            att_rel[:, e * hd : (e + 1) * hd] = att[e]

        work[:, 0:width] = x_all[...] + dot_nn(att_rel[...], turned[...])
        for r in range(0, total, HEAD):
            m = work[r : r + HEAD, 0:width]
            m_all[r : r + HEAD, :] = m
            n2[r : r + HEAD, :] = layer_norm(m, gain_ref[3:4, :]).astype(BF)
        wait_all(passed[1])
        work[:, 0:fj] = dot_nn(n2[...], wi_ref[...])
        for r in range(0, total, HEAD):
            value, rate = gelu_both(work[r : r + HEAD, 0:fj])
            hid[r : r + HEAD, :] = value.astype(BF)
            slope[r : r + HEAD, :] = rate
        wait_all(passed[2])
        work[:, 0:width] = dot_nt(hid[...], wd_ref[...])

        def give_out(scatter, source):
            for e in reversed(range(fs_count)):
                value = source[pl.ds(base_of(e, short), short), 0:width]
                if e % 2:
                    scatter.sbuf[e // 2] = value.astype(BF)
                    scatter.send_odd(e // 2)
                else:
                    scatter.acc[e // 2] = value

        fwd = Scatter(net, dp, fs, fs_count, sf, rf, xf, yf, af)
        give_out(fwd, work)
        for e in range(fs_count):
            df_f.ready(e)
            df_all[pl.ds(base_of(e, short), short), :] = dfs[e]
        work[:, 0:fj] = dot_nn(df_all[...], wd_ref[...])
        for r in range(0, total, HEAD):
            at = slice(r, r + HEAD)
            dpre[at, :] = (work[at, 0:fj] * slope[at, :]).astype(BF)
        work[:, 0:width] = dot_nt(dpre[...], wi_ref[...])
        bwd = Scatter(net, dp, fs, fs_count, sb, rb, xb, yb, ab)
        give_out(bwd, work)
        for j in range(1, half):
            bwd.join(j)
        bwd.upper()
        for j in range(1, half):
            fwd.join(j)
        fwd.upper()
        g_ff[:, 0:fj] = dot_tn(n2[...], dpre[...]).astype(BF)
        g_ff[:, fj : 2 * fj] = dot_tn(df_all[...], hid[...]).astype(BF)
        ff_rows = RowSum(net, (dp, fs, y_count, z_count, fs_count, rw), g_ff, yg, zsg, zrg, sum_ff)
        ff_rows.start()
        bwd.join(0)
        bwd.finish()
        m_own = m_all[pl.ds(base_of(0, short), short), :]
        dx, dg = layer_norm_back(m_own, gain_ref[3:4, :], ab[0])
        dx = dx + dm[...]
        dm[...] = dx
        das[0] = dx.astype(BF)
        da_f = spread(das)
        gain_two = jnp.sum(dg, axis=0, keepdims=True)

        fwd.join(0)
        fwd.finish()
        s1s[0] = (m_own + af[0]).astype(BF)
        s1_f = spread(s1s)
        z_f = exchange(z_ref, z_rel)
        da_f.relay()
        s1_f.relay()
        for e in range(fs_count):
            da_f.ready(e)
            at = pl.ds(base_of(e, short), short)
            do = widen(dot_nt(das[e], turned[0:hd, :]))
            lane_head = lax.broadcasted_iota(jnp.int32, (short, LANES), 1) // HEAD
            for h in range(heads):
                ks[h, at, :] = jnp.where(lane_head == h, do, 0.0).astype(BF)
            for k in range(fs_count):

                @pl.when(fs == k)
                def _():
                    cols[at, :] = das[e, :, k * hd : (k + 1) * hd]

        g_out = dot_tn(att_rel[...], cols[...]).astype(BF)
        for e in range(fs_count):
            group[pl.ds(base_of(e, hd), hd), cb - hd : cb] = g_out[e * hd : (e + 1) * hd, :]
        for n in range(blocks):
            r, stop = n * blk, (n + 1) * blk
            at = slice(r, stop)
            found = []
            add_k = add_v = None
            for h in range(heads):
                p = ps[n][h]
                grad = dot_nt(widen(qkv[0:stop, 2 * hd : 3 * hd]), ks[h, at, :])
                wide = p.astype(F32)
                inner = jnp.sum(wide * grad, axis=0, keepdims=True)
                dr = (wide * (grad - inner) * 0.125).astype(BF)
                part_v = dot_nn(p, ks[h, at, :])
                part_k = dot_nn(dr, qs[h, at, :])
                add_v = part_v if add_v is None else add_v + part_v
                add_k = part_k if add_k is None else add_k + part_k
                found.append(dot_nn(kt[h * HEAD : (h + 1) * HEAD, 0:stop], dr))
            dk[0:stop, :] += add_k
            dv[0:stop, :] += add_v
            dq = jnp.concatenate(found, axis=0).T
            dqkv[at, 0:hd] = (dq * cos_ref[at, :] - partner(dq) * sin_ref[at, :]).astype(BF)
        for r in range(0, total, blk):
            at = slice(r, r + blk)
            grad = dk[at, 0:hd]
            dqkv[at, hd : 2 * hd] = (grad * cos_ref[at, :] - partner(grad) * sin_ref[at, :]).astype(BF)
            dqkv[at, 2 * hd : 3 * hd] = dv[at, 0:hd].astype(BF)
        work[:, 0:width] = dot_nt(dqkv[...], wq_ref[...])
        first = Scatter(net, dp, fs, fs_count, sa, ra, xa, ya, aa)
        give_out(first, work)
        for j in range(1, half):
            first.join(j)
        first.upper()
        group[:, 0 : 3 * hd] = dot_tn(n1[...], dqkv[...]).astype(BF)
        s1_f.all_ready()
        lift_f = []
        for e in range(fs_count):
            part = dot_nn(s1s[e], wu_ref[...]).astype(BF)
            if e:
                lift_send[e] = part
                lift_f.append(net.start(lift_send.at[e], lift_rel.at[e], (dp, flip(fs, e))))
            else:
                lift_rel[0] = part
        g_up = jnp.zeros((width, pc), F32)
        for e in range(fs_count):
            g_up = g_up + dot_tn(s1s[e], c_ref[e])
        group[:, 3 * hd + pc : 3 * hd + 2 * pc] = g_up.astype(BF)
        for m in range(1, z_count):
            ff_rows.service(m)
        first.join(0)
        first.finish()
        dx, dg = layer_norm_back(s0_ref[...], gain_ref[2:3, :], aa[0])
        ds0s[0] = (dx + dm[...]).astype(BF)
        gain_one = jnp.sum(dg, axis=0, keepdims=True)
        which = lax.broadcasted_iota(jnp.int32, (8, width), 0)
        dgain[...] = jnp.where(which == 0, gain_one, jnp.where(which == 1, gain_two, 0.0))

        hop = net.make(ds0s.at[0, 0:HALO, :], nxt, (dp, lax.rem(fs + fs_count - 1, fs_count)))

        @pl.when(fs > 0)
        def _():
            hop.start()

        ds0_f = spread(ds0s)
        row = lax.broadcasted_iota(jnp.int32, (short, LANES), 0) + fs * short + 1
        shut = jnp.max(jnp.where((row == lane_first) | (row >= total), 1.0, 0.0), axis=1, keepdims=True) > 0.0

        @pl.when(fs < fs_count - 1)
        def _():
            hop.wait_recv()

        grad = jnp.concatenate([ds0s[0], nxt[...]], axis=0)
        for e in range(fs_count):
            lift_at = dot_nn(grad, wp_ref[e])
            spread_rows[flip(fs, e)] = lift_at
        dz = jnp.concatenate([spread_rows[e] for e in range(fs_count)], axis=1)
        strided_write(thin, 0, short, dz[0:short, 2 * width : 3 * width])
        for k in range(2):
            part = dz[1 : short + 1, k * width : (k + 1) * width]
            strided_write(thin, k + 1, short, jnp.where(shut, 0.0, part))
        value = cot_ref[...].astype(F32) + spread_read(thin)
        da[...] = value
        dfs_out[0] = value.astype(BF)
        out_f = spread(dfs_out)
        ff_rows.service(0)
        ds0_f.relay()
        for copy in z_f:
            copy.wait_recv()
        g_pool = jnp.zeros((width, pc), F32)
        for e in range(fs_count):
            ds0_f.ready(e)
            g_pool = g_pool + dot_tn(ds0s[e], z_rel[e])
        group[:, 3 * hd : 3 * hd + pc] = g_pool.astype(BF)

        wait_all(lift_f)
        for e in range(fs_count):
            lift[flip(fs, e)] = lift_rel[e].astype(F32)
        lifted = jnp.concatenate([lift[e] for e in range(fs_count)], axis=1)
        for n in range(3):
            strided_write(thin, n, short, lifted[:, n * width : (n + 1) * width])
        out[...] = (after_ref[...] + spread_read(thin)).astype(BF)
        ff_rows.finish()
        out_f.relay()
        out_f.all_ready()

        @pl.when(fs > 0)
        def _():
            hop.wait_send()

        net.finish()

    wide = max(width, fj)
    pieces = (fs_count, short, width)
    scatter = [((half, short, width), BF)] * 2 + [((half - 1, short, width), BF)] * 2 + [((half, short, width), F32)]
    outs = [((rows, width), BF), ((rows, width), F32), ((fs_count, rows, width), BF), ((width, cb), BF), ((rw, 2 * fj), F32), ((8, width), F32)]
    scratch = [
        ((fs_count, width, hd), BF),
        ((width, fj), BF),
        ((width, fj), BF),
        ((width, 2 * fj), BF),
        ((y_count - 1, z_count, rw, 2 * fj), BF),
        ((z_count - 1, rw, 2 * fj), BF),
        ((z_count - 1, rw, 2 * fj), BF),
        *scatter,
        ((fs_count, short, pc), BF),
        ((fs_count, short, pc), BF),
        (pieces, BF),
        ((total, width), F32),
        ((fs_count, width, hd), BF),
        ((width, width), BF),
        ((width, width), BF),
        ((fs_count, short, pc), BF),
        (pieces, BF),
        ((total, width), BF),
        (pieces, BF),
        ((total, hd), BF),
        (pieces, BF),
        (pieces, BF),
        ((HALO, width), BF),
        ((total, width), BF),
        ((total, width), BF),
        ((total, 3 * hd), BF),
        ((fs_count, total, hd), BF),
        ((total, width), BF),
        ((heads, total, LANES), BF),
        ((heads, total, LANES), BF),
        ((hd, total), BF),
        ((hd, total), BF),
        ((total, LANES), F32),
        ((total, LANES), F32),
        ((total, 3 * hd), BF),
        ((total, wide), F32),
        ((total, fj), BF),
        ((total, fj), F32),
        ((total, fj), BF),
        ((total, width), F32),
        ((short, width), F32),
        *scatter,
        *scatter,
        *scatter,
        ((width // LANES, rows, LANES), F32),
        ((fs_count, short + HALO, pc), F32),
        ((fs_count, short, pc), F32),
    ]
    tail = [pltpu.VMEM((heads, (n + 1) * blk, blk), BF) for n in range(blocks)]
    arrays = (s0, after, z_blocks, cot, c_rel, wq, wu, wout, win, wdown, wp, gain_rows, cos, sin, triples)
    return pl.pallas_call(
        body,
        out_shape=[jax.ShapeDtypeStruct(s, t) for s, t in outs],
        in_specs=[vmem()] * 14 + [smem()],
        out_specs=[vmem()] * len(outs),
        scratch_shapes=[pltpu.VMEM(s, t) for s, t in scratch] + [pltpu.SemaphoreType.DMA((sems,))] * 2 + tail,
        compiler_params=pltpu.CompilerParams(collective_id=2, has_side_effects=True, vmem_limit_bytes=VMEM_BYTES),
        cost_estimate=cost(2e10, 2e7),
        name="middle",
    )(*arrays)


def owners_of(amount, dp_count, fs_count):
    found = []
    half = dp_count // 2
    for k in range(amount):
        found.append((dp_count // 4 + k % half, (2 * (k // half)) % fs_count + (2 * (k // half)) // fs_count))
    return found


def round_up(width):
    return -(-width // LANES) * LANES


def newton_schulz(box, x, norm, count, width, dp_count, rw, done):
    coef_a, coef_b, coef_c = NS_COEFS
    rows = dp_count * rw
    square = jnp.zeros((1, 1), F32)
    for at in range(count):
        block = box[at * dp_count : (at + 1) * dp_count, :, 0:width].reshape(rows, width)
        x[:, at * width : (at + 1) * width] = block
        wide = block.astype(F32)
        square = square + jnp.sum(jnp.sum(wide * wide, axis=0, keepdims=True), axis=1, keepdims=True)
    length = jnp.sqrt(square)
    norm[...] = jnp.broadcast_to(length, norm.shape)
    scale = 1.0 / (length + NORM_EPS)
    span = count * width
    for turn in range(NS_STEPS):
        gram = dot_nt(x[:, 0:span], x[:, 0:span])
        if turn == 0:
            gram = gram * (scale * scale)
        gram = gram.astype(BF)
        poly = (coef_b * gram.astype(F32) + coef_c * dot_nn(gram, gram)).astype(BF)
        for at in range(count):
            here = slice(at * width, (at + 1) * width)
            block = x[:, here]
            new = coef_a * block.astype(F32) + dot_nn(poly, block)
            if turn == 0:
                new = new * scale
            if turn < NS_STEPS - 1:
                x[:, here] = new.astype(BF)
            else:
                box[at * dp_count : (at + 1) * dp_count, :, 0:width] = new.astype(BF).reshape(dp_count, rw, width)
                done(at)


def muon(y_count, dp_count, fs_count, sums, moments, dgain):
    sum_q, sum_o, sum_ff, sum_ff1, sum_rest = sums
    rw, hd = sum_o.shape
    fj = sum_ff.shape[1] // 2
    pc = moments[4].shape[1]
    width = rw * dp_count
    z_count = dp_count // y_count
    devices = dp_count * fs_count
    widths = [fj, fj, fj, fj, 3 * hd, 3 * hd, pc, pc, hd, hd]
    widths = [round_up(w) for w in widths]
    amount, wide = len(widths), max(widths)
    owners = owners_of(amount, dp_count, fs_count)
    classes = sorted(set(widths))
    sems = 16
    z_bits = z_count.bit_length() - 1

    def body(
        q_ref, o_ref, ff_ref, ff1_ref, rest_ref, mq, mo, mi, md, mp, mu, ga,
        out, norms, dgain_out, box, x, norm, tiles, tsend, *rest_refs,
    ):
        pieces = rest_refs[:amount]
        send_sem, recv_sem, push_send, push_recv, give_send, give_recv, norm_send, norm_recv = rest_refs[amount:]
        dp, fs = lax.axis_index("dp"), lax.axis_index("fsdp")
        slot = fs * dp_count + dp
        net = Net(send_sem, recv_sem)

        def put(k, value):
            have = value.shape[1]
            if have < widths[k]:
                value = jnp.concatenate([value, jnp.zeros((rw, widths[k] - have), F32)], axis=1)
            pieces[k][...] = value.astype(BF)

        at = 2 * pc
        put(0, MOMENT_DECAY * mi[0] + ff_ref[:, 0:fj])
        put(1, MOMENT_DECAY * mi[1] + ff1_ref[:, 0:fj])
        put(2, MOMENT_DECAY * md[0] + ff_ref[:, fj : 2 * fj])
        put(3, MOMENT_DECAY * md[1] + ff1_ref[:, fj : 2 * fj])
        for b in range(2):
            put(4 + b, MOMENT_DECAY * mq[b] + jnp.concatenate([q_ref[b, t] for t in range(3)], axis=1))
        put(6, MOMENT_DECAY * mp[...] + rest_ref[:, 0:pc])
        put(7, MOMENT_DECAY * mu[...] + rest_ref[:, pc : 2 * pc])
        put(8, MOMENT_DECAY * mo[0] + o_ref[...])
        put(9, MOMENT_DECAY * mo[1] + rest_ref[:, at:])
        if any(w != wide for w in widths):
            box[...] = jnp.zeros(box.shape, BF)

        barrier = pltpu.get_barrier_semaphore()

        def greet(t, carry):
            @pl.when(t != slot)
            def _():
                there = (lax.rem(t, dp_count), lax.div(t, dp_count))
                pl.semaphore_signal(barrier, inc=1, device_id=there, device_id_type=MESH)

            return carry

        lax.fori_loop(0, devices, greet, 0)
        pl.semaphore_wait(barrier, devices - 1)

        mine = [(dp == owners[k][0]) & (fs == owners[k][1]) for k in range(amount)]
        for k in range(amount):
            copy = pltpu.make_async_remote_copy(
                src_ref=pieces[k],
                dst_ref=box.at[slot, :, 0 : widths[k]],
                send_sem=push_send.at[k],
                recv_sem=push_recv,
                device_id=owners[k],
                device_id_type=MESH,
            )

            @pl.when(jnp.logical_not(mine[k]))
            def _():
                copy.start()

            @pl.when(mine[k])
            def _():
                box[slot, :, 0 : widths[k]] = pieces[k][...]

        total = ga[...]
        for n in range(z_bits):
            tsend[n] = total
            hop = net.start(tsend.at[n], tiles.at[n], (flip(dp, y_count << n), fs))
            hop.wait_recv()
            total = total + tiles[n]
        dgain_out[...] = total

        for k in range(amount):

            @pl.when(mine[k])
            def _():
                landed = box.at[0 : devices - 1, :, 0 : widths[k]]
                pltpu.make_async_copy(landed, landed, push_recv).wait()

        which_k = jnp.int32(0)
        for k in range(1, amount):
            which_k = which_k + k * mine[k].astype(jnp.int32)
        for w in classes:
            chosen = None
            for k in range(amount):
                if widths[k] == w:
                    chosen = mine[k] if chosen is None else chosen | mine[k]

            @pl.when(chosen)
            def _():
                def done(block):
                    def give(i, carry):
                        t = block * dp_count + i

                        @pl.when(t != slot)
                        def _():
                            pltpu.make_async_remote_copy(
                                src_ref=box.at[t, :, 0:w],
                                dst_ref=out.at[which_k, :, 0:w],
                                send_sem=give_send,
                                recv_sem=give_recv.at[which_k],
                                device_id=(i, block),
                                device_id_type=MESH,
                            ).start()
                            pltpu.make_async_remote_copy(
                                src_ref=norm,
                                dst_ref=norms.at[which_k],
                                send_sem=norm_send,
                                recv_sem=norm_recv.at[which_k],
                                device_id=(i, block),
                                device_id_type=MESH,
                            ).start()

                        return carry

                    lax.fori_loop(0, dp_count, give, 0)

                newton_schulz(box, x, norm, fs_count, w, dp_count, rw, done)
                out[which_k, :, 0:w] = box[slot, :, 0:w]
                norms[which_k] = norm[...]

        for k in range(amount):
            w = widths[k]

            @pl.when(jnp.logical_not(mine[k]))
            def _():
                landed = out.at[k, :, 0:w]
                pltpu.make_async_copy(landed, landed, give_recv.at[k]).wait()
                pltpu.make_async_copy(norms.at[k], norms.at[k], norm_recv.at[k]).wait()
                pltpu.make_async_copy(pieces[k], pieces[k], push_send.at[k]).wait()

            @pl.when(mine[k])
            def _():
                left = box.at[0 : devices - 1, :, 0:w]
                pltpu.make_async_copy(left, left, give_send).wait()

                def drain(t, carry):
                    pltpu.make_async_copy(norm, norm, norm_send).wait()
                    return carry

                lax.fori_loop(0, devices - 1, drain, 0)

        net.finish()

    outs = [((amount, rw, wide), BF), ((amount, 8, LANES), F32), ((8, width), F32)]
    scratch = [
        ((devices, rw, wide), BF),
        ((width, fs_count * wide), BF),
        ((8, LANES), F32),
        ((z_bits, 8, width), F32),
        ((z_bits, 8, width), F32),
    ] + [((rw, w), BF) for w in widths]
    dma = pltpu.SemaphoreType.DMA
    return pl.pallas_call(
        body,
        out_shape=[jax.ShapeDtypeStruct(s, t) for s, t in outs],
        in_specs=[vmem()] * 12,
        out_specs=[vmem()] * len(outs),
        scratch_shapes=[pltpu.VMEM(s, t) for s, t in scratch]
        + [dma((sems,)), dma((sems,)), dma((amount,)), dma, dma, dma((amount,)), dma, dma((amount,))],
        compiler_params=pltpu.CompilerParams(collective_id=1, has_side_effects=True, vmem_limit_bytes=VMEM_BYTES),
        name="muon",
    )(sum_q, sum_o, sum_ff, sum_ff1, sum_rest, *moments, dgain)


def update(dp_arr, sums, results, norms, roots, dgain, moments, weights, m_gains_t, gains_t, layer_out, grad_in):
    sum_q, sum_o, sum_ff, sum_ff1, sum_rest = sums
    rw, hd = sum_o.shape
    fj = sum_ff.shape[1] // 2
    pc = moments[4].shape[1]
    width = dgain.shape[1]

    def body(me_ref, q_ref, o_ref, ff_ref, ff1_ref, rest_ref, res, norms_ref, roots_ref, dg, *refs):
        m_in, w_in, (mg, g, act, grad), refs = refs[:6], refs[6:12], refs[12:16], refs[16:]
        m_out, w_out, (mg_out, g_out, act_out, grad_out, rms), turned = refs[:6], refs[6:12], refs[12:17], refs[17]
        act_out[...] = act[...]
        grad_out[...] = grad[...]
        at = 2 * pc
        grads = [
            [jnp.concatenate([q_ref[b, t] for t in range(3)], axis=1) for b in range(2)],
            [o_ref[...], rest_ref[:, at:]],
            [ff_ref[:, 0:fj], ff1_ref[:, 0:fj]],
            [ff_ref[:, fj : 2 * fj], ff1_ref[:, fj : 2 * fj]],
            [rest_ref[:, 0:pc]],
            [rest_ref[:, pc : 2 * pc]],
        ]
        places = [(4, 5), (8, 9), (0, 1), (2, 3), (6,), (7,)]
        for kind in range(6):
            for b in range(len(grads[kind])):
                here = (b,) if kind < 4 else (slice(None),)
                have = m_in[kind].shape[-1]
                m_out[kind][here] = MOMENT_DECAY * m_in[kind][here] + grads[kind][b]
                turn = res[places[kind][b], :, 0:have].astype(F32)
                w_out[kind][here] = w_in[kind][here] - STEP_SCALES[kind] * turn
        turned[...] = jnp.concatenate([dg[...], jnp.zeros((LANES - 8, width), F32)], axis=0).T
        mine = turned[pl.ds(pl.multiple_of(me_ref[0] * rw, 16), rw), :].T
        fresh = GAIN_DECAY * mg[...] + mine[0:4, :]
        mg_out[...] = fresh
        g_out[...] = g[...] - GAIN_RATE * fresh
        places = (4, 5, 8, 9, 0, 1, 2, 3, 6, 7)
        lengths = jnp.concatenate([norms_ref[p, 0:1, :] for p in places] + [norms_ref[0, 0:6, :]], axis=0)
        rms[...] = lengths / roots_ref[...]

    outs = [(a.shape, a.dtype) for a in (*moments, *weights, m_gains_t, gains_t, layer_out, grad_in)] + [((16, LANES), F32)]
    return local_kernel(
        body,
        "update",
        outs,
        [((width, LANES), F32)],
        dp_arr,
        sum_q,
        sum_o,
        sum_ff,
        sum_ff1,
        sum_rest,
        results,
        norms,
        roots,
        dgain,
        *moments,
        *weights,
        m_gains_t,
        gains_t,
        layer_out,
        grad_in,
    )


def rope_tables(total, hd):
    half = HEAD // 2
    frequency = (np.float32(10000.0) ** (-np.arange(half, dtype=np.float32) / np.float32(half))).astype(np.float32)
    angle = (np.arange(total, dtype=np.float32)[:, None] * frequency[None, :]).astype(np.float32)
    cos, sin = np.cos(angle), np.sin(angle)
    cos = np.tile(np.concatenate([cos, cos], axis=1), (1, hd // HEAD))
    sin = np.tile(np.concatenate([-sin, sin], axis=1), (1, hd // HEAD))
    return jnp.asarray(cos, F32), jnp.asarray(sin, F32)


def on_device(
    y_count,
    tokens,
    cotangent,
    doc_triples,
    w_qkv,
    w_out,
    w_in,
    w_down,
    w_pool,
    w_up,
    gains,
    m_qkv,
    m_out,
    m_in,
    m_down,
    m_pool,
    m_up,
    m_gains,
):
    rows, width = tokens.shape
    fs_count, dp_count = lax.axis_size("fsdp"), lax.axis_size("dp")
    dp_arr = lax.axis_index("dp").astype(jnp.int32).reshape(1)
    total = rows * fs_count
    hd = width // fs_count

    cos0, sin0 = rope_tables(total, hd)

    old_weights = (w_qkv, w_out, w_in, w_down, w_pool, w_up)
    if total <= 2048:
        n1, qkv, att_rel, n2, wo_own, mid, wqkv0, wi0, wd0, gain_rows, layer_out, da, dfs, group_b, sum_ff1, dgain_b = forward_all(
            y_count, dp_count, fs_count, tokens, cotangent, doc_triples, old_weights, gains.T, cos0, sin0
        )
    else:
        cos1, sin1 = cos0[: total // 3], sin0[: total // 3]
        n1, qkv, att_rel, wo_own, n2, mid, after, z_blocks, s0, wqkv0, wi0, wd0, wp, wqkv1, wu, c_rel, gain_rows = forward_one(
            y_count, dp_count, fs_count, tokens, cotangent, doc_triples, old_weights, gains.T, cos0, sin0
        )
        layer_out, da, dfs, group_b, sum_ff1, dgain_b = middle(
            y_count, dp_count, fs_count, s0, after, z_blocks, cotangent, c_rel, wqkv1, wu, old_weights[1:4], wp, gain_rows,
            cos1, sin1, doc_triples,
        )
    grad_in, dgain, sum_rest, sum_ff, sum_o, sum_q = backward_one(
        y_count, dp_count, fs_count, da, dfs, n2, wi0, wd0, mid, gain_rows, qkv, wo_own, wqkv0, cos0, sin0, doc_triples, n1,
        att_rel, tokens, group_b, dgain_b,
    )

    sums = (sum_q, sum_o, sum_ff, sum_ff1, sum_rest)
    moments = (m_qkv, m_out, m_in, m_down, m_pool, m_up)
    results, norms, dgain = muon(y_count, dp_count, fs_count, sums, moments, dgain)
    all_tokens = float(total * dp_count)
    entries = [m.size // (2 if m.ndim == 3 else 1) for m in moments for _ in range(2 if m.ndim == 3 else 1)]
    roots = np.ones((16, LANES), np.float64)
    roots[:10] = np.array([float(n * fs_count * dp_count) * all_tokens for n in entries])[:, None] ** 0.5
    *fresh, gain_moments, new_gains, layer_out, grad_in, rms = update(
        dp_arr, sums, results, norms, jnp.asarray(roots, F32), dgain, moments, old_weights, m_gains.T, gains.T, layer_out, grad_in
    )
    return (layer_out, grad_in, *fresh, gain_moments.T, new_gains.T, rms[:10, 0])


def solution(mesh):
    by_row, by_dp = P(("dp", "fsdp"), None), P("dp", None)
    stacked, flat = P(None, "dp", "fsdp"), P("dp", "fsdp")
    matrices = (stacked,) * 4 + (flat,) * 2
    y_count = max(1, mesh.shape["fsdp"] // 2)
    return jax.shard_map(
        functools.partial(on_device, y_count),
        mesh=mesh,
        in_specs=(by_row, by_row, by_dp, *matrices, by_dp, *matrices, by_dp),
        out_specs=(by_row, by_row, *matrices, *matrices, by_dp, by_dp, P()),
        check_vma=False,
    )
```

```python
import functools

import jax
import jax.numpy as jnp
import numpy as np
from jax import lax
from jax.experimental import pallas as pl
from jax.experimental.pallas import tpu as pltpu
from jax.sharding import PartitionSpec as P

HEAD = 64
NS_STEPS = 5
NS_COEFS = (3.4445, -4.775, 2.0315)
STEP_SCALES = (0.8660254, 1.4142136, 1.0, 0.5, 0.5, 0.8660254)
MOMENT_DECAY = 0.95
GAIN_DECAY = 0.9
GAIN_RATE = 0.001
LN_EPS = 1e-05
NORM_EPS = 1e-07
MASKED = -1e30
HALO = 16
QB = 256
LANES = 128
VMEM_BYTES = 61 << 20
BF = jnp.bfloat16
F32 = jnp.float32
MESH = pl.DeviceIdType.MESH


def dot_nn(left, right):
    return lax.dot_general(left, right, (((1,), (0,)), ((), ())), preferred_element_type=F32)


def dot_nt(left, right):
    return lax.dot_general(left, right, (((1,), (1,)), ((), ())), preferred_element_type=F32)


def dot_tn(left, right):
    return lax.dot_general(left, right, (((0,), (0,)), ((), ())), preferred_element_type=F32)


def layer_norm(values, gain):
    mean = jnp.mean(values, axis=-1, keepdims=True)
    centred = values - mean
    spread = jnp.mean(centred * centred, axis=-1, keepdims=True)
    return centred * lax.rsqrt(spread + LN_EPS) * gain


def layer_norm_back(values, gain, grad):
    mean = jnp.mean(values, axis=-1, keepdims=True)
    centred = values - mean
    spread = jnp.mean(centred * centred, axis=-1, keepdims=True)
    scale = lax.rsqrt(spread + LN_EPS)
    unit = centred * scale
    scaled = grad * gain
    part = jnp.mean(scaled, axis=-1, keepdims=True)
    along = jnp.mean(scaled * unit, axis=-1, keepdims=True)
    return scale * (scaled - part - unit * along), grad * unit


def gelu(values):
    return 0.5 * values * (1.0 + jnp.tanh(0.7978845608028654 * (values + 0.044715 * values * values * values)))


def gelu_both(values):
    square = values * values
    turn = jnp.tanh(0.7978845608028654 * (values + 0.044715 * values * square))
    slope = 0.7978845608028654 * (1.0 + 3.0 * 0.044715 * square)
    half = 0.5 * (1.0 + turn)
    return values * half, half + 0.5 * values * (1.0 - turn * turn) * slope


def partner(values):
    width = values.shape[1]
    if width == LANES:
        lane = lax.broadcasted_iota(jnp.int32, values.shape, 1)
        ahead = pltpu.roll(values, LANES - HEAD // 2, 1)
        behind = pltpu.roll(values, HEAD // 2, 1)
        return jnp.where(lane % HEAD < HEAD // 2, ahead, behind)
    parts = []
    for at in range(0, width, HEAD):
        parts += [values[:, at + HEAD // 2 : at + HEAD], values[:, at : at + HEAD // 2]]
    return jnp.concatenate(parts, axis=1)


def widen(values):
    rows, width = values.shape
    if width >= LANES:
        return values
    return jnp.concatenate([values, jnp.zeros((rows, LANES - width), values.dtype)], axis=1)


def params():
    return pltpu.CompilerParams(vmem_limit_bytes=VMEM_BYTES)


def smem():
    return pl.BlockSpec(memory_space=pltpu.SMEM)


def vmem():
    return pl.BlockSpec(memory_space=pltpu.VMEM)


def hbm():
    return pl.BlockSpec(memory_space=pl.ANY)


def cost(flops, moved):
    return pl.CostEstimate(flops=int(flops), bytes_accessed=int(moved), transcendentals=0)


def local_kernel(body, name, outs, scratch, me, *arrays, flops=0):
    moved = sum(a.size * a.dtype.itemsize for a in arrays)
    moved += sum(int(np.prod(s)) * jnp.dtype(t).itemsize for s, t in outs)
    return pl.pallas_call(
        body,
        out_shape=[jax.ShapeDtypeStruct(s, t) for s, t in outs],
        in_specs=[smem()] + [vmem()] * len(arrays),
        out_specs=[vmem()] * len(outs),
        scratch_shapes=[pltpu.VMEM(s, t) for s, t in scratch],
        compiler_params=params(),
        cost_estimate=cost(flops, moved),
        name=name,
    )(me, *arrays)


def at_rows(me, step, rows):
    return pl.multiple_of((me ^ step) * rows, 16)


def head_inputs(qs, ks, rows, q, k, fq, fk, heads):
    lane = lax.broadcasted_iota(jnp.int32, (q.shape[0], LANES), 1)
    q, k = widen(q), widen(k)
    for h in range(heads):
        mine = lane // HEAD == h
        qs[h, rows, :] = jnp.where(mine, q * 0.125, fq).astype(BF)
        ks[h, rows, :] = jnp.where(mine, k, fk).astype(BF)


def scores_t(ks, qs, h, start, stop):
    top = dot_nt(ks[h, 0:stop, :], qs[h, start:stop, :])
    key = lax.broadcasted_iota(jnp.int32, (stop - start, stop - start), 0)
    query = lax.broadcasted_iota(jnp.int32, (stop - start, stop - start), 1)
    last = jnp.where(key <= query, top[start:, :], MASKED)
    if start == 0:
        return last
    return jnp.concatenate([top[:start, :], last], axis=0)


def spread_write(hold, values):
    for c in range(hold.shape[0]):
        hold[c] = values[:, c * LANES : (c + 1) * LANES]


def spread_read(hold):
    return jnp.concatenate([hold[c] for c in range(hold.shape[0])], axis=1)


def strided_read(hold, start, amount):
    return jnp.concatenate([hold[c, pl.ds(start, amount, stride=3), :] for c in range(hold.shape[0])], axis=1)


def strided_write(hold, start, amount, values):
    for c in range(hold.shape[0]):
        hold[c, pl.ds(start, amount, stride=3), :] = values[:, c * LANES : (c + 1) * LANES]


def flip(value, step):
    bit = 1
    while bit <= step:
        if step & bit:
            value = value + bit - 2 * bit * lax.rem(lax.div(value, bit), 2)
        bit *= 2
    return value


class Net:
    def __init__(self, send, recv):
        self.send, self.recv, self.used, self.open = send, recv, 0, []

    def make(self, src, dst, device):
        at = self.used
        self.used += 1
        return pltpu.make_async_remote_copy(
            src_ref=src,
            dst_ref=dst,
            send_sem=self.send.at[at],
            recv_sem=self.recv.at[at],
            device_id=device,
            device_id_type=MESH,
        )

    def start(self, src, dst, device):
        copy = self.make(src, dst, device)
        copy.start()
        self.open.append(copy)
        return copy

    def local(self, src, dst):
        at = self.used
        self.used += 1
        copy = pltpu.make_async_copy(src, dst, self.send.at[at])
        copy.start()
        return copy

    def finish(self):
        for copy in self.open:
            copy.wait_send()


class Flight:
    def __init__(self, net, dp, fs, fs_count, pieces, src):
        self.net, self.dp, self.fs, self.pieces = net, dp, fs, pieces
        self.top, self.copies, self.waited = fs_count // 2, {}, set()
        bit = self.top
        while bit:
            self.copies[bit] = net.start(src, pieces.at[bit], (dp, flip(fs, bit)))
            bit //= 2

    def ready(self, step):
        if step and step not in self.waited:
            self.waited.add(step)
            self.copies[step].wait_recv()

    def relay(self):
        known, bit = [self.top], self.top // 2
        while bit:
            fresh = []
            for step in known:
                self.ready(step)
                there = (self.dp, flip(self.fs, bit))
                self.copies[step + bit] = self.net.start(self.pieces.at[step], self.pieces.at[step + bit], there)
                fresh.append(step + bit)
            known = known + [bit] + fresh
            bit //= 2

    def all_ready(self):
        for step in sorted(self.copies):
            self.ready(step)


def doc_bounds(triples, docs):
    lane = lax.broadcasted_iota(jnp.int32, (1, LANES), 1)
    lane = jnp.where(lane >= HEAD, lane - HEAD, lane)
    first = jnp.full((1, LANES), -1, jnp.int32)
    end = jnp.full((1, LANES), -1, jnp.int32)
    at = jnp.int32(0)
    for j in range(docs):
        here = lane == j
        first = jnp.where(here, at, first)
        at = at + triples[0, j]
        end = jnp.where(here, at, end)
    return first, end, lane


def softmax_block(ks, qs, h, r, stop):
    s = scores_t(ks, qs, h, r, stop)
    e = jnp.exp(s - jnp.max(s, axis=0, keepdims=True))
    return e, 1.0 / jnp.sum(e, axis=0, keepdims=True)


def forward_one(y_count, dp_count, fs_count, tokens, cot, triples, weights, gains_t, cos, sin):
    rows, width = tokens.shape
    total, short = rows * fs_count, rows // 3
    long_rows = rows + HALO
    wqkv, wout, win, wdown, wpool, wup = weights
    rw = wqkv.shape[1]
    hd, fj, pc = wout.shape[2], win.shape[2], wpool.shape[1]
    heads = hd // HEAD
    docs = triples.shape[1]
    z_count = dp_count // y_count
    blk = QB
    sems = 96 + 16 * dp_count

    def body(
        tok, cot_ref, triples_ref, q_in, o_in, i_in, d_in, p_in, u_in, g_in, cos_ref, sin_ref,
        n1_hbm, qkv_hbm, att_hbm, wo_full, n2_hbm, hid_hbm, slope_hbm, mid, after, z_out, s0_out, wq_out, wi, wd, wp, wq1_out, wu, c_rel, gain_out,
        n1, qkv, att_rel, n2, hid0, slope0, toks, c_own, st_q, wq0, wq1, gall, wo, wo_at, att, qs, ks, vt, turned, hold, work, low, part, m_tail, part_tail,
        sbuf, rbuf, xsend, xrecv, acc, thin, send_sem, recv_sem,
    ):
        dp, fs = lax.axis_index("dp"), lax.axis_index("fsdp")
        net = Net(send_sem, recv_sem)

        def own(buf):
            return buf.at[pl.ds(pl.multiple_of(dp * rw, 16), rw), :]

        def of(buf, step):
            return buf.at[pl.ds(pl.multiple_of(flip(dp, step) * rw, 16), rw), :]

        for b in range(2):
            for t in range(3):
                st_q[b, t] = q_in[b, :, t * hd : (t + 1) * hd].astype(BF)
        here = pl.ds(pl.multiple_of(dp * rw, 16), rw)
        wide_gain = jnp.concatenate([g_in[...], jnp.zeros((LANES - 4, rw), F32)], axis=0).T
        gall[here, :] = wide_gain.astype(BF)
        wo[0, here, :] = o_in[0].astype(BF)
        wi[here, :] = i_in[0].astype(BF)
        wd[here, :] = d_in[0].astype(BF)
        wp[0, here, :] = p_in[...].astype(BF)
        wu[here, :] = u_in[...].astype(BF)

        barrier = pltpu.get_barrier_semaphore()
        for m in range(z_count):
            for e in range(fs_count):
                if m or e:
                    there = (flip(dp, m * y_count), flip(fs, e))
                    pl.semaphore_signal(barrier, inc=1, device_id=there, device_id_type=MESH)
        for j in range(1, y_count):
            pl.semaphore_signal(barrier, inc=1, device_id=(flip(dp, j), fs), device_id_type=MESH)
        pl.semaphore_wait(barrier, z_count * fs_count - 1 + y_count - 1)

        def along_z(bufs):
            found = [[] for _ in range(z_count)]
            for m in range(1, z_count):
                for buf in bufs:
                    found[m].append(net.start(own(buf), own(buf), (flip(dp, m * y_count), fs)))
            return found

        def along_y(bufs, m):
            return [
                net.start(of(buf, m * y_count), of(buf, m * y_count), (flip(dp, j), fs))
                for j in range(1, y_count)
                for buf in bufs
            ]

        def wait_all(copies):
            for copy in copies:
                copy.wait_recv()

        def heads_along_z(b, wq):
            found = []
            for m in range(z_count):
                line = []
                for t in range(3):
                    place = 3 * fs + t
                    kind, to = lax.div(place, fs_count), lax.rem(place, fs_count)
                    copy = net.make(st_q.at[b, t], wq.at[kind, here, :], (flip(dp, m * y_count), to))
                    if m == 0:

                        @pl.when(to != fs)
                        def _():
                            copy.start()

                        @pl.when(to == fs)
                        def _():
                            wq[kind, here, :] = st_q[b, t]

                        line.append((copy, to != fs))
                    else:
                        copy.start()
                        net.open.append(copy)
                        line.append((copy, None))
                found.append(line)
            return found

        def heads_along_y(wq, line, m):
            for copy, when in line:
                if when is None:
                    copy.wait_recv()
                else:

                    @pl.when(when)
                    def _():
                        copy.wait_recv()
                        copy.wait_send()

            at = pl.ds(pl.multiple_of(flip(dp, m * y_count) * rw, 16), rw)
            return [
                net.start(wq.at[:, at, :], wq.at[:, at, :], (flip(dp, j), fs)) for j in range(1, y_count)
            ]


        def spread(pieces, src):
            return Flight(net, dp, fs, fs_count, pieces, src)

        heads0 = heads_along_z(0, wq0)
        gz = along_z([gall])
        y0 = along_y([gall], 0)
        thirds = [slice(n * short, (n + 1) * short) for n in range(3)]
        tks = [spread(toks.at[:, third, :], tok.at[third, :]) for third in thirds]
        toks[0] = tok[...]
        zs = {}
        zs["wo"] = along_z([wo.at[0]])
        zs["wi"] = along_z([wi])
        ys = {"wo": along_y([wo.at[0]], 0), "wi": along_y([wi], 0)}
        spread_write(thin.at[:, 0:rows, :], cot_ref[...].astype(F32))
        lifted = jnp.concatenate([strided_read(thin, n, short) for n in range(3)], axis=1).astype(BF)
        for e in range(fs_count):
            c_own[e] = lifted[:, e * pc : (e + 1) * pc]
        c_rel[0] = c_own[fs]
        c_f = [
            net.start(c_own.at[flip(fs, e)], c_rel.at[e], (dp, flip(fs, e))) for e in range(1, fs_count)
        ]
        lane_first, lane_end, lane = doc_bounds(triples_ref, docs)
        for m in range(z_count):
            y0 += heads_along_y(wq0, heads0[m], m)
            if m:
                wait_all(gz[m])
                y0 += along_y([gall], m)
        zs["wp"] = along_z([wp.at[0]])
        zs["wd"] = along_z([wd])
        ys["wp"] = along_y([wp.at[0]], 0)
        ys["wd"] = along_y([wd], 0)

        def pass_on(name, bufs):
            for m in range(1, z_count):
                wait_all(zs[name][m])
                ys[name] += along_y(bufs, m)

        pass_on("wo", [wo.at[0]])
        heads1 = heads_along_z(1, wq1)
        zs["wu"] = along_z([wu])
        wait_all(y0)
        gain_rows = gall[...].astype(F32).T[0:8, :]
        gain_out[...] = gain_rows
        for t in range(3):
            wq_out[:, t * hd : (t + 1) * hd] = wq0[t]

        def to_heads(e, first, amount):
            base = pl.multiple_of(flip(fs, e) * rows + first, 16)
            for r in range(0, amount, LANES):
                block = toks[e, first + r : first + r + LANES, :].astype(F32)
                n1[pl.ds(base + r, LANES), :] = layer_norm(block, gain_rows[0:1]).astype(BF)
            at = pl.ds(base, amount)
            got = dot_nn(n1[at, :], wq_out[...])
            q, k, v = got[:, :hd], got[:, hd : 2 * hd], got[:, 2 * hd :]
            q = (q * cos_ref[at, :] + partner(q) * sin_ref[at, :]).astype(BF)
            k = (k * cos_ref[at, :] + partner(k) * sin_ref[at, :]).astype(BF)
            qkv[at, 0:hd] = q
            qkv[at, hd : 2 * hd] = k
            qkv[at, 2 * hd : 3 * hd] = v.astype(BF)
            row = lax.broadcasted_iota(jnp.int32, (amount, LANES), 0) + base
            inside = (row >= 3 * lane_first) & (row < 3 * lane_end)
            fk = jnp.where(inside, 1.0, 0.0)
            fq = jnp.where(inside | (lane >= docs), 0.0, MASKED)
            head_inputs(qs, ks, at, q.astype(F32), k.astype(F32), fq, fk, heads)

        to_heads(0, 0, rows)
        for tk in tks:
            tk.ready(1)
        to_heads(1, 0, rows)
        for n, tk in enumerate(tks):
            tk.relay()
            for e in range(2, fs_count):
                tk.ready(e)
                to_heads(e, n * short, short)
        for r in range(0, total, blk):
            at = slice(r, r + blk)
            vt[:, at] = qkv[at, 2 * hd : 3 * hd].astype(F32).T.astype(BF)
        stores = [net.local(n1, n1_hbm)]
        stores.append(net.local(qkv, qkv_hbm))

        flights = []
        for n, r in enumerate(range(0, total, blk)):
            stop = r + blk
            found = []
            for h in range(heads):
                e, inv = softmax_block(ks, qs, h, r, stop)
                found.append(dot_nn(vt[h * HEAD : (h + 1) * HEAD, 0:stop], e.astype(BF)) * inv)
            att[0, r:stop, :] = jnp.concatenate(found, axis=0).T.astype(BF)
            flights.append(spread(att.at[:, r:stop, :], att.at[0, r:stop, :]))
            if n == 0:
                wait_all(ys["wo"])
                wo_f = spread(wo, wo.at[0])
            if n == 1:
                pass_on("wi", [wi])
            if n == 3:
                pass_on("wp", [wp.at[0]])
                wo_f.relay()
            if n == 5:
                pass_on("wd", [wd])
                ys["wu"] = along_y([wu], 0)
            if n >= 2:
                flights[n - 2].relay()
        for flight in flights[-2:]:
            flight.relay()
        wait_all(ys["wp"])
        wp_f = spread(wp, wp.at[0])
        ys["heads1"] = []
        for m in range(z_count):
            ys["heads1"] += heads_along_y(wq1, heads1[m], m)
        wo_f.all_ready()
        for e in range(fs_count):
            wo_at[flip(fs, e)] = wo[e]
        for e in range(fs_count):
            hold[:, e * hd : (e + 1) * hd] = wo_at[e]
        for e in range(fs_count):
            base = pl.multiple_of(flip(fs, e) * hd, 16)
            turned[e * hd : (e + 1) * hd, :] = hold[pl.ds(base, hd), :]
        wo_full[...] = hold[...]
        for flight in flights:
            flight.all_ready()
        wait_all(ys["wi"])
        wait_all(ys["wd"])

        def mix(x_block, o_block, amount, keep_mid, keep, out):
            work[0:amount, 0:width] = x_block.astype(F32) + dot_nn(o_block, turned[...])
            for r in range(0, amount, HEAD):
                m = work[r : r + HEAD, 0:width]
                if keep_mid is not None:
                    keep_mid[r : r + HEAD, :] = m
                value = layer_norm(m, gain_rows[1:2]).astype(BF)
                low[r : r + HEAD, 0:width] = value
                if keep is not None:
                    n2[keep + r : keep + r + HEAD, :] = value
            work[0:amount, 0:fj] = dot_nn(low[0:amount, 0:width], wi[...])
            for r in range(0, amount, HEAD):
                if keep is None:
                    low[r : r + HEAD, 0:fj] = gelu(work[r : r + HEAD, 0:fj]).astype(BF)
                    continue
                value, rate = gelu_both(work[r : r + HEAD, 0:fj])
                low[r : r + HEAD, 0:fj] = value.astype(BF)
                hid0[keep + r : keep + r + HEAD, :] = value.astype(BF)
                slope0[keep + r : keep + r + HEAD, :] = rate.astype(BF)
            out[0:amount, :] = dot_nt(low[0:amount, 0:fj], wd[...])

        for e in range(fs_count):
            at = pl.ds(pl.multiple_of(flip(fs, e) * rows + rows - HALO, 16), HALO)
            for k in range(fs_count):
                att_rel[e * HALO : (e + 1) * HALO, k * hd : (k + 1) * hd] = att[k, at, :]
        tails = jnp.concatenate([toks[e, rows - HALO : rows, :] for e in range(fs_count)], axis=0)
        mix(tails, att_rel[0 : fs_count * HALO, :], fs_count * HALO, m_tail, None, part_tail)

        for e in range(fs_count):
            base = pl.multiple_of(flip(fs, e) * rows, 16)
            for k in range(fs_count):
                att_rel[pl.ds(base, rows), k * hd : (k + 1) * hd] = att[k, pl.ds(base, rows), :]

        def before(e):
            place = flip(fs, e) + fs_count - 1
            place = lax.rem(place, fs_count)
            apart = jnp.int32(0)
            bit = 1
            while bit < fs_count:
                one = lax.rem(lax.div(place, bit), 2)
                two = lax.rem(lax.div(fs, bit), 2)
                apart = apart + bit * lax.rem(one + two, 2)
                bit *= 2
            return pl.multiple_of(apart * HALO, 16)

        def partial_for(e, out):
            base = pl.multiple_of(flip(fs, e) * rows, 16)
            mix(
                toks[e],
                att_rel[pl.ds(base, rows), :],
                rows,
                mid if e == 0 else None,
                e * rows,
                part,
            )
            out[0:HALO, :] = part_tail[pl.ds(before(e), HALO), :].astype(out.dtype)
            out[HALO:long_rows, :] = part[0:rows, :].astype(out.dtype)

        stores.append(net.local(att_rel, att_hbm))
        half = fs_count // 2
        first_hops = {}
        for j in reversed(range(half)):
            partial_for(2 * j + 1, sbuf.at[j])
            first_hops[j] = net.start(sbuf.at[j], rbuf.at[j], (dp, flip(fs, 1)))
            if j == half - 1:
                pass_on("wu", [wu])
            if j:
                partial_for(2 * j, acc.at[j])
                first_hops[j].wait_recv()
                acc[j] = acc[j] + rbuf[j].astype(F32)
                if half == 2:
                    xsend[0] = acc[1].astype(BF)
                    last_hop = net.start(xsend.at[0], xrecv.at[0], (dp, flip(fs, 2)))
            if j == half - 1:
                wp_f.relay()
        partial_for(0, acc.at[0])
        first_hops[0].wait_recv()
        acc[0] = acc[0] + rbuf[0].astype(F32)
        if half > 2:
            bit, active = 2, list(range(half))
            slot = 0
            while bit < fs_count:
                stay = [j for j in active if not (2 * j) & bit]
                hops = {}
                for j in stay:
                    give = j + bit // 2
                    xsend[slot] = acc[give].astype(BF)
                    hops[j] = (net.start(xsend.at[slot], xrecv.at[slot], (dp, flip(fs, bit))), slot)
                    slot += 1
                for j in stay:
                    hops[j][0].wait_recv()
                    acc[j] = acc[j] + xrecv[hops[j][1]].astype(F32)
                active, bit = stay, bit * 2
        elif half == 2:
            last_hop.wait_recv()
            acc[0] = acc[0] + xrecv[0].astype(F32)
        a_tail = acc[0, 0:HALO, :] + m_tail[pl.ds(before(0), HALO), :]
        a_own = acc[0, HALO:long_rows, :] + mid[...]
        after[...] = a_own
        for c in range(width // LANES):
            thin[c, 0:HALO, :] = a_tail[:, c * LANES : (c + 1) * LANES]
            thin[c, HALO:long_rows, :] = a_own[:, c * LANES : (c + 1) * LANES]

        stores.append(net.local(n2, n2_hbm))
        stores.append(net.local(hid0, hid_hbm))
        stores.append(net.local(slope0, slope_hbm))

        row = lax.broadcasted_iota(jnp.int32, (short, LANES), 0) + fs * short
        begins = jnp.max(jnp.where(row == lane_first, 1.0, 0.0), axis=1, keepdims=True)
        parts = []
        for k in range(3):
            value = strided_read(thin, HALO - 2 + k, short)
            parts.append(jnp.where(begins > 0.0, 0.0, value) if k < 2 else value)
        z = jnp.concatenate(parts, axis=1).astype(BF)
        for e in range(fs_count):
            z_out[e] = z[:, e * pc : (e + 1) * pc]
        pooled = jnp.zeros((short, width), F32)
        for e in range(fs_count):
            wp_f.ready(e)
            pooled = pooled + dot_nt(z_out[flip(fs, e)], wp[e])
        s0_out[...] = pooled
        for name in ("heads1", "wu"):
            wait_all(ys[name])
        wait_all(c_f)
        for t in range(3):
            wq1_out[:, t * hd : (t + 1) * hd] = wq1[t]
        for copy in stores:
            copy.wait()
        net.finish()

    half = fs_count // 2
    outs = [
        ((total, width), BF),
        ((total, 3 * hd), BF),
        ((total, width), BF),
        ((width, width), BF),
        ((total, width), BF),
        ((total, fj), BF),
        ((total, fj), BF),
        ((rows, width), F32),
        ((rows, width), F32),
        ((fs_count, short, pc), BF),
        ((short, width), F32),
        ((width, 3 * hd), BF),
        ((width, fj), BF),
        ((width, fj), BF),
        ((fs_count, width, pc), BF),
        ((width, 3 * hd), BF),
        ((width, pc), BF),
        ((fs_count, short, pc), BF),
        ((8, width), F32),
    ]
    wide = max(width, fj)
    scratch = [
        ((total, width), BF),
        ((total, 3 * hd), BF),
        ((total, width), BF),
        ((total, width), BF),
        ((total, fj), BF),
        ((total, fj), BF),
        ((fs_count, rows, width), BF),
        ((fs_count, short, pc), BF),
        ((2, 3, rw, hd), BF),
        ((3, width, hd), BF),
        ((3, width, hd), BF),
        ((width, LANES), BF),
        ((fs_count, width, hd), BF),
        ((fs_count, width, hd), BF),
        ((fs_count, total, hd), BF),
        ((heads, total, LANES), BF),
        ((heads, total, LANES), BF),
        ((hd, total), BF),
        ((width, width), BF),
        ((width, width), BF),
        ((rows, wide), F32),
        ((rows, wide), BF),
        ((rows, width), F32),
        ((fs_count * HALO, width), F32),
        ((fs_count * HALO, width), F32),
        ((half, long_rows, width), BF),
        ((half, long_rows, width), BF),
        ((half - 1, long_rows, width), BF),
        ((half - 1, long_rows, width), BF),
        ((half, long_rows, width), F32),
        ((width // LANES, long_rows, LANES), F32),
    ]
    return pl.pallas_call(
        body,
        out_shape=[jax.ShapeDtypeStruct(s, t) for s, t in outs],
        in_specs=[vmem(), vmem(), smem()] + [vmem()] * 9,
        out_specs=[hbm() if n in (0, 1, 2, 4, 5, 6) else vmem() for n in range(len(outs))],
        scratch_shapes=[pltpu.VMEM(s, t) for s, t in scratch] + [pltpu.SemaphoreType.DMA((sems,))] * 2,
        compiler_params=pltpu.CompilerParams(collective_id=3, has_side_effects=True, vmem_limit_bytes=VMEM_BYTES),
        cost_estimate=cost(2e10, 3e7),
        name="forward_one",
    )(tokens, cot, triples, *weights, gains_t, cos, sin)


def forward_all(y_count, dp_count, fs_count, tokens, cot, triples, weights, gains_t, cos, sin):
    rows, width = tokens.shape
    total, short = rows * fs_count, rows // 3
    long_rows = rows + HALO
    wqkv, wout, win, wdown, wpool, wup = weights
    rw = wqkv.shape[1]
    hd, fj, pc = wout.shape[2], win.shape[2], wpool.shape[1]
    heads = hd // HEAD
    docs = triples.shape[1]
    z_count = dp_count // y_count
    blk = query_rows(total)
    total_b = short * fs_count
    blk_b = min(QB, total_b)
    blocks_b, half = total_b // blk_b, fs_count // 2
    cb = 4 * hd + 2 * pc
    sems = 192 + 22 * dp_count + 16 * fs_count

    def body(
        tok, cot_ref, triples_ref, q_in, o_in, i_in, d_in, p_in, u_in, g_in, cos_ref, sin_ref,
        n1_hbm, qkv_hbm, att_hbm, n2_hbm, hid_hbm, slope_hbm, wo_full, mid, wq_out, wi, wd, gain_out, out, da, dfs_out, group, sum_ff, dgain,
        after, z_out, s0_out, wp, wq1_out, wu, c_rel,
        n1, qkv, att_rel, n2, hid0, slope0, toks, c_own, st_q, wq0, wq1, gall, wo, wo_at, att, qs, ks, vt, turned, hold, work, low, part, m_tail, part_tail, sbuf, rbuf, xsend, xrecv, acc, thin,
        b_wos, b_wi_ref, b_wd_ref, b_g_ff, b_yg, b_zsg, b_zrg, b_sd, b_rd, b_xd, b_yd, b_ad, b_lift_send, b_lift_rel, b_s0s, b_x_all, b_wo_at, b_hold, b_turned, b_z_rel, b_dfs, b_df_all, b_do_out, b_do_in, b_da_out, b_da_in, b_cols, b_s1s, b_ds0s, b_nxt, b_n1, b_n2, b_qkv, b_att, b_att_rel, b_qs, b_ks, b_vt, b_kt, b_dk, b_dv, b_dqkv, b_work, b_hid, b_slope, b_dpre, b_m_all, b_dm, b_sf, b_rf, b_xf, b_yf, b_af, b_sb, b_rb, b_xb, b_yb, b_ab, b_sa, b_ra, b_xa, b_ya, b_aa, b_thin, b_spread_rows, b_lift,
        send_sem, recv_sem, *ps,
    ):
        dp, fs = lax.axis_index("dp"), lax.axis_index("fsdp")
        net = Net(send_sem, recv_sem)

        def own(buf):
            return buf.at[pl.ds(pl.multiple_of(dp * rw, 16), rw), :]

        def of(buf, step):
            return buf.at[pl.ds(pl.multiple_of(flip(dp, step) * rw, 16), rw), :]

        for b in range(2):
            for t in range(3):
                st_q[b, t] = q_in[b, :, t * hd : (t + 1) * hd].astype(BF)
        here = pl.ds(pl.multiple_of(dp * rw, 16), rw)
        wide_gain = jnp.concatenate([g_in[...], jnp.zeros((LANES - 4, rw), F32)], axis=0).T
        gall[here, :] = wide_gain.astype(BF)
        wo[0, here, :] = o_in[0].astype(BF)
        wi[here, :] = i_in[0].astype(BF)
        wd[here, :] = d_in[0].astype(BF)
        wp[0, here, :] = p_in[...].astype(BF)
        wu[here, :] = u_in[...].astype(BF)
        b_wos[0, here, :] = o_in[1].astype(BF)
        b_wi_ref[here, :] = i_in[1].astype(BF)
        b_wd_ref[here, :] = d_in[1].astype(BF)

        barrier = pltpu.get_barrier_semaphore()
        for m in range(z_count):
            for e in range(fs_count):
                if m or e:
                    there = (flip(dp, m * y_count), flip(fs, e))
                    pl.semaphore_signal(barrier, inc=1, device_id=there, device_id_type=MESH)
        for j in range(1, y_count):
            pl.semaphore_signal(barrier, inc=1, device_id=(flip(dp, j), fs), device_id_type=MESH)
        pl.semaphore_wait(barrier, z_count * fs_count - 1 + y_count - 1)

        def along_z(bufs):
            found = [[] for _ in range(z_count)]
            for m in range(1, z_count):
                for buf in bufs:
                    found[m].append(net.start(own(buf), own(buf), (flip(dp, m * y_count), fs)))
            return found

        def along_y(bufs, m):
            return [
                net.start(of(buf, m * y_count), of(buf, m * y_count), (flip(dp, j), fs))
                for j in range(1, y_count)
                for buf in bufs
            ]

        def wait_all(copies):
            for copy in copies:
                copy.wait_recv()

        def heads_along_z(b, wq):
            found = []
            for m in range(z_count):
                line = []
                for t in range(3):
                    place = 3 * fs + t
                    kind, to = lax.div(place, fs_count), lax.rem(place, fs_count)
                    copy = net.make(st_q.at[b, t], wq.at[kind, here, :], (flip(dp, m * y_count), to))
                    if m == 0:

                        @pl.when(to != fs)
                        def _():
                            copy.start()

                        @pl.when(to == fs)
                        def _():
                            wq[kind, here, :] = st_q[b, t]

                        line.append((copy, to != fs))
                    else:
                        copy.start()
                        net.open.append(copy)
                        line.append((copy, None))
                found.append(line)
            return found

        def heads_along_y(wq, line, m):
            for copy, when in line:
                if when is None:
                    copy.wait_recv()
                else:

                    @pl.when(when)
                    def _():
                        copy.wait_recv()
                        copy.wait_send()

            at = pl.ds(pl.multiple_of(flip(dp, m * y_count) * rw, 16), rw)
            return [
                net.start(wq.at[:, at, :], wq.at[:, at, :], (flip(dp, j), fs)) for j in range(1, y_count)
            ]


        def spread(pieces, src):
            return Flight(net, dp, fs, fs_count, pieces, src)

        heads0 = heads_along_z(0, wq0)
        gz = along_z([gall])
        y0 = along_y([gall], 0)
        thirds = [slice(n * short, (n + 1) * short) for n in range(3)]
        tks = [spread(toks.at[:, third, :], tok.at[third, :]) for third in thirds]
        toks[0] = tok[...]
        zs = {}
        zs["wo"] = along_z([wo.at[0]])
        zs["wi"] = along_z([wi])
        ys = {"wo": along_y([wo.at[0]], 0), "wi": along_y([wi], 0)}
        spread_write(thin.at[:, 0:rows, :], cot_ref[...].astype(F32))
        lifted = jnp.concatenate([strided_read(thin, n, short) for n in range(3)], axis=1).astype(BF)
        for e in range(fs_count):
            c_own[e] = lifted[:, e * pc : (e + 1) * pc]
        c_rel[0] = c_own[fs]
        c_f = [
            net.start(c_own.at[flip(fs, e)], c_rel.at[e], (dp, flip(fs, e))) for e in range(1, fs_count)
        ]
        lane_first, lane_end, lane = doc_bounds(triples_ref, docs)
        for m in range(z_count):
            y0 += heads_along_y(wq0, heads0[m], m)
            if m:
                wait_all(gz[m])
                y0 += along_y([gall], m)
        zs["wp"] = along_z([wp.at[0]])
        zs["wd"] = along_z([wd])
        ys["wp"] = along_y([wp.at[0]], 0)
        ys["wd"] = along_y([wd], 0)

        def pass_on(name, bufs):
            for m in range(1, z_count):
                wait_all(zs[name][m])
                ys[name] += along_y(bufs, m)

        pass_on("wo", [wo.at[0]])
        heads1 = heads_along_z(1, wq1)
        zs["wu"] = along_z([wu])
        later = (b_wos.at[0], b_wi_ref, b_wd_ref)
        came = [[line[0] for line in along_z([buf])[1:]] for buf in later]
        wait_all(y0)
        gain_rows = gall[...].astype(F32).T[0:8, :]
        gain_out[...] = gain_rows
        for t in range(3):
            wq_out[:, t * hd : (t + 1) * hd] = wq0[t]

        def to_heads(e, first, amount):
            base = pl.multiple_of(flip(fs, e) * rows + first, 16)
            for r in range(0, amount, LANES):
                block = toks[e, first + r : first + r + LANES, :].astype(F32)
                n1[pl.ds(base + r, LANES), :] = layer_norm(block, gain_rows[0:1]).astype(BF)
            at = pl.ds(base, amount)
            got = dot_nn(n1[at, :], wq_out[...])
            q, k, v = got[:, :hd], got[:, hd : 2 * hd], got[:, 2 * hd :]
            q = (q * cos_ref[at, :] + partner(q) * sin_ref[at, :]).astype(BF)
            k = (k * cos_ref[at, :] + partner(k) * sin_ref[at, :]).astype(BF)
            qkv[at, 0:hd] = q
            qkv[at, hd : 2 * hd] = k
            qkv[at, 2 * hd : 3 * hd] = v.astype(BF)
            row = lax.broadcasted_iota(jnp.int32, (amount, LANES), 0) + base
            inside = (row >= 3 * lane_first) & (row < 3 * lane_end)
            fk = jnp.where(inside, 1.0, 0.0)
            fq = jnp.where(inside | (lane >= docs), 0.0, MASKED)
            head_inputs(qs, ks, at, q.astype(F32), k.astype(F32), fq, fk, heads)

        to_heads(0, 0, rows)
        for tk in tks:
            tk.ready(1)
        to_heads(1, 0, rows)
        for n, tk in enumerate(tks):
            tk.relay()
            for e in range(2, fs_count):
                tk.ready(e)
                to_heads(e, n * short, short)
        for r in range(0, total, blk):
            at = slice(r, r + blk)
            vt[:, at] = qkv[at, 2 * hd : 3 * hd].astype(F32).T.astype(BF)
        stores = [net.local(n1, n1_hbm)]
        stores.append(net.local(qkv, qkv_hbm))

        flights = []
        for n, r in enumerate(range(0, total, blk)):
            stop = r + blk
            found = []
            for h in range(heads):
                e, inv = softmax_block(ks, qs, h, r, stop)
                found.append(dot_nn(vt[h * HEAD : (h + 1) * HEAD, 0:stop], e.astype(BF)) * inv)
            att[0, r:stop, :] = jnp.concatenate(found, axis=0).T.astype(BF)
            flights.append(spread(att.at[:, r:stop, :], att.at[0, r:stop, :]))
            if n == 0:
                wait_all(ys["wo"])
                wo_f = spread(wo, wo.at[0])
            if n == 1:
                pass_on("wi", [wi])
            if n == 3:
                pass_on("wp", [wp.at[0]])
                wo_f.relay()
            if n == 5:
                pass_on("wd", [wd])
                ys["wu"] = along_y([wu], 0)
                passed = [along_y([buf], 0) for buf in later]
            if n >= 2:
                flights[n - 2].relay()
        for flight in flights[-2:]:
            flight.relay()
        wait_all(ys["wp"])
        wp_f = spread(wp, wp.at[0])
        ys["heads1"] = []
        for m in range(z_count):
            ys["heads1"] += heads_along_y(wq1, heads1[m], m)
        wo_f.all_ready()
        for e in range(fs_count):
            wo_at[flip(fs, e)] = wo[e]
        for e in range(fs_count):
            hold[:, e * hd : (e + 1) * hd] = wo_at[e]
        for e in range(fs_count):
            base = pl.multiple_of(flip(fs, e) * hd, 16)
            turned[e * hd : (e + 1) * hd, :] = hold[pl.ds(base, hd), :]
        wo_full[...] = hold[...]
        for flight in flights:
            flight.all_ready()
        wait_all(ys["wi"])
        wait_all(ys["wd"])

        def mix(x_block, o_block, amount, keep_mid, keep, out):
            work[0:amount, 0:width] = x_block.astype(F32) + dot_nn(o_block, turned[...])
            for r in range(0, amount, HEAD):
                m = work[r : r + HEAD, 0:width]
                if keep_mid is not None:
                    keep_mid[r : r + HEAD, :] = m
                value = layer_norm(m, gain_rows[1:2]).astype(BF)
                low[r : r + HEAD, 0:width] = value
                if keep is not None:
                    n2[keep + r : keep + r + HEAD, :] = value
            work[0:amount, 0:fj] = dot_nn(low[0:amount, 0:width], wi[...])
            for r in range(0, amount, HEAD):
                if keep is None:
                    low[r : r + HEAD, 0:fj] = gelu(work[r : r + HEAD, 0:fj]).astype(BF)
                    continue
                value, rate = gelu_both(work[r : r + HEAD, 0:fj])
                low[r : r + HEAD, 0:fj] = value.astype(BF)
                hid0[keep + r : keep + r + HEAD, :] = value.astype(BF)
                slope0[keep + r : keep + r + HEAD, :] = rate.astype(BF)
            out[0:amount, :] = dot_nt(low[0:amount, 0:fj], wd[...])

        for e in range(fs_count):
            at = pl.ds(pl.multiple_of(flip(fs, e) * rows + rows - HALO, 16), HALO)
            for k in range(fs_count):
                att_rel[e * HALO : (e + 1) * HALO, k * hd : (k + 1) * hd] = att[k, at, :]
        tails = jnp.concatenate([toks[e, rows - HALO : rows, :] for e in range(fs_count)], axis=0)
        mix(tails, att_rel[0 : fs_count * HALO, :], fs_count * HALO, m_tail, None, part_tail)

        for e in range(fs_count):
            base = pl.multiple_of(flip(fs, e) * rows, 16)
            for k in range(fs_count):
                att_rel[pl.ds(base, rows), k * hd : (k + 1) * hd] = att[k, pl.ds(base, rows), :]

        def before(e):
            place = flip(fs, e) + fs_count - 1
            place = lax.rem(place, fs_count)
            apart = jnp.int32(0)
            bit = 1
            while bit < fs_count:
                one = lax.rem(lax.div(place, bit), 2)
                two = lax.rem(lax.div(fs, bit), 2)
                apart = apart + bit * lax.rem(one + two, 2)
                bit *= 2
            return pl.multiple_of(apart * HALO, 16)

        def partial_for(e, out):
            base = pl.multiple_of(flip(fs, e) * rows, 16)
            mix(
                toks[e],
                att_rel[pl.ds(base, rows), :],
                rows,
                mid if e == 0 else None,
                e * rows,
                part,
            )
            out[0:HALO, :] = part_tail[pl.ds(before(e), HALO), :].astype(out.dtype)
            out[HALO:long_rows, :] = part[0:rows, :].astype(out.dtype)

        stores.append(net.local(att_rel, att_hbm))
        first_hops = {}
        for j in reversed(range(half)):
            partial_for(2 * j + 1, sbuf.at[j])
            first_hops[j] = net.start(sbuf.at[j], rbuf.at[j], (dp, flip(fs, 1)))
            if j == half - 1:
                pass_on("wu", [wu])
            if j:
                partial_for(2 * j, acc.at[j])
                first_hops[j].wait_recv()
                acc[j] = acc[j] + rbuf[j].astype(F32)
                if half == 2:
                    xsend[0] = acc[1].astype(BF)
                    last_hop = net.start(xsend.at[0], xrecv.at[0], (dp, flip(fs, 2)))
            if j == half - 1:
                wp_f.relay()
        partial_for(0, acc.at[0])
        first_hops[0].wait_recv()
        acc[0] = acc[0] + rbuf[0].astype(F32)
        if half > 2:
            bit, active = 2, list(range(half))
            slot = 0
            while bit < fs_count:
                stay = [j for j in active if not (2 * j) & bit]
                hops = {}
                for j in stay:
                    give = j + bit // 2
                    xsend[slot] = acc[give].astype(BF)
                    hops[j] = (net.start(xsend.at[slot], xrecv.at[slot], (dp, flip(fs, bit))), slot)
                    slot += 1
                for j in stay:
                    hops[j][0].wait_recv()
                    acc[j] = acc[j] + xrecv[hops[j][1]].astype(F32)
                active, bit = stay, bit * 2
        elif half == 2:
            last_hop.wait_recv()
            acc[0] = acc[0] + xrecv[0].astype(F32)
        a_tail = acc[0, 0:HALO, :] + m_tail[pl.ds(before(0), HALO), :]
        a_own = acc[0, HALO:long_rows, :] + mid[...]
        after[...] = a_own
        for c in range(width // LANES):
            thin[c, 0:HALO, :] = a_tail[:, c * LANES : (c + 1) * LANES]
            thin[c, HALO:long_rows, :] = a_own[:, c * LANES : (c + 1) * LANES]

        stores.append(net.local(n2, n2_hbm))
        stores.append(net.local(hid0, hid_hbm))
        stores.append(net.local(slope0, slope_hbm))

        row = lax.broadcasted_iota(jnp.int32, (short, LANES), 0) + fs * short
        begins = jnp.max(jnp.where(row == lane_first, 1.0, 0.0), axis=1, keepdims=True)
        parts = []
        for k in range(3):
            value = strided_read(thin, HALO - 2 + k, short)
            parts.append(jnp.where(begins > 0.0, 0.0, value) if k < 2 else value)
        z = jnp.concatenate(parts, axis=1).astype(BF)
        for e in range(fs_count):
            z_out[e] = z[:, e * pc : (e + 1) * pc]
        pooled = jnp.zeros((short, width), F32)
        for e in range(fs_count):
            wp_f.ready(e)
            pooled = pooled + dot_nt(z_out[flip(fs, e)], wp[e])
        s0_out[...] = pooled
        for name in ("heads1", "wu"):
            wait_all(ys[name])
        wait_all(c_f)
        for t in range(3):
            wq1_out[:, t * hd : (t + 1) * hd] = wq1[t]
        (wos, wi_ref, wd_ref, g_ff, yg, zsg, zrg, sd, rd, xd, yd, ad, lift_send, lift_rel, s0s, x_all, wo_at, hold, turned, z_rel, dfs, df_all, do_out, do_in, da_out, da_in, cols, s1s, ds0s, nxt, n1, n2, qkv, att, att_rel, qs, ks, vt, kt, dk, dv, dqkv, work, hid, slope, dpre, m_all, dm, sf, rf, xf, yf, af, sb, rb, xb, yb, ab, sa, ra, xa, ya, aa, thin, spread_rows, lift) = (
            b_wos, b_wi_ref, b_wd_ref, b_g_ff, b_yg, b_zsg, b_zrg, b_sd, b_rd, b_xd, b_yd, b_ad, b_lift_send, b_lift_rel, b_s0s, b_x_all, b_wo_at, b_hold, b_turned, b_z_rel, b_dfs, b_df_all, b_do_out, b_do_in, b_da_out, b_da_in, b_cols, b_s1s, b_ds0s, b_nxt, b_n1, b_n2, b_qkv, b_att, b_att_rel, b_qs, b_ks, b_vt, b_kt, b_dk, b_dv, b_dqkv, b_work, b_hid, b_slope, b_dpre, b_m_all, b_dm, b_sf, b_rf, b_xf, b_yf, b_af, b_sb, b_rb, b_xb, b_yb, b_ab, b_sa, b_ra, b_xa, b_ya, b_aa, b_thin, b_spread_rows, b_lift
        )
        def base_of(e, amount):
            return pl.multiple_of(flip(fs, e) * amount, 16)

        def spread(pieces, src=None):
            return Flight(net, dp, fs, fs_count, pieces, pieces.at[0] if src is None else src)

        s0s[0] = s0_out[...].astype(BF)
        nxt[...] = jnp.zeros(nxt.shape, BF)
        here = pl.ds(pl.multiple_of(dp * rw, 16), rw)
        def of(buf, step):
            return buf.at[pl.ds(pl.multiple_of(flip(dp, step) * rw, 16), rw), :]

        def along_z(buf):
            return [
                net.start(of(buf, 0), of(buf, 0), (flip(dp, m * y_count), fs)) for m in range(1, z_count)
            ]

        def along_y(buf, m):
            return [
                net.start(of(buf, m * y_count), of(buf, m * y_count), (flip(dp, n), fs)) for n in range(1, y_count)
            ]

        def pass_on(buf, came, passed):
            for m in range(1, z_count):
                came[m - 1].wait_recv()
                passed += along_y(buf, m)

        def wait_all(copies):
            for copy in copies:
                copy.wait_recv()

        s0_f = spread(s0s)

        dsum = Scatter(net, dp, fs, fs_count, sd, rd, xd, yd, ad)
        for e in reversed(range(fs_count)):
            part = dot_nt(c_rel[e], wu[...])
            if e % 2:
                sd[e // 2] = part.astype(BF)
                dsum.send_odd(e // 2)
            else:
                ad[e // 2] = part

        def exchange(blocks_of, landed):
            found = []
            for e in range(1, fs_count):
                found.append(net.start(blocks_of.at[flip(fs, e)], landed.at[e], (dp, flip(fs, e))))
            landed[0] = blocks_of[fs]
            return found

        lane_first, lane_end, lane = doc_bounds(triples_ref, docs)
        for n in range(1, half):
            dsum.join(n)
        dsum.upper()
        s0_f.relay()
        pass_on(wos.at[0], came[0], passed[0])
        for e in range(fs_count):
            s0_f.ready(e)
            at = pl.ds(base_of(e, short), short)
            value = s0_out[...] if e == 0 else s0s[e].astype(F32)
            x_all[at, :] = value
            n1[at, :] = layer_norm(value, gain_out[2:3, :]).astype(BF)
        for r in range(0, total_b, blk_b):
            at = slice(r, r + blk_b)
            got = dot_nn(n1[at, :], wq1_out[...])
            q, k, v = got[:, :hd], got[:, hd : 2 * hd], got[:, 2 * hd :]
            q = (q * cos_ref[at, :] + partner(q) * sin_ref[at, :]).astype(BF)
            k = (k * cos_ref[at, :] + partner(k) * sin_ref[at, :]).astype(BF)
            qkv[at, 0:hd] = q
            qkv[at, hd : 2 * hd] = k
            qkv[at, 2 * hd : 3 * hd] = v.astype(BF)
            row = lax.broadcasted_iota(jnp.int32, (blk_b, LANES), 0) + r
            inside = (row >= lane_first) & (row < lane_end)
            fk = jnp.where(inside, 1.0, 0.0)
            fq = jnp.where(inside | (lane >= docs), 0.0, MASKED)
            head_inputs(qs, ks, at, q.astype(F32), k.astype(F32), fq, fk, heads)
            vt[:, at] = v.T.astype(BF)
            kt[:, at] = k.astype(F32).T.astype(BF)
            dk[at, :] = jnp.zeros((blk_b, LANES), F32)
            dv[at, :] = jnp.zeros((blk_b, LANES), F32)
        dsum.join(0)
        dsum.finish()
        dm[...] = ad[0]
        dfs[0] = ad[0].astype(BF)
        df_f = spread(dfs)
        wait_all(passed[0])
        wo_f = spread(wos, wos.at[0])
        flights = []
        for n in range(blocks_b):
            r, stop = n * blk_b, (n + 1) * blk_b
            found = []
            for h in range(heads):
                e, inv = softmax_block(ks, qs, h, r, stop)
                ps[n][h] = (e * inv).astype(BF)
                found.append(dot_nn(vt[h * HEAD : (h + 1) * HEAD, 0:stop], ps[n][h]))
            att[0, r:stop, :] = jnp.concatenate(found, axis=0).T.astype(BF)
            flights.append(spread(att.at[:, r:stop, :], att.at[0, r:stop, :]))
            if n == 0:
                pass_on(wi_ref, came[1], passed[1])
                df_f.relay()
                wo_f.relay()
        place_of = lax.broadcasted_iota(jnp.int32, (blk_b, LANES), 1) // HEAD
        for r in range(0, total_b, blk_b):
            at = slice(r, r + blk_b)
            q = widen(qkv[at, 0:hd].astype(F32))
            for h in range(heads):
                qs[h, at, :] = jnp.where(place_of == h, q, 0.0).astype(BF)

        pass_on(wd_ref, came[2], passed[2])
        wo_f.all_ready()
        for e in range(fs_count):
            wo_at[flip(fs, e)] = wos[e]
        for e in range(fs_count):
            hold[:, e * hd : (e + 1) * hd] = wo_at[e]
        for e in range(fs_count):
            turned[e * hd : (e + 1) * hd, :] = hold[pl.ds(base_of(e, hd), hd), :]
        for flight in flights:
            flight.relay()
        for flight in flights:
            flight.all_ready()
        for e in range(fs_count):
            att_rel[:, e * hd : (e + 1) * hd] = att[e]

        work[:, 0:width] = x_all[...] + dot_nn(att_rel[...], turned[...])
        for r in range(0, total_b, HEAD):
            m = work[r : r + HEAD, 0:width]
            m_all[r : r + HEAD, :] = m
            n2[r : r + HEAD, :] = layer_norm(m, gain_out[3:4, :]).astype(BF)
        wait_all(passed[1])
        work[:, 0:fj] = dot_nn(n2[...], wi_ref[...])
        for r in range(0, total_b, HEAD):
            value, rate = gelu_both(work[r : r + HEAD, 0:fj])
            hid[r : r + HEAD, :] = value.astype(BF)
            slope[r : r + HEAD, :] = rate
        wait_all(passed[2])
        work[:, 0:width] = dot_nt(hid[...], wd_ref[...])

        def give_out(scatter, source):
            for e in reversed(range(fs_count)):
                value = source[pl.ds(base_of(e, short), short), 0:width]
                if e % 2:
                    scatter.sbuf[e // 2] = value.astype(BF)
                    scatter.send_odd(e // 2)
                else:
                    scatter.acc[e // 2] = value

        fwd = Scatter(net, dp, fs, fs_count, sf, rf, xf, yf, af)
        give_out(fwd, work)
        for e in range(fs_count):
            df_f.ready(e)
            df_all[pl.ds(base_of(e, short), short), :] = dfs[e]
        work[:, 0:fj] = dot_nn(df_all[...], wd_ref[...])
        for r in range(0, total_b, HEAD):
            at = slice(r, r + HEAD)
            dpre[at, :] = (work[at, 0:fj] * slope[at, :]).astype(BF)
        work[:, 0:width] = dot_nt(dpre[...], wi_ref[...])
        bwd = Scatter(net, dp, fs, fs_count, sb, rb, xb, yb, ab)
        give_out(bwd, work)
        for j in range(1, half):
            bwd.join(j)
        bwd.upper()
        for j in range(1, half):
            fwd.join(j)
        fwd.upper()
        g_ff[:, 0:fj] = dot_tn(n2[...], dpre[...]).astype(BF)
        g_ff[:, fj : 2 * fj] = dot_tn(df_all[...], hid[...]).astype(BF)
        ff_rows = RowSum(net, (dp, fs, y_count, z_count, fs_count, rw), g_ff, yg, zsg, zrg, sum_ff)
        ff_rows.start()
        bwd.join(0)
        bwd.finish()
        m_own = m_all[pl.ds(base_of(0, short), short), :]
        dx, dg = layer_norm_back(m_own, gain_out[3:4, :], ab[0])
        dx = dx + dm[...]
        dm[...] = dx
        low_dx = dx.astype(BF)
        got = dot_nt(low_dx, hold[...]).astype(BF)
        for e in range(fs_count):
            do_out[e] = got[:, e * hd : (e + 1) * hd]
            da_out[e] = low_dx[:, e * hd : (e + 1) * hd]
        do_f = exchange(do_out, do_in)
        da_f = exchange(da_out, da_in)
        gain_two = jnp.sum(dg, axis=0, keepdims=True)

        fwd.join(0)
        fwd.finish()
        s1s[0] = (m_own + af[0]).astype(BF)
        s1_f = spread(s1s)
        z_f = exchange(z_out, z_rel)
        wait_all(do_f)
        for e in range(fs_count):
            at = pl.ds(base_of(e, short), short)
            do = widen(do_in[e].astype(F32))
            lane_head = lax.broadcasted_iota(jnp.int32, (short, LANES), 1) // HEAD
            for h in range(heads):
                ks[h, at, :] = jnp.where(lane_head == h, do, 0.0).astype(BF)
        wait_all(da_f)
        for e in range(fs_count):
            cols[pl.ds(base_of(e, short), short), :] = da_in[e]
        s1_f.relay()

        g_out = dot_tn(att_rel[...], cols[...]).astype(BF)
        for e in range(fs_count):
            group[pl.ds(base_of(e, hd), hd), cb - hd : cb] = g_out[e * hd : (e + 1) * hd, :]
        for n in range(blocks_b):
            r, stop = n * blk_b, (n + 1) * blk_b
            at = slice(r, stop)
            found = []
            add_k = add_v = None
            for h in range(heads):
                p = ps[n][h]
                grad = dot_nt(widen(qkv[0:stop, 2 * hd : 3 * hd]), ks[h, at, :])
                wide = p.astype(F32)
                inner = jnp.sum(wide * grad, axis=0, keepdims=True)
                dr = (wide * (grad - inner) * 0.125).astype(BF)
                part_v = dot_nn(p, ks[h, at, :])
                part_k = dot_nn(dr, qs[h, at, :])
                add_v = part_v if add_v is None else add_v + part_v
                add_k = part_k if add_k is None else add_k + part_k
                found.append(dot_nn(kt[h * HEAD : (h + 1) * HEAD, 0:stop], dr))
            dk[0:stop, :] += add_k
            dv[0:stop, :] += add_v
            dq = jnp.concatenate(found, axis=0).T
            dqkv[at, 0:hd] = (dq * cos_ref[at, :] - partner(dq) * sin_ref[at, :]).astype(BF)
        for r in range(0, total_b, blk_b):
            at = slice(r, r + blk_b)
            grad = dk[at, 0:hd]
            dqkv[at, hd : 2 * hd] = (grad * cos_ref[at, :] - partner(grad) * sin_ref[at, :]).astype(BF)
            dqkv[at, 2 * hd : 3 * hd] = dv[at, 0:hd].astype(BF)
        work[:, 0:width] = dot_nt(dqkv[...], wq1_out[...])
        first = Scatter(net, dp, fs, fs_count, sa, ra, xa, ya, aa)
        give_out(first, work)
        for j in range(1, half):
            first.join(j)
        first.upper()
        group[:, 0 : 3 * hd] = dot_tn(n1[...], dqkv[...]).astype(BF)
        s1_f.all_ready()
        lift_f = []
        for e in range(fs_count):
            part = dot_nn(s1s[e], wu[...]).astype(BF)
            if e:
                lift_send[e] = part
                lift_f.append(net.start(lift_send.at[e], lift_rel.at[e], (dp, flip(fs, e))))
            else:
                lift_rel[0] = part
        g_up = jnp.zeros((width, pc), F32)
        for e in range(fs_count):
            g_up = g_up + dot_tn(s1s[e], c_rel[e])
        group[:, 3 * hd + pc : 3 * hd + 2 * pc] = g_up.astype(BF)
        for m in range(1, z_count):
            ff_rows.service(m)
        first.join(0)
        first.finish()
        dx, dg = layer_norm_back(s0_out[...], gain_out[2:3, :], aa[0])
        ds0s[0] = (dx + dm[...]).astype(BF)
        gain_one = jnp.sum(dg, axis=0, keepdims=True)
        which = lax.broadcasted_iota(jnp.int32, (8, width), 0)
        dgain[...] = jnp.where(which == 0, gain_one, jnp.where(which == 1, gain_two, 0.0))

        hop = net.make(ds0s.at[0, 0:HALO, :], nxt, (dp, lax.rem(fs + fs_count - 1, fs_count)))

        @pl.when(fs > 0)
        def _():
            hop.start()

        ds0_f = spread(ds0s)
        row = lax.broadcasted_iota(jnp.int32, (short, LANES), 0) + fs * short + 1
        shut = jnp.max(jnp.where((row == lane_first) | (row >= total_b), 1.0, 0.0), axis=1, keepdims=True) > 0.0

        @pl.when(fs < fs_count - 1)
        def _():
            hop.wait_recv()

        grad = jnp.concatenate([ds0s[0], nxt[...]], axis=0)
        for e in range(fs_count):
            lift_at = dot_nn(grad, wp[e])
            spread_rows[flip(fs, e)] = lift_at
        dz = jnp.concatenate([spread_rows[e] for e in range(fs_count)], axis=1)
        strided_write(thin, 0, short, dz[0:short, 2 * width : 3 * width])
        for k in range(2):
            part = dz[1 : short + 1, k * width : (k + 1) * width]
            strided_write(thin, k + 1, short, jnp.where(shut, 0.0, part))
        value = cot_ref[...].astype(F32) + spread_read(thin)
        da[...] = value
        dfs_out[0] = value.astype(BF)
        out_f = spread(dfs_out)
        ff_rows.service(0)
        ds0_f.relay()
        for copy in z_f:
            copy.wait_recv()
        g_pool = jnp.zeros((width, pc), F32)
        for e in range(fs_count):
            ds0_f.ready(e)
            g_pool = g_pool + dot_tn(ds0s[e], z_rel[e])
        group[:, 3 * hd : 3 * hd + pc] = g_pool.astype(BF)

        wait_all(lift_f)
        for e in range(fs_count):
            lift[flip(fs, e)] = lift_rel[e].astype(F32)
        lifted = jnp.concatenate([lift[e] for e in range(fs_count)], axis=1)
        for n in range(3):
            strided_write(thin, n, short, lifted[:, n * width : (n + 1) * width])
        out[...] = (after[...] + spread_read(thin)).astype(BF)
        ff_rows.finish()
        out_f.relay()
        out_f.all_ready()

        @pl.when(fs > 0)
        def _():
            hop.wait_send()

        for copy in stores:
            copy.wait()
        net.finish()

    outs = [
        ((total, width), BF),
        ((total, 3 * hd), BF),
        ((total, width), BF),
        ((total, width), BF),
        ((total, fj), BF),
        ((total, fj), BF),
        ((width, width), BF),
        ((rows, width), F32),
        ((width, 3 * hd), BF),
        ((width, fj), BF),
        ((width, fj), BF),
        ((8, width), F32),
        ((rows, width), BF),
        ((rows, width), F32),
        ((fs_count, rows, width), BF),
        ((width, cb), BF),
        ((rw, 2 * fj), F32),
        ((8, width), F32),
    ]
    wide = max(width, fj)
    pieces = (fs_count, short, width)
    scatter = [((half, short, width), BF)] * 2 + [((half - 1, short, width), BF)] * 2 + [((half, short, width), F32)]
    scratch = [
        ((rows, width), F32),
        ((fs_count, short, pc), BF),
        ((short, width), F32),
        ((fs_count, width, pc), BF),
        ((width, 3 * hd), BF),
        ((width, pc), BF),
        ((fs_count, short, pc), BF),
        ((total, width), BF),
        ((total, 3 * hd), BF),
        ((total, width), BF),
        ((total, width), BF),
        ((total, fj), BF),
        ((total, fj), BF),
        ((fs_count, rows, width), BF),
        ((fs_count, short, pc), BF),
        ((2, 3, rw, hd), BF),
        ((3, width, hd), BF),
        ((3, width, hd), BF),
        ((width, LANES), BF),
        ((fs_count, width, hd), BF),
        ((fs_count, width, hd), BF),
        ((fs_count, total, hd), BF),
        ((heads, total, LANES), BF),
        ((heads, total, LANES), BF),
        ((hd, total), BF),
        ((width, width), BF),
        ((width, width), BF),
        ((rows, wide), F32),
        ((rows, wide), BF),
        ((rows, width), F32),
        ((fs_count * HALO, width), F32),
        ((fs_count * HALO, width), F32),
        ((half, long_rows, width), BF),
        ((half, long_rows, width), BF),
        ((half - 1, long_rows, width), BF),
        ((half - 1, long_rows, width), BF),
        ((half, long_rows, width), F32),
        ((width // LANES, long_rows, LANES), F32),
        ((fs_count, width, hd), BF),
        ((width, fj), BF),
        ((width, fj), BF),
        ((width, 2 * fj), BF),
        ((y_count - 1, z_count, rw, 2 * fj), BF),
        ((z_count - 1, rw, 2 * fj), BF),
        ((z_count - 1, rw, 2 * fj), BF),
        *scatter,
        ((fs_count, short, pc), BF),
        ((fs_count, short, pc), BF),
        (pieces, BF),
        ((total_b, width), F32),
        ((fs_count, width, hd), BF),
        ((width, width), BF),
        ((width, width), BF),
        ((fs_count, short, pc), BF),
        (pieces, BF),
        ((total_b, width), BF),
        ((fs_count, short, hd), BF),
        ((fs_count, short, hd), BF),
        ((fs_count, short, hd), BF),
        ((fs_count, short, hd), BF),
        ((total_b, hd), BF),
        (pieces, BF),
        (pieces, BF),
        ((HALO, width), BF),
        ((total_b, width), BF),
        ((total_b, width), BF),
        ((total_b, 3 * hd), BF),
        ((fs_count, total_b, hd), BF),
        ((total_b, width), BF),
        ((heads, total_b, LANES), BF),
        ((heads, total_b, LANES), BF),
        ((hd, total_b), BF),
        ((hd, total_b), BF),
        ((total_b, LANES), F32),
        ((total_b, LANES), F32),
        ((total_b, 3 * hd), BF),
        ((total_b, wide), F32),
        ((total_b, fj), BF),
        ((total_b, fj), F32),
        ((total_b, fj), BF),
        ((total_b, width), F32),
        ((short, width), F32),
        *scatter,
        *scatter,
        *scatter,
        ((width // LANES, rows, LANES), F32),
        ((fs_count, short + HALO, pc), F32),
        ((fs_count, short, pc), F32),
    ]
    tail = [pltpu.VMEM((heads, (n + 1) * blk_b, blk_b), BF) for n in range(blocks_b)]
    return pl.pallas_call(
        body,
        out_shape=[jax.ShapeDtypeStruct(s, t) for s, t in outs],
        in_specs=[vmem(), vmem(), smem()] + [vmem()] * 9,
        out_specs=[hbm()] * 6 + [vmem()] * (len(outs) - 6),
        scratch_shapes=[pltpu.VMEM(s, t) for s, t in scratch] + [pltpu.SemaphoreType.DMA((sems,))] * 2 + tail,
        compiler_params=pltpu.CompilerParams(collective_id=3, has_side_effects=True, vmem_limit_bytes=VMEM_BYTES),
        cost_estimate=cost(4e10, 5e7),
        name="forward_all",
    )(tokens, cot, triples, *weights, gains_t, cos, sin)


class RowSum:
    def __init__(self, net, place, grad, ybuf, zsend, zrecv, total, q_send=None, q_recv=None, q_total=None):
        self.net, self.grad, self.ybuf = net, grad, ybuf
        self.zsend, self.zrecv, self.total = zsend, zrecv, total
        self.q_send, self.q_recv, self.q_total = q_send, q_recv, q_total
        self.dp, self.fs, self.y_count, self.z_count, self.fs_count, self.rw = place
        self.ys, self.zs, self.qs = {}, {}, []

    def rows_of(self, step):
        return pl.ds(pl.multiple_of(flip(self.dp, step) * self.rw, 16), self.rw)

    def start(self):
        for m in list(range(1, self.z_count)) + [0]:
            self.ys[m] = [
                self.net.start(
                    self.grad.at[self.rows_of(m * self.y_count + j), :],
                    self.ybuf.at[j - 1, m],
                    (flip(self.dp, j), self.fs),
                )
                for j in range(1, self.y_count)
            ]
        if self.q_send is not None:
            self.q_base = self.net.used
            self.net.used += 3 * self.z_count

    def owner(self, kind):
        place = kind * self.fs_count + self.fs
        return lax.div(place, 3), lax.rem(place, 3)

    def service(self, m):
        for copy in self.ys[m]:
            copy.wait_recv()
        got = self.grad[self.rows_of(m * self.y_count), :].astype(F32)
        for j in range(1, self.y_count):
            got = got + self.ybuf[j - 1, m].astype(F32)
        there = flip(self.dp, m * self.y_count)
        lo = 0
        if self.q_send is not None:
            hd = self.q_send.shape[3]
            lo = 3 * hd
            for kind in range(3):
                to, slot = self.owner(kind)
                self.q_send[m, kind] = got[:, kind * hd : (kind + 1) * hd].astype(BF)
                copy = pltpu.make_async_remote_copy(
                    src_ref=self.q_send.at[m, kind],
                    dst_ref=self.q_recv.at[m, slot],
                    send_sem=self.net.send.at[self.q_base + 3 * m + kind],
                    recv_sem=self.net.recv.at[self.q_base + 3 * m + slot],
                    device_id=(there, to),
                    device_id_type=MESH,
                )
                if m:
                    copy.start()
                    self.qs.append((copy, None))
                else:

                    @pl.when(to != self.fs)
                    def _():
                        copy.start()

                    @pl.when(to == self.fs)
                    def _():
                        self.q_recv[0, slot] = self.q_send[0, kind]

                    self.qs.append((copy, to != self.fs))
        width = self.total.shape[1]
        rest = got[:, lo : lo + width]
        if m:
            self.zsend[m - 1] = rest.astype(BF)
            self.zs[m] = self.net.start(self.zsend.at[m - 1], self.zrecv.at[m - 1], (there, self.fs))
        else:
            self.total[...] = rest

    def finish(self):
        rest = self.total[...]
        for m in range(1, self.z_count):
            self.zs[m].wait_recv()
            rest = rest + self.zrecv[m - 1].astype(F32)
        self.total[...] = rest
        if self.q_send is None:
            return
        for t in range(3):
            giver = lax.rem(3 * self.fs + t, self.fs_count)
            for m in range(self.z_count):
                landed = self.q_recv.at[m, t]
                wait = pltpu.make_async_copy(landed, landed, self.net.recv.at[self.q_base + 3 * m + t])
                if m:
                    wait.wait()
                else:

                    @pl.when(giver != self.fs)
                    def _():
                        wait.wait()

        for t in range(3):
            block = self.q_recv[0, t].astype(F32)
            for m in range(1, self.z_count):
                block = block + self.q_recv[m, t].astype(F32)
            self.q_total[t] = block
        for copy, when in self.qs:
            if when is None:
                copy.wait_send()
            else:

                @pl.when(when)
                def _():
                    copy.wait_send()


class HeadSum:
    def __init__(self, net, place, grad, send, recv, total):
        self.net, self.grad, self.send, self.recv, self.total = net, grad, send, recv, total
        self.dp, self.fs, self.y_count, self.z_count, self.fs_count, self.rw = place
        self.count, self.copies = send.shape[0], []

    def start(self):
        base, hd = self.net.used, self.send.shape[3]
        self.base = base
        self.net.used += 3 * self.count
        for step in reversed(range(self.count)):
            rows = pl.ds(pl.multiple_of(flip(self.dp, step) * self.rw, 16), self.rw)
            for kind in range(3):
                place = kind * self.fs_count + self.fs
                to, slot = lax.div(place, 3), lax.rem(place, 3)
                self.send[step, kind] = self.grad[rows, kind * hd : (kind + 1) * hd]
                copy = pltpu.make_async_remote_copy(
                    src_ref=self.send.at[step, kind],
                    dst_ref=self.recv.at[step, slot],
                    send_sem=self.net.send.at[base + 3 * step + kind],
                    recv_sem=self.net.recv.at[base + 3 * step + slot],
                    device_id=(flip(self.dp, step), to),
                    device_id_type=MESH,
                )
                if step:
                    copy.start()
                    self.copies.append((copy, None))
                else:

                    @pl.when(to != self.fs)
                    def _():
                        copy.start()

                    @pl.when(to == self.fs)
                    def _():
                        self.recv[0, slot] = self.send[0, kind]

                    self.copies.append((copy, to != self.fs))

    def finish(self):
        for t in range(3):
            giver = lax.rem(3 * self.fs + t, self.fs_count)
            for step in range(self.count):
                landed = self.recv.at[step, t]
                wait = pltpu.make_async_copy(landed, landed, self.net.recv.at[self.base + 3 * step + t])
                if step:
                    wait.wait()
                else:

                    @pl.when(giver != self.fs)
                    def _():
                        wait.wait()

            block = self.recv[0, t].astype(F32)
            for step in range(1, self.count):
                block = block + self.recv[step, t].astype(F32)
            self.total[t] = block
        for copy, when in self.copies:
            if when is None:
                copy.wait_send()
            else:

                @pl.when(when)
                def _():
                    copy.wait_send()


class Scatter:
    def __init__(self, net, dp, fs, fs_count, sbuf, rbuf, xsend, xrecv, acc):
        self.net, self.dp, self.fs, self.half = net, dp, fs, fs_count // 2
        self.sbuf, self.rbuf, self.xsend, self.xrecv, self.acc = sbuf, rbuf, xsend, xrecv, acc
        self.first, self.hops, self.slot = {}, {}, 0

    def send_odd(self, j):
        self.first[j] = self.net.start(self.sbuf.at[j], self.rbuf.at[j], (self.dp, flip(self.fs, 1)))

    def join(self, j):
        self.first[j].wait_recv()
        self.acc[j] = self.acc[j] + self.rbuf[j].astype(F32)

    def give(self, j):
        bit = (2 * j) & -(2 * j)
        slot = self.slot
        self.slot += 1
        self.xsend[slot] = self.acc[j].astype(BF)
        self.hops[j] = (self.net.start(self.xsend.at[slot], self.xrecv.at[slot], (self.dp, flip(self.fs, bit))), slot)

    def take(self, j):
        low = j & -j
        copy, slot = self.hops[j]
        copy.wait_recv()
        self.acc[j - low] = self.acc[j - low] + self.xrecv[slot].astype(F32)

    def sent(self):
        for copy in list(self.first.values()) + [copy for copy, _ in self.hops.values()]:
            copy.wait_send()
            self.net.open = [other for other in self.net.open if other is not copy]

    def upper(self):
        if self.half == 2:
            self.give(1)

    def finish(self):
        if self.half == 2:
            self.take(1)
            return
        bit = 1
        while bit < self.half:
            gives = [j for j in range(self.half) if j & bit and not j & (bit - 1)]
            for j in gives:
                self.give(j)
            for j in gives:
                self.take(j)
            bit *= 2


def query_rows(total):
    return QB if total <= 2048 else QB // 2


def backward_one(
    y_count, dp_count, fs_count, da, dfs, n2, hid_in, slope_in, wi, wd, mid, gain_rows, qkv, wo_full, wq, cos, sin, triples, n1, att_rel, tokens, group_b, dgain_b
):
    rows, width = tokens.shape
    total = rows * fs_count
    fj, hd = wi.shape[1], wq.shape[1] // 3
    heads, docs = hd // HEAD, triples.shape[1]
    z_count, rw = dp_count // y_count, width // dp_count
    cb = group_b.shape[1]
    blk, half = query_rows(total), fs_count // 2
    blocks = total // blk
    sems = 96 + 12 * dp_count

    def body(
        da_ref, dfs, n2_hbm, hid_hbm, slope_hbm, wi_ref, wd_ref, mid_hbm, gain_ref, qkv_hbm, wo_ref, wq_ref, cos_hbm, sin_hbm, triples_ref, n1_hbm, att_hbm, tok, gb, dgain_two,
        grad_in, dgain, sum_b, sum_ff, sum_o, sum_q,
        n2_ref, mid_ref, qkv_ref, cos_ref, sin_ref, n1_ref, att_ref, da_low, do_out, do_in, da_out, da_in, hid, slope, dpre, work, qs, ks, kt, dk, dv, dm, cols, g_ff, g_at,
        sbuf, rbuf, xsend, xrecv, acc, yb, zsb, zrb, qsb, qrb, yf, zsf, zrf, ya, zsa, zra, qsa, qra, tiles, send_sem, recv_sem,
        *ps,
    ):
        dp, fs = lax.axis_index("dp"), lax.axis_index("fsdp")
        net = Net(send_sem, recv_sem)
        place = (dp, fs, y_count, z_count, fs_count, rw)
        dqkv = qkv_ref
        loads = {}
        for name, src, dst in (
            ("slope", slope_hbm, slope),
            ("n2", n2_hbm, n2_ref),
            ("hid", hid_hbm, hid),
            ("mid", mid_hbm, mid_ref),
            ("qkv", qkv_hbm, qkv_ref),
            ("att", att_hbm, att_ref),
            ("cos", cos_hbm, cos_ref),
            ("sin", sin_hbm, sin_ref),
            ("n1", n1_hbm, n1_ref),
        ):
            loads[name] = net.local(src, dst)
        barrier = pltpu.get_barrier_semaphore()
        for m in range(z_count):
            for e in range(fs_count):
                if m or e:
                    there = (flip(dp, m * y_count), flip(fs, e))
                    pl.semaphore_signal(barrier, inc=1, device_id=there, device_id_type=MESH)
        for j in range(1, y_count):
            pl.semaphore_signal(barrier, inc=1, device_id=(flip(dp, j), fs), device_id_type=MESH)
        pl.semaphore_wait(barrier, z_count * fs_count - 1 + y_count - 1)

        sum_of_b = RowSum(net, place, gb, yb, zsb, zrb, sum_b, qsb, qrb, sum_q.at[1])
        sum_of_b.start()

        def pull(e, out):
            work[:, 0:fj] = dot_nn(dfs[e], wd_ref[...])
            for r in range(0, rows, HEAD):
                at = slice(e * rows + r, e * rows + r + HEAD)
                dpre[at, :] = (work[r : r + HEAD, 0:fj] * slope[at, :].astype(F32)).astype(BF)
            out[...] = dot_nt(dpre[e * rows : (e + 1) * rows, :], wi_ref[...]).astype(out.dtype)

        def part_into(scatter, e, fill):
            if e % 2:
                fill(e, scatter.sbuf.at[e // 2])
                scatter.send_odd(e // 2)
            else:
                fill(e, scatter.acc.at[e // 2])

        ff_sum = Scatter(net, dp, fs, fs_count, sbuf, rbuf, xsend, xrecv, acc)
        loads["slope"].wait()

        def both_steps(e):
            part_into(ff_sum, e, pull)

        for j in reversed(range(1, half)):
            both_steps(2 * j + 1)
            both_steps(2 * j)
        for j in range(1, half):
            ff_sum.join(j)
        ff_sum.upper()
        both_steps(1)
        both_steps(0)
        sum_of_b.service(1)
        for m in range(2, z_count):
            sum_of_b.service(m)
        ff_sum.join(0)
        loads["hid"].wait()
        loads["n2"].wait()
        g_ff[:, 0:fj] = dot_tn(n2_ref[...], dpre[...]).astype(BF)
        g_ff[:, fj : 2 * fj] = dot_tn(dfs[...].reshape(total, width), hid[...]).astype(BF)
        sum_of_b.service(0)
        sum_of_ff = RowSum(net, place, g_ff, yf, zsf, zrf, sum_ff)
        sum_of_ff.start()

        loads["qkv"].wait()
        lane_first, lane_end, lane = doc_bounds(triples_ref, docs)
        for r in range(0, total, blk):
            at = slice(r, r + blk)
            q = qkv_ref[at, 0:hd].astype(F32)
            k = qkv_ref[at, hd : 2 * hd].astype(F32)
            row = lax.broadcasted_iota(jnp.int32, (blk, LANES), 0) + r
            inside = (row >= 3 * lane_first) & (row < 3 * lane_end)
            fk = jnp.where(inside, 1.0, 0.0)
            fq = jnp.where(inside | (lane >= docs), 0.0, MASKED)
            head_inputs(qs, ks, at, q, k, fq, fk, heads)
            kt[:, at] = k.T.astype(BF)
            dk[at, :] = jnp.zeros((blk, LANES), F32)
            dv[at, :] = jnp.zeros((blk, LANES), F32)

        def recompute(n):
            r = n * blk
            for h in range(heads):
                e, inv = softmax_block(ks, qs, h, r, r + blk)
                ps[n][h] = (e * inv).astype(BF)

        for n in range(blocks // 2):
            recompute(n)

        ff_sum.finish()
        loads["mid"].wait()
        for r in range(0, rows, LANES):
            at = slice(r, r + LANES)
            dx, dg = layer_norm_back(mid_ref[at, :], gain_ref[1:2, :], acc[0, at, :])
            dx = dx + da_ref[at, :]
            dm[at, :] = dx
            da_low[at, :] = dx.astype(BF)
            dg = jnp.sum(dg, axis=0, keepdims=True)
            gain_two = dg if r == 0 else gain_two + dg
        got = dot_nt(da_low[...], wo_ref[...]).astype(BF)
        for e in range(fs_count):
            do_out[e] = got[:, e * hd : (e + 1) * hd]
            da_out[e] = da_low[:, e * hd : (e + 1) * hd]

        def exchange(blocks_of, landed):
            found = []
            for e in range(1, fs_count):
                found.append(net.start(blocks_of.at[flip(fs, e)], landed.at[e], (dp, flip(fs, e))))
            landed[0] = blocks_of[fs]
            return found

        do_f = exchange(do_out, do_in)
        da_f = exchange(da_out, da_in)
        for n in range(blocks // 2, blocks):
            recompute(n)
        for m in range(1, z_count):
            sum_of_ff.service(m)
        sum_of_ff.service(0)

        place_of = lax.broadcasted_iota(jnp.int32, (blk, LANES), 1) // HEAD
        for r in range(0, total, blk):
            at = slice(r, r + blk)
            q = widen(qkv_ref[at, 0:hd].astype(F32))
            for h in range(heads):
                qs[h, at, :] = jnp.where(place_of == h, q, 0.0).astype(BF)
        lane_head = lax.broadcasted_iota(jnp.int32, (rows, LANES), 1) // HEAD
        for e in range(fs_count):
            if e:
                do_f[e - 1].wait_recv()
            base = pl.multiple_of(flip(fs, e) * rows, 16)
            do = widen(do_in[e].astype(F32))
            for h in range(heads):
                ks[h, pl.ds(base, rows), :] = jnp.where(lane_head == h, do, 0.0).astype(BF)
        for e in range(fs_count):
            if e:
                da_f[e - 1].wait_recv()
            cols[pl.ds(pl.multiple_of(flip(fs, e) * rows, 16), rows), :] = da_in[e]

        loads["att"].wait()
        g_out = dot_tn(att_ref[...], cols[...]).astype(BF)
        for e in range(fs_count):
            base = pl.multiple_of(flip(fs, e) * hd, 16)
            g_at[pl.ds(base, hd), 3 * hd : 4 * hd] = g_out[e * hd : (e + 1) * hd, :]
        sum_of_b.finish()

        loads["cos"].wait()
        loads["sin"].wait()
        for n in range(blocks):
            r, stop = n * blk, (n + 1) * blk
            at = slice(r, stop)
            found = []
            add_k = add_v = None
            for h in range(heads):
                p = ps[n][h]
                v = widen(qkv_ref[0:stop, 2 * hd : 3 * hd])
                grad = dot_nt(v, ks[h, at, :])
                wide = p.astype(F32)
                middle = jnp.sum(wide * grad, axis=0, keepdims=True)
                dr = (wide * (grad - middle) * 0.125).astype(BF)
                part_v = dot_nn(p, ks[h, at, :])
                part_k = dot_nn(dr, qs[h, at, :])
                add_v = part_v if add_v is None else add_v + part_v
                add_k = part_k if add_k is None else add_k + part_k
                found.append(dot_nn(kt[h * HEAD : (h + 1) * HEAD, 0:stop], dr))
            dk[0:stop, :] += add_k
            dv[0:stop, :] += add_v
            dq = jnp.concatenate(found, axis=0).T
            dqkv[at, 0:hd] = (dq * cos_ref[at, :] - partner(dq) * sin_ref[at, :]).astype(BF)
        for r in range(0, total, blk):
            at = slice(r, r + blk)
            grad = dk[at, 0:hd]
            dqkv[at, hd : 2 * hd] = (grad * cos_ref[at, :] - partner(grad) * sin_ref[at, :]).astype(BF)
            dqkv[at, 2 * hd : 3 * hd] = dv[at, 0:hd].astype(BF)
        loads["n1"].wait()
        g_at[:, 0 : 3 * hd] = dot_tn(n1_ref[...], dqkv[...]).astype(BF)
        sum_of_at = RowSum(net, place, g_at, ya, zsa, zra, sum_o, qsa, qra, sum_q.at[0])
        sum_of_at.start()

        ff_sum.sent()
        at_sum = Scatter(net, dp, fs, fs_count, sbuf, rbuf, xsend, xrecv, acc)
        tiles[0] = jnp.zeros((8, width), F32)

        def push_out(e, out):
            base = pl.multiple_of(flip(fs, e) * rows, 16)
            part = dot_nt(dqkv[pl.ds(base, rows), :], wq_ref[...])
            out[...] = part.astype(out.dtype)
            work[:, 0:width] = part
            total_of = jnp.zeros((8, width), F32)
            for r in range(0, rows, HEAD):
                grown = work[r : r + HEAD, 0:width] * n1_ref[pl.ds(base + r, HEAD), :].astype(F32)
                total_of = total_of + jnp.sum(grown.reshape(HEAD // 8, 8, width), axis=0)
            tiles[0] = tiles[0] + total_of

        for e in reversed(range(2, fs_count)):
            part_into(at_sum, e, push_out)
        part_into(at_sum, 1, push_out)
        for j in range(1, half):
            at_sum.join(j)
        at_sum.upper()
        part_into(at_sum, 0, push_out)
        gain_one = jnp.sum(tiles[0], axis=0, keepdims=True) / gain_ref[0:1, :]
        which = lax.broadcasted_iota(jnp.int32, (8, width), 0)
        both = jnp.where(which == 0, gain_one, jnp.where(which == 1, gain_two, 0.0))
        both = jnp.where(which == 2, dgain_two[0:1, :], jnp.where(which == 3, dgain_two[1:2, :], both))
        hops = [(dp, flip(fs, 1 << n)) for n in range(fs_count.bit_length() - 1)]
        hops += [(flip(dp, 1 << n), fs) for n in range(y_count.bit_length() - 1)]

        def hop_out(n, value):
            tiles[1 + n] = value
            return net.start(tiles.at[1 + n], tiles.at[1 + len(hops) + n], hops[n])

        hop = hop_out(0, both)
        sum_of_at.service(1)
        for n in range(1, len(hops) - 1):
            hop.wait_recv()
            both = both + tiles[len(hops) + n]
            hop = hop_out(n, both)
        for m in range(2, z_count):
            sum_of_at.service(m)
        sum_of_at.service(0)
        at_sum.join(0)
        sum_of_ff.finish()
        at_sum.finish()
        last = len(hops) - 1
        hop.wait_recv()
        both = both + tiles[len(hops) + last]
        hop = hop_out(last, both)
        for r in range(0, rows, LANES):
            at = slice(r, r + LANES)
            dx, _ = layer_norm_back(tok[at, :].astype(F32), gain_ref[0:1, :], acc[0, at, :])
            grad_in[at, :] = dx + dm[at, :]
        hop.wait_recv()
        dgain[...] = both + tiles[1 + len(hops) + last]
        sum_of_at.finish()
        net.finish()

    outs = [
        ((rows, width), F32),
        ((8, width), F32),
        ((rw, cb - 3 * hd), F32),
        ((rw, 2 * fj), F32),
        ((rw, hd), F32),
        ((2, 3, rw, hd), F32),
    ]
    wide = max(width, fj)
    zy = (y_count - 1, z_count, rw)
    scratch = [
        ((total, width), BF),
        ((rows, width), F32),
        ((total, 3 * hd), BF),
        ((total, hd), F32),
        ((total, hd), F32),
        ((total, width), BF),
        ((total, width), BF),
        ((rows, width), BF),
        ((fs_count, rows, hd), BF),
        ((fs_count, rows, hd), BF),
        ((fs_count, rows, hd), BF),
        ((fs_count, rows, hd), BF),
        ((total, fj), BF),
        ((total, fj), BF),
        ((total, fj), BF),
        ((rows, wide), F32),
        ((heads, total, LANES), BF),
        ((heads, total, LANES), BF),
        ((hd, total), BF),
        ((total, LANES), F32),
        ((total, LANES), F32),
        ((rows, width), F32),
        ((total, hd), BF),
        ((width, 2 * fj), BF),
        ((width, 4 * hd), BF),
        ((half, rows, width), BF),
        ((half, rows, width), BF),
        ((half - 1, rows, width), BF),
        ((half - 1, rows, width), BF),
        ((half, rows, width), F32),
        (zy + (cb,), BF),
        ((z_count - 1, rw, cb - 3 * hd), BF),
        ((z_count - 1, rw, cb - 3 * hd), BF),
        ((z_count, 3, rw, hd), BF),
        ((z_count, 3, rw, hd), BF),
        (zy + (2 * fj,), BF),
        ((z_count - 1, rw, 2 * fj), BF),
        ((z_count - 1, rw, 2 * fj), BF),
        (zy + (4 * hd,), BF),
        ((z_count - 1, rw, hd), BF),
        ((z_count - 1, rw, hd), BF),
        ((z_count, 3, rw, hd), BF),
        ((z_count, 3, rw, hd), BF),
        ((2 * (fs_count.bit_length() + y_count.bit_length() - 2) + 1, 8, width), F32),
    ]
    tail = [pltpu.VMEM((heads, (n + 1) * blk, blk), BF) for n in range(blocks)]
    arrays = (da, dfs, n2, hid_in, slope_in, wi, wd, mid, gain_rows, qkv, wo_full, wq, cos, sin, triples, n1, att_rel, tokens, group_b, dgain_b)
    return pl.pallas_call(
        body,
        out_shape=[jax.ShapeDtypeStruct(s, t) for s, t in outs],
        in_specs=[hbm() if n in (2, 3, 4, 7, 9, 12, 13, 15, 16) else smem() if n == 14 else vmem() for n in range(20)],
        out_specs=[vmem()] * len(outs),
        scratch_shapes=[pltpu.VMEM(s, t) for s, t in scratch] + [pltpu.SemaphoreType.DMA((sems,))] * 2 + tail,
        compiler_params=pltpu.CompilerParams(collective_id=4, has_side_effects=True, vmem_limit_bytes=VMEM_BYTES),
        cost_estimate=cost(4e10, 3e7),
        name="backward_one",
    )(*arrays)


def middle(y_count, dp_count, fs_count, s0, after, z_blocks, cot, c_rel, wq, wu, weights, wp, gain_rows, cos, sin, triples):
    short, width = s0.shape
    rows, total = short * 3, short * fs_count
    hd = wq.shape[1] // 3
    pc = wp.shape[2]
    wout, win, wdown = weights
    fj, rw = win.shape[2], win.shape[1]
    z_count = dp_count // y_count
    heads, docs = hd // HEAD, triples.shape[1]
    blk = min(QB, total)
    blocks, half = total // blk, fs_count // 2
    cb = 4 * hd + 2 * pc
    sems = 96 + 16 * fs_count + 6 * dp_count

    def body(
        s0_ref, after_ref, z_ref, cot_ref, c_ref, wq_ref, wu_ref, o_in, i_in, d_in, wp_ref, gain_ref, cos_ref, sin_ref, triples_ref,
        out, da, dfs_out, group, sum_ff, dgain,
        wos, wi_ref, wd_ref, g_ff, yg, zsg, zrg, sd, rd, xd, yd, ad, lift_send, lift_rel,
        s0s, x_all, wo_at, hold, turned, z_rel, dfs, df_all, do_out, do_in, da_out, da_in, cols, s1s, ds0s, nxt,
        n1, n2, qkv, att, att_rel, qs, ks, vt, kt, dk, dv, dqkv, work, hid, slope, dpre, m_all, dm,
        sf, rf, xf, yf, af, sb, rb, xb, yb, ab, sa, ra, xa, ya, aa, thin, spread_rows, lift, send_sem, recv_sem, *ps,
    ):
        dp, fs = lax.axis_index("dp"), lax.axis_index("fsdp")
        net = Net(send_sem, recv_sem)

        def base_of(e, amount):
            return pl.multiple_of(flip(fs, e) * amount, 16)

        def spread(pieces, src=None):
            return Flight(net, dp, fs, fs_count, pieces, pieces.at[0] if src is None else src)

        s0s[0] = s0_ref[...].astype(BF)
        nxt[...] = jnp.zeros(nxt.shape, BF)
        here = pl.ds(pl.multiple_of(dp * rw, 16), rw)
        wos[0, here, :] = o_in[1].astype(BF)
        wi_ref[here, :] = i_in[1].astype(BF)
        wd_ref[here, :] = d_in[1].astype(BF)
        barrier = pltpu.get_barrier_semaphore()
        for e in range(1, fs_count):
            pl.semaphore_signal(barrier, inc=1, device_id=(dp, flip(fs, e)), device_id_type=MESH)
        others = [m * y_count for m in range(1, z_count)] + list(range(1, y_count))
        for step in others:
            pl.semaphore_signal(barrier, inc=1, device_id=(flip(dp, step), fs), device_id_type=MESH)
        pl.semaphore_wait(barrier, fs_count - 1 + len(others))

        def of(buf, step):
            return buf.at[pl.ds(pl.multiple_of(flip(dp, step) * rw, 16), rw), :]

        def along_z(buf):
            return [
                net.start(of(buf, 0), of(buf, 0), (flip(dp, m * y_count), fs)) for m in range(1, z_count)
            ]

        def along_y(buf, m):
            return [
                net.start(of(buf, m * y_count), of(buf, m * y_count), (flip(dp, n), fs)) for n in range(1, y_count)
            ]

        def pass_on(buf, came, passed):
            for m in range(1, z_count):
                came[m - 1].wait_recv()
                passed += along_y(buf, m)

        def wait_all(copies):
            for copy in copies:
                copy.wait_recv()

        s0_f = spread(s0s)
        came = [along_z(buf) for buf in (wos.at[0], wi_ref, wd_ref)]
        passed = [along_y(buf, 0) for buf in (wos.at[0], wi_ref, wd_ref)]

        dsum = Scatter(net, dp, fs, fs_count, sd, rd, xd, yd, ad)
        for e in reversed(range(fs_count)):
            part = dot_nt(c_ref[e], wu_ref[...])
            if e % 2:
                sd[e // 2] = part.astype(BF)
                dsum.send_odd(e // 2)
            else:
                ad[e // 2] = part

        def exchange(blocks_of, landed):
            found = []
            for e in range(1, fs_count):
                found.append(net.start(blocks_of.at[flip(fs, e)], landed.at[e], (dp, flip(fs, e))))
            landed[0] = blocks_of[fs]
            return found

        lane_first, lane_end, lane = doc_bounds(triples_ref, docs)
        for n in range(1, half):
            dsum.join(n)
        dsum.upper()
        s0_f.relay()
        pass_on(wos.at[0], came[0], passed[0])
        for e in range(fs_count):
            s0_f.ready(e)
            at = pl.ds(base_of(e, short), short)
            value = s0_ref[...] if e == 0 else s0s[e].astype(F32)
            x_all[at, :] = value
            n1[at, :] = layer_norm(value, gain_ref[2:3, :]).astype(BF)
        for r in range(0, total, blk):
            at = slice(r, r + blk)
            got = dot_nn(n1[at, :], wq_ref[...])
            q, k, v = got[:, :hd], got[:, hd : 2 * hd], got[:, 2 * hd :]
            q = (q * cos_ref[at, :] + partner(q) * sin_ref[at, :]).astype(BF)
            k = (k * cos_ref[at, :] + partner(k) * sin_ref[at, :]).astype(BF)
            qkv[at, 0:hd] = q
            qkv[at, hd : 2 * hd] = k
            qkv[at, 2 * hd : 3 * hd] = v.astype(BF)
            row = lax.broadcasted_iota(jnp.int32, (blk, LANES), 0) + r
            inside = (row >= lane_first) & (row < lane_end)
            fk = jnp.where(inside, 1.0, 0.0)
            fq = jnp.where(inside | (lane >= docs), 0.0, MASKED)
            head_inputs(qs, ks, at, q.astype(F32), k.astype(F32), fq, fk, heads)
            vt[:, at] = v.T.astype(BF)
            kt[:, at] = k.astype(F32).T.astype(BF)
            dk[at, :] = jnp.zeros((blk, LANES), F32)
            dv[at, :] = jnp.zeros((blk, LANES), F32)
        dsum.join(0)
        dsum.finish()
        dm[...] = ad[0]
        dfs[0] = ad[0].astype(BF)
        df_f = spread(dfs)
        wait_all(passed[0])
        wo_f = spread(wos, wos.at[0])
        flights = []
        for n in range(blocks):
            r, stop = n * blk, (n + 1) * blk
            found = []
            for h in range(heads):
                e, inv = softmax_block(ks, qs, h, r, stop)
                ps[n][h] = (e * inv).astype(BF)
                found.append(dot_nn(vt[h * HEAD : (h + 1) * HEAD, 0:stop], ps[n][h]))
            att[0, r:stop, :] = jnp.concatenate(found, axis=0).T.astype(BF)
            flights.append(spread(att.at[:, r:stop, :], att.at[0, r:stop, :]))
            if n == 0:
                pass_on(wi_ref, came[1], passed[1])
                df_f.relay()
                wo_f.relay()
        place_of = lax.broadcasted_iota(jnp.int32, (blk, LANES), 1) // HEAD
        for r in range(0, total, blk):
            at = slice(r, r + blk)
            q = widen(qkv[at, 0:hd].astype(F32))
            for h in range(heads):
                qs[h, at, :] = jnp.where(place_of == h, q, 0.0).astype(BF)

        pass_on(wd_ref, came[2], passed[2])
        wo_f.all_ready()
        for e in range(fs_count):
            wo_at[flip(fs, e)] = wos[e]
        for e in range(fs_count):
            hold[:, e * hd : (e + 1) * hd] = wo_at[e]
        for e in range(fs_count):
            turned[e * hd : (e + 1) * hd, :] = hold[pl.ds(base_of(e, hd), hd), :]
        for flight in flights:
            flight.relay()
        for flight in flights:
            flight.all_ready()
        for e in range(fs_count):
            att_rel[:, e * hd : (e + 1) * hd] = att[e]

        work[:, 0:width] = x_all[...] + dot_nn(att_rel[...], turned[...])
        for r in range(0, total, HEAD):
            m = work[r : r + HEAD, 0:width]
            m_all[r : r + HEAD, :] = m
            n2[r : r + HEAD, :] = layer_norm(m, gain_ref[3:4, :]).astype(BF)
        wait_all(passed[1])
        work[:, 0:fj] = dot_nn(n2[...], wi_ref[...])
        for r in range(0, total, HEAD):
            value, rate = gelu_both(work[r : r + HEAD, 0:fj])
            hid[r : r + HEAD, :] = value.astype(BF)
            slope[r : r + HEAD, :] = rate
        wait_all(passed[2])
        work[:, 0:width] = dot_nt(hid[...], wd_ref[...])

        def give_out(scatter, source):
            for e in reversed(range(fs_count)):
                value = source[pl.ds(base_of(e, short), short), 0:width]
                if e % 2:
                    scatter.sbuf[e // 2] = value.astype(BF)
                    scatter.send_odd(e // 2)
                else:
                    scatter.acc[e // 2] = value

        fwd = Scatter(net, dp, fs, fs_count, sf, rf, xf, yf, af)
        give_out(fwd, work)
        for e in range(fs_count):
            df_f.ready(e)
            df_all[pl.ds(base_of(e, short), short), :] = dfs[e]
        work[:, 0:fj] = dot_nn(df_all[...], wd_ref[...])
        for r in range(0, total, HEAD):
            at = slice(r, r + HEAD)
            dpre[at, :] = (work[at, 0:fj] * slope[at, :]).astype(BF)
        work[:, 0:width] = dot_nt(dpre[...], wi_ref[...])
        bwd = Scatter(net, dp, fs, fs_count, sb, rb, xb, yb, ab)
        give_out(bwd, work)
        for j in range(1, half):
            bwd.join(j)
        bwd.upper()
        for j in range(1, half):
            fwd.join(j)
        fwd.upper()
        g_ff[:, 0:fj] = dot_tn(n2[...], dpre[...]).astype(BF)
        g_ff[:, fj : 2 * fj] = dot_tn(df_all[...], hid[...]).astype(BF)
        ff_rows = RowSum(net, (dp, fs, y_count, z_count, fs_count, rw), g_ff, yg, zsg, zrg, sum_ff)
        ff_rows.start()
        bwd.join(0)
        bwd.finish()
        m_own = m_all[pl.ds(base_of(0, short), short), :]
        dx, dg = layer_norm_back(m_own, gain_ref[3:4, :], ab[0])
        dx = dx + dm[...]
        dm[...] = dx
        low_dx = dx.astype(BF)
        got = dot_nt(low_dx, hold[...]).astype(BF)
        for e in range(fs_count):
            do_out[e] = got[:, e * hd : (e + 1) * hd]
            da_out[e] = low_dx[:, e * hd : (e + 1) * hd]
        do_f = exchange(do_out, do_in)
        da_f = exchange(da_out, da_in)
        gain_two = jnp.sum(dg, axis=0, keepdims=True)

        fwd.join(0)
        fwd.finish()
        s1s[0] = (m_own + af[0]).astype(BF)
        s1_f = spread(s1s)
        z_f = exchange(z_ref, z_rel)
        wait_all(do_f)
        for e in range(fs_count):
            at = pl.ds(base_of(e, short), short)
            do = widen(do_in[e].astype(F32))
            lane_head = lax.broadcasted_iota(jnp.int32, (short, LANES), 1) // HEAD
            for h in range(heads):
                ks[h, at, :] = jnp.where(lane_head == h, do, 0.0).astype(BF)
        wait_all(da_f)
        for e in range(fs_count):
            cols[pl.ds(base_of(e, short), short), :] = da_in[e]
        s1_f.relay()

        g_out = dot_tn(att_rel[...], cols[...]).astype(BF)
        for e in range(fs_count):
            group[pl.ds(base_of(e, hd), hd), cb - hd : cb] = g_out[e * hd : (e + 1) * hd, :]
        for n in range(blocks):
            r, stop = n * blk, (n + 1) * blk
            at = slice(r, stop)
            found = []
            add_k = add_v = None
            for h in range(heads):
                p = ps[n][h]
                grad = dot_nt(widen(qkv[0:stop, 2 * hd : 3 * hd]), ks[h, at, :])
                wide = p.astype(F32)
                inner = jnp.sum(wide * grad, axis=0, keepdims=True)
                dr = (wide * (grad - inner) * 0.125).astype(BF)
                part_v = dot_nn(p, ks[h, at, :])
                part_k = dot_nn(dr, qs[h, at, :])
                add_v = part_v if add_v is None else add_v + part_v
                add_k = part_k if add_k is None else add_k + part_k
                found.append(dot_nn(kt[h * HEAD : (h + 1) * HEAD, 0:stop], dr))
            dk[0:stop, :] += add_k
            dv[0:stop, :] += add_v
            dq = jnp.concatenate(found, axis=0).T
            dqkv[at, 0:hd] = (dq * cos_ref[at, :] - partner(dq) * sin_ref[at, :]).astype(BF)
        for r in range(0, total, blk):
            at = slice(r, r + blk)
            grad = dk[at, 0:hd]
            dqkv[at, hd : 2 * hd] = (grad * cos_ref[at, :] - partner(grad) * sin_ref[at, :]).astype(BF)
            dqkv[at, 2 * hd : 3 * hd] = dv[at, 0:hd].astype(BF)
        work[:, 0:width] = dot_nt(dqkv[...], wq_ref[...])
        first = Scatter(net, dp, fs, fs_count, sa, ra, xa, ya, aa)
        give_out(first, work)
        for j in range(1, half):
            first.join(j)
        first.upper()
        group[:, 0 : 3 * hd] = dot_tn(n1[...], dqkv[...]).astype(BF)
        s1_f.all_ready()
        lift_f = []
        for e in range(fs_count):
            part = dot_nn(s1s[e], wu_ref[...]).astype(BF)
            if e:
                lift_send[e] = part
                lift_f.append(net.start(lift_send.at[e], lift_rel.at[e], (dp, flip(fs, e))))
            else:
                lift_rel[0] = part
        g_up = jnp.zeros((width, pc), F32)
        for e in range(fs_count):
            g_up = g_up + dot_tn(s1s[e], c_ref[e])
        group[:, 3 * hd + pc : 3 * hd + 2 * pc] = g_up.astype(BF)
        for m in range(1, z_count):
            ff_rows.service(m)
        first.join(0)
        first.finish()
        dx, dg = layer_norm_back(s0_ref[...], gain_ref[2:3, :], aa[0])
        ds0s[0] = (dx + dm[...]).astype(BF)
        gain_one = jnp.sum(dg, axis=0, keepdims=True)
        which = lax.broadcasted_iota(jnp.int32, (8, width), 0)
        dgain[...] = jnp.where(which == 0, gain_one, jnp.where(which == 1, gain_two, 0.0))

        hop = net.make(ds0s.at[0, 0:HALO, :], nxt, (dp, lax.rem(fs + fs_count - 1, fs_count)))

        @pl.when(fs > 0)
        def _():
            hop.start()

        ds0_f = spread(ds0s)
        row = lax.broadcasted_iota(jnp.int32, (short, LANES), 0) + fs * short + 1
        shut = jnp.max(jnp.where((row == lane_first) | (row >= total), 1.0, 0.0), axis=1, keepdims=True) > 0.0

        @pl.when(fs < fs_count - 1)
        def _():
            hop.wait_recv()

        grad = jnp.concatenate([ds0s[0], nxt[...]], axis=0)
        for e in range(fs_count):
            lift_at = dot_nn(grad, wp_ref[e])
            spread_rows[flip(fs, e)] = lift_at
        dz = jnp.concatenate([spread_rows[e] for e in range(fs_count)], axis=1)
        strided_write(thin, 0, short, dz[0:short, 2 * width : 3 * width])
        for k in range(2):
            part = dz[1 : short + 1, k * width : (k + 1) * width]
            strided_write(thin, k + 1, short, jnp.where(shut, 0.0, part))
        value = cot_ref[...].astype(F32) + spread_read(thin)
        da[...] = value
        dfs_out[0] = value.astype(BF)
        out_f = spread(dfs_out)
        ff_rows.service(0)
        ds0_f.relay()
        for copy in z_f:
            copy.wait_recv()
        g_pool = jnp.zeros((width, pc), F32)
        for e in range(fs_count):
            ds0_f.ready(e)
            g_pool = g_pool + dot_tn(ds0s[e], z_rel[e])
        group[:, 3 * hd : 3 * hd + pc] = g_pool.astype(BF)

        wait_all(lift_f)
        for e in range(fs_count):
            lift[flip(fs, e)] = lift_rel[e].astype(F32)
        lifted = jnp.concatenate([lift[e] for e in range(fs_count)], axis=1)
        for n in range(3):
            strided_write(thin, n, short, lifted[:, n * width : (n + 1) * width])
        out[...] = (after_ref[...] + spread_read(thin)).astype(BF)
        ff_rows.finish()
        out_f.relay()
        out_f.all_ready()

        @pl.when(fs > 0)
        def _():
            hop.wait_send()

        net.finish()

    wide = max(width, fj)
    pieces = (fs_count, short, width)
    scatter = [((half, short, width), BF)] * 2 + [((half - 1, short, width), BF)] * 2 + [((half, short, width), F32)]
    outs = [((rows, width), BF), ((rows, width), F32), ((fs_count, rows, width), BF), ((width, cb), BF), ((rw, 2 * fj), F32), ((8, width), F32)]
    scratch = [
        ((fs_count, width, hd), BF),
        ((width, fj), BF),
        ((width, fj), BF),
        ((width, 2 * fj), BF),
        ((y_count - 1, z_count, rw, 2 * fj), BF),
        ((z_count - 1, rw, 2 * fj), BF),
        ((z_count - 1, rw, 2 * fj), BF),
        *scatter,
        ((fs_count, short, pc), BF),
        ((fs_count, short, pc), BF),
        (pieces, BF),
        ((total, width), F32),
        ((fs_count, width, hd), BF),
        ((width, width), BF),
        ((width, width), BF),
        ((fs_count, short, pc), BF),
        (pieces, BF),
        ((total, width), BF),
        ((fs_count, short, hd), BF),
        ((fs_count, short, hd), BF),
        ((fs_count, short, hd), BF),
        ((fs_count, short, hd), BF),
        ((total, hd), BF),
        (pieces, BF),
        (pieces, BF),
        ((HALO, width), BF),
        ((total, width), BF),
        ((total, width), BF),
        ((total, 3 * hd), BF),
        ((fs_count, total, hd), BF),
        ((total, width), BF),
        ((heads, total, LANES), BF),
        ((heads, total, LANES), BF),
        ((hd, total), BF),
        ((hd, total), BF),
        ((total, LANES), F32),
        ((total, LANES), F32),
        ((total, 3 * hd), BF),
        ((total, wide), F32),
        ((total, fj), BF),
        ((total, fj), F32),
        ((total, fj), BF),
        ((total, width), F32),
        ((short, width), F32),
        *scatter,
        *scatter,
        *scatter,
        ((width // LANES, rows, LANES), F32),
        ((fs_count, short + HALO, pc), F32),
        ((fs_count, short, pc), F32),
    ]
    tail = [pltpu.VMEM((heads, (n + 1) * blk, blk), BF) for n in range(blocks)]
    arrays = (s0, after, z_blocks, cot, c_rel, wq, wu, wout, win, wdown, wp, gain_rows, cos, sin, triples)
    return pl.pallas_call(
        body,
        out_shape=[jax.ShapeDtypeStruct(s, t) for s, t in outs],
        in_specs=[vmem()] * 14 + [smem()],
        out_specs=[vmem()] * len(outs),
        scratch_shapes=[pltpu.VMEM(s, t) for s, t in scratch] + [pltpu.SemaphoreType.DMA((sems,))] * 2 + tail,
        compiler_params=pltpu.CompilerParams(collective_id=2, has_side_effects=True, vmem_limit_bytes=VMEM_BYTES),
        cost_estimate=cost(2e10, 2e7),
        name="middle",
    )(*arrays)


def owners_of(amount, dp_count, fs_count):
    found = []
    half = dp_count // 2
    for k in range(amount):
        found.append((dp_count // 4 + k % half, (2 * (k // half)) % fs_count + (2 * (k // half)) // fs_count))
    return found


def round_up(width):
    return -(-width // LANES) * LANES


def newton_schulz(box, x, norm, count, width, dp_count, rw, done):
    coef_a, coef_b, coef_c = NS_COEFS
    rows = dp_count * rw
    square = jnp.zeros((1, 1), F32)
    for at in range(count):
        block = box[at * dp_count : (at + 1) * dp_count, :, 0:width].reshape(rows, width)
        x[:, at * width : (at + 1) * width] = block
        wide = block.astype(F32)
        square = square + jnp.sum(jnp.sum(wide * wide, axis=0, keepdims=True), axis=1, keepdims=True)
    length = jnp.sqrt(square)
    norm[...] = jnp.broadcast_to(length, norm.shape)
    scale = 1.0 / (length + NORM_EPS)
    span = count * width
    for turn in range(NS_STEPS):
        gram = dot_nt(x[:, 0:span], x[:, 0:span])
        if turn == 0:
            gram = gram * (scale * scale)
        gram = gram.astype(BF)
        poly = (coef_b * gram.astype(F32) + coef_c * dot_nn(gram, gram)).astype(BF)
        for at in range(count):
            here = slice(at * width, (at + 1) * width)
            block = x[:, here]
            new = coef_a * block.astype(F32) + dot_nn(poly, block)
            if turn == 0:
                new = new * scale
            if turn < NS_STEPS - 1:
                x[:, here] = new.astype(BF)
            else:
                box[at * dp_count : (at + 1) * dp_count, :, 0:width] = new.astype(BF).reshape(dp_count, rw, width)
                done(at)


def muon(y_count, dp_count, fs_count, sums, moments, dgain):
    sum_q, sum_o, sum_ff, sum_ff1, sum_rest = sums
    rw, hd = sum_o.shape
    fj = sum_ff.shape[1] // 2
    pc = moments[4].shape[1]
    width = rw * dp_count
    z_count = dp_count // y_count
    devices = dp_count * fs_count
    widths = [fj, fj, fj, fj, 3 * hd, 3 * hd, pc, pc, hd, hd]
    widths = [round_up(w) for w in widths]
    amount, wide = len(widths), max(widths)
    owners = owners_of(amount, dp_count, fs_count)
    classes = sorted(set(widths))
    sems = 16
    z_bits = z_count.bit_length() - 1

    def body(
        q_ref, o_ref, ff_ref, ff1_ref, rest_ref, mq, mo, mi, md, mp, mu, ga,
        out, norms, dgain_out, box, x, norm, tiles, tsend, *rest_refs,
    ):
        pieces = rest_refs[:amount]
        send_sem, recv_sem, push_send, push_recv, give_send, give_recv, norm_send, norm_recv = rest_refs[amount:]
        dp, fs = lax.axis_index("dp"), lax.axis_index("fsdp")
        slot = fs * dp_count + dp
        net = Net(send_sem, recv_sem)

        def put(k, value):
            have = value.shape[1]
            if have < widths[k]:
                value = jnp.concatenate([value, jnp.zeros((rw, widths[k] - have), F32)], axis=1)
            pieces[k][...] = value.astype(BF)

        at = 2 * pc
        put(0, MOMENT_DECAY * mi[0] + ff_ref[:, 0:fj])
        put(1, MOMENT_DECAY * mi[1] + ff1_ref[:, 0:fj])
        put(2, MOMENT_DECAY * md[0] + ff_ref[:, fj : 2 * fj])
        put(3, MOMENT_DECAY * md[1] + ff1_ref[:, fj : 2 * fj])
        for b in range(2):
            put(4 + b, MOMENT_DECAY * mq[b] + jnp.concatenate([q_ref[b, t] for t in range(3)], axis=1))
        put(6, MOMENT_DECAY * mp[...] + rest_ref[:, 0:pc])
        put(7, MOMENT_DECAY * mu[...] + rest_ref[:, pc : 2 * pc])
        put(8, MOMENT_DECAY * mo[0] + o_ref[...])
        put(9, MOMENT_DECAY * mo[1] + rest_ref[:, at:])
        if any(w != wide for w in widths):
            box[...] = jnp.zeros(box.shape, BF)

        barrier = pltpu.get_barrier_semaphore()

        def greet(t, carry):
            @pl.when(t != slot)
            def _():
                there = (lax.rem(t, dp_count), lax.div(t, dp_count))
                pl.semaphore_signal(barrier, inc=1, device_id=there, device_id_type=MESH)

            return carry

        lax.fori_loop(0, devices, greet, 0)
        pl.semaphore_wait(barrier, devices - 1)

        mine = [(dp == owners[k][0]) & (fs == owners[k][1]) for k in range(amount)]
        for k in range(amount):
            copy = pltpu.make_async_remote_copy(
                src_ref=pieces[k],
                dst_ref=box.at[slot, :, 0 : widths[k]],
                send_sem=push_send.at[k],
                recv_sem=push_recv,
                device_id=owners[k],
                device_id_type=MESH,
            )

            @pl.when(jnp.logical_not(mine[k]))
            def _():
                copy.start()

            @pl.when(mine[k])
            def _():
                box[slot, :, 0 : widths[k]] = pieces[k][...]

        total = ga[...]
        for n in range(z_bits):
            tsend[n] = total
            hop = net.start(tsend.at[n], tiles.at[n], (flip(dp, y_count << n), fs))
            hop.wait_recv()
            total = total + tiles[n]
        dgain_out[...] = total

        for k in range(amount):

            @pl.when(mine[k])
            def _():
                landed = box.at[0 : devices - 1, :, 0 : widths[k]]
                pltpu.make_async_copy(landed, landed, push_recv).wait()

        which_k = jnp.int32(0)
        for k in range(1, amount):
            which_k = which_k + k * mine[k].astype(jnp.int32)
        for w in classes:
            chosen = None
            for k in range(amount):
                if widths[k] == w:
                    chosen = mine[k] if chosen is None else chosen | mine[k]

            @pl.when(chosen)
            def _():
                def done(block):
                    def give(i, carry):
                        t = block * dp_count + i

                        @pl.when(t != slot)
                        def _():
                            pltpu.make_async_remote_copy(
                                src_ref=box.at[t, :, 0:w],
                                dst_ref=out.at[which_k, :, 0:w],
                                send_sem=give_send,
                                recv_sem=give_recv.at[which_k],
                                device_id=(i, block),
                                device_id_type=MESH,
                            ).start()
                            pltpu.make_async_remote_copy(
                                src_ref=norm,
                                dst_ref=norms.at[which_k],
                                send_sem=norm_send,
                                recv_sem=norm_recv.at[which_k],
                                device_id=(i, block),
                                device_id_type=MESH,
                            ).start()

                        return carry

                    lax.fori_loop(0, dp_count, give, 0)

                newton_schulz(box, x, norm, fs_count, w, dp_count, rw, done)
                out[which_k, :, 0:w] = box[slot, :, 0:w]
                norms[which_k] = norm[...]

        for k in range(amount):
            w = widths[k]

            @pl.when(jnp.logical_not(mine[k]))
            def _():
                landed = out.at[k, :, 0:w]
                pltpu.make_async_copy(landed, landed, give_recv.at[k]).wait()
                pltpu.make_async_copy(norms.at[k], norms.at[k], norm_recv.at[k]).wait()
                pltpu.make_async_copy(pieces[k], pieces[k], push_send.at[k]).wait()

            @pl.when(mine[k])
            def _():
                left = box.at[0 : devices - 1, :, 0:w]
                pltpu.make_async_copy(left, left, give_send).wait()

                def drain(t, carry):
                    pltpu.make_async_copy(norm, norm, norm_send).wait()
                    return carry

                lax.fori_loop(0, devices - 1, drain, 0)

        net.finish()

    outs = [((amount, rw, wide), BF), ((amount, 8, LANES), F32), ((8, width), F32)]
    scratch = [
        ((devices, rw, wide), BF),
        ((width, fs_count * wide), BF),
        ((8, LANES), F32),
        ((z_bits, 8, width), F32),
        ((z_bits, 8, width), F32),
    ] + [((rw, w), BF) for w in widths]
    dma = pltpu.SemaphoreType.DMA
    return pl.pallas_call(
        body,
        out_shape=[jax.ShapeDtypeStruct(s, t) for s, t in outs],
        in_specs=[vmem()] * 12,
        out_specs=[vmem()] * len(outs),
        scratch_shapes=[pltpu.VMEM(s, t) for s, t in scratch]
        + [dma((sems,)), dma((sems,)), dma((amount,)), dma, dma, dma((amount,)), dma, dma((amount,))],
        compiler_params=pltpu.CompilerParams(collective_id=1, has_side_effects=True, vmem_limit_bytes=VMEM_BYTES),
        name="muon",
    )(sum_q, sum_o, sum_ff, sum_ff1, sum_rest, *moments, dgain)


def backward_all(
    y_count, dp_count, fs_count, da, dfs, n2, hid_in, slope_in, wi, wd, mid, gain_rows, qkv, wo_full, wq, cos, sin, triples, n1, att_rel, tokens, group_b, dgain_b,
    sum_ff1, moments,
):
    rows, width = tokens.shape
    total = rows * fs_count
    fj, hd = wi.shape[1], wq.shape[1] // 3
    heads, docs = hd // HEAD, triples.shape[1]
    z_count, rw = dp_count // y_count, width // dp_count
    cb = group_b.shape[1]
    blk, half = query_rows(total), fs_count // 2
    blocks = total // blk
    sems = 96 + 16 * dp_count

    pc = moments[4].shape[1]
    devices = dp_count * fs_count
    widths = [round_up(w) for w in (fj, fj, fj, fj, 3 * hd, 3 * hd, pc, pc, hd, hd)]
    amount, wide = len(widths), max(widths)
    owners = owners_of(amount, dp_count, fs_count)
    classes = sorted(set(widths))

    def body(
        da_ref, dfs, n2_hbm, hid_hbm, slope_hbm, wi_ref, wd_ref, mid_hbm, gain_ref, qkv_hbm, wo_ref, wq_ref, cos_hbm, sin_hbm, triples_ref, n1_hbm, att_hbm, tok, gb, dgain_two, ff1_ref, mq, mo, mi, md, mp, mu,
        grad_in, dgain_out, sum_b, sum_ff, sum_o, sum_q, out, norms,
        n2_ref, mid_ref, qkv_ref, cos_ref, sin_ref, n1_ref, att_ref, da_low, do_out, do_in, da_out, da_in, hid, slope, dpre, work, qs, ks, kt, dk, dv, dm, cols, g_ff, g_at, g_o,
        sbuf, rbuf, xsend, xrecv, acc, yb, zsb, zrb, qsb, qrb, yf, zsf, zrf, yo, zso, zro, qsa, qra, tiles,
        box, x, norm, send_sem, recv_sem, push_send, push_recv, give_send, give_recv, norm_send, norm_recv,
        *rest,
    ):
        ps, pieces = rest[:blocks], rest[blocks:]
        dp, fs = lax.axis_index("dp"), lax.axis_index("fsdp")
        net = Net(send_sem, recv_sem)
        place = (dp, fs, y_count, z_count, fs_count, rw)
        dqkv = qkv_ref
        loads = {}
        for name, src, dst in (
            ("slope", slope_hbm, slope),
            ("n2", n2_hbm, n2_ref),
            ("hid", hid_hbm, hid),
            ("mid", mid_hbm, mid_ref),
            ("qkv", qkv_hbm, qkv_ref),
            ("att", att_hbm, att_ref),
            ("cos", cos_hbm, cos_ref),
            ("sin", sin_hbm, sin_ref),
            ("n1", n1_hbm, n1_ref),
        ):
            loads[name] = net.local(src, dst)
        barrier = pltpu.get_barrier_semaphore()
        slot = fs * dp_count + dp

        def greet(t, carry):
            @pl.when(t != slot)
            def _():
                there = (lax.rem(t, dp_count), lax.div(t, dp_count))
                pl.semaphore_signal(barrier, inc=1, device_id=there, device_id_type=MESH)

            return carry

        lax.fori_loop(0, devices, greet, 0)
        pl.semaphore_wait(barrier, devices - 1)

        mine = [(dp == owners[k][0]) & (fs == owners[k][1]) for k in range(amount)]

        def push(k, value):
            have = value.shape[1]
            if have < widths[k]:
                value = jnp.concatenate([value, jnp.zeros((rw, widths[k] - have), F32)], axis=1)
            pieces[k][...] = value.astype(BF)
            copy = pltpu.make_async_remote_copy(
                src_ref=pieces[k],
                dst_ref=box.at[slot, :, 0 : widths[k]],
                send_sem=push_send.at[k],
                recv_sem=push_recv,
                device_id=owners[k],
                device_id_type=MESH,
            )

            @pl.when(jnp.logical_not(mine[k]))
            def _():
                copy.start()

            @pl.when(mine[k])
            def _():
                box[slot, :, 0 : widths[k]] = pieces[k][...]

        sum_of_b = RowSum(net, place, gb, yb, zsb, zrb, sum_b, qsb, qrb, sum_q.at[1])
        sum_of_b.start()

        def pull(e, out):
            work[:, 0:fj] = dot_nn(dfs[e], wd_ref[...])
            for r in range(0, rows, HEAD):
                at = slice(e * rows + r, e * rows + r + HEAD)
                dpre[at, :] = (work[r : r + HEAD, 0:fj] * slope[at, :].astype(F32)).astype(BF)
            out[...] = dot_nt(dpre[e * rows : (e + 1) * rows, :], wi_ref[...]).astype(out.dtype)

        def part_into(scatter, e, fill):
            if e % 2:
                fill(e, scatter.sbuf.at[e // 2])
                scatter.send_odd(e // 2)
            else:
                fill(e, scatter.acc.at[e // 2])

        ff_sum = Scatter(net, dp, fs, fs_count, sbuf, rbuf, xsend, xrecv, acc)
        loads["slope"].wait()

        def both_steps(e):
            part_into(ff_sum, e, pull)

        for j in reversed(range(1, half)):
            both_steps(2 * j + 1)
            both_steps(2 * j)
        for j in range(1, half):
            ff_sum.join(j)
        ff_sum.upper()
        both_steps(1)
        both_steps(0)
        sum_of_b.service(1)
        for m in range(2, z_count):
            sum_of_b.service(m)
        ff_sum.join(0)
        loads["hid"].wait()
        loads["n2"].wait()
        g_ff[:, 0:fj] = dot_tn(n2_ref[...], dpre[...]).astype(BF)
        g_ff[:, fj : 2 * fj] = dot_tn(dfs[...].reshape(total, width), hid[...]).astype(BF)
        sum_of_b.service(0)
        sum_of_ff = RowSum(net, place, g_ff, yf, zsf, zrf, sum_ff)
        sum_of_ff.start()

        loads["qkv"].wait()
        lane_first, lane_end, lane = doc_bounds(triples_ref, docs)
        for r in range(0, total, blk):
            at = slice(r, r + blk)
            q = qkv_ref[at, 0:hd].astype(F32)
            k = qkv_ref[at, hd : 2 * hd].astype(F32)
            row = lax.broadcasted_iota(jnp.int32, (blk, LANES), 0) + r
            inside = (row >= 3 * lane_first) & (row < 3 * lane_end)
            fk = jnp.where(inside, 1.0, 0.0)
            fq = jnp.where(inside | (lane >= docs), 0.0, MASKED)
            head_inputs(qs, ks, at, q, k, fq, fk, heads)
            kt[:, at] = k.T.astype(BF)
            dk[at, :] = jnp.zeros((blk, LANES), F32)
            dv[at, :] = jnp.zeros((blk, LANES), F32)

        def recompute(n):
            r = n * blk
            for h in range(heads):
                e, inv = softmax_block(ks, qs, h, r, r + blk)
                ps[n][h] = (e * inv).astype(BF)

        for n in range(blocks // 2):
            recompute(n)

        push(1, MOMENT_DECAY * mi[1] + ff1_ref[:, 0:fj])
        push(3, MOMENT_DECAY * md[1] + ff1_ref[:, fj : 2 * fj])

        ff_sum.finish()
        loads["mid"].wait()
        for r in range(0, rows, LANES):
            at = slice(r, r + LANES)
            dx, dg = layer_norm_back(mid_ref[at, :], gain_ref[1:2, :], acc[0, at, :])
            dx = dx + da_ref[at, :]
            dm[at, :] = dx
            da_low[at, :] = dx.astype(BF)
            dg = jnp.sum(dg, axis=0, keepdims=True)
            gain_two = dg if r == 0 else gain_two + dg
        got = dot_nt(da_low[...], wo_ref[...]).astype(BF)
        for e in range(fs_count):
            do_out[e] = got[:, e * hd : (e + 1) * hd]
            da_out[e] = da_low[:, e * hd : (e + 1) * hd]

        def exchange(blocks_of, landed):
            found = []
            for e in range(1, fs_count):
                found.append(net.start(blocks_of.at[flip(fs, e)], landed.at[e], (dp, flip(fs, e))))
            landed[0] = blocks_of[fs]
            return found

        do_f = exchange(do_out, do_in)
        da_f = exchange(da_out, da_in)
        for n in range(blocks // 2, blocks):
            recompute(n)
        for m in range(1, z_count):
            sum_of_ff.service(m)
        sum_of_ff.service(0)

        place_of = lax.broadcasted_iota(jnp.int32, (blk, LANES), 1) // HEAD
        for r in range(0, total, blk):
            at = slice(r, r + blk)
            q = widen(qkv_ref[at, 0:hd].astype(F32))
            for h in range(heads):
                qs[h, at, :] = jnp.where(place_of == h, q, 0.0).astype(BF)
        lane_head = lax.broadcasted_iota(jnp.int32, (rows, LANES), 1) // HEAD
        for e in range(fs_count):
            if e:
                do_f[e - 1].wait_recv()
            base = pl.multiple_of(flip(fs, e) * rows, 16)
            do = widen(do_in[e].astype(F32))
            for h in range(heads):
                ks[h, pl.ds(base, rows), :] = jnp.where(lane_head == h, do, 0.0).astype(BF)
        for e in range(fs_count):
            if e:
                da_f[e - 1].wait_recv()
            cols[pl.ds(pl.multiple_of(flip(fs, e) * rows, 16), rows), :] = da_in[e]

        loads["att"].wait()
        g_out = dot_tn(att_ref[...], cols[...]).astype(BF)
        for e in range(fs_count):
            base = pl.multiple_of(flip(fs, e) * hd, 16)
            g_o[pl.ds(base, hd), :] = g_out[e * hd : (e + 1) * hd, :]
        sum_of_o = RowSum(net, place, g_o, yo, zso, zro, sum_o)
        sum_of_o.start()
        sum_of_b.finish()
        push(5, MOMENT_DECAY * mq[1] + jnp.concatenate([sum_q[1, t] for t in range(3)], axis=1))
        push(6, MOMENT_DECAY * mp[...] + sum_b[:, 0:pc])
        push(7, MOMENT_DECAY * mu[...] + sum_b[:, pc : 2 * pc])
        push(9, MOMENT_DECAY * mo[1] + sum_b[:, 2 * pc :])

        loads["cos"].wait()
        loads["sin"].wait()
        for n in range(blocks):
            r, stop = n * blk, (n + 1) * blk
            at = slice(r, stop)
            found = []
            add_k = add_v = None
            for h in range(heads):
                p = ps[n][h]
                v = widen(qkv_ref[0:stop, 2 * hd : 3 * hd])
                grad = dot_nt(v, ks[h, at, :])
                wide = p.astype(F32)
                middle = jnp.sum(wide * grad, axis=0, keepdims=True)
                dr = (wide * (grad - middle) * 0.125).astype(BF)
                part_v = dot_nn(p, ks[h, at, :])
                part_k = dot_nn(dr, qs[h, at, :])
                add_v = part_v if add_v is None else add_v + part_v
                add_k = part_k if add_k is None else add_k + part_k
                found.append(dot_nn(kt[h * HEAD : (h + 1) * HEAD, 0:stop], dr))
            dk[0:stop, :] += add_k
            dv[0:stop, :] += add_v
            dq = jnp.concatenate(found, axis=0).T
            dqkv[at, 0:hd] = (dq * cos_ref[at, :] - partner(dq) * sin_ref[at, :]).astype(BF)
            if n == blocks // 2:
                for m in range(1, z_count):
                    sum_of_o.service(m)
                sum_of_o.service(0)
        for r in range(0, total, blk):
            at = slice(r, r + blk)
            grad = dk[at, 0:hd]
            dqkv[at, hd : 2 * hd] = (grad * cos_ref[at, :] - partner(grad) * sin_ref[at, :]).astype(BF)
            dqkv[at, 2 * hd : 3 * hd] = dv[at, 0:hd].astype(BF)
        loads["n1"].wait()
        g_at[...] = dot_tn(n1_ref[...], dqkv[...]).astype(BF)
        sum_of_at = HeadSum(net, place, g_at, qsa, qra, sum_q.at[0])
        sum_of_at.start()

        ff_sum.sent()
        at_sum = Scatter(net, dp, fs, fs_count, sbuf, rbuf, xsend, xrecv, acc)
        tiles[0] = jnp.zeros((8, width), F32)

        def push_out(e, out):
            base = pl.multiple_of(flip(fs, e) * rows, 16)
            part = dot_nt(dqkv[pl.ds(base, rows), :], wq_ref[...])
            out[...] = part.astype(out.dtype)
            work[:, 0:width] = part
            total_of = jnp.zeros((8, width), F32)
            for r in range(0, rows, HEAD):
                grown = work[r : r + HEAD, 0:width] * n1_ref[pl.ds(base + r, HEAD), :].astype(F32)
                total_of = total_of + jnp.sum(grown.reshape(HEAD // 8, 8, width), axis=0)
            tiles[0] = tiles[0] + total_of

        for e in reversed(range(2, fs_count)):
            part_into(at_sum, e, push_out)
        part_into(at_sum, 1, push_out)
        for j in range(1, half):
            at_sum.join(j)
        at_sum.upper()
        part_into(at_sum, 0, push_out)
        gain_one = jnp.sum(tiles[0], axis=0, keepdims=True) / gain_ref[0:1, :]
        which = lax.broadcasted_iota(jnp.int32, (8, width), 0)
        both = jnp.where(which == 0, gain_one, jnp.where(which == 1, gain_two, 0.0))
        both = jnp.where(which == 2, dgain_two[0:1, :], jnp.where(which == 3, dgain_two[1:2, :], both))
        hops = [(dp, flip(fs, 1 << n)) for n in range(fs_count.bit_length() - 1)]
        hops += [(flip(dp, 1 << n), fs) for n in range(dp_count.bit_length() - 1)]

        def hop_out(n, value):
            tiles[1 + n] = value
            return net.start(tiles.at[1 + n], tiles.at[1 + len(hops) + n], hops[n])

        hop = hop_out(0, both)
        sum_of_ff.finish()
        push(0, MOMENT_DECAY * mi[0] + sum_ff[:, 0:fj])
        push(2, MOMENT_DECAY * md[0] + sum_ff[:, fj : 2 * fj])
        sum_of_o.finish()
        push(8, MOMENT_DECAY * mo[0] + sum_o[...])
        at_sum.join(0)
        sum_of_at.finish()
        push(4, MOMENT_DECAY * mq[0] + jnp.concatenate([sum_q[0, t] for t in range(3)], axis=1))
        hop.wait_recv()
        both = both + tiles[len(hops) + 1]
        hop = hop_out(1, both)
        at_sum.finish()
        for n in range(2, len(hops) - 1):
            hop.wait_recv()
            both = both + tiles[len(hops) + n]
            hop = hop_out(n, both)
        for r in range(0, rows, LANES):
            at = slice(r, r + LANES)
            dx, _ = layer_norm_back(tok[at, :].astype(F32), gain_ref[0:1, :], acc[0, at, :])
            grad_in[at, :] = dx + dm[at, :]

        for k in range(amount):

            @pl.when(mine[k])
            def _():
                landed = box.at[0 : devices - 1, :, 0 : widths[k]]
                pltpu.make_async_copy(landed, landed, push_recv).wait()

        which_k = jnp.int32(0)
        for k in range(1, amount):
            which_k = which_k + k * mine[k].astype(jnp.int32)
        for w in classes:
            chosen = None
            for k in range(amount):
                if widths[k] == w:
                    chosen = mine[k] if chosen is None else chosen | mine[k]

            @pl.when(chosen)
            def _():
                def done(block):
                    def give(i, carry):
                        t = block * dp_count + i

                        @pl.when(t != slot)
                        def _():
                            pltpu.make_async_remote_copy(
                                src_ref=box.at[t, :, 0:w],
                                dst_ref=out.at[which_k, :, 0:w],
                                send_sem=give_send,
                                recv_sem=give_recv.at[which_k],
                                device_id=(i, block),
                                device_id_type=MESH,
                            ).start()
                            pltpu.make_async_remote_copy(
                                src_ref=norm,
                                dst_ref=norms.at[which_k],
                                send_sem=norm_send,
                                recv_sem=norm_recv.at[which_k],
                                device_id=(i, block),
                                device_id_type=MESH,
                            ).start()

                        return carry

                    lax.fori_loop(0, dp_count, give, 0)

                newton_schulz(box, x, norm, fs_count, w, dp_count, rw, done)
                out[which_k, :, 0:w] = box[slot, :, 0:w]
                norms[which_k] = norm[...]

        last = len(hops) - 1
        hop.wait_recv()
        both = both + tiles[len(hops) + last]
        hop = hop_out(last, both)
        hop.wait_recv()
        dgain_out[...] = both + tiles[1 + len(hops) + last]

        for k in range(amount):
            w = widths[k]

            @pl.when(jnp.logical_not(mine[k]))
            def _():
                landed = out.at[k, :, 0:w]
                pltpu.make_async_copy(landed, landed, give_recv.at[k]).wait()
                pltpu.make_async_copy(norms.at[k], norms.at[k], norm_recv.at[k]).wait()
                pltpu.make_async_copy(pieces[k], pieces[k], push_send.at[k]).wait()

            @pl.when(mine[k])
            def _():
                left = box.at[0 : devices - 1, :, 0:w]
                pltpu.make_async_copy(left, left, give_send).wait()

                def drain(t, carry):
                    pltpu.make_async_copy(norm, norm, norm_send).wait()
                    return carry

                lax.fori_loop(0, devices - 1, drain, 0)

        net.finish()

    outs = [
        ((rows, width), F32),
        ((8, width), F32),
        ((rw, cb - 3 * hd), F32),
        ((rw, 2 * fj), F32),
        ((rw, hd), F32),
        ((2, 3, rw, hd), F32),
        ((amount, rw, wide), BF),
        ((amount, 8, LANES), F32),
    ]
    span = max(width, fj)
    zy = (y_count - 1, z_count, rw)
    scratch = [
        ((total, width), BF),
        ((rows, width), F32),
        ((total, 3 * hd), BF),
        ((total, hd), F32),
        ((total, hd), F32),
        ((total, width), BF),
        ((total, width), BF),
        ((rows, width), BF),
        ((fs_count, rows, hd), BF),
        ((fs_count, rows, hd), BF),
        ((fs_count, rows, hd), BF),
        ((fs_count, rows, hd), BF),
        ((total, fj), BF),
        ((total, fj), BF),
        ((total, fj), BF),
        ((rows, span), F32),
        ((heads, total, LANES), BF),
        ((heads, total, LANES), BF),
        ((hd, total), BF),
        ((total, LANES), F32),
        ((total, LANES), F32),
        ((rows, width), F32),
        ((total, hd), BF),
        ((width, 2 * fj), BF),
        ((width, 3 * hd), BF),
        ((width, hd), BF),
        ((half, rows, width), BF),
        ((half, rows, width), BF),
        ((half - 1, rows, width), BF),
        ((half - 1, rows, width), BF),
        ((half, rows, width), F32),
        (zy + (cb,), BF),
        ((z_count - 1, rw, cb - 3 * hd), BF),
        ((z_count - 1, rw, cb - 3 * hd), BF),
        ((z_count, 3, rw, hd), BF),
        ((z_count, 3, rw, hd), BF),
        (zy + (2 * fj,), BF),
        ((z_count - 1, rw, 2 * fj), BF),
        ((z_count - 1, rw, 2 * fj), BF),
        (zy + (hd,), BF),
        ((z_count - 1, rw, hd), BF),
        ((z_count - 1, rw, hd), BF),
        ((dp_count, 3, rw, hd), BF),
        ((dp_count, 3, rw, hd), BF),
        ((2 * (fs_count.bit_length() + dp_count.bit_length() - 2) + 1, 8, width), F32),
        ((devices, rw, wide), BF),
        ((width, fs_count * wide), BF),
        ((8, LANES), F32),
    ]
    tail = [pltpu.VMEM((heads, (n + 1) * blk, blk), BF) for n in range(blocks)]
    tail += [pltpu.VMEM((rw, w), BF) for w in widths]
    dma = pltpu.SemaphoreType.DMA
    tail = [dma((sems,)), dma((sems,)), dma((amount,)), dma, dma, dma((amount,)), dma, dma((amount,))] + tail
    arrays = (da, dfs, n2, hid_in, slope_in, wi, wd, mid, gain_rows, qkv, wo_full, wq, cos, sin, triples, n1, att_rel, tokens, group_b, dgain_b, sum_ff1, *moments)
    return pl.pallas_call(
        body,
        out_shape=[jax.ShapeDtypeStruct(s, t) for s, t in outs],
        in_specs=[hbm() if n in (2, 3, 4, 7, 9, 12, 13, 15, 16) else smem() if n == 14 else vmem() for n in range(27)],
        out_specs=[vmem()] * len(outs),
        scratch_shapes=[pltpu.VMEM(s, t) for s, t in scratch] + tail,
        compiler_params=pltpu.CompilerParams(collective_id=5, has_side_effects=True, vmem_limit_bytes=VMEM_BYTES),
        cost_estimate=cost(4e10, 3e7),
        name="backward_all",
    )(*arrays)


def update(dp_arr, sums, results, norms, roots, dgain, moments, weights, m_gains_t, gains_t, layer_out, grad_in):
    sum_q, sum_o, sum_ff, sum_ff1, sum_rest = sums
    rw, hd = sum_o.shape
    fj = sum_ff.shape[1] // 2
    pc = moments[4].shape[1]
    width = dgain.shape[1]

    def body(me_ref, q_ref, o_ref, ff_ref, ff1_ref, rest_ref, res, norms_ref, roots_ref, dg, *refs):
        m_in, w_in, (mg, g, act, grad), refs = refs[:6], refs[6:12], refs[12:16], refs[16:]
        m_out, w_out, (mg_out, g_out, act_out, grad_out, rms), turned = refs[:6], refs[6:12], refs[12:17], refs[17]
        act_out[...] = act[...]
        grad_out[...] = grad[...]
        at = 2 * pc
        grads = [
            [jnp.concatenate([q_ref[b, t] for t in range(3)], axis=1) for b in range(2)],
            [o_ref[...], rest_ref[:, at:]],
            [ff_ref[:, 0:fj], ff1_ref[:, 0:fj]],
            [ff_ref[:, fj : 2 * fj], ff1_ref[:, fj : 2 * fj]],
            [rest_ref[:, 0:pc]],
            [rest_ref[:, pc : 2 * pc]],
        ]
        places = [(4, 5), (8, 9), (0, 1), (2, 3), (6,), (7,)]
        for kind in range(6):
            for b in range(len(grads[kind])):
                here = (b,) if kind < 4 else (slice(None),)
                have = m_in[kind].shape[-1]
                m_out[kind][here] = MOMENT_DECAY * m_in[kind][here] + grads[kind][b]
                turn = res[places[kind][b], :, 0:have].astype(F32)
                w_out[kind][here] = w_in[kind][here] - STEP_SCALES[kind] * turn
        turned[...] = jnp.concatenate([dg[...], jnp.zeros((LANES - 8, width), F32)], axis=0).T
        mine = turned[pl.ds(pl.multiple_of(me_ref[0] * rw, 16), rw), :].T
        fresh = GAIN_DECAY * mg[...] + mine[0:4, :]
        mg_out[...] = fresh
        g_out[...] = g[...] - GAIN_RATE * fresh
        places = (4, 5, 8, 9, 0, 1, 2, 3, 6, 7)
        lengths = jnp.concatenate([norms_ref[p, 0:1, :] for p in places] + [norms_ref[0, 0:6, :]], axis=0)
        rms[...] = lengths / roots_ref[...]

    outs = [(a.shape, a.dtype) for a in (*moments, *weights, m_gains_t, gains_t, layer_out, grad_in)] + [((16, LANES), F32)]
    return local_kernel(
        body,
        "update",
        outs,
        [((width, LANES), F32)],
        dp_arr,
        sum_q,
        sum_o,
        sum_ff,
        sum_ff1,
        sum_rest,
        results,
        norms,
        roots,
        dgain,
        *moments,
        *weights,
        m_gains_t,
        gains_t,
        layer_out,
        grad_in,
    )


def rope_tables(total, hd):
    half = HEAD // 2
    frequency = (np.float32(10000.0) ** (-np.arange(half, dtype=np.float32) / np.float32(half))).astype(np.float32)
    angle = (np.arange(total, dtype=np.float32)[:, None] * frequency[None, :]).astype(np.float32)
    cos, sin = np.cos(angle), np.sin(angle)
    cos = np.tile(np.concatenate([cos, cos], axis=1), (1, hd // HEAD))
    sin = np.tile(np.concatenate([-sin, sin], axis=1), (1, hd // HEAD))
    return jnp.asarray(cos, F32), jnp.asarray(sin, F32)


def on_device(
    y_count,
    tokens,
    cotangent,
    doc_triples,
    w_qkv,
    w_out,
    w_in,
    w_down,
    w_pool,
    w_up,
    gains,
    m_qkv,
    m_out,
    m_in,
    m_down,
    m_pool,
    m_up,
    m_gains,
):
    rows, width = tokens.shape
    fs_count, dp_count = lax.axis_size("fsdp"), lax.axis_size("dp")
    dp_arr = lax.axis_index("dp").astype(jnp.int32).reshape(1)
    total = rows * fs_count
    hd = width // fs_count

    cos0, sin0 = rope_tables(total, hd)

    old_weights = (w_qkv, w_out, w_in, w_down, w_pool, w_up)
    if total <= 2048:
        (
            n1, qkv, att_rel, n2, hid, slope, wo_full, mid, wqkv0, wi0, wd0, gain_rows, layer_out, da, dfs, group_b, sum_ff1, dgain_b
        ) = forward_all(
            y_count, dp_count, fs_count, tokens, cotangent, doc_triples, old_weights, gains.T, cos0, sin0
        )
    else:
        cos1, sin1 = cos0[: total // 3], sin0[: total // 3]
        (
            n1, qkv, att_rel, wo_full, n2, hid, slope, mid, after, z_blocks, s0, wqkv0, wi0, wd0, wp, wqkv1, wu, c_rel, gain_rows
        ) = forward_one(
            y_count, dp_count, fs_count, tokens, cotangent, doc_triples, old_weights, gains.T, cos0, sin0
        )
        layer_out, da, dfs, group_b, sum_ff1, dgain_b = middle(
            y_count, dp_count, fs_count, s0, after, z_blocks, cotangent, c_rel, wqkv1, wu, old_weights[1:4], wp, gain_rows,
            cos1, sin1, doc_triples,
        )
    moments = (m_qkv, m_out, m_in, m_down, m_pool, m_up)
    kept = (da, dfs, n2, hid, slope, wi0, wd0, mid, gain_rows, qkv, wo_full, wqkv0, cos0, sin0, doc_triples, n1, att_rel, tokens)
    if total <= 2048:
        grad_in, dgain, sum_rest, sum_ff, sum_o, sum_q, results, norms = backward_all(
            y_count, dp_count, fs_count, *kept, group_b, dgain_b, sum_ff1, moments
        )
        sums = (sum_q, sum_o, sum_ff, sum_ff1, sum_rest)
    else:
        grad_in, dgain, sum_rest, sum_ff, sum_o, sum_q = backward_one(
            y_count, dp_count, fs_count, *kept, group_b, dgain_b
        )
        sums = (sum_q, sum_o, sum_ff, sum_ff1, sum_rest)
        results, norms, dgain = muon(y_count, dp_count, fs_count, sums, moments, dgain)

    all_tokens = float(total * dp_count)
    entries = [m.size // (2 if m.ndim == 3 else 1) for m in moments for _ in range(2 if m.ndim == 3 else 1)]
    roots = np.ones((16, LANES), np.float64)
    roots[:10] = np.array([float(n * fs_count * dp_count) * all_tokens for n in entries])[:, None] ** 0.5
    *fresh, gain_moments, new_gains, layer_out, grad_in, rms = update(
        dp_arr, sums, results, norms, jnp.asarray(roots, F32), dgain, moments, old_weights, m_gains.T, gains.T, layer_out, grad_in
    )
    return (layer_out, grad_in, *fresh, gain_moments.T, new_gains.T, rms[:10, 0])


def solution(mesh):
    by_row, by_dp = P(("dp", "fsdp"), None), P("dp", None)
    stacked, flat = P(None, "dp", "fsdp"), P("dp", "fsdp")
    matrices = (stacked,) * 4 + (flat,) * 2
    y_count = max(1, mesh.shape["fsdp"] // 2)
    return jax.shard_map(
        functools.partial(on_device, y_count),
        mesh=mesh,
        in_specs=(by_row, by_row, by_dp, *matrices, by_dp, *matrices, by_dp),
        out_specs=(by_row, by_row, *matrices, *matrices, by_dp, by_dp, P()),
        check_vma=False,
    )
```

```python
import functools

import jax
import jax.numpy as jnp
import numpy as np
from jax import lax
from jax.experimental import pallas as pl
from jax.experimental.pallas import tpu as pltpu
from jax.sharding import PartitionSpec as P

HEAD = 64
NS_STEPS = 5
NS_COEFS = (3.4445, -4.775, 2.0315)
STEP_SCALES = (0.8660254, 1.4142136, 1.0, 0.5, 0.5, 0.8660254)
MOMENT_DECAY = 0.95
GAIN_DECAY = 0.9
GAIN_RATE = 0.001
LN_EPS = 1e-05
NORM_EPS = 1e-07
MASKED = -1e30
HALO = 16
QB = 256
LANES = 128
VMEM_BYTES = 62 << 20
BF = jnp.bfloat16
F32 = jnp.float32
MESH = pl.DeviceIdType.MESH


def dot_nn(left, right):
    return lax.dot_general(left, right, (((1,), (0,)), ((), ())), preferred_element_type=F32)


def dot_nt(left, right):
    return lax.dot_general(left, right, (((1,), (1,)), ((), ())), preferred_element_type=F32)


def dot_tn(left, right):
    return lax.dot_general(left, right, (((0,), (0,)), ((), ())), preferred_element_type=F32)


def layer_norm(values, gain):
    mean = jnp.mean(values, axis=-1, keepdims=True)
    centred = values - mean
    spread = jnp.mean(centred * centred, axis=-1, keepdims=True)
    return centred * lax.rsqrt(spread + LN_EPS) * gain


def layer_norm_back(values, gain, grad):
    mean = jnp.mean(values, axis=-1, keepdims=True)
    centred = values - mean
    spread = jnp.mean(centred * centred, axis=-1, keepdims=True)
    scale = lax.rsqrt(spread + LN_EPS)
    unit = centred * scale
    scaled = grad * gain
    part = jnp.mean(scaled, axis=-1, keepdims=True)
    along = jnp.mean(scaled * unit, axis=-1, keepdims=True)
    return scale * (scaled - part - unit * along), grad * unit


def gelu(values):
    return 0.5 * values * (1.0 + jnp.tanh(0.7978845608028654 * (values + 0.044715 * values * values * values)))


def gelu_both(values):
    square = values * values
    turn = jnp.tanh(0.7978845608028654 * (values + 0.044715 * values * square))
    slope = 0.7978845608028654 * (1.0 + 3.0 * 0.044715 * square)
    half = 0.5 * (1.0 + turn)
    return values * half, half + 0.5 * values * (1.0 - turn * turn) * slope


def partner(values):
    width = values.shape[1]
    if width == LANES:
        lane = lax.broadcasted_iota(jnp.int32, values.shape, 1)
        ahead = pltpu.roll(values, LANES - HEAD // 2, 1)
        behind = pltpu.roll(values, HEAD // 2, 1)
        return jnp.where(lane % HEAD < HEAD // 2, ahead, behind)
    parts = []
    for at in range(0, width, HEAD):
        parts += [values[:, at + HEAD // 2 : at + HEAD], values[:, at : at + HEAD // 2]]
    return jnp.concatenate(parts, axis=1)


def widen(values):
    rows, width = values.shape
    if width >= LANES:
        return values
    return jnp.concatenate([values, jnp.zeros((rows, LANES - width), values.dtype)], axis=1)


def params():
    return pltpu.CompilerParams(vmem_limit_bytes=VMEM_BYTES)


def smem():
    return pl.BlockSpec(memory_space=pltpu.SMEM)


def vmem():
    return pl.BlockSpec(memory_space=pltpu.VMEM)


def hbm():
    return pl.BlockSpec(memory_space=pl.ANY)


def cost(flops, moved):
    return pl.CostEstimate(flops=int(flops), bytes_accessed=int(moved), transcendentals=0)


def local_kernel(body, name, outs, scratch, me, *arrays, flops=0):
    moved = sum(a.size * a.dtype.itemsize for a in arrays)
    moved += sum(int(np.prod(s)) * jnp.dtype(t).itemsize for s, t in outs)
    return pl.pallas_call(
        body,
        out_shape=[jax.ShapeDtypeStruct(s, t) for s, t in outs],
        in_specs=[smem()] + [vmem()] * len(arrays),
        out_specs=[vmem()] * len(outs),
        scratch_shapes=[pltpu.VMEM(s, t) for s, t in scratch],
        compiler_params=params(),
        cost_estimate=cost(flops, moved),
        name=name,
    )(me, *arrays)


def at_rows(me, step, rows):
    return pl.multiple_of((me ^ step) * rows, 16)


def head_inputs(qs, ks, rows, q, k, fq, fk, heads):
    lane = lax.broadcasted_iota(jnp.int32, (q.shape[0], LANES), 1)
    q, k = widen(q), widen(k)
    for h in range(heads):
        mine = lane // HEAD == h
        qs[h, rows, :] = jnp.where(mine, q * 0.125, fq).astype(BF)
        ks[h, rows, :] = jnp.where(mine, k, fk).astype(BF)


def scores_t(ks, qs, h, start, stop):
    top = dot_nt(ks[h, 0:stop, :], qs[h, start:stop, :])
    key = lax.broadcasted_iota(jnp.int32, (stop - start, stop - start), 0)
    query = lax.broadcasted_iota(jnp.int32, (stop - start, stop - start), 1)
    last = jnp.where(key <= query, top[start:, :], MASKED)
    if start == 0:
        return last
    return jnp.concatenate([top[:start, :], last], axis=0)


def spread_write(hold, values):
    for c in range(hold.shape[0]):
        hold[c] = values[:, c * LANES : (c + 1) * LANES]


def spread_read(hold):
    return jnp.concatenate([hold[c] for c in range(hold.shape[0])], axis=1)


def strided_read(hold, start, amount):
    return jnp.concatenate([hold[c, pl.ds(start, amount, stride=3), :] for c in range(hold.shape[0])], axis=1)


def strided_write(hold, start, amount, values):
    for c in range(hold.shape[0]):
        hold[c, pl.ds(start, amount, stride=3), :] = values[:, c * LANES : (c + 1) * LANES]


def row_loop(amount, run):
    def step(i, carry):
        run(pl.multiple_of(i * HEAD, HEAD))
        return carry

    lax.fori_loop(0, amount // HEAD, step, 0)


def flip(value, step):
    bit = 1
    while bit <= step:
        if step & bit:
            value = value + bit - 2 * bit * lax.rem(lax.div(value, bit), 2)
        bit *= 2
    return value


class Net:
    def __init__(self, send, recv):
        self.send, self.recv, self.used, self.open = send, recv, 0, []

    def make(self, src, dst, device):
        at = self.used
        self.used += 1
        return pltpu.make_async_remote_copy(
            src_ref=src,
            dst_ref=dst,
            send_sem=self.send.at[at],
            recv_sem=self.recv.at[at],
            device_id=device,
            device_id_type=MESH,
        )

    def start(self, src, dst, device):
        copy = self.make(src, dst, device)
        copy.start()
        self.open.append(copy)
        return copy

    def local(self, src, dst):
        at = self.used
        self.used += 1
        copy = pltpu.make_async_copy(src, dst, self.send.at[at])
        copy.start()
        return copy

    def finish(self):
        for copy in self.open:
            copy.wait_send()


class Flight:
    def __init__(self, net, dp, fs, fs_count, pieces, src):
        self.net, self.dp, self.fs, self.pieces = net, dp, fs, pieces
        self.top, self.copies, self.waited = fs_count // 2, {}, set()
        bit = self.top
        while bit:
            self.copies[bit] = net.start(src, pieces.at[bit], (dp, flip(fs, bit)))
            bit //= 2

    def ready(self, step):
        if step and step not in self.waited:
            self.waited.add(step)
            self.copies[step].wait_recv()

    def relay(self):
        known, bit = [self.top], self.top // 2
        while bit:
            fresh = []
            for step in known:
                self.ready(step)
                there = (self.dp, flip(self.fs, bit))
                self.copies[step + bit] = self.net.start(self.pieces.at[step], self.pieces.at[step + bit], there)
                fresh.append(step + bit)
            known = known + [bit] + fresh
            bit //= 2

    def all_ready(self):
        for step in sorted(self.copies):
            self.ready(step)


def doc_bounds(triples, docs):
    lane = lax.broadcasted_iota(jnp.int32, (1, LANES), 1)
    lane = jnp.where(lane >= HEAD, lane - HEAD, lane)
    first = jnp.full((1, LANES), -1, jnp.int32)
    end = jnp.full((1, LANES), -1, jnp.int32)
    at = jnp.int32(0)
    for j in range(docs):
        here = lane == j
        first = jnp.where(here, at, first)
        at = at + triples[0, j]
        end = jnp.where(here, at, end)
    return first, end, lane


def softmax_block(ks, qs, h, r, stop):
    s = scores_t(ks, qs, h, r, stop)
    e = jnp.exp(s - jnp.max(s, axis=0, keepdims=True))
    return e, 1.0 / jnp.sum(e, axis=0, keepdims=True)


def forward_one(y_count, dp_count, fs_count, tokens, cot, triples, weights, gains_t, cos, sin):
    rows, width = tokens.shape
    total, short = rows * fs_count, rows // 3
    long_rows = rows + HALO
    wqkv, wout, win, wdown, wpool, wup = weights
    rw = wqkv.shape[1]
    hd, fj, pc = wout.shape[2], win.shape[2], wpool.shape[1]
    heads = hd // HEAD
    docs = triples.shape[1]
    z_count = dp_count // y_count
    blk = QB
    sems = 96 + 16 * dp_count

    def body(
        tok, cot_ref, triples_ref, q_in, o_in, i_in, d_in, p_in, u_in, g_in, cos_ref, sin_ref,
        n1_hbm, qkv_hbm, att_hbm, wo_full, n2_hbm, hid_hbm, slope_hbm, mid, after, z_out, s0_out, wq_out, wi, wd, wp, wq1_out, wu, c_rel, gain_out,
        n1, qkv, att_rel, n2, hid0, slope0, toks, c_own, st_q, wq0, wq1, gall, wo, wo_at, att, qs, ks, vt, turned, hold, work, low, part, m_tail, part_tail,
        sbuf, rbuf, xsend, xrecv, acc, thin, send_sem, recv_sem,
    ):
        dp, fs = lax.axis_index("dp"), lax.axis_index("fsdp")
        net = Net(send_sem, recv_sem)

        def own(buf):
            return buf.at[pl.ds(pl.multiple_of(dp * rw, 16), rw), :]

        def of(buf, step):
            return buf.at[pl.ds(pl.multiple_of(flip(dp, step) * rw, 16), rw), :]

        for b in range(2):
            for t in range(3):
                st_q[b, t] = q_in[b, :, t * hd : (t + 1) * hd].astype(BF)
        here = pl.ds(pl.multiple_of(dp * rw, 16), rw)
        wide_gain = jnp.concatenate([g_in[...], jnp.zeros((LANES - 4, rw), F32)], axis=0).T
        gall[here, :] = wide_gain.astype(BF)
        wo[0, here, :] = o_in[0].astype(BF)
        wi[here, :] = i_in[0].astype(BF)
        wd[here, :] = d_in[0].astype(BF)
        wp[0, here, :] = p_in[...].astype(BF)
        wu[here, :] = u_in[...].astype(BF)

        barrier = pltpu.get_barrier_semaphore()
        for m in range(z_count):
            for e in range(fs_count):
                if m or e:
                    there = (flip(dp, m * y_count), flip(fs, e))
                    pl.semaphore_signal(barrier, inc=1, device_id=there, device_id_type=MESH)
        for j in range(1, y_count):
            pl.semaphore_signal(barrier, inc=1, device_id=(flip(dp, j), fs), device_id_type=MESH)
        pl.semaphore_wait(barrier, z_count * fs_count - 1 + y_count - 1)

        def along_z(bufs):
            found = [[] for _ in range(z_count)]
            for m in range(1, z_count):
                for buf in bufs:
                    found[m].append(net.start(own(buf), own(buf), (flip(dp, m * y_count), fs)))
            return found

        def along_y(bufs, m):
            return [
                net.start(of(buf, m * y_count), of(buf, m * y_count), (flip(dp, j), fs))
                for j in range(1, y_count)
                for buf in bufs
            ]

        def wait_all(copies):
            for copy in copies:
                copy.wait_recv()

        def heads_along_z(b, wq):
            found = []
            for m in range(z_count):
                line = []
                for t in range(3):
                    place = 3 * fs + t
                    kind, to = lax.div(place, fs_count), lax.rem(place, fs_count)
                    copy = net.make(st_q.at[b, t], wq.at[kind, here, :], (flip(dp, m * y_count), to))
                    if m == 0:

                        @pl.when(to != fs)
                        def _():
                            copy.start()

                        @pl.when(to == fs)
                        def _():
                            wq[kind, here, :] = st_q[b, t]

                        line.append((copy, to != fs))
                    else:
                        copy.start()
                        net.open.append(copy)
                        line.append((copy, None))
                found.append(line)
            return found

        def heads_along_y(wq, line, m):
            for copy, when in line:
                if when is None:
                    copy.wait_recv()
                else:

                    @pl.when(when)
                    def _():
                        copy.wait_recv()
                        copy.wait_send()

            at = pl.ds(pl.multiple_of(flip(dp, m * y_count) * rw, 16), rw)
            return [
                net.start(wq.at[:, at, :], wq.at[:, at, :], (flip(dp, j), fs)) for j in range(1, y_count)
            ]


        def spread(pieces, src):
            return Flight(net, dp, fs, fs_count, pieces, src)

        heads0 = heads_along_z(0, wq0)
        gz = along_z([gall])
        y0 = along_y([gall], 0)
        thirds = [slice(n * short, (n + 1) * short) for n in range(3)]
        tks = [spread(toks.at[:, third, :], tok.at[third, :]) for third in thirds]
        toks[0] = tok[...]
        zs = {}
        zs["wo"] = along_z([wo.at[0]])
        zs["wi"] = along_z([wi])
        ys = {"wo": along_y([wo.at[0]], 0), "wi": along_y([wi], 0)}
        spread_write(thin.at[:, 0:rows, :], cot_ref[...].astype(F32))
        lifted = jnp.concatenate([strided_read(thin, n, short) for n in range(3)], axis=1).astype(BF)
        for e in range(fs_count):
            c_own[e] = lifted[:, e * pc : (e + 1) * pc]
        c_rel[0] = c_own[fs]
        c_f = [
            net.start(c_own.at[flip(fs, e)], c_rel.at[e], (dp, flip(fs, e))) for e in range(1, fs_count)
        ]
        lane_first, lane_end, lane = doc_bounds(triples_ref, docs)
        for m in range(z_count):
            y0 += heads_along_y(wq0, heads0[m], m)
            if m:
                wait_all(gz[m])
                y0 += along_y([gall], m)
        zs["wp"] = along_z([wp.at[0]])
        zs["wd"] = along_z([wd])
        ys["wp"] = along_y([wp.at[0]], 0)
        ys["wd"] = along_y([wd], 0)

        def pass_on(name, bufs):
            for m in range(1, z_count):
                wait_all(zs[name][m])
                ys[name] += along_y(bufs, m)

        pass_on("wo", [wo.at[0]])
        heads1 = heads_along_z(1, wq1)
        zs["wu"] = along_z([wu])
        wait_all(y0)
        gain_rows = gall[...].astype(F32).T[0:8, :]
        gain_out[...] = gain_rows
        for t in range(3):
            wq_out[:, t * hd : (t + 1) * hd] = wq0[t]

        def to_heads(e, first, amount):
            base = pl.multiple_of(flip(fs, e) * rows + first, 16)
            for r in range(0, amount, LANES):
                block = toks[e, first + r : first + r + LANES, :].astype(F32)
                n1[pl.ds(base + r, LANES), :] = layer_norm(block, gain_rows[0:1]).astype(BF)
            at = pl.ds(base, amount)
            got = dot_nn(n1[at, :], wq_out[...])
            q, k, v = got[:, :hd], got[:, hd : 2 * hd], got[:, 2 * hd :]
            q = (q * cos_ref[at, :] + partner(q) * sin_ref[at, :]).astype(BF)
            k = (k * cos_ref[at, :] + partner(k) * sin_ref[at, :]).astype(BF)
            qkv[at, 0:hd] = q
            qkv[at, hd : 2 * hd] = k
            qkv[at, 2 * hd : 3 * hd] = v.astype(BF)
            row = lax.broadcasted_iota(jnp.int32, (amount, LANES), 0) + base
            inside = (row >= 3 * lane_first) & (row < 3 * lane_end)
            fk = jnp.where(inside, 1.0, 0.0)
            fq = jnp.where(inside | (lane >= docs), 0.0, MASKED)
            head_inputs(qs, ks, at, q.astype(F32), k.astype(F32), fq, fk, heads)

        to_heads(0, 0, rows)
        for tk in tks:
            tk.ready(1)
        to_heads(1, 0, rows)
        for n, tk in enumerate(tks):
            tk.relay()
            for e in range(2, fs_count):
                tk.ready(e)
                to_heads(e, n * short, short)
        for r in range(0, total, blk):
            at = slice(r, r + blk)
            vt[:, at] = qkv[at, 2 * hd : 3 * hd].astype(F32).T.astype(BF)
        stores = [net.local(n1, n1_hbm)]
        stores.append(net.local(qkv, qkv_hbm))

        flights = []
        for n, r in enumerate(range(0, total, blk)):
            stop = r + blk
            found = []
            for h in range(heads):
                e, inv = softmax_block(ks, qs, h, r, stop)
                found.append(dot_nn(vt[h * HEAD : (h + 1) * HEAD, 0:stop], e.astype(BF)) * inv)
            att[0, r:stop, :] = jnp.concatenate(found, axis=0).T.astype(BF)
            flights.append(spread(att.at[:, r:stop, :], att.at[0, r:stop, :]))
            if n == 0:
                wait_all(ys["wo"])
                wo_f = spread(wo, wo.at[0])
            if n == 1:
                pass_on("wi", [wi])
            if n == 3:
                pass_on("wp", [wp.at[0]])
                wo_f.relay()
            if n == 5:
                pass_on("wd", [wd])
                ys["wu"] = along_y([wu], 0)
            if n >= 2:
                flights[n - 2].relay()
        for flight in flights[-2:]:
            flight.relay()
        wait_all(ys["wp"])
        wp_f = spread(wp, wp.at[0])
        ys["heads1"] = []
        for m in range(z_count):
            ys["heads1"] += heads_along_y(wq1, heads1[m], m)
        wo_f.all_ready()
        for e in range(fs_count):
            wo_at[flip(fs, e)] = wo[e]
        for e in range(fs_count):
            hold[:, e * hd : (e + 1) * hd] = wo_at[e]
        for e in range(fs_count):
            base = pl.multiple_of(flip(fs, e) * hd, 16)
            turned[e * hd : (e + 1) * hd, :] = hold[pl.ds(base, hd), :]
        wo_full[...] = hold[...]
        for flight in flights:
            flight.all_ready()
        wait_all(ys["wi"])
        wait_all(ys["wd"])

        def mix(x_block, o_block, amount, keep_mid, keep, out):
            work[0:amount, 0:width] = x_block.astype(F32) + dot_nn(o_block, turned[...])

            def norm(r):
                at = pl.ds(r, HEAD)
                m = work[at, 0:width]
                if keep_mid is not None:
                    keep_mid[at, :] = m
                value = layer_norm(m, gain_rows[1:2]).astype(BF)
                low[at, 0:width] = value
                if keep is not None:
                    n2[pl.ds(pl.multiple_of(keep + r, HEAD), HEAD), :] = value

            row_loop(amount, norm)
            work[0:amount, 0:fj] = dot_nn(low[0:amount, 0:width], wi[...])

            def activate(r):
                at = pl.ds(r, HEAD)
                if keep is None:
                    low[at, 0:fj] = gelu(work[at, 0:fj]).astype(BF)
                    return
                value, rate = gelu_both(work[at, 0:fj])
                low[at, 0:fj] = value.astype(BF)
                here = pl.ds(pl.multiple_of(keep + r, HEAD), HEAD)
                hid0[here, :] = value.astype(BF)
                slope0[here, :] = rate.astype(BF)

            row_loop(amount, activate)
            out[0:amount, :] = dot_nt(low[0:amount, 0:fj], wd[...])

        for e in range(fs_count):
            at = pl.ds(pl.multiple_of(flip(fs, e) * rows + rows - HALO, 16), HALO)
            for k in range(fs_count):
                att_rel[e * HALO : (e + 1) * HALO, k * hd : (k + 1) * hd] = att[k, at, :]
        tails = jnp.concatenate([toks[e, rows - HALO : rows, :] for e in range(fs_count)], axis=0)
        mix(tails, att_rel[0 : fs_count * HALO, :], fs_count * HALO, m_tail, None, part_tail)

        for e in range(fs_count):
            base = pl.multiple_of(flip(fs, e) * rows, 16)
            for k in range(fs_count):
                att_rel[pl.ds(base, rows), k * hd : (k + 1) * hd] = att[k, pl.ds(base, rows), :]

        def before(e):
            place = flip(fs, e) + fs_count - 1
            place = lax.rem(place, fs_count)
            apart = jnp.int32(0)
            bit = 1
            while bit < fs_count:
                one = lax.rem(lax.div(place, bit), 2)
                two = lax.rem(lax.div(fs, bit), 2)
                apart = apart + bit * lax.rem(one + two, 2)
                bit *= 2
            return pl.multiple_of(apart * HALO, 16)

        def partial_for(e, out):
            base = pl.multiple_of(flip(fs, e) * rows, 16)
            mix(
                toks[e],
                att_rel[pl.ds(base, rows), :],
                rows,
                mid if e == 0 else None,
                e * rows,
                part,
            )
            out[0:HALO, :] = part_tail[pl.ds(before(e), HALO), :].astype(out.dtype)
            out[HALO:long_rows, :] = part[0:rows, :].astype(out.dtype)

        stores.append(net.local(att_rel, att_hbm))
        half = fs_count // 2
        first_hops = {}
        for j in reversed(range(half)):
            partial_for(2 * j + 1, sbuf.at[j])
            first_hops[j] = net.start(sbuf.at[j], rbuf.at[j], (dp, flip(fs, 1)))
            if j == half - 1:
                pass_on("wu", [wu])
            if j:
                partial_for(2 * j, acc.at[j])
                first_hops[j].wait_recv()
                acc[j] = acc[j] + rbuf[j].astype(F32)
                if half == 2:
                    xsend[0] = acc[1].astype(BF)
                    last_hop = net.start(xsend.at[0], xrecv.at[0], (dp, flip(fs, 2)))
            if j == half - 1:
                wp_f.relay()
        partial_for(0, acc.at[0])
        first_hops[0].wait_recv()
        acc[0] = acc[0] + rbuf[0].astype(F32)
        if half > 2:
            bit, active = 2, list(range(half))
            slot = 0
            while bit < fs_count:
                stay = [j for j in active if not (2 * j) & bit]
                hops = {}
                for j in stay:
                    give = j + bit // 2
                    xsend[slot] = acc[give].astype(BF)
                    hops[j] = (net.start(xsend.at[slot], xrecv.at[slot], (dp, flip(fs, bit))), slot)
                    slot += 1
                for j in stay:
                    hops[j][0].wait_recv()
                    acc[j] = acc[j] + xrecv[hops[j][1]].astype(F32)
                active, bit = stay, bit * 2
        elif half == 2:
            last_hop.wait_recv()
            acc[0] = acc[0] + xrecv[0].astype(F32)
        a_tail = acc[0, 0:HALO, :] + m_tail[pl.ds(before(0), HALO), :]
        a_own = acc[0, HALO:long_rows, :] + mid[...]
        after[...] = a_own
        for c in range(width // LANES):
            thin[c, 0:HALO, :] = a_tail[:, c * LANES : (c + 1) * LANES]
            thin[c, HALO:long_rows, :] = a_own[:, c * LANES : (c + 1) * LANES]

        stores.append(net.local(n2, n2_hbm))
        stores.append(net.local(hid0, hid_hbm))
        stores.append(net.local(slope0, slope_hbm))

        row = lax.broadcasted_iota(jnp.int32, (short, LANES), 0) + fs * short
        begins = jnp.max(jnp.where(row == lane_first, 1.0, 0.0), axis=1, keepdims=True)
        parts = []
        for k in range(3):
            value = strided_read(thin, HALO - 2 + k, short)
            parts.append(jnp.where(begins > 0.0, 0.0, value) if k < 2 else value)
        z = jnp.concatenate(parts, axis=1).astype(BF)
        for e in range(fs_count):
            z_out[e] = z[:, e * pc : (e + 1) * pc]
        pooled = jnp.zeros((short, width), F32)
        for e in range(fs_count):
            wp_f.ready(e)
            pooled = pooled + dot_nt(z_out[flip(fs, e)], wp[e])
        s0_out[...] = pooled
        for name in ("heads1", "wu"):
            wait_all(ys[name])
        wait_all(c_f)
        for t in range(3):
            wq1_out[:, t * hd : (t + 1) * hd] = wq1[t]
        for copy in stores:
            copy.wait()
        net.finish()

    half = fs_count // 2
    outs = [
        ((total, width), BF),
        ((total, 3 * hd), BF),
        ((total, width), BF),
        ((width, width), BF),
        ((total, width), BF),
        ((total, fj), BF),
        ((total, fj), BF),
        ((rows, width), F32),
        ((rows, width), F32),
        ((fs_count, short, pc), BF),
        ((short, width), F32),
        ((width, 3 * hd), BF),
        ((width, fj), BF),
        ((width, fj), BF),
        ((fs_count, width, pc), BF),
        ((width, 3 * hd), BF),
        ((width, pc), BF),
        ((fs_count, short, pc), BF),
        ((8, width), F32),
    ]
    wide = max(width, fj)
    scratch = [
        ((total, width), BF),
        ((total, 3 * hd), BF),
        ((total, width), BF),
        ((total, width), BF),
        ((total, fj), BF),
        ((total, fj), BF),
        ((fs_count, rows, width), BF),
        ((fs_count, short, pc), BF),
        ((2, 3, rw, hd), BF),
        ((3, width, hd), BF),
        ((3, width, hd), BF),
        ((width, LANES), BF),
        ((fs_count, width, hd), BF),
        ((fs_count, width, hd), BF),
        ((fs_count, total, hd), BF),
        ((heads, total, LANES), BF),
        ((heads, total, LANES), BF),
        ((hd, total), BF),
        ((width, width), BF),
        ((width, width), BF),
        ((rows, wide), F32),
        ((rows, wide), BF),
        ((rows, width), F32),
        ((fs_count * HALO, width), F32),
        ((fs_count * HALO, width), F32),
        ((half, long_rows, width), BF),
        ((half, long_rows, width), BF),
        ((half - 1, long_rows, width), BF),
        ((half - 1, long_rows, width), BF),
        ((half, long_rows, width), F32),
        ((width // LANES, long_rows, LANES), F32),
    ]
    return pl.pallas_call(
        body,
        out_shape=[jax.ShapeDtypeStruct(s, t) for s, t in outs],
        in_specs=[vmem(), vmem(), smem()] + [vmem()] * 9,
        out_specs=[hbm() if n in (0, 1, 2, 4, 5, 6) else vmem() for n in range(len(outs))],
        scratch_shapes=[pltpu.VMEM(s, t) for s, t in scratch] + [pltpu.SemaphoreType.DMA((sems,))] * 2,
        compiler_params=pltpu.CompilerParams(collective_id=3, has_side_effects=True, vmem_limit_bytes=VMEM_BYTES),
        cost_estimate=cost(2e10, 3e7),
        name="forward_one",
    )(tokens, cot, triples, *weights, gains_t, cos, sin)


def forward_all(y_count, dp_count, fs_count, tokens, cot, triples, weights, gains_t, cos, sin):
    rows, width = tokens.shape
    total, short = rows * fs_count, rows // 3
    long_rows = rows + HALO
    wqkv, wout, win, wdown, wpool, wup = weights
    rw = wqkv.shape[1]
    hd, fj, pc = wout.shape[2], win.shape[2], wpool.shape[1]
    heads = hd // HEAD
    docs = triples.shape[1]
    z_count = dp_count // y_count
    blk = query_rows(total)
    total_b = short * fs_count
    blk_b = min(QB, total_b)
    blocks_b, half = total_b // blk_b, fs_count // 2
    cb = 4 * hd + 2 * pc
    sems = 192 + 22 * dp_count + 16 * fs_count

    def body(
        tok, cot_ref, triples_ref, q_in, o_in, i_in, d_in, p_in, u_in, g_in, cos_ref, sin_ref,
        n1_hbm, qkv_hbm, att_hbm, n2_hbm, hid_hbm, slope_hbm, wo_full, mid, wq_out, wi, wd, gain_out, out, da, dfs_out, group, sum_ff, dgain,
        after, z_out, s0_out, wp, wq1_out, wu, c_rel,
        n1, qkv, att_rel, n2, hid0, slope0, toks, c_own, st_q, wq0, wq1, gall, wo, wo_at, att, qs, ks, vt, turned, hold, work, low, part, m_tail, part_tail, sbuf, rbuf, xsend, xrecv, acc, thin,
        b_wos, b_wi_ref, b_wd_ref, b_g_ff, b_yg, b_zsg, b_zrg, b_sd, b_rd, b_xd, b_yd, b_ad, b_lift_send, b_lift_rel, b_s0s, b_x_all, b_z_rel, b_dfs, b_df_all, b_do_out, b_do_in, b_da_out, b_da_in, b_cols, b_s1s, b_ds0s, b_nxt, b_n1, b_n2, b_qkv, b_att, b_att_rel, b_kt, b_dk, b_dv, b_dqkv, b_work, b_hid, b_slope, b_dpre, b_m_all, b_dm, b_sf, b_rf, b_xf, b_yf, b_af, b_sb, b_rb, b_xb, b_yb, b_ab, b_sa, b_ra, b_xa, b_ya, b_aa, b_spread_rows, b_lift,
        send_sem, recv_sem, *ps,
    ):
        dp, fs = lax.axis_index("dp"), lax.axis_index("fsdp")
        net = Net(send_sem, recv_sem)

        def own(buf):
            return buf.at[pl.ds(pl.multiple_of(dp * rw, 16), rw), :]

        def of(buf, step):
            return buf.at[pl.ds(pl.multiple_of(flip(dp, step) * rw, 16), rw), :]

        for b in range(2):
            for t in range(3):
                st_q[b, t] = q_in[b, :, t * hd : (t + 1) * hd].astype(BF)
        here = pl.ds(pl.multiple_of(dp * rw, 16), rw)
        wide_gain = jnp.concatenate([g_in[...], jnp.zeros((LANES - 4, rw), F32)], axis=0).T
        gall[here, :] = wide_gain.astype(BF)
        wo[0, here, :] = o_in[0].astype(BF)
        wi[here, :] = i_in[0].astype(BF)
        wd[here, :] = d_in[0].astype(BF)
        wp[0, here, :] = p_in[...].astype(BF)
        wu[here, :] = u_in[...].astype(BF)
        b_wos[0, here, :] = o_in[1].astype(BF)
        b_wi_ref[here, :] = i_in[1].astype(BF)
        b_wd_ref[here, :] = d_in[1].astype(BF)

        barrier = pltpu.get_barrier_semaphore()
        for m in range(z_count):
            for e in range(fs_count):
                if m or e:
                    there = (flip(dp, m * y_count), flip(fs, e))
                    pl.semaphore_signal(barrier, inc=1, device_id=there, device_id_type=MESH)
        for j in range(1, y_count):
            pl.semaphore_signal(barrier, inc=1, device_id=(flip(dp, j), fs), device_id_type=MESH)
        pl.semaphore_wait(barrier, z_count * fs_count - 1 + y_count - 1)

        def along_z(bufs):
            found = [[] for _ in range(z_count)]
            for m in range(1, z_count):
                for buf in bufs:
                    found[m].append(net.start(own(buf), own(buf), (flip(dp, m * y_count), fs)))
            return found

        def along_y(bufs, m):
            return [
                net.start(of(buf, m * y_count), of(buf, m * y_count), (flip(dp, j), fs))
                for j in range(1, y_count)
                for buf in bufs
            ]

        def wait_all(copies):
            for copy in copies:
                copy.wait_recv()

        def heads_along_z(b, wq):
            found = []
            for m in range(z_count):
                line = []
                for t in range(3):
                    place = 3 * fs + t
                    kind, to = lax.div(place, fs_count), lax.rem(place, fs_count)
                    copy = net.make(st_q.at[b, t], wq.at[kind, here, :], (flip(dp, m * y_count), to))
                    if m == 0:

                        @pl.when(to != fs)
                        def _():
                            copy.start()

                        @pl.when(to == fs)
                        def _():
                            wq[kind, here, :] = st_q[b, t]

                        line.append((copy, to != fs))
                    else:
                        copy.start()
                        net.open.append(copy)
                        line.append((copy, None))
                found.append(line)
            return found

        def heads_along_y(wq, line, m):
            for copy, when in line:
                if when is None:
                    copy.wait_recv()
                else:

                    @pl.when(when)
                    def _():
                        copy.wait_recv()
                        copy.wait_send()

            at = pl.ds(pl.multiple_of(flip(dp, m * y_count) * rw, 16), rw)
            return [
                net.start(wq.at[:, at, :], wq.at[:, at, :], (flip(dp, j), fs)) for j in range(1, y_count)
            ]


        def spread(pieces, src):
            return Flight(net, dp, fs, fs_count, pieces, src)

        heads0 = heads_along_z(0, wq0)
        gz = along_z([gall])
        y0 = along_y([gall], 0)
        thirds = [slice(n * short, (n + 1) * short) for n in range(3)]
        tks = [spread(toks.at[:, third, :], tok.at[third, :]) for third in thirds]
        toks[0] = tok[...]
        zs = {}
        zs["wo"] = along_z([wo.at[0]])
        zs["wi"] = along_z([wi])
        ys = {"wo": along_y([wo.at[0]], 0), "wi": along_y([wi], 0)}
        spread_write(thin.at[:, 0:rows, :], cot_ref[...].astype(F32))
        lifted = jnp.concatenate([strided_read(thin, n, short) for n in range(3)], axis=1).astype(BF)
        for e in range(fs_count):
            c_own[e] = lifted[:, e * pc : (e + 1) * pc]
        c_rel[0] = c_own[fs]
        c_f = [
            net.start(c_own.at[flip(fs, e)], c_rel.at[e], (dp, flip(fs, e))) for e in range(1, fs_count)
        ]
        lane_first, lane_end, lane = doc_bounds(triples_ref, docs)
        for m in range(z_count):
            y0 += heads_along_y(wq0, heads0[m], m)
            if m:
                wait_all(gz[m])
                y0 += along_y([gall], m)
        zs["wp"] = along_z([wp.at[0]])
        zs["wd"] = along_z([wd])
        ys["wp"] = along_y([wp.at[0]], 0)
        ys["wd"] = along_y([wd], 0)

        def pass_on(name, bufs):
            for m in range(1, z_count):
                wait_all(zs[name][m])
                ys[name] += along_y(bufs, m)

        pass_on("wo", [wo.at[0]])
        heads1 = heads_along_z(1, wq1)
        zs["wu"] = along_z([wu])
        later = (b_wos.at[0], b_wi_ref, b_wd_ref)
        came = [[line[0] for line in along_z([buf])[1:]] for buf in later]
        wait_all(y0)
        gain_rows = gall[...].astype(F32).T[0:8, :]
        gain_out[...] = gain_rows
        for t in range(3):
            wq_out[:, t * hd : (t + 1) * hd] = wq0[t]

        def to_heads(e, first, amount):
            base = pl.multiple_of(flip(fs, e) * rows + first, 16)
            for r in range(0, amount, LANES):
                block = toks[e, first + r : first + r + LANES, :].astype(F32)
                n1[pl.ds(base + r, LANES), :] = layer_norm(block, gain_rows[0:1]).astype(BF)
            at = pl.ds(base, amount)
            got = dot_nn(n1[at, :], wq_out[...])
            q, k, v = got[:, :hd], got[:, hd : 2 * hd], got[:, 2 * hd :]
            q = (q * cos_ref[at, :] + partner(q) * sin_ref[at, :]).astype(BF)
            k = (k * cos_ref[at, :] + partner(k) * sin_ref[at, :]).astype(BF)
            qkv[at, 0:hd] = q
            qkv[at, hd : 2 * hd] = k
            qkv[at, 2 * hd : 3 * hd] = v.astype(BF)
            row = lax.broadcasted_iota(jnp.int32, (amount, LANES), 0) + base
            inside = (row >= 3 * lane_first) & (row < 3 * lane_end)
            fk = jnp.where(inside, 1.0, 0.0)
            fq = jnp.where(inside | (lane >= docs), 0.0, MASKED)
            head_inputs(qs, ks, at, q.astype(F32), k.astype(F32), fq, fk, heads)

        to_heads(0, 0, rows)
        for tk in tks:
            tk.ready(1)
        to_heads(1, 0, rows)
        for n, tk in enumerate(tks):
            tk.relay()
            for e in range(2, fs_count):
                tk.ready(e)
                to_heads(e, n * short, short)
        for r in range(0, total, blk):
            at = slice(r, r + blk)
            vt[:, at] = qkv[at, 2 * hd : 3 * hd].astype(F32).T.astype(BF)
        stores = [net.local(n1, n1_hbm)]
        stores.append(net.local(qkv, qkv_hbm))

        flights = []
        for n, r in enumerate(range(0, total, blk)):
            stop = r + blk
            found = []
            for h in range(heads):
                e, inv = softmax_block(ks, qs, h, r, stop)
                found.append(dot_nn(vt[h * HEAD : (h + 1) * HEAD, 0:stop], e.astype(BF)) * inv)
            att[0, r:stop, :] = jnp.concatenate(found, axis=0).T.astype(BF)
            flights.append(spread(att.at[:, r:stop, :], att.at[0, r:stop, :]))
            if n == 0:
                wait_all(ys["wo"])
                wo_f = spread(wo, wo.at[0])
            if n == 1:
                pass_on("wi", [wi])
            if n == 3:
                pass_on("wp", [wp.at[0]])
                wo_f.relay()
            if n == 5:
                pass_on("wd", [wd])
                ys["wu"] = along_y([wu], 0)
                passed = [along_y([buf], 0) for buf in later]
            if n >= 2:
                flights[n - 2].relay()
        for flight in flights[-2:]:
            flight.relay()
        wait_all(ys["wp"])
        wp_f = spread(wp, wp.at[0])
        ys["heads1"] = []
        for m in range(z_count):
            ys["heads1"] += heads_along_y(wq1, heads1[m], m)
        wo_f.all_ready()
        for e in range(fs_count):
            wo_at[flip(fs, e)] = wo[e]
        for e in range(fs_count):
            hold[:, e * hd : (e + 1) * hd] = wo_at[e]
        for e in range(fs_count):
            base = pl.multiple_of(flip(fs, e) * hd, 16)
            turned[e * hd : (e + 1) * hd, :] = hold[pl.ds(base, hd), :]
        wo_full[...] = hold[...]
        for flight in flights:
            flight.all_ready()
        wait_all(ys["wi"])
        wait_all(ys["wd"])

        def mix(x_block, o_block, amount, keep_mid, keep, out):
            work[0:amount, 0:width] = x_block.astype(F32) + dot_nn(o_block, turned[...])

            def norm(r):
                at = pl.ds(r, HEAD)
                m = work[at, 0:width]
                if keep_mid is not None:
                    keep_mid[at, :] = m
                value = layer_norm(m, gain_rows[1:2]).astype(BF)
                low[at, 0:width] = value
                if keep is not None:
                    n2[pl.ds(pl.multiple_of(keep + r, HEAD), HEAD), :] = value

            row_loop(amount, norm)
            work[0:amount, 0:fj] = dot_nn(low[0:amount, 0:width], wi[...])

            def activate(r):
                at = pl.ds(r, HEAD)
                if keep is None:
                    low[at, 0:fj] = gelu(work[at, 0:fj]).astype(BF)
                    return
                value, rate = gelu_both(work[at, 0:fj])
                low[at, 0:fj] = value.astype(BF)
                here = pl.ds(pl.multiple_of(keep + r, HEAD), HEAD)
                hid0[here, :] = value.astype(BF)
                slope0[here, :] = rate.astype(BF)

            row_loop(amount, activate)
            out[0:amount, :] = dot_nt(low[0:amount, 0:fj], wd[...])

        for e in range(fs_count):
            at = pl.ds(pl.multiple_of(flip(fs, e) * rows + rows - HALO, 16), HALO)
            for k in range(fs_count):
                att_rel[e * HALO : (e + 1) * HALO, k * hd : (k + 1) * hd] = att[k, at, :]
        tails = jnp.concatenate([toks[e, rows - HALO : rows, :] for e in range(fs_count)], axis=0)
        mix(tails, att_rel[0 : fs_count * HALO, :], fs_count * HALO, m_tail, None, part_tail)

        for e in range(fs_count):
            base = pl.multiple_of(flip(fs, e) * rows, 16)
            for k in range(fs_count):
                att_rel[pl.ds(base, rows), k * hd : (k + 1) * hd] = att[k, pl.ds(base, rows), :]

        def before(e):
            place = flip(fs, e) + fs_count - 1
            place = lax.rem(place, fs_count)
            apart = jnp.int32(0)
            bit = 1
            while bit < fs_count:
                one = lax.rem(lax.div(place, bit), 2)
                two = lax.rem(lax.div(fs, bit), 2)
                apart = apart + bit * lax.rem(one + two, 2)
                bit *= 2
            return pl.multiple_of(apart * HALO, 16)

        def partial_for(e, out):
            base = pl.multiple_of(flip(fs, e) * rows, 16)
            mix(
                toks[e],
                att_rel[pl.ds(base, rows), :],
                rows,
                mid if e == 0 else None,
                e * rows,
                part,
            )
            out[0:HALO, :] = part_tail[pl.ds(before(e), HALO), :].astype(out.dtype)
            out[HALO:long_rows, :] = part[0:rows, :].astype(out.dtype)

        stores.append(net.local(att_rel, att_hbm))
        first_hops = {}
        for j in reversed(range(half)):
            partial_for(2 * j + 1, sbuf.at[j])
            first_hops[j] = net.start(sbuf.at[j], rbuf.at[j], (dp, flip(fs, 1)))
            if j == half - 1:
                pass_on("wu", [wu])
            if j:
                partial_for(2 * j, acc.at[j])
                first_hops[j].wait_recv()
                acc[j] = acc[j] + rbuf[j].astype(F32)
                if half == 2:
                    xsend[0] = acc[1].astype(BF)
                    last_hop = net.start(xsend.at[0], xrecv.at[0], (dp, flip(fs, 2)))
            if j == half - 1:
                wp_f.relay()
        partial_for(0, acc.at[0])
        first_hops[0].wait_recv()
        acc[0] = acc[0] + rbuf[0].astype(F32)
        if half > 2:
            bit, active = 2, list(range(half))
            slot = 0
            while bit < fs_count:
                stay = [j for j in active if not (2 * j) & bit]
                hops = {}
                for j in stay:
                    give = j + bit // 2
                    xsend[slot] = acc[give].astype(BF)
                    hops[j] = (net.start(xsend.at[slot], xrecv.at[slot], (dp, flip(fs, bit))), slot)
                    slot += 1
                for j in stay:
                    hops[j][0].wait_recv()
                    acc[j] = acc[j] + xrecv[hops[j][1]].astype(F32)
                active, bit = stay, bit * 2
        elif half == 2:
            last_hop.wait_recv()
            acc[0] = acc[0] + xrecv[0].astype(F32)
        a_tail = acc[0, 0:HALO, :] + m_tail[pl.ds(before(0), HALO), :]
        a_own = acc[0, HALO:long_rows, :] + mid[...]
        after[...] = a_own
        for c in range(width // LANES):
            thin[c, 0:HALO, :] = a_tail[:, c * LANES : (c + 1) * LANES]
            thin[c, HALO:long_rows, :] = a_own[:, c * LANES : (c + 1) * LANES]

        stores.append(net.local(n2, n2_hbm))
        stores.append(net.local(hid0, hid_hbm))
        stores.append(net.local(slope0, slope_hbm))

        row = lax.broadcasted_iota(jnp.int32, (short, LANES), 0) + fs * short
        begins = jnp.max(jnp.where(row == lane_first, 1.0, 0.0), axis=1, keepdims=True)
        parts = []
        for k in range(3):
            value = strided_read(thin, HALO - 2 + k, short)
            parts.append(jnp.where(begins > 0.0, 0.0, value) if k < 2 else value)
        z = jnp.concatenate(parts, axis=1).astype(BF)
        for e in range(fs_count):
            z_out[e] = z[:, e * pc : (e + 1) * pc]
        pooled = jnp.zeros((short, width), F32)
        for e in range(fs_count):
            wp_f.ready(e)
            pooled = pooled + dot_nt(z_out[flip(fs, e)], wp[e])
        s0_out[...] = pooled
        for name in ("heads1", "wu"):
            wait_all(ys[name])
        wait_all(c_f)
        for t in range(3):
            wq1_out[:, t * hd : (t + 1) * hd] = wq1[t]
        (wos, wi_ref, wd_ref, g_ff, yg, zsg, zrg, sd, rd, xd, yd, ad, lift_send, lift_rel, s0s, x_all, z_rel, dfs, df_all, do_out, do_in, da_out, da_in, cols, s1s, ds0s, nxt, n1, n2, qkv, att, att_rel, kt, dk, dv, dqkv, work, hid, slope, dpre, m_all, dm, sf, rf, xf, yf, af, sb, rb, xb, yb, ab, sa, ra, xa, ya, aa, spread_rows, lift) = (
            b_wos, b_wi_ref, b_wd_ref, b_g_ff, b_yg, b_zsg, b_zrg, b_sd, b_rd, b_xd, b_yd, b_ad, b_lift_send, b_lift_rel, b_s0s, b_x_all, b_z_rel, b_dfs, b_df_all, b_do_out, b_do_in, b_da_out, b_da_in, b_cols, b_s1s, b_ds0s, b_nxt, b_n1, b_n2, b_qkv, b_att, b_att_rel, b_kt, b_dk, b_dv, b_dqkv, b_work, b_hid, b_slope, b_dpre, b_m_all, b_dm, b_sf, b_rf, b_xf, b_yf, b_af, b_sb, b_rb, b_xb, b_yb, b_ab, b_sa, b_ra, b_xa, b_ya, b_aa, b_spread_rows, b_lift
        )
        thin = thin.at[:, 0:rows, :]
        def base_of(e, amount):
            return pl.multiple_of(flip(fs, e) * amount, 16)

        def spread(pieces, src=None):
            return Flight(net, dp, fs, fs_count, pieces, pieces.at[0] if src is None else src)

        s0s[0] = s0_out[...].astype(BF)
        nxt[...] = jnp.zeros(nxt.shape, BF)
        here = pl.ds(pl.multiple_of(dp * rw, 16), rw)
        def of(buf, step):
            return buf.at[pl.ds(pl.multiple_of(flip(dp, step) * rw, 16), rw), :]

        def along_z(buf):
            return [
                net.start(of(buf, 0), of(buf, 0), (flip(dp, m * y_count), fs)) for m in range(1, z_count)
            ]

        def along_y(buf, m):
            return [
                net.start(of(buf, m * y_count), of(buf, m * y_count), (flip(dp, n), fs)) for n in range(1, y_count)
            ]

        def pass_on(buf, came, passed):
            for m in range(1, z_count):
                came[m - 1].wait_recv()
                passed += along_y(buf, m)

        def wait_all(copies):
            for copy in copies:
                copy.wait_recv()

        s0_f = spread(s0s)

        dsum = Scatter(net, dp, fs, fs_count, sd, rd, xd, yd, ad)
        for e in reversed(range(fs_count)):
            part = dot_nt(c_rel[e], wu[...])
            if e % 2:
                sd[e // 2] = part.astype(BF)
                dsum.send_odd(e // 2)
            else:
                ad[e // 2] = part

        def exchange(blocks_of, landed):
            found = []
            for e in range(1, fs_count):
                found.append(net.start(blocks_of.at[flip(fs, e)], landed.at[e], (dp, flip(fs, e))))
            landed[0] = blocks_of[fs]
            return found

        lane_first, lane_end, lane = doc_bounds(triples_ref, docs)
        for n in range(1, half):
            dsum.join(n)
        dsum.upper()
        s0_f.relay()
        pass_on(wos.at[0], came[0], passed[0])
        for e in range(fs_count):
            s0_f.ready(e)
            at = pl.ds(base_of(e, short), short)
            value = s0_out[...] if e == 0 else s0s[e].astype(F32)
            x_all[at, :] = value
            n1[at, :] = layer_norm(value, gain_out[2:3, :]).astype(BF)
        for r in range(0, total_b, blk_b):
            at = slice(r, r + blk_b)
            got = dot_nn(n1[at, :], wq1_out[...])
            q, k, v = got[:, :hd], got[:, hd : 2 * hd], got[:, 2 * hd :]
            q = (q * cos_ref[at, :] + partner(q) * sin_ref[at, :]).astype(BF)
            k = (k * cos_ref[at, :] + partner(k) * sin_ref[at, :]).astype(BF)
            qkv[at, 0:hd] = q
            qkv[at, hd : 2 * hd] = k
            qkv[at, 2 * hd : 3 * hd] = v.astype(BF)
            row = lax.broadcasted_iota(jnp.int32, (blk_b, LANES), 0) + r
            inside = (row >= lane_first) & (row < lane_end)
            fk = jnp.where(inside, 1.0, 0.0)
            fq = jnp.where(inside | (lane >= docs), 0.0, MASKED)
            head_inputs(qs, ks, at, q.astype(F32), k.astype(F32), fq, fk, heads)
            vt[:, at] = v.T.astype(BF)
            kt[:, at] = k.astype(F32).T.astype(BF)
            dk[at, :] = jnp.zeros((blk_b, LANES), F32)
            dv[at, :] = jnp.zeros((blk_b, LANES), F32)
        dsum.join(0)
        dsum.finish()
        dm[...] = ad[0]
        dfs[0] = ad[0].astype(BF)
        df_f = spread(dfs)
        wait_all(passed[0])
        wo_f = spread(wos, wos.at[0])
        flights = []
        for n in range(blocks_b):
            r, stop = n * blk_b, (n + 1) * blk_b
            found = []
            for h in range(heads):
                e, inv = softmax_block(ks, qs, h, r, stop)
                ps[n][h] = (e * inv).astype(BF)
                found.append(dot_nn(vt[h * HEAD : (h + 1) * HEAD, 0:stop], ps[n][h]))
            att[0, r:stop, :] = jnp.concatenate(found, axis=0).T.astype(BF)
            flights.append(spread(att.at[:, r:stop, :], att.at[0, r:stop, :]))
            if n == 0:
                pass_on(wi_ref, came[1], passed[1])
                df_f.relay()
                wo_f.relay()
        place_of = lax.broadcasted_iota(jnp.int32, (blk_b, LANES), 1) // HEAD
        for r in range(0, total_b, blk_b):
            at = slice(r, r + blk_b)
            q = widen(qkv[at, 0:hd].astype(F32))
            for h in range(heads):
                qs[h, at, :] = jnp.where(place_of == h, q, 0.0).astype(BF)

        pass_on(wd_ref, came[2], passed[2])
        wo_f.all_ready()
        for e in range(fs_count):
            wo_at[flip(fs, e)] = wos[e]
        for e in range(fs_count):
            hold[:, e * hd : (e + 1) * hd] = wo_at[e]
        for e in range(fs_count):
            turned[e * hd : (e + 1) * hd, :] = hold[pl.ds(base_of(e, hd), hd), :]
        for flight in flights:
            flight.relay()
        for flight in flights:
            flight.all_ready()
        for e in range(fs_count):
            att_rel[:, e * hd : (e + 1) * hd] = att[e]

        work[:, 0:width] = x_all[...] + dot_nn(att_rel[...], turned[...])

        def norm_all(r):
            at = pl.ds(r, HEAD)
            m = work[at, 0:width]
            m_all[at, :] = m
            n2[at, :] = layer_norm(m, gain_out[3:4, :]).astype(BF)

        row_loop(total_b, norm_all)
        wait_all(passed[1])
        work[:, 0:fj] = dot_nn(n2[...], wi_ref[...])

        def activate_all(r):
            at = pl.ds(r, HEAD)
            value, rate = gelu_both(work[at, 0:fj])
            hid[at, :] = value.astype(BF)
            slope[at, :] = rate

        row_loop(total_b, activate_all)
        wait_all(passed[2])
        work[:, 0:width] = dot_nt(hid[...], wd_ref[...])

        def give_out(scatter, source):
            for e in reversed(range(fs_count)):
                value = source[pl.ds(base_of(e, short), short), 0:width]
                if e % 2:
                    scatter.sbuf[e // 2] = value.astype(BF)
                    scatter.send_odd(e // 2)
                else:
                    scatter.acc[e // 2] = value

        fwd = Scatter(net, dp, fs, fs_count, sf, rf, xf, yf, af)
        give_out(fwd, work)
        for e in range(fs_count):
            df_f.ready(e)
            df_all[pl.ds(base_of(e, short), short), :] = dfs[e]
        work[:, 0:fj] = dot_nn(df_all[...], wd_ref[...])

        def pull_all(r):
            at = pl.ds(r, HEAD)
            dpre[at, :] = (work[at, 0:fj] * slope[at, :]).astype(BF)

        row_loop(total_b, pull_all)
        work[:, 0:width] = dot_nt(dpre[...], wi_ref[...])
        bwd = Scatter(net, dp, fs, fs_count, sb, rb, xb, yb, ab)
        give_out(bwd, work)
        for j in range(1, half):
            bwd.join(j)
        bwd.upper()
        for j in range(1, half):
            fwd.join(j)
        fwd.upper()
        g_ff[:, 0:fj] = dot_tn(n2[...], dpre[...]).astype(BF)
        g_ff[:, fj : 2 * fj] = dot_tn(df_all[...], hid[...]).astype(BF)
        ff_rows = RowSum(net, (dp, fs, y_count, z_count, fs_count, rw), g_ff, yg, zsg, zrg, sum_ff)
        ff_rows.start()
        bwd.join(0)
        bwd.finish()
        m_own = m_all[pl.ds(base_of(0, short), short), :]
        dx, dg = layer_norm_back(m_own, gain_out[3:4, :], ab[0])
        dx = dx + dm[...]
        dm[...] = dx
        low_dx = dx.astype(BF)
        got = dot_nt(low_dx, hold[...]).astype(BF)
        for e in range(fs_count):
            do_out[e] = got[:, e * hd : (e + 1) * hd]
            da_out[e] = low_dx[:, e * hd : (e + 1) * hd]
        do_f = exchange(do_out, do_in)
        da_f = exchange(da_out, da_in)
        gain_two = jnp.sum(dg, axis=0, keepdims=True)

        fwd.join(0)
        fwd.finish()
        s1s[0] = (m_own + af[0]).astype(BF)
        s1_f = spread(s1s)
        z_f = exchange(z_out, z_rel)
        wait_all(do_f)
        for e in range(fs_count):
            at = pl.ds(base_of(e, short), short)
            do = widen(do_in[e].astype(F32))
            lane_head = lax.broadcasted_iota(jnp.int32, (short, LANES), 1) // HEAD
            for h in range(heads):
                ks[h, at, :] = jnp.where(lane_head == h, do, 0.0).astype(BF)
        wait_all(da_f)
        for e in range(fs_count):
            cols[pl.ds(base_of(e, short), short), :] = da_in[e]
        s1_f.relay()

        g_out = dot_tn(att_rel[...], cols[...]).astype(BF)
        for e in range(fs_count):
            group[pl.ds(base_of(e, hd), hd), cb - hd : cb] = g_out[e * hd : (e + 1) * hd, :]
        for n in range(blocks_b):
            r, stop = n * blk_b, (n + 1) * blk_b
            at = slice(r, stop)
            found = []
            add_k = add_v = None
            for h in range(heads):
                p = ps[n][h]
                grad = dot_nt(widen(qkv[0:stop, 2 * hd : 3 * hd]), ks[h, at, :])
                wide = p.astype(F32)
                inner = jnp.sum(wide * grad, axis=0, keepdims=True)
                dr = (wide * (grad - inner) * 0.125).astype(BF)
                part_v = dot_nn(p, ks[h, at, :])
                part_k = dot_nn(dr, qs[h, at, :])
                add_v = part_v if add_v is None else add_v + part_v
                add_k = part_k if add_k is None else add_k + part_k
                found.append(dot_nn(kt[h * HEAD : (h + 1) * HEAD, 0:stop], dr))
            dk[0:stop, :] += add_k
            dv[0:stop, :] += add_v
            dq = jnp.concatenate(found, axis=0).T
            dqkv[at, 0:hd] = (dq * cos_ref[at, :] - partner(dq) * sin_ref[at, :]).astype(BF)
        for r in range(0, total_b, blk_b):
            at = slice(r, r + blk_b)
            grad = dk[at, 0:hd]
            dqkv[at, hd : 2 * hd] = (grad * cos_ref[at, :] - partner(grad) * sin_ref[at, :]).astype(BF)
            dqkv[at, 2 * hd : 3 * hd] = dv[at, 0:hd].astype(BF)
        work[:, 0:width] = dot_nt(dqkv[...], wq1_out[...])
        first = Scatter(net, dp, fs, fs_count, sa, ra, xa, ya, aa)
        give_out(first, work)
        for j in range(1, half):
            first.join(j)
        first.upper()
        group[:, 0 : 3 * hd] = dot_tn(n1[...], dqkv[...]).astype(BF)
        s1_f.all_ready()
        lift_f = []
        for e in range(fs_count):
            part = dot_nn(s1s[e], wu[...]).astype(BF)
            if e:
                lift_send[e] = part
                lift_f.append(net.start(lift_send.at[e], lift_rel.at[e], (dp, flip(fs, e))))
            else:
                lift_rel[0] = part
        g_up = jnp.zeros((width, pc), F32)
        for e in range(fs_count):
            g_up = g_up + dot_tn(s1s[e], c_rel[e])
        group[:, 3 * hd + pc : 3 * hd + 2 * pc] = g_up.astype(BF)
        for m in range(1, z_count):
            ff_rows.service(m)
        first.join(0)
        first.finish()
        dx, dg = layer_norm_back(s0_out[...], gain_out[2:3, :], aa[0])
        ds0s[0] = (dx + dm[...]).astype(BF)
        gain_one = jnp.sum(dg, axis=0, keepdims=True)
        which = lax.broadcasted_iota(jnp.int32, (8, width), 0)
        dgain[...] = jnp.where(which == 0, gain_one, jnp.where(which == 1, gain_two, 0.0))

        hop = net.make(ds0s.at[0, 0:HALO, :], nxt, (dp, lax.rem(fs + fs_count - 1, fs_count)))

        @pl.when(fs > 0)
        def _():
            hop.start()

        ds0_f = spread(ds0s)
        row = lax.broadcasted_iota(jnp.int32, (short, LANES), 0) + fs * short + 1
        shut = jnp.max(jnp.where((row == lane_first) | (row >= total_b), 1.0, 0.0), axis=1, keepdims=True) > 0.0

        @pl.when(fs < fs_count - 1)
        def _():
            hop.wait_recv()

        grad = jnp.concatenate([ds0s[0], nxt[...]], axis=0)
        for e in range(fs_count):
            lift_at = dot_nn(grad, wp[e])
            spread_rows[flip(fs, e)] = lift_at
        dz = jnp.concatenate([spread_rows[e] for e in range(fs_count)], axis=1)
        strided_write(thin, 0, short, dz[0:short, 2 * width : 3 * width])
        for k in range(2):
            part = dz[1 : short + 1, k * width : (k + 1) * width]
            strided_write(thin, k + 1, short, jnp.where(shut, 0.0, part))
        value = cot_ref[...].astype(F32) + spread_read(thin)
        da[...] = value
        dfs_out[0] = value.astype(BF)
        out_f = spread(dfs_out)
        ff_rows.service(0)
        ds0_f.relay()
        for copy in z_f:
            copy.wait_recv()
        g_pool = jnp.zeros((width, pc), F32)
        for e in range(fs_count):
            ds0_f.ready(e)
            g_pool = g_pool + dot_tn(ds0s[e], z_rel[e])
        group[:, 3 * hd : 3 * hd + pc] = g_pool.astype(BF)

        wait_all(lift_f)
        for e in range(fs_count):
            lift[flip(fs, e)] = lift_rel[e].astype(F32)
        lifted = jnp.concatenate([lift[e] for e in range(fs_count)], axis=1)
        for n in range(3):
            strided_write(thin, n, short, lifted[:, n * width : (n + 1) * width])
        out[...] = (after[...] + spread_read(thin)).astype(BF)
        ff_rows.finish()
        out_f.relay()
        out_f.all_ready()

        @pl.when(fs > 0)
        def _():
            hop.wait_send()

        for copy in stores:
            copy.wait()
        net.finish()

    outs = [
        ((total, width), BF),
        ((total, 3 * hd), BF),
        ((total, width), BF),
        ((total, width), BF),
        ((total, fj), BF),
        ((total, fj), BF),
        ((width, width), BF),
        ((rows, width), F32),
        ((width, 3 * hd), BF),
        ((width, fj), BF),
        ((width, fj), BF),
        ((8, width), F32),
        ((rows, width), BF),
        ((rows, width), F32),
        ((fs_count, rows, width), BF),
        ((width, cb), BF),
        ((rw, 2 * fj), F32),
        ((8, width), F32),
    ]
    wide = max(width, fj)
    pieces = (fs_count, short, width)
    scatter = [((half, short, width), BF)] * 2 + [((half - 1, short, width), BF)] * 2 + [((half, short, width), F32)]
    scratch = [
        ((rows, width), F32),
        ((fs_count, short, pc), BF),
        ((short, width), F32),
        ((fs_count, width, pc), BF),
        ((width, 3 * hd), BF),
        ((width, pc), BF),
        ((fs_count, short, pc), BF),
        ((total, width), BF),
        ((total, 3 * hd), BF),
        ((total, width), BF),
        ((total, width), BF),
        ((total, fj), BF),
        ((total, fj), BF),
        ((fs_count, rows, width), BF),
        ((fs_count, short, pc), BF),
        ((2, 3, rw, hd), BF),
        ((3, width, hd), BF),
        ((3, width, hd), BF),
        ((width, LANES), BF),
        ((fs_count, width, hd), BF),
        ((fs_count, width, hd), BF),
        ((fs_count, total, hd), BF),
        ((heads, total, LANES), BF),
        ((heads, total, LANES), BF),
        ((hd, total), BF),
        ((width, width), BF),
        ((width, width), BF),
        ((rows, wide), F32),
        ((rows, wide), BF),
        ((rows, width), F32),
        ((fs_count * HALO, width), F32),
        ((fs_count * HALO, width), F32),
        ((half, long_rows, width), BF),
        ((half, long_rows, width), BF),
        ((half - 1, long_rows, width), BF),
        ((half - 1, long_rows, width), BF),
        ((half, long_rows, width), F32),
        ((width // LANES, long_rows, LANES), F32),
        ((fs_count, width, hd), BF),
        ((width, fj), BF),
        ((width, fj), BF),
        ((width, 2 * fj), BF),
        ((y_count - 1, z_count, rw, 2 * fj), BF),
        ((z_count - 1, rw, 2 * fj), BF),
        ((z_count - 1, rw, 2 * fj), BF),
        *scatter,
        ((fs_count, short, pc), BF),
        ((fs_count, short, pc), BF),
        (pieces, BF),
        ((total_b, width), F32),
        ((fs_count, short, pc), BF),
        (pieces, BF),
        ((total_b, width), BF),
        ((fs_count, short, hd), BF),
        ((fs_count, short, hd), BF),
        ((fs_count, short, hd), BF),
        ((fs_count, short, hd), BF),
        ((total_b, hd), BF),
        (pieces, BF),
        (pieces, BF),
        ((HALO, width), BF),
        ((total_b, width), BF),
        ((total_b, width), BF),
        ((total_b, 3 * hd), BF),
        ((fs_count, total_b, hd), BF),
        ((total_b, width), BF),
        ((hd, total_b), BF),
        ((total_b, LANES), F32),
        ((total_b, LANES), F32),
        ((total_b, 3 * hd), BF),
        ((total_b, wide), F32),
        ((total_b, fj), BF),
        ((total_b, fj), F32),
        ((total_b, fj), BF),
        ((total_b, width), F32),
        ((short, width), F32),
        *scatter,
        *scatter,
        *scatter,
        ((fs_count, short + HALO, pc), F32),
        ((fs_count, short, pc), F32),
    ]
    tail = [pltpu.VMEM((heads, (n + 1) * blk_b, blk_b), BF) for n in range(blocks_b)]
    return pl.pallas_call(
        body,
        out_shape=[jax.ShapeDtypeStruct(s, t) for s, t in outs],
        in_specs=[vmem(), vmem(), smem()] + [vmem()] * 9,
        out_specs=[hbm()] * 6 + [vmem()] * (len(outs) - 6),
        scratch_shapes=[pltpu.VMEM(s, t) for s, t in scratch] + [pltpu.SemaphoreType.DMA((sems,))] * 2 + tail,
        compiler_params=pltpu.CompilerParams(collective_id=3, has_side_effects=True, vmem_limit_bytes=VMEM_BYTES),
        cost_estimate=cost(4e10, 5e7),
        name="forward_all",
    )(tokens, cot, triples, *weights, gains_t, cos, sin)


class RowSum:
    def __init__(self, net, place, grad, ybuf, zsend, zrecv, total, q_send=None, q_recv=None, q_total=None):
        self.net, self.grad, self.ybuf = net, grad, ybuf
        self.zsend, self.zrecv, self.total = zsend, zrecv, total
        self.q_send, self.q_recv, self.q_total = q_send, q_recv, q_total
        self.dp, self.fs, self.y_count, self.z_count, self.fs_count, self.rw = place
        self.ys, self.zs, self.qs = {}, {}, []

    def rows_of(self, step):
        return pl.ds(pl.multiple_of(flip(self.dp, step) * self.rw, 16), self.rw)

    def start(self):
        for m in list(range(1, self.z_count)) + [0]:
            self.ys[m] = [
                self.net.start(
                    self.grad.at[self.rows_of(m * self.y_count + j), :],
                    self.ybuf.at[j - 1, m],
                    (flip(self.dp, j), self.fs),
                )
                for j in range(1, self.y_count)
            ]
        if self.q_send is not None:
            self.q_base = self.net.used
            self.net.used += 3 * self.z_count

    def owner(self, kind):
        place = kind * self.fs_count + self.fs
        return lax.div(place, 3), lax.rem(place, 3)

    def service(self, m):
        for copy in self.ys[m]:
            copy.wait_recv()
        got = self.grad[self.rows_of(m * self.y_count), :].astype(F32)
        for j in range(1, self.y_count):
            got = got + self.ybuf[j - 1, m].astype(F32)
        there = flip(self.dp, m * self.y_count)
        lo = 0
        if self.q_send is not None:
            hd = self.q_send.shape[3]
            lo = 3 * hd
            for kind in range(3):
                to, slot = self.owner(kind)
                self.q_send[m, kind] = got[:, kind * hd : (kind + 1) * hd].astype(BF)
                copy = pltpu.make_async_remote_copy(
                    src_ref=self.q_send.at[m, kind],
                    dst_ref=self.q_recv.at[m, slot],
                    send_sem=self.net.send.at[self.q_base + 3 * m + kind],
                    recv_sem=self.net.recv.at[self.q_base + 3 * m + slot],
                    device_id=(there, to),
                    device_id_type=MESH,
                )
                if m:
                    copy.start()
                    self.qs.append((copy, None))
                else:

                    @pl.when(to != self.fs)
                    def _():
                        copy.start()

                    @pl.when(to == self.fs)
                    def _():
                        self.q_recv[0, slot] = self.q_send[0, kind]

                    self.qs.append((copy, to != self.fs))
        width = self.total.shape[1]
        rest = got[:, lo : lo + width]
        if m:
            self.zsend[m - 1] = rest.astype(BF)
            self.zs[m] = self.net.start(self.zsend.at[m - 1], self.zrecv.at[m - 1], (there, self.fs))
        else:
            self.total[...] = rest

    def finish(self):
        rest = self.total[...]
        for m in range(1, self.z_count):
            self.zs[m].wait_recv()
            rest = rest + self.zrecv[m - 1].astype(F32)
        self.total[...] = rest
        if self.q_send is None:
            return
        for t in range(3):
            giver = lax.rem(3 * self.fs + t, self.fs_count)
            for m in range(self.z_count):
                landed = self.q_recv.at[m, t]
                wait = pltpu.make_async_copy(landed, landed, self.net.recv.at[self.q_base + 3 * m + t])
                if m:
                    wait.wait()
                else:

                    @pl.when(giver != self.fs)
                    def _():
                        wait.wait()

        for t in range(3):
            block = self.q_recv[0, t].astype(F32)
            for m in range(1, self.z_count):
                block = block + self.q_recv[m, t].astype(F32)
            self.q_total[t] = block
        for copy, when in self.qs:
            if when is None:
                copy.wait_send()
            else:

                @pl.when(when)
                def _():
                    copy.wait_send()


class HeadSum:
    def __init__(self, net, place, grad, send, recv, total):
        self.net, self.grad, self.send, self.recv, self.total = net, grad, send, recv, total
        self.dp, self.fs, self.y_count, self.z_count, self.fs_count, self.rw = place
        self.count, self.copies = send.shape[0], []

    def start(self):
        base, hd = self.net.used, self.send.shape[3]
        self.base = base
        self.net.used += 3 * self.count
        for step in reversed(range(self.count)):
            rows = pl.ds(pl.multiple_of(flip(self.dp, step) * self.rw, 16), self.rw)
            for kind in range(3):
                place = kind * self.fs_count + self.fs
                to, slot = lax.div(place, 3), lax.rem(place, 3)
                self.send[step, kind] = self.grad[rows, kind * hd : (kind + 1) * hd]
                copy = pltpu.make_async_remote_copy(
                    src_ref=self.send.at[step, kind],
                    dst_ref=self.recv.at[step, slot],
                    send_sem=self.net.send.at[base + 3 * step + kind],
                    recv_sem=self.net.recv.at[base + 3 * step + slot],
                    device_id=(flip(self.dp, step), to),
                    device_id_type=MESH,
                )
                if step:
                    copy.start()
                    self.copies.append((copy, None))
                else:

                    @pl.when(to != self.fs)
                    def _():
                        copy.start()

                    @pl.when(to == self.fs)
                    def _():
                        self.recv[0, slot] = self.send[0, kind]

                    self.copies.append((copy, to != self.fs))

    def finish(self):
        for t in range(3):
            giver = lax.rem(3 * self.fs + t, self.fs_count)
            for step in range(self.count):
                landed = self.recv.at[step, t]
                wait = pltpu.make_async_copy(landed, landed, self.net.recv.at[self.base + 3 * step + t])
                if step:
                    wait.wait()
                else:

                    @pl.when(giver != self.fs)
                    def _():
                        wait.wait()

            block = self.recv[0, t].astype(F32)
            for step in range(1, self.count):
                block = block + self.recv[step, t].astype(F32)
            self.total[t] = block
        for copy, when in self.copies:
            if when is None:
                copy.wait_send()
            else:

                @pl.when(when)
                def _():
                    copy.wait_send()


class Scatter:
    def __init__(self, net, dp, fs, fs_count, sbuf, rbuf, xsend, xrecv, acc):
        self.net, self.dp, self.fs, self.half = net, dp, fs, fs_count // 2
        self.sbuf, self.rbuf, self.xsend, self.xrecv, self.acc = sbuf, rbuf, xsend, xrecv, acc
        self.first, self.hops, self.slot = {}, {}, 0

    def send_odd(self, j):
        self.first[j] = self.net.start(self.sbuf.at[j], self.rbuf.at[j], (self.dp, flip(self.fs, 1)))

    def join(self, j):
        self.first[j].wait_recv()
        self.acc[j] = self.acc[j] + self.rbuf[j].astype(F32)

    def give(self, j):
        bit = (2 * j) & -(2 * j)
        slot = self.slot
        self.slot += 1
        self.xsend[slot] = self.acc[j].astype(BF)
        self.hops[j] = (self.net.start(self.xsend.at[slot], self.xrecv.at[slot], (self.dp, flip(self.fs, bit))), slot)

    def take(self, j):
        low = j & -j
        copy, slot = self.hops[j]
        copy.wait_recv()
        self.acc[j - low] = self.acc[j - low] + self.xrecv[slot].astype(F32)

    def sent(self):
        for copy in list(self.first.values()) + [copy for copy, _ in self.hops.values()]:
            copy.wait_send()
            self.net.open = [other for other in self.net.open if other is not copy]

    def upper(self):
        if self.half == 2:
            self.give(1)

    def finish(self):
        if self.half == 2:
            self.take(1)
            return
        bit = 1
        while bit < self.half:
            gives = [j for j in range(self.half) if j & bit and not j & (bit - 1)]
            for j in gives:
                self.give(j)
            for j in gives:
                self.take(j)
            bit *= 2


def query_rows(total):
    return QB if total <= 2048 else QB // 2


def backward_one(
    y_count, dp_count, fs_count, da, dfs, n2, hid_in, slope_in, wi, wd, mid, gain_rows, qkv, wo_full, wq, cos, sin, triples, n1, att_rel, tokens, group_b, dgain_b
):
    rows, width = tokens.shape
    total = rows * fs_count
    fj, hd = wi.shape[1], wq.shape[1] // 3
    heads, docs = hd // HEAD, triples.shape[1]
    z_count, rw = dp_count // y_count, width // dp_count
    cb = group_b.shape[1]
    blk, half = query_rows(total), fs_count // 2
    blocks = total // blk
    sems = 96 + 12 * dp_count

    def body(
        da_ref, dfs, n2_hbm, hid_hbm, slope_hbm, wi_ref, wd_ref, mid_hbm, gain_ref, qkv_hbm, wo_ref, wq_ref, cos_hbm, sin_hbm, triples_ref, n1_hbm, att_hbm, tok, gb, dgain_two,
        grad_in, dgain, sum_b, sum_ff, sum_o, sum_q,
        n2_ref, mid_ref, qkv_ref, cos_ref, sin_ref, n1_ref, att_ref, da_low, do_out, do_in, da_out, da_in, hid, slope, dpre, work, qs, ks, kt, dk, dv, dm, cols, g_ff, g_at,
        sbuf, rbuf, xsend, xrecv, acc, yb, zsb, zrb, qsb, qrb, yf, zsf, zrf, ya, zsa, zra, qsa, qra, tiles, send_sem, recv_sem,
        *ps,
    ):
        dp, fs = lax.axis_index("dp"), lax.axis_index("fsdp")
        net = Net(send_sem, recv_sem)
        place = (dp, fs, y_count, z_count, fs_count, rw)
        dqkv = qkv_ref
        loads = {}
        for name, src, dst in (
            ("slope", slope_hbm, slope),
            ("n2", n2_hbm, n2_ref),
            ("hid", hid_hbm, hid),
            ("mid", mid_hbm, mid_ref),
            ("qkv", qkv_hbm, qkv_ref),
            ("att", att_hbm, att_ref),
            ("cos", cos_hbm, cos_ref),
            ("sin", sin_hbm, sin_ref),
            ("n1", n1_hbm, n1_ref),
        ):
            loads[name] = net.local(src, dst)
        barrier = pltpu.get_barrier_semaphore()
        for m in range(z_count):
            for e in range(fs_count):
                if m or e:
                    there = (flip(dp, m * y_count), flip(fs, e))
                    pl.semaphore_signal(barrier, inc=1, device_id=there, device_id_type=MESH)
        for j in range(1, y_count):
            pl.semaphore_signal(barrier, inc=1, device_id=(flip(dp, j), fs), device_id_type=MESH)
        pl.semaphore_wait(barrier, z_count * fs_count - 1 + y_count - 1)

        sum_of_b = RowSum(net, place, gb, yb, zsb, zrb, sum_b, qsb, qrb, sum_q.at[1])
        sum_of_b.start()

        def pull(e, out):
            work[:, 0:fj] = dot_nn(dfs[e], wd_ref[...])

            def one(r):
                at = pl.ds(pl.multiple_of(e * rows + r, HEAD), HEAD)
                dpre[at, :] = (work[pl.ds(r, HEAD), 0:fj] * slope[at, :].astype(F32)).astype(BF)

            row_loop(rows, one)
            out[...] = dot_nt(dpre[e * rows : (e + 1) * rows, :], wi_ref[...]).astype(out.dtype)

        def part_into(scatter, e, fill):
            if e % 2:
                fill(e, scatter.sbuf.at[e // 2])
                scatter.send_odd(e // 2)
            else:
                fill(e, scatter.acc.at[e // 2])

        ff_sum = Scatter(net, dp, fs, fs_count, sbuf, rbuf, xsend, xrecv, acc)
        loads["slope"].wait()

        def both_steps(e):
            part_into(ff_sum, e, pull)

        for j in reversed(range(1, half)):
            both_steps(2 * j + 1)
            both_steps(2 * j)
        for j in range(1, half):
            ff_sum.join(j)
        ff_sum.upper()
        both_steps(1)
        both_steps(0)
        sum_of_b.service(1)
        for m in range(2, z_count):
            sum_of_b.service(m)
        ff_sum.join(0)
        loads["hid"].wait()
        loads["n2"].wait()
        g_ff[:, 0:fj] = dot_tn(n2_ref[...], dpre[...]).astype(BF)
        g_ff[:, fj : 2 * fj] = dot_tn(dfs[...].reshape(total, width), hid[...]).astype(BF)
        sum_of_b.service(0)
        sum_of_ff = RowSum(net, place, g_ff, yf, zsf, zrf, sum_ff)
        sum_of_ff.start()

        loads["qkv"].wait()
        lane_first, lane_end, lane = doc_bounds(triples_ref, docs)
        for r in range(0, total, blk):
            at = slice(r, r + blk)
            q = qkv_ref[at, 0:hd].astype(F32)
            k = qkv_ref[at, hd : 2 * hd].astype(F32)
            row = lax.broadcasted_iota(jnp.int32, (blk, LANES), 0) + r
            inside = (row >= 3 * lane_first) & (row < 3 * lane_end)
            fk = jnp.where(inside, 1.0, 0.0)
            fq = jnp.where(inside | (lane >= docs), 0.0, MASKED)
            head_inputs(qs, ks, at, q, k, fq, fk, heads)
            kt[:, at] = k.T.astype(BF)
            dk[at, :] = jnp.zeros((blk, LANES), F32)
            dv[at, :] = jnp.zeros((blk, LANES), F32)

        def recompute(n):
            r = n * blk
            for h in range(heads):
                e, inv = softmax_block(ks, qs, h, r, r + blk)
                ps[n][h] = (e * inv).astype(BF)

        for n in range(blocks // 2):
            recompute(n)

        ff_sum.finish()
        loads["mid"].wait()
        for r in range(0, rows, LANES):
            at = slice(r, r + LANES)
            dx, dg = layer_norm_back(mid_ref[at, :], gain_ref[1:2, :], acc[0, at, :])
            dx = dx + da_ref[at, :]
            dm[at, :] = dx
            da_low[at, :] = dx.astype(BF)
            dg = jnp.sum(dg, axis=0, keepdims=True)
            gain_two = dg if r == 0 else gain_two + dg
        got = dot_nt(da_low[...], wo_ref[...]).astype(BF)
        for e in range(fs_count):
            do_out[e] = got[:, e * hd : (e + 1) * hd]
            da_out[e] = da_low[:, e * hd : (e + 1) * hd]

        def exchange(blocks_of, landed):
            found = []
            for e in range(1, fs_count):
                found.append(net.start(blocks_of.at[flip(fs, e)], landed.at[e], (dp, flip(fs, e))))
            landed[0] = blocks_of[fs]
            return found

        do_f = exchange(do_out, do_in)
        da_f = exchange(da_out, da_in)
        for n in range(blocks // 2, blocks):
            recompute(n)
        for m in range(1, z_count):
            sum_of_ff.service(m)
        sum_of_ff.service(0)

        place_of = lax.broadcasted_iota(jnp.int32, (blk, LANES), 1) // HEAD
        for r in range(0, total, blk):
            at = slice(r, r + blk)
            q = widen(qkv_ref[at, 0:hd].astype(F32))
            for h in range(heads):
                qs[h, at, :] = jnp.where(place_of == h, q, 0.0).astype(BF)
        lane_head = lax.broadcasted_iota(jnp.int32, (rows, LANES), 1) // HEAD
        for e in range(fs_count):
            if e:
                do_f[e - 1].wait_recv()
            base = pl.multiple_of(flip(fs, e) * rows, 16)
            do = widen(do_in[e].astype(F32))
            for h in range(heads):
                ks[h, pl.ds(base, rows), :] = jnp.where(lane_head == h, do, 0.0).astype(BF)
        for e in range(fs_count):
            if e:
                da_f[e - 1].wait_recv()
            cols[pl.ds(pl.multiple_of(flip(fs, e) * rows, 16), rows), :] = da_in[e]

        loads["att"].wait()
        g_out = dot_tn(att_ref[...], cols[...]).astype(BF)
        for e in range(fs_count):
            base = pl.multiple_of(flip(fs, e) * hd, 16)
            g_at[pl.ds(base, hd), 3 * hd : 4 * hd] = g_out[e * hd : (e + 1) * hd, :]
        sum_of_b.finish()

        loads["cos"].wait()
        loads["sin"].wait()
        for n in range(blocks):
            r, stop = n * blk, (n + 1) * blk
            at = slice(r, stop)
            found = []
            add_k = add_v = None
            for h in range(heads):
                p = ps[n][h]
                v = widen(qkv_ref[0:stop, 2 * hd : 3 * hd])
                grad = dot_nt(v, ks[h, at, :])
                wide = p.astype(F32)
                middle = jnp.sum(wide * grad, axis=0, keepdims=True)
                dr = (wide * (grad - middle) * 0.125).astype(BF)
                part_v = dot_nn(p, ks[h, at, :])
                part_k = dot_nn(dr, qs[h, at, :])
                add_v = part_v if add_v is None else add_v + part_v
                add_k = part_k if add_k is None else add_k + part_k
                found.append(dot_nn(kt[h * HEAD : (h + 1) * HEAD, 0:stop], dr))
            dk[0:stop, :] += add_k
            dv[0:stop, :] += add_v
            dq = jnp.concatenate(found, axis=0).T
            dqkv[at, 0:hd] = (dq * cos_ref[at, :] - partner(dq) * sin_ref[at, :]).astype(BF)
        for r in range(0, total, blk):
            at = slice(r, r + blk)
            grad = dk[at, 0:hd]
            dqkv[at, hd : 2 * hd] = (grad * cos_ref[at, :] - partner(grad) * sin_ref[at, :]).astype(BF)
            dqkv[at, 2 * hd : 3 * hd] = dv[at, 0:hd].astype(BF)
        loads["n1"].wait()
        g_at[:, 0 : 3 * hd] = dot_tn(n1_ref[...], dqkv[...]).astype(BF)
        sum_of_at = RowSum(net, place, g_at, ya, zsa, zra, sum_o, qsa, qra, sum_q.at[0])
        sum_of_at.start()

        ff_sum.sent()
        at_sum = Scatter(net, dp, fs, fs_count, sbuf, rbuf, xsend, xrecv, acc)
        tiles[0] = jnp.zeros((8, width), F32)

        def push_out(e, out):
            base = pl.multiple_of(flip(fs, e) * rows, 16)
            part = dot_nt(dqkv[pl.ds(base, rows), :], wq_ref[...])
            out[...] = part.astype(out.dtype)
            work[:, 0:width] = part
            total_of = jnp.zeros((8, width), F32)
            for r in range(0, rows, HEAD):
                grown = work[r : r + HEAD, 0:width] * n1_ref[pl.ds(base + r, HEAD), :].astype(F32)
                total_of = total_of + jnp.sum(grown.reshape(HEAD // 8, 8, width), axis=0)
            tiles[0] = tiles[0] + total_of

        for e in reversed(range(2, fs_count)):
            part_into(at_sum, e, push_out)
        part_into(at_sum, 1, push_out)
        for j in range(1, half):
            at_sum.join(j)
        at_sum.upper()
        part_into(at_sum, 0, push_out)
        gain_one = jnp.sum(tiles[0], axis=0, keepdims=True) / gain_ref[0:1, :]
        which = lax.broadcasted_iota(jnp.int32, (8, width), 0)
        both = jnp.where(which == 0, gain_one, jnp.where(which == 1, gain_two, 0.0))
        both = jnp.where(which == 2, dgain_two[0:1, :], jnp.where(which == 3, dgain_two[1:2, :], both))
        hops = [(dp, flip(fs, 1 << n)) for n in range(fs_count.bit_length() - 1)]
        hops += [(flip(dp, 1 << n), fs) for n in range(y_count.bit_length() - 1)]

        def hop_out(n, value):
            tiles[1 + n] = value
            return net.start(tiles.at[1 + n], tiles.at[1 + len(hops) + n], hops[n])

        hop = hop_out(0, both)
        sum_of_at.service(1)
        for n in range(1, len(hops) - 1):
            hop.wait_recv()
            both = both + tiles[len(hops) + n]
            hop = hop_out(n, both)
        for m in range(2, z_count):
            sum_of_at.service(m)
        sum_of_at.service(0)
        at_sum.join(0)
        sum_of_ff.finish()
        at_sum.finish()
        last = len(hops) - 1
        hop.wait_recv()
        both = both + tiles[len(hops) + last]
        hop = hop_out(last, both)
        for r in range(0, rows, LANES):
            at = slice(r, r + LANES)
            dx, _ = layer_norm_back(tok[at, :].astype(F32), gain_ref[0:1, :], acc[0, at, :])
            grad_in[at, :] = dx + dm[at, :]
        hop.wait_recv()
        dgain[...] = both + tiles[1 + len(hops) + last]
        sum_of_at.finish()
        net.finish()

    outs = [
        ((rows, width), F32),
        ((8, width), F32),
        ((rw, cb - 3 * hd), F32),
        ((rw, 2 * fj), F32),
        ((rw, hd), F32),
        ((2, 3, rw, hd), F32),
    ]
    wide = max(width, fj)
    zy = (y_count - 1, z_count, rw)
    scratch = [
        ((total, width), BF),
        ((rows, width), F32),
        ((total, 3 * hd), BF),
        ((total, hd), F32),
        ((total, hd), F32),
        ((total, width), BF),
        ((total, width), BF),
        ((rows, width), BF),
        ((fs_count, rows, hd), BF),
        ((fs_count, rows, hd), BF),
        ((fs_count, rows, hd), BF),
        ((fs_count, rows, hd), BF),
        ((total, fj), BF),
        ((total, fj), BF),
        ((total, fj), BF),
        ((rows, wide), F32),
        ((heads, total, LANES), BF),
        ((heads, total, LANES), BF),
        ((hd, total), BF),
        ((total, LANES), F32),
        ((total, LANES), F32),
        ((rows, width), F32),
        ((total, hd), BF),
        ((width, 2 * fj), BF),
        ((width, 4 * hd), BF),
        ((half, rows, width), BF),
        ((half, rows, width), BF),
        ((half - 1, rows, width), BF),
        ((half - 1, rows, width), BF),
        ((half, rows, width), F32),
        (zy + (cb,), BF),
        ((z_count - 1, rw, cb - 3 * hd), BF),
        ((z_count - 1, rw, cb - 3 * hd), BF),
        ((z_count, 3, rw, hd), BF),
        ((z_count, 3, rw, hd), BF),
        (zy + (2 * fj,), BF),
        ((z_count - 1, rw, 2 * fj), BF),
        ((z_count - 1, rw, 2 * fj), BF),
        (zy + (4 * hd,), BF),
        ((z_count - 1, rw, hd), BF),
        ((z_count - 1, rw, hd), BF),
        ((z_count, 3, rw, hd), BF),
        ((z_count, 3, rw, hd), BF),
        ((2 * (fs_count.bit_length() + y_count.bit_length() - 2) + 1, 8, width), F32),
    ]
    tail = [pltpu.VMEM((heads, (n + 1) * blk, blk), BF) for n in range(blocks)]
    arrays = (da, dfs, n2, hid_in, slope_in, wi, wd, mid, gain_rows, qkv, wo_full, wq, cos, sin, triples, n1, att_rel, tokens, group_b, dgain_b)
    return pl.pallas_call(
        body,
        out_shape=[jax.ShapeDtypeStruct(s, t) for s, t in outs],
        in_specs=[hbm() if n in (2, 3, 4, 7, 9, 12, 13, 15, 16) else smem() if n == 14 else vmem() for n in range(20)],
        out_specs=[vmem()] * len(outs),
        scratch_shapes=[pltpu.VMEM(s, t) for s, t in scratch] + [pltpu.SemaphoreType.DMA((sems,))] * 2 + tail,
        compiler_params=pltpu.CompilerParams(collective_id=4, has_side_effects=True, vmem_limit_bytes=VMEM_BYTES),
        cost_estimate=cost(4e10, 3e7),
        name="backward_one",
    )(*arrays)


def middle(y_count, dp_count, fs_count, s0, after, z_blocks, cot, c_rel, wq, wu, weights, wp, gain_rows, cos, sin, triples):
    short, width = s0.shape
    rows, total = short * 3, short * fs_count
    hd = wq.shape[1] // 3
    pc = wp.shape[2]
    wout, win, wdown = weights
    fj, rw = win.shape[2], win.shape[1]
    z_count = dp_count // y_count
    heads, docs = hd // HEAD, triples.shape[1]
    blk = min(QB, total)
    blocks, half = total // blk, fs_count // 2
    cb = 4 * hd + 2 * pc
    sems = 96 + 16 * fs_count + 6 * dp_count

    def body(
        s0_ref, after_ref, z_ref, cot_ref, c_ref, wq_ref, wu_ref, o_in, i_in, d_in, wp_ref, gain_ref, cos_ref, sin_ref, triples_ref,
        out, da, dfs_out, group, sum_ff, dgain,
        wos, wi_ref, wd_ref, g_ff, yg, zsg, zrg, sd, rd, xd, yd, ad, lift_send, lift_rel,
        s0s, x_all, wo_at, hold, turned, z_rel, dfs, df_all, do_out, do_in, da_out, da_in, cols, s1s, ds0s, nxt,
        n1, n2, qkv, att, att_rel, qs, ks, vt, kt, dk, dv, dqkv, work, hid, slope, dpre, m_all, dm,
        sf, rf, xf, yf, af, sb, rb, xb, yb, ab, sa, ra, xa, ya, aa, thin, spread_rows, lift, send_sem, recv_sem, *ps,
    ):
        dp, fs = lax.axis_index("dp"), lax.axis_index("fsdp")
        net = Net(send_sem, recv_sem)

        def base_of(e, amount):
            return pl.multiple_of(flip(fs, e) * amount, 16)

        def spread(pieces, src=None):
            return Flight(net, dp, fs, fs_count, pieces, pieces.at[0] if src is None else src)

        s0s[0] = s0_ref[...].astype(BF)
        nxt[...] = jnp.zeros(nxt.shape, BF)
        here = pl.ds(pl.multiple_of(dp * rw, 16), rw)
        wos[0, here, :] = o_in[1].astype(BF)
        wi_ref[here, :] = i_in[1].astype(BF)
        wd_ref[here, :] = d_in[1].astype(BF)
        barrier = pltpu.get_barrier_semaphore()
        for e in range(1, fs_count):
            pl.semaphore_signal(barrier, inc=1, device_id=(dp, flip(fs, e)), device_id_type=MESH)
        others = [m * y_count for m in range(1, z_count)] + list(range(1, y_count))
        for step in others:
            pl.semaphore_signal(barrier, inc=1, device_id=(flip(dp, step), fs), device_id_type=MESH)
        pl.semaphore_wait(barrier, fs_count - 1 + len(others))

        def of(buf, step):
            return buf.at[pl.ds(pl.multiple_of(flip(dp, step) * rw, 16), rw), :]

        def along_z(buf):
            return [
                net.start(of(buf, 0), of(buf, 0), (flip(dp, m * y_count), fs)) for m in range(1, z_count)
            ]

        def along_y(buf, m):
            return [
                net.start(of(buf, m * y_count), of(buf, m * y_count), (flip(dp, n), fs)) for n in range(1, y_count)
            ]

        def pass_on(buf, came, passed):
            for m in range(1, z_count):
                came[m - 1].wait_recv()
                passed += along_y(buf, m)

        def wait_all(copies):
            for copy in copies:
                copy.wait_recv()

        s0_f = spread(s0s)
        came = [along_z(buf) for buf in (wos.at[0], wi_ref, wd_ref)]
        passed = [along_y(buf, 0) for buf in (wos.at[0], wi_ref, wd_ref)]

        dsum = Scatter(net, dp, fs, fs_count, sd, rd, xd, yd, ad)
        for e in reversed(range(fs_count)):
            part = dot_nt(c_ref[e], wu_ref[...])
            if e % 2:
                sd[e // 2] = part.astype(BF)
                dsum.send_odd(e // 2)
            else:
                ad[e // 2] = part

        def exchange(blocks_of, landed):
            found = []
            for e in range(1, fs_count):
                found.append(net.start(blocks_of.at[flip(fs, e)], landed.at[e], (dp, flip(fs, e))))
            landed[0] = blocks_of[fs]
            return found

        lane_first, lane_end, lane = doc_bounds(triples_ref, docs)
        for n in range(1, half):
            dsum.join(n)
        dsum.upper()
        s0_f.relay()
        pass_on(wos.at[0], came[0], passed[0])
        for e in range(fs_count):
            s0_f.ready(e)
            at = pl.ds(base_of(e, short), short)
            value = s0_ref[...] if e == 0 else s0s[e].astype(F32)
            x_all[at, :] = value
            n1[at, :] = layer_norm(value, gain_ref[2:3, :]).astype(BF)
        for r in range(0, total, blk):
            at = slice(r, r + blk)
            got = dot_nn(n1[at, :], wq_ref[...])
            q, k, v = got[:, :hd], got[:, hd : 2 * hd], got[:, 2 * hd :]
            q = (q * cos_ref[at, :] + partner(q) * sin_ref[at, :]).astype(BF)
            k = (k * cos_ref[at, :] + partner(k) * sin_ref[at, :]).astype(BF)
            qkv[at, 0:hd] = q
            qkv[at, hd : 2 * hd] = k
            qkv[at, 2 * hd : 3 * hd] = v.astype(BF)
            row = lax.broadcasted_iota(jnp.int32, (blk, LANES), 0) + r
            inside = (row >= lane_first) & (row < lane_end)
            fk = jnp.where(inside, 1.0, 0.0)
            fq = jnp.where(inside | (lane >= docs), 0.0, MASKED)
            head_inputs(qs, ks, at, q.astype(F32), k.astype(F32), fq, fk, heads)
            vt[:, at] = v.T.astype(BF)
            kt[:, at] = k.astype(F32).T.astype(BF)
            dk[at, :] = jnp.zeros((blk, LANES), F32)
            dv[at, :] = jnp.zeros((blk, LANES), F32)
        dsum.join(0)
        dsum.finish()
        dm[...] = ad[0]
        dfs[0] = ad[0].astype(BF)
        df_f = spread(dfs)
        wait_all(passed[0])
        wo_f = spread(wos, wos.at[0])
        flights = []
        for n in range(blocks):
            r, stop = n * blk, (n + 1) * blk
            found = []
            for h in range(heads):
                e, inv = softmax_block(ks, qs, h, r, stop)
                ps[n][h] = (e * inv).astype(BF)
                found.append(dot_nn(vt[h * HEAD : (h + 1) * HEAD, 0:stop], ps[n][h]))
            att[0, r:stop, :] = jnp.concatenate(found, axis=0).T.astype(BF)
            flights.append(spread(att.at[:, r:stop, :], att.at[0, r:stop, :]))
            if n == 0:
                pass_on(wi_ref, came[1], passed[1])
                df_f.relay()
                wo_f.relay()
        place_of = lax.broadcasted_iota(jnp.int32, (blk, LANES), 1) // HEAD
        for r in range(0, total, blk):
            at = slice(r, r + blk)
            q = widen(qkv[at, 0:hd].astype(F32))
            for h in range(heads):
                qs[h, at, :] = jnp.where(place_of == h, q, 0.0).astype(BF)

        pass_on(wd_ref, came[2], passed[2])
        wo_f.all_ready()
        for e in range(fs_count):
            wo_at[flip(fs, e)] = wos[e]
        for e in range(fs_count):
            hold[:, e * hd : (e + 1) * hd] = wo_at[e]
        for e in range(fs_count):
            turned[e * hd : (e + 1) * hd, :] = hold[pl.ds(base_of(e, hd), hd), :]
        for flight in flights:
            flight.relay()
        for flight in flights:
            flight.all_ready()
        for e in range(fs_count):
            att_rel[:, e * hd : (e + 1) * hd] = att[e]

        work[:, 0:width] = x_all[...] + dot_nn(att_rel[...], turned[...])

        def norm_all(r):
            at = pl.ds(r, HEAD)
            m = work[at, 0:width]
            m_all[at, :] = m
            n2[at, :] = layer_norm(m, gain_ref[3:4, :]).astype(BF)

        row_loop(total, norm_all)
        wait_all(passed[1])
        work[:, 0:fj] = dot_nn(n2[...], wi_ref[...])

        def activate_all(r):
            at = pl.ds(r, HEAD)
            value, rate = gelu_both(work[at, 0:fj])
            hid[at, :] = value.astype(BF)
            slope[at, :] = rate

        row_loop(total, activate_all)
        wait_all(passed[2])
        work[:, 0:width] = dot_nt(hid[...], wd_ref[...])

        def give_out(scatter, source):
            for e in reversed(range(fs_count)):
                value = source[pl.ds(base_of(e, short), short), 0:width]
                if e % 2:
                    scatter.sbuf[e // 2] = value.astype(BF)
                    scatter.send_odd(e // 2)
                else:
                    scatter.acc[e // 2] = value

        fwd = Scatter(net, dp, fs, fs_count, sf, rf, xf, yf, af)
        give_out(fwd, work)
        for e in range(fs_count):
            df_f.ready(e)
            df_all[pl.ds(base_of(e, short), short), :] = dfs[e]
        work[:, 0:fj] = dot_nn(df_all[...], wd_ref[...])

        def pull_all(r):
            at = pl.ds(r, HEAD)
            dpre[at, :] = (work[at, 0:fj] * slope[at, :]).astype(BF)

        row_loop(total, pull_all)
        work[:, 0:width] = dot_nt(dpre[...], wi_ref[...])
        bwd = Scatter(net, dp, fs, fs_count, sb, rb, xb, yb, ab)
        give_out(bwd, work)
        for j in range(1, half):
            bwd.join(j)
        bwd.upper()
        for j in range(1, half):
            fwd.join(j)
        fwd.upper()
        g_ff[:, 0:fj] = dot_tn(n2[...], dpre[...]).astype(BF)
        g_ff[:, fj : 2 * fj] = dot_tn(df_all[...], hid[...]).astype(BF)
        ff_rows = RowSum(net, (dp, fs, y_count, z_count, fs_count, rw), g_ff, yg, zsg, zrg, sum_ff)
        ff_rows.start()
        bwd.join(0)
        bwd.finish()
        m_own = m_all[pl.ds(base_of(0, short), short), :]
        dx, dg = layer_norm_back(m_own, gain_ref[3:4, :], ab[0])
        dx = dx + dm[...]
        dm[...] = dx
        low_dx = dx.astype(BF)
        got = dot_nt(low_dx, hold[...]).astype(BF)
        for e in range(fs_count):
            do_out[e] = got[:, e * hd : (e + 1) * hd]
            da_out[e] = low_dx[:, e * hd : (e + 1) * hd]
        do_f = exchange(do_out, do_in)
        da_f = exchange(da_out, da_in)
        gain_two = jnp.sum(dg, axis=0, keepdims=True)

        fwd.join(0)
        fwd.finish()
        s1s[0] = (m_own + af[0]).astype(BF)
        s1_f = spread(s1s)
        z_f = exchange(z_ref, z_rel)
        wait_all(do_f)
        for e in range(fs_count):
            at = pl.ds(base_of(e, short), short)
            do = widen(do_in[e].astype(F32))
            lane_head = lax.broadcasted_iota(jnp.int32, (short, LANES), 1) // HEAD
            for h in range(heads):
                ks[h, at, :] = jnp.where(lane_head == h, do, 0.0).astype(BF)
        wait_all(da_f)
        for e in range(fs_count):
            cols[pl.ds(base_of(e, short), short), :] = da_in[e]
        s1_f.relay()

        g_out = dot_tn(att_rel[...], cols[...]).astype(BF)
        for e in range(fs_count):
            group[pl.ds(base_of(e, hd), hd), cb - hd : cb] = g_out[e * hd : (e + 1) * hd, :]
        for n in range(blocks):
            r, stop = n * blk, (n + 1) * blk
            at = slice(r, stop)
            found = []
            add_k = add_v = None
            for h in range(heads):
                p = ps[n][h]
                grad = dot_nt(widen(qkv[0:stop, 2 * hd : 3 * hd]), ks[h, at, :])
                wide = p.astype(F32)
                inner = jnp.sum(wide * grad, axis=0, keepdims=True)
                dr = (wide * (grad - inner) * 0.125).astype(BF)
                part_v = dot_nn(p, ks[h, at, :])
                part_k = dot_nn(dr, qs[h, at, :])
                add_v = part_v if add_v is None else add_v + part_v
                add_k = part_k if add_k is None else add_k + part_k
                found.append(dot_nn(kt[h * HEAD : (h + 1) * HEAD, 0:stop], dr))
            dk[0:stop, :] += add_k
            dv[0:stop, :] += add_v
            dq = jnp.concatenate(found, axis=0).T
            dqkv[at, 0:hd] = (dq * cos_ref[at, :] - partner(dq) * sin_ref[at, :]).astype(BF)
        for r in range(0, total, blk):
            at = slice(r, r + blk)
            grad = dk[at, 0:hd]
            dqkv[at, hd : 2 * hd] = (grad * cos_ref[at, :] - partner(grad) * sin_ref[at, :]).astype(BF)
            dqkv[at, 2 * hd : 3 * hd] = dv[at, 0:hd].astype(BF)
        work[:, 0:width] = dot_nt(dqkv[...], wq_ref[...])
        first = Scatter(net, dp, fs, fs_count, sa, ra, xa, ya, aa)
        give_out(first, work)
        for j in range(1, half):
            first.join(j)
        first.upper()
        group[:, 0 : 3 * hd] = dot_tn(n1[...], dqkv[...]).astype(BF)
        s1_f.all_ready()
        lift_f = []
        for e in range(fs_count):
            part = dot_nn(s1s[e], wu_ref[...]).astype(BF)
            if e:
                lift_send[e] = part
                lift_f.append(net.start(lift_send.at[e], lift_rel.at[e], (dp, flip(fs, e))))
            else:
                lift_rel[0] = part
        g_up = jnp.zeros((width, pc), F32)
        for e in range(fs_count):
            g_up = g_up + dot_tn(s1s[e], c_ref[e])
        group[:, 3 * hd + pc : 3 * hd + 2 * pc] = g_up.astype(BF)
        for m in range(1, z_count):
            ff_rows.service(m)
        first.join(0)
        first.finish()
        dx, dg = layer_norm_back(s0_ref[...], gain_ref[2:3, :], aa[0])
        ds0s[0] = (dx + dm[...]).astype(BF)
        gain_one = jnp.sum(dg, axis=0, keepdims=True)
        which = lax.broadcasted_iota(jnp.int32, (8, width), 0)
        dgain[...] = jnp.where(which == 0, gain_one, jnp.where(which == 1, gain_two, 0.0))

        hop = net.make(ds0s.at[0, 0:HALO, :], nxt, (dp, lax.rem(fs + fs_count - 1, fs_count)))

        @pl.when(fs > 0)
        def _():
            hop.start()

        ds0_f = spread(ds0s)
        row = lax.broadcasted_iota(jnp.int32, (short, LANES), 0) + fs * short + 1
        shut = jnp.max(jnp.where((row == lane_first) | (row >= total), 1.0, 0.0), axis=1, keepdims=True) > 0.0

        @pl.when(fs < fs_count - 1)
        def _():
            hop.wait_recv()

        grad = jnp.concatenate([ds0s[0], nxt[...]], axis=0)
        for e in range(fs_count):
            lift_at = dot_nn(grad, wp_ref[e])
            spread_rows[flip(fs, e)] = lift_at
        dz = jnp.concatenate([spread_rows[e] for e in range(fs_count)], axis=1)
        strided_write(thin, 0, short, dz[0:short, 2 * width : 3 * width])
        for k in range(2):
            part = dz[1 : short + 1, k * width : (k + 1) * width]
            strided_write(thin, k + 1, short, jnp.where(shut, 0.0, part))
        value = cot_ref[...].astype(F32) + spread_read(thin)
        da[...] = value
        dfs_out[0] = value.astype(BF)
        out_f = spread(dfs_out)
        ff_rows.service(0)
        ds0_f.relay()
        for copy in z_f:
            copy.wait_recv()
        g_pool = jnp.zeros((width, pc), F32)
        for e in range(fs_count):
            ds0_f.ready(e)
            g_pool = g_pool + dot_tn(ds0s[e], z_rel[e])
        group[:, 3 * hd : 3 * hd + pc] = g_pool.astype(BF)

        wait_all(lift_f)
        for e in range(fs_count):
            lift[flip(fs, e)] = lift_rel[e].astype(F32)
        lifted = jnp.concatenate([lift[e] for e in range(fs_count)], axis=1)
        for n in range(3):
            strided_write(thin, n, short, lifted[:, n * width : (n + 1) * width])
        out[...] = (after_ref[...] + spread_read(thin)).astype(BF)
        ff_rows.finish()
        out_f.relay()
        out_f.all_ready()

        @pl.when(fs > 0)
        def _():
            hop.wait_send()

        net.finish()

    wide = max(width, fj)
    pieces = (fs_count, short, width)
    scatter = [((half, short, width), BF)] * 2 + [((half - 1, short, width), BF)] * 2 + [((half, short, width), F32)]
    outs = [((rows, width), BF), ((rows, width), F32), ((fs_count, rows, width), BF), ((width, cb), BF), ((rw, 2 * fj), F32), ((8, width), F32)]
    scratch = [
        ((fs_count, width, hd), BF),
        ((width, fj), BF),
        ((width, fj), BF),
        ((width, 2 * fj), BF),
        ((y_count - 1, z_count, rw, 2 * fj), BF),
        ((z_count - 1, rw, 2 * fj), BF),
        ((z_count - 1, rw, 2 * fj), BF),
        *scatter,
        ((fs_count, short, pc), BF),
        ((fs_count, short, pc), BF),
        (pieces, BF),
        ((total, width), F32),
        ((fs_count, width, hd), BF),
        ((width, width), BF),
        ((width, width), BF),
        ((fs_count, short, pc), BF),
        (pieces, BF),
        ((total, width), BF),
        ((fs_count, short, hd), BF),
        ((fs_count, short, hd), BF),
        ((fs_count, short, hd), BF),
        ((fs_count, short, hd), BF),
        ((total, hd), BF),
        (pieces, BF),
        (pieces, BF),
        ((HALO, width), BF),
        ((total, width), BF),
        ((total, width), BF),
        ((total, 3 * hd), BF),
        ((fs_count, total, hd), BF),
        ((total, width), BF),
        ((heads, total, LANES), BF),
        ((heads, total, LANES), BF),
        ((hd, total), BF),
        ((hd, total), BF),
        ((total, LANES), F32),
        ((total, LANES), F32),
        ((total, 3 * hd), BF),
        ((total, wide), F32),
        ((total, fj), BF),
        ((total, fj), F32),
        ((total, fj), BF),
        ((total, width), F32),
        ((short, width), F32),
        *scatter,
        *scatter,
        *scatter,
        ((width // LANES, rows, LANES), F32),
        ((fs_count, short + HALO, pc), F32),
        ((fs_count, short, pc), F32),
    ]
    tail = [pltpu.VMEM((heads, (n + 1) * blk, blk), BF) for n in range(blocks)]
    arrays = (s0, after, z_blocks, cot, c_rel, wq, wu, wout, win, wdown, wp, gain_rows, cos, sin, triples)
    return pl.pallas_call(
        body,
        out_shape=[jax.ShapeDtypeStruct(s, t) for s, t in outs],
        in_specs=[vmem()] * 14 + [smem()],
        out_specs=[vmem()] * len(outs),
        scratch_shapes=[pltpu.VMEM(s, t) for s, t in scratch] + [pltpu.SemaphoreType.DMA((sems,))] * 2 + tail,
        compiler_params=pltpu.CompilerParams(collective_id=2, has_side_effects=True, vmem_limit_bytes=VMEM_BYTES),
        cost_estimate=cost(2e10, 2e7),
        name="middle",
    )(*arrays)


def owners_of(amount, dp_count, fs_count):
    found = []
    half = dp_count // 2
    for k in range(amount):
        found.append((dp_count // 4 + k % half, (2 * (k // half)) % fs_count + (2 * (k // half)) // fs_count))
    return found


def round_up(width):
    return -(-width // LANES) * LANES


def newton_schulz(box, x, norm, count, width, dp_count, rw, done):
    coef_a, coef_b, coef_c = NS_COEFS
    rows = dp_count * rw
    square = jnp.zeros((1, 1), F32)
    for at in range(count):
        block = box[at * dp_count : (at + 1) * dp_count, :, 0:width].reshape(rows, width)
        x[:, at * width : (at + 1) * width] = block
        wide = block.astype(F32)
        square = square + jnp.sum(jnp.sum(wide * wide, axis=0, keepdims=True), axis=1, keepdims=True)
    length = jnp.sqrt(square)
    norm[...] = jnp.broadcast_to(length, norm.shape)
    scale = 1.0 / (length + NORM_EPS)
    span = count * width
    for turn in range(NS_STEPS):
        gram = dot_nt(x[:, 0:span], x[:, 0:span])
        if turn == 0:
            gram = gram * (scale * scale)
        gram = gram.astype(BF)
        poly = (coef_b * gram.astype(F32) + coef_c * dot_nn(gram, gram)).astype(BF)
        for at in range(count):
            here = slice(at * width, (at + 1) * width)
            block = x[:, here]
            new = coef_a * block.astype(F32) + dot_nn(poly, block)
            if turn == 0:
                new = new * scale
            if turn < NS_STEPS - 1:
                x[:, here] = new.astype(BF)
            else:
                box[at * dp_count : (at + 1) * dp_count, :, 0:width] = new.astype(BF).reshape(dp_count, rw, width)
                done(at)


def muon(y_count, dp_count, fs_count, sums, moments, dgain):
    sum_q, sum_o, sum_ff, sum_ff1, sum_rest = sums
    rw, hd = sum_o.shape
    fj = sum_ff.shape[1] // 2
    pc = moments[4].shape[1]
    width = rw * dp_count
    z_count = dp_count // y_count
    devices = dp_count * fs_count
    widths = [fj, fj, fj, fj, 3 * hd, 3 * hd, pc, pc, hd, hd]
    widths = [round_up(w) for w in widths]
    amount, wide = len(widths), max(widths)
    owners = owners_of(amount, dp_count, fs_count)
    classes = sorted(set(widths))
    sems = 16
    z_bits = z_count.bit_length() - 1

    def body(
        q_ref, o_ref, ff_ref, ff1_ref, rest_ref, mq, mo, mi, md, mp, mu, ga,
        out, norms, dgain_out, box, x, norm, tiles, tsend, *rest_refs,
    ):
        pieces = rest_refs[:amount]
        send_sem, recv_sem, push_send, push_recv, give_send, give_recv, norm_send, norm_recv = rest_refs[amount:]
        dp, fs = lax.axis_index("dp"), lax.axis_index("fsdp")
        slot = fs * dp_count + dp
        net = Net(send_sem, recv_sem)

        def put(k, value):
            have = value.shape[1]
            if have < widths[k]:
                value = jnp.concatenate([value, jnp.zeros((rw, widths[k] - have), F32)], axis=1)
            pieces[k][...] = value.astype(BF)

        at = 2 * pc
        put(0, MOMENT_DECAY * mi[0] + ff_ref[:, 0:fj])
        put(1, MOMENT_DECAY * mi[1] + ff1_ref[:, 0:fj])
        put(2, MOMENT_DECAY * md[0] + ff_ref[:, fj : 2 * fj])
        put(3, MOMENT_DECAY * md[1] + ff1_ref[:, fj : 2 * fj])
        for b in range(2):
            put(4 + b, MOMENT_DECAY * mq[b] + jnp.concatenate([q_ref[b, t] for t in range(3)], axis=1))
        put(6, MOMENT_DECAY * mp[...] + rest_ref[:, 0:pc])
        put(7, MOMENT_DECAY * mu[...] + rest_ref[:, pc : 2 * pc])
        put(8, MOMENT_DECAY * mo[0] + o_ref[...])
        put(9, MOMENT_DECAY * mo[1] + rest_ref[:, at:])
        if any(w != wide for w in widths):
            box[...] = jnp.zeros(box.shape, BF)

        barrier = pltpu.get_barrier_semaphore()

        def greet(t, carry):
            @pl.when(t != slot)
            def _():
                there = (lax.rem(t, dp_count), lax.div(t, dp_count))
                pl.semaphore_signal(barrier, inc=1, device_id=there, device_id_type=MESH)

            return carry

        lax.fori_loop(0, devices, greet, 0)
        pl.semaphore_wait(barrier, devices - 1)

        mine = [(dp == owners[k][0]) & (fs == owners[k][1]) for k in range(amount)]
        for k in range(amount):
            copy = pltpu.make_async_remote_copy(
                src_ref=pieces[k],
                dst_ref=box.at[slot, :, 0 : widths[k]],
                send_sem=push_send.at[k],
                recv_sem=push_recv,
                device_id=owners[k],
                device_id_type=MESH,
            )

            @pl.when(jnp.logical_not(mine[k]))
            def _():
                copy.start()

            @pl.when(mine[k])
            def _():
                box[slot, :, 0 : widths[k]] = pieces[k][...]

        total = ga[...]
        for n in range(z_bits):
            tsend[n] = total
            hop = net.start(tsend.at[n], tiles.at[n], (flip(dp, y_count << n), fs))
            hop.wait_recv()
            total = total + tiles[n]
        dgain_out[...] = total

        for k in range(amount):

            @pl.when(mine[k])
            def _():
                landed = box.at[0 : devices - 1, :, 0 : widths[k]]
                pltpu.make_async_copy(landed, landed, push_recv).wait()

        which_k = jnp.int32(0)
        for k in range(1, amount):
            which_k = which_k + k * mine[k].astype(jnp.int32)
        for w in classes:
            chosen = None
            for k in range(amount):
                if widths[k] == w:
                    chosen = mine[k] if chosen is None else chosen | mine[k]

            @pl.when(chosen)
            def _():
                def done(block):
                    def give(i, carry):
                        t = block * dp_count + i

                        @pl.when(t != slot)
                        def _():
                            pltpu.make_async_remote_copy(
                                src_ref=box.at[t, :, 0:w],
                                dst_ref=out.at[which_k, :, 0:w],
                                send_sem=give_send,
                                recv_sem=give_recv.at[which_k],
                                device_id=(i, block),
                                device_id_type=MESH,
                            ).start()
                            pltpu.make_async_remote_copy(
                                src_ref=norm,
                                dst_ref=norms.at[which_k],
                                send_sem=norm_send,
                                recv_sem=norm_recv.at[which_k],
                                device_id=(i, block),
                                device_id_type=MESH,
                            ).start()

                        return carry

                    lax.fori_loop(0, dp_count, give, 0)

                newton_schulz(box, x, norm, fs_count, w, dp_count, rw, done)
                out[which_k, :, 0:w] = box[slot, :, 0:w]
                norms[which_k] = norm[...]

        for k in range(amount):
            w = widths[k]

            @pl.when(jnp.logical_not(mine[k]))
            def _():
                landed = out.at[k, :, 0:w]
                pltpu.make_async_copy(landed, landed, give_recv.at[k]).wait()
                pltpu.make_async_copy(norms.at[k], norms.at[k], norm_recv.at[k]).wait()
                pltpu.make_async_copy(pieces[k], pieces[k], push_send.at[k]).wait()

            @pl.when(mine[k])
            def _():
                left = box.at[0 : devices - 1, :, 0:w]
                pltpu.make_async_copy(left, left, give_send).wait()

                def drain(t, carry):
                    pltpu.make_async_copy(norm, norm, norm_send).wait()
                    return carry

                lax.fori_loop(0, devices - 1, drain, 0)

        net.finish()

    outs = [((amount, rw, wide), BF), ((amount, 8, LANES), F32), ((8, width), F32)]
    scratch = [
        ((devices, rw, wide), BF),
        ((width, fs_count * wide), BF),
        ((8, LANES), F32),
        ((z_bits, 8, width), F32),
        ((z_bits, 8, width), F32),
    ] + [((rw, w), BF) for w in widths]
    dma = pltpu.SemaphoreType.DMA
    return pl.pallas_call(
        body,
        out_shape=[jax.ShapeDtypeStruct(s, t) for s, t in outs],
        in_specs=[vmem()] * 12,
        out_specs=[vmem()] * len(outs),
        scratch_shapes=[pltpu.VMEM(s, t) for s, t in scratch]
        + [dma((sems,)), dma((sems,)), dma((amount,)), dma, dma, dma((amount,)), dma, dma((amount,))],
        compiler_params=pltpu.CompilerParams(collective_id=1, has_side_effects=True, vmem_limit_bytes=VMEM_BYTES),
        name="muon",
    )(sum_q, sum_o, sum_ff, sum_ff1, sum_rest, *moments, dgain)


def backward_all(
    y_count, dp_count, fs_count, da, dfs, n2, hid_in, slope_in, wi, wd, mid, gain_rows, qkv, wo_full, wq, cos, sin, triples, n1, att_rel, tokens, group_b, dgain_b,
    sum_ff1, moments,
):
    rows, width = tokens.shape
    total = rows * fs_count
    fj, hd = wi.shape[1], wq.shape[1] // 3
    heads, docs = hd // HEAD, triples.shape[1]
    z_count, rw = dp_count // y_count, width // dp_count
    cb = group_b.shape[1]
    blk, half = query_rows(total), fs_count // 2
    blocks = total // blk
    sems = 96 + 16 * dp_count

    pc = moments[4].shape[1]
    devices = dp_count * fs_count
    widths = [round_up(w) for w in (fj, fj, fj, fj, 3 * hd, 3 * hd, pc, pc, hd, hd)]
    amount, wide = len(widths), max(widths)
    owners = owners_of(amount, dp_count, fs_count)
    classes = sorted(set(widths))

    def body(
        da_ref, dfs, n2_hbm, hid_hbm, slope_hbm, wi_ref, wd_ref, mid_hbm, gain_ref, qkv_hbm, wo_ref, wq_ref, cos_hbm, sin_hbm, triples_ref, n1_hbm, att_hbm, tok, gb, dgain_two, ff1_ref, mq, mo, mi, md, mp, mu,
        grad_in, dgain_out, sum_b, sum_ff, sum_o, sum_q, out, norms,
        n2_ref, mid_ref, qkv_ref, cos_ref, sin_ref, n1_ref, att_ref, da_low, do_out, do_in, da_out, da_in, hid, slope, dpre, work, qs, ks, kt, dk, dv, dm, cols, g_ff, g_at, g_o,
        sbuf, rbuf, xsend, xrecv, acc, yb, zsb, zrb, qsb, qrb, yf, zsf, zrf, yo, zso, zro, qsa, qra, tiles,
        box, x, norm, send_sem, recv_sem, push_send, push_recv, give_send, give_recv, norm_send, norm_recv,
        *rest,
    ):
        ps, pieces = rest[:blocks], rest[blocks:]
        dp, fs = lax.axis_index("dp"), lax.axis_index("fsdp")
        net = Net(send_sem, recv_sem)
        place = (dp, fs, y_count, z_count, fs_count, rw)
        dqkv = qkv_ref
        loads = {}
        for name, src, dst in (
            ("slope", slope_hbm, slope),
            ("n2", n2_hbm, n2_ref),
            ("hid", hid_hbm, hid),
            ("mid", mid_hbm, mid_ref),
            ("qkv", qkv_hbm, qkv_ref),
            ("att", att_hbm, att_ref),
            ("cos", cos_hbm, cos_ref),
            ("sin", sin_hbm, sin_ref),
            ("n1", n1_hbm, n1_ref),
        ):
            loads[name] = net.local(src, dst)
        barrier = pltpu.get_barrier_semaphore()
        slot = fs * dp_count + dp

        def greet(t, carry):
            @pl.when(t != slot)
            def _():
                there = (lax.rem(t, dp_count), lax.div(t, dp_count))
                pl.semaphore_signal(barrier, inc=1, device_id=there, device_id_type=MESH)

            return carry

        lax.fori_loop(0, devices, greet, 0)
        pl.semaphore_wait(barrier, devices - 1)

        mine = [(dp == owners[k][0]) & (fs == owners[k][1]) for k in range(amount)]

        def push(k, value):
            have = value.shape[1]
            if have < widths[k]:
                value = jnp.concatenate([value, jnp.zeros((rw, widths[k] - have), F32)], axis=1)
            pieces[k][...] = value.astype(BF)
            copy = pltpu.make_async_remote_copy(
                src_ref=pieces[k],
                dst_ref=box.at[slot, :, 0 : widths[k]],
                send_sem=push_send.at[k],
                recv_sem=push_recv,
                device_id=owners[k],
                device_id_type=MESH,
            )

            @pl.when(jnp.logical_not(mine[k]))
            def _():
                copy.start()

            @pl.when(mine[k])
            def _():
                box[slot, :, 0 : widths[k]] = pieces[k][...]

        sum_of_b = RowSum(net, place, gb, yb, zsb, zrb, sum_b, qsb, qrb, sum_q.at[1])
        sum_of_b.start()

        def pull(e, out):
            work[:, 0:fj] = dot_nn(dfs[e], wd_ref[...])

            def one(r):
                at = pl.ds(pl.multiple_of(e * rows + r, HEAD), HEAD)
                dpre[at, :] = (work[pl.ds(r, HEAD), 0:fj] * slope[at, :].astype(F32)).astype(BF)

            row_loop(rows, one)
            out[...] = dot_nt(dpre[e * rows : (e + 1) * rows, :], wi_ref[...]).astype(out.dtype)

        def part_into(scatter, e, fill):
            if e % 2:
                fill(e, scatter.sbuf.at[e // 2])
                scatter.send_odd(e // 2)
            else:
                fill(e, scatter.acc.at[e // 2])

        ff_sum = Scatter(net, dp, fs, fs_count, sbuf, rbuf, xsend, xrecv, acc)
        loads["slope"].wait()

        def both_steps(e):
            part_into(ff_sum, e, pull)

        for j in reversed(range(1, half)):
            both_steps(2 * j + 1)
            both_steps(2 * j)
        for j in range(1, half):
            ff_sum.join(j)
        ff_sum.upper()
        both_steps(1)
        both_steps(0)
        sum_of_b.service(1)
        for m in range(2, z_count):
            sum_of_b.service(m)
        ff_sum.join(0)
        loads["hid"].wait()
        loads["n2"].wait()
        g_ff[:, 0:fj] = dot_tn(n2_ref[...], dpre[...]).astype(BF)
        g_ff[:, fj : 2 * fj] = dot_tn(dfs[...].reshape(total, width), hid[...]).astype(BF)
        sum_of_b.service(0)
        sum_of_ff = RowSum(net, place, g_ff, yf, zsf, zrf, sum_ff)
        sum_of_ff.start()

        loads["qkv"].wait()
        lane_first, lane_end, lane = doc_bounds(triples_ref, docs)
        for r in range(0, total, blk):
            at = slice(r, r + blk)
            q = qkv_ref[at, 0:hd].astype(F32)
            k = qkv_ref[at, hd : 2 * hd].astype(F32)
            row = lax.broadcasted_iota(jnp.int32, (blk, LANES), 0) + r
            inside = (row >= 3 * lane_first) & (row < 3 * lane_end)
            fk = jnp.where(inside, 1.0, 0.0)
            fq = jnp.where(inside | (lane >= docs), 0.0, MASKED)
            head_inputs(qs, ks, at, q, k, fq, fk, heads)
            kt[:, at] = k.T.astype(BF)
            dk[at, :] = jnp.zeros((blk, LANES), F32)
            dv[at, :] = jnp.zeros((blk, LANES), F32)

        def recompute(n):
            r = n * blk
            for h in range(heads):
                e, inv = softmax_block(ks, qs, h, r, r + blk)
                ps[n][h] = (e * inv).astype(BF)

        for n in range(blocks // 2):
            recompute(n)

        push(1, MOMENT_DECAY * mi[1] + ff1_ref[:, 0:fj])
        push(3, MOMENT_DECAY * md[1] + ff1_ref[:, fj : 2 * fj])

        ff_sum.finish()
        loads["mid"].wait()
        for r in range(0, rows, LANES):
            at = slice(r, r + LANES)
            dx, dg = layer_norm_back(mid_ref[at, :], gain_ref[1:2, :], acc[0, at, :])
            dx = dx + da_ref[at, :]
            dm[at, :] = dx
            da_low[at, :] = dx.astype(BF)
            dg = jnp.sum(dg, axis=0, keepdims=True)
            gain_two = dg if r == 0 else gain_two + dg
        got = dot_nt(da_low[...], wo_ref[...]).astype(BF)
        for e in range(fs_count):
            do_out[e] = got[:, e * hd : (e + 1) * hd]
            da_out[e] = da_low[:, e * hd : (e + 1) * hd]

        def exchange(blocks_of, landed):
            found = []
            for e in range(1, fs_count):
                found.append(net.start(blocks_of.at[flip(fs, e)], landed.at[e], (dp, flip(fs, e))))
            landed[0] = blocks_of[fs]
            return found

        do_f = exchange(do_out, do_in)
        da_f = exchange(da_out, da_in)
        for n in range(blocks // 2, blocks):
            recompute(n)
        for m in range(1, z_count):
            sum_of_ff.service(m)
        sum_of_ff.service(0)

        place_of = lax.broadcasted_iota(jnp.int32, (blk, LANES), 1) // HEAD
        for r in range(0, total, blk):
            at = slice(r, r + blk)
            q = widen(qkv_ref[at, 0:hd].astype(F32))
            for h in range(heads):
                qs[h, at, :] = jnp.where(place_of == h, q, 0.0).astype(BF)
        lane_head = lax.broadcasted_iota(jnp.int32, (rows, LANES), 1) // HEAD
        for e in range(fs_count):
            if e:
                do_f[e - 1].wait_recv()
            base = pl.multiple_of(flip(fs, e) * rows, 16)
            do = widen(do_in[e].astype(F32))
            for h in range(heads):
                ks[h, pl.ds(base, rows), :] = jnp.where(lane_head == h, do, 0.0).astype(BF)
        for e in range(fs_count):
            if e:
                da_f[e - 1].wait_recv()
            cols[pl.ds(pl.multiple_of(flip(fs, e) * rows, 16), rows), :] = da_in[e]

        loads["att"].wait()
        g_out = dot_tn(att_ref[...], cols[...]).astype(BF)
        for e in range(fs_count):
            base = pl.multiple_of(flip(fs, e) * hd, 16)
            g_o[pl.ds(base, hd), :] = g_out[e * hd : (e + 1) * hd, :]
        sum_of_o = RowSum(net, place, g_o, yo, zso, zro, sum_o)
        sum_of_o.start()
        sum_of_b.finish()
        push(5, MOMENT_DECAY * mq[1] + jnp.concatenate([sum_q[1, t] for t in range(3)], axis=1))
        push(6, MOMENT_DECAY * mp[...] + sum_b[:, 0:pc])
        push(7, MOMENT_DECAY * mu[...] + sum_b[:, pc : 2 * pc])
        push(9, MOMENT_DECAY * mo[1] + sum_b[:, 2 * pc :])

        loads["cos"].wait()
        loads["sin"].wait()
        for n in range(blocks):
            r, stop = n * blk, (n + 1) * blk
            at = slice(r, stop)
            found = []
            add_k = add_v = None
            for h in range(heads):
                p = ps[n][h]
                v = widen(qkv_ref[0:stop, 2 * hd : 3 * hd])
                grad = dot_nt(v, ks[h, at, :])
                wide = p.astype(F32)
                middle = jnp.sum(wide * grad, axis=0, keepdims=True)
                dr = (wide * (grad - middle) * 0.125).astype(BF)
                part_v = dot_nn(p, ks[h, at, :])
                part_k = dot_nn(dr, qs[h, at, :])
                add_v = part_v if add_v is None else add_v + part_v
                add_k = part_k if add_k is None else add_k + part_k
                found.append(dot_nn(kt[h * HEAD : (h + 1) * HEAD, 0:stop], dr))
            dk[0:stop, :] += add_k
            dv[0:stop, :] += add_v
            dq = jnp.concatenate(found, axis=0).T
            dqkv[at, 0:hd] = (dq * cos_ref[at, :] - partner(dq) * sin_ref[at, :]).astype(BF)
            if n == blocks // 2:
                for m in range(1, z_count):
                    sum_of_o.service(m)
                sum_of_o.service(0)
        for r in range(0, total, blk):
            at = slice(r, r + blk)
            grad = dk[at, 0:hd]
            dqkv[at, hd : 2 * hd] = (grad * cos_ref[at, :] - partner(grad) * sin_ref[at, :]).astype(BF)
            dqkv[at, 2 * hd : 3 * hd] = dv[at, 0:hd].astype(BF)
        loads["n1"].wait()
        g_at[...] = dot_tn(n1_ref[...], dqkv[...]).astype(BF)
        sum_of_at = HeadSum(net, place, g_at, qsa, qra, sum_q.at[0])
        sum_of_at.start()

        ff_sum.sent()
        at_sum = Scatter(net, dp, fs, fs_count, sbuf, rbuf, xsend, xrecv, acc)
        tiles[0] = jnp.zeros((8, width), F32)

        def push_out(e, out):
            base = pl.multiple_of(flip(fs, e) * rows, 16)
            part = dot_nt(dqkv[pl.ds(base, rows), :], wq_ref[...])
            out[...] = part.astype(out.dtype)
            work[:, 0:width] = part
            total_of = jnp.zeros((8, width), F32)
            for r in range(0, rows, HEAD):
                grown = work[r : r + HEAD, 0:width] * n1_ref[pl.ds(base + r, HEAD), :].astype(F32)
                total_of = total_of + jnp.sum(grown.reshape(HEAD // 8, 8, width), axis=0)
            tiles[0] = tiles[0] + total_of

        for e in reversed(range(2, fs_count)):
            part_into(at_sum, e, push_out)
        part_into(at_sum, 1, push_out)
        for j in range(1, half):
            at_sum.join(j)
        at_sum.upper()
        part_into(at_sum, 0, push_out)
        gain_one = jnp.sum(tiles[0], axis=0, keepdims=True) / gain_ref[0:1, :]
        which = lax.broadcasted_iota(jnp.int32, (8, width), 0)
        both = jnp.where(which == 0, gain_one, jnp.where(which == 1, gain_two, 0.0))
        both = jnp.where(which == 2, dgain_two[0:1, :], jnp.where(which == 3, dgain_two[1:2, :], both))
        hops = [(dp, flip(fs, 1 << n)) for n in range(fs_count.bit_length() - 1)]
        hops += [(flip(dp, 1 << n), fs) for n in range(dp_count.bit_length() - 1)]

        def hop_out(n, value):
            tiles[1 + n] = value
            return net.start(tiles.at[1 + n], tiles.at[1 + len(hops) + n], hops[n])

        hop = hop_out(0, both)
        sum_of_ff.finish()
        push(0, MOMENT_DECAY * mi[0] + sum_ff[:, 0:fj])
        push(2, MOMENT_DECAY * md[0] + sum_ff[:, fj : 2 * fj])
        sum_of_o.finish()
        push(8, MOMENT_DECAY * mo[0] + sum_o[...])
        at_sum.join(0)
        sum_of_at.finish()
        push(4, MOMENT_DECAY * mq[0] + jnp.concatenate([sum_q[0, t] for t in range(3)], axis=1))
        hop.wait_recv()
        both = both + tiles[len(hops) + 1]
        hop = hop_out(1, both)
        at_sum.finish()
        for n in range(2, len(hops) - 1):
            hop.wait_recv()
            both = both + tiles[len(hops) + n]
            hop = hop_out(n, both)
        for r in range(0, rows, LANES):
            at = slice(r, r + LANES)
            dx, _ = layer_norm_back(tok[at, :].astype(F32), gain_ref[0:1, :], acc[0, at, :])
            grad_in[at, :] = dx + dm[at, :]

        for k in range(amount):

            @pl.when(mine[k])
            def _():
                landed = box.at[0 : devices - 1, :, 0 : widths[k]]
                pltpu.make_async_copy(landed, landed, push_recv).wait()

        which_k = jnp.int32(0)
        for k in range(1, amount):
            which_k = which_k + k * mine[k].astype(jnp.int32)
        for w in classes:
            chosen = None
            for k in range(amount):
                if widths[k] == w:
                    chosen = mine[k] if chosen is None else chosen | mine[k]

            @pl.when(chosen)
            def _():
                def done(block):
                    def give(i, carry):
                        t = block * dp_count + i

                        @pl.when(t != slot)
                        def _():
                            pltpu.make_async_remote_copy(
                                src_ref=box.at[t, :, 0:w],
                                dst_ref=out.at[which_k, :, 0:w],
                                send_sem=give_send,
                                recv_sem=give_recv.at[which_k],
                                device_id=(i, block),
                                device_id_type=MESH,
                            ).start()
                            pltpu.make_async_remote_copy(
                                src_ref=norm,
                                dst_ref=norms.at[which_k],
                                send_sem=norm_send,
                                recv_sem=norm_recv.at[which_k],
                                device_id=(i, block),
                                device_id_type=MESH,
                            ).start()

                        return carry

                    lax.fori_loop(0, dp_count, give, 0)

                newton_schulz(box, x, norm, fs_count, w, dp_count, rw, done)
                out[which_k, :, 0:w] = box[slot, :, 0:w]
                norms[which_k] = norm[...]

        last = len(hops) - 1
        hop.wait_recv()
        both = both + tiles[len(hops) + last]
        hop = hop_out(last, both)
        hop.wait_recv()
        dgain_out[...] = both + tiles[1 + len(hops) + last]

        for k in range(amount):
            w = widths[k]

            @pl.when(jnp.logical_not(mine[k]))
            def _():
                landed = out.at[k, :, 0:w]
                pltpu.make_async_copy(landed, landed, give_recv.at[k]).wait()
                pltpu.make_async_copy(norms.at[k], norms.at[k], norm_recv.at[k]).wait()
                pltpu.make_async_copy(pieces[k], pieces[k], push_send.at[k]).wait()

            @pl.when(mine[k])
            def _():
                left = box.at[0 : devices - 1, :, 0:w]
                pltpu.make_async_copy(left, left, give_send).wait()

                def drain(t, carry):
                    pltpu.make_async_copy(norm, norm, norm_send).wait()
                    return carry

                lax.fori_loop(0, devices - 1, drain, 0)

        net.finish()

    outs = [
        ((rows, width), F32),
        ((8, width), F32),
        ((rw, cb - 3 * hd), F32),
        ((rw, 2 * fj), F32),
        ((rw, hd), F32),
        ((2, 3, rw, hd), F32),
        ((amount, rw, wide), BF),
        ((amount, 8, LANES), F32),
    ]
    span = max(width, fj)
    zy = (y_count - 1, z_count, rw)
    scratch = [
        ((total, width), BF),
        ((rows, width), F32),
        ((total, 3 * hd), BF),
        ((total, hd), F32),
        ((total, hd), F32),
        ((total, width), BF),
        ((total, width), BF),
        ((rows, width), BF),
        ((fs_count, rows, hd), BF),
        ((fs_count, rows, hd), BF),
        ((fs_count, rows, hd), BF),
        ((fs_count, rows, hd), BF),
        ((total, fj), BF),
        ((total, fj), BF),
        ((total, fj), BF),
        ((rows, span), F32),
        ((heads, total, LANES), BF),
        ((heads, total, LANES), BF),
        ((hd, total), BF),
        ((total, LANES), F32),
        ((total, LANES), F32),
        ((rows, width), F32),
        ((total, hd), BF),
        ((width, 2 * fj), BF),
        ((width, 3 * hd), BF),
        ((width, hd), BF),
        ((half, rows, width), BF),
        ((half, rows, width), BF),
        ((half - 1, rows, width), BF),
        ((half - 1, rows, width), BF),
        ((half, rows, width), F32),
        (zy + (cb,), BF),
        ((z_count - 1, rw, cb - 3 * hd), BF),
        ((z_count - 1, rw, cb - 3 * hd), BF),
        ((z_count, 3, rw, hd), BF),
        ((z_count, 3, rw, hd), BF),
        (zy + (2 * fj,), BF),
        ((z_count - 1, rw, 2 * fj), BF),
        ((z_count - 1, rw, 2 * fj), BF),
        (zy + (hd,), BF),
        ((z_count - 1, rw, hd), BF),
        ((z_count - 1, rw, hd), BF),
        ((dp_count, 3, rw, hd), BF),
        ((dp_count, 3, rw, hd), BF),
        ((2 * (fs_count.bit_length() + dp_count.bit_length() - 2) + 1, 8, width), F32),
        ((devices, rw, wide), BF),
        ((width, fs_count * wide), BF),
        ((8, LANES), F32),
    ]
    tail = [pltpu.VMEM((heads, (n + 1) * blk, blk), BF) for n in range(blocks)]
    tail += [pltpu.VMEM((rw, w), BF) for w in widths]
    dma = pltpu.SemaphoreType.DMA
    tail = [dma((sems,)), dma((sems,)), dma((amount,)), dma, dma, dma((amount,)), dma, dma((amount,))] + tail
    arrays = (da, dfs, n2, hid_in, slope_in, wi, wd, mid, gain_rows, qkv, wo_full, wq, cos, sin, triples, n1, att_rel, tokens, group_b, dgain_b, sum_ff1, *moments)
    return pl.pallas_call(
        body,
        out_shape=[jax.ShapeDtypeStruct(s, t) for s, t in outs],
        in_specs=[hbm() if n in (2, 3, 4, 7, 9, 12, 13, 15, 16) else smem() if n == 14 else vmem() for n in range(27)],
        out_specs=[vmem()] * len(outs),
        scratch_shapes=[pltpu.VMEM(s, t) for s, t in scratch] + tail,
        compiler_params=pltpu.CompilerParams(collective_id=5, has_side_effects=True, vmem_limit_bytes=VMEM_BYTES),
        cost_estimate=cost(4e10, 3e7),
        name="backward_all",
    )(*arrays)


def update(dp_arr, sums, results, norms, roots, dgain, moments, weights, m_gains_t, gains_t, layer_out, grad_in):
    sum_q, sum_o, sum_ff, sum_ff1, sum_rest = sums
    rw, hd = sum_o.shape
    fj = sum_ff.shape[1] // 2
    pc = moments[4].shape[1]
    width = dgain.shape[1]

    def body(me_ref, q_ref, o_ref, ff_ref, ff1_ref, rest_ref, res, norms_ref, roots_ref, dg, *refs):
        m_in, w_in, (mg, g, act, grad), refs = refs[:6], refs[6:12], refs[12:16], refs[16:]
        m_out, w_out, (mg_out, g_out, act_out, grad_out, rms), turned = refs[:6], refs[6:12], refs[12:17], refs[17]
        act_out[...] = act[...]
        grad_out[...] = grad[...]
        at = 2 * pc
        grads = [
            [jnp.concatenate([q_ref[b, t] for t in range(3)], axis=1) for b in range(2)],
            [o_ref[...], rest_ref[:, at:]],
            [ff_ref[:, 0:fj], ff1_ref[:, 0:fj]],
            [ff_ref[:, fj : 2 * fj], ff1_ref[:, fj : 2 * fj]],
            [rest_ref[:, 0:pc]],
            [rest_ref[:, pc : 2 * pc]],
        ]
        places = [(4, 5), (8, 9), (0, 1), (2, 3), (6,), (7,)]
        for kind in range(6):
            for b in range(len(grads[kind])):
                here = (b,) if kind < 4 else (slice(None),)
                have = m_in[kind].shape[-1]
                m_out[kind][here] = MOMENT_DECAY * m_in[kind][here] + grads[kind][b]
                turn = res[places[kind][b], :, 0:have].astype(F32)
                w_out[kind][here] = w_in[kind][here] - STEP_SCALES[kind] * turn
        turned[...] = jnp.concatenate([dg[...], jnp.zeros((LANES - 8, width), F32)], axis=0).T
        mine = turned[pl.ds(pl.multiple_of(me_ref[0] * rw, 16), rw), :].T
        fresh = GAIN_DECAY * mg[...] + mine[0:4, :]
        mg_out[...] = fresh
        g_out[...] = g[...] - GAIN_RATE * fresh
        places = (4, 5, 8, 9, 0, 1, 2, 3, 6, 7)
        lengths = jnp.concatenate([norms_ref[p, 0:1, :] for p in places] + [norms_ref[0, 0:6, :]], axis=0)
        rms[...] = lengths / roots_ref[...]

    outs = [(a.shape, a.dtype) for a in (*moments, *weights, m_gains_t, gains_t, layer_out, grad_in)] + [((16, LANES), F32)]
    return local_kernel(
        body,
        "update",
        outs,
        [((width, LANES), F32)],
        dp_arr,
        sum_q,
        sum_o,
        sum_ff,
        sum_ff1,
        sum_rest,
        results,
        norms,
        roots,
        dgain,
        *moments,
        *weights,
        m_gains_t,
        gains_t,
        layer_out,
        grad_in,
    )


def rope_tables(total, hd):
    half = HEAD // 2
    frequency = (np.float32(10000.0) ** (-np.arange(half, dtype=np.float32) / np.float32(half))).astype(np.float32)
    angle = (np.arange(total, dtype=np.float32)[:, None] * frequency[None, :]).astype(np.float32)
    cos, sin = np.cos(angle), np.sin(angle)
    cos = np.tile(np.concatenate([cos, cos], axis=1), (1, hd // HEAD))
    sin = np.tile(np.concatenate([-sin, sin], axis=1), (1, hd // HEAD))
    return jnp.asarray(cos, F32), jnp.asarray(sin, F32)


def on_device(
    y_count,
    tokens,
    cotangent,
    doc_triples,
    w_qkv,
    w_out,
    w_in,
    w_down,
    w_pool,
    w_up,
    gains,
    m_qkv,
    m_out,
    m_in,
    m_down,
    m_pool,
    m_up,
    m_gains,
):
    rows, width = tokens.shape
    fs_count, dp_count = lax.axis_size("fsdp"), lax.axis_size("dp")
    dp_arr = lax.axis_index("dp").astype(jnp.int32).reshape(1)
    total = rows * fs_count
    hd = width // fs_count

    cos0, sin0 = rope_tables(total, hd)

    old_weights = (w_qkv, w_out, w_in, w_down, w_pool, w_up)
    if total <= 2048:
        (
            n1, qkv, att_rel, n2, hid, slope, wo_full, mid, wqkv0, wi0, wd0, gain_rows, layer_out, da, dfs, group_b, sum_ff1, dgain_b
        ) = forward_all(
            y_count, dp_count, fs_count, tokens, cotangent, doc_triples, old_weights, gains.T, cos0, sin0
        )
    else:
        cos1, sin1 = cos0[: total // 3], sin0[: total // 3]
        (
            n1, qkv, att_rel, wo_full, n2, hid, slope, mid, after, z_blocks, s0, wqkv0, wi0, wd0, wp, wqkv1, wu, c_rel, gain_rows
        ) = forward_one(
            y_count, dp_count, fs_count, tokens, cotangent, doc_triples, old_weights, gains.T, cos0, sin0
        )
        layer_out, da, dfs, group_b, sum_ff1, dgain_b = middle(
            y_count, dp_count, fs_count, s0, after, z_blocks, cotangent, c_rel, wqkv1, wu, old_weights[1:4], wp, gain_rows,
            cos1, sin1, doc_triples,
        )
    moments = (m_qkv, m_out, m_in, m_down, m_pool, m_up)
    kept = (da, dfs, n2, hid, slope, wi0, wd0, mid, gain_rows, qkv, wo_full, wqkv0, cos0, sin0, doc_triples, n1, att_rel, tokens)
    if total <= 2048:
        grad_in, dgain, sum_rest, sum_ff, sum_o, sum_q, results, norms = backward_all(
            y_count, dp_count, fs_count, *kept, group_b, dgain_b, sum_ff1, moments
        )
        sums = (sum_q, sum_o, sum_ff, sum_ff1, sum_rest)
    else:
        grad_in, dgain, sum_rest, sum_ff, sum_o, sum_q = backward_one(
            y_count, dp_count, fs_count, *kept, group_b, dgain_b
        )
        sums = (sum_q, sum_o, sum_ff, sum_ff1, sum_rest)
        results, norms, dgain = muon(y_count, dp_count, fs_count, sums, moments, dgain)

    all_tokens = float(total * dp_count)
    entries = [m.size // (2 if m.ndim == 3 else 1) for m in moments for _ in range(2 if m.ndim == 3 else 1)]
    roots = np.ones((16, LANES), np.float64)
    roots[:10] = np.array([float(n * fs_count * dp_count) * all_tokens for n in entries])[:, None] ** 0.5
    *fresh, gain_moments, new_gains, layer_out, grad_in, rms = update(
        dp_arr, sums, results, norms, jnp.asarray(roots, F32), dgain, moments, old_weights, m_gains.T, gains.T, layer_out, grad_in
    )
    return (layer_out, grad_in, *fresh, gain_moments.T, new_gains.T, rms[:10, 0])


def solution(mesh):
    by_row, by_dp = P(("dp", "fsdp"), None), P("dp", None)
    stacked, flat = P(None, "dp", "fsdp"), P("dp", "fsdp")
    matrices = (stacked,) * 4 + (flat,) * 2
    y_count = max(1, mesh.shape["fsdp"] // 2)
    return jax.shard_map(
        functools.partial(on_device, y_count),
        mesh=mesh,
        in_specs=(by_row, by_row, by_dp, *matrices, by_dp, *matrices, by_dp),
        out_specs=(by_row, by_row, *matrices, *matrices, by_dp, by_dp, P()),
        check_vma=False,
    )
```

```python
import functools

import jax
import jax.numpy as jnp
import numpy as np
from jax import lax
from jax.experimental import pallas as pl
from jax.experimental.pallas import tpu as pltpu
from jax.sharding import PartitionSpec as P

HEAD = 64
NS_STEPS = 5
NS_COEFS = (3.4445, -4.775, 2.0315)
STEP_SCALES = (0.8660254, 1.4142136, 1.0, 0.5, 0.5, 0.8660254)
MOMENT_DECAY = 0.95
GAIN_DECAY = 0.9
GAIN_RATE = 0.001
LN_EPS = 1e-05
NORM_EPS = 1e-07
MASKED = -1e30
HALO = 16
QB = 256
LANES = 128
VMEM_BYTES = 62 << 20
BF = jnp.bfloat16
F32 = jnp.float32
MESH = pl.DeviceIdType.MESH


def dot_nn(left, right):
    return lax.dot_general(left, right, (((1,), (0,)), ((), ())), preferred_element_type=F32)


def dot_nt(left, right):
    return lax.dot_general(left, right, (((1,), (1,)), ((), ())), preferred_element_type=F32)


def dot_tn(left, right):
    return lax.dot_general(left, right, (((0,), (0,)), ((), ())), preferred_element_type=F32)


def layer_norm(values, gain):
    mean = jnp.mean(values, axis=-1, keepdims=True)
    centred = values - mean
    spread = jnp.mean(centred * centred, axis=-1, keepdims=True)
    return centred * lax.rsqrt(spread + LN_EPS) * gain


def layer_norm_back(values, gain, grad):
    mean = jnp.mean(values, axis=-1, keepdims=True)
    centred = values - mean
    spread = jnp.mean(centred * centred, axis=-1, keepdims=True)
    scale = lax.rsqrt(spread + LN_EPS)
    unit = centred * scale
    scaled = grad * gain
    part = jnp.mean(scaled, axis=-1, keepdims=True)
    along = jnp.mean(scaled * unit, axis=-1, keepdims=True)
    return scale * (scaled - part - unit * along), grad * unit


def gelu(values):
    return 0.5 * values * (1.0 + jnp.tanh(0.7978845608028654 * (values + 0.044715 * values * values * values)))


def gelu_both(values):
    square = values * values
    turn = jnp.tanh(0.7978845608028654 * (values + 0.044715 * values * square))
    slope = 0.7978845608028654 * (1.0 + 3.0 * 0.044715 * square)
    half = 0.5 * (1.0 + turn)
    return values * half, half + 0.5 * values * (1.0 - turn * turn) * slope


def partner(values):
    width = values.shape[1]
    if width == LANES:
        lane = lax.broadcasted_iota(jnp.int32, values.shape, 1)
        ahead = pltpu.roll(values, LANES - HEAD // 2, 1)
        behind = pltpu.roll(values, HEAD // 2, 1)
        return jnp.where(lane % HEAD < HEAD // 2, ahead, behind)
    parts = []
    for at in range(0, width, HEAD):
        parts += [values[:, at + HEAD // 2 : at + HEAD], values[:, at : at + HEAD // 2]]
    return jnp.concatenate(parts, axis=1)


def widen(values):
    rows, width = values.shape
    if width >= LANES:
        return values
    return jnp.concatenate([values, jnp.zeros((rows, LANES - width), values.dtype)], axis=1)


def params():
    return pltpu.CompilerParams(vmem_limit_bytes=VMEM_BYTES)


def smem():
    return pl.BlockSpec(memory_space=pltpu.SMEM)


def vmem():
    return pl.BlockSpec(memory_space=pltpu.VMEM)


def hbm():
    return pl.BlockSpec(memory_space=pl.ANY)


def cost(flops, moved):
    return pl.CostEstimate(flops=int(flops), bytes_accessed=int(moved), transcendentals=0)


def local_kernel(body, name, outs, scratch, me, *arrays, flops=0):
    moved = sum(a.size * a.dtype.itemsize for a in arrays)
    moved += sum(int(np.prod(s)) * jnp.dtype(t).itemsize for s, t in outs)
    return pl.pallas_call(
        body,
        out_shape=[jax.ShapeDtypeStruct(s, t) for s, t in outs],
        in_specs=[smem()] + [vmem()] * len(arrays),
        out_specs=[vmem()] * len(outs),
        scratch_shapes=[pltpu.VMEM(s, t) for s, t in scratch],
        compiler_params=params(),
        cost_estimate=cost(flops, moved),
        name=name,
    )(me, *arrays)


def at_rows(me, step, rows):
    return pl.multiple_of((me ^ step) * rows, 16)


def head_inputs(qs, ks, rows, q, k, fq, fk, heads):
    lane = lax.broadcasted_iota(jnp.int32, (q.shape[0], LANES), 1)
    q, k = widen(q), widen(k)
    for h in range(heads):
        mine = lane // HEAD == h
        qs[h, rows, :] = jnp.where(mine, q * 0.125, fq).astype(BF)
        ks[h, rows, :] = jnp.where(mine, k, fk).astype(BF)


def scores_t(ks, qs, h, start, stop):
    top = dot_nt(ks[h, 0:stop, :], qs[h, start:stop, :])
    key = lax.broadcasted_iota(jnp.int32, (stop - start, stop - start), 0)
    query = lax.broadcasted_iota(jnp.int32, (stop - start, stop - start), 1)
    last = jnp.where(key <= query, top[start:, :], MASKED)
    if start == 0:
        return last
    return jnp.concatenate([top[:start, :], last], axis=0)


def spread_write(hold, values):
    for c in range(hold.shape[0]):
        hold[c] = values[:, c * LANES : (c + 1) * LANES]


def spread_read(hold):
    return jnp.concatenate([hold[c] for c in range(hold.shape[0])], axis=1)


def strided_read(hold, start, amount):
    return jnp.concatenate([hold[c, pl.ds(start, amount, stride=3), :] for c in range(hold.shape[0])], axis=1)


def strided_write(hold, start, amount, values):
    for c in range(hold.shape[0]):
        hold[c, pl.ds(start, amount, stride=3), :] = values[:, c * LANES : (c + 1) * LANES]


def row_loop(amount, run):
    def step(i, carry):
        run(pl.multiple_of(i * HEAD, HEAD))
        return carry

    lax.fori_loop(0, amount // HEAD, step, 0)


def flip(value, step):
    bit = 1
    while bit <= step:
        if step & bit:
            value = value + bit - 2 * bit * lax.rem(lax.div(value, bit), 2)
        bit *= 2
    return value


class Net:
    def __init__(self, send, recv):
        self.send, self.recv, self.used, self.open = send, recv, 0, []

    def make(self, src, dst, device):
        at = self.used
        self.used += 1
        return pltpu.make_async_remote_copy(
            src_ref=src,
            dst_ref=dst,
            send_sem=self.send.at[at],
            recv_sem=self.recv.at[at],
            device_id=device,
            device_id_type=MESH,
        )

    def start(self, src, dst, device):
        copy = self.make(src, dst, device)
        copy.start()
        self.open.append(copy)
        return copy

    def local(self, src, dst):
        at = self.used
        self.used += 1
        copy = pltpu.make_async_copy(src, dst, self.send.at[at])
        copy.start()
        return copy

    def finish(self):
        for copy in self.open:
            copy.wait_send()


class Flight:
    def __init__(self, net, dp, fs, fs_count, pieces, src):
        self.net, self.dp, self.fs, self.pieces = net, dp, fs, pieces
        self.top, self.copies, self.waited = fs_count // 2, {}, set()
        bit = self.top
        while bit:
            self.copies[bit] = net.start(src, pieces.at[bit], (dp, flip(fs, bit)))
            bit //= 2

    def ready(self, step):
        if step and step not in self.waited:
            self.waited.add(step)
            self.copies[step].wait_recv()

    def relay(self):
        known, bit = [self.top], self.top // 2
        while bit:
            fresh = []
            for step in known:
                self.ready(step)
                there = (self.dp, flip(self.fs, bit))
                self.copies[step + bit] = self.net.start(self.pieces.at[step], self.pieces.at[step + bit], there)
                fresh.append(step + bit)
            known = known + [bit] + fresh
            bit //= 2

    def all_ready(self):
        for step in sorted(self.copies):
            self.ready(step)


def doc_bounds(triples, docs):
    lane = lax.broadcasted_iota(jnp.int32, (1, LANES), 1)
    lane = jnp.where(lane >= HEAD, lane - HEAD, lane)
    first = jnp.full((1, LANES), -1, jnp.int32)
    end = jnp.full((1, LANES), -1, jnp.int32)
    at = jnp.int32(0)
    for j in range(docs):
        here = lane == j
        first = jnp.where(here, at, first)
        at = at + triples[0, j]
        end = jnp.where(here, at, end)
    return first, end, lane


def softmax_block(ks, qs, h, r, stop):
    s = scores_t(ks, qs, h, r, stop)
    e = jnp.exp(s - jnp.max(s, axis=0, keepdims=True))
    return e, 1.0 / jnp.sum(e, axis=0, keepdims=True)


def forward_one(y_count, dp_count, fs_count, tokens, cot, triples, weights, gains_t, cos, sin):
    rows, width = tokens.shape
    total, short = rows * fs_count, rows // 3
    long_rows = rows + HALO
    wqkv, wout, win, wdown, wpool, wup = weights
    rw = wqkv.shape[1]
    hd, fj, pc = wout.shape[2], win.shape[2], wpool.shape[1]
    heads = hd // HEAD
    docs = triples.shape[1]
    z_count = dp_count // y_count
    blk = QB
    sems = 96 + 16 * dp_count

    def body(
        tok, cot_ref, triples_ref, q_in, o_in, i_in, d_in, p_in, u_in, g_in, cos_ref, sin_ref,
        n1_hbm, qkv_hbm, att_hbm, wo_full, n2_hbm, hid_hbm, slope_hbm, mid, after, z_out, s0_out, wq_out, wi, wd, wp, wq1_out, wu, c_rel, gain_out,
        n1, qkv, att_rel, n2, hid0, slope0, toks, c_own, st_q, wq0, wq1, gall, wo, wo_at, att, qs, ks, vt, turned, hold, work, low, part, m_tail, part_tail,
        sbuf, rbuf, xsend, xrecv, acc, thin, send_sem, recv_sem,
    ):
        dp, fs = lax.axis_index("dp"), lax.axis_index("fsdp")
        net = Net(send_sem, recv_sem)

        def own(buf):
            return buf.at[pl.ds(pl.multiple_of(dp * rw, 16), rw), :]

        def of(buf, step):
            return buf.at[pl.ds(pl.multiple_of(flip(dp, step) * rw, 16), rw), :]

        for b in range(2):
            for t in range(3):
                st_q[b, t] = q_in[b, :, t * hd : (t + 1) * hd].astype(BF)
        here = pl.ds(pl.multiple_of(dp * rw, 16), rw)
        wide_gain = jnp.concatenate([g_in[...], jnp.zeros((LANES - 4, rw), F32)], axis=0).T
        gall[here, :] = wide_gain.astype(BF)
        wo[0, here, :] = o_in[0].astype(BF)
        wi[here, :] = i_in[0].astype(BF)
        wd[here, :] = d_in[0].astype(BF)
        wp[0, here, :] = p_in[...].astype(BF)
        wu[here, :] = u_in[...].astype(BF)

        barrier = pltpu.get_barrier_semaphore()
        for m in range(z_count):
            for e in range(fs_count):
                if m or e:
                    there = (flip(dp, m * y_count), flip(fs, e))
                    pl.semaphore_signal(barrier, inc=1, device_id=there, device_id_type=MESH)
        for j in range(1, y_count):
            pl.semaphore_signal(barrier, inc=1, device_id=(flip(dp, j), fs), device_id_type=MESH)
        pl.semaphore_wait(barrier, z_count * fs_count - 1 + y_count - 1)

        def along_z(bufs):
            found = [[] for _ in range(z_count)]
            for m in range(1, z_count):
                for buf in bufs:
                    found[m].append(net.start(own(buf), own(buf), (flip(dp, m * y_count), fs)))
            return found

        def along_y(bufs, m):
            return [
                net.start(of(buf, m * y_count), of(buf, m * y_count), (flip(dp, j), fs))
                for j in range(1, y_count)
                for buf in bufs
            ]

        def wait_all(copies):
            for copy in copies:
                copy.wait_recv()

        def heads_along_z(b, wq):
            found = []
            for m in range(z_count):
                line = []
                for t in range(3):
                    place = 3 * fs + t
                    kind, to = lax.div(place, fs_count), lax.rem(place, fs_count)
                    copy = net.make(st_q.at[b, t], wq.at[kind, here, :], (flip(dp, m * y_count), to))
                    if m == 0:

                        @pl.when(to != fs)
                        def _():
                            copy.start()

                        @pl.when(to == fs)
                        def _():
                            wq[kind, here, :] = st_q[b, t]

                        line.append((copy, to != fs))
                    else:
                        copy.start()
                        net.open.append(copy)
                        line.append((copy, None))
                found.append(line)
            return found

        def heads_along_y(wq, line, m):
            for copy, when in line:
                if when is None:
                    copy.wait_recv()
                else:

                    @pl.when(when)
                    def _():
                        copy.wait_recv()
                        copy.wait_send()

            at = pl.ds(pl.multiple_of(flip(dp, m * y_count) * rw, 16), rw)
            return [
                net.start(wq.at[:, at, :], wq.at[:, at, :], (flip(dp, j), fs)) for j in range(1, y_count)
            ]


        def spread(pieces, src):
            return Flight(net, dp, fs, fs_count, pieces, src)

        heads0 = heads_along_z(0, wq0)
        gz = along_z([gall])
        y0 = along_y([gall], 0)
        thirds = [slice(n * short, (n + 1) * short) for n in range(3)]
        tks = [spread(toks.at[:, third, :], tok.at[third, :]) for third in thirds]
        toks[0] = tok[...]
        zs = {}
        zs["wo"] = along_z([wo.at[0]])
        zs["wi"] = along_z([wi])
        ys = {"wo": along_y([wo.at[0]], 0), "wi": along_y([wi], 0)}
        spread_write(thin.at[:, 0:rows, :], cot_ref[...].astype(F32))
        lifted = jnp.concatenate([strided_read(thin, n, short) for n in range(3)], axis=1).astype(BF)
        for e in range(fs_count):
            c_own[e] = lifted[:, e * pc : (e + 1) * pc]
        c_rel[0] = c_own[fs]
        c_f = [
            net.start(c_own.at[flip(fs, e)], c_rel.at[e], (dp, flip(fs, e))) for e in range(1, fs_count)
        ]
        lane_first, lane_end, lane = doc_bounds(triples_ref, docs)
        for m in range(z_count):
            y0 += heads_along_y(wq0, heads0[m], m)
            if m:
                wait_all(gz[m])
                y0 += along_y([gall], m)
        zs["wp"] = along_z([wp.at[0]])
        zs["wd"] = along_z([wd])
        ys["wp"] = along_y([wp.at[0]], 0)
        ys["wd"] = along_y([wd], 0)

        def pass_on(name, bufs):
            for m in range(1, z_count):
                wait_all(zs[name][m])
                ys[name] += along_y(bufs, m)

        pass_on("wo", [wo.at[0]])
        heads1 = heads_along_z(1, wq1)
        zs["wu"] = along_z([wu])
        wait_all(y0)
        gain_rows = gall[...].astype(F32).T[0:8, :]
        gain_out[...] = gain_rows
        for t in range(3):
            wq_out[:, t * hd : (t + 1) * hd] = wq0[t]

        def to_heads(e, first, amount):
            base = pl.multiple_of(flip(fs, e) * rows + first, 16)
            for r in range(0, amount, LANES):
                block = toks[e, first + r : first + r + LANES, :].astype(F32)
                n1[pl.ds(base + r, LANES), :] = layer_norm(block, gain_rows[0:1]).astype(BF)
            at = pl.ds(base, amount)
            got = dot_nn(n1[at, :], wq_out[...])
            q, k, v = got[:, :hd], got[:, hd : 2 * hd], got[:, 2 * hd :]
            q = (q * cos_ref[at, :] + partner(q) * sin_ref[at, :]).astype(BF)
            k = (k * cos_ref[at, :] + partner(k) * sin_ref[at, :]).astype(BF)
            qkv[at, 0:hd] = q
            qkv[at, hd : 2 * hd] = k
            qkv[at, 2 * hd : 3 * hd] = v.astype(BF)
            row = lax.broadcasted_iota(jnp.int32, (amount, LANES), 0) + base
            inside = (row >= 3 * lane_first) & (row < 3 * lane_end)
            fk = jnp.where(inside, 1.0, 0.0)
            fq = jnp.where(inside | (lane >= docs), 0.0, MASKED)
            head_inputs(qs, ks, at, q.astype(F32), k.astype(F32), fq, fk, heads)

        to_heads(0, 0, rows)
        for tk in tks:
            tk.ready(1)
        to_heads(1, 0, rows)
        for n, tk in enumerate(tks):
            tk.relay()
            for e in range(2, fs_count):
                tk.ready(e)
                to_heads(e, n * short, short)
        for r in range(0, total, blk):
            at = slice(r, r + blk)
            vt[:, at] = qkv[at, 2 * hd : 3 * hd].astype(F32).T.astype(BF)
        stores = [net.local(n1, n1_hbm)]
        stores.append(net.local(qkv, qkv_hbm))

        flights = []
        for n, r in enumerate(range(0, total, blk)):
            stop = r + blk
            found = []
            for h in range(heads):
                e, inv = softmax_block(ks, qs, h, r, stop)
                found.append(dot_nn(vt[h * HEAD : (h + 1) * HEAD, 0:stop], e.astype(BF)) * inv)
            att[0, r:stop, :] = jnp.concatenate(found, axis=0).T.astype(BF)
            flights.append(spread(att.at[:, r:stop, :], att.at[0, r:stop, :]))
            if n == 0:
                wait_all(ys["wo"])
                wo_f = spread(wo, wo.at[0])
            if n == 1:
                pass_on("wi", [wi])
            if n == 3:
                pass_on("wp", [wp.at[0]])
                wo_f.relay()
            if n == 5:
                pass_on("wd", [wd])
                ys["wu"] = along_y([wu], 0)
            if n >= 2:
                flights[n - 2].relay()
        for flight in flights[-2:]:
            flight.relay()
        wait_all(ys["wp"])
        wp_f = spread(wp, wp.at[0])
        ys["heads1"] = []
        for m in range(z_count):
            ys["heads1"] += heads_along_y(wq1, heads1[m], m)
        wo_f.all_ready()
        for e in range(fs_count):
            wo_at[flip(fs, e)] = wo[e]
        for e in range(fs_count):
            hold[:, e * hd : (e + 1) * hd] = wo_at[e]
        for e in range(fs_count):
            base = pl.multiple_of(flip(fs, e) * hd, 16)
            turned[e * hd : (e + 1) * hd, :] = hold[pl.ds(base, hd), :]
        wo_full[...] = hold[...]
        for flight in flights:
            flight.all_ready()
        wait_all(ys["wi"])
        wait_all(ys["wd"])

        def mix(x_block, o_block, amount, keep_mid, keep, out):
            work[0:amount, 0:width] = x_block.astype(F32) + dot_nn(o_block, turned[...])

            def norm(r):
                at = pl.ds(r, HEAD)
                m = work[at, 0:width]
                if keep_mid is not None:
                    keep_mid[at, :] = m
                value = layer_norm(m, gain_rows[1:2]).astype(BF)
                low[at, 0:width] = value
                if keep is not None:
                    n2[pl.ds(pl.multiple_of(keep + r, HEAD), HEAD), :] = value

            row_loop(amount, norm)
            work[0:amount, 0:fj] = dot_nn(low[0:amount, 0:width], wi[...])

            def activate(r):
                at = pl.ds(r, HEAD)
                if keep is None:
                    low[at, 0:fj] = gelu(work[at, 0:fj]).astype(BF)
                    return
                value, rate = gelu_both(work[at, 0:fj])
                low[at, 0:fj] = value.astype(BF)
                here = pl.ds(pl.multiple_of(keep + r, HEAD), HEAD)
                hid0[here, :] = value.astype(BF)
                slope0[here, :] = rate.astype(BF)

            row_loop(amount, activate)
            out[0:amount, :] = dot_nt(low[0:amount, 0:fj], wd[...])

        for e in range(fs_count):
            at = pl.ds(pl.multiple_of(flip(fs, e) * rows + rows - HALO, 16), HALO)
            for k in range(fs_count):
                att_rel[e * HALO : (e + 1) * HALO, k * hd : (k + 1) * hd] = att[k, at, :]
        tails = jnp.concatenate([toks[e, rows - HALO : rows, :] for e in range(fs_count)], axis=0)
        mix(tails, att_rel[0 : fs_count * HALO, :], fs_count * HALO, m_tail, None, part_tail)

        for e in range(fs_count):
            base = pl.multiple_of(flip(fs, e) * rows, 16)
            for k in range(fs_count):
                att_rel[pl.ds(base, rows), k * hd : (k + 1) * hd] = att[k, pl.ds(base, rows), :]

        def before(e):
            place = flip(fs, e) + fs_count - 1
            place = lax.rem(place, fs_count)
            apart = jnp.int32(0)
            bit = 1
            while bit < fs_count:
                one = lax.rem(lax.div(place, bit), 2)
                two = lax.rem(lax.div(fs, bit), 2)
                apart = apart + bit * lax.rem(one + two, 2)
                bit *= 2
            return pl.multiple_of(apart * HALO, 16)

        def partial_for(e, out):
            base = pl.multiple_of(flip(fs, e) * rows, 16)
            mix(
                toks[e],
                att_rel[pl.ds(base, rows), :],
                rows,
                mid if e == 0 else None,
                e * rows,
                part,
            )
            out[0:HALO, :] = part_tail[pl.ds(before(e), HALO), :].astype(out.dtype)
            out[HALO:long_rows, :] = part[0:rows, :].astype(out.dtype)

        stores.append(net.local(att_rel, att_hbm))
        half = fs_count // 2
        first_hops = {}
        for j in reversed(range(half)):
            partial_for(2 * j + 1, sbuf.at[j])
            first_hops[j] = net.start(sbuf.at[j], rbuf.at[j], (dp, flip(fs, 1)))
            if j == half - 1:
                pass_on("wu", [wu])
            if j:
                partial_for(2 * j, acc.at[j])
                first_hops[j].wait_recv()
                acc[j] = acc[j] + rbuf[j].astype(F32)
                if half == 2:
                    xsend[0] = acc[1].astype(BF)
                    last_hop = net.start(xsend.at[0], xrecv.at[0], (dp, flip(fs, 2)))
            if j == half - 1:
                wp_f.relay()
        partial_for(0, acc.at[0])
        first_hops[0].wait_recv()
        acc[0] = acc[0] + rbuf[0].astype(F32)
        if half > 2:
            bit, active = 2, list(range(half))
            slot = 0
            while bit < fs_count:
                stay = [j for j in active if not (2 * j) & bit]
                hops = {}
                for j in stay:
                    give = j + bit // 2
                    xsend[slot] = acc[give].astype(BF)
                    hops[j] = (net.start(xsend.at[slot], xrecv.at[slot], (dp, flip(fs, bit))), slot)
                    slot += 1
                for j in stay:
                    hops[j][0].wait_recv()
                    acc[j] = acc[j] + xrecv[hops[j][1]].astype(F32)
                active, bit = stay, bit * 2
        elif half == 2:
            last_hop.wait_recv()
            acc[0] = acc[0] + xrecv[0].astype(F32)
        a_tail = acc[0, 0:HALO, :] + m_tail[pl.ds(before(0), HALO), :]
        a_own = acc[0, HALO:long_rows, :] + mid[...]
        after[...] = a_own
        for c in range(width // LANES):
            thin[c, 0:HALO, :] = a_tail[:, c * LANES : (c + 1) * LANES]
            thin[c, HALO:long_rows, :] = a_own[:, c * LANES : (c + 1) * LANES]

        stores.append(net.local(n2, n2_hbm))
        stores.append(net.local(hid0, hid_hbm))
        stores.append(net.local(slope0, slope_hbm))

        row = lax.broadcasted_iota(jnp.int32, (short, LANES), 0) + fs * short
        begins = jnp.max(jnp.where(row == lane_first, 1.0, 0.0), axis=1, keepdims=True)
        parts = []
        for k in range(3):
            value = strided_read(thin, HALO - 2 + k, short)
            parts.append(jnp.where(begins > 0.0, 0.0, value) if k < 2 else value)
        z = jnp.concatenate(parts, axis=1).astype(BF)
        for e in range(fs_count):
            z_out[e] = z[:, e * pc : (e + 1) * pc]
        pooled = jnp.zeros((short, width), F32)
        for e in range(fs_count):
            wp_f.ready(e)
            pooled = pooled + dot_nt(z_out[flip(fs, e)], wp[e])
        s0_out[...] = pooled
        for name in ("heads1", "wu"):
            wait_all(ys[name])
        wait_all(c_f)
        for t in range(3):
            wq1_out[:, t * hd : (t + 1) * hd] = wq1[t]
        for copy in stores:
            copy.wait()
        net.finish()

    half = fs_count // 2
    outs = [
        ((total, width), BF),
        ((total, 3 * hd), BF),
        ((total, width), BF),
        ((width, width), BF),
        ((total, width), BF),
        ((total, fj), BF),
        ((total, fj), BF),
        ((rows, width), F32),
        ((rows, width), F32),
        ((fs_count, short, pc), BF),
        ((short, width), F32),
        ((width, 3 * hd), BF),
        ((width, fj), BF),
        ((width, fj), BF),
        ((fs_count, width, pc), BF),
        ((width, 3 * hd), BF),
        ((width, pc), BF),
        ((fs_count, short, pc), BF),
        ((8, width), F32),
    ]
    wide = max(width, fj)
    scratch = [
        ((total, width), BF),
        ((total, 3 * hd), BF),
        ((total, width), BF),
        ((total, width), BF),
        ((total, fj), BF),
        ((total, fj), BF),
        ((fs_count, rows, width), BF),
        ((fs_count, short, pc), BF),
        ((2, 3, rw, hd), BF),
        ((3, width, hd), BF),
        ((3, width, hd), BF),
        ((width, LANES), BF),
        ((fs_count, width, hd), BF),
        ((fs_count, width, hd), BF),
        ((fs_count, total, hd), BF),
        ((heads, total, LANES), BF),
        ((heads, total, LANES), BF),
        ((hd, total), BF),
        ((width, width), BF),
        ((width, width), BF),
        ((rows, wide), F32),
        ((rows, wide), BF),
        ((rows, width), F32),
        ((fs_count * HALO, width), F32),
        ((fs_count * HALO, width), F32),
        ((half, long_rows, width), BF),
        ((half, long_rows, width), BF),
        ((half - 1, long_rows, width), BF),
        ((half - 1, long_rows, width), BF),
        ((half, long_rows, width), F32),
        ((width // LANES, long_rows, LANES), F32),
    ]
    return pl.pallas_call(
        body,
        out_shape=[jax.ShapeDtypeStruct(s, t) for s, t in outs],
        in_specs=[vmem(), vmem(), smem()] + [vmem()] * 9,
        out_specs=[hbm() if n in (0, 1, 2, 4, 5, 6) else vmem() for n in range(len(outs))],
        scratch_shapes=[pltpu.VMEM(s, t) for s, t in scratch] + [pltpu.SemaphoreType.DMA((sems,))] * 2,
        compiler_params=pltpu.CompilerParams(collective_id=3, has_side_effects=True, vmem_limit_bytes=VMEM_BYTES),
        cost_estimate=cost(2e10, 3e7),
        name="forward_one",
    )(tokens, cot, triples, *weights, gains_t, cos, sin)


def forward_all(y_count, dp_count, fs_count, tokens, cot, triples, weights, gains_t, cos, sin):
    rows, width = tokens.shape
    total, short = rows * fs_count, rows // 3
    long_rows = rows + HALO
    wqkv, wout, win, wdown, wpool, wup = weights
    rw = wqkv.shape[1]
    hd, fj, pc = wout.shape[2], win.shape[2], wpool.shape[1]
    heads = hd // HEAD
    docs = triples.shape[1]
    z_count = dp_count // y_count
    blk = query_rows(total)
    total_b = short * fs_count
    blk_b = min(QB, total_b)
    blocks_b, half = total_b // blk_b, fs_count // 2
    cb = 4 * hd + 2 * pc
    sems = 192 + 22 * dp_count + 16 * fs_count

    def body(
        tok, cot_ref, triples_ref, q_in, o_in, i_in, d_in, p_in, u_in, g_in, cos_ref, sin_ref,
        n1_hbm, qkv_hbm, att_hbm, n2_hbm, hid_hbm, slope_hbm, wo_full, mid, wq_out, wi, wd, gain_out, out, da, dfs_out, group, sum_ff, dgain,
        after, z_out, s0_out, wp, wq1_out, wu, c_rel,
        n1, qkv, att_rel, n2, hid0, slope0, toks, c_own, st_q, wq0, wq1, gall, wo, wo_at, att, qs, ks, vt, turned, hold, work, low, part, m_tail, part_tail, sbuf, rbuf, xsend, xrecv, acc, thin,
        b_wos, b_wi_ref, b_wd_ref, b_g_ff, b_yg, b_zsg, b_zrg, b_sd, b_rd, b_xd, b_yd, b_ad, b_lift_send, b_lift_rel, b_s0s, b_x_all, b_z_rel, b_dfs, b_df_all, b_do_out, b_do_in, b_da_out, b_da_in, b_cols, b_s1s, b_ds0s, b_nxt, b_n1, b_n2, b_qkv, b_att, b_att_rel, b_kt, b_dk, b_dv, b_dqkv, b_work, b_hid, b_slope, b_dpre, b_m_all, b_dm, b_sf, b_rf, b_xf, b_yf, b_af, b_sb, b_rb, b_xb, b_yb, b_ab, b_sa, b_ra, b_xa, b_ya, b_aa, b_spread_rows, b_lift,
        send_sem, recv_sem, *ps,
    ):
        dp, fs = lax.axis_index("dp"), lax.axis_index("fsdp")
        net = Net(send_sem, recv_sem)

        def own(buf):
            return buf.at[pl.ds(pl.multiple_of(dp * rw, 16), rw), :]

        def of(buf, step):
            return buf.at[pl.ds(pl.multiple_of(flip(dp, step) * rw, 16), rw), :]

        for b in range(2):
            for t in range(3):
                st_q[b, t] = q_in[b, :, t * hd : (t + 1) * hd].astype(BF)
        here = pl.ds(pl.multiple_of(dp * rw, 16), rw)
        wide_gain = jnp.concatenate([g_in[...], jnp.zeros((LANES - 4, rw), F32)], axis=0).T
        gall[here, :] = wide_gain.astype(BF)
        wo[0, here, :] = o_in[0].astype(BF)
        wi[here, :] = i_in[0].astype(BF)
        wd[here, :] = d_in[0].astype(BF)
        wp[0, here, :] = p_in[...].astype(BF)
        wu[here, :] = u_in[...].astype(BF)
        b_wos[0, here, :] = o_in[1].astype(BF)
        b_wi_ref[here, :] = i_in[1].astype(BF)
        b_wd_ref[here, :] = d_in[1].astype(BF)

        barrier = pltpu.get_barrier_semaphore()
        for m in range(z_count):
            for e in range(fs_count):
                if m or e:
                    there = (flip(dp, m * y_count), flip(fs, e))
                    pl.semaphore_signal(barrier, inc=1, device_id=there, device_id_type=MESH)
        for j in range(1, y_count):
            pl.semaphore_signal(barrier, inc=1, device_id=(flip(dp, j), fs), device_id_type=MESH)
        pl.semaphore_wait(barrier, z_count * fs_count - 1 + y_count - 1)

        def along_z(bufs):
            found = [[] for _ in range(z_count)]
            for m in range(1, z_count):
                for buf in bufs:
                    found[m].append(net.start(own(buf), own(buf), (flip(dp, m * y_count), fs)))
            return found

        def along_y(bufs, m):
            return [
                net.start(of(buf, m * y_count), of(buf, m * y_count), (flip(dp, j), fs))
                for j in range(1, y_count)
                for buf in bufs
            ]

        def wait_all(copies):
            for copy in copies:
                copy.wait_recv()

        def heads_along_z(b, wq):
            found = []
            for m in range(z_count):
                line = []
                for t in range(3):
                    place = 3 * fs + t
                    kind, to = lax.div(place, fs_count), lax.rem(place, fs_count)
                    copy = net.make(st_q.at[b, t], wq.at[kind, here, :], (flip(dp, m * y_count), to))
                    if m == 0:

                        @pl.when(to != fs)
                        def _():
                            copy.start()

                        @pl.when(to == fs)
                        def _():
                            wq[kind, here, :] = st_q[b, t]

                        line.append((copy, to != fs))
                    else:
                        copy.start()
                        net.open.append(copy)
                        line.append((copy, None))
                found.append(line)
            return found

        def heads_along_y(wq, line, m):
            for copy, when in line:
                if when is None:
                    copy.wait_recv()
                else:

                    @pl.when(when)
                    def _():
                        copy.wait_recv()
                        copy.wait_send()

            at = pl.ds(pl.multiple_of(flip(dp, m * y_count) * rw, 16), rw)
            return [
                net.start(wq.at[:, at, :], wq.at[:, at, :], (flip(dp, j), fs)) for j in range(1, y_count)
            ]


        def spread(pieces, src):
            return Flight(net, dp, fs, fs_count, pieces, src)

        heads0 = heads_along_z(0, wq0)
        gz = along_z([gall])
        y0 = along_y([gall], 0)
        thirds = [slice(n * short, (n + 1) * short) for n in range(3)]
        tks = [spread(toks.at[:, third, :], tok.at[third, :]) for third in thirds]
        toks[0] = tok[...]
        zs = {}
        zs["wo"] = along_z([wo.at[0]])
        zs["wi"] = along_z([wi])
        ys = {"wo": along_y([wo.at[0]], 0), "wi": along_y([wi], 0)}
        spread_write(thin.at[:, 0:rows, :], cot_ref[...].astype(F32))
        lifted = jnp.concatenate([strided_read(thin, n, short) for n in range(3)], axis=1).astype(BF)
        for e in range(fs_count):
            c_own[e] = lifted[:, e * pc : (e + 1) * pc]
        c_rel[0] = c_own[fs]
        c_f = [
            net.start(c_own.at[flip(fs, e)], c_rel.at[e], (dp, flip(fs, e))) for e in range(1, fs_count)
        ]
        lane_first, lane_end, lane = doc_bounds(triples_ref, docs)
        for m in range(z_count):
            y0 += heads_along_y(wq0, heads0[m], m)
            if m:
                wait_all(gz[m])
                y0 += along_y([gall], m)
        zs["wp"] = along_z([wp.at[0]])
        zs["wd"] = along_z([wd])
        ys["wp"] = along_y([wp.at[0]], 0)
        ys["wd"] = along_y([wd], 0)

        def pass_on(name, bufs):
            for m in range(1, z_count):
                wait_all(zs[name][m])
                ys[name] += along_y(bufs, m)

        pass_on("wo", [wo.at[0]])
        heads1 = heads_along_z(1, wq1)
        zs["wu"] = along_z([wu])
        later = (b_wos.at[0], b_wi_ref, b_wd_ref)
        came = [[line[0] for line in along_z([buf])[1:]] for buf in later]
        wait_all(y0)
        gain_rows = gall[...].astype(F32).T[0:8, :]
        gain_out[...] = gain_rows
        for t in range(3):
            wq_out[:, t * hd : (t + 1) * hd] = wq0[t]

        def to_heads(e, first, amount):
            base = pl.multiple_of(flip(fs, e) * rows + first, 16)
            for r in range(0, amount, LANES):
                block = toks[e, first + r : first + r + LANES, :].astype(F32)
                n1[pl.ds(base + r, LANES), :] = layer_norm(block, gain_rows[0:1]).astype(BF)
            at = pl.ds(base, amount)
            got = dot_nn(n1[at, :], wq_out[...])
            q, k, v = got[:, :hd], got[:, hd : 2 * hd], got[:, 2 * hd :]
            q = (q * cos_ref[at, :] + partner(q) * sin_ref[at, :]).astype(BF)
            k = (k * cos_ref[at, :] + partner(k) * sin_ref[at, :]).astype(BF)
            qkv[at, 0:hd] = q
            qkv[at, hd : 2 * hd] = k
            qkv[at, 2 * hd : 3 * hd] = v.astype(BF)
            row = lax.broadcasted_iota(jnp.int32, (amount, LANES), 0) + base
            inside = (row >= 3 * lane_first) & (row < 3 * lane_end)
            fk = jnp.where(inside, 1.0, 0.0)
            fq = jnp.where(inside | (lane >= docs), 0.0, MASKED)
            head_inputs(qs, ks, at, q.astype(F32), k.astype(F32), fq, fk, heads)

        to_heads(0, 0, rows)
        for tk in tks:
            tk.ready(1)
        to_heads(1, 0, rows)
        for n, tk in enumerate(tks):
            tk.relay()
            for e in range(2, fs_count):
                tk.ready(e)
                to_heads(e, n * short, short)
        for r in range(0, total, blk):
            at = slice(r, r + blk)
            vt[:, at] = qkv[at, 2 * hd : 3 * hd].astype(F32).T.astype(BF)
        stores = [net.local(n1, n1_hbm)]
        stores.append(net.local(qkv, qkv_hbm))

        flights = []
        for n, r in enumerate(range(0, total, blk)):
            stop = r + blk
            found = []
            for h in range(heads):
                e, inv = softmax_block(ks, qs, h, r, stop)
                found.append(dot_nn(vt[h * HEAD : (h + 1) * HEAD, 0:stop], e.astype(BF)) * inv)
            att[0, r:stop, :] = jnp.concatenate(found, axis=0).T.astype(BF)
            flights.append(spread(att.at[:, r:stop, :], att.at[0, r:stop, :]))
            if n == 0:
                wait_all(ys["wo"])
                wo_f = spread(wo, wo.at[0])
            if n == 1:
                pass_on("wi", [wi])
            if n == 3:
                pass_on("wp", [wp.at[0]])
                wo_f.relay()
            if n == 5:
                pass_on("wd", [wd])
                ys["wu"] = along_y([wu], 0)
                passed = [along_y([buf], 0) for buf in later]
            if n >= 2:
                flights[n - 2].relay()
        for flight in flights[-2:]:
            flight.relay()
        wait_all(ys["wp"])
        wp_f = spread(wp, wp.at[0])
        ys["heads1"] = []
        for m in range(z_count):
            ys["heads1"] += heads_along_y(wq1, heads1[m], m)
        wo_f.all_ready()
        for e in range(fs_count):
            wo_at[flip(fs, e)] = wo[e]
        for e in range(fs_count):
            hold[:, e * hd : (e + 1) * hd] = wo_at[e]
        for e in range(fs_count):
            base = pl.multiple_of(flip(fs, e) * hd, 16)
            turned[e * hd : (e + 1) * hd, :] = hold[pl.ds(base, hd), :]
        wo_full[...] = hold[...]
        for flight in flights:
            flight.all_ready()
        wait_all(ys["wi"])
        wait_all(ys["wd"])

        def mix(x_block, o_block, amount, keep_mid, keep, out):
            work[0:amount, 0:width] = x_block.astype(F32) + dot_nn(o_block, turned[...])

            def norm(r):
                at = pl.ds(r, HEAD)
                m = work[at, 0:width]
                if keep_mid is not None:
                    keep_mid[at, :] = m
                value = layer_norm(m, gain_rows[1:2]).astype(BF)
                low[at, 0:width] = value
                if keep is not None:
                    n2[pl.ds(pl.multiple_of(keep + r, HEAD), HEAD), :] = value

            row_loop(amount, norm)
            work[0:amount, 0:fj] = dot_nn(low[0:amount, 0:width], wi[...])

            def activate(r):
                at = pl.ds(r, HEAD)
                if keep is None:
                    low[at, 0:fj] = gelu(work[at, 0:fj]).astype(BF)
                    return
                value, rate = gelu_both(work[at, 0:fj])
                low[at, 0:fj] = value.astype(BF)
                here = pl.ds(pl.multiple_of(keep + r, HEAD), HEAD)
                hid0[here, :] = value.astype(BF)
                slope0[here, :] = rate.astype(BF)

            row_loop(amount, activate)
            out[0:amount, :] = dot_nt(low[0:amount, 0:fj], wd[...])

        for e in range(fs_count):
            at = pl.ds(pl.multiple_of(flip(fs, e) * rows + rows - HALO, 16), HALO)
            for k in range(fs_count):
                att_rel[e * HALO : (e + 1) * HALO, k * hd : (k + 1) * hd] = att[k, at, :]
        tails = jnp.concatenate([toks[e, rows - HALO : rows, :] for e in range(fs_count)], axis=0)
        mix(tails, att_rel[0 : fs_count * HALO, :], fs_count * HALO, m_tail, None, part_tail)

        for e in range(fs_count):
            base = pl.multiple_of(flip(fs, e) * rows, 16)
            for k in range(fs_count):
                att_rel[pl.ds(base, rows), k * hd : (k + 1) * hd] = att[k, pl.ds(base, rows), :]

        def before(e):
            place = flip(fs, e) + fs_count - 1
            place = lax.rem(place, fs_count)
            apart = jnp.int32(0)
            bit = 1
            while bit < fs_count:
                one = lax.rem(lax.div(place, bit), 2)
                two = lax.rem(lax.div(fs, bit), 2)
                apart = apart + bit * lax.rem(one + two, 2)
                bit *= 2
            return pl.multiple_of(apart * HALO, 16)

        def partial_for(e, out):
            base = pl.multiple_of(flip(fs, e) * rows, 16)
            mix(
                toks[e],
                att_rel[pl.ds(base, rows), :],
                rows,
                mid if e == 0 else None,
                e * rows,
                part,
            )
            out[0:HALO, :] = part_tail[pl.ds(before(e), HALO), :].astype(out.dtype)
            out[HALO:long_rows, :] = part[0:rows, :].astype(out.dtype)

        stores.append(net.local(att_rel, att_hbm))
        first_hops = {}
        for j in reversed(range(half)):
            partial_for(2 * j + 1, sbuf.at[j])
            first_hops[j] = net.start(sbuf.at[j], rbuf.at[j], (dp, flip(fs, 1)))
            if j == half - 1:
                pass_on("wu", [wu])
            if j:
                partial_for(2 * j, acc.at[j])
                first_hops[j].wait_recv()
                acc[j] = acc[j] + rbuf[j].astype(F32)
                if half == 2:
                    xsend[0] = acc[1].astype(BF)
                    last_hop = net.start(xsend.at[0], xrecv.at[0], (dp, flip(fs, 2)))
            if j == half - 1:
                wp_f.relay()
        partial_for(0, acc.at[0])
        first_hops[0].wait_recv()
        acc[0] = acc[0] + rbuf[0].astype(F32)
        if half > 2:
            bit, active = 2, list(range(half))
            slot = 0
            while bit < fs_count:
                stay = [j for j in active if not (2 * j) & bit]
                hops = {}
                for j in stay:
                    give = j + bit // 2
                    xsend[slot] = acc[give].astype(BF)
                    hops[j] = (net.start(xsend.at[slot], xrecv.at[slot], (dp, flip(fs, bit))), slot)
                    slot += 1
                for j in stay:
                    hops[j][0].wait_recv()
                    acc[j] = acc[j] + xrecv[hops[j][1]].astype(F32)
                active, bit = stay, bit * 2
        elif half == 2:
            last_hop.wait_recv()
            acc[0] = acc[0] + xrecv[0].astype(F32)
        a_tail = acc[0, 0:HALO, :] + m_tail[pl.ds(before(0), HALO), :]
        a_own = acc[0, HALO:long_rows, :] + mid[...]
        after[...] = a_own
        for c in range(width // LANES):
            thin[c, 0:HALO, :] = a_tail[:, c * LANES : (c + 1) * LANES]
            thin[c, HALO:long_rows, :] = a_own[:, c * LANES : (c + 1) * LANES]

        stores.append(net.local(n2, n2_hbm))
        stores.append(net.local(hid0, hid_hbm))
        stores.append(net.local(slope0, slope_hbm))

        row = lax.broadcasted_iota(jnp.int32, (short, LANES), 0) + fs * short
        begins = jnp.max(jnp.where(row == lane_first, 1.0, 0.0), axis=1, keepdims=True)
        parts = []
        for k in range(3):
            value = strided_read(thin, HALO - 2 + k, short)
            parts.append(jnp.where(begins > 0.0, 0.0, value) if k < 2 else value)
        z = jnp.concatenate(parts, axis=1).astype(BF)
        for e in range(fs_count):
            z_out[e] = z[:, e * pc : (e + 1) * pc]
        pooled = jnp.zeros((short, width), F32)
        for e in range(fs_count):
            wp_f.ready(e)
            pooled = pooled + dot_nt(z_out[flip(fs, e)], wp[e])
        s0_out[...] = pooled
        for name in ("heads1", "wu"):
            wait_all(ys[name])
        wait_all(c_f)
        for t in range(3):
            wq1_out[:, t * hd : (t + 1) * hd] = wq1[t]
        (wos, wi_ref, wd_ref, g_ff, yg, zsg, zrg, sd, rd, xd, yd, ad, lift_send, lift_rel, s0s, x_all, z_rel, dfs, df_all, do_out, do_in, da_out, da_in, cols, s1s, ds0s, nxt, n1, n2, qkv, att, att_rel, kt, dk, dv, dqkv, work, hid, slope, dpre, m_all, dm, sf, rf, xf, yf, af, sb, rb, xb, yb, ab, sa, ra, xa, ya, aa, spread_rows, lift) = (
            b_wos, b_wi_ref, b_wd_ref, b_g_ff, b_yg, b_zsg, b_zrg, b_sd, b_rd, b_xd, b_yd, b_ad, b_lift_send, b_lift_rel, b_s0s, b_x_all, b_z_rel, b_dfs, b_df_all, b_do_out, b_do_in, b_da_out, b_da_in, b_cols, b_s1s, b_ds0s, b_nxt, b_n1, b_n2, b_qkv, b_att, b_att_rel, b_kt, b_dk, b_dv, b_dqkv, b_work, b_hid, b_slope, b_dpre, b_m_all, b_dm, b_sf, b_rf, b_xf, b_yf, b_af, b_sb, b_rb, b_xb, b_yb, b_ab, b_sa, b_ra, b_xa, b_ya, b_aa, b_spread_rows, b_lift
        )
        thin = thin.at[:, 0:rows, :]
        def base_of(e, amount):
            return pl.multiple_of(flip(fs, e) * amount, 16)

        def spread(pieces, src=None):
            return Flight(net, dp, fs, fs_count, pieces, pieces.at[0] if src is None else src)

        s0s[0] = s0_out[...].astype(BF)
        nxt[...] = jnp.zeros(nxt.shape, BF)
        here = pl.ds(pl.multiple_of(dp * rw, 16), rw)
        def of(buf, step):
            return buf.at[pl.ds(pl.multiple_of(flip(dp, step) * rw, 16), rw), :]

        def along_z(buf):
            return [
                net.start(of(buf, 0), of(buf, 0), (flip(dp, m * y_count), fs)) for m in range(1, z_count)
            ]

        def along_y(buf, m):
            return [
                net.start(of(buf, m * y_count), of(buf, m * y_count), (flip(dp, n), fs)) for n in range(1, y_count)
            ]

        def pass_on(buf, came, passed):
            for m in range(1, z_count):
                came[m - 1].wait_recv()
                passed += along_y(buf, m)

        def wait_all(copies):
            for copy in copies:
                copy.wait_recv()

        s0_f = spread(s0s)

        dsum = Scatter(net, dp, fs, fs_count, sd, rd, xd, yd, ad)
        for e in reversed(range(fs_count)):
            part = dot_nt(c_rel[e], wu[...])
            if e % 2:
                sd[e // 2] = part.astype(BF)
                dsum.send_odd(e // 2)
            else:
                ad[e // 2] = part

        def exchange(blocks_of, landed):
            found = []
            for e in range(1, fs_count):
                found.append(net.start(blocks_of.at[flip(fs, e)], landed.at[e], (dp, flip(fs, e))))
            landed[0] = blocks_of[fs]
            return found

        lane_first, lane_end, lane = doc_bounds(triples_ref, docs)
        for n in range(1, half):
            dsum.join(n)
        dsum.upper()
        s0_f.relay()
        pass_on(wos.at[0], came[0], passed[0])
        for e in range(fs_count):
            s0_f.ready(e)
            at = pl.ds(base_of(e, short), short)
            value = s0_out[...] if e == 0 else s0s[e].astype(F32)
            x_all[at, :] = value
            n1[at, :] = layer_norm(value, gain_out[2:3, :]).astype(BF)
        for r in range(0, total_b, blk_b):
            at = slice(r, r + blk_b)
            got = dot_nn(n1[at, :], wq1_out[...])
            q, k, v = got[:, :hd], got[:, hd : 2 * hd], got[:, 2 * hd :]
            q = (q * cos_ref[at, :] + partner(q) * sin_ref[at, :]).astype(BF)
            k = (k * cos_ref[at, :] + partner(k) * sin_ref[at, :]).astype(BF)
            qkv[at, 0:hd] = q
            qkv[at, hd : 2 * hd] = k
            qkv[at, 2 * hd : 3 * hd] = v.astype(BF)
            row = lax.broadcasted_iota(jnp.int32, (blk_b, LANES), 0) + r
            inside = (row >= lane_first) & (row < lane_end)
            fk = jnp.where(inside, 1.0, 0.0)
            fq = jnp.where(inside | (lane >= docs), 0.0, MASKED)
            head_inputs(qs, ks, at, q.astype(F32), k.astype(F32), fq, fk, heads)
            vt[:, at] = v.T.astype(BF)
            kt[:, at] = k.astype(F32).T.astype(BF)
            dk[at, :] = jnp.zeros((blk_b, LANES), F32)
            dv[at, :] = jnp.zeros((blk_b, LANES), F32)
        dsum.join(0)
        dsum.finish()
        dm[...] = ad[0]
        dfs[0] = ad[0].astype(BF)
        df_f = spread(dfs)
        wait_all(passed[0])
        wo_f = spread(wos, wos.at[0])
        flights = []
        for n in range(blocks_b):
            r, stop = n * blk_b, (n + 1) * blk_b
            found = []
            for h in range(heads):
                e, inv = softmax_block(ks, qs, h, r, stop)
                ps[n][h] = (e * inv).astype(BF)
                found.append(dot_nn(vt[h * HEAD : (h + 1) * HEAD, 0:stop], ps[n][h]))
            att[0, r:stop, :] = jnp.concatenate(found, axis=0).T.astype(BF)
            flights.append(spread(att.at[:, r:stop, :], att.at[0, r:stop, :]))
            if n == 0:
                pass_on(wi_ref, came[1], passed[1])
                df_f.relay()
                wo_f.relay()
        place_of = lax.broadcasted_iota(jnp.int32, (blk_b, LANES), 1) // HEAD
        for r in range(0, total_b, blk_b):
            at = slice(r, r + blk_b)
            q = widen(qkv[at, 0:hd].astype(F32))
            for h in range(heads):
                qs[h, at, :] = jnp.where(place_of == h, q, 0.0).astype(BF)

        pass_on(wd_ref, came[2], passed[2])
        wo_f.all_ready()
        for e in range(fs_count):
            wo_at[flip(fs, e)] = wos[e]
        for e in range(fs_count):
            hold[:, e * hd : (e + 1) * hd] = wo_at[e]
        for e in range(fs_count):
            turned[e * hd : (e + 1) * hd, :] = hold[pl.ds(base_of(e, hd), hd), :]
        for flight in flights:
            flight.relay()
        for flight in flights:
            flight.all_ready()
        for e in range(fs_count):
            att_rel[:, e * hd : (e + 1) * hd] = att[e]

        work[:, 0:width] = x_all[...] + dot_nn(att_rel[...], turned[...])

        def norm_all(r):
            at = pl.ds(r, HEAD)
            m = work[at, 0:width]
            m_all[at, :] = m
            n2[at, :] = layer_norm(m, gain_out[3:4, :]).astype(BF)

        row_loop(total_b, norm_all)
        wait_all(passed[1])
        work[:, 0:fj] = dot_nn(n2[...], wi_ref[...])

        def activate_all(r):
            at = pl.ds(r, HEAD)
            value, rate = gelu_both(work[at, 0:fj])
            hid[at, :] = value.astype(BF)
            slope[at, :] = rate

        row_loop(total_b, activate_all)
        wait_all(passed[2])
        work[:, 0:width] = dot_nt(hid[...], wd_ref[...])

        def give_out(scatter, source):
            for e in reversed(range(fs_count)):
                value = source[pl.ds(base_of(e, short), short), 0:width]
                if e % 2:
                    scatter.sbuf[e // 2] = value.astype(BF)
                    scatter.send_odd(e // 2)
                else:
                    scatter.acc[e // 2] = value

        fwd = Scatter(net, dp, fs, fs_count, sf, rf, xf, yf, af)
        give_out(fwd, work)
        for e in range(fs_count):
            df_f.ready(e)
            df_all[pl.ds(base_of(e, short), short), :] = dfs[e]
        work[:, 0:fj] = dot_nn(df_all[...], wd_ref[...])

        def pull_all(r):
            at = pl.ds(r, HEAD)
            dpre[at, :] = (work[at, 0:fj] * slope[at, :]).astype(BF)

        row_loop(total_b, pull_all)
        work[:, 0:width] = dot_nt(dpre[...], wi_ref[...])
        bwd = Scatter(net, dp, fs, fs_count, sb, rb, xb, yb, ab)
        give_out(bwd, work)
        for j in range(1, half):
            bwd.join(j)
        bwd.upper()
        for j in range(1, half):
            fwd.join(j)
        fwd.upper()
        g_ff[:, 0:fj] = dot_tn(n2[...], dpre[...]).astype(BF)
        g_ff[:, fj : 2 * fj] = dot_tn(df_all[...], hid[...]).astype(BF)
        ff_rows = RowSum(net, (dp, fs, y_count, z_count, fs_count, rw), g_ff, yg, zsg, zrg, sum_ff)
        ff_rows.start()
        bwd.join(0)
        bwd.finish()
        m_own = m_all[pl.ds(base_of(0, short), short), :]
        dx, dg = layer_norm_back(m_own, gain_out[3:4, :], ab[0])
        dx = dx + dm[...]
        dm[...] = dx
        low_dx = dx.astype(BF)
        got = dot_nt(low_dx, hold[...]).astype(BF)
        for e in range(fs_count):
            do_out[e] = got[:, e * hd : (e + 1) * hd]
            da_out[e] = low_dx[:, e * hd : (e + 1) * hd]
        do_f = exchange(do_out, do_in)
        da_f = exchange(da_out, da_in)
        gain_two = jnp.sum(dg, axis=0, keepdims=True)

        fwd.join(0)
        fwd.finish()
        s1s[0] = (m_own + af[0]).astype(BF)
        s1_f = spread(s1s)
        z_f = exchange(z_out, z_rel)
        wait_all(do_f)
        for e in range(fs_count):
            at = pl.ds(base_of(e, short), short)
            do = widen(do_in[e].astype(F32))
            lane_head = lax.broadcasted_iota(jnp.int32, (short, LANES), 1) // HEAD
            for h in range(heads):
                ks[h, at, :] = jnp.where(lane_head == h, do, 0.0).astype(BF)
        wait_all(da_f)
        for e in range(fs_count):
            cols[pl.ds(base_of(e, short), short), :] = da_in[e]
        s1_f.relay()

        g_out = dot_tn(att_rel[...], cols[...]).astype(BF)
        for e in range(fs_count):
            group[pl.ds(base_of(e, hd), hd), cb - hd : cb] = g_out[e * hd : (e + 1) * hd, :]
        for n in range(blocks_b):
            r, stop = n * blk_b, (n + 1) * blk_b
            at = slice(r, stop)
            found = []
            add_k = add_v = None
            for h in range(heads):
                p = ps[n][h]
                grad = dot_nt(widen(qkv[0:stop, 2 * hd : 3 * hd]), ks[h, at, :])
                wide = p.astype(F32)
                inner = jnp.sum(wide * grad, axis=0, keepdims=True)
                dr = (wide * (grad - inner) * 0.125).astype(BF)
                part_v = dot_nn(p, ks[h, at, :])
                part_k = dot_nn(dr, qs[h, at, :])
                add_v = part_v if add_v is None else add_v + part_v
                add_k = part_k if add_k is None else add_k + part_k
                found.append(dot_nn(kt[h * HEAD : (h + 1) * HEAD, 0:stop], dr))
            dk[0:stop, :] += add_k
            dv[0:stop, :] += add_v
            dq = jnp.concatenate(found, axis=0).T
            dqkv[at, 0:hd] = (dq * cos_ref[at, :] - partner(dq) * sin_ref[at, :]).astype(BF)
        for r in range(0, total_b, blk_b):
            at = slice(r, r + blk_b)
            grad = dk[at, 0:hd]
            dqkv[at, hd : 2 * hd] = (grad * cos_ref[at, :] - partner(grad) * sin_ref[at, :]).astype(BF)
            dqkv[at, 2 * hd : 3 * hd] = dv[at, 0:hd].astype(BF)
        work[:, 0:width] = dot_nt(dqkv[...], wq1_out[...])
        first = Scatter(net, dp, fs, fs_count, sa, ra, xa, ya, aa)
        give_out(first, work)
        for j in range(1, half):
            first.join(j)
        first.upper()
        group[:, 0 : 3 * hd] = dot_tn(n1[...], dqkv[...]).astype(BF)
        s1_f.all_ready()
        lift_f = []
        for e in range(fs_count):
            part = dot_nn(s1s[e], wu[...]).astype(BF)
            if e:
                lift_send[e] = part
                lift_f.append(net.start(lift_send.at[e], lift_rel.at[e], (dp, flip(fs, e))))
            else:
                lift_rel[0] = part
        g_up = jnp.zeros((width, pc), F32)
        for e in range(fs_count):
            g_up = g_up + dot_tn(s1s[e], c_rel[e])
        group[:, 3 * hd + pc : 3 * hd + 2 * pc] = g_up.astype(BF)
        for m in range(1, z_count):
            ff_rows.service(m)
        first.join(0)
        first.finish()
        dx, dg = layer_norm_back(s0_out[...], gain_out[2:3, :], aa[0])
        ds0s[0] = (dx + dm[...]).astype(BF)
        gain_one = jnp.sum(dg, axis=0, keepdims=True)
        which = lax.broadcasted_iota(jnp.int32, (8, width), 0)
        dgain[...] = jnp.where(which == 0, gain_one, jnp.where(which == 1, gain_two, 0.0))

        hop = net.make(ds0s.at[0, 0:HALO, :], nxt, (dp, lax.rem(fs + fs_count - 1, fs_count)))

        @pl.when(fs > 0)
        def _():
            hop.start()

        ds0_f = spread(ds0s)
        row = lax.broadcasted_iota(jnp.int32, (short, LANES), 0) + fs * short + 1
        shut = jnp.max(jnp.where((row == lane_first) | (row >= total_b), 1.0, 0.0), axis=1, keepdims=True) > 0.0

        @pl.when(fs < fs_count - 1)
        def _():
            hop.wait_recv()

        grad = jnp.concatenate([ds0s[0], nxt[...]], axis=0)
        for e in range(fs_count):
            lift_at = dot_nn(grad, wp[e])
            spread_rows[flip(fs, e)] = lift_at
        dz = jnp.concatenate([spread_rows[e] for e in range(fs_count)], axis=1)
        strided_write(thin, 0, short, dz[0:short, 2 * width : 3 * width])
        for k in range(2):
            part = dz[1 : short + 1, k * width : (k + 1) * width]
            strided_write(thin, k + 1, short, jnp.where(shut, 0.0, part))
        value = cot_ref[...].astype(F32) + spread_read(thin)
        da[...] = value
        dfs_out[0] = value.astype(BF)
        out_f = spread(dfs_out)
        ff_rows.service(0)
        ds0_f.relay()
        for copy in z_f:
            copy.wait_recv()
        g_pool = jnp.zeros((width, pc), F32)
        for e in range(fs_count):
            ds0_f.ready(e)
            g_pool = g_pool + dot_tn(ds0s[e], z_rel[e])
        group[:, 3 * hd : 3 * hd + pc] = g_pool.astype(BF)

        wait_all(lift_f)
        for e in range(fs_count):
            lift[flip(fs, e)] = lift_rel[e].astype(F32)
        lifted = jnp.concatenate([lift[e] for e in range(fs_count)], axis=1)
        for n in range(3):
            strided_write(thin, n, short, lifted[:, n * width : (n + 1) * width])
        out[...] = (after[...] + spread_read(thin)).astype(BF)
        ff_rows.finish()
        out_f.relay()
        out_f.all_ready()

        @pl.when(fs > 0)
        def _():
            hop.wait_send()

        for copy in stores:
            copy.wait()
        net.finish()

    outs = [
        ((total, width), BF),
        ((total, 3 * hd), BF),
        ((total, width), BF),
        ((total, width), BF),
        ((total, fj), BF),
        ((total, fj), BF),
        ((width, width), BF),
        ((rows, width), F32),
        ((width, 3 * hd), BF),
        ((width, fj), BF),
        ((width, fj), BF),
        ((8, width), F32),
        ((rows, width), BF),
        ((rows, width), F32),
        ((fs_count, rows, width), BF),
        ((width, cb), BF),
        ((rw, 2 * fj), F32),
        ((8, width), F32),
    ]
    wide = max(width, fj)
    pieces = (fs_count, short, width)
    scatter = [((half, short, width), BF)] * 2 + [((half - 1, short, width), BF)] * 2 + [((half, short, width), F32)]
    scratch = [
        ((rows, width), F32),
        ((fs_count, short, pc), BF),
        ((short, width), F32),
        ((fs_count, width, pc), BF),
        ((width, 3 * hd), BF),
        ((width, pc), BF),
        ((fs_count, short, pc), BF),
        ((total, width), BF),
        ((total, 3 * hd), BF),
        ((total, width), BF),
        ((total, width), BF),
        ((total, fj), BF),
        ((total, fj), BF),
        ((fs_count, rows, width), BF),
        ((fs_count, short, pc), BF),
        ((2, 3, rw, hd), BF),
        ((3, width, hd), BF),
        ((3, width, hd), BF),
        ((width, LANES), BF),
        ((fs_count, width, hd), BF),
        ((fs_count, width, hd), BF),
        ((fs_count, total, hd), BF),
        ((heads, total, LANES), BF),
        ((heads, total, LANES), BF),
        ((hd, total), BF),
        ((width, width), BF),
        ((width, width), BF),
        ((rows, wide), F32),
        ((rows, wide), BF),
        ((rows, width), F32),
        ((fs_count * HALO, width), F32),
        ((fs_count * HALO, width), F32),
        ((half, long_rows, width), BF),
        ((half, long_rows, width), BF),
        ((half - 1, long_rows, width), BF),
        ((half - 1, long_rows, width), BF),
        ((half, long_rows, width), F32),
        ((width // LANES, long_rows, LANES), F32),
        ((fs_count, width, hd), BF),
        ((width, fj), BF),
        ((width, fj), BF),
        ((width, 2 * fj), BF),
        ((y_count - 1, z_count, rw, 2 * fj), BF),
        ((z_count - 1, rw, 2 * fj), BF),
        ((z_count - 1, rw, 2 * fj), BF),
        *scatter,
        ((fs_count, short, pc), BF),
        ((fs_count, short, pc), BF),
        (pieces, BF),
        ((total_b, width), F32),
        ((fs_count, short, pc), BF),
        (pieces, BF),
        ((total_b, width), BF),
        ((fs_count, short, hd), BF),
        ((fs_count, short, hd), BF),
        ((fs_count, short, hd), BF),
        ((fs_count, short, hd), BF),
        ((total_b, hd), BF),
        (pieces, BF),
        (pieces, BF),
        ((HALO, width), BF),
        ((total_b, width), BF),
        ((total_b, width), BF),
        ((total_b, 3 * hd), BF),
        ((fs_count, total_b, hd), BF),
        ((total_b, width), BF),
        ((hd, total_b), BF),
        ((total_b, LANES), F32),
        ((total_b, LANES), F32),
        ((total_b, 3 * hd), BF),
        ((total_b, wide), F32),
        ((total_b, fj), BF),
        ((total_b, fj), F32),
        ((total_b, fj), BF),
        ((total_b, width), F32),
        ((short, width), F32),
        *scatter,
        *scatter,
        *scatter,
        ((fs_count, short + HALO, pc), F32),
        ((fs_count, short, pc), F32),
    ]
    tail = [pltpu.VMEM((heads, (n + 1) * blk_b, blk_b), BF) for n in range(blocks_b)]
    return pl.pallas_call(
        body,
        out_shape=[jax.ShapeDtypeStruct(s, t) for s, t in outs],
        in_specs=[vmem(), vmem(), smem()] + [vmem()] * 9,
        out_specs=[hbm()] * 6 + [vmem()] * (len(outs) - 6),
        scratch_shapes=[pltpu.VMEM(s, t) for s, t in scratch] + [pltpu.SemaphoreType.DMA((sems,))] * 2 + tail,
        compiler_params=pltpu.CompilerParams(collective_id=3, has_side_effects=True, vmem_limit_bytes=VMEM_BYTES),
        cost_estimate=cost(4e10, 5e7),
        name="forward_all",
    )(tokens, cot, triples, *weights, gains_t, cos, sin)


class RowSum:
    def __init__(self, net, place, grad, ybuf, zsend, zrecv, total, q_send=None, q_recv=None, q_total=None):
        self.net, self.grad, self.ybuf = net, grad, ybuf
        self.zsend, self.zrecv, self.total = zsend, zrecv, total
        self.q_send, self.q_recv, self.q_total = q_send, q_recv, q_total
        self.dp, self.fs, self.y_count, self.z_count, self.fs_count, self.rw = place
        self.ys, self.zs, self.qs = {}, {}, []

    def rows_of(self, step):
        return pl.ds(pl.multiple_of(flip(self.dp, step) * self.rw, 16), self.rw)

    def start(self):
        for m in list(range(1, self.z_count)) + [0]:
            self.ys[m] = [
                self.net.start(
                    self.grad.at[self.rows_of(m * self.y_count + j), :],
                    self.ybuf.at[j - 1, m],
                    (flip(self.dp, j), self.fs),
                )
                for j in range(1, self.y_count)
            ]
        if self.q_send is not None:
            self.q_base = self.net.used
            self.net.used += 3 * self.z_count

    def owner(self, kind):
        place = kind * self.fs_count + self.fs
        return lax.div(place, 3), lax.rem(place, 3)

    def service(self, m):
        for copy in self.ys[m]:
            copy.wait_recv()
        got = self.grad[self.rows_of(m * self.y_count), :].astype(F32)
        for j in range(1, self.y_count):
            got = got + self.ybuf[j - 1, m].astype(F32)
        there = flip(self.dp, m * self.y_count)
        lo = 0
        if self.q_send is not None:
            hd = self.q_send.shape[3]
            lo = 3 * hd
            for kind in range(3):
                to, slot = self.owner(kind)
                self.q_send[m, kind] = got[:, kind * hd : (kind + 1) * hd].astype(BF)
                copy = pltpu.make_async_remote_copy(
                    src_ref=self.q_send.at[m, kind],
                    dst_ref=self.q_recv.at[m, slot],
                    send_sem=self.net.send.at[self.q_base + 3 * m + kind],
                    recv_sem=self.net.recv.at[self.q_base + 3 * m + slot],
                    device_id=(there, to),
                    device_id_type=MESH,
                )
                if m:
                    copy.start()
                    self.qs.append((copy, None))
                else:

                    @pl.when(to != self.fs)
                    def _():
                        copy.start()

                    @pl.when(to == self.fs)
                    def _():
                        self.q_recv[0, slot] = self.q_send[0, kind]

                    self.qs.append((copy, to != self.fs))
        width = self.total.shape[1]
        rest = got[:, lo : lo + width]
        if m:
            self.zsend[m - 1] = rest.astype(BF)
            self.zs[m] = self.net.start(self.zsend.at[m - 1], self.zrecv.at[m - 1], (there, self.fs))
        else:
            self.total[...] = rest

    def finish(self):
        rest = self.total[...]
        for m in range(1, self.z_count):
            self.zs[m].wait_recv()
            rest = rest + self.zrecv[m - 1].astype(F32)
        self.total[...] = rest
        if self.q_send is None:
            return
        for t in range(3):
            giver = lax.rem(3 * self.fs + t, self.fs_count)
            for m in range(self.z_count):
                landed = self.q_recv.at[m, t]
                wait = pltpu.make_async_copy(landed, landed, self.net.recv.at[self.q_base + 3 * m + t])
                if m:
                    wait.wait()
                else:

                    @pl.when(giver != self.fs)
                    def _():
                        wait.wait()

        for t in range(3):
            block = self.q_recv[0, t].astype(F32)
            for m in range(1, self.z_count):
                block = block + self.q_recv[m, t].astype(F32)
            self.q_total[t] = block
        for copy, when in self.qs:
            if when is None:
                copy.wait_send()
            else:

                @pl.when(when)
                def _():
                    copy.wait_send()


class HeadSum:
    def __init__(self, net, place, grad, send, recv, total):
        self.net, self.grad, self.send, self.recv, self.total = net, grad, send, recv, total
        self.dp, self.fs, self.y_count, self.z_count, self.fs_count, self.rw = place
        self.count, self.copies = send.shape[0], []

    def start(self):
        base, hd = self.net.used, self.send.shape[3]
        self.base = base
        self.net.used += 3 * self.count
        for step in reversed(range(self.count)):
            rows = pl.ds(pl.multiple_of(flip(self.dp, step) * self.rw, 16), self.rw)
            for kind in range(3):
                place = kind * self.fs_count + self.fs
                to, slot = lax.div(place, 3), lax.rem(place, 3)
                self.send[step, kind] = self.grad[rows, kind * hd : (kind + 1) * hd]
                copy = pltpu.make_async_remote_copy(
                    src_ref=self.send.at[step, kind],
                    dst_ref=self.recv.at[step, slot],
                    send_sem=self.net.send.at[base + 3 * step + kind],
                    recv_sem=self.net.recv.at[base + 3 * step + slot],
                    device_id=(flip(self.dp, step), to),
                    device_id_type=MESH,
                )
                if step:
                    copy.start()
                    self.copies.append((copy, None))
                else:

                    @pl.when(to != self.fs)
                    def _():
                        copy.start()

                    @pl.when(to == self.fs)
                    def _():
                        self.recv[0, slot] = self.send[0, kind]

                    self.copies.append((copy, to != self.fs))

    def finish(self):
        for t in range(3):
            giver = lax.rem(3 * self.fs + t, self.fs_count)
            for step in range(self.count):
                landed = self.recv.at[step, t]
                wait = pltpu.make_async_copy(landed, landed, self.net.recv.at[self.base + 3 * step + t])
                if step:
                    wait.wait()
                else:

                    @pl.when(giver != self.fs)
                    def _():
                        wait.wait()

            block = self.recv[0, t].astype(F32)
            for step in range(1, self.count):
                block = block + self.recv[step, t].astype(F32)
            self.total[t] = block
        for copy, when in self.copies:
            if when is None:
                copy.wait_send()
            else:

                @pl.when(when)
                def _():
                    copy.wait_send()


class Scatter:
    def __init__(self, net, dp, fs, fs_count, sbuf, rbuf, xsend, xrecv, acc):
        self.net, self.dp, self.fs, self.half = net, dp, fs, fs_count // 2
        self.sbuf, self.rbuf, self.xsend, self.xrecv, self.acc = sbuf, rbuf, xsend, xrecv, acc
        self.first, self.hops, self.slot = {}, {}, 0

    def send_odd(self, j):
        self.first[j] = self.net.start(self.sbuf.at[j], self.rbuf.at[j], (self.dp, flip(self.fs, 1)))

    def join(self, j):
        self.first[j].wait_recv()
        self.acc[j] = self.acc[j] + self.rbuf[j].astype(F32)

    def give(self, j):
        bit = (2 * j) & -(2 * j)
        slot = self.slot
        self.slot += 1
        self.xsend[slot] = self.acc[j].astype(BF)
        self.hops[j] = (self.net.start(self.xsend.at[slot], self.xrecv.at[slot], (self.dp, flip(self.fs, bit))), slot)

    def take(self, j):
        low = j & -j
        copy, slot = self.hops[j]
        copy.wait_recv()
        self.acc[j - low] = self.acc[j - low] + self.xrecv[slot].astype(F32)

    def sent(self):
        for copy in list(self.first.values()) + [copy for copy, _ in self.hops.values()]:
            copy.wait_send()
            self.net.open = [other for other in self.net.open if other is not copy]

    def upper(self):
        if self.half == 2:
            self.give(1)

    def finish(self):
        if self.half == 2:
            self.take(1)
            return
        bit = 1
        while bit < self.half:
            gives = [j for j in range(self.half) if j & bit and not j & (bit - 1)]
            for j in gives:
                self.give(j)
            for j in gives:
                self.take(j)
            bit *= 2


def query_rows(total):
    return QB if total <= 2048 else QB // 2


def backward_one(
    y_count, dp_count, fs_count, da, dfs, n2, hid_in, slope_in, wi, wd, mid, gain_rows, qkv, wo_full, wq, cos, sin, triples, n1, att_rel, tokens, group_b, dgain_b
):
    rows, width = tokens.shape
    total = rows * fs_count
    fj, hd = wi.shape[1], wq.shape[1] // 3
    heads, docs = hd // HEAD, triples.shape[1]
    z_count, rw = dp_count // y_count, width // dp_count
    cb = group_b.shape[1]
    blk, half = query_rows(total), fs_count // 2
    blocks = total // blk
    sems = 96 + 12 * dp_count

    def body(
        da_ref, dfs, n2_hbm, hid_hbm, slope_hbm, wi_ref, wd_ref, mid_hbm, gain_ref, qkv_hbm, wo_ref, wq_ref, cos_hbm, sin_hbm, triples_ref, n1_hbm, att_hbm, tok, gb, dgain_two,
        grad_in, dgain, sum_b, sum_ff, sum_o, sum_q,
        n2_ref, mid_ref, qkv_ref, cos_ref, sin_ref, n1_ref, att_ref, da_low, do_out, do_in, da_out, da_in, hid, slope, dpre, work, qs, ks, kt, dk, dv, dm, cols, g_ff, g_at,
        sbuf, rbuf, xsend, xrecv, acc, yb, zsb, zrb, qsb, qrb, yf, zsf, zrf, ya, zsa, zra, qsa, qra, tiles, send_sem, recv_sem,
        *ps,
    ):
        dp, fs = lax.axis_index("dp"), lax.axis_index("fsdp")
        net = Net(send_sem, recv_sem)
        place = (dp, fs, y_count, z_count, fs_count, rw)
        dqkv = qkv_ref
        loads = {}
        for name, src, dst in (
            ("slope", slope_hbm, slope),
            ("n2", n2_hbm, n2_ref),
            ("hid", hid_hbm, hid),
            ("mid", mid_hbm, mid_ref),
            ("qkv", qkv_hbm, qkv_ref),
            ("att", att_hbm, att_ref),
            ("cos", cos_hbm, cos_ref),
            ("sin", sin_hbm, sin_ref),
            ("n1", n1_hbm, n1_ref),
        ):
            loads[name] = net.local(src, dst)
        barrier = pltpu.get_barrier_semaphore()
        for m in range(z_count):
            for e in range(fs_count):
                if m or e:
                    there = (flip(dp, m * y_count), flip(fs, e))
                    pl.semaphore_signal(barrier, inc=1, device_id=there, device_id_type=MESH)
        for j in range(1, y_count):
            pl.semaphore_signal(barrier, inc=1, device_id=(flip(dp, j), fs), device_id_type=MESH)
        pl.semaphore_wait(barrier, z_count * fs_count - 1 + y_count - 1)

        sum_of_b = RowSum(net, place, gb, yb, zsb, zrb, sum_b, qsb, qrb, sum_q.at[1])
        sum_of_b.start()

        def pull(e, out):
            work[:, 0:fj] = dot_nn(dfs[e], wd_ref[...])

            def one(r):
                at = pl.ds(pl.multiple_of(e * rows + r, HEAD), HEAD)
                dpre[at, :] = (work[pl.ds(r, HEAD), 0:fj] * slope[at, :].astype(F32)).astype(BF)

            row_loop(rows, one)
            out[...] = dot_nt(dpre[e * rows : (e + 1) * rows, :], wi_ref[...]).astype(out.dtype)

        def part_into(scatter, e, fill):
            if e % 2:
                fill(e, scatter.sbuf.at[e // 2])
                scatter.send_odd(e // 2)
            else:
                fill(e, scatter.acc.at[e // 2])

        ff_sum = Scatter(net, dp, fs, fs_count, sbuf, rbuf, xsend, xrecv, acc)
        loads["slope"].wait()

        def both_steps(e):
            part_into(ff_sum, e, pull)

        for j in reversed(range(1, half)):
            both_steps(2 * j + 1)
            both_steps(2 * j)
        for j in range(1, half):
            ff_sum.join(j)
        ff_sum.upper()
        both_steps(1)
        both_steps(0)
        sum_of_b.service(1)
        for m in range(2, z_count):
            sum_of_b.service(m)
        ff_sum.join(0)
        loads["hid"].wait()
        loads["n2"].wait()
        g_ff[:, 0:fj] = dot_tn(n2_ref[...], dpre[...]).astype(BF)
        g_ff[:, fj : 2 * fj] = dot_tn(dfs[...].reshape(total, width), hid[...]).astype(BF)
        sum_of_b.service(0)
        sum_of_ff = RowSum(net, place, g_ff, yf, zsf, zrf, sum_ff)
        sum_of_ff.start()

        loads["qkv"].wait()
        lane_first, lane_end, lane = doc_bounds(triples_ref, docs)
        for r in range(0, total, blk):
            at = slice(r, r + blk)
            q = qkv_ref[at, 0:hd].astype(F32)
            k = qkv_ref[at, hd : 2 * hd].astype(F32)
            row = lax.broadcasted_iota(jnp.int32, (blk, LANES), 0) + r
            inside = (row >= 3 * lane_first) & (row < 3 * lane_end)
            fk = jnp.where(inside, 1.0, 0.0)
            fq = jnp.where(inside | (lane >= docs), 0.0, MASKED)
            head_inputs(qs, ks, at, q, k, fq, fk, heads)
            kt[:, at] = k.T.astype(BF)
            dk[at, :] = jnp.zeros((blk, LANES), F32)
            dv[at, :] = jnp.zeros((blk, LANES), F32)

        def recompute(n):
            r = n * blk
            for h in range(heads):
                e, inv = softmax_block(ks, qs, h, r, r + blk)
                ps[n][h] = (e * inv).astype(BF)

        for n in range(blocks // 2):
            recompute(n)

        ff_sum.finish()
        loads["mid"].wait()
        for r in range(0, rows, LANES):
            at = slice(r, r + LANES)
            dx, dg = layer_norm_back(mid_ref[at, :], gain_ref[1:2, :], acc[0, at, :])
            dx = dx + da_ref[at, :]
            dm[at, :] = dx
            da_low[at, :] = dx.astype(BF)
            dg = jnp.sum(dg, axis=0, keepdims=True)
            gain_two = dg if r == 0 else gain_two + dg
        got = dot_nt(da_low[...], wo_ref[...]).astype(BF)
        for e in range(fs_count):
            do_out[e] = got[:, e * hd : (e + 1) * hd]
            da_out[e] = da_low[:, e * hd : (e + 1) * hd]

        def exchange(blocks_of, landed):
            found = []
            for e in range(1, fs_count):
                found.append(net.start(blocks_of.at[flip(fs, e)], landed.at[e], (dp, flip(fs, e))))
            landed[0] = blocks_of[fs]
            return found

        do_f = exchange(do_out, do_in)
        da_f = exchange(da_out, da_in)
        for n in range(blocks // 2, blocks):
            recompute(n)
        for m in range(1, z_count):
            sum_of_ff.service(m)
        sum_of_ff.service(0)

        place_of = lax.broadcasted_iota(jnp.int32, (blk, LANES), 1) // HEAD
        for r in range(0, total, blk):
            at = slice(r, r + blk)
            q = widen(qkv_ref[at, 0:hd].astype(F32))
            for h in range(heads):
                qs[h, at, :] = jnp.where(place_of == h, q, 0.0).astype(BF)
        lane_head = lax.broadcasted_iota(jnp.int32, (rows, LANES), 1) // HEAD
        for e in range(fs_count):
            if e:
                do_f[e - 1].wait_recv()
            base = pl.multiple_of(flip(fs, e) * rows, 16)
            do = widen(do_in[e].astype(F32))
            for h in range(heads):
                ks[h, pl.ds(base, rows), :] = jnp.where(lane_head == h, do, 0.0).astype(BF)
        for e in range(fs_count):
            if e:
                da_f[e - 1].wait_recv()
            cols[pl.ds(pl.multiple_of(flip(fs, e) * rows, 16), rows), :] = da_in[e]

        loads["att"].wait()
        g_out = dot_tn(att_ref[...], cols[...]).astype(BF)
        for e in range(fs_count):
            base = pl.multiple_of(flip(fs, e) * hd, 16)
            g_at[pl.ds(base, hd), 3 * hd : 4 * hd] = g_out[e * hd : (e + 1) * hd, :]
        sum_of_b.finish()

        loads["cos"].wait()
        loads["sin"].wait()
        for n in range(blocks):
            r, stop = n * blk, (n + 1) * blk
            at = slice(r, stop)
            found = []
            add_k = add_v = None
            for h in range(heads):
                p = ps[n][h]
                v = widen(qkv_ref[0:stop, 2 * hd : 3 * hd])
                grad = dot_nt(v, ks[h, at, :])
                wide = p.astype(F32)
                middle = jnp.sum(wide * grad, axis=0, keepdims=True)
                dr = (wide * (grad - middle) * 0.125).astype(BF)
                part_v = dot_nn(p, ks[h, at, :])
                part_k = dot_nn(dr, qs[h, at, :])
                add_v = part_v if add_v is None else add_v + part_v
                add_k = part_k if add_k is None else add_k + part_k
                found.append(dot_nn(kt[h * HEAD : (h + 1) * HEAD, 0:stop], dr))
            dk[0:stop, :] += add_k
            dv[0:stop, :] += add_v
            dq = jnp.concatenate(found, axis=0).T
            dqkv[at, 0:hd] = (dq * cos_ref[at, :] - partner(dq) * sin_ref[at, :]).astype(BF)
        for r in range(0, total, blk):
            at = slice(r, r + blk)
            grad = dk[at, 0:hd]
            dqkv[at, hd : 2 * hd] = (grad * cos_ref[at, :] - partner(grad) * sin_ref[at, :]).astype(BF)
            dqkv[at, 2 * hd : 3 * hd] = dv[at, 0:hd].astype(BF)
        loads["n1"].wait()
        g_at[:, 0 : 3 * hd] = dot_tn(n1_ref[...], dqkv[...]).astype(BF)
        sum_of_at = RowSum(net, place, g_at, ya, zsa, zra, sum_o, qsa, qra, sum_q.at[0])
        sum_of_at.start()

        ff_sum.sent()
        at_sum = Scatter(net, dp, fs, fs_count, sbuf, rbuf, xsend, xrecv, acc)
        tiles[0] = jnp.zeros((8, width), F32)

        def push_out(e, out):
            base = pl.multiple_of(flip(fs, e) * rows, 16)
            part = dot_nt(dqkv[pl.ds(base, rows), :], wq_ref[...])
            out[...] = part.astype(out.dtype)
            work[:, 0:width] = part
            total_of = jnp.zeros((8, width), F32)
            for r in range(0, rows, HEAD):
                grown = work[r : r + HEAD, 0:width] * n1_ref[pl.ds(base + r, HEAD), :].astype(F32)
                total_of = total_of + jnp.sum(grown.reshape(HEAD // 8, 8, width), axis=0)
            tiles[0] = tiles[0] + total_of

        for e in reversed(range(2, fs_count)):
            part_into(at_sum, e, push_out)
        part_into(at_sum, 1, push_out)
        for j in range(1, half):
            at_sum.join(j)
        at_sum.upper()
        part_into(at_sum, 0, push_out)
        gain_one = jnp.sum(tiles[0], axis=0, keepdims=True) / gain_ref[0:1, :]
        which = lax.broadcasted_iota(jnp.int32, (8, width), 0)
        both = jnp.where(which == 0, gain_one, jnp.where(which == 1, gain_two, 0.0))
        both = jnp.where(which == 2, dgain_two[0:1, :], jnp.where(which == 3, dgain_two[1:2, :], both))
        hops = [(dp, flip(fs, 1 << n)) for n in range(fs_count.bit_length() - 1)]
        hops += [(flip(dp, 1 << n), fs) for n in range(y_count.bit_length() - 1)]

        def hop_out(n, value):
            tiles[1 + n] = value
            return net.start(tiles.at[1 + n], tiles.at[1 + len(hops) + n], hops[n])

        hop = hop_out(0, both)
        sum_of_at.service(1)
        for n in range(1, len(hops) - 1):
            hop.wait_recv()
            both = both + tiles[len(hops) + n]
            hop = hop_out(n, both)
        for m in range(2, z_count):
            sum_of_at.service(m)
        sum_of_at.service(0)
        at_sum.join(0)
        sum_of_ff.finish()
        at_sum.finish()
        last = len(hops) - 1
        hop.wait_recv()
        both = both + tiles[len(hops) + last]
        hop = hop_out(last, both)
        for r in range(0, rows, LANES):
            at = slice(r, r + LANES)
            dx, _ = layer_norm_back(tok[at, :].astype(F32), gain_ref[0:1, :], acc[0, at, :])
            grad_in[at, :] = dx + dm[at, :]
        hop.wait_recv()
        dgain[...] = both + tiles[1 + len(hops) + last]
        sum_of_at.finish()
        net.finish()

    outs = [
        ((rows, width), F32),
        ((8, width), F32),
        ((rw, cb - 3 * hd), F32),
        ((rw, 2 * fj), F32),
        ((rw, hd), F32),
        ((2, 3, rw, hd), F32),
    ]
    wide = max(width, fj)
    zy = (y_count - 1, z_count, rw)
    scratch = [
        ((total, width), BF),
        ((rows, width), F32),
        ((total, 3 * hd), BF),
        ((total, hd), F32),
        ((total, hd), F32),
        ((total, width), BF),
        ((total, width), BF),
        ((rows, width), BF),
        ((fs_count, rows, hd), BF),
        ((fs_count, rows, hd), BF),
        ((fs_count, rows, hd), BF),
        ((fs_count, rows, hd), BF),
        ((total, fj), BF),
        ((total, fj), BF),
        ((total, fj), BF),
        ((rows, wide), F32),
        ((heads, total, LANES), BF),
        ((heads, total, LANES), BF),
        ((hd, total), BF),
        ((total, LANES), F32),
        ((total, LANES), F32),
        ((rows, width), F32),
        ((total, hd), BF),
        ((width, 2 * fj), BF),
        ((width, 4 * hd), BF),
        ((half, rows, width), BF),
        ((half, rows, width), BF),
        ((half - 1, rows, width), BF),
        ((half - 1, rows, width), BF),
        ((half, rows, width), F32),
        (zy + (cb,), BF),
        ((z_count - 1, rw, cb - 3 * hd), BF),
        ((z_count - 1, rw, cb - 3 * hd), BF),
        ((z_count, 3, rw, hd), BF),
        ((z_count, 3, rw, hd), BF),
        (zy + (2 * fj,), BF),
        ((z_count - 1, rw, 2 * fj), BF),
        ((z_count - 1, rw, 2 * fj), BF),
        (zy + (4 * hd,), BF),
        ((z_count - 1, rw, hd), BF),
        ((z_count - 1, rw, hd), BF),
        ((z_count, 3, rw, hd), BF),
        ((z_count, 3, rw, hd), BF),
        ((2 * (fs_count.bit_length() + y_count.bit_length() - 2) + 1, 8, width), F32),
    ]
    tail = [pltpu.VMEM((heads, (n + 1) * blk, blk), BF) for n in range(blocks)]
    arrays = (da, dfs, n2, hid_in, slope_in, wi, wd, mid, gain_rows, qkv, wo_full, wq, cos, sin, triples, n1, att_rel, tokens, group_b, dgain_b)
    return pl.pallas_call(
        body,
        out_shape=[jax.ShapeDtypeStruct(s, t) for s, t in outs],
        in_specs=[hbm() if n in (2, 3, 4, 7, 9, 12, 13, 15, 16) else smem() if n == 14 else vmem() for n in range(20)],
        out_specs=[vmem()] * len(outs),
        scratch_shapes=[pltpu.VMEM(s, t) for s, t in scratch] + [pltpu.SemaphoreType.DMA((sems,))] * 2 + tail,
        compiler_params=pltpu.CompilerParams(collective_id=4, has_side_effects=True, vmem_limit_bytes=VMEM_BYTES),
        cost_estimate=cost(4e10, 3e7),
        name="backward_one",
    )(*arrays)


def middle(y_count, dp_count, fs_count, s0, after, z_blocks, cot, c_rel, wq, wu, weights, wp, gain_rows, cos, sin, triples):
    short, width = s0.shape
    rows, total = short * 3, short * fs_count
    hd = wq.shape[1] // 3
    pc = wp.shape[2]
    wout, win, wdown = weights
    fj, rw = win.shape[2], win.shape[1]
    z_count = dp_count // y_count
    heads, docs = hd // HEAD, triples.shape[1]
    blk = min(QB, total)
    blocks, half = total // blk, fs_count // 2
    cb = 4 * hd + 2 * pc
    sems = 96 + 16 * fs_count + 6 * dp_count

    def body(
        s0_ref, after_ref, z_ref, cot_ref, c_ref, wq_ref, wu_ref, o_in, i_in, d_in, wp_ref, gain_ref, cos_ref, sin_ref, triples_ref,
        out, da, dfs_out, group, sum_ff, dgain,
        wos, wi_ref, wd_ref, g_ff, yg, zsg, zrg, sd, rd, xd, yd, ad, lift_send, lift_rel,
        s0s, x_all, wo_at, hold, turned, z_rel, dfs, df_all, do_out, do_in, da_out, da_in, cols, s1s, ds0s, nxt,
        n1, n2, qkv, att, att_rel, qs, ks, vt, kt, dk, dv, dqkv, work, hid, slope, dpre, m_all, dm,
        sf, rf, xf, yf, af, sb, rb, xb, yb, ab, sa, ra, xa, ya, aa, thin, spread_rows, lift, send_sem, recv_sem, *ps,
    ):
        dp, fs = lax.axis_index("dp"), lax.axis_index("fsdp")
        net = Net(send_sem, recv_sem)

        def base_of(e, amount):
            return pl.multiple_of(flip(fs, e) * amount, 16)

        def spread(pieces, src=None):
            return Flight(net, dp, fs, fs_count, pieces, pieces.at[0] if src is None else src)

        s0s[0] = s0_ref[...].astype(BF)
        nxt[...] = jnp.zeros(nxt.shape, BF)
        here = pl.ds(pl.multiple_of(dp * rw, 16), rw)
        wos[0, here, :] = o_in[1].astype(BF)
        wi_ref[here, :] = i_in[1].astype(BF)
        wd_ref[here, :] = d_in[1].astype(BF)
        barrier = pltpu.get_barrier_semaphore()
        for e in range(1, fs_count):
            pl.semaphore_signal(barrier, inc=1, device_id=(dp, flip(fs, e)), device_id_type=MESH)
        others = [m * y_count for m in range(1, z_count)] + list(range(1, y_count))
        for step in others:
            pl.semaphore_signal(barrier, inc=1, device_id=(flip(dp, step), fs), device_id_type=MESH)
        pl.semaphore_wait(barrier, fs_count - 1 + len(others))

        def of(buf, step):
            return buf.at[pl.ds(pl.multiple_of(flip(dp, step) * rw, 16), rw), :]

        def along_z(buf):
            return [
                net.start(of(buf, 0), of(buf, 0), (flip(dp, m * y_count), fs)) for m in range(1, z_count)
            ]

        def along_y(buf, m):
            return [
                net.start(of(buf, m * y_count), of(buf, m * y_count), (flip(dp, n), fs)) for n in range(1, y_count)
            ]

        def pass_on(buf, came, passed):
            for m in range(1, z_count):
                came[m - 1].wait_recv()
                passed += along_y(buf, m)

        def wait_all(copies):
            for copy in copies:
                copy.wait_recv()

        s0_f = spread(s0s)
        came = [along_z(buf) for buf in (wos.at[0], wi_ref, wd_ref)]
        passed = [along_y(buf, 0) for buf in (wos.at[0], wi_ref, wd_ref)]

        dsum = Scatter(net, dp, fs, fs_count, sd, rd, xd, yd, ad)
        for e in reversed(range(fs_count)):
            part = dot_nt(c_ref[e], wu_ref[...])
            if e % 2:
                sd[e // 2] = part.astype(BF)
                dsum.send_odd(e // 2)
            else:
                ad[e // 2] = part

        def exchange(blocks_of, landed):
            found = []
            for e in range(1, fs_count):
                found.append(net.start(blocks_of.at[flip(fs, e)], landed.at[e], (dp, flip(fs, e))))
            landed[0] = blocks_of[fs]
            return found

        lane_first, lane_end, lane = doc_bounds(triples_ref, docs)
        for n in range(1, half):
            dsum.join(n)
        dsum.upper()
        s0_f.relay()
        pass_on(wos.at[0], came[0], passed[0])
        for e in range(fs_count):
            s0_f.ready(e)
            at = pl.ds(base_of(e, short), short)
            value = s0_ref[...] if e == 0 else s0s[e].astype(F32)
            x_all[at, :] = value
            n1[at, :] = layer_norm(value, gain_ref[2:3, :]).astype(BF)
        for r in range(0, total, blk):
            at = slice(r, r + blk)
            got = dot_nn(n1[at, :], wq_ref[...])
            q, k, v = got[:, :hd], got[:, hd : 2 * hd], got[:, 2 * hd :]
            q = (q * cos_ref[at, :] + partner(q) * sin_ref[at, :]).astype(BF)
            k = (k * cos_ref[at, :] + partner(k) * sin_ref[at, :]).astype(BF)
            qkv[at, 0:hd] = q
            qkv[at, hd : 2 * hd] = k
            qkv[at, 2 * hd : 3 * hd] = v.astype(BF)
            row = lax.broadcasted_iota(jnp.int32, (blk, LANES), 0) + r
            inside = (row >= lane_first) & (row < lane_end)
            fk = jnp.where(inside, 1.0, 0.0)
            fq = jnp.where(inside | (lane >= docs), 0.0, MASKED)
            head_inputs(qs, ks, at, q.astype(F32), k.astype(F32), fq, fk, heads)
            vt[:, at] = v.T.astype(BF)
            kt[:, at] = k.astype(F32).T.astype(BF)
            dk[at, :] = jnp.zeros((blk, LANES), F32)
            dv[at, :] = jnp.zeros((blk, LANES), F32)
        dsum.join(0)
        dsum.finish()
        dm[...] = ad[0]
        dfs[0] = ad[0].astype(BF)
        df_f = spread(dfs)
        wait_all(passed[0])
        wo_f = spread(wos, wos.at[0])
        flights = []
        for n in range(blocks):
            r, stop = n * blk, (n + 1) * blk
            found = []
            for h in range(heads):
                e, inv = softmax_block(ks, qs, h, r, stop)
                ps[n][h] = (e * inv).astype(BF)
                found.append(dot_nn(vt[h * HEAD : (h + 1) * HEAD, 0:stop], ps[n][h]))
            att[0, r:stop, :] = jnp.concatenate(found, axis=0).T.astype(BF)
            flights.append(spread(att.at[:, r:stop, :], att.at[0, r:stop, :]))
            if n == 0:
                pass_on(wi_ref, came[1], passed[1])
                df_f.relay()
                wo_f.relay()
        place_of = lax.broadcasted_iota(jnp.int32, (blk, LANES), 1) // HEAD
        for r in range(0, total, blk):
            at = slice(r, r + blk)
            q = widen(qkv[at, 0:hd].astype(F32))
            for h in range(heads):
                qs[h, at, :] = jnp.where(place_of == h, q, 0.0).astype(BF)

        pass_on(wd_ref, came[2], passed[2])
        wo_f.all_ready()
        for e in range(fs_count):
            wo_at[flip(fs, e)] = wos[e]
        for e in range(fs_count):
            hold[:, e * hd : (e + 1) * hd] = wo_at[e]
        for e in range(fs_count):
            turned[e * hd : (e + 1) * hd, :] = hold[pl.ds(base_of(e, hd), hd), :]
        for flight in flights:
            flight.relay()
        for flight in flights:
            flight.all_ready()
        for e in range(fs_count):
            att_rel[:, e * hd : (e + 1) * hd] = att[e]

        work[:, 0:width] = x_all[...] + dot_nn(att_rel[...], turned[...])

        def norm_all(r):
            at = pl.ds(r, HEAD)
            m = work[at, 0:width]
            m_all[at, :] = m
            n2[at, :] = layer_norm(m, gain_ref[3:4, :]).astype(BF)

        row_loop(total, norm_all)
        wait_all(passed[1])
        work[:, 0:fj] = dot_nn(n2[...], wi_ref[...])

        def activate_all(r):
            at = pl.ds(r, HEAD)
            value, rate = gelu_both(work[at, 0:fj])
            hid[at, :] = value.astype(BF)
            slope[at, :] = rate

        row_loop(total, activate_all)
        wait_all(passed[2])
        work[:, 0:width] = dot_nt(hid[...], wd_ref[...])

        def give_out(scatter, source):
            for e in reversed(range(fs_count)):
                value = source[pl.ds(base_of(e, short), short), 0:width]
                if e % 2:
                    scatter.sbuf[e // 2] = value.astype(BF)
                    scatter.send_odd(e // 2)
                else:
                    scatter.acc[e // 2] = value

        fwd = Scatter(net, dp, fs, fs_count, sf, rf, xf, yf, af)
        give_out(fwd, work)
        for e in range(fs_count):
            df_f.ready(e)
            df_all[pl.ds(base_of(e, short), short), :] = dfs[e]
        work[:, 0:fj] = dot_nn(df_all[...], wd_ref[...])

        def pull_all(r):
            at = pl.ds(r, HEAD)
            dpre[at, :] = (work[at, 0:fj] * slope[at, :]).astype(BF)

        row_loop(total, pull_all)
        work[:, 0:width] = dot_nt(dpre[...], wi_ref[...])
        bwd = Scatter(net, dp, fs, fs_count, sb, rb, xb, yb, ab)
        give_out(bwd, work)
        for j in range(1, half):
            bwd.join(j)
        bwd.upper()
        for j in range(1, half):
            fwd.join(j)
        fwd.upper()
        g_ff[:, 0:fj] = dot_tn(n2[...], dpre[...]).astype(BF)
        g_ff[:, fj : 2 * fj] = dot_tn(df_all[...], hid[...]).astype(BF)
        ff_rows = RowSum(net, (dp, fs, y_count, z_count, fs_count, rw), g_ff, yg, zsg, zrg, sum_ff)
        ff_rows.start()
        bwd.join(0)
        bwd.finish()
        m_own = m_all[pl.ds(base_of(0, short), short), :]
        dx, dg = layer_norm_back(m_own, gain_ref[3:4, :], ab[0])
        dx = dx + dm[...]
        dm[...] = dx
        low_dx = dx.astype(BF)
        got = dot_nt(low_dx, hold[...]).astype(BF)
        for e in range(fs_count):
            do_out[e] = got[:, e * hd : (e + 1) * hd]
            da_out[e] = low_dx[:, e * hd : (e + 1) * hd]
        do_f = exchange(do_out, do_in)
        da_f = exchange(da_out, da_in)
        gain_two = jnp.sum(dg, axis=0, keepdims=True)

        fwd.join(0)
        fwd.finish()
        s1s[0] = (m_own + af[0]).astype(BF)
        s1_f = spread(s1s)
        z_f = exchange(z_ref, z_rel)
        wait_all(do_f)
        for e in range(fs_count):
            at = pl.ds(base_of(e, short), short)
            do = widen(do_in[e].astype(F32))
            lane_head = lax.broadcasted_iota(jnp.int32, (short, LANES), 1) // HEAD
            for h in range(heads):
                ks[h, at, :] = jnp.where(lane_head == h, do, 0.0).astype(BF)
        wait_all(da_f)
        for e in range(fs_count):
            cols[pl.ds(base_of(e, short), short), :] = da_in[e]
        s1_f.relay()

        g_out = dot_tn(att_rel[...], cols[...]).astype(BF)
        for e in range(fs_count):
            group[pl.ds(base_of(e, hd), hd), cb - hd : cb] = g_out[e * hd : (e + 1) * hd, :]
        for n in range(blocks):
            r, stop = n * blk, (n + 1) * blk
            at = slice(r, stop)
            found = []
            add_k = add_v = None
            for h in range(heads):
                p = ps[n][h]
                grad = dot_nt(widen(qkv[0:stop, 2 * hd : 3 * hd]), ks[h, at, :])
                wide = p.astype(F32)
                inner = jnp.sum(wide * grad, axis=0, keepdims=True)
                dr = (wide * (grad - inner) * 0.125).astype(BF)
                part_v = dot_nn(p, ks[h, at, :])
                part_k = dot_nn(dr, qs[h, at, :])
                add_v = part_v if add_v is None else add_v + part_v
                add_k = part_k if add_k is None else add_k + part_k
                found.append(dot_nn(kt[h * HEAD : (h + 1) * HEAD, 0:stop], dr))
            dk[0:stop, :] += add_k
            dv[0:stop, :] += add_v
            dq = jnp.concatenate(found, axis=0).T
            dqkv[at, 0:hd] = (dq * cos_ref[at, :] - partner(dq) * sin_ref[at, :]).astype(BF)
        for r in range(0, total, blk):
            at = slice(r, r + blk)
            grad = dk[at, 0:hd]
            dqkv[at, hd : 2 * hd] = (grad * cos_ref[at, :] - partner(grad) * sin_ref[at, :]).astype(BF)
            dqkv[at, 2 * hd : 3 * hd] = dv[at, 0:hd].astype(BF)
        work[:, 0:width] = dot_nt(dqkv[...], wq_ref[...])
        first = Scatter(net, dp, fs, fs_count, sa, ra, xa, ya, aa)
        give_out(first, work)
        for j in range(1, half):
            first.join(j)
        first.upper()
        group[:, 0 : 3 * hd] = dot_tn(n1[...], dqkv[...]).astype(BF)
        s1_f.all_ready()
        lift_f = []
        for e in range(fs_count):
            part = dot_nn(s1s[e], wu_ref[...]).astype(BF)
            if e:
                lift_send[e] = part
                lift_f.append(net.start(lift_send.at[e], lift_rel.at[e], (dp, flip(fs, e))))
            else:
                lift_rel[0] = part
        g_up = jnp.zeros((width, pc), F32)
        for e in range(fs_count):
            g_up = g_up + dot_tn(s1s[e], c_ref[e])
        group[:, 3 * hd + pc : 3 * hd + 2 * pc] = g_up.astype(BF)
        for m in range(1, z_count):
            ff_rows.service(m)
        first.join(0)
        first.finish()
        dx, dg = layer_norm_back(s0_ref[...], gain_ref[2:3, :], aa[0])
        ds0s[0] = (dx + dm[...]).astype(BF)
        gain_one = jnp.sum(dg, axis=0, keepdims=True)
        which = lax.broadcasted_iota(jnp.int32, (8, width), 0)
        dgain[...] = jnp.where(which == 0, gain_one, jnp.where(which == 1, gain_two, 0.0))

        hop = net.make(ds0s.at[0, 0:HALO, :], nxt, (dp, lax.rem(fs + fs_count - 1, fs_count)))

        @pl.when(fs > 0)
        def _():
            hop.start()

        ds0_f = spread(ds0s)
        row = lax.broadcasted_iota(jnp.int32, (short, LANES), 0) + fs * short + 1
        shut = jnp.max(jnp.where((row == lane_first) | (row >= total), 1.0, 0.0), axis=1, keepdims=True) > 0.0

        @pl.when(fs < fs_count - 1)
        def _():
            hop.wait_recv()

        grad = jnp.concatenate([ds0s[0], nxt[...]], axis=0)
        for e in range(fs_count):
            lift_at = dot_nn(grad, wp_ref[e])
            spread_rows[flip(fs, e)] = lift_at
        dz = jnp.concatenate([spread_rows[e] for e in range(fs_count)], axis=1)
        strided_write(thin, 0, short, dz[0:short, 2 * width : 3 * width])
        for k in range(2):
            part = dz[1 : short + 1, k * width : (k + 1) * width]
            strided_write(thin, k + 1, short, jnp.where(shut, 0.0, part))
        value = cot_ref[...].astype(F32) + spread_read(thin)
        da[...] = value
        dfs_out[0] = value.astype(BF)
        out_f = spread(dfs_out)
        ff_rows.service(0)
        ds0_f.relay()
        for copy in z_f:
            copy.wait_recv()
        g_pool = jnp.zeros((width, pc), F32)
        for e in range(fs_count):
            ds0_f.ready(e)
            g_pool = g_pool + dot_tn(ds0s[e], z_rel[e])
        group[:, 3 * hd : 3 * hd + pc] = g_pool.astype(BF)

        wait_all(lift_f)
        for e in range(fs_count):
            lift[flip(fs, e)] = lift_rel[e].astype(F32)
        lifted = jnp.concatenate([lift[e] for e in range(fs_count)], axis=1)
        for n in range(3):
            strided_write(thin, n, short, lifted[:, n * width : (n + 1) * width])
        out[...] = (after_ref[...] + spread_read(thin)).astype(BF)
        ff_rows.finish()
        out_f.relay()
        out_f.all_ready()

        @pl.when(fs > 0)
        def _():
            hop.wait_send()

        net.finish()

    wide = max(width, fj)
    pieces = (fs_count, short, width)
    scatter = [((half, short, width), BF)] * 2 + [((half - 1, short, width), BF)] * 2 + [((half, short, width), F32)]
    outs = [((rows, width), BF), ((rows, width), F32), ((fs_count, rows, width), BF), ((width, cb), BF), ((rw, 2 * fj), F32), ((8, width), F32)]
    scratch = [
        ((fs_count, width, hd), BF),
        ((width, fj), BF),
        ((width, fj), BF),
        ((width, 2 * fj), BF),
        ((y_count - 1, z_count, rw, 2 * fj), BF),
        ((z_count - 1, rw, 2 * fj), BF),
        ((z_count - 1, rw, 2 * fj), BF),
        *scatter,
        ((fs_count, short, pc), BF),
        ((fs_count, short, pc), BF),
        (pieces, BF),
        ((total, width), F32),
        ((fs_count, width, hd), BF),
        ((width, width), BF),
        ((width, width), BF),
        ((fs_count, short, pc), BF),
        (pieces, BF),
        ((total, width), BF),
        ((fs_count, short, hd), BF),
        ((fs_count, short, hd), BF),
        ((fs_count, short, hd), BF),
        ((fs_count, short, hd), BF),
        ((total, hd), BF),
        (pieces, BF),
        (pieces, BF),
        ((HALO, width), BF),
        ((total, width), BF),
        ((total, width), BF),
        ((total, 3 * hd), BF),
        ((fs_count, total, hd), BF),
        ((total, width), BF),
        ((heads, total, LANES), BF),
        ((heads, total, LANES), BF),
        ((hd, total), BF),
        ((hd, total), BF),
        ((total, LANES), F32),
        ((total, LANES), F32),
        ((total, 3 * hd), BF),
        ((total, wide), F32),
        ((total, fj), BF),
        ((total, fj), F32),
        ((total, fj), BF),
        ((total, width), F32),
        ((short, width), F32),
        *scatter,
        *scatter,
        *scatter,
        ((width // LANES, rows, LANES), F32),
        ((fs_count, short + HALO, pc), F32),
        ((fs_count, short, pc), F32),
    ]
    tail = [pltpu.VMEM((heads, (n + 1) * blk, blk), BF) for n in range(blocks)]
    arrays = (s0, after, z_blocks, cot, c_rel, wq, wu, wout, win, wdown, wp, gain_rows, cos, sin, triples)
    return pl.pallas_call(
        body,
        out_shape=[jax.ShapeDtypeStruct(s, t) for s, t in outs],
        in_specs=[vmem()] * 14 + [smem()],
        out_specs=[vmem()] * len(outs),
        scratch_shapes=[pltpu.VMEM(s, t) for s, t in scratch] + [pltpu.SemaphoreType.DMA((sems,))] * 2 + tail,
        compiler_params=pltpu.CompilerParams(collective_id=2, has_side_effects=True, vmem_limit_bytes=VMEM_BYTES),
        cost_estimate=cost(2e10, 2e7),
        name="middle",
    )(*arrays)


def owners_of(amount, dp_count, fs_count):
    found = []
    half = dp_count // 2
    for k in range(amount):
        found.append((dp_count // 4 + k % half, (2 * (k // half)) % fs_count + (2 * (k // half)) // fs_count))
    return found


def round_up(width):
    return -(-width // LANES) * LANES


def newton_schulz(box, x, norm, count, width, dp_count, rw, done):
    coef_a, coef_b, coef_c = NS_COEFS
    rows = dp_count * rw
    square = jnp.zeros((1, 1), F32)
    for at in range(count):
        block = box[at * dp_count : (at + 1) * dp_count, :, 0:width].reshape(rows, width)
        x[:, at * width : (at + 1) * width] = block
        wide = block.astype(F32)
        square = square + jnp.sum(jnp.sum(wide * wide, axis=0, keepdims=True), axis=1, keepdims=True)
    length = jnp.sqrt(square)
    norm[...] = jnp.broadcast_to(length, norm.shape)
    scale = 1.0 / (length + NORM_EPS)
    span = count * width
    for turn in range(NS_STEPS):
        gram = dot_nt(x[:, 0:span], x[:, 0:span])
        if turn == 0:
            gram = gram * (scale * scale)
        gram = gram.astype(BF)
        poly = (coef_b * gram.astype(F32) + coef_c * dot_nn(gram, gram)).astype(BF)
        for at in range(count):
            here = slice(at * width, (at + 1) * width)
            block = x[:, here]
            new = coef_a * block.astype(F32) + dot_nn(poly, block)
            if turn == 0:
                new = new * scale
            if turn < NS_STEPS - 1:
                x[:, here] = new.astype(BF)
            else:
                box[at * dp_count : (at + 1) * dp_count, :, 0:width] = new.astype(BF).reshape(dp_count, rw, width)
                done(at)


def muon(y_count, dp_count, fs_count, sums, moments, dgain):
    sum_q, sum_o, sum_ff, sum_ff1, sum_rest = sums
    rw, hd = sum_o.shape
    fj = sum_ff.shape[1] // 2
    pc = moments[4].shape[1]
    width = rw * dp_count
    z_count = dp_count // y_count
    devices = dp_count * fs_count
    widths = [fj, fj, fj, fj, 3 * hd, 3 * hd, pc, pc, hd, hd]
    widths = [round_up(w) for w in widths]
    amount, wide = len(widths), max(widths)
    owners = owners_of(amount, dp_count, fs_count)
    classes = sorted(set(widths))
    sems = 16
    z_bits = z_count.bit_length() - 1

    def body(
        q_ref, o_ref, ff_ref, ff1_ref, rest_ref, mq, mo, mi, md, mp, mu, ga,
        out, norms, dgain_out, box, x, norm, tiles, tsend, *rest_refs,
    ):
        pieces = rest_refs[:amount]
        send_sem, recv_sem, push_send, push_recv, give_send, give_recv, norm_send, norm_recv = rest_refs[amount:]
        dp, fs = lax.axis_index("dp"), lax.axis_index("fsdp")
        slot = fs * dp_count + dp
        net = Net(send_sem, recv_sem)

        def put(k, value):
            have = value.shape[1]
            if have < widths[k]:
                value = jnp.concatenate([value, jnp.zeros((rw, widths[k] - have), F32)], axis=1)
            pieces[k][...] = value.astype(BF)

        at = 2 * pc
        put(0, MOMENT_DECAY * mi[0] + ff_ref[:, 0:fj])
        put(1, MOMENT_DECAY * mi[1] + ff1_ref[:, 0:fj])
        put(2, MOMENT_DECAY * md[0] + ff_ref[:, fj : 2 * fj])
        put(3, MOMENT_DECAY * md[1] + ff1_ref[:, fj : 2 * fj])
        for b in range(2):
            put(4 + b, MOMENT_DECAY * mq[b] + jnp.concatenate([q_ref[b, t] for t in range(3)], axis=1))
        put(6, MOMENT_DECAY * mp[...] + rest_ref[:, 0:pc])
        put(7, MOMENT_DECAY * mu[...] + rest_ref[:, pc : 2 * pc])
        put(8, MOMENT_DECAY * mo[0] + o_ref[...])
        put(9, MOMENT_DECAY * mo[1] + rest_ref[:, at:])
        if any(w != wide for w in widths):
            box[...] = jnp.zeros(box.shape, BF)

        barrier = pltpu.get_barrier_semaphore()

        def greet(t, carry):
            @pl.when(t != slot)
            def _():
                there = (lax.rem(t, dp_count), lax.div(t, dp_count))
                pl.semaphore_signal(barrier, inc=1, device_id=there, device_id_type=MESH)

            return carry

        lax.fori_loop(0, devices, greet, 0)
        pl.semaphore_wait(barrier, devices - 1)

        mine = [(dp == owners[k][0]) & (fs == owners[k][1]) for k in range(amount)]
        for k in range(amount):
            copy = pltpu.make_async_remote_copy(
                src_ref=pieces[k],
                dst_ref=box.at[slot, :, 0 : widths[k]],
                send_sem=push_send.at[k],
                recv_sem=push_recv,
                device_id=owners[k],
                device_id_type=MESH,
            )

            @pl.when(jnp.logical_not(mine[k]))
            def _():
                copy.start()

            @pl.when(mine[k])
            def _():
                box[slot, :, 0 : widths[k]] = pieces[k][...]

        total = ga[...]
        for n in range(z_bits):
            tsend[n] = total
            hop = net.start(tsend.at[n], tiles.at[n], (flip(dp, y_count << n), fs))
            hop.wait_recv()
            total = total + tiles[n]
        dgain_out[...] = total

        for k in range(amount):

            @pl.when(mine[k])
            def _():
                landed = box.at[0 : devices - 1, :, 0 : widths[k]]
                pltpu.make_async_copy(landed, landed, push_recv).wait()

        which_k = jnp.int32(0)
        for k in range(1, amount):
            which_k = which_k + k * mine[k].astype(jnp.int32)
        for w in classes:
            chosen = None
            for k in range(amount):
                if widths[k] == w:
                    chosen = mine[k] if chosen is None else chosen | mine[k]

            @pl.when(chosen)
            def _():
                def done(block):
                    def give(i, carry):
                        t = block * dp_count + i

                        @pl.when(t != slot)
                        def _():
                            pltpu.make_async_remote_copy(
                                src_ref=box.at[t, :, 0:w],
                                dst_ref=out.at[which_k, :, 0:w],
                                send_sem=give_send,
                                recv_sem=give_recv.at[which_k],
                                device_id=(i, block),
                                device_id_type=MESH,
                            ).start()
                            pltpu.make_async_remote_copy(
                                src_ref=norm,
                                dst_ref=norms.at[which_k],
                                send_sem=norm_send,
                                recv_sem=norm_recv.at[which_k],
                                device_id=(i, block),
                                device_id_type=MESH,
                            ).start()

                        return carry

                    lax.fori_loop(0, dp_count, give, 0)

                newton_schulz(box, x, norm, fs_count, w, dp_count, rw, done)
                out[which_k, :, 0:w] = box[slot, :, 0:w]
                norms[which_k] = norm[...]

        for k in range(amount):
            w = widths[k]

            @pl.when(jnp.logical_not(mine[k]))
            def _():
                landed = out.at[k, :, 0:w]
                pltpu.make_async_copy(landed, landed, give_recv.at[k]).wait()
                pltpu.make_async_copy(norms.at[k], norms.at[k], norm_recv.at[k]).wait()
                pltpu.make_async_copy(pieces[k], pieces[k], push_send.at[k]).wait()

            @pl.when(mine[k])
            def _():
                left = box.at[0 : devices - 1, :, 0:w]
                pltpu.make_async_copy(left, left, give_send).wait()

                def drain(t, carry):
                    pltpu.make_async_copy(norm, norm, norm_send).wait()
                    return carry

                lax.fori_loop(0, devices - 1, drain, 0)

        net.finish()

    outs = [((amount, rw, wide), BF), ((amount, 8, LANES), F32), ((8, width), F32)]
    scratch = [
        ((devices, rw, wide), BF),
        ((width, fs_count * wide), BF),
        ((8, LANES), F32),
        ((z_bits, 8, width), F32),
        ((z_bits, 8, width), F32),
    ] + [((rw, w), BF) for w in widths]
    dma = pltpu.SemaphoreType.DMA
    return pl.pallas_call(
        body,
        out_shape=[jax.ShapeDtypeStruct(s, t) for s, t in outs],
        in_specs=[vmem()] * 12,
        out_specs=[vmem()] * len(outs),
        scratch_shapes=[pltpu.VMEM(s, t) for s, t in scratch]
        + [dma((sems,)), dma((sems,)), dma((amount,)), dma, dma, dma((amount,)), dma, dma((amount,))],
        compiler_params=pltpu.CompilerParams(collective_id=1, has_side_effects=True, vmem_limit_bytes=VMEM_BYTES),
        name="muon",
    )(sum_q, sum_o, sum_ff, sum_ff1, sum_rest, *moments, dgain)


def backward_all(
    y_count, dp_count, fs_count, da, dfs, n2, hid_in, slope_in, wi, wd, mid, gain_rows, qkv, wo_full, wq, cos, sin, triples, n1, att_rel, tokens, group_b, dgain_b,
    sum_ff1, moments,
):
    rows, width = tokens.shape
    total = rows * fs_count
    fj, hd = wi.shape[1], wq.shape[1] // 3
    heads, docs = hd // HEAD, triples.shape[1]
    z_count, rw = dp_count // y_count, width // dp_count
    cb = group_b.shape[1]
    blk, half = query_rows(total), fs_count // 2
    blocks = total // blk
    sems = 96 + 16 * dp_count

    pc = moments[4].shape[1]
    devices = dp_count * fs_count
    widths = [round_up(w) for w in (fj, fj, fj, fj, 3 * hd, 3 * hd, pc, pc, hd, hd)]
    amount, wide = len(widths), max(widths)
    owners = owners_of(amount, dp_count, fs_count)
    classes = sorted(set(widths))

    def body(
        da_ref, dfs, n2_hbm, hid_hbm, slope_hbm, wi_ref, wd_ref, mid_hbm, gain_ref, qkv_hbm, wo_ref, wq_ref, cos_hbm, sin_hbm, triples_ref, n1_hbm, att_hbm, tok, gb, dgain_two, ff1_ref, mq, mo, mi, md, mp, mu,
        grad_in, dgain_out, sum_b, sum_ff, sum_o, sum_q, out, norms,
        n2_ref, mid_ref, qkv_ref, cos_ref, sin_ref, n1_ref, att_ref, da_low, do_out, do_in, da_out, da_in, hid, slope, dpre, work, qs, ks, kt, dk, dv, dm, cols, g_ff, g_at, g_o,
        sbuf, rbuf, xsend, xrecv, acc, yb, zsb, zrb, qsb, qrb, yf, zsf, zrf, yo, zso, zro, qsa, qra, tiles,
        box, x, norm, send_sem, recv_sem, push_send, push_recv, give_send, give_recv, norm_send, norm_recv,
        *rest,
    ):
        ps, pieces = rest[:blocks], rest[blocks:]
        dp, fs = lax.axis_index("dp"), lax.axis_index("fsdp")
        net = Net(send_sem, recv_sem)
        place = (dp, fs, y_count, z_count, fs_count, rw)
        dqkv = qkv_ref
        loads = {}
        for name, src, dst in (
            ("slope", slope_hbm, slope),
            ("n2", n2_hbm, n2_ref),
            ("hid", hid_hbm, hid),
            ("mid", mid_hbm, mid_ref),
            ("qkv", qkv_hbm, qkv_ref),
            ("att", att_hbm, att_ref),
            ("cos", cos_hbm, cos_ref),
            ("sin", sin_hbm, sin_ref),
            ("n1", n1_hbm, n1_ref),
        ):
            loads[name] = net.local(src, dst)
        barrier = pltpu.get_barrier_semaphore()
        slot = fs * dp_count + dp

        def greet(t, carry):
            @pl.when(t != slot)
            def _():
                there = (lax.rem(t, dp_count), lax.div(t, dp_count))
                pl.semaphore_signal(barrier, inc=1, device_id=there, device_id_type=MESH)

            return carry

        lax.fori_loop(0, devices, greet, 0)
        pl.semaphore_wait(barrier, devices - 1)

        mine = [(dp == owners[k][0]) & (fs == owners[k][1]) for k in range(amount)]

        def push(k, value):
            have = value.shape[1]
            if have < widths[k]:
                value = jnp.concatenate([value, jnp.zeros((rw, widths[k] - have), F32)], axis=1)
            pieces[k][...] = value.astype(BF)
            copy = pltpu.make_async_remote_copy(
                src_ref=pieces[k],
                dst_ref=box.at[slot, :, 0 : widths[k]],
                send_sem=push_send.at[k],
                recv_sem=push_recv,
                device_id=owners[k],
                device_id_type=MESH,
            )

            @pl.when(jnp.logical_not(mine[k]))
            def _():
                copy.start()

            @pl.when(mine[k])
            def _():
                box[slot, :, 0 : widths[k]] = pieces[k][...]

        sum_of_b = RowSum(net, place, gb, yb, zsb, zrb, sum_b, qsb, qrb, sum_q.at[1])
        sum_of_b.start()

        def pull(e, out):
            work[:, 0:fj] = dot_nn(dfs[e], wd_ref[...])

            def one(r):
                at = pl.ds(pl.multiple_of(e * rows + r, HEAD), HEAD)
                dpre[at, :] = (work[pl.ds(r, HEAD), 0:fj] * slope[at, :].astype(F32)).astype(BF)

            row_loop(rows, one)
            out[...] = dot_nt(dpre[e * rows : (e + 1) * rows, :], wi_ref[...]).astype(out.dtype)

        def part_into(scatter, e, fill):
            if e % 2:
                fill(e, scatter.sbuf.at[e // 2])
                scatter.send_odd(e // 2)
            else:
                fill(e, scatter.acc.at[e // 2])

        ff_sum = Scatter(net, dp, fs, fs_count, sbuf, rbuf, xsend, xrecv, acc)
        loads["slope"].wait()

        def both_steps(e):
            part_into(ff_sum, e, pull)

        for j in reversed(range(1, half)):
            both_steps(2 * j + 1)
            both_steps(2 * j)
        for j in range(1, half):
            ff_sum.join(j)
        ff_sum.upper()
        both_steps(1)
        both_steps(0)
        sum_of_b.service(1)
        for m in range(2, z_count):
            sum_of_b.service(m)
        ff_sum.join(0)
        loads["hid"].wait()
        loads["n2"].wait()
        g_ff[:, 0:fj] = dot_tn(n2_ref[...], dpre[...]).astype(BF)
        g_ff[:, fj : 2 * fj] = dot_tn(dfs[...].reshape(total, width), hid[...]).astype(BF)
        sum_of_b.service(0)
        sum_of_ff = RowSum(net, place, g_ff, yf, zsf, zrf, sum_ff)
        sum_of_ff.start()

        loads["qkv"].wait()
        lane_first, lane_end, lane = doc_bounds(triples_ref, docs)
        for r in range(0, total, blk):
            at = slice(r, r + blk)
            q = qkv_ref[at, 0:hd].astype(F32)
            k = qkv_ref[at, hd : 2 * hd].astype(F32)
            row = lax.broadcasted_iota(jnp.int32, (blk, LANES), 0) + r
            inside = (row >= 3 * lane_first) & (row < 3 * lane_end)
            fk = jnp.where(inside, 1.0, 0.0)
            fq = jnp.where(inside | (lane >= docs), 0.0, MASKED)
            head_inputs(qs, ks, at, q, k, fq, fk, heads)
            kt[:, at] = k.T.astype(BF)
            dk[at, :] = jnp.zeros((blk, LANES), F32)
            dv[at, :] = jnp.zeros((blk, LANES), F32)

        def recompute(n):
            r = n * blk
            for h in range(heads):
                e, inv = softmax_block(ks, qs, h, r, r + blk)
                ps[n][h] = (e * inv).astype(BF)

        for n in range(blocks // 2):
            recompute(n)

        push(1, MOMENT_DECAY * mi[1] + ff1_ref[:, 0:fj])
        push(3, MOMENT_DECAY * md[1] + ff1_ref[:, fj : 2 * fj])

        ff_sum.finish()
        loads["mid"].wait()
        for r in range(0, rows, LANES):
            at = slice(r, r + LANES)
            dx, dg = layer_norm_back(mid_ref[at, :], gain_ref[1:2, :], acc[0, at, :])
            dx = dx + da_ref[at, :]
            dm[at, :] = dx
            da_low[at, :] = dx.astype(BF)
            dg = jnp.sum(dg, axis=0, keepdims=True)
            gain_two = dg if r == 0 else gain_two + dg
        got = dot_nt(da_low[...], wo_ref[...]).astype(BF)
        for e in range(fs_count):
            do_out[e] = got[:, e * hd : (e + 1) * hd]
            da_out[e] = da_low[:, e * hd : (e + 1) * hd]

        def exchange(blocks_of, landed):
            found = []
            for e in range(1, fs_count):
                found.append(net.start(blocks_of.at[flip(fs, e)], landed.at[e], (dp, flip(fs, e))))
            landed[0] = blocks_of[fs]
            return found

        do_f = exchange(do_out, do_in)
        da_f = exchange(da_out, da_in)
        for n in range(blocks // 2, blocks):
            recompute(n)
        for m in range(1, z_count):
            sum_of_ff.service(m)
        sum_of_ff.service(0)

        place_of = lax.broadcasted_iota(jnp.int32, (blk, LANES), 1) // HEAD
        for r in range(0, total, blk):
            at = slice(r, r + blk)
            q = widen(qkv_ref[at, 0:hd].astype(F32))
            for h in range(heads):
                qs[h, at, :] = jnp.where(place_of == h, q, 0.0).astype(BF)
        lane_head = lax.broadcasted_iota(jnp.int32, (rows, LANES), 1) // HEAD
        for e in range(fs_count):
            if e:
                do_f[e - 1].wait_recv()
            base = pl.multiple_of(flip(fs, e) * rows, 16)
            do = widen(do_in[e].astype(F32))
            for h in range(heads):
                ks[h, pl.ds(base, rows), :] = jnp.where(lane_head == h, do, 0.0).astype(BF)
        for e in range(fs_count):
            if e:
                da_f[e - 1].wait_recv()
            cols[pl.ds(pl.multiple_of(flip(fs, e) * rows, 16), rows), :] = da_in[e]

        loads["att"].wait()
        g_out = dot_tn(att_ref[...], cols[...]).astype(BF)
        for e in range(fs_count):
            base = pl.multiple_of(flip(fs, e) * hd, 16)
            g_o[pl.ds(base, hd), :] = g_out[e * hd : (e + 1) * hd, :]
        sum_of_o = RowSum(net, place, g_o, yo, zso, zro, sum_o)
        sum_of_o.start()
        sum_of_b.finish()
        push(5, MOMENT_DECAY * mq[1] + jnp.concatenate([sum_q[1, t] for t in range(3)], axis=1))
        push(6, MOMENT_DECAY * mp[...] + sum_b[:, 0:pc])
        push(7, MOMENT_DECAY * mu[...] + sum_b[:, pc : 2 * pc])
        push(9, MOMENT_DECAY * mo[1] + sum_b[:, 2 * pc :])

        loads["cos"].wait()
        loads["sin"].wait()
        for n in range(blocks):
            r, stop = n * blk, (n + 1) * blk
            at = slice(r, stop)
            found = []
            add_k = add_v = None
            for h in range(heads):
                p = ps[n][h]
                v = widen(qkv_ref[0:stop, 2 * hd : 3 * hd])
                grad = dot_nt(v, ks[h, at, :])
                wide = p.astype(F32)
                middle = jnp.sum(wide * grad, axis=0, keepdims=True)
                dr = (wide * (grad - middle) * 0.125).astype(BF)
                part_v = dot_nn(p, ks[h, at, :])
                part_k = dot_nn(dr, qs[h, at, :])
                add_v = part_v if add_v is None else add_v + part_v
                add_k = part_k if add_k is None else add_k + part_k
                found.append(dot_nn(kt[h * HEAD : (h + 1) * HEAD, 0:stop], dr))
            dk[0:stop, :] += add_k
            dv[0:stop, :] += add_v
            dq = jnp.concatenate(found, axis=0).T
            dqkv[at, 0:hd] = (dq * cos_ref[at, :] - partner(dq) * sin_ref[at, :]).astype(BF)
            if n == blocks // 2:
                for m in range(1, z_count):
                    sum_of_o.service(m)
                sum_of_o.service(0)
        for r in range(0, total, blk):
            at = slice(r, r + blk)
            grad = dk[at, 0:hd]
            dqkv[at, hd : 2 * hd] = (grad * cos_ref[at, :] - partner(grad) * sin_ref[at, :]).astype(BF)
            dqkv[at, 2 * hd : 3 * hd] = dv[at, 0:hd].astype(BF)
        loads["n1"].wait()
        g_at[...] = dot_tn(n1_ref[...], dqkv[...]).astype(BF)
        sum_of_at = HeadSum(net, place, g_at, qsa, qra, sum_q.at[0])
        sum_of_at.start()

        ff_sum.sent()
        at_sum = Scatter(net, dp, fs, fs_count, sbuf, rbuf, xsend, xrecv, acc)
        tiles[0] = jnp.zeros((8, width), F32)

        def push_out(e, out):
            base = pl.multiple_of(flip(fs, e) * rows, 16)
            part = dot_nt(dqkv[pl.ds(base, rows), :], wq_ref[...])
            out[...] = part.astype(out.dtype)
            work[:, 0:width] = part

            def grow(r):
                here = pl.ds(pl.multiple_of(base + r, HEAD), HEAD)
                grown = work[pl.ds(r, HEAD), 0:width] * n1_ref[here, :].astype(F32)
                tiles[0] = tiles[0] + jnp.sum(grown.reshape(HEAD // 8, 8, width), axis=0)

            row_loop(rows, grow)

        for e in reversed(range(2, fs_count)):
            part_into(at_sum, e, push_out)
        part_into(at_sum, 1, push_out)
        for j in range(1, half):
            at_sum.join(j)
        at_sum.upper()
        part_into(at_sum, 0, push_out)
        gain_one = jnp.sum(tiles[0], axis=0, keepdims=True) / gain_ref[0:1, :]
        which = lax.broadcasted_iota(jnp.int32, (8, width), 0)
        both = jnp.where(which == 0, gain_one, jnp.where(which == 1, gain_two, 0.0))
        both = jnp.where(which == 2, dgain_two[0:1, :], jnp.where(which == 3, dgain_two[1:2, :], both))
        hops = [(dp, flip(fs, 1 << n)) for n in range(fs_count.bit_length() - 1)]
        hops += [(flip(dp, 1 << n), fs) for n in range(dp_count.bit_length() - 1)]

        def hop_out(n, value):
            tiles[1 + n] = value
            return net.start(tiles.at[1 + n], tiles.at[1 + len(hops) + n], hops[n])

        hop = hop_out(0, both)
        sum_of_ff.finish()
        push(0, MOMENT_DECAY * mi[0] + sum_ff[:, 0:fj])
        push(2, MOMENT_DECAY * md[0] + sum_ff[:, fj : 2 * fj])
        sum_of_o.finish()
        push(8, MOMENT_DECAY * mo[0] + sum_o[...])
        at_sum.join(0)
        sum_of_at.finish()
        push(4, MOMENT_DECAY * mq[0] + jnp.concatenate([sum_q[0, t] for t in range(3)], axis=1))
        hop.wait_recv()
        both = both + tiles[len(hops) + 1]
        hop = hop_out(1, both)
        at_sum.finish()
        for n in range(2, len(hops) - 1):
            hop.wait_recv()
            both = both + tiles[len(hops) + n]
            hop = hop_out(n, both)

        def through_first(r):
            at = pl.ds(r, HEAD)
            dx, _ = layer_norm_back(tok[at, :].astype(F32), gain_ref[0:1, :], acc[0, at, :])
            grad_in[at, :] = dx + dm[at, :]

        row_loop(rows, through_first)

        for k in range(amount):

            @pl.when(mine[k])
            def _():
                landed = box.at[0 : devices - 1, :, 0 : widths[k]]
                pltpu.make_async_copy(landed, landed, push_recv).wait()

        which_k = jnp.int32(0)
        for k in range(1, amount):
            which_k = which_k + k * mine[k].astype(jnp.int32)
        for w in classes:
            chosen = None
            for k in range(amount):
                if widths[k] == w:
                    chosen = mine[k] if chosen is None else chosen | mine[k]

            @pl.when(chosen)
            def _():
                def done(block):
                    def give(i, carry):
                        t = block * dp_count + i

                        @pl.when(t != slot)
                        def _():
                            pltpu.make_async_remote_copy(
                                src_ref=box.at[t, :, 0:w],
                                dst_ref=out.at[which_k, :, 0:w],
                                send_sem=give_send,
                                recv_sem=give_recv.at[which_k],
                                device_id=(i, block),
                                device_id_type=MESH,
                            ).start()
                            pltpu.make_async_remote_copy(
                                src_ref=norm,
                                dst_ref=norms.at[which_k],
                                send_sem=norm_send,
                                recv_sem=norm_recv.at[which_k],
                                device_id=(i, block),
                                device_id_type=MESH,
                            ).start()

                        return carry

                    lax.fori_loop(0, dp_count, give, 0)

                newton_schulz(box, x, norm, fs_count, w, dp_count, rw, done)
                out[which_k, :, 0:w] = box[slot, :, 0:w]
                norms[which_k] = norm[...]

        last = len(hops) - 1
        hop.wait_recv()
        both = both + tiles[len(hops) + last]
        hop = hop_out(last, both)
        hop.wait_recv()
        dgain_out[...] = both + tiles[1 + len(hops) + last]

        for k in range(amount):
            w = widths[k]

            @pl.when(jnp.logical_not(mine[k]))
            def _():
                landed = out.at[k, :, 0:w]
                pltpu.make_async_copy(landed, landed, give_recv.at[k]).wait()
                pltpu.make_async_copy(norms.at[k], norms.at[k], norm_recv.at[k]).wait()
                pltpu.make_async_copy(pieces[k], pieces[k], push_send.at[k]).wait()

            @pl.when(mine[k])
            def _():
                left = box.at[0 : devices - 1, :, 0:w]
                pltpu.make_async_copy(left, left, give_send).wait()

                def drain(t, carry):
                    pltpu.make_async_copy(norm, norm, norm_send).wait()
                    return carry

                lax.fori_loop(0, devices - 1, drain, 0)

        net.finish()

    outs = [
        ((rows, width), F32),
        ((8, width), F32),
        ((rw, cb - 3 * hd), F32),
        ((rw, 2 * fj), F32),
        ((rw, hd), F32),
        ((2, 3, rw, hd), F32),
        ((amount, rw, wide), BF),
        ((amount, 8, LANES), F32),
    ]
    span = max(width, fj)
    zy = (y_count - 1, z_count, rw)
    scratch = [
        ((total, width), BF),
        ((rows, width), F32),
        ((total, 3 * hd), BF),
        ((total, hd), F32),
        ((total, hd), F32),
        ((total, width), BF),
        ((total, width), BF),
        ((rows, width), BF),
        ((fs_count, rows, hd), BF),
        ((fs_count, rows, hd), BF),
        ((fs_count, rows, hd), BF),
        ((fs_count, rows, hd), BF),
        ((total, fj), BF),
        ((total, fj), BF),
        ((total, fj), BF),
        ((rows, span), F32),
        ((heads, total, LANES), BF),
        ((heads, total, LANES), BF),
        ((hd, total), BF),
        ((total, LANES), F32),
        ((total, LANES), F32),
        ((rows, width), F32),
        ((total, hd), BF),
        ((width, 2 * fj), BF),
        ((width, 3 * hd), BF),
        ((width, hd), BF),
        ((half, rows, width), BF),
        ((half, rows, width), BF),
        ((half - 1, rows, width), BF),
        ((half - 1, rows, width), BF),
        ((half, rows, width), F32),
        (zy + (cb,), BF),
        ((z_count - 1, rw, cb - 3 * hd), BF),
        ((z_count - 1, rw, cb - 3 * hd), BF),
        ((z_count, 3, rw, hd), BF),
        ((z_count, 3, rw, hd), BF),
        (zy + (2 * fj,), BF),
        ((z_count - 1, rw, 2 * fj), BF),
        ((z_count - 1, rw, 2 * fj), BF),
        (zy + (hd,), BF),
        ((z_count - 1, rw, hd), BF),
        ((z_count - 1, rw, hd), BF),
        ((dp_count, 3, rw, hd), BF),
        ((dp_count, 3, rw, hd), BF),
        ((2 * (fs_count.bit_length() + dp_count.bit_length() - 2) + 1, 8, width), F32),
        ((devices, rw, wide), BF),
        ((width, fs_count * wide), BF),
        ((8, LANES), F32),
    ]
    tail = [pltpu.VMEM((heads, (n + 1) * blk, blk), BF) for n in range(blocks)]
    tail += [pltpu.VMEM((rw, w), BF) for w in widths]
    dma = pltpu.SemaphoreType.DMA
    tail = [dma((sems,)), dma((sems,)), dma((amount,)), dma, dma, dma((amount,)), dma, dma((amount,))] + tail
    arrays = (da, dfs, n2, hid_in, slope_in, wi, wd, mid, gain_rows, qkv, wo_full, wq, cos, sin, triples, n1, att_rel, tokens, group_b, dgain_b, sum_ff1, *moments)
    return pl.pallas_call(
        body,
        out_shape=[jax.ShapeDtypeStruct(s, t) for s, t in outs],
        in_specs=[hbm() if n in (2, 3, 4, 7, 9, 12, 13, 15, 16) else smem() if n == 14 else vmem() for n in range(27)],
        out_specs=[vmem()] * len(outs),
        scratch_shapes=[pltpu.VMEM(s, t) for s, t in scratch] + tail,
        compiler_params=pltpu.CompilerParams(collective_id=5, has_side_effects=True, vmem_limit_bytes=VMEM_BYTES),
        cost_estimate=cost(4e10, 3e7),
        name="backward_all",
    )(*arrays)


def update(dp_arr, sums, results, norms, roots, dgain, moments, weights, m_gains_t, gains_t, layer_out, grad_in):
    sum_q, sum_o, sum_ff, sum_ff1, sum_rest = sums
    rw, hd = sum_o.shape
    fj = sum_ff.shape[1] // 2
    pc = moments[4].shape[1]
    width = dgain.shape[1]

    def body(me_ref, q_ref, o_ref, ff_ref, ff1_ref, rest_ref, res, norms_ref, roots_ref, dg, *refs):
        m_in, w_in, (mg, g, act, grad), refs = refs[:6], refs[6:12], refs[12:16], refs[16:]
        m_out, w_out, (mg_out, g_out, act_out, grad_out, rms), turned = refs[:6], refs[6:12], refs[12:17], refs[17]
        act_out[...] = act[...]
        grad_out[...] = grad[...]
        at = 2 * pc
        grads = [
            [jnp.concatenate([q_ref[b, t] for t in range(3)], axis=1) for b in range(2)],
            [o_ref[...], rest_ref[:, at:]],
            [ff_ref[:, 0:fj], ff1_ref[:, 0:fj]],
            [ff_ref[:, fj : 2 * fj], ff1_ref[:, fj : 2 * fj]],
            [rest_ref[:, 0:pc]],
            [rest_ref[:, pc : 2 * pc]],
        ]
        places = [(4, 5), (8, 9), (0, 1), (2, 3), (6,), (7,)]
        for kind in range(6):
            for b in range(len(grads[kind])):
                here = (b,) if kind < 4 else (slice(None),)
                have = m_in[kind].shape[-1]
                m_out[kind][here] = MOMENT_DECAY * m_in[kind][here] + grads[kind][b]
                turn = res[places[kind][b], :, 0:have].astype(F32)
                w_out[kind][here] = w_in[kind][here] - STEP_SCALES[kind] * turn
        turned[...] = jnp.concatenate([dg[...], jnp.zeros((LANES - 8, width), F32)], axis=0).T
        mine = turned[pl.ds(pl.multiple_of(me_ref[0] * rw, 16), rw), :].T
        fresh = GAIN_DECAY * mg[...] + mine[0:4, :]
        mg_out[...] = fresh
        g_out[...] = g[...] - GAIN_RATE * fresh
        places = (4, 5, 8, 9, 0, 1, 2, 3, 6, 7)
        lengths = jnp.concatenate([norms_ref[p, 0:1, :] for p in places] + [norms_ref[0, 0:6, :]], axis=0)
        rms[...] = lengths / roots_ref[...]

    outs = [(a.shape, a.dtype) for a in (*moments, *weights, m_gains_t, gains_t, layer_out, grad_in)] + [((16, LANES), F32)]
    return local_kernel(
        body,
        "update",
        outs,
        [((width, LANES), F32)],
        dp_arr,
        sum_q,
        sum_o,
        sum_ff,
        sum_ff1,
        sum_rest,
        results,
        norms,
        roots,
        dgain,
        *moments,
        *weights,
        m_gains_t,
        gains_t,
        layer_out,
        grad_in,
    )


def rope_tables(total, hd):
    half = HEAD // 2
    frequency = (np.float32(10000.0) ** (-np.arange(half, dtype=np.float32) / np.float32(half))).astype(np.float32)
    angle = (np.arange(total, dtype=np.float32)[:, None] * frequency[None, :]).astype(np.float32)
    cos, sin = np.cos(angle), np.sin(angle)
    cos = np.tile(np.concatenate([cos, cos], axis=1), (1, hd // HEAD))
    sin = np.tile(np.concatenate([-sin, sin], axis=1), (1, hd // HEAD))
    return jnp.asarray(cos, F32), jnp.asarray(sin, F32)


def on_device(
    y_count,
    tokens,
    cotangent,
    doc_triples,
    w_qkv,
    w_out,
    w_in,
    w_down,
    w_pool,
    w_up,
    gains,
    m_qkv,
    m_out,
    m_in,
    m_down,
    m_pool,
    m_up,
    m_gains,
):
    rows, width = tokens.shape
    fs_count, dp_count = lax.axis_size("fsdp"), lax.axis_size("dp")
    dp_arr = lax.axis_index("dp").astype(jnp.int32).reshape(1)
    total = rows * fs_count
    hd = width // fs_count

    cos0, sin0 = rope_tables(total, hd)

    old_weights = (w_qkv, w_out, w_in, w_down, w_pool, w_up)
    if total <= 2048:
        (
            n1, qkv, att_rel, n2, hid, slope, wo_full, mid, wqkv0, wi0, wd0, gain_rows, layer_out, da, dfs, group_b, sum_ff1, dgain_b
        ) = forward_all(
            y_count, dp_count, fs_count, tokens, cotangent, doc_triples, old_weights, gains.T, cos0, sin0
        )
    else:
        cos1, sin1 = cos0[: total // 3], sin0[: total // 3]
        (
            n1, qkv, att_rel, wo_full, n2, hid, slope, mid, after, z_blocks, s0, wqkv0, wi0, wd0, wp, wqkv1, wu, c_rel, gain_rows
        ) = forward_one(
            y_count, dp_count, fs_count, tokens, cotangent, doc_triples, old_weights, gains.T, cos0, sin0
        )
        layer_out, da, dfs, group_b, sum_ff1, dgain_b = middle(
            y_count, dp_count, fs_count, s0, after, z_blocks, cotangent, c_rel, wqkv1, wu, old_weights[1:4], wp, gain_rows,
            cos1, sin1, doc_triples,
        )
    moments = (m_qkv, m_out, m_in, m_down, m_pool, m_up)
    kept = (da, dfs, n2, hid, slope, wi0, wd0, mid, gain_rows, qkv, wo_full, wqkv0, cos0, sin0, doc_triples, n1, att_rel, tokens)
    if total <= 2048:
        grad_in, dgain, sum_rest, sum_ff, sum_o, sum_q, results, norms = backward_all(
            y_count, dp_count, fs_count, *kept, group_b, dgain_b, sum_ff1, moments
        )
        sums = (sum_q, sum_o, sum_ff, sum_ff1, sum_rest)
    else:
        grad_in, dgain, sum_rest, sum_ff, sum_o, sum_q = backward_one(
            y_count, dp_count, fs_count, *kept, group_b, dgain_b
        )
        sums = (sum_q, sum_o, sum_ff, sum_ff1, sum_rest)
        results, norms, dgain = muon(y_count, dp_count, fs_count, sums, moments, dgain)

    all_tokens = float(total * dp_count)
    entries = [m.size // (2 if m.ndim == 3 else 1) for m in moments for _ in range(2 if m.ndim == 3 else 1)]
    roots = np.ones((16, LANES), np.float64)
    roots[:10] = np.array([float(n * fs_count * dp_count) * all_tokens for n in entries])[:, None] ** 0.5
    *fresh, gain_moments, new_gains, layer_out, grad_in, rms = update(
        dp_arr, sums, results, norms, jnp.asarray(roots, F32), dgain, moments, old_weights, m_gains.T, gains.T, layer_out, grad_in
    )
    return (layer_out, grad_in, *fresh, gain_moments.T, new_gains.T, rms[:10, 0])


def solution(mesh):
    by_row, by_dp = P(("dp", "fsdp"), None), P("dp", None)
    stacked, flat = P(None, "dp", "fsdp"), P("dp", "fsdp")
    matrices = (stacked,) * 4 + (flat,) * 2
    y_count = max(1, mesh.shape["fsdp"] // 2)
    return jax.shard_map(
        functools.partial(on_device, y_count),
        mesh=mesh,
        in_specs=(by_row, by_row, by_dp, *matrices, by_dp, *matrices, by_dp),
        out_specs=(by_row, by_row, *matrices, *matrices, by_dp, by_dp, P()),
        check_vma=False,
    )
```
